32 devices in a mesh: section: 2 (over core), dp: 4 (over z), tensor: 4 (over y, x).
Axes of the slice: x: 2, y: 2, z: 4, core: 2. Of those that a mesh axis runs over, the one named last changes fastest.
Arguments:
- inputs: bfloat16 [16, 512, 768], P('dp', 'tensor'), may hold values from -6 to 6
- cls_pos: int32 [16, 4], P('dp'), may hold values from 0 to 496, as said below
- w_qkv: bfloat16 [2, 768, 3, 768], P('section', 'dp', None, 'tensor'), may hold values from -0.21875 to 0.21875
- qv_bias: bfloat16 [2, 2, 4, 192], P('section', None, 'tensor', 'dp'), may hold values from -3 to 3
- w_out: bfloat16 [2, 768, 768], P('section', 'tensor', 'dp'), may hold values from -0.875 to 0.875
- w_in: bfloat16 [2, 768, 3072], P('section', 'dp', 'tensor'), may hold values from -0.21875 to 0.21875
- in_bias: bfloat16 [2, 4, 768], P('section', 'tensor', 'dp'), may hold values from -3 to 3
- w_ffn_out: bfloat16 [2, 3072, 768], P('section', 'tensor', 'dp'), may hold values from -0.109375 to 0.109375
- layer_gains: bfloat16 [2, 2, 768], P('section', None, ('dp', 'tensor')), may hold values from 0.5 to 1.5
- shifts: bfloat16 [2, 4, 768], P('section', None, ('dp', 'tensor')), may hold values from -3 to 3
- queries: bfloat16 [64, 768], P(('dp', 'tensor')), may hold values from -0.59765625 to 0.59765625
- positive: int32 [64], P(('dp', 'tensor')), may hold values from 0 to 63
- token_grad: bfloat16 [16, 512, 768], P('dp', 'tensor'), may hold values from -6 to 6
Outputs:
- grad_qkv: float32 [2, 768, 3, 768], P('section', 'dp', None, 'tensor')
- grad_qv_bias: float32 [2, 2, 4, 192], P('section', None, 'tensor', 'dp')
- grad_out: float32 [2, 768, 768], P('section', 'tensor', 'dp')
- grad_in: float32 [2, 768, 3072], P('section', 'dp', 'tensor')
- grad_in_bias: float32 [2, 4, 768], P('section', 'tensor', 'dp')
- grad_ffn_out: float32 [2, 3072, 768], P('section', 'tensor', 'dp')
- grad_gains: float32 [2, 2, 768], P('section', None, ('dp', 'tensor'))
- grad_shifts: float32 [2, 4, 768], P('section', None, ('dp', 'tensor'))
- boundary: float32 [2, 16, 512, 768], P('section', 'dp', 'tensor')
- mean_loss: float32 [], replicated
The draws below stay inside these ranges and needn't reach their ends.
Inputs may be any that keep to these rules, and one draw needn't show every extreme that they name: `cls_pos`: in each row the entries rise and the first is 0; each passage (up to the next entry, the last up to 512) has 16 tokens or more.
All inputs are finite; a program needn't handle non-finite values.
Results may differ from the reference program's by a relative error of at most 0.02.
Values may be sent and summed in bfloat16 or wider, within the bound.
No kernel may reach another device: no remote copies, remote signals or barrier semaphores. Data moves between devices by JAX's collectives and lax.ppermute only.
A program may use at most 192 MiB of HBM per device.

```python
import jax
import jax.numpy as jnp
from jax import lax

D = 768
HEADS = 12
HD = 64
FF = 3072
L = 512
ROWS = 16
P_ALL = 64
NQ = 64
DT = 192
FT = 768
N_TENSOR = 4


def draw_cls_pos(key, part):
    key = jax.random.fold_in(key, 11)
    key_list = jax.random.split(key, 6)
    step_unit = L // 32
    longest_first = jax.random.randint(key_list[0], (ROWS,), 0, 2)
    far_end = jax.random.randint(key_list[1], (ROWS,), 25 * step_unit, 28 * step_unit)
    near_start = jax.random.randint(key_list[2], (ROWS,), step_unit, 7 * step_unit)
    extra_len = jax.random.randint(key_list[3], (ROWS,), step_unit, (L - far_end) // 2)
    first_cut = jnp.where(longest_first == 1, far_end, near_start)
    second_cut = jnp.where(longest_first == 1, far_end + extra_len, far_end)
    third_cut = second_cut + jax.random.randint(key_list[4], (ROWS,), step_unit, L - second_cut - step_unit + 1)
    chosen_row = jax.random.randint(key_list[5], (), 0, ROWS)
    third_cut = jnp.where(jnp.arange(ROWS, dtype=jnp.int32) == chosen_row, L - step_unit, third_cut)
    return jnp.stack([jnp.zeros_like(first_cut), first_cut, second_cut, third_cut], -1).astype(jnp.int32)


def touch_ends(values, stream_key, smallest, largest):
    index_at = [jax.random.randint(jax.random.fold_in(stream_key, axis), (), 0, length) for axis, length in enumerate(values.shape)]
    main_axis = values.shape.index(max(values.shape))
    beside = index_at[:main_axis] + [(index_at[main_axis] + 1) % values.shape[main_axis]] + index_at[main_axis + 1:]
    return values.at[tuple(index_at)].set(smallest).at[tuple(beside)].set(largest)


def block_scale(stream_key, shape, pieces, low, top_value):
    level, own = 1.0, jax.random.fold_in(stream_key, 6)
    for dim, shards_of in pieces:
        draws = jnp.exp(jax.random.uniform(jax.random.fold_in(own, dim), (shards_of,), jnp.float32, low / len(pieces), top_value / len(pieces)))
        level = level * jnp.repeat(draws, shape[dim] // shards_of).reshape([-1 if axis == dim else 1 for axis in range(len(shape))])
    return level


def noise(stream_key, shape, scale, most, cuts=(), kind=jnp.bfloat16):
    entries = scale * jax.random.normal(stream_key, shape, jnp.float32)
    if cuts:
        entries = entries * block_scale(stream_key, shape, cuts, -0.22, 0.18)
    return jnp.clip(entries, -most, most).astype(kind)


def setup_inputs(seed: int = 0) -> dict:
    seeds = jax.random.split(jax.random.key(seed), 14)
    return {
        "inputs": noise(seeds[0], (ROWS, L, D), 1.0, 6.0, ((0, 4), (1, 4))),
        "cls_pos": draw_cls_pos(jax.random.fold_in(seeds[13], 71), 0),
        "w_qkv": noise(seeds[2], (2, D, 3, D), D ** -0.5, 0.21875, ((0, 2), (1, 4), (3, 4))),
        "qv_bias": noise(seeds[3], (2, 2, N_TENSOR, DT), 0.5, 3.0, ((0, 2), (2, 4), (3, 4))),
        "w_out": noise(seeds[4], (2, D, D), (D // 16) ** -0.5, 0.875, ((0, 2), (1, 4), (2, 4))),
        "w_in": noise(seeds[5], (2, D, FF), D ** -0.5, 0.21875, ((0, 2), (1, 4), (2, 4))),
        "in_bias": noise(seeds[6], (2, N_TENSOR, FT), 0.5, 3.0, ((0, 2), (1, 4), (2, 4))),
        "w_ffn_out": noise(seeds[7], (2, FF, D), FF ** -0.5, 0.109375, ((0, 2), (1, 4), (2, 4))),
        "layer_gains": jnp.clip(1.0 + 0.1 * jax.random.normal(seeds[8], (2, 2, D), jnp.float32), 0.5, 1.5).astype(jnp.bfloat16),
        "shifts": noise(seeds[9], (2, 4, D), 0.5, 3.0, ((0, 2), (2, 16))),
        "queries": noise(seeds[10], (NQ, D), 0.1, 0.59765625, ((0, 16),)),
        "positive": touch_ends(jax.random.randint(seeds[11], (NQ,), 0, P_ALL), jax.random.fold_in(seeds[11], 1), 0, P_ALL - 1).astype(jnp.int32),
        "token_grad": noise(seeds[12], (ROWS, L, D), 1.0, 6.0, ((0, 4), (1, 4))),
    }


@jax.custom_vjp
def low(v):
    return lax.optimization_barrier(v.astype(jnp.bfloat16)).astype(jnp.float32)

@jax.custom_vjp
def low_back(v):
    return v

def low_keep(v):
    return (low(v), None)

def low_pass(kept, grad):
    return (grad,)

def back_keep(v):
    return (v, None)

def back_low(kept, grad):
    return (low(grad),)
low.defvjp(low_keep, low_pass)
low_back.defvjp(back_keep, back_low)
highest = lax.Precision.HIGHEST

def layer_norm(values, gain, shift):
    centre = values - lax.optimization_barrier(jnp.mean(values, -1, keepdims=True))
    spread = lax.optimization_barrier(jnp.mean(centre * centre, -1, keepdims=True))
    return centre * lax.rsqrt(spread + 1e-05) * gain + shift

def attend_row(row_items):
    query_row, key_rows, value_rows, segments = row_items
    scores = jnp.einsum('qhd,khd->hqk', query_row, key_rows, precision=highest) * 0.125
    same = segments[:, None] == segments[None, :]
    scores = low_back(jnp.where(same[None], scores, -1e+30))
    log_total = jax.nn.logsumexp(scores, -1, keepdims=True)
    weights = low(jnp.exp(scores - log_total))
    context = jnp.einsum('hqk,khd->qhd', weights, value_rows, precision=highest)
    return context.reshape(context.shape[0], -1)

def encoder_layer(hidden, proj_qkv, bias_qv, proj_out, proj_in, bias_in, proj_ffn, gain_rows, shift_rows, segments):
    rows_all = hidden.shape[0]
    bias_rows = jnp.stack([bias_qv[0], jnp.zeros_like(bias_qv[0]), bias_qv[1]])
    projected = jnp.einsum('rld,dcf->rlcf', hidden, proj_qkv, precision=highest) + bias_rows
    projected = low_back(low(projected))
    split_rows = projected.reshape(rows_all, L, 3, HEADS, HD)
    context = lax.map(jax.checkpoint(attend_row), (split_rows[:, :, 0], split_rows[:, :, 1], split_rows[:, :, 2], segments))
    context = low_back(low(context))
    attn_out = low_back(jnp.einsum('rlf,fd->rld', context, proj_out, precision=highest))
    middle = layer_norm(hidden + attn_out + shift_rows[0], gain_rows[0], shift_rows[1])
    pre_act = low_back(jnp.einsum('rld,df->rlf', low(middle), proj_in, precision=highest) + bias_in)
    activated = low(jax.nn.gelu(pre_act, approximate=False))
    ffn_out = low_back(jnp.einsum('rlf,fd->rld', activated, proj_ffn, precision=highest))
    return layer_norm(middle + ffn_out + shift_rows[2], gain_rows[1], shift_rows[3])

def reference(inputs, cls_pos, w_qkv, qv_bias, w_out, w_in, in_bias, w_ffn_out, layer_gains, shifts, queries, positive, token_grad):
    positions = jnp.arange(L, dtype=jnp.int32)
    segments = lax.optimization_barrier(jnp.sum((positions[None, :, None] >= cls_pos[:, None, :]).astype(jnp.int32), -1)) - 1
    query_rows = queries.astype(jnp.float32)

    def forward(hidden, proj_qkv, bias_qv, proj_out, proj_in, bias_in, proj_ffn, gain_all, shift_all):
        for level in range(2):
            hidden = encoder_layer(hidden, proj_qkv[level], bias_qv[level], proj_out[level], proj_in[level], bias_in[level], proj_ffn[level], gain_all[level], shift_all[level], segments)
            if level == 0:
                hidden = low_back(low(hidden))
        output = low(hidden)
        passages = jnp.take_along_axis(output, cls_pos[:, :, None], axis=1).reshape(-1, D)
        logits = low_back(jnp.dot(query_rows, passages.T, precision=highest, preferred_element_type=jnp.float32))
        chosen = jnp.take_along_axis(logits, positive[:, None], axis=1)[:, 0]
        return (output, jnp.sum(jax.nn.logsumexp(logits, -1) - chosen))
    primal, pull = jax.vjp(forward, inputs.astype(jnp.float32), w_qkv.astype(jnp.float32), qv_bias.reshape(2, 2, D).astype(jnp.float32), w_out.astype(jnp.float32), w_in.astype(jnp.float32), in_bias.reshape(2, FF).astype(jnp.float32), w_ffn_out.astype(jnp.float32), layer_gains.astype(jnp.float32), shifts.astype(jnp.float32))
    output, total = primal
    grads = pull((token_grad.astype(jnp.float32), jnp.asarray(16.0, dtype=jnp.float32)))
    d_input, g_qkv, g_qv, g_out, g_in, g_inb, g_ffn, g_gain, g_shift = grads
    boundary = jnp.stack([d_input, output])
    return (g_qkv, g_qv.reshape(2, 2, N_TENSOR, DT), g_out, g_in, g_inb.reshape(2, N_TENSOR, FT), g_ffn, g_gain, g_shift, boundary, total / NQ)
```

```python
import jax
import jax.numpy as jnp
from jax import lax
from jax.sharding import PartitionSpec as P

HD = 64
EXTRA = 16
BF16 = jnp.bfloat16
F32 = jnp.float32


def mm(left, right, dims):
    return lax.dot_general(left, right, (dims, ((), ())), preferred_element_type=F32)


def nn(left, right):
    return mm(left, right, ((1,), (0,)))


def nt(left, right):
    return mm(left, right, ((1,), (1,)))


def tn(left, right):
    return mm(left, right, ((0,), (0,)))


def swap_cores(block):
    return lax.ppermute(block, "section", [(0, 1), (1, 0)])


def hop_tensor(block, flip):
    return lax.ppermute(block, "tensor", [(i, i ^ flip) for i in range(lax.axis_size("tensor"))])


def hop_mirrored(block, flips):
    size = lax.axis_size("tensor")
    route = [(s * size + i, s * size + (i ^ flips[s])) for s in range(2) for i in range(size)]
    return lax.ppermute(block, ("section", "tensor"), route)


def direct_dp():
    return lax.axis_size("dp") == 4


def dp_order():
    size = lax.axis_size("dp")
    if direct_dp():
        return lax.axis_index("dp") ^ jnp.arange(size, dtype=jnp.int32)
    return jnp.arange(size, dtype=jnp.int32)


def gather_dp(block):
    if direct_dp():
        others = [
            lax.ppermute(block, "dp", [(i, i ^ k) for i in range(4)]) for k in range(1, 4)
        ]
        return jnp.stack([block] + others)
    return lax.all_gather(block, "dp", axis=0, tiled=False)


def scatter_dp(slots):
    if direct_dp():
        total = slots[0].astype(F32)
        for k in range(1, 4):
            got = lax.ppermute(slots[k], "dp", [(i, i ^ k) for i in range(4)])
            total = total + got.astype(F32)
        return total
    return lax.psum_scatter(slots, "dp", scatter_dimension=0, tiled=False).astype(F32)


def add_low(left, right):
    return (left.astype(F32) + right.astype(F32)).astype(BF16)


def gather_tensor(block, first, second):
    near = hop_mirrored(block, first)
    far = hop_mirrored(block, second)
    both = hop_mirrored(near, second)
    return [block, near, far, both]


def scatter_tensor(slots, first, second):
    got_own = hop_mirrored(slots[2], second)
    got_near = hop_mirrored(slots[3], second)
    own = add_low(slots[0], got_own)
    near = add_low(slots[1], got_near)
    return add_low(own, hop_mirrored(near, first))


PLAIN = ((1, 1), (2, 2))
CROSS = ((2, 2), (1, 1))
MIRROR = ((1, 2), (2, 1))


def slot_of(slots, own):
    order = dp_order()
    return jnp.concatenate(
        [lax.dynamic_index_in_dim(slots, order[k], 0, keepdims=True) for k in range(slots.shape[0])]
    )


def norm_parts(values):
    centre = values - jnp.mean(values, -1, keepdims=True)
    spread = jnp.mean(centre * centre, -1, keepdims=True)
    scale = lax.rsqrt(spread + 1e-05)
    return centre * scale, scale


def norm_back(d_out, gain, xhat, scale):
    g = d_out * gain
    return scale * (
        g - jnp.mean(g, -1, keepdims=True) - xhat * jnp.mean(g * xhat, -1, keepdims=True)
    )


def heads_of(block):
    return jnp.stack([block[:, i : i + HD] for i in range(0, block.shape[1], HD)])


def unheads(block):
    return jnp.concatenate([block[i] for i in range(block.shape[0])], 1)


def bmm(left, right, ca, cb):
    return lax.dot_general(left, right, (((ca,), (cb,)), ((0,), (0,))), preferred_element_type=F32)


def attention_forward(x, w_qk, w_vo, bias_q, bias_v, same):
    cols = w_qk[0].shape[1] // 2
    kept = []
    part = 0.0
    for j in range(2):
        q = (nn(x, w_qk[j][:, :cols]) + bias_q[j]).astype(BF16)
        k = nn(x, w_qk[j][:, cols:]).astype(BF16)
        v = (nn(x, w_vo[j][:, :cols]) + bias_v[j]).astype(BF16)
        qh, kh, vh = heads_of(q), heads_of(k), heads_of(v)
        scores = jnp.where(same, bmm(qh, kh, 2, 2) * 0.125, -1e30)
        top = jnp.max(scores, -1, keepdims=True)
        log_total = top + jnp.log(jnp.sum(jnp.exp(scores - top), -1, keepdims=True))
        probs = jnp.exp(scores - log_total).astype(BF16)
        context = unheads(bmm(probs, vh, 2, 1).astype(BF16))
        part = part + nt(context, w_vo[j][:, cols:])
        kept.append((q, k, v, log_total, context))
    return part.astype(BF16), kept


def attention_backward(x, d_attn, kept, w_qk, w_vo, same):
    cols = w_qk[0].shape[1] // 2
    part = 0.0
    grad_qk, grad_vo, grad_bias = [], [], []
    for j in range(2):
        q, k, v, log_total, context = kept[j]
        d_context = nn(d_attn, w_vo[j][:, cols:]).astype(BF16)
        qh, kh, vh, dh = heads_of(q), heads_of(k), heads_of(v), heads_of(d_context)
        scores = jnp.where(same, bmm(qh, kh, 2, 2) * 0.125, -1e30)
        weights = jnp.exp(scores - log_total)
        d_v = unheads(bmm(weights.astype(BF16), dh, 1, 1)).astype(BF16)
        d_w = bmm(dh, vh, 2, 2)
        d_s = (weights * (d_w - jnp.sum(weights * d_w, -1, keepdims=True))).astype(BF16)
        d_q = unheads(bmm(d_s, kh, 2, 1) * 0.125).astype(BF16)
        d_k = unheads(bmm(d_s, qh, 1, 1) * 0.125).astype(BF16)
        d_qk = jnp.concatenate([d_q, d_k], 1)
        part = part + nt(d_qk, w_qk[j]) + nt(d_v, w_vo[j][:, :cols])
        grad_qk.append(tn(x, d_qk))
        grad_vo.append(jnp.concatenate([tn(x, d_v), tn(d_attn, context)], 1))
        grad_bias.append((jnp.sum(d_q.astype(F32), 0), jnp.sum(d_v.astype(F32), 0)))
    return part.astype(BF16), grad_qk, grad_vo, grad_bias


def feed_forward(mid, w_b, bias_in):
    part = 0.0
    kept = []
    for j in range(4):
        units = w_b[j].shape[1] // 2
        pre = nn(mid, w_b[j][:, :units]) + bias_in[j]
        cdf = 0.5 * (1.0 + lax.erf(pre * 0.7071067811865476))
        slope = cdf + pre * jnp.exp(-0.5 * pre * pre) * 0.3989422804014327
        act = (pre * cdf).astype(BF16)
        part = part + nt(act, w_b[j][:, units:])
        kept.append((act, slope))
    return part.astype(BF16), kept


def feed_back(mid, d_ffn, kept, w_b):
    part = 0.0
    grads, grad_bias = [], []
    for j in range(4):
        units = w_b[j].shape[1] // 2
        act, slope = kept[j]
        d_pre = (slope * nn(d_ffn, w_b[j][:, units:])).astype(BF16)
        part = part + nt(d_pre, w_b[j][:, :units])
        grads.append(jnp.concatenate([tn(mid, d_pre), tn(d_ffn, act)], 1))
        grad_bias.append(jnp.sum(d_pre.astype(F32), 0))
    return part.astype(BF16), grads, grad_bias


def on_device(
    inputs, cls_pos, w_qkv, qv_bias, w_out, w_in, in_bias, w_ffn_out,
    layer_gains, shifts, queries, positive, token_grad,
):
    core = lax.axis_index("section")
    dp = lax.axis_index("dp")
    me = lax.axis_index("tensor")
    n_dp = lax.axis_size("dp")
    n_t = lax.axis_size("tensor")
    first_core = core == 0
    rows_dev, share, width = inputs.shape
    rows = w_qkv.shape[1]
    cols = w_qkv.shape[3]
    half = w_in.shape[2] // 2
    units = in_bias.shape[2]

    out_t = w_out[0].T
    ffn_t = w_ffn_out[0].T
    vec = jnp.concatenate(
        [
            layer_gains.reshape(-1), shifts.reshape(-1), qv_bias.reshape(-1), in_bias.reshape(-1),
            queries.reshape(-1), (positive // 16).astype(BF16), (positive % 16).astype(BF16),
        ]
    )
    n_vec = vec.shape[0]
    vec = jnp.pad(vec, (0, EXTRA * 2 * cols - n_vec)).reshape(EXTRA, 2 * cols)
    pack_a = [
        jnp.concatenate([jnp.concatenate([left, right], 1), vec])
        for left, right in ((w_qkv[0, :, 0], w_qkv[0, :, 1]), (w_qkv[0, :, 2], out_t))
    ]
    pack_b = [
        jnp.concatenate([w_in[0, :, c * half : (c + 1) * half], ffn_t[:, c * half : (c + 1) * half]], 1)
        for c in range(2)
    ]

    def by_layer(pack):
        keep = jnp.where(first_core, pack[0], pack[1])
        got = swap_cores(jnp.where(first_core, pack[1], pack[0]))
        return [jnp.where(first_core, keep, got), jnp.where(first_core, got, keep)]

    shard_a = by_layer(pack_a)
    shard_b = by_layer(pack_b)

    def spread_rows(block):
        own = lax.dynamic_index_in_dim(block, me, 0, keepdims=False)
        parts = [own] + [
            hop_tensor(lax.dynamic_index_in_dim(block, me ^ k, 0, keepdims=False), k)
            for k in range(1, n_t)
        ]
        return jnp.concatenate(parts, 0)

    x_low = spread_rows(inputs)
    length = n_t * share
    positions = jnp.concatenate(
        [(me ^ k) * share + jnp.arange(share, dtype=jnp.int32) for k in range(n_t)]
    )
    cls_row = lax.dynamic_index_in_dim(cls_pos, me, 0, keepdims=False)
    segments = jnp.sum((positions[:, None] >= cls_row[None, :]).astype(jnp.int32), -1)
    same = (segments[:, None] == segments[None, :])[None]

    order = dp_order()

    def gather_a(shard, plan):
        slots = gather_tensor(gather_dp(shard), *plan)
        extra = jnp.stack([s[:, rows:].reshape(n_dp, -1) for s in slots])
        slots = [slot_of(s[:, :rows], dp).reshape(width, -1) for s in slots]
        keep = jnp.where(first_core, jnp.stack(slots[:2]), jnp.stack(slots[2:]))
        got = swap_cores(jnp.where(first_core, jnp.stack(slots[2:]), jnp.stack(slots[:2])))
        qk = jnp.where(first_core, keep, got)
        vo = jnp.where(first_core, got, keep)
        return qk, vo, extra

    def gather_b(shard):
        slots = gather_tensor(gather_dp(shard), *MIRROR)
        return [slot_of(s, dp).reshape(width, -1) for s in slots]

    a_plan = (PLAIN, CROSS)
    a_flips = [jnp.array(flips, jnp.int32) for flips in ((0, 1, 2, 3), (0, 2, 1, 3))]
    n_chips = n_dp * n_t

    def reorder(flips):
        slot_ids = (order[None, :] * n_t + (me ^ flips)[:, None]).reshape(-1)
        return (jnp.arange(n_chips, dtype=jnp.int32)[:, None] == slot_ids[None, :]).astype(BF16)

    to_natural = [reorder(flips) for flips in a_flips]

    def natural(extra, level):
        flat = extra.reshape(n_chips, -1)[:, :n_vec]
        return nn(to_natural[level], flat)

    layers = []
    for level in range(2):
        qk, vo, extra = gather_a(shard_a[level], a_plan[level])
        wb = gather_b(shard_b[level])
        vecs = natural(extra, level)
        layers.append((qk, vo, wb, vecs))

    n_gain = layer_gains.size
    n_shift = shifts.size
    n_qv = qv_bias.size
    n_inb = units
    piece = width // n_chips

    def read_vectors(vecs):
        at = 0
        gains = vecs[:, at : at + n_gain].reshape(n_chips, 2, piece).transpose(1, 0, 2).reshape(2, width)
        at += n_gain
        shift = vecs[:, at : at + n_shift].reshape(n_chips, 4, piece).transpose(1, 0, 2).reshape(4, width)
        at += n_shift
        qv = vecs[:, at : at + n_qv].reshape(n_dp, n_t, 2, cols // n_dp).transpose(2, 1, 0, 3).reshape(2, n_t, cols)
        at += n_qv
        inb = vecs[:, at : at + n_inb].reshape(n_dp, n_t, units).transpose(1, 0, 2).reshape(n_t, 2 * half)
        return gains, shift, qv, inb

    head_slots = [me ^ lax.dynamic_slice_in_dim(flips, 2 * core, 2) for flips in a_flips]
    unit_flip = jnp.where(first_core, jnp.array([0, 1, 2, 3]), jnp.array([0, 2, 1, 3]))
    unit_slots = me ^ unit_flip

    def pick(table, slots):
        hot = (slots[:, None] == jnp.arange(n_t, dtype=jnp.int32)[None, :]).astype(F32)
        return jnp.sum(hot[:, :, None] * table[None], 1)

    x = x_low
    saved = []
    for level in range(2):
        qk, vo, wb, vecs = layers[level]
        gains, shift, qv, inb = read_vectors(vecs)
        bias_q = pick(qv[0], head_slots[level])
        bias_v = pick(qv[1], head_slots[level])
        bias_in = pick(lax.dynamic_slice_in_dim(inb, core * half, half, 1), unit_slots)
        part, kept_a = attention_forward(x, qk, vo, bias_q, bias_v, same)
        first = x.astype(F32) + (part.astype(F32) + swap_cores(part).astype(F32)) + shift[0]
        xhat1, scale1 = norm_parts(first)
        middle = xhat1 * gains[0] + shift[1]
        mid_low = middle.astype(BF16)
        part, kept_f = feed_forward(mid_low, wb, bias_in)
        second = middle + (part.astype(F32) + swap_cores(part).astype(F32)) + shift[2]
        xhat2, scale2 = norm_parts(second)
        out = (xhat2 * gains[1] + shift[3]).astype(BF16)
        saved.append((x, kept_a, kept_f, xhat1, scale1, mid_low, xhat2, scale2, gains))
        x = out
    y = x

    extra = layers[1][3]
    at = n_gain + n_shift + n_qv + n_inb
    q_dev = queries.shape[0]
    all_q = extra[:, at : at + q_dev * width].reshape(-1, width).astype(BF16)
    at += q_dev * width
    all_pos = (extra[:, at : at + q_dev] * 16.0 + extra[:, at + q_dev : at + 2 * q_dev]).astype(jnp.int32).reshape(-1)
    picker = (cls_row[:, None] == positions[None, :]).astype(BF16)
    n_cls = cls_row.shape[0]
    cls_own = nn(picker, y).astype(BF16)
    cls_slots = jnp.stack(gather_tensor(gather_dp(cls_own), *PLAIN))
    passages = nn(to_natural[0], cls_slots.reshape(n_chips, -1)).astype(BF16).reshape(-1, width)
    logits = nt(all_q, passages)
    top = jnp.max(logits, -1, keepdims=True)
    log_total = top + jnp.log(jnp.sum(jnp.exp(logits - top), -1, keepdims=True))
    hits = all_pos[:, None] == jnp.arange(logits.shape[1], dtype=jnp.int32)[None, :]
    chosen = jnp.sum(jnp.where(hits, logits, 0.0), -1)
    mean_loss = jnp.sum(log_total[:, 0] - chosen) / logits.shape[0]
    d_logits = (16.0 * (jnp.exp(logits - log_total) - hits.astype(F32))).astype(BF16)
    own_cols = lax.dynamic_slice_in_dim(d_logits, (dp * n_t + me) * n_cls, n_cls, 1)
    d_cls = tn(own_cols, all_q)
    d_out = spread_rows(token_grad).astype(F32) + tn(picker.astype(F32), d_cls)

    def pack_extra(level, gain_rows, shift_rows, bias_rows, inb_rows):
        gs = jnp.where(first_core, jnp.concatenate([gain_rows, shift_rows]), 0.0)
        gs = gs.reshape(6, n_chips, piece).transpose(1, 0, 2).reshape(n_chips, -1)
        hot_h = (head_slots[level][:, None] == jnp.arange(n_t, dtype=jnp.int32)[None, :]).astype(F32)
        qv = jnp.sum(hot_h[:, None, :, None] * bias_rows[:, :, None, :], 0)
        qv = qv.reshape(2, n_t, n_dp, -1).transpose(2, 1, 0, 3).reshape(n_chips, -1)
        hot_u = (unit_slots[:, None] == jnp.arange(n_t, dtype=jnp.int32)[None, :]).astype(F32)
        inb = jnp.sum(hot_u[:, :, None] * inb_rows[:, None, :], 0)
        inb = jnp.where(
            (jnp.arange(2) == core)[None, :, None], inb[:, None, :], 0.0
        ).reshape(n_t, n_dp, units).transpose(1, 0, 2).reshape(n_chips, -1)
        flat = jnp.concatenate([gs, qv, inb], 1).astype(BF16)
        flat = tn(to_natural[level], flat).astype(BF16)
        flat = jnp.pad(flat, ((0, 0), (0, EXTRA * 2 * cols - flat.shape[1])))
        return flat.reshape(n_t, n_dp, EXTRA, 2 * cols)

    def to_slots(grad):
        return slot_of(grad.astype(BF16).reshape(n_dp, rows, -1), dp)

    totals = [None, None]
    for level in (1, 0):
        qk, vo, wb, vecs = layers[level]
        x, kept_a, kept_f, xhat1, scale1, mid_low, xhat2, scale2, gains = saved[level]
        d_second = norm_back(d_out, gains[1], xhat2, scale2)
        g_gain2 = jnp.sum(d_out * xhat2, 0)
        g_shift3 = jnp.sum(d_out, 0)
        g_shift2 = jnp.sum(d_second, 0)
        part, grads_b, grad_inb = feed_back(mid_low, d_second.astype(BF16), kept_f, wb)
        d_middle = d_second + (part.astype(F32) + swap_cores(part).astype(F32))
        tot_b = scatter_dp(scatter_tensor([to_slots(g) for g in grads_b], *MIRROR)).astype(BF16)
        d_first = norm_back(d_middle, gains[0], xhat1, scale1)
        g_gain1 = jnp.sum(d_middle * xhat1, 0)
        g_shift1 = jnp.sum(d_middle, 0)
        g_shift0 = jnp.sum(d_first, 0)
        part, grads_qk, grads_vo, grad_bias = attention_backward(
            x, d_first.astype(BF16), kept_a, qk, vo, same
        )
        d_hidden = d_first + (part.astype(F32) + swap_cores(part).astype(F32))
        extra = pack_extra(
            level,
            jnp.stack([g_gain1, g_gain2]),
            jnp.stack([g_shift0, g_shift1, g_shift2, g_shift3]),
            jnp.stack([jnp.stack(pair) for pair in grad_bias]),
            jnp.stack(grad_inb),
        )
        g_qk = jnp.stack([to_slots(g) for g in grads_qk])
        g_vo = jnp.stack([to_slots(g) for g in grads_vo])
        keep = jnp.where(first_core, g_qk, g_vo)
        got = swap_cores(jnp.where(first_core, g_vo, g_qk))
        slots = [jnp.where(first_core, keep[j], got[j]) for j in range(2)]
        slots += [jnp.where(first_core, got[j], keep[j]) for j in range(2)]
        slots = [jnp.concatenate([s, extra[j]], 1) for j, s in enumerate(slots)]
        tot_a = scatter_dp(scatter_tensor(slots, *a_plan[level])).astype(BF16)
        route = [(1 - level, level)]
        totals[level] = (
            tot_a, lax.ppermute(tot_a, "section", route),
            tot_b, lax.ppermute(tot_b, "section", route),
        )
        d_out = d_hidden.astype(BF16).astype(F32)

    own_a, got_a, own_b, got_b = (
        jnp.where(first_core, left, right).astype(F32) for left, right in zip(*totals)
    )
    halves_a = (jnp.where(first_core, own_a, got_a), jnp.where(first_core, got_a, own_a))
    halves_b = (jnp.where(first_core, own_b, got_b), jnp.where(first_core, got_b, own_b))
    grad_qkv = jnp.stack(
        [halves_a[0][:rows, :cols], halves_a[0][:rows, cols:], halves_a[1][:rows, :cols]], 1
    )[None]
    grad_out = halves_a[1][:rows, cols:].T[None]
    grad_in = jnp.concatenate([h[:, :half] for h in halves_b], 1)[None]
    grad_ffn = jnp.concatenate([h[:, half:] for h in halves_b], 1).T[None]
    flat = (halves_a[0][rows:] + halves_a[1][rows:]).reshape(-1)
    at = 0
    grad_gains = flat[at : at + n_gain].reshape(layer_gains.shape)
    at += n_gain
    grad_shifts = flat[at : at + n_shift].reshape(shifts.shape)
    at += n_shift
    grad_qv = flat[at : at + n_qv].reshape(qv_bias.shape)
    at += n_qv
    grad_inb = flat[at : at + n_inb].reshape(in_bias.shape)

    def send_rows(block, section):
        size = n_t
        out = jnp.zeros((n_t, share, width), F32)
        low = block.astype(BF16).reshape(n_t, share, width)
        out = lax.dynamic_update_index_in_dim(out, block[:share].astype(F32), me, 0)
        for k in range(1, n_t):
            route = [(section * size + i, section * size + (i ^ k)) for i in range(size)]
            got = lax.ppermute(low[k], ("section", "tensor"), route)
            out = lax.dynamic_update_index_in_dim(out, got.astype(F32), me ^ k, 0)
        return out

    boundary = jnp.where(first_core, send_rows(d_hidden, 0), send_rows(y, 1))[None]
    return (
        grad_qkv, grad_qv, grad_out, grad_in, grad_inb, grad_ffn,
        grad_gains, grad_shifts, boundary, mean_loss,
    )


def solution(mesh):
    return jax.shard_map(
        on_device,
        mesh=mesh,
        in_specs=(
            P("dp", "tensor", None),
            P("dp", None),
            P("section", "dp", None, "tensor"),
            P("section", None, "tensor", "dp"),
            P("section", "tensor", "dp"),
            P("section", "dp", "tensor"),
            P("section", "tensor", "dp"),
            P("section", "tensor", "dp"),
            P("section", None, ("dp", "tensor")),
            P("section", None, ("dp", "tensor")),
            P(("dp", "tensor"), None),
            P(("dp", "tensor")),
            P("dp", "tensor", None),
        ),
        out_specs=(
            P("section", "dp", None, "tensor"),
            P("section", None, "tensor", "dp"),
            P("section", "tensor", "dp"),
            P("section", "dp", "tensor"),
            P("section", "tensor", "dp"),
            P("section", "tensor", "dp"),
            P("section", None, ("dp", "tensor")),
            P("section", None, ("dp", "tensor")),
            P("section", "dp", "tensor", None),
            P(),
        ),
        check_vma=False,
    )
```

```python
import jax
import jax.numpy as jnp
from jax import lax
from jax.experimental import pallas as pl
from jax.experimental.pallas import tpu as pltpu
from jax.sharding import PartitionSpec as P

HD = 64
BF16 = jnp.bfloat16
F32 = jnp.float32


def mm(left, right, dims):
    return lax.dot_general(left, right, (dims, ((), ())), preferred_element_type=F32)


def nn(left, right):
    return mm(left, right, ((1,), (0,)))


def nt(left, right):
    return mm(left, right, ((1,), (1,)))


def tn(left, right):
    return mm(left, right, ((0,), (0,)))


def swap_cores(block):
    return lax.ppermute(block, "section", [(0, 1), (1, 0)])


def hop_tensor(block, flip):
    return lax.ppermute(block, "tensor", [(i, i ^ flip) for i in range(lax.axis_size("tensor"))])


def hop_mirrored(block, flips):
    size = lax.axis_size("tensor")
    route = [(s * size + i, s * size + (i ^ flips[s])) for s in range(2) for i in range(size)]
    return lax.ppermute(block, ("section", "tensor"), route)


def direct_dp():
    return lax.axis_size("dp") == 4


def dp_order():
    size = lax.axis_size("dp")
    if direct_dp():
        return lax.axis_index("dp") ^ jnp.arange(size, dtype=jnp.int32)
    return jnp.arange(size, dtype=jnp.int32)


def gather_dp(block):
    if direct_dp():
        others = [
            lax.ppermute(block, "dp", [(i, i ^ k) for i in range(4)]) for k in range(1, 4)
        ]
        return jnp.stack([block] + others)
    return lax.all_gather(block, "dp", axis=0, tiled=False)


def scatter_dp(slots):
    if direct_dp():
        total = slots[0].astype(F32)
        for k in range(1, 4):
            got = lax.ppermute(slots[k], "dp", [(i, i ^ k) for i in range(4)])
            total = total + got.astype(F32)
        return total
    return lax.psum_scatter(slots, "dp", scatter_dimension=0, tiled=False).astype(F32)


def add_low(left, right):
    return (left.astype(F32) + right.astype(F32)).astype(BF16)


def gather_tensor(block, first, second):
    near = hop_mirrored(block, first)
    far = hop_mirrored(block, second)
    both = hop_mirrored(near, second)
    return [block, near, far, both]


def scatter_tensor(slots, first, second):
    got_own = hop_mirrored(slots[2], second)
    got_near = hop_mirrored(slots[3], second)
    own = add_low(slots[0], got_own)
    near = add_low(slots[1], got_near)
    return add_low(own, hop_mirrored(near, first))


PLAIN = ((1, 1), (2, 2))
CROSS = ((2, 2), (1, 1))
MIRROR = ((1, 2), (2, 1))


VMEM_LIMIT = 48 * 1024 * 1024
CHUNK = 128


def params():
    return pltpu.CompilerParams(vmem_limit_bytes=VMEM_LIMIT)


ANY = pl.BlockSpec(memory_space=pl.ANY)
VM = pl.BlockSpec(memory_space=pltpu.VMEM)
SM = pl.BlockSpec(memory_space=pltpu.SMEM)


def sds(shape, dtype):
    return jax.ShapeDtypeStruct(shape, dtype)


def chunks(length, step=CHUNK):
    return [slice(i, i + step) for i in range(0, length, step)]


def norm_rows(z):
    centre = z - jnp.mean(z, -1, keepdims=True)
    spread = jnp.mean(centre * centre, -1, keepdims=True)
    scale = lax.rsqrt(spread + 1e-05)
    return centre * scale, scale


def norm_back_rows(d_out, gain, xhat, scale):
    g = d_out * gain
    m1 = jnp.mean(g, -1, keepdims=True)
    m2 = jnp.mean(g * xhat, -1, keepdims=True)
    return scale * (g - m1 - xhat * m2)


def gelu_parts(x):
    e = jnp.exp(-0.5 * x * x)
    t = 1.0 / (1.0 + 0.2316418882 * jnp.abs(x))
    poly = t * (
        0.127414796 + t * (-0.142248368 + t * (0.7107068705 + t * (-0.7265760135 + t * 0.5307027145)))
    )
    tail = poly * e
    cdf = jnp.where(x < 0.0, tail, 1.0 - tail)
    return x * cdf, cdf + x * e * 0.3989422804014327


class Weights:
    def __init__(self, sems):
        self.sems = sems
        self.count = 0

    def copy(self, src, dst):
        made = pltpu.make_async_copy(src, dst, self.sems.at[self.count])
        self.count += 1
        return made


def zrows(meta, k, rz):
    return pl.ds(pl.multiple_of(meta[1 + k], 64), rz)


def load_a(meta, s, got, w_qk, w_vo, sems, nz, rz):
    core = meta[0]
    group = Weights(sems)
    waits = []
    for j in range(2):
        for k in range(nz):
            rows = zrows(meta, k, rz)
            for side, dst in ((0, w_qk), (1, w_vo)):
                to = dst.at[j, rows, :]
                mine = group.copy(s[j + 2 * side].at[k], to)
                group.count -= 1
                other = group.copy(got.at[j, k], to)

                @pl.when(core == side)
                def _():
                    mine.start()

                @pl.when(core != side)
                def _():
                    other.start()

                waits.append(mine)
    return waits


def load_b(meta, s, w_in, w_out, sems, nz, rz):
    group = Weights(sems)
    first, second = [], []
    for dst, side, waits in ((w_in, 0, first), (w_out, 1, second)):
        for j in range(4):
            width = s[j].shape[2] // 2
            for k in range(nz):
                made = group.copy(
                    s[j].at[k, :, pl.ds(side * width, width)],
                    dst.at[zrows(meta, k, rz), pl.ds(j * width, width)],
                )
                made.start()
                waits.append(made)
    return first, second


def wait_all(waits):
    for made in waits:
        made.wait()


def attn_forward(level, meta, x_or_mid, parts, norms, a_slots, got, bias, seg_col, seg_row):
    nz, rz, two = a_slots[0].shape
    length, width = x_or_mid.shape
    cols = two // 2
    heads = 2 * cols // HD
    step = 256

    def body(meta, *refs):
        refs = list(refs)
        src = refs.pop(0)
        if level:
            own, other, gain, shift = (refs.pop(0) for _ in range(4))
        s = [refs.pop(0) for _ in range(4)]
        got, bias_qk, bias_v, sc, sr = (refs.pop(0) for _ in range(5))
        part_out, qk_out, v_out, probs_out, ctx_out = (refs.pop(0) for _ in range(5))
        if level:
            x_out, xhat_out, scale_out = (refs.pop(0) for _ in range(3))
        w_qk, w_vo, sems = refs
        waits = load_a(meta, s, got, w_qk, w_vo, sems, nz, rz)
        if level:
            for rows in chunks(length):
                z = src[rows, :] + (own[rows, :].astype(F32) + other[rows, :].astype(F32)) + shift[2:3, :]
                xhat, scale = norm_rows(z)
                x_out[rows, :] = (xhat * gain[1:2, :] + shift[3:4, :]).astype(BF16)
                xhat_out[rows, :] = xhat.astype(BF16)
                scale_out[rows, :] = scale
            x_ref = x_out
        else:
            x_ref = src
        wait_all(waits)
        for j in range(2):
            for rows in chunks(length, 256):
                x = x_ref[rows, :]
                qk_out[rows, j * two : (j + 1) * two] = (
                    nn(x, w_qk[j]) + bias_qk[:, j * two : (j + 1) * two]
                ).astype(BF16)
                v_out[rows, j * cols : (j + 1) * cols] = (
                    nn(x, w_vo[j, :, :cols]) + bias_v[:, j * cols : (j + 1) * cols]
                ).astype(BF16)
        v_t = v_out[...].astype(F32).T.astype(BF16)
        for queries in chunks(length, step):
            same = sc[...] == sr[:, queries]
            outs = []
            for h in range(heads):
                j, i = divmod(h, cols // HD)
                at = j * two + i * HD
                q = qk_out[queries, at : at + HD]
                k = qk_out[:, at + cols : at + cols + HD]
                st = jnp.where(same, nt(k, q) * 0.125, -1e30)
                p = jnp.exp(st - jnp.max(st, 0, keepdims=True))
                p = (p * (1.0 / jnp.sum(p, 0, keepdims=True))).astype(BF16)
                probs_out[h, :, queries] = p
                outs.append(nn(v_t[h * HD : (h + 1) * HD], p))
            ctx = jnp.concatenate(outs, 0).T.astype(BF16)
            ctx_out[queries, :] = ctx
            part_out[queries, :] = (
                nt(ctx[:, :cols], w_vo[0, :, cols:]) + nt(ctx[:, cols:], w_vo[1, :, cols:])
            ).astype(BF16)

    outs = [
        sds((length, width), BF16), sds((length, 2 * two), BF16), sds((length, two), BF16),
        sds((heads, length, length), BF16), sds((length, two), BF16),
    ]
    args = [meta, x_or_mid]
    if level:
        args += [*parts, *norms]
        outs += [sds((length, width), BF16), sds((length, width), BF16), sds((length, 1), F32)]
    specs = [SM] + [VM] * (len(args) - 1) + [ANY] * 5 + [VM] * 4
    args += [*a_slots, got, *bias, seg_col, seg_row]
    return pl.pallas_call(
        body,
        out_shape=outs,
        in_specs=specs,
        out_specs=[VM] * len(outs),
        scratch_shapes=[
            pltpu.VMEM((2, width, two), BF16), pltpu.VMEM((2, width, two), BF16),
            pltpu.SemaphoreType.DMA((4 * nz,)),
        ],
        compiler_params=params(),
        name="attn_forward",
    )(*args)


def ffn_forward(meta, x, parts, gains, shifts, b_slots, bias_in):
    nz, rz, two = b_slots[0].shape
    length, width = x.shape
    units = 2 * two

    def body(meta, x, own, other, gain, shift, s0, s1, s2, s3, bias,
             part_out, mid_out, xhat_out, scale_out, act_out, slope_out, w_i, w_f, low, sems):
        first, second = load_b(meta, (s0, s1, s2, s3), w_i, w_f, sems, nz, rz)
        for rows in chunks(length):
            z = x[rows, :].astype(F32) + (own[rows, :].astype(F32) + other[rows, :].astype(F32)) + shift[0:1, :]
            xhat, scale = norm_rows(z)
            mid = xhat * gain[0:1, :] + shift[1:2, :]
            mid_out[rows, :] = mid
            low[rows, :] = mid.astype(BF16)
            xhat_out[rows, :] = xhat.astype(BF16)
            scale_out[rows, :] = scale
        wait_all(first)
        for rows in chunks(length, 256):
            for c in chunks(units, 512):
                pre = nn(low[rows, :], w_i[:, c]) + bias[:, c]
                act, slope = gelu_parts(pre)
                act_out[rows, c] = act.astype(BF16)
                slope_out[rows, c] = slope.astype(BF16)
        wait_all(second)
        for rows in chunks(length, 256):
            part_out[rows, :] = nt(act_out[rows, :], w_f[...]).astype(BF16)

    return pl.pallas_call(
        body,
        out_shape=[
            sds((length, width), BF16), sds((length, width), F32), sds((length, width), BF16),
            sds((length, 1), F32), sds((length, units), BF16), sds((length, units), BF16),
        ],
        in_specs=[SM] + [VM] * 5 + [ANY] * 4 + [VM],
        out_specs=[VM] * 6,
        scratch_shapes=[
            pltpu.VMEM((width, units), BF16), pltpu.VMEM((width, units), BF16),
            pltpu.VMEM((length, width), BF16), pltpu.SemaphoreType.DMA((8 * nz,)),
        ],
        compiler_params=params(),
        name="ffn_forward",
    )(meta, x, *parts, gains, shifts, *b_slots, bias_in)


def last_norm(mid, parts, gains, shifts, tok_row, cls_pos):
    length, width = mid.shape
    n_cls = cls_pos.shape[0]

    def body(cls, mid, own, other, gain, shift, tok, y_out, xhat_out, scale_out, cls_out):
        for rows in chunks(length):
            z = mid[rows, :] + (own[rows, :].astype(F32) + other[rows, :].astype(F32)) + shift[2:3, :]
            xhat, scale = norm_rows(z)
            y_out[rows, :] = (xhat * gain[1:2, :] + shift[3:4, :]).astype(BF16)
            xhat_out[rows, :] = xhat.astype(BF16)
            scale_out[rows, :] = scale
        which = lax.broadcasted_iota(jnp.int32, (16, length), 0)
        hot = jnp.zeros((16, length), F32)
        for p in range(n_cls):
            hot = jnp.where(jnp.logical_and(which == p, tok[...] == cls[p]), 1.0, hot)
        cls_out[...] = nn(hot.astype(BF16), y_out[...])[:n_cls].astype(BF16)

    return pl.pallas_call(
        body,
        out_shape=[
            sds((length, width), BF16), sds((length, width), BF16), sds((length, 1), F32),
            sds((n_cls, width), BF16),
        ],
        in_specs=[SM] + [VM] * 6,
        out_specs=[VM] * 4,
        compiler_params=params(),
        name="last_norm",
    )(cls_pos, mid, *parts, gains, shifts, tok_row)


def ffn_backward(level, meta, sources, xhat, scale, gains, slope, b_slots):
    nz, rz, two = b_slots[0].shape
    length, width = xhat.shape
    units = 2 * two
    n_cls = sources[3].shape[0] if level else 0

    def body(meta, *refs):
        refs = list(refs)
        if level:
            cls, grad, d_cls, tok = (refs.pop(0) for _ in range(4))
        else:
            d_above, own, other = (refs.pop(0) for _ in range(3))
        xhat, scale, gain, slope, s0, s1, s2, s3 = (refs.pop(0) for _ in range(8))
        part_out, second_out, low_out, pre_out, vec_out, inb_out, w_i, w_f, sems = refs
        first, second = load_b(meta, (s0, s1, s2, s3), w_i, w_f, sems, nz, rz)
        sums = [jnp.zeros((1, width), F32) for _ in range(3)]
        for rows in chunks(length):
            if level:
                d_out = grad[rows, :].astype(F32)
                for p in range(n_cls):
                    d_out = d_out + jnp.where(tok[rows, :] == cls[p], 1.0, 0.0) * d_cls[p : p + 1, :]
            else:
                d_out = d_above[rows, :] + (own[rows, :].astype(F32) + other[rows, :].astype(F32))
                d_out = d_out.astype(BF16).astype(F32)
            hat = xhat[rows, :].astype(F32)
            d_second = norm_back_rows(d_out, gain[1:2, :], hat, scale[rows, :])
            second_out[rows, :] = d_second
            low_out[rows, :] = d_second.astype(BF16)
            for n, item in enumerate((d_out * hat, d_out, d_second)):
                sums[n] = sums[n] + jnp.sum(item, 0, keepdims=True)
        for n in range(3):
            vec_out[n : n + 1, :] = sums[n]
        wait_all(second)
        for n, rows in enumerate(chunks(length, 256)):
            for c in chunks(units, 512):
                d_act = nn(low_out[rows, :], w_f[:, c])
                d_pre = (slope[rows, c].astype(F32) * d_act).astype(BF16)
                pre_out[rows, c] = d_pre
                total = jnp.sum(d_pre.astype(F32), 0, keepdims=True)
                inb_out[:, c] = total if n == 0 else inb_out[:, c] + total
        wait_all(first)
        for rows in chunks(length, 256):
            part_out[rows, :] = nt(pre_out[rows, :], w_i[...]).astype(BF16)

    if level:
        token_grad, d_cls, tok_col, cls_pos = sources
        args, specs = [meta, cls_pos, token_grad, d_cls, tok_col], [SM, SM, VM, VM, VM]
    else:
        args, specs = [meta, *sources], [SM, VM, VM, VM]
    args += [xhat, scale, gains, slope, *b_slots]
    specs += [VM] * 4 + [ANY] * 4
    return pl.pallas_call(
        body,
        out_shape=[
            sds((length, width), BF16), sds((length, width), F32), sds((length, width), BF16),
            sds((length, units), BF16), sds((3, width), F32), sds((1, units), F32),
        ],
        in_specs=specs,
        out_specs=[VM] * 6,
        scratch_shapes=[
            pltpu.VMEM((width, units), BF16), pltpu.VMEM((width, units), BF16),
            pltpu.SemaphoreType.DMA((8 * nz,)),
        ],
        compiler_params=params(),
        name="ffn_backward",
    )(*args)


def ffn_grads(meta, mid, d_pre, d_ffn, act, nz, which):
    length, width = mid.shape
    units = d_pre.shape[1]
    two = units // 2
    one = units // 4
    rz = width // nz

    def body(meta, mid, d_pre, d_ffn, act, *refs):
        outs, (mid_t, ffn_t) = refs[: len(which)], refs[len(which) :]
        mid_t[...] = mid[...].T.astype(BF16)
        ffn_t[...] = d_ffn[...].astype(F32).T.astype(BF16)
        for out, j in zip(outs, which):
            c = slice(j * one, (j + 1) * one)
            for k in range(nz):
                rows = zrows(meta, k, rz)
                out[k, :, :one] = nn(mid_t[rows, :], d_pre[:, c]).astype(BF16)
                out[k, :, one:] = nn(ffn_t[rows, :], act[:, c]).astype(BF16)

    return pl.pallas_call(
        body,
        out_shape=[sds((nz, rz, two), BF16)] * len(which),
        in_specs=[SM] + [VM] * 4,
        out_specs=[VM] * len(which),
        scratch_shapes=[pltpu.VMEM((width, length), BF16)] * 2,
        compiler_params=params(),
        name="ffn_grads",
    )(meta, mid, d_pre, d_ffn, act)


def attn_backward(meta, d_second, parts, xhat, scale, gains, qk, v, probs, a_slots, got):
    nz, rz, two = a_slots[0].shape
    length, width = d_second.shape
    cols = two // 2
    heads = 2 * cols // HD

    def body(meta, d_second, own, other, xhat, scale, gain, qk, v, probs, s0, s1, s2, s3, got,
             part_out, first_out, low_out, dqk_out, dv_out, vec_out, sum_qk, sum_v,
             w_qk, w_vo, d_ctx, acc_v, acc_k, sems):
        waits = load_a(meta, (s0, s1, s2, s3), got, w_qk, w_vo, sems, nz, rz)
        sums = [jnp.zeros((1, width), F32) for _ in range(3)]
        for rows in chunks(length):
            d_mid = d_second[rows, :] + (own[rows, :].astype(F32) + other[rows, :].astype(F32))
            hat = xhat[rows, :].astype(F32)
            d_first = norm_back_rows(d_mid, gain[0:1, :], hat, scale[rows, :])
            first_out[rows, :] = d_first
            low_out[rows, :] = d_first.astype(BF16)
            for n, item in enumerate((d_mid * hat, d_mid, d_first)):
                sums[n] = sums[n] + jnp.sum(item, 0, keepdims=True)
        for n in range(3):
            vec_out[n : n + 1, :] = sums[n]
        wait_all(waits)
        for j in range(2):
            for rows in chunks(length, 256):
                d_ctx[rows, j * cols : (j + 1) * cols] = nn(low_out[rows, :], w_vo[j, :, cols:]).astype(BF16)
        k_t = jnp.concatenate(
            [qk[:, j * two + cols : (j + 1) * two] for j in range(2)], 1
        ).astype(F32).T.astype(BF16)
        for h in range(heads):
            j, i = divmod(h, cols // HD)
            at = j * two + i * HD
            q_cols, k_cols, v_cols = (
                slice(at, at + HD), slice(at + cols, at + cols + HD), slice(h * HD, (h + 1) * HD),
            )
            for n, queries in enumerate(chunks(length, 256)):
                d_o = d_ctx[queries, v_cols]
                d_p = nt(v[:, v_cols], d_o)
                p = probs[h, :, queries]
                wide = p.astype(F32)
                d_s = (wide * (d_p - jnp.sum(wide * d_p, 0, keepdims=True))).astype(BF16)
                d_v = nn(p, d_o)
                d_k = nn(d_s, qk[queries, q_cols])
                acc_v[...] = d_v if n == 0 else acc_v[...] + d_v
                acc_k[...] = d_k if n == 0 else acc_k[...] + d_k
                d_q = nn(k_t[h * HD : (h + 1) * HD], d_s)
                dqk_out[queries, q_cols] = (d_q.T * 0.125).astype(BF16)
            dv_out[:, v_cols] = acc_v[...].astype(BF16)
            dqk_out[:, k_cols] = (acc_k[...] * 0.125).astype(BF16)
        sum_qk[...] = jnp.sum(dqk_out[...].astype(F32), 0, keepdims=True)
        sum_v[...] = jnp.sum(dv_out[...].astype(F32), 0, keepdims=True)
        for rows in chunks(length, 256):
            part_out[rows, :] = (
                nt(dqk_out[rows, :two], w_qk[0]) + nt(dqk_out[rows, two:], w_qk[1])
                + nt(dv_out[rows, :cols], w_vo[0, :, :cols]) + nt(dv_out[rows, cols:], w_vo[1, :, :cols])
            ).astype(BF16)

    return pl.pallas_call(
        body,
        out_shape=[
            sds((length, width), BF16), sds((length, width), F32), sds((length, width), BF16),
            sds((length, 2 * two), BF16), sds((length, two), BF16), sds((3, width), F32),
            sds((1, 2 * two), F32), sds((1, two), F32),
        ],
        in_specs=[SM] + [VM] * 9 + [ANY] * 5,
        out_specs=[VM] * 8,
        scratch_shapes=[
            pltpu.VMEM((2, width, two), BF16), pltpu.VMEM((2, width, two), BF16),
            pltpu.VMEM((length, two), BF16), pltpu.VMEM((length, HD), F32), pltpu.VMEM((length, HD), F32),
            pltpu.SemaphoreType.DMA((4 * nz,)),
        ],
        compiler_params=params(),
        name="attn_backward",
    )(meta, d_second, *parts, xhat, scale, gains, qk, v, probs, *a_slots, got)


def attn_grads(meta, x, d_attn, d_qk, d_v, ctx, nz):
    length, width = x.shape
    two = d_v.shape[1]
    cols = two // 2
    rz = width // nz

    def body(meta, x, d_attn, d_qk, d_v, ctx, keep, send, x_t, a_t):
        x_t[...] = x[...].astype(F32).T.astype(BF16)
        a_t[...] = d_attn[...].astype(F32).T.astype(BF16)

        def fill(qk_out, vo_out):
            for j in range(2):
                for k in range(nz):
                    rows = zrows(meta, k, rz)
                    c = slice(j * cols, (j + 1) * cols)
                    qk_out[j, k] = nn(x_t[rows, :], d_qk[:, j * two : (j + 1) * two]).astype(BF16)
                    vo_out[j, k, :, :cols] = nn(x_t[rows, :], d_v[:, c]).astype(BF16)
                    vo_out[j, k, :, cols:] = nn(a_t[rows, :], ctx[:, c]).astype(BF16)

        @pl.when(meta[0] == 0)
        def _():
            fill(keep, send)

        @pl.when(meta[0] != 0)
        def _():
            fill(send, keep)

    return pl.pallas_call(
        body,
        out_shape=[sds((2, nz, rz, two), BF16)] * 2,
        in_specs=[SM] + [VM] * 5,
        out_specs=[VM] * 2,
        scratch_shapes=[pltpu.VMEM((width, length), BF16)] * 2,
        compiler_params=params(),
        name="attn_grads",
    )(meta, x, d_attn, d_qk, d_v, ctx)


def loss_kernel(own, passages, queries, positive_col, own_row):
    n_q, width = queries.shape
    n_p = passages.shape[0]
    n_own = own_row

    def body(own, passages, queries, pos, loss_out, d_out):
        logits = nt(queries[...], passages[...])
        top = jnp.max(logits, -1, keepdims=True)
        log_total = top + jnp.log(jnp.sum(jnp.exp(logits - top), -1, keepdims=True))
        index = lax.broadcasted_iota(jnp.int32, (n_q, n_p), 1)
        hits = pos[...] == index
        chosen = jnp.sum(jnp.where(hits, logits, 0.0), -1, keepdims=True)
        loss_out[...] = jnp.sum(log_total - chosen, 0, keepdims=True) / n_q
        d_logits = (16.0 * (jnp.exp(logits - log_total) - jnp.where(hits, 1.0, 0.0))).astype(BF16)
        pick = jnp.where(
            lax.broadcasted_iota(jnp.int32, (n_p, 128), 0)
            == lax.broadcasted_iota(jnp.int32, (n_p, 128), 1) + own[0],
            1.0, 0.0,
        ).astype(BF16)
        cols = nn(d_logits, pick)
        d_out[...] = nn(cols.T.astype(BF16), queries[...])[:n_own]

    return pl.pallas_call(
        body,
        out_shape=[sds((1, 1), F32), sds((n_own, width), F32)],
        in_specs=[SM] + [VM] * 3,
        out_specs=[VM] * 2,
        compiler_params=params(),
        name="contrast",
    )(own, passages, queries, positive_col)


def after(block, *earlier):
    return lax.optimization_barrier((block, *earlier))[0]


def pad_flat(flat):
    size = -(-flat.shape[0] // 2048) * 2048
    return jnp.pad(flat, (0, size - flat.shape[0])).reshape(-1, 128)


def on_device(
    inputs, cls_pos, w_qkv, qv_bias, w_out, w_in, in_bias, w_ffn_out,
    layer_gains, shifts, queries, positive, token_grad,
):
    core = lax.axis_index("section")
    dp = lax.axis_index("dp")
    me = lax.axis_index("tensor")
    n_dp = lax.axis_size("dp")
    n_t = lax.axis_size("tensor")
    first_core = core == 0
    rows_dev, share, width = inputs.shape
    rows = w_qkv.shape[1]
    cols = w_qkv.shape[3]
    half = w_in.shape[2] // 2
    units = in_bias.shape[2]
    length = n_t * share
    n_chips = n_dp * n_t
    piece = width // n_chips
    order = dp_order()
    direct = direct_dp()
    t_ids = jnp.arange(n_t, dtype=jnp.int32)

    out_t = w_out[0].T
    ffn_t = w_ffn_out[0].T
    pack_a = [
        jnp.concatenate([w_qkv[0, :, 0], w_qkv[0, :, 1]], 1),
        jnp.concatenate([w_qkv[0, :, 2], out_t], 1),
    ]
    pack_b = [
        jnp.concatenate([w_in[0, :, c * half : (c + 1) * half], ffn_t[:, c * half : (c + 1) * half]], 1)
        for c in range(2)
    ]
    vec = jnp.concatenate(
        [layer_gains.reshape(-1), shifts.reshape(-1), qv_bias.reshape(-1), in_bias.reshape(-1)]
    )
    n_vec = vec.shape[0]

    def by_layer(pack):
        got = swap_cores(jnp.where(first_core, pack[1], pack[0]))
        return [jnp.where(first_core, pack[0], got), jnp.where(first_core, got, pack[1])]

    shard_a = by_layer(pack_a)
    shard_b = by_layer(pack_b)
    got = swap_cores(vec)
    message = pad_flat(
        jnp.concatenate(
            [
                jnp.where(first_core, vec, got), jnp.where(first_core, got, vec),
                queries.reshape(-1), (positive // 16).astype(BF16), (positive % 16).astype(BF16),
            ]
        )
    )

    def spread_rows(block):
        parts = [lax.dynamic_index_in_dim(block, me ^ k, 0, keepdims=False) for k in range(n_t)]
        return jnp.concatenate([parts[0]] + [hop_tensor(parts[k], k) for k in range(1, n_t)], 0)

    positions = jnp.concatenate(
        [(me ^ k) * share + jnp.arange(share, dtype=jnp.int32) for k in range(n_t)]
    )
    cls_row = lax.dynamic_index_in_dim(cls_pos, me, 0, keepdims=False)
    segments = jnp.sum((positions[:, None] >= cls_row[None, :]).astype(jnp.int32), -1)
    seg_col, seg_row = segments[:, None], segments[None, :]
    tok_col, tok_row = positions[:, None], positions[None, :]
    zrow = order * rows if direct else jnp.zeros((1,), jnp.int32)
    meta = jnp.concatenate([core[None].astype(jnp.int32), zrow])

    def whole(slots):
        if direct:
            return slots
        return [s.reshape(1, width, -1) for s in slots]

    a_plan = (PLAIN, CROSS)
    a_flips = [jnp.array(flips, jnp.int32) for flips in ((0, 1, 2, 3), (0, 2, 1, 3))]

    def exchange_a(slots):
        return swap_cores(
            jnp.where(first_core, jnp.stack(slots[2:]), jnp.stack(slots[:2]))
        )

    z_a0 = gather_dp(shard_a[0])
    z_vec = gather_dp(message)
    x_low = spread_rows(inputs)
    z_b0 = gather_dp(after(shard_b[0], z_a0))
    a0 = whole(gather_tensor(z_a0, *a_plan[0]))
    got_a0 = exchange_a(a0)
    z_a1 = gather_dp(after(shard_a[1], z_b0))
    b0 = whole(gather_tensor(after(z_b0, a0[3]), *MIRROR))
    z_b1 = gather_dp(after(shard_b[1], z_a1))
    a1 = whole(gather_tensor(after(z_a1, b0[3]), *a_plan[1]))
    got_a1 = exchange_a(a1)
    b1 = whole(gather_tensor(after(z_b1, a1[3]), *MIRROR))
    slots_a, slots_b, gots = (a0, a1), (b0, b1), (got_a0, got_a1)

    slot_ids = (order[None, :] * n_t + (me ^ t_ids)[:, None]).reshape(-1)
    to_natural = (jnp.arange(n_chips, dtype=jnp.int32)[:, None] == slot_ids[None, :]).astype(BF16)
    table = nn(to_natural, jnp.stack(gather_tensor(z_vec, *PLAIN)).reshape(n_chips, -1))
    n_gain, n_shift, n_qv, n_inb = layer_gains.size, shifts.size, qv_bias.size, units

    def read_vectors(vecs):
        at = 0
        gains = vecs[:, at : at + n_gain].reshape(n_chips, 2, piece).transpose(1, 0, 2).reshape(2, width)
        at += n_gain
        shift = vecs[:, at : at + n_shift].reshape(n_chips, 4, piece).transpose(1, 0, 2).reshape(4, width)
        at += n_shift
        qv = vecs[:, at : at + n_qv].reshape(n_dp, n_t, 2, cols // n_dp).transpose(2, 1, 0, 3).reshape(2, n_t, cols)
        at += n_qv
        inb = vecs[:, at : at + n_inb].reshape(n_dp, n_t, units).transpose(1, 0, 2).reshape(n_t, 2 * half)
        return gains, shift, qv, inb

    head_slots = [me ^ lax.dynamic_slice_in_dim(flips, 2 * core, 2) for flips in a_flips]
    unit_slots = me ^ jnp.where(first_core, a_flips[0], a_flips[1])

    def pick(values, slots):
        hot = (slots[:, None] == t_ids[None, :]).astype(F32)
        return jnp.sum(hot[:, :, None] * values[None], 1)

    vectors = []
    for level in range(2):
        gains, shift, qv, inb = read_vectors(table[:, level * n_vec : (level + 1) * n_vec])
        bias_q, bias_v = pick(qv[0], head_slots[level]), pick(qv[1], head_slots[level])
        bias_qk = jnp.concatenate([bias_q, jnp.zeros_like(bias_q)], 1).reshape(1, -1)
        bias_in = pick(lax.dynamic_slice_in_dim(inb, core * half, half, 1), unit_slots).reshape(1, -1)
        vectors.append((gains, shift, (bias_qk, bias_v.reshape(1, -1)), bias_in))
    at = 2 * n_vec
    q_dev = queries.shape[0]
    all_q = table[:, at : at + q_dev * width].reshape(-1, width).astype(BF16)
    at += q_dev * width
    all_pos = table[:, at : at + q_dev] * 16.0 + table[:, at + q_dev : at + 2 * q_dev]
    all_pos = all_pos.astype(jnp.int32).reshape(-1, 1)

    saved = []
    source, parts, norms = x_low, None, None
    for level in range(2):
        gains, shift, biases, bias_in = vectors[level]
        outs = attn_forward(
            level, meta, source, parts, norms, slots_a[level], gots[level], biases, seg_col, seg_row
        )
        part, qk, v, probs, ctx = outs[:5]
        if level:
            x, xhat2, scale2 = outs[5:]
            saved[0]["second"] = (xhat2, scale2)
        else:
            x = x_low
        part, mid, xhat1, scale1, act, slope = ffn_forward(
            meta, x, (part, swap_cores(part)), gains, shift, slots_b[level], bias_in
        )
        saved.append(
            dict(x=x, qk=qk, v=v, probs=probs, ctx=ctx, mid=mid, xhat1=xhat1, scale1=scale1, act=act, slope=slope)
        )
        source, parts, norms = mid, (part, swap_cores(part)), (gains, shift)
    y, xhat2, scale2, cls_own = last_norm(source, parts, *norms, tok_row, cls_row)
    saved[1]["second"] = (xhat2, scale2)

    n_cls = cls_row.shape[0]
    cls_slots = jnp.stack(gather_tensor(gather_dp(cls_own), *PLAIN))
    passages = nn(to_natural, cls_slots.reshape(n_chips, -1)).astype(BF16).reshape(-1, width)
    first_own = ((dp * n_t + me) * n_cls).astype(jnp.int32)[None]
    mean_loss, d_cls = loss_kernel(first_own, passages, all_q, all_pos, n_cls)

    def send_rows(block, section):
        out = jnp.zeros((n_t, share, width), F32)
        low = block.astype(BF16).reshape(n_t, share, width)
        out = lax.dynamic_update_index_in_dim(out, block[:share].astype(F32), me, 0)
        for k in range(1, n_t):
            route = [(section * n_t + i, section * n_t + (i ^ k)) for i in range(n_t)]
            got = lax.ppermute(low[k], ("section", "tensor"), route)
            out = lax.dynamic_update_index_in_dim(out, got.astype(F32), me ^ k, 0)
        return out

    y_rows = send_rows(y, 1)

    totals = [None, None]
    vector_rows = [None, None]
    sources = (spread_rows(token_grad), d_cls, tok_col, cls_row)
    for level in (1, 0):
        gains, shift, _, _ = vectors[level]
        kept = saved[level]
        xhat2, scale2 = kept["second"]
        part, d_second, d_ffn, d_pre, vec2, sum_inb = ffn_backward(
            level, meta, sources, xhat2, scale2, gains, kept["slope"], slots_b[level]
        )
        other = swap_cores(part)
        nz = 4 if direct else 1
        far = ffn_grads(meta, kept["mid"], d_pre, d_ffn, kept["act"], nz, (2, 3))
        near = ffn_grads(meta, kept["mid"], d_pre, d_ffn, kept["act"], nz, (0, 1))
        grads_b = [*near, *far]
        outs = attn_backward(
            meta, d_second, (part, other), kept["xhat1"], kept["scale1"], gains,
            kept["qk"], kept["v"], kept["probs"], slots_a[level], gots[level],
        )
        part, d_first, d_attn, d_qk, d_v, vec1, sum_qk, sum_v = outs
        other = swap_cores(part)
        keep, send = attn_grads(meta, kept["x"], d_attn, d_qk, d_v, kept["ctx"], nz)
        got = swap_cores(send)
        grads_a = [jnp.where(first_core, keep[j], got[j]) for j in range(2)]
        grads_a += [jnp.where(first_core, got[j], keep[j]) for j in range(2)]
        if not direct:
            grads_a = [g.reshape(n_dp, rows, -1) for g in grads_a]
            grads_b = [g.reshape(n_dp, rows, -1) for g in grads_b]
        tot_b = scatter_dp(scatter_tensor(grads_b, *MIRROR)).astype(BF16)
        tot_a = scatter_dp(scatter_tensor(grads_a, *a_plan[level])).astype(BF16)
        route = [(1 - level, level)]
        totals[level] = (
            tot_a, lax.ppermute(tot_a, "section", route),
            tot_b, lax.ppermute(tot_b, "section", route),
        )
        vector_rows[level] = (vec1, vec2, sum_qk, sum_v, sum_inb)
        sources = (d_first, part, other)
    d_hidden = d_first + (part.astype(F32) + other.astype(F32))

    def vector_table(level):
        vec1, vec2, sum_qk, sum_v, sum_inb = vector_rows[level]
        gs = jnp.concatenate([vec1[0:1], vec2[0:1], vec1[2:3], vec1[1:2], vec2[2:3], vec2[1:2]])
        gs = jnp.where(first_core, gs, 0.0).reshape(6, n_chips, piece).transpose(1, 0, 2).reshape(n_chips, -1)
        qv = jnp.stack([sum_qk.reshape(2, 2 * cols)[:, :cols], sum_v.reshape(2, cols)], 1)
        hot = (head_slots[level][:, None] == t_ids[None, :]).astype(F32)
        qv = jnp.sum(hot[:, None, :, None] * qv[:, :, None, :], 0)
        qv = qv.reshape(2, n_t, n_dp, -1).transpose(2, 1, 0, 3).reshape(n_chips, -1)
        hot = (unit_slots[:, None] == t_ids[None, :]).astype(F32)
        inb = jnp.sum(hot[:, :, None] * sum_inb.reshape(n_t, 1, half), 0)
        inb = jnp.where((jnp.arange(2) == core)[None, :, None], inb[:, None, :], 0.0)
        inb = inb.reshape(n_t, n_dp, units).transpose(1, 0, 2).reshape(n_chips, -1)
        return jnp.concatenate([gs, qv, inb], 1)

    flat = jnp.concatenate([vector_table(0), vector_table(1)], 1)
    flat = lax.dot_general(
        to_natural.astype(F32), flat, (((0,), (0,)), ((), ())), precision=lax.Precision.HIGHEST
    )
    flat = jnp.pad(flat, ((0, 0), (0, -flat.shape[1] % 1024))).reshape(n_t, n_dp, -1, 128)
    got = hop_tensor(flat[2:], 2)
    flat = flat[:2] + got
    flat = flat[0] + hop_tensor(flat[1], 1)
    if direct:
        flat = flat[0] + sum(
            lax.ppermute(flat[k], "dp", [(i, i ^ k) for i in range(4)]) for k in range(1, 4)
        )
    else:
        flat = lax.psum_scatter(flat, "dp", scatter_dimension=0, tiled=False)
    flat = (flat + swap_cores(flat)).reshape(-1)
    flat = jnp.where(first_core, flat[:n_vec], flat[n_vec : 2 * n_vec])
    at = 0
    grad_gains = flat[at : at + n_gain].reshape(layer_gains.shape)
    at += n_gain
    grad_shifts = flat[at : at + n_shift].reshape(shifts.shape)
    at += n_shift
    grad_qv = flat[at : at + n_qv].reshape(qv_bias.shape)
    at += n_qv
    grad_inb = flat[at : at + n_inb].reshape(in_bias.shape)

    own_a, got_a, own_b, got_b = (
        jnp.where(first_core, left, right).astype(F32) for left, right in zip(*totals)
    )
    halves_a = (jnp.where(first_core, own_a, got_a), jnp.where(first_core, got_a, own_a))
    halves_b = (jnp.where(first_core, own_b, got_b), jnp.where(first_core, got_b, own_b))
    grad_qkv = jnp.stack(
        [halves_a[0][:, :cols], halves_a[0][:, cols:], halves_a[1][:, :cols]], 1
    )[None]
    grad_out = halves_a[1][:, cols:].T[None]
    grad_in = jnp.concatenate([h[:, :half] for h in halves_b], 1)[None]
    grad_ffn = jnp.concatenate([h[:, half:] for h in halves_b], 1).T[None]
    boundary = jnp.where(first_core, send_rows(d_hidden, 0), y_rows)[None]
    return (
        grad_qkv, grad_qv, grad_out, grad_in, grad_inb, grad_ffn,
        grad_gains, grad_shifts, boundary, mean_loss.reshape(()),
    )


def solution(mesh):
    return jax.shard_map(
        on_device,
        mesh=mesh,
        in_specs=(
            P("dp", "tensor", None),
            P("dp", None),
            P("section", "dp", None, "tensor"),
            P("section", None, "tensor", "dp"),
            P("section", "tensor", "dp"),
            P("section", "dp", "tensor"),
            P("section", "tensor", "dp"),
            P("section", "tensor", "dp"),
            P("section", None, ("dp", "tensor")),
            P("section", None, ("dp", "tensor")),
            P(("dp", "tensor"), None),
            P(("dp", "tensor")),
            P("dp", "tensor", None),
        ),
        out_specs=(
            P("section", "dp", None, "tensor"),
            P("section", None, "tensor", "dp"),
            P("section", "tensor", "dp"),
            P("section", "dp", "tensor"),
            P("section", "tensor", "dp"),
            P("section", "tensor", "dp"),
            P("section", None, ("dp", "tensor")),
            P("section", None, ("dp", "tensor")),
            P("section", "dp", "tensor", None),
            P(),
        ),
        check_vma=False,
    )
```

```python
import jax
import jax.numpy as jnp
from jax import lax
from jax.experimental import pallas as pl
from jax.experimental.pallas import tpu as pltpu
from jax.sharding import PartitionSpec as P

HD = 64
BF16 = jnp.bfloat16
F32 = jnp.float32


def mm(left, right, dims):
    return lax.dot_general(left, right, (dims, ((), ())), preferred_element_type=F32)


def nn(left, right):
    return mm(left, right, ((1,), (0,)))


def nt(left, right):
    return mm(left, right, ((1,), (1,)))


def tn(left, right):
    return mm(left, right, ((0,), (0,)))


def swap_cores(block):
    return lax.ppermute(block, "section", [(0, 1), (1, 0)])


def hop_tensor(block, flip):
    return lax.ppermute(block, "tensor", [(i, i ^ flip) for i in range(lax.axis_size("tensor"))])


def hop_mirrored(block, flips):
    size = lax.axis_size("tensor")
    route = [(s * size + i, s * size + (i ^ flips[s])) for s in range(2) for i in range(size)]
    return lax.ppermute(block, ("section", "tensor"), route)


def direct_dp():
    return lax.axis_size("dp") == 4


def dp_order():
    size = lax.axis_size("dp")
    if direct_dp():
        return lax.axis_index("dp") ^ jnp.arange(size, dtype=jnp.int32)
    return jnp.arange(size, dtype=jnp.int32)


def gather_dp(block):
    if direct_dp():
        others = [
            lax.ppermute(block, "dp", [(i, i ^ k) for i in range(4)]) for k in range(1, 4)
        ]
        return jnp.stack([block] + others)
    return lax.all_gather(block, "dp", axis=0, tiled=False)


def scatter_dp(slots):
    if direct_dp():
        total = slots[0].astype(F32)
        for k in range(1, 4):
            got = lax.ppermute(slots[k], "dp", [(i, i ^ k) for i in range(4)])
            total = total + got.astype(F32)
        return total
    return lax.psum_scatter(slots, "dp", scatter_dimension=0, tiled=False).astype(F32)


def add_low(left, right):
    return (left.astype(F32) + right.astype(F32)).astype(BF16)


def gather_tensor(block, first, second):
    near = hop_mirrored(block, first)
    far = hop_mirrored(block, second)
    both = hop_mirrored(near, second)
    return [block, near, far, both]


def scatter_first(slots, first, second):
    got_own = hop_mirrored(slots[2], second)
    got_near = hop_mirrored(slots[3], second)
    return add_low(slots[0], got_own), add_low(slots[1], got_near)


def scatter_second(own, near, first, second):
    return add_low(own, hop_mirrored(near, first))


PLAIN = ((1, 1), (2, 2))
CROSS = ((2, 2), (1, 1))
MIRROR = ((1, 2), (2, 1))


VMEM_LIMIT = 48 * 1024 * 1024
CHUNK = 128


def takes(micros):
    return pl.CostEstimate(flops=int(micros * 1.1e9), bytes_accessed=0, transcendentals=0)


def params():
    return pltpu.CompilerParams(vmem_limit_bytes=VMEM_LIMIT)


ANY = pl.BlockSpec(memory_space=pl.ANY)
VM = pl.BlockSpec(memory_space=pltpu.VMEM)
SM = pl.BlockSpec(memory_space=pltpu.SMEM)


def sds(shape, dtype):
    return jax.ShapeDtypeStruct(shape, dtype)


def chunks(length, step=CHUNK):
    return [slice(i, i + step) for i in range(0, length, step)]


def norm_rows(z):
    centre = z - jnp.mean(z, -1, keepdims=True)
    spread = jnp.mean(centre * centre, -1, keepdims=True)
    scale = lax.rsqrt(spread + 1e-05)
    return centre * scale, scale


def norm_back_rows(d_out, gain, xhat, scale):
    g = d_out * gain
    m1 = jnp.mean(g, -1, keepdims=True)
    m2 = jnp.mean(g * xhat, -1, keepdims=True)
    return scale * (g - m1 - xhat * m2)


def gelu_parts(x):
    e = jnp.exp(-0.5 * x * x)
    t = 1.0 / (1.0 + 0.2316418882 * jnp.abs(x))
    poly = t * (
        0.127414796 + t * (-0.142248368 + t * (0.7107068705 + t * (-0.7265760135 + t * 0.5307027145)))
    )
    tail = poly * e
    cdf = jnp.where(x < 0.0, tail, 1.0 - tail)
    return x * cdf, cdf + x * e * 0.3989422804014327


class Weights:
    def __init__(self, sems):
        self.sems = sems
        self.count = 0

    def copy(self, src, dst):
        made = pltpu.make_async_copy(src, dst, self.sems.at[self.count])
        self.count += 1
        return made


def zrows(meta, k, rz):
    return pl.ds(pl.multiple_of(meta[1 + k], 64), rz)


def load_a(meta, s, got, w_qk, w_vo, sems, nz, rz):
    core = meta[0]
    group = Weights(sems)
    waits = []
    for j in range(2):
        for k in range(nz):
            rows = zrows(meta, k, rz)
            for side, dst in ((0, w_qk), (1, w_vo)):
                to = dst.at[j, rows, :]
                mine = group.copy(s[j + 2 * side].at[k], to)
                group.count -= 1
                other = group.copy(got.at[j, k], to)

                @pl.when(core == side)
                def _():
                    mine.start()

                @pl.when(core != side)
                def _():
                    other.start()

                waits.append(mine)
    return waits


def load_b(meta, s, w_in, w_out, sems, nz, rz):
    group = Weights(sems)
    first, second = [], []
    for dst, side, waits in ((w_in, 0, first), (w_out, 1, second)):
        for j in range(4):
            width = s[j].shape[2] // 2
            for k in range(nz):
                made = group.copy(
                    s[j].at[k, :, pl.ds(side * width, width)],
                    dst.at[zrows(meta, k, rz), pl.ds(j * width, width)],
                )
                made.start()
                waits.append(made)
    return first, second


def wait_all(waits):
    for made in waits:
        made.wait()


def attn_forward(level, meta, x_or_mid, parts, norms, a_slots, got, bias, seg_col, seg_row):
    nz, rz, two = a_slots[0].shape
    length, width = x_or_mid.shape
    cols = two // 2
    heads = 2 * cols // HD
    step = 256

    def body(meta, *refs):
        refs = list(refs)
        src = refs.pop(0)
        if level:
            own, other, gain, shift = (refs.pop(0) for _ in range(4))
        s = [refs.pop(0) for _ in range(4)]
        got, bias_qk, bias_v, sc, sr = (refs.pop(0) for _ in range(5))
        part_out, qk_out, v_out, probs_out, ctx_out = (refs.pop(0) for _ in range(5))
        if level:
            x_out, xhat_out, scale_out = (refs.pop(0) for _ in range(3))
        w_qk, w_vo, sems = refs
        waits = load_a(meta, s, got, w_qk, w_vo, sems, nz, rz)
        if level:
            for rows in chunks(length):
                z = src[rows, :] + (own[rows, :].astype(F32) + other[rows, :].astype(F32)) + shift[2:3, :]
                xhat, scale = norm_rows(z)
                x_out[rows, :] = (xhat * gain[1:2, :] + shift[3:4, :]).astype(BF16)
                xhat_out[rows, :] = xhat.astype(BF16)
                scale_out[rows, :] = scale
            x_ref = x_out
        else:
            x_ref = src
        wait_all(waits)
        for j in range(2):
            for rows in chunks(length, 256):
                x = x_ref[rows, :]
                qk_out[rows, j * two : (j + 1) * two] = (
                    nn(x, w_qk[j]) + bias_qk[:, j * two : (j + 1) * two]
                ).astype(BF16)
                v_out[rows, j * cols : (j + 1) * cols] = (
                    nn(x, w_vo[j, :, :cols]) + bias_v[:, j * cols : (j + 1) * cols]
                ).astype(BF16)
        v_t = v_out[...].astype(F32).T.astype(BF16)
        for queries in chunks(length, step):
            same = sc[...] == sr[:, queries]
            outs = []
            for h in range(heads):
                j, i = divmod(h, cols // HD)
                at = j * two + i * HD
                q = qk_out[queries, at : at + HD]
                k = qk_out[:, at + cols : at + cols + HD]
                st = jnp.where(same, nt(k, q) * 0.125, -1e30)
                p = jnp.exp(st - jnp.max(st, 0, keepdims=True))
                p = (p * (1.0 / jnp.sum(p, 0, keepdims=True))).astype(BF16)
                probs_out[h, :, queries] = p
                outs.append(nn(v_t[h * HD : (h + 1) * HD], p))
            ctx = jnp.concatenate(outs, 0).T.astype(BF16)
            ctx_out[queries, :] = ctx
            part_out[queries, :] = (
                nt(ctx[:, :cols], w_vo[0, :, cols:]) + nt(ctx[:, cols:], w_vo[1, :, cols:])
            ).astype(BF16)

    outs = [
        sds((length, width), BF16), sds((length, 2 * two), BF16), sds((length, two), BF16),
        sds((heads, length, length), BF16), sds((length, two), BF16),
    ]
    args = [meta, x_or_mid]
    if level:
        args += [*parts, *norms]
        outs += [sds((length, width), BF16), sds((length, width), BF16), sds((length, 1), F32)]
    specs = [SM] + [VM] * (len(args) - 1) + [ANY] * 5 + [VM] * 4
    args += [*a_slots, got, *bias, seg_col, seg_row]
    return pl.pallas_call(
        body,
        out_shape=outs,
        in_specs=specs,
        out_specs=[VM] * len(outs),
        scratch_shapes=[
            pltpu.VMEM((2, width, two), BF16), pltpu.VMEM((2, width, two), BF16),
            pltpu.SemaphoreType.DMA((4 * nz,)),
        ],
        compiler_params=params(),
        cost_estimate=takes(13),
        name="attn_forward",
    )(*args)


def ffn_forward(meta, x, parts, gains, shifts, b_slots, bias_in):
    nz, rz, two = b_slots[0].shape
    length, width = x.shape
    units = 2 * two

    def body(meta, x, own, other, gain, shift, s0, s1, s2, s3, bias,
             part_out, mid_out, xhat_out, scale_out, act_out, slope_out, w_i, w_f, low, sems):
        first, second = load_b(meta, (s0, s1, s2, s3), w_i, w_f, sems, nz, rz)
        for rows in chunks(length):
            z = x[rows, :].astype(F32) + (own[rows, :].astype(F32) + other[rows, :].astype(F32)) + shift[0:1, :]
            xhat, scale = norm_rows(z)
            mid = xhat * gain[0:1, :] + shift[1:2, :]
            mid_out[rows, :] = mid
            low[rows, :] = mid.astype(BF16)
            xhat_out[rows, :] = xhat.astype(BF16)
            scale_out[rows, :] = scale
        wait_all(first)
        for rows in chunks(length, 256):
            for c in chunks(units, 512):
                pre = nn(low[rows, :], w_i[:, c]) + bias[:, c]
                act, slope = gelu_parts(pre)
                act_out[rows, c] = act.astype(BF16)
                slope_out[rows, c] = slope.astype(BF16)
        wait_all(second)
        for rows in chunks(length, 256):
            part_out[rows, :] = nt(act_out[rows, :], w_f[...]).astype(BF16)

    return pl.pallas_call(
        body,
        out_shape=[
            sds((length, width), BF16), sds((length, width), F32), sds((length, width), BF16),
            sds((length, 1), F32), sds((length, units), BF16), sds((length, units), BF16),
        ],
        in_specs=[SM] + [VM] * 5 + [ANY] * 4 + [VM],
        out_specs=[VM] * 6,
        scratch_shapes=[
            pltpu.VMEM((width, units), BF16), pltpu.VMEM((width, units), BF16),
            pltpu.VMEM((length, width), BF16), pltpu.SemaphoreType.DMA((8 * nz,)),
        ],
        compiler_params=params(),
        cost_estimate=takes(9),
        name="ffn_forward",
    )(meta, x, *parts, gains, shifts, *b_slots, bias_in)


def last_norm(mid, parts, gains, shifts, tok_row, cls_pos):
    length, width = mid.shape
    n_cls = cls_pos.shape[0]

    def body(cls, mid, own, other, gain, shift, tok, y_out, xhat_out, scale_out, cls_out):
        for rows in chunks(length):
            z = mid[rows, :] + (own[rows, :].astype(F32) + other[rows, :].astype(F32)) + shift[2:3, :]
            xhat, scale = norm_rows(z)
            y_out[rows, :] = (xhat * gain[1:2, :] + shift[3:4, :]).astype(BF16)
            xhat_out[rows, :] = xhat.astype(BF16)
            scale_out[rows, :] = scale
        which = lax.broadcasted_iota(jnp.int32, (16, length), 0)
        hot = jnp.zeros((16, length), F32)
        for p in range(n_cls):
            hot = jnp.where(jnp.logical_and(which == p, tok[...] == cls[p]), 1.0, hot)
        cls_out[...] = nn(hot.astype(BF16), y_out[...])[:n_cls].astype(BF16)

    return pl.pallas_call(
        body,
        out_shape=[
            sds((length, width), BF16), sds((length, width), BF16), sds((length, 1), F32),
            sds((n_cls, width), BF16),
        ],
        in_specs=[SM] + [VM] * 6,
        out_specs=[VM] * 4,
        compiler_params=params(),
        cost_estimate=takes(2),
        name="last_norm",
    )(cls_pos, mid, *parts, gains, shifts, tok_row)


def ffn_backward(level, meta, sources, xhat, scale, gains, slope, b_slots):
    nz, rz, two = b_slots[0].shape
    length, width = xhat.shape
    units = 2 * two
    n_cls = sources[3].shape[0] if level else 0

    def body(meta, *refs):
        refs = list(refs)
        if level:
            cls, grad, d_cls, tok = (refs.pop(0) for _ in range(4))
        else:
            d_above, own, other = (refs.pop(0) for _ in range(3))
        xhat, scale, gain, slope, s0, s1, s2, s3 = (refs.pop(0) for _ in range(8))
        part_out, second_out, low_out, pre_out, vec_out, inb_out, w_i, w_f, sems = refs
        first, second = load_b(meta, (s0, s1, s2, s3), w_i, w_f, sems, nz, rz)
        sums = [jnp.zeros((1, width), F32) for _ in range(3)]
        for rows in chunks(length):
            if level:
                d_out = grad[rows, :].astype(F32)
                for p in range(n_cls):
                    d_out = d_out + jnp.where(tok[rows, :] == cls[p], 1.0, 0.0) * d_cls[p : p + 1, :]
            else:
                d_out = d_above[rows, :] + (own[rows, :].astype(F32) + other[rows, :].astype(F32))
                d_out = d_out.astype(BF16).astype(F32)
            hat = xhat[rows, :].astype(F32)
            d_second = norm_back_rows(d_out, gain[1:2, :], hat, scale[rows, :])
            second_out[rows, :] = d_second
            low_out[rows, :] = d_second.astype(BF16)
            for n, item in enumerate((d_out * hat, d_out, d_second)):
                sums[n] = sums[n] + jnp.sum(item, 0, keepdims=True)
        for n in range(3):
            vec_out[n : n + 1, :] = sums[n]
        wait_all(second)
        for n, rows in enumerate(chunks(length, 256)):
            for c in chunks(units, 512):
                d_act = nn(low_out[rows, :], w_f[:, c])
                d_pre = (slope[rows, c].astype(F32) * d_act).astype(BF16)
                pre_out[rows, c] = d_pre
                total = jnp.sum(d_pre.astype(F32), 0, keepdims=True)
                inb_out[:, c] = total if n == 0 else inb_out[:, c] + total
        wait_all(first)
        for rows in chunks(length, 256):
            part_out[rows, :] = nt(pre_out[rows, :], w_i[...]).astype(BF16)

    if level:
        token_grad, d_cls, tok_col, cls_pos = sources
        args, specs = [meta, cls_pos, token_grad, d_cls, tok_col], [SM, SM, VM, VM, VM]
    else:
        args, specs = [meta, *sources], [SM, VM, VM, VM]
    args += [xhat, scale, gains, slope, *b_slots]
    specs += [VM] * 4 + [ANY] * 4
    return pl.pallas_call(
        body,
        out_shape=[
            sds((length, width), BF16), sds((length, width), F32), sds((length, width), BF16),
            sds((length, units), BF16), sds((3, width), F32), sds((1, units), F32),
        ],
        in_specs=specs,
        out_specs=[VM] * 6,
        scratch_shapes=[
            pltpu.VMEM((width, units), BF16), pltpu.VMEM((width, units), BF16),
            pltpu.SemaphoreType.DMA((8 * nz,)),
        ],
        compiler_params=params(),
        cost_estimate=takes(9),
        name="ffn_backward",
    )(*args)


def ffn_grads(meta, mid, d_pre, d_ffn, act, nz, which):
    length, width = mid.shape
    units = d_pre.shape[1]
    two = units // 2
    one = units // 4
    rz = width // nz

    def body(meta, mid, d_pre, d_ffn, act, *refs):
        outs, (mid_t, ffn_t) = refs[: len(which)], refs[len(which) :]
        mid_t[...] = mid[...].T.astype(BF16)
        ffn_t[...] = d_ffn[...].astype(F32).T.astype(BF16)
        for out, j in zip(outs, which):
            c = slice(j * one, (j + 1) * one)
            for k in range(nz):
                rows = zrows(meta, k, rz)
                out[k, :, :one] = nn(mid_t[rows, :], d_pre[:, c]).astype(BF16)
                out[k, :, one:] = nn(ffn_t[rows, :], act[:, c]).astype(BF16)

    return pl.pallas_call(
        body,
        out_shape=[sds((nz, rz, two), BF16)] * len(which),
        in_specs=[SM] + [VM] * 4,
        out_specs=[VM] * len(which),
        scratch_shapes=[pltpu.VMEM((width, length), BF16)] * 2,
        compiler_params=params(),
        cost_estimate=takes(4),
        name="ffn_grads",
    )(meta, mid, d_pre, d_ffn, act)


def attn_backward(meta, d_second, parts, xhat, scale, gains, qk, v, probs, a_slots, got):
    nz, rz, two = a_slots[0].shape
    length, width = d_second.shape
    cols = two // 2
    heads = 2 * cols // HD

    def body(meta, d_second, own, other, xhat, scale, gain, qk, v, probs, s0, s1, s2, s3, got,
             part_out, first_out, low_out, dqk_out, dv_out, vec_out, sum_qk, sum_v,
             w_qk, w_vo, d_ctx, acc_v, acc_k, sems):
        waits = load_a(meta, (s0, s1, s2, s3), got, w_qk, w_vo, sems, nz, rz)
        sums = [jnp.zeros((1, width), F32) for _ in range(3)]
        for rows in chunks(length):
            d_mid = d_second[rows, :] + (own[rows, :].astype(F32) + other[rows, :].astype(F32))
            hat = xhat[rows, :].astype(F32)
            d_first = norm_back_rows(d_mid, gain[0:1, :], hat, scale[rows, :])
            first_out[rows, :] = d_first
            low_out[rows, :] = d_first.astype(BF16)
            for n, item in enumerate((d_mid * hat, d_mid, d_first)):
                sums[n] = sums[n] + jnp.sum(item, 0, keepdims=True)
        for n in range(3):
            vec_out[n : n + 1, :] = sums[n]
        wait_all(waits)
        for j in range(2):
            for rows in chunks(length, 256):
                d_ctx[rows, j * cols : (j + 1) * cols] = nn(low_out[rows, :], w_vo[j, :, cols:]).astype(BF16)
        k_t = jnp.concatenate(
            [qk[:, j * two + cols : (j + 1) * two] for j in range(2)], 1
        ).astype(F32).T.astype(BF16)
        for h in range(heads):
            j, i = divmod(h, cols // HD)
            at = j * two + i * HD
            q_cols, k_cols, v_cols = (
                slice(at, at + HD), slice(at + cols, at + cols + HD), slice(h * HD, (h + 1) * HD),
            )
            for n, queries in enumerate(chunks(length, 256)):
                d_o = d_ctx[queries, v_cols]
                d_p = nt(v[:, v_cols], d_o)
                p = probs[h, :, queries]
                wide = p.astype(F32)
                d_s = (wide * (d_p - jnp.sum(wide * d_p, 0, keepdims=True))).astype(BF16)
                d_v = nn(p, d_o)
                d_k = nn(d_s, qk[queries, q_cols])
                acc_v[...] = d_v if n == 0 else acc_v[...] + d_v
                acc_k[...] = d_k if n == 0 else acc_k[...] + d_k
                d_q = nn(k_t[h * HD : (h + 1) * HD], d_s)
                dqk_out[queries, q_cols] = (d_q.T * 0.125).astype(BF16)
            dv_out[:, v_cols] = acc_v[...].astype(BF16)
            dqk_out[:, k_cols] = (acc_k[...] * 0.125).astype(BF16)
        sum_qk[...] = jnp.sum(dqk_out[...].astype(F32), 0, keepdims=True)
        sum_v[...] = jnp.sum(dv_out[...].astype(F32), 0, keepdims=True)
        for rows in chunks(length, 256):
            part_out[rows, :] = (
                nt(dqk_out[rows, :two], w_qk[0]) + nt(dqk_out[rows, two:], w_qk[1])
                + nt(dv_out[rows, :cols], w_vo[0, :, :cols]) + nt(dv_out[rows, cols:], w_vo[1, :, :cols])
            ).astype(BF16)

    return pl.pallas_call(
        body,
        out_shape=[
            sds((length, width), BF16), sds((length, width), F32), sds((length, width), BF16),
            sds((length, 2 * two), BF16), sds((length, two), BF16), sds((3, width), F32),
            sds((1, 2 * two), F32), sds((1, two), F32),
        ],
        in_specs=[SM] + [VM] * 9 + [ANY] * 5,
        out_specs=[VM] * 8,
        scratch_shapes=[
            pltpu.VMEM((2, width, two), BF16), pltpu.VMEM((2, width, two), BF16),
            pltpu.VMEM((length, two), BF16), pltpu.VMEM((length, HD), F32), pltpu.VMEM((length, HD), F32),
            pltpu.SemaphoreType.DMA((4 * nz,)),
        ],
        compiler_params=params(),
        cost_estimate=takes(15),
        name="attn_backward",
    )(meta, d_second, *parts, xhat, scale, gains, qk, v, probs, *a_slots, got)


def attn_grads(meta, x, d_attn, d_qk, d_v, ctx, nz):
    length, width = x.shape
    two = d_v.shape[1]
    cols = two // 2
    rz = width // nz

    def body(meta, x, d_attn, d_qk, d_v, ctx, keep, send, x_t, a_t):
        x_t[...] = x[...].astype(F32).T.astype(BF16)
        a_t[...] = d_attn[...].astype(F32).T.astype(BF16)

        def fill(qk_out, vo_out):
            for j in range(2):
                for k in range(nz):
                    rows = zrows(meta, k, rz)
                    c = slice(j * cols, (j + 1) * cols)
                    qk_out[j, k] = nn(x_t[rows, :], d_qk[:, j * two : (j + 1) * two]).astype(BF16)
                    vo_out[j, k, :, :cols] = nn(x_t[rows, :], d_v[:, c]).astype(BF16)
                    vo_out[j, k, :, cols:] = nn(a_t[rows, :], ctx[:, c]).astype(BF16)

        @pl.when(meta[0] == 0)
        def _():
            fill(keep, send)

        @pl.when(meta[0] != 0)
        def _():
            fill(send, keep)

    return pl.pallas_call(
        body,
        out_shape=[sds((2, nz, rz, two), BF16)] * 2,
        in_specs=[SM] + [VM] * 5,
        out_specs=[VM] * 2,
        scratch_shapes=[pltpu.VMEM((width, length), BF16)] * 2,
        compiler_params=params(),
        cost_estimate=takes(4),
        name="attn_grads",
    )(meta, x, d_attn, d_qk, d_v, ctx)


def loss_kernel(own, passages, queries, positive_col, own_row):
    n_q, width = queries.shape
    n_p = passages.shape[0]
    n_own = own_row

    def body(own, passages, queries, pos, loss_out, d_out):
        logits = nt(queries[...], passages[...])
        top = jnp.max(logits, -1, keepdims=True)
        log_total = top + jnp.log(jnp.sum(jnp.exp(logits - top), -1, keepdims=True))
        index = lax.broadcasted_iota(jnp.int32, (n_q, n_p), 1)
        hits = pos[...] == index
        chosen = jnp.sum(jnp.where(hits, logits, 0.0), -1, keepdims=True)
        loss_out[...] = jnp.sum(log_total - chosen, 0, keepdims=True) / n_q
        d_logits = (16.0 * (jnp.exp(logits - log_total) - jnp.where(hits, 1.0, 0.0))).astype(BF16)
        pick = jnp.where(
            lax.broadcasted_iota(jnp.int32, (n_p, 128), 0)
            == lax.broadcasted_iota(jnp.int32, (n_p, 128), 1) + own[0],
            1.0, 0.0,
        ).astype(BF16)
        cols = nn(d_logits, pick)
        d_out[...] = nn(cols.T.astype(BF16), queries[...])[:n_own]

    return pl.pallas_call(
        body,
        out_shape=[sds((1, 1), F32), sds((n_own, width), F32)],
        in_specs=[SM] + [VM] * 3,
        out_specs=[VM] * 2,
        compiler_params=params(),
        cost_estimate=takes(1),
        name="contrast",
    )(own, passages, queries, positive_col)


def after(block, *earlier):
    return lax.optimization_barrier((block, *earlier))[0]


def pad_flat(flat):
    size = -(-flat.shape[0] // 2048) * 2048
    return jnp.pad(flat, (0, size - flat.shape[0])).reshape(-1, 128)


def on_device(
    inputs, cls_pos, w_qkv, qv_bias, w_out, w_in, in_bias, w_ffn_out,
    layer_gains, shifts, queries, positive, token_grad,
):
    core = lax.axis_index("section")
    dp = lax.axis_index("dp")
    me = lax.axis_index("tensor")
    n_dp = lax.axis_size("dp")
    n_t = lax.axis_size("tensor")
    first_core = core == 0
    rows_dev, share, width = inputs.shape
    rows = w_qkv.shape[1]
    cols = w_qkv.shape[3]
    half = w_in.shape[2] // 2
    units = in_bias.shape[2]
    length = n_t * share
    n_chips = n_dp * n_t
    piece = width // n_chips
    order = dp_order()
    direct = direct_dp()
    t_ids = jnp.arange(n_t, dtype=jnp.int32)

    out_t = w_out[0].T
    ffn_t = w_ffn_out[0].T
    pack_a = [
        jnp.concatenate([w_qkv[0, :, 0], w_qkv[0, :, 1]], 1),
        jnp.concatenate([w_qkv[0, :, 2], out_t], 1),
    ]
    pack_b = [
        jnp.concatenate([w_in[0, :, c * half : (c + 1) * half], ffn_t[:, c * half : (c + 1) * half]], 1)
        for c in range(2)
    ]
    vec = jnp.concatenate(
        [layer_gains.reshape(-1), shifts.reshape(-1), qv_bias.reshape(-1), in_bias.reshape(-1)]
    )
    n_vec = vec.shape[0]

    def by_layer(pack):
        got = swap_cores(jnp.where(first_core, pack[1], pack[0]))
        return [jnp.where(first_core, pack[0], got), jnp.where(first_core, got, pack[1])]

    shard_a = by_layer(pack_a)
    shard_b = by_layer(pack_b)
    got = swap_cores(vec)
    message = pad_flat(
        jnp.concatenate(
            [
                jnp.where(first_core, vec, got), jnp.where(first_core, got, vec),
                queries.reshape(-1), (positive // 16).astype(BF16), (positive % 16).astype(BF16),
            ]
        )
    )

    def spread_rows(block):
        parts = [lax.dynamic_index_in_dim(block, me ^ k, 0, keepdims=False) for k in range(n_t)]
        return jnp.concatenate([parts[0]] + [hop_tensor(parts[k], k) for k in range(1, n_t)], 0)

    positions = jnp.concatenate(
        [(me ^ k) * share + jnp.arange(share, dtype=jnp.int32) for k in range(n_t)]
    )
    cls_row = lax.dynamic_index_in_dim(cls_pos, me, 0, keepdims=False)
    segments = jnp.sum((positions[:, None] >= cls_row[None, :]).astype(jnp.int32), -1)
    seg_col, seg_row = segments[:, None], segments[None, :]
    tok_col, tok_row = positions[:, None], positions[None, :]
    zrow = order * rows if direct else jnp.zeros((1,), jnp.int32)
    meta = jnp.concatenate([core[None].astype(jnp.int32), zrow])

    def whole(slots):
        if direct:
            return slots
        return [s.reshape(1, width, -1) for s in slots]

    a_plan = (PLAIN, CROSS)
    a_flips = [jnp.array(flips, jnp.int32) for flips in ((0, 1, 2, 3), (0, 2, 1, 3))]

    def exchange_a(slots):
        return swap_cores(
            jnp.where(first_core, jnp.stack(slots[2:]), jnp.stack(slots[:2]))
        )

    z_a0 = gather_dp(shard_a[0])
    z_vec = gather_dp(message)
    x_low = spread_rows(inputs)
    vec_slots = jnp.stack(gather_tensor(z_vec, *PLAIN))
    z_b0 = gather_dp(after(shard_b[0], z_a0, z_vec))
    a0 = whole(gather_tensor(z_a0, *a_plan[0]))
    got_a0 = exchange_a(a0)
    z_a1 = gather_dp(after(shard_a[1], z_b0))
    b0 = whole(gather_tensor(after(z_b0, a0[3], vec_slots, x_low), *MIRROR))
    z_b1 = gather_dp(after(shard_b[1], z_a1))
    a1 = whole(gather_tensor(after(z_a1, b0[3]), *a_plan[1]))
    got_a1 = exchange_a(a1)
    b1 = whole(gather_tensor(after(z_b1, a1[3]), *MIRROR))
    slots_a, slots_b, gots = (a0, a1), (b0, b1), (got_a0, got_a1)
    ahead = (z_b0, z_b1)

    slot_ids = (order[None, :] * n_t + (me ^ t_ids)[:, None]).reshape(-1)
    to_natural = (jnp.arange(n_chips, dtype=jnp.int32)[:, None] == slot_ids[None, :]).astype(BF16)
    table = nn(to_natural, vec_slots.reshape(n_chips, -1))
    n_gain, n_shift, n_qv, n_inb = layer_gains.size, shifts.size, qv_bias.size, units

    def read_vectors(vecs):
        at = 0
        gains = vecs[:, at : at + n_gain].reshape(n_chips, 2, piece).transpose(1, 0, 2).reshape(2, width)
        at += n_gain
        shift = vecs[:, at : at + n_shift].reshape(n_chips, 4, piece).transpose(1, 0, 2).reshape(4, width)
        at += n_shift
        qv = vecs[:, at : at + n_qv].reshape(n_dp, n_t, 2, cols // n_dp).transpose(2, 1, 0, 3).reshape(2, n_t, cols)
        at += n_qv
        inb = vecs[:, at : at + n_inb].reshape(n_dp, n_t, units).transpose(1, 0, 2).reshape(n_t, 2 * half)
        return gains, shift, qv, inb

    head_slots = [me ^ lax.dynamic_slice_in_dim(flips, 2 * core, 2) for flips in a_flips]
    unit_slots = me ^ jnp.where(first_core, a_flips[0], a_flips[1])

    def pick(values, slots):
        hot = (slots[:, None] == t_ids[None, :]).astype(F32)
        return jnp.sum(hot[:, :, None] * values[None], 1)

    vectors = []
    for level in range(2):
        gains, shift, qv, inb = read_vectors(table[:, level * n_vec : (level + 1) * n_vec])
        bias_q, bias_v = pick(qv[0], head_slots[level]), pick(qv[1], head_slots[level])
        bias_qk = jnp.concatenate([bias_q, jnp.zeros_like(bias_q)], 1).reshape(1, -1)
        bias_in = pick(lax.dynamic_slice_in_dim(inb, core * half, half, 1), unit_slots).reshape(1, -1)
        vectors.append((gains, shift, (bias_qk, bias_v.reshape(1, -1)), bias_in))
    at = 2 * n_vec
    q_dev = queries.shape[0]
    all_q = table[:, at : at + q_dev * width].reshape(-1, width).astype(BF16)
    at += q_dev * width
    all_pos = table[:, at : at + q_dev] * 16.0 + table[:, at + q_dev : at + 2 * q_dev]
    all_pos = all_pos.astype(jnp.int32).reshape(-1, 1)

    vectors, all_q, all_pos, x_low = lax.optimization_barrier((vectors, all_q, all_pos, x_low))
    saved = []
    source, parts, norms = x_low, None, None
    for level in range(2):
        gains, shift, biases, bias_in = vectors[level]
        outs = attn_forward(
            level, meta, after(source, ahead[level]), parts, norms, slots_a[level], gots[level], biases, seg_col, seg_row
        )
        part, qk, v, probs, ctx = outs[:5]
        if level:
            x, xhat2, scale2 = outs[5:]
            saved[0]["second"] = (xhat2, scale2)
        else:
            x = x_low
        part, mid, xhat1, scale1, act, slope = ffn_forward(
            meta, after(x, z_a1) if level == 0 else x, (part, swap_cores(part)), gains, shift,
            slots_b[level], bias_in,
        )
        saved.append(
            dict(x=x, qk=qk, v=v, probs=probs, ctx=ctx, mid=mid, xhat1=xhat1, scale1=scale1, act=act, slope=slope)
        )
        source, parts, norms = mid, (part, swap_cores(part)), (gains, shift)
    y, xhat2, scale2, cls_own = last_norm(source, parts, *norms, tok_row, cls_row)
    saved[1]["second"] = (xhat2, scale2)

    n_cls = cls_row.shape[0]
    cls_slots = jnp.stack(gather_tensor(gather_dp(cls_own), *PLAIN))
    passages = nn(to_natural, cls_slots.reshape(n_chips, -1)).astype(BF16).reshape(-1, width)
    first_own = ((dp * n_t + me) * n_cls).astype(jnp.int32)[None]
    mean_loss, d_cls = loss_kernel(first_own, passages, all_q, all_pos, n_cls)

    def send_rows(block, section):
        low = block.astype(BF16).reshape(n_t, share, width)
        routes = [
            [(section * n_t + i, section * n_t + (i ^ k)) for i in range(n_t)] for k in range(n_t)
        ]
        return [lax.ppermute(low[k], ("section", "tensor"), routes[k]) for k in range(1, n_t)]

    y_rows = send_rows(y, 1)

    totals = [None, None]
    vector_rows = [None, None]
    sources = (spread_rows(token_grad), d_cls, tok_col, cls_row)
    for level in (1, 0):
        gains, shift, _, _ = vectors[level]
        kept = saved[level]
        xhat2, scale2 = kept["second"]
        if level == 0:
            sources = (after(sources[0], *steps_b), *sources[1:])
        part, d_second, d_ffn, d_pre, vec2, sum_inb = ffn_backward(
            level, meta, sources, xhat2, scale2, gains, kept["slope"], slots_b[level]
        )
        other = swap_cores(part)
        nz = 4 if direct else 1
        far = ffn_grads(meta, kept["mid"], d_pre, d_ffn, kept["act"], nz, (2, 3))
        near = ffn_grads(meta, kept["mid"], d_pre, after(d_ffn, far[0]), kept["act"], nz, (0, 1))
        grads_b = [*near, *far]
        if not direct:
            grads_b = [g.reshape(n_dp, rows, -1) for g in grads_b]
        steps_b = scatter_first(grads_b, *MIRROR)
        tot_b = scatter_second(*steps_b, *MIRROR)
        if level == 0:
            d_second = after(d_second, near[0], tot_b_above)
        else:
            d_second = after(d_second, near[0])
            tot_b_above = tot_b
        outs = attn_backward(
            meta, d_second, (part, other), kept["xhat1"], kept["scale1"], gains,
            kept["qk"], kept["v"], kept["probs"], slots_a[level], gots[level],
        )
        part, d_first, d_attn, d_qk, d_v, vec1, sum_qk, sum_v = outs
        other = swap_cores(part)
        if level == 0:
            d_attn = after(d_attn, *steps_a, *steps_b)
        keep, send = attn_grads(meta, kept["x"], d_attn, d_qk, d_v, kept["ctx"], nz)
        got = swap_cores(send)
        grads_a = [jnp.where(first_core, keep[j], got[j]) for j in range(2)]
        grads_a += [jnp.where(first_core, got[j], keep[j]) for j in range(2)]
        if not direct:
            grads_a = [g.reshape(n_dp, rows, -1) for g in grads_a]
        steps_a = scatter_first(grads_a, *a_plan[level])
        tot_a = scatter_dp(scatter_second(*steps_a, *a_plan[level])).astype(BF16)
        tot_b = scatter_dp(tot_b).astype(BF16)
        route = [(1 - level, level)]
        totals[level] = (
            tot_a, lax.ppermute(tot_a, "section", route),
            tot_b, lax.ppermute(tot_b, "section", route),
        )
        vector_rows[level] = (vec1, vec2, sum_qk, sum_v, sum_inb)
        sources = (d_first, part, other)
    d_hidden = d_first + (part.astype(F32) + other.astype(F32))

    vector_rows, _ = lax.optimization_barrier((vector_rows, steps_a))

    def vector_table(level):
        vec1, vec2, sum_qk, sum_v, sum_inb = vector_rows[level]
        gs = jnp.concatenate([vec1[0:1], vec2[0:1], vec1[2:3], vec1[1:2], vec2[2:3], vec2[1:2]])
        gs = jnp.where(first_core, gs, 0.0).reshape(6, n_chips, piece).transpose(1, 0, 2).reshape(n_chips, -1)
        qv = jnp.stack([sum_qk.reshape(2, 2 * cols)[:, :cols], sum_v.reshape(2, cols)], 1)
        hot = (head_slots[level][:, None] == t_ids[None, :]).astype(F32)
        qv = jnp.sum(hot[:, None, :, None] * qv[:, :, None, :], 0)
        qv = qv.reshape(2, n_t, n_dp, -1).transpose(2, 1, 0, 3).reshape(n_chips, -1)
        hot = (unit_slots[:, None] == t_ids[None, :]).astype(F32)
        inb = jnp.sum(hot[:, :, None] * sum_inb.reshape(n_t, 1, half), 0)
        inb = jnp.where((jnp.arange(2) == core)[None, :, None], inb[:, None, :], 0.0)
        inb = inb.reshape(n_t, n_dp, units).transpose(1, 0, 2).reshape(n_chips, -1)
        return jnp.concatenate([gs, qv, inb], 1)

    flat = jnp.concatenate([vector_table(0), vector_table(1)], 1)
    flat = lax.dot_general(
        to_natural.astype(F32), flat, (((0,), (0,)), ((), ())), precision=lax.Precision.HIGHEST
    )
    flat = jnp.pad(flat, ((0, 0), (0, -flat.shape[1] % 1024))).reshape(n_t, n_dp, -1, 128)
    got = hop_tensor(flat[2:], 2)
    flat = flat[:2] + got
    flat = flat[0] + hop_tensor(flat[1], 1)
    if direct:
        flat = flat[0] + sum(
            lax.ppermute(flat[k], "dp", [(i, i ^ k) for i in range(4)]) for k in range(1, 4)
        )
    else:
        flat = lax.psum_scatter(flat, "dp", scatter_dimension=0, tiled=False)
    flat = (flat + swap_cores(flat)).reshape(-1)
    flat = jnp.where(first_core, flat[:n_vec], flat[n_vec : 2 * n_vec])
    at = 0
    grad_gains = flat[at : at + n_gain].reshape(layer_gains.shape)
    at += n_gain
    grad_shifts = flat[at : at + n_shift].reshape(shifts.shape)
    at += n_shift
    grad_qv = flat[at : at + n_qv].reshape(qv_bias.shape)
    at += n_qv
    grad_inb = flat[at : at + n_inb].reshape(in_bias.shape)

    own_a, got_a, own_b, got_b = (
        jnp.where(first_core, left, right).astype(F32) for left, right in zip(*totals)
    )
    halves_a = (jnp.where(first_core, own_a, got_a), jnp.where(first_core, got_a, own_a))
    halves_b = (jnp.where(first_core, own_b, got_b), jnp.where(first_core, got_b, own_b))
    grad_qkv = jnp.stack(
        [halves_a[0][:, :cols], halves_a[0][:, cols:], halves_a[1][:, :cols]], 1
    )[None]
    grad_out = halves_a[1][:, cols:].T[None]
    grad_in = jnp.concatenate([h[:, :half] for h in halves_b], 1)[None]
    grad_ffn = jnp.concatenate([h[:, half:] for h in halves_b], 1).T[None]
    h_rows = send_rows(d_hidden, 0)
    pieces = [jnp.where(first_core, d_hidden[:share], y[:share].astype(F32))]
    pieces += [jnp.where(first_core, h, g).astype(F32) for h, g in zip(h_rows, y_rows)]
    boundary = jnp.zeros((n_t, share, width), F32)
    for k in range(n_t):
        boundary = lax.dynamic_update_index_in_dim(boundary, pieces[k], me ^ k, 0)
    boundary = boundary[None]
    return (
        grad_qkv, grad_qv, grad_out, grad_in, grad_inb, grad_ffn,
        grad_gains, grad_shifts, boundary, mean_loss.reshape(()),
    )


def solution(mesh):
    return jax.shard_map(
        on_device,
        mesh=mesh,
        in_specs=(
            P("dp", "tensor", None),
            P("dp", None),
            P("section", "dp", None, "tensor"),
            P("section", None, "tensor", "dp"),
            P("section", "tensor", "dp"),
            P("section", "dp", "tensor"),
            P("section", "tensor", "dp"),
            P("section", "tensor", "dp"),
            P("section", None, ("dp", "tensor")),
            P("section", None, ("dp", "tensor")),
            P(("dp", "tensor"), None),
            P(("dp", "tensor")),
            P("dp", "tensor", None),
        ),
        out_specs=(
            P("section", "dp", None, "tensor"),
            P("section", None, "tensor", "dp"),
            P("section", "tensor", "dp"),
            P("section", "dp", "tensor"),
            P("section", "tensor", "dp"),
            P("section", "tensor", "dp"),
            P("section", None, ("dp", "tensor")),
            P("section", None, ("dp", "tensor")),
            P("section", "dp", "tensor", None),
            P(),
        ),
        check_vma=False,
    )
```

```python
import jax
import jax.numpy as jnp
from jax import lax
from jax.experimental import pallas as pl
from jax.experimental.pallas import tpu as pltpu
from jax.sharding import PartitionSpec as P

HD = 64
PARTNER = 1
CROSS = 2
BF16 = jnp.bfloat16
F32 = jnp.float32


def mm(left, right, dims):
    return lax.dot_general(left, right, (dims, ((), ())), preferred_element_type=F32)


def nn(left, right):
    return mm(left, right, ((1,), (0,)))


def nt(left, right):
    return mm(left, right, ((1,), (1,)))


def after(block, *earlier):
    return lax.optimization_barrier((block, *earlier))[0]


def swap_cores(block):
    return lax.ppermute(block, "section", [(0, 1), (1, 0)])


def hop(block, axis, flip):
    return lax.ppermute(block, axis, [(i, i ^ flip) for i in range(lax.axis_size(axis))])


def core_hop(block, axis, flip, core):
    size = lax.axis_size(axis)
    route = [(core * size + i, core * size + (i ^ flip)) for i in range(size)]
    route += [((1 - core) * size + i, (1 - core) * size + i) for i in range(size)]
    return lax.ppermute(block, ("section", axis), route)


def cross_hop(block, source):
    size = lax.axis_size("tensor")
    route = [(source * size + i, (1 - source) * size + (i ^ CROSS)) for i in range(size)]
    return lax.ppermute(block, ("section", "tensor"), route)


def direct_dp():
    return lax.axis_size("dp") == 4


def dp_order():
    size = lax.axis_size("dp")
    if direct_dp():
        return lax.axis_index("dp") ^ jnp.arange(size, dtype=jnp.int32)
    return jnp.arange(size, dtype=jnp.int32)


def gather_small(block):
    if direct_dp():
        block = jnp.stack([block] + [hop(block, "dp", k) for k in range(1, 4)])
    else:
        block = lax.all_gather(block, "dp", axis=0, tiled=False)
    return jnp.stack([block] + [hop(block, "tensor", k) for k in range(1, lax.axis_size("tensor"))])


def gather_dp(block, core):
    if direct_dp():
        one, two, three = (core_hop(block, "dp", k, core) for k in range(1, 4))
        return jnp.stack([block, one]), jnp.stack([two, three])
    whole = lax.all_gather(block, "dp", axis=0, tiled=True)
    whole = whole.reshape(2, whole.shape[0] // 2, whole.shape[1])
    return whole[:1], whole[1:]


def gather_layer(halves, core):
    a, b = halves
    near_a = core_hop(a, "tensor", PARTNER, core)
    far_b = cross_hop(b, core)
    near_b = core_hop(b, "tensor", PARTNER, core)
    far_a = cross_hop(a, core)
    both_a = cross_hop(near_a, core)
    both_b = core_hop(far_b, "tensor", PARTNER, 1 - core)
    return [a, b, near_a, near_b, far_a, far_b, both_a, both_b]


def add_low(*items):
    total = items[0].astype(F32)
    for item in items[1:]:
        total = total + item.astype(F32)
    return total.astype(BF16)


class Reduction:
    def __init__(self, grads, core):
        self.core = core
        self.grads = own_a, own_b, next_a, next_b = grads
        got_a = cross_hop(next_a, 1 - core)
        got_b = core_hop(next_b, "tensor", PARTNER, 1 - core)
        self.far_a = cross_hop(own_a, 1 - core)
        self.near_b = core_hop(next_b, "tensor", PARTNER, core)
        self.first = add_low(next_a, got_a), add_low(own_b, got_b)

    def second(self):
        own_a, own_b = self.grads[:2]
        next_a, far_b = self.first
        near_a = core_hop(next_a, "tensor", PARTNER, self.core)
        far_b = cross_hop(far_b, 1 - self.core)
        self.sums = add_low(own_a, self.far_a, near_a), add_low(own_b, far_b, self.near_b)
        return self.sums

    def third(self):
        a, b = self.sums
        if not direct_dp():
            whole = jnp.concatenate([a, b]).reshape(-1, a.shape[2])
            return lax.psum_scatter(whole, "dp", scatter_dimension=0, tiled=True).astype(F32)
        total = a[0].astype(F32)
        for k, block in ((1, a[1]), (2, b[0]), (3, b[1])):
            total = total + core_hop(block, "dp", k, self.core).astype(F32)
        return total


VMEM_LIMIT = 48 * 1024 * 1024
CHUNK = 128


def takes(micros):
    return pl.CostEstimate(flops=int(micros * 1.1e9), bytes_accessed=0, transcendentals=0)


def params():
    return pltpu.CompilerParams(vmem_limit_bytes=VMEM_LIMIT)


ANY = pl.BlockSpec(memory_space=pl.ANY)
VM = pl.BlockSpec(memory_space=pltpu.VMEM)
SM = pl.BlockSpec(memory_space=pltpu.SMEM)


def sds(shape, dtype):
    return jax.ShapeDtypeStruct(shape, dtype)


def chunks(length, step=CHUNK):
    return [slice(i, i + step) for i in range(0, length, step)]


def norm_rows(z):
    centre = z - jnp.mean(z, -1, keepdims=True)
    spread = jnp.mean(centre * centre, -1, keepdims=True)
    scale = lax.rsqrt(spread + 1e-05)
    return centre * scale, scale


def norm_back_rows(d_out, gain, xhat, scale):
    g = d_out * gain
    m1 = jnp.mean(g, -1, keepdims=True)
    m2 = jnp.mean(g * xhat, -1, keepdims=True)
    return scale * (g - m1 - xhat * m2)


def gelu_parts(x):
    e = jnp.exp(-0.5 * x * x)
    t = 1.0 / (1.0 + 0.2316418882 * jnp.abs(x))
    poly = t * (
        0.127414796 + t * (-0.142248368 + t * (0.7107068705 + t * (-0.7265760135 + t * 0.5307027145)))
    )
    tail = poly * e
    cdf = jnp.where(x < 0.0, tail, 1.0 - tail)
    return x * cdf, cdf + x * e * 0.3989422804014327


def zrows(meta, k, rz):
    return pl.ds(pl.multiple_of(meta[1 + k], 64), rz)


def load_weights(meta, pieces, place, sems):
    own, near, far, both = pieces[0:2], pieces[2:4], pieces[4:6], pieces[6:8]
    half, rz, _ = own[0].shape
    home = meta[0] == 1
    lists = None
    at = 0
    for j, (mine, others) in enumerate(((own, far), (near, both))):
        for k in range(2 * half):
            targets = place(j, zrows(meta, k, rz))
            lists = lists or [[] for _ in targets]
            for n, (dst, columns) in enumerate(targets):
                first = pltpu.make_async_copy(mine[k // half].at[k % half, :, columns], dst, sems.at[at])
                second = pltpu.make_async_copy(others[k // half].at[k % half, :, columns], dst, sems.at[at])
                at += 1

                @pl.when(home)
                def _():
                    first.start()

                @pl.when(jnp.logical_not(home))
                def _():
                    second.start()

                lists[n].append(first)
    return lists


def wait_all(waits):
    for made in waits:
        made.wait()


def load_a(meta, pieces, w_a, sems):
    width = w_a.shape[2]
    return load_weights(meta, pieces, lambda j, rows: [(w_a.at[j, rows, :], pl.ds(0, width))], sems)[0]


def load_b(meta, pieces, w_i, w_f, sems):
    one = w_i.shape[1] // 2
    return load_weights(
        meta,
        pieces,
        lambda j, rows: [
            (w_i.at[rows, pl.ds(j * one, one)], pl.ds(0, one)),
            (w_f.at[rows, pl.ds(j * one, one)], pl.ds(one, one)),
        ],
        sems,
    )


def attn_forward(level, meta, x_or_mid, parts, norms, pieces, bias, seg_col, seg_row):
    half, rz, four = pieces[0].shape
    length, width = x_or_mid.shape
    cols = four // 4
    three = 3 * cols
    heads = 2 * cols // HD

    def body(meta, *refs):
        refs = list(refs)
        src = refs.pop(0)
        if level:
            own, other, gain, shift = (refs.pop(0) for _ in range(4))
        pieces = [refs.pop(0) for _ in range(8)]
        bias, sc, sr = (refs.pop(0) for _ in range(3))
        part_out, qkv_out, probs_out, ctx_out = (refs.pop(0) for _ in range(4))
        if level:
            x_out, xhat_out, scale_out = (refs.pop(0) for _ in range(3))
        w_a, sems = refs
        waits = load_a(meta, pieces, w_a, sems)
        if level:
            for rows in chunks(length):
                z = src[rows, :] + (own[rows, :].astype(F32) + other[rows, :].astype(F32)) + shift[2:3, :]
                xhat, scale = norm_rows(z)
                x_out[rows, :] = (xhat * gain[1:2, :] + shift[3:4, :]).astype(BF16)
                xhat_out[rows, :] = xhat.astype(BF16)
                scale_out[rows, :] = scale
            x_ref = x_out
        else:
            x_ref = src
        wait_all(waits)
        for j in range(2):
            c = slice(j * three, (j + 1) * three)
            for rows in chunks(length, 256):
                qkv_out[rows, c] = (nn(x_ref[rows, :], w_a[j, :, :three]) + bias[:, c]).astype(BF16)
        v_t = jnp.concatenate(
            [qkv_out[:, j * three + 2 * cols : (j + 1) * three].astype(F32) for j in range(2)], 1
        ).T.astype(BF16)
        for queries in chunks(length, 256):
            same = sc[...] == sr[:, queries]
            outs = []
            for h in range(heads):
                j, i = divmod(h, cols // HD)
                at = j * three + i * HD
                q = qkv_out[queries, at : at + HD]
                k = qkv_out[:, at + cols : at + cols + HD]
                st = jnp.where(same, nt(k, q) * 0.125, -1e30)
                p = jnp.exp(st - jnp.max(st, 0, keepdims=True))
                p = (p * (1.0 / jnp.sum(p, 0, keepdims=True))).astype(BF16)
                probs_out[h, :, queries] = p
                outs.append(nn(v_t[h * HD : (h + 1) * HD], p))
            ctx = jnp.concatenate(outs, 0).T.astype(BF16)
            ctx_out[queries, :] = ctx
            part_out[queries, :] = (
                nt(ctx[:, :cols], w_a[0, :, three:]) + nt(ctx[:, cols:], w_a[1, :, three:])
            ).astype(BF16)

    outs = [
        sds((length, width), BF16), sds((length, 2 * three), BF16),
        sds((heads, length, length), BF16), sds((length, 2 * cols), BF16),
    ]
    args = [meta, x_or_mid]
    if level:
        args += [*parts, *norms]
        outs += [sds((length, width), BF16), sds((length, width), BF16), sds((length, 1), F32)]
    specs = [SM] + [VM] * (len(args) - 1) + [ANY] * 8 + [VM] * 3
    args += [*pieces, bias, seg_col, seg_row]
    return pl.pallas_call(
        body,
        out_shape=outs,
        in_specs=specs,
        out_specs=[VM] * len(outs),
        scratch_shapes=[pltpu.VMEM((2, width, four), BF16), pltpu.SemaphoreType.DMA((4 * half,))],
        compiler_params=params(),
        cost_estimate=takes(13),
        name="attn_forward",
    )(*args)


def ffn_forward(meta, x, parts, gains, shifts, pieces, bias_in):
    half, rz, units = pieces[0].shape
    length, width = x.shape

    def body(meta, x, own, other, gain, shift, p0, p1, p2, p3, p4, p5, p6, p7, bias,
             part_out, mid_out, xhat_out, scale_out, act_out, slope_out, w_i, w_f, low, sems):
        first, second = load_b(meta, (p0, p1, p2, p3, p4, p5, p6, p7), w_i, w_f, sems)
        for rows in chunks(length):
            z = x[rows, :].astype(F32) + (own[rows, :].astype(F32) + other[rows, :].astype(F32)) + shift[0:1, :]
            xhat, scale = norm_rows(z)
            mid = xhat * gain[0:1, :] + shift[1:2, :]
            mid_out[rows, :] = mid
            low[rows, :] = mid.astype(BF16)
            xhat_out[rows, :] = xhat.astype(BF16)
            scale_out[rows, :] = scale
        wait_all(first)
        for rows in chunks(length, 256):
            for c in chunks(units, 512):
                pre = nn(low[rows, :], w_i[:, c]) + bias[:, c]
                act, slope = gelu_parts(pre)
                act_out[rows, c] = act.astype(BF16)
                slope_out[rows, c] = slope.astype(BF16)
        wait_all(second)
        for rows in chunks(length, 256):
            part_out[rows, :] = nt(act_out[rows, :], w_f[...]).astype(BF16)

    return pl.pallas_call(
        body,
        out_shape=[
            sds((length, width), BF16), sds((length, width), F32), sds((length, width), BF16),
            sds((length, 1), F32), sds((length, units), BF16), sds((length, units), BF16),
        ],
        in_specs=[SM] + [VM] * 5 + [ANY] * 8 + [VM],
        out_specs=[VM] * 6,
        scratch_shapes=[
            pltpu.VMEM((width, units), BF16), pltpu.VMEM((width, units), BF16),
            pltpu.VMEM((length, width), BF16), pltpu.SemaphoreType.DMA((8 * half,)),
        ],
        compiler_params=params(),
        cost_estimate=takes(9),
        name="ffn_forward",
    )(meta, x, *parts, gains, shifts, *pieces, bias_in)


def last_norm(mid, parts, gains, shifts, tok_row, cls_pos):
    length, width = mid.shape
    n_cls = cls_pos.shape[0]

    def body(cls, mid, own, other, gain, shift, tok, y_out, xhat_out, scale_out, cls_out):
        for rows in chunks(length):
            z = mid[rows, :] + (own[rows, :].astype(F32) + other[rows, :].astype(F32)) + shift[2:3, :]
            xhat, scale = norm_rows(z)
            y_out[rows, :] = (xhat * gain[1:2, :] + shift[3:4, :]).astype(BF16)
            xhat_out[rows, :] = xhat.astype(BF16)
            scale_out[rows, :] = scale
        which = lax.broadcasted_iota(jnp.int32, (16, length), 0)
        hot = jnp.zeros((16, length), F32)
        for p in range(n_cls):
            hot = jnp.where(jnp.logical_and(which == p, tok[...] == cls[p]), 1.0, hot)
        cls_out[...] = nn(hot.astype(BF16), y_out[...])[:n_cls].astype(BF16)

    return pl.pallas_call(
        body,
        out_shape=[
            sds((length, width), BF16), sds((length, width), BF16), sds((length, 1), F32),
            sds((n_cls, width), BF16),
        ],
        in_specs=[SM] + [VM] * 6,
        out_specs=[VM] * 4,
        compiler_params=params(),
        cost_estimate=takes(2),
        name="last_norm",
    )(cls_pos, mid, *parts, gains, shifts, tok_row)


def ffn_backward(level, meta, sources, xhat, scale, gains, slope, pieces):
    half, rz, units = pieces[0].shape
    length, width = xhat.shape
    n_cls = sources[3].shape[0] if level else 0

    def body(meta, *refs):
        refs = list(refs)
        if level:
            cls, grad, d_cls, tok = (refs.pop(0) for _ in range(4))
        else:
            d_above, own, other = (refs.pop(0) for _ in range(3))
        xhat, scale, gain, slope = (refs.pop(0) for _ in range(4))
        pieces = [refs.pop(0) for _ in range(8)]
        part_out, second_out, low_out, pre_out, vec_out, inb_out, w_i, w_f, sems = refs
        first, second = load_b(meta, pieces, w_i, w_f, sems)
        sums = [jnp.zeros((1, width), F32) for _ in range(3)]
        for rows in chunks(length):
            if level:
                d_out = grad[rows, :].astype(F32)
                for p in range(n_cls):
                    d_out = d_out + jnp.where(tok[rows, :] == cls[p], 1.0, 0.0) * d_cls[p : p + 1, :]
            else:
                d_out = d_above[rows, :] + (own[rows, :].astype(F32) + other[rows, :].astype(F32))
                d_out = d_out.astype(BF16).astype(F32)
            hat = xhat[rows, :].astype(F32)
            d_second = norm_back_rows(d_out, gain[1:2, :], hat, scale[rows, :])
            second_out[rows, :] = d_second
            low_out[rows, :] = d_second.astype(BF16)
            for n, item in enumerate((d_out * hat, d_out, d_second)):
                sums[n] = sums[n] + jnp.sum(item, 0, keepdims=True)
        for n in range(3):
            vec_out[n : n + 1, :] = sums[n]
        wait_all(second)
        for n, rows in enumerate(chunks(length, 256)):
            for c in chunks(units, 512):
                d_act = nn(low_out[rows, :], w_f[:, c])
                d_pre = (slope[rows, c].astype(F32) * d_act).astype(BF16)
                pre_out[rows, c] = d_pre
                total = jnp.sum(d_pre.astype(F32), 0, keepdims=True)
                inb_out[:, c] = total if n == 0 else inb_out[:, c] + total
        wait_all(first)
        for rows in chunks(length, 256):
            part_out[rows, :] = nt(pre_out[rows, :], w_i[...]).astype(BF16)

    if level:
        token_grad, d_cls, tok_col, cls_pos = sources
        args, specs = [meta, cls_pos, token_grad, d_cls, tok_col], [SM, SM, VM, VM, VM]
    else:
        args, specs = [meta, *sources], [SM, VM, VM, VM]
    args += [xhat, scale, gains, slope, *pieces]
    specs += [VM] * 4 + [ANY] * 8
    return pl.pallas_call(
        body,
        out_shape=[
            sds((length, width), BF16), sds((length, width), F32), sds((length, width), BF16),
            sds((length, units), BF16), sds((3, width), F32), sds((1, units), F32),
        ],
        in_specs=specs,
        out_specs=[VM] * 6,
        scratch_shapes=[
            pltpu.VMEM((width, units), BF16), pltpu.VMEM((width, units), BF16),
            pltpu.SemaphoreType.DMA((8 * half,)),
        ],
        compiler_params=params(),
        cost_estimate=takes(9),
        name="ffn_backward",
    )(*args)


def ffn_grads(meta, mid, d_pre, d_ffn, act, nz):
    length, width = mid.shape
    units = d_pre.shape[1]
    one = units // 2
    rz = width // nz

    def body(meta, mid, d_pre, d_ffn, act, *refs):
        outs, (mid_t, ffn_t) = refs[:4], refs[4:]
        mid_t[...] = mid[...].T.astype(BF16)
        ffn_t[...] = d_ffn[...].astype(F32).T.astype(BF16)
        for j in range(2):
            c = slice(j * one, (j + 1) * one)
            for k in range(nz):
                rows = zrows(meta, k, rz)
                out, at = outs[2 * j + k // (nz // 2)], k % (nz // 2)
                out[at, :, :one] = nn(mid_t[rows, :], d_pre[:, c]).astype(BF16)
                out[at, :, one:] = nn(ffn_t[rows, :], act[:, c]).astype(BF16)

    return pl.pallas_call(
        body,
        out_shape=[sds((nz // 2, rz, units), BF16)] * 4,
        in_specs=[SM] + [VM] * 4,
        out_specs=[VM] * 4,
        scratch_shapes=[pltpu.VMEM((width, length), BF16)] * 2,
        compiler_params=params(),
        cost_estimate=takes(7),
        name="ffn_grads",
    )(meta, mid, d_pre, d_ffn, act)


def attn_backward(meta, d_second, parts, xhat, scale, gains, qkv, probs, pieces):
    half, rz, four = pieces[0].shape
    length, width = d_second.shape
    cols = four // 4
    three = 3 * cols
    heads = 2 * cols // HD

    def body(meta, d_second, own, other, xhat, scale, gain, qkv, probs, p0, p1, p2, p3, p4, p5, p6, p7,
             part_out, first_out, low_out, dqkv_out, vec_out, sum_out,
             w_a, d_ctx, acc_v, acc_k, sems):
        waits = load_a(meta, (p0, p1, p2, p3, p4, p5, p6, p7), w_a, sems)
        sums = [jnp.zeros((1, width), F32) for _ in range(3)]
        for rows in chunks(length):
            d_mid = d_second[rows, :] + (own[rows, :].astype(F32) + other[rows, :].astype(F32))
            hat = xhat[rows, :].astype(F32)
            d_first = norm_back_rows(d_mid, gain[0:1, :], hat, scale[rows, :])
            first_out[rows, :] = d_first
            low_out[rows, :] = d_first.astype(BF16)
            for n, item in enumerate((d_mid * hat, d_mid, d_first)):
                sums[n] = sums[n] + jnp.sum(item, 0, keepdims=True)
        for n in range(3):
            vec_out[n : n + 1, :] = sums[n]
        wait_all(waits)
        for j in range(2):
            for rows in chunks(length, 256):
                d_ctx[rows, j * cols : (j + 1) * cols] = nn(low_out[rows, :], w_a[j, :, three:]).astype(BF16)
        k_t = jnp.concatenate(
            [qkv[:, j * three + cols : j * three + 2 * cols].astype(F32) for j in range(2)], 1
        ).T.astype(BF16)
        for h in range(heads):
            j, i = divmod(h, cols // HD)
            at = j * three + i * HD
            q_cols, k_cols, v_cols = (slice(at + n * cols, at + n * cols + HD) for n in range(3))
            for n, queries in enumerate(chunks(length, 256)):
                d_o = d_ctx[queries, h * HD : (h + 1) * HD]
                d_p = nt(qkv[:, v_cols], d_o)
                p = probs[h, :, queries]
                wide = p.astype(F32)
                d_s = (wide * (d_p - jnp.sum(wide * d_p, 0, keepdims=True))).astype(BF16)
                d_v = nn(p, d_o)
                d_k = nn(d_s, qkv[queries, q_cols])
                acc_v[...] = d_v if n == 0 else acc_v[...] + d_v
                acc_k[...] = d_k if n == 0 else acc_k[...] + d_k
                d_q = nn(k_t[h * HD : (h + 1) * HD], d_s)
                dqkv_out[queries, q_cols] = (d_q.T * 0.125).astype(BF16)
            dqkv_out[:, v_cols] = acc_v[...].astype(BF16)
            dqkv_out[:, k_cols] = (acc_k[...] * 0.125).astype(BF16)
        sum_out[...] = jnp.sum(dqkv_out[...].astype(F32), 0, keepdims=True)
        for rows in chunks(length, 256):
            part_out[rows, :] = (
                nt(dqkv_out[rows, :three], w_a[0, :, :three]) + nt(dqkv_out[rows, three:], w_a[1, :, :three])
            ).astype(BF16)

    return pl.pallas_call(
        body,
        out_shape=[
            sds((length, width), BF16), sds((length, width), F32), sds((length, width), BF16),
            sds((length, 2 * three), BF16), sds((3, width), F32), sds((1, 2 * three), F32),
        ],
        in_specs=[SM] + [VM] * 8 + [ANY] * 8,
        out_specs=[VM] * 6,
        scratch_shapes=[
            pltpu.VMEM((2, width, four), BF16), pltpu.VMEM((length, 2 * cols), BF16),
            pltpu.VMEM((length, HD), F32), pltpu.VMEM((length, HD), F32),
            pltpu.SemaphoreType.DMA((4 * half,)),
        ],
        compiler_params=params(),
        cost_estimate=takes(15),
        name="attn_backward",
    )(meta, d_second, *parts, xhat, scale, gains, qkv, probs, *pieces)


def attn_grads(meta, x, d_attn, d_qkv, ctx, nz):
    length, width = x.shape
    three = d_qkv.shape[1] // 2
    cols = ctx.shape[1] // 2
    rz = width // nz

    def body(meta, x, d_attn, d_qkv, ctx, *refs):
        outs, (x_t, a_t) = refs[:4], refs[4:]
        x_t[...] = x[...].astype(F32).T.astype(BF16)
        a_t[...] = d_attn[...].astype(F32).T.astype(BF16)
        for j in range(2):
            for k in range(nz):
                rows = zrows(meta, k, rz)
                out, at = outs[2 * j + k // (nz // 2)], k % (nz // 2)
                out[at, :, :three] = nn(x_t[rows, :], d_qkv[:, j * three : (j + 1) * three]).astype(BF16)
                out[at, :, three:] = nn(a_t[rows, :], ctx[:, j * cols : (j + 1) * cols]).astype(BF16)

    return pl.pallas_call(
        body,
        out_shape=[sds((nz // 2, rz, three + cols), BF16)] * 4,
        in_specs=[SM] + [VM] * 4,
        out_specs=[VM] * 4,
        scratch_shapes=[pltpu.VMEM((width, length), BF16)] * 2,
        compiler_params=params(),
        cost_estimate=takes(4),
        name="attn_grads",
    )(meta, x, d_attn, d_qkv, ctx)


def loss_kernel(own, perm, slots, queries, positive_col, n_own):
    n_q, width = queries.shape
    n_p = slots.shape[0]

    def body(own, perm, slots, queries, pos, loss_out, d_out):
        passages = nn(perm[...], slots[...]).astype(BF16)
        logits = nt(queries[...], passages)
        top = jnp.max(logits, -1, keepdims=True)
        log_total = top + jnp.log(jnp.sum(jnp.exp(logits - top), -1, keepdims=True))
        index = lax.broadcasted_iota(jnp.int32, (n_q, n_p), 1)
        hits = pos[...] == index
        chosen = jnp.sum(jnp.where(hits, logits, 0.0), -1, keepdims=True)
        loss_out[...] = jnp.sum(log_total - chosen, 0, keepdims=True) / n_q
        d_logits = (16.0 * (jnp.exp(logits - log_total) - jnp.where(hits, 1.0, 0.0))).astype(BF16)
        pick = jnp.where(
            lax.broadcasted_iota(jnp.int32, (n_p, 128), 0)
            == lax.broadcasted_iota(jnp.int32, (n_p, 128), 1) + own[0],
            1.0, 0.0,
        ).astype(BF16)
        cols = nn(d_logits, pick)
        d_out[...] = nn(cols.T.astype(BF16), queries[...])[:n_own]

    return pl.pallas_call(
        body,
        out_shape=[sds((1, 1), F32), sds((n_own, width), F32)],
        in_specs=[SM] + [VM] * 4,
        out_specs=[VM] * 2,
        compiler_params=params(),
        cost_estimate=takes(1),
        name="contrast",
    )(own, perm, slots, queries, positive_col)


def on_device(
    inputs, cls_pos, w_qkv, qv_bias, w_out, w_in, in_bias, w_ffn_out,
    layer_gains, shifts, queries, positive, token_grad,
):
    core = lax.axis_index("section")
    dp = lax.axis_index("dp")
    me = lax.axis_index("tensor")
    n_dp = lax.axis_size("dp")
    n_t = lax.axis_size("tensor")
    first_core = core == 0
    rows_dev, share, width = inputs.shape
    cols = w_qkv.shape[3]
    units = w_in.shape[2]
    length = n_t * share
    n_chips = n_dp * n_t
    piece = width // n_chips
    order = dp_order()
    direct = direct_dp()
    nz = 4 if direct else 2
    t_ids = jnp.arange(n_t, dtype=jnp.int32)

    vec = jnp.concatenate(
        [layer_gains.reshape(-1), shifts.reshape(-1), qv_bias.reshape(-1), in_bias.reshape(-1)]
    )
    n_gain, n_shift, n_qv, n_inb = layer_gains.size, shifts.size, qv_bias.size, in_bias.size
    n_vec = vec.shape[0]
    flat = jnp.concatenate(
        [vec, queries.reshape(-1), (positive // 16).astype(BF16), (positive % 16).astype(BF16)]
    )
    flat = jnp.pad(flat, (0, -flat.shape[0] % 2048)).reshape(-1, 128)
    message = gather_small(flat)

    def spread_rows(block):
        parts = [lax.dynamic_index_in_dim(block, me ^ k, 0, keepdims=False) for k in range(n_t)]
        return jnp.concatenate([parts[0]] + [hop(parts[k], "tensor", k) for k in range(1, n_t)], 0)

    x_low = spread_rows(inputs)

    pack_a = jnp.concatenate([w_qkv[0, :, 0], w_qkv[0, :, 1], w_qkv[0, :, 2], w_out[0].T], 1)
    pack_b = jnp.concatenate([w_in[0], w_ffn_out[0].T], 1)
    z_a0 = gather_dp(after(pack_a, message), 0)
    z_b0 = gather_dp(after(pack_b, z_a0), 0)
    a0 = gather_layer(after(z_a0, x_low), 0)
    z_a1 = gather_dp(after(pack_a, z_b0), 1)
    b0 = gather_layer(after(z_b0, a0[3], a0[5]), 0)
    z_b1 = gather_dp(after(pack_b, z_a1), 1)
    a1 = gather_layer(after(z_a1, b0[3], b0[5]), 1)
    b1 = gather_layer(after(z_b1, a1[3], a1[5]), 1)
    pieces_a, pieces_b = (a0, a1), (b0, b1)

    zrow = order * (width // n_dp) if direct else jnp.arange(2, dtype=jnp.int32) * (width // 2)
    metas = [
        jnp.concatenate([(core == level)[None].astype(jnp.int32), zrow.astype(jnp.int32)])
        for level in range(2)
    ]
    slots = [me ^ (2 * (core != level) + jnp.arange(2, dtype=jnp.int32)) for level in range(2)]
    hots = [(s[:, None] == t_ids[None, :]).astype(F32) for s in slots]

    positions = jnp.concatenate(
        [(me ^ k) * share + jnp.arange(share, dtype=jnp.int32) for k in range(n_t)]
    )
    cls_row = lax.dynamic_index_in_dim(cls_pos, me, 0, keepdims=False)
    segments = jnp.sum((positions[:, None] >= cls_row[None, :]).astype(jnp.int32), -1)
    seg_col, seg_row = segments[:, None], segments[None, :]
    tok_col, tok_row = positions[:, None], positions[None, :]

    slot_ids = (order[None, :] * n_t + (me ^ t_ids)[:, None]).reshape(-1)
    to_natural = (jnp.arange(n_chips, dtype=jnp.int32)[:, None] == slot_ids[None, :]).astype(BF16)
    table = nn(to_natural, message.reshape(n_chips, -1))
    own_table = table[:, :n_vec].astype(BF16)
    other_table = swap_cores(own_table)
    tables = jnp.where(
        first_core, jnp.stack([own_table, other_table]), jnp.stack([other_table, own_table])
    ).astype(F32)
    at = 0
    gains = tables[:, :, at : at + n_gain].reshape(2, n_chips, 2, piece).transpose(0, 2, 1, 3).reshape(2, 2, width)
    at += n_gain
    shift = tables[:, :, at : at + n_shift].reshape(2, n_chips, 4, piece).transpose(0, 2, 1, 3).reshape(2, 4, width)
    at += n_shift
    qv = tables[:, :, at : at + n_qv].reshape(2, n_dp, n_t, 2, cols // n_dp)
    qv = qv.transpose(0, 3, 2, 1, 4).reshape(2, 2, n_t, cols)
    at += n_qv
    inb = tables[:, :, at : at + n_inb].reshape(2, n_dp, n_t, n_inb).transpose(0, 2, 1, 3).reshape(2, n_t, units)
    vectors = []
    for level in range(2):
        bias = jnp.sum(hots[level][None, :, :, None] * qv[level][:, None], 2)
        bias = jnp.stack([bias[0], jnp.zeros_like(bias[0]), bias[1]], 1).reshape(1, -1)
        bias_in = jnp.sum(hots[level][:, :, None] * inb[level][None], 1).reshape(1, -1)
        vectors.append((gains[level], shift[level], bias, bias_in))
    at = n_vec
    q_dev = queries.shape[0]
    all_q = table[:, at : at + q_dev * width].reshape(-1, width).astype(BF16)
    at += q_dev * width
    all_pos = table[:, at : at + q_dev] * 16.0 + table[:, at + q_dev : at + 2 * q_dev]
    all_pos = all_pos.astype(jnp.int32).reshape(-1, 1)
    n_cls = cls_row.shape[0]
    perm = jnp.repeat(jnp.repeat(to_natural, n_cls, 0), n_cls, 1)
    perm = perm * jnp.tile(jnp.eye(n_cls, dtype=BF16), (n_chips, n_chips))

    vectors, all_q, all_pos, perm, x_low = lax.optimization_barrier(
        (vectors, all_q, all_pos, perm, x_low)
    )
    saved = []
    source, parts, norms = after(x_low, z_b0), None, None
    for level in range(2):
        gain, shift, bias, bias_in = vectors[level]
        outs = attn_forward(
            level, metas[level], source, parts, norms, pieces_a[level], bias, seg_col, seg_row
        )
        part, qkv, probs, ctx = outs[:4]
        if level:
            x, xhat2, scale2 = outs[4:]
            saved[0]["second"] = (xhat2, scale2)
        else:
            x = x_low
        part, mid, xhat1, scale1, act, slope = ffn_forward(
            metas[level], after(x, z_a1) if level == 0 else x, (part, swap_cores(part)), gain, shift,
            pieces_b[level], bias_in,
        )
        saved.append(
            dict(x=x, qkv=qkv, probs=probs, ctx=ctx, mid=mid, xhat1=xhat1, scale1=scale1, act=act, slope=slope)
        )
        source, parts, norms = mid, (part, swap_cores(part)), (gain, shift)
        source = after(source, z_b1) if level == 0 else source
    tokens = spread_rows(token_grad)
    y, xhat2, scale2, cls_own = last_norm(after(source, tokens), parts, *norms, tok_row, cls_row)
    saved[1]["second"] = (xhat2, scale2)

    cls_slots = gather_small(cls_own).reshape(n_chips * n_cls, width)
    first_own = ((dp * n_t + me) * n_cls).astype(jnp.int32)[None]
    mean_loss, d_cls = loss_kernel(first_own, perm, cls_slots, all_q, all_pos, n_cls)

    def send_rows(block, section):
        low = block.astype(BF16).reshape(n_t, share, width)
        return [core_hop(low[k], "tensor", k, section) for k in range(1, n_t)]

    y_rows = send_rows(after(y, d_cls), 1)

    vector_rows = [None, None]
    sources = (tokens, d_cls, tok_col, cls_row)
    sums_a, sums_b = [None, None], [None, None]
    for level in (1, 0):
        gain = vectors[level][0]
        kept = saved[level]
        meta = metas[level]
        xhat2, scale2 = kept["second"]
        if level == 0:
            sources = (after(sources[0], *sums_b[1].first), *sources[1:])
        part, d_second, d_ffn, d_pre, vec2, sum_inb = ffn_backward(
            level, meta, sources, xhat2, scale2, gain, kept["slope"], pieces_b[level]
        )
        other = swap_cores(part)
        if level == 0:
            d_ffn = after(d_ffn, *sums_b[1].second())
        grads_b = ffn_grads(meta, kept["mid"], d_pre, d_ffn, kept["act"], nz)
        sums_b[level] = Reduction(grads_b, level)
        d_second = after(d_second, grads_b[0])
        if level == 0:
            d_second = after(d_second, *sums_a[1].first)
        part, d_first, d_attn, d_qkv, vec1, sum_qkv = attn_backward(
            meta, d_second, (part, other), kept["xhat1"], kept["scale1"], gain,
            kept["qkv"], kept["probs"], pieces_a[level],
        )
        other = swap_cores(part)
        if level == 0:
            d_attn = after(d_attn, *sums_a[1].second(), *sums_b[0].first)
        grads_a = attn_grads(meta, kept["x"], d_attn, d_qkv, kept["ctx"], nz)
        sums_a[level] = Reduction(grads_a, level)
        vector_rows[level] = (vec1, vec2, sum_qkv, sum_inb)
        sources = (d_first, part, other)
    d_hidden = d_first + (part.astype(F32) + other.astype(F32))
    h_rows = send_rows(d_hidden, 0)
    sums_b[0].second()
    sums_a[0].second()
    tot_b = jnp.where(first_core, sums_b[0].third(), sums_b[1].third())
    tot_a = jnp.where(first_core, sums_a[0].third(), sums_a[1].third())

    vector_rows, _ = lax.optimization_barrier((vector_rows, sums_a[0].first))

    def vector_table(level):
        vec1, vec2, sum_qkv, sum_inb = vector_rows[level]
        gs = jnp.concatenate([vec1[0:1], vec2[0:1], vec1[2:3], vec1[1:2], vec2[2:3], vec2[1:2]])
        gs = (0.5 * gs).reshape(6, n_chips, piece).transpose(1, 0, 2).reshape(n_chips, -1)
        qv = sum_qkv.reshape(2, 3, cols)
        qv = jnp.stack([qv[:, 0], qv[:, 2]])
        qv = jnp.sum(hots[level][None, :, :, None] * qv[:, :, None, :], 1)
        qv = qv.reshape(2, n_t, n_dp, -1).transpose(2, 1, 0, 3).reshape(n_chips, -1)
        inb = jnp.sum(hots[level][:, :, None] * sum_inb.reshape(2, 1, units), 0)
        inb = inb.reshape(n_t, n_dp, n_inb).transpose(1, 0, 2).reshape(n_chips, -1)
        return jnp.concatenate([gs, qv, inb], 1)

    rows0, rows1 = vector_table(0), vector_table(1)
    flat = jnp.where(first_core, rows0, rows1) + swap_cores(jnp.where(first_core, rows1, rows0))
    flat = lax.dot_general(
        to_natural.astype(F32), flat, (((0,), (0,)), ((), ())), precision=lax.Precision.HIGHEST
    )
    flat = jnp.pad(flat, ((0, 0), (0, -flat.shape[1] % 1024))).reshape(n_t, n_dp, -1, 128)
    flat = flat[0] + sum(hop(flat[k], "tensor", k) for k in range(1, n_t))
    if direct:
        flat = flat[0] + sum(hop(flat[k], "dp", k) for k in range(1, 4))
    else:
        flat = lax.psum_scatter(flat, "dp", scatter_dimension=0, tiled=False)
    flat = flat.reshape(-1)
    at = 0
    grad_gains = flat[at : at + n_gain].reshape(layer_gains.shape)
    at += n_gain
    grad_shifts = flat[at : at + n_shift].reshape(shifts.shape)
    at += n_shift
    grad_qv = flat[at : at + n_qv].reshape(qv_bias.shape)
    at += n_qv
    grad_inb = flat[at : at + n_inb].reshape(in_bias.shape)

    grad_qkv = jnp.stack([tot_a[:, n * cols : (n + 1) * cols] for n in range(3)], 1)[None]
    grad_out = tot_a[:, 3 * cols :].T[None]
    grad_in = tot_b[:, :units][None]
    grad_ffn = tot_b[:, units:].T[None]
    tokens_out = [jnp.where(first_core, d_hidden[:share], y[:share].astype(F32))]
    tokens_out += [jnp.where(first_core, h, g).astype(F32) for h, g in zip(h_rows, y_rows)]
    boundary = jnp.zeros((n_t, share, width), F32)
    for k in range(n_t):
        boundary = lax.dynamic_update_index_in_dim(boundary, tokens_out[k], me ^ k, 0)
    return (
        grad_qkv, grad_qv, grad_out, grad_in, grad_inb, grad_ffn,
        grad_gains, grad_shifts, boundary[None], mean_loss.reshape(()),
    )


def solution(mesh):
    return jax.shard_map(
        on_device,
        mesh=mesh,
        in_specs=(
            P("dp", "tensor", None),
            P("dp", None),
            P("section", "dp", None, "tensor"),
            P("section", None, "tensor", "dp"),
            P("section", "tensor", "dp"),
            P("section", "dp", "tensor"),
            P("section", "tensor", "dp"),
            P("section", "tensor", "dp"),
            P("section", None, ("dp", "tensor")),
            P("section", None, ("dp", "tensor")),
            P(("dp", "tensor"), None),
            P(("dp", "tensor")),
            P("dp", "tensor", None),
        ),
        out_specs=(
            P("section", "dp", None, "tensor"),
            P("section", None, "tensor", "dp"),
            P("section", "tensor", "dp"),
            P("section", "dp", "tensor"),
            P("section", "tensor", "dp"),
            P("section", "tensor", "dp"),
            P("section", None, ("dp", "tensor")),
            P("section", None, ("dp", "tensor")),
            P("section", "dp", "tensor", None),
            P(),
        ),
        check_vma=False,
    )
```

```python
import jax
import jax.numpy as jnp
from jax import lax
from jax.experimental import pallas as pl
from jax.experimental.pallas import tpu as pltpu
from jax.sharding import PartitionSpec as P

HD = 64
PARTNER = 1
CROSS = 2
BF16 = jnp.bfloat16
F32 = jnp.float32


def mm(left, right, dims):
    return lax.dot_general(left, right, (dims, ((), ())), preferred_element_type=F32)


def nn(left, right):
    return mm(left, right, ((1,), (0,)))


def nt(left, right):
    return mm(left, right, ((1,), (1,)))


def after(block, *earlier):
    return lax.optimization_barrier((block, *earlier))[0]


def swap_cores(block):
    return lax.ppermute(block, "section", [(0, 1), (1, 0)])


def hop(block, axis, flip):
    return lax.ppermute(block, axis, [(i, i ^ flip) for i in range(lax.axis_size(axis))])


def core_hop(block, axis, flip, core):
    size = lax.axis_size(axis)
    route = [(core * size + i, core * size + (i ^ flip)) for i in range(size)]
    route += [((1 - core) * size + i, (1 - core) * size + i) for i in range(size)]
    return lax.ppermute(block, ("section", axis), route)


def cross_hop(block, source):
    size = lax.axis_size("tensor")
    route = [(source * size + i, (1 - source) * size + (i ^ CROSS)) for i in range(size)]
    return lax.ppermute(block, ("section", "tensor"), route)


def direct_dp():
    return lax.axis_size("dp") == 4


def dp_order():
    size = lax.axis_size("dp")
    if direct_dp():
        return lax.axis_index("dp") ^ jnp.arange(size, dtype=jnp.int32)
    return jnp.arange(size, dtype=jnp.int32)


def gather_small(block):
    if direct_dp():
        block = jnp.stack([block] + [hop(block, "dp", k) for k in range(1, 4)])
    else:
        block = lax.all_gather(block, "dp", axis=0, tiled=False)
    return jnp.stack([block] + [hop(block, "tensor", k) for k in range(1, lax.axis_size("tensor"))])


def gather_dp(block, core):
    if direct_dp():
        return [block] + [core_hop(block, "dp", k, core) for k in range(1, 4)]
    return [lax.all_gather(block, "dp", axis=0, tiled=True)]


def stack_dp(blocks, *earlier):
    blocks = after(blocks, *earlier)
    if len(blocks) > 1:
        return jnp.stack(blocks)
    return blocks[0].reshape(2, blocks[0].shape[0] // 2, blocks[0].shape[1])


def gather_near(own, core):
    return core_hop(own, "tensor", PARTNER, core), cross_hop(own, core)


def gather_both(near, far, core):
    half = near.shape[0] // 2
    return cross_hop(near[:half], core), core_hop(far[half:], "tensor", PARTNER, 1 - core)


def add_low(*items):
    total = items[0].astype(F32)
    for item in items[1:]:
        total = total + item.astype(F32)
    return total.astype(BF16)


class Reduction:
    def __init__(self, grads, core):
        self.core = core
        self.pair, self.next_b, self.own_b = grads
        self.got = cross_hop(self.pair, 1 - core)
        self.near_b = hop(self.next_b, "tensor", PARTNER)

    def first(self, *earlier):
        half = self.next_b.shape[0]
        pair, own_b, got, near_b = after((self.pair, self.own_b, self.got, self.near_b), *earlier)
        self.parts = (pair[half:], got[half:]), (own_b, near_b)
        self.added = add_low(pair[:half], got[:half]), add_low(own_b, near_b)
        self.near_a = core_hop(self.added[0], "tensor", PARTNER, self.core)
        self.far_b = cross_hop(self.added[1], 1 - self.core)
        return self.added

    def second(self, *earlier):
        near_a, far_b, (parts_a, parts_b) = after((self.near_a, self.far_b, self.parts), *earlier)
        a, b = self.sums = add_low(*parts_a, near_a), add_low(*parts_b, far_b)
        if direct_dp():
            self.pieces = [a[0]] + [
                core_hop(block, "dp", k, self.core) for k, block in ((1, a[1]), (2, b[0]), (3, b[1]))
            ]
        else:
            whole = jnp.concatenate([a, b]).reshape(-1, a.shape[2])
            self.pieces = [lax.psum_scatter(whole, "dp", scatter_dimension=0, tiled=True)]
        return self.sums

    def third(self, *earlier):
        self.total = sum(block.astype(F32) for block in after(self.pieces, *earlier))
        return self.total


VMEM_LIMIT = 48 * 1024 * 1024
CHUNK = 128


def takes(micros):
    return pl.CostEstimate(flops=int(micros * 1.1e9), bytes_accessed=0, transcendentals=0)


def params():
    return pltpu.CompilerParams(vmem_limit_bytes=VMEM_LIMIT)


ANY = pl.BlockSpec(memory_space=pl.ANY)
VM = pl.BlockSpec(memory_space=pltpu.VMEM)
SM = pl.BlockSpec(memory_space=pltpu.SMEM)


def sds(shape, dtype):
    return jax.ShapeDtypeStruct(shape, dtype)


def chunks(length, step=CHUNK):
    return [slice(i, i + step) for i in range(0, length, step)]


def norm_rows(z):
    centre = z - jnp.mean(z, -1, keepdims=True)
    spread = jnp.mean(centre * centre, -1, keepdims=True)
    scale = lax.rsqrt(spread + 1e-05)
    return centre * scale, scale


def norm_back_rows(d_out, gain, xhat, scale):
    g = d_out * gain
    m1 = jnp.mean(g, -1, keepdims=True)
    m2 = jnp.mean(g * xhat, -1, keepdims=True)
    return scale * (g - m1 - xhat * m2)


def gelu_parts(x):
    e = jnp.exp(-0.5 * x * x)
    t = 1.0 / (1.0 + 0.2316418882 * jnp.abs(x))
    poly = t * (
        0.127414796 + t * (-0.142248368 + t * (0.7107068705 + t * (-0.7265760135 + t * 0.5307027145)))
    )
    tail = poly * e
    cdf = jnp.where(x < 0.0, tail, 1.0 - tail)
    return x * cdf, cdf + x * e * 0.3989422804014327


def zrows(meta, k, rz):
    return pl.ds(pl.multiple_of(meta[1 + k], 64), rz)


def load_weights(meta, pieces, place, sems):
    own, near, far = pieces[:3]
    nz, rz, _ = own.shape
    half = nz // 2
    home = meta[0] == 1
    lists = None
    at = 0
    for j, mine in enumerate((own, near)):
        for k in range(nz):
            targets = place(j, zrows(meta, k, rz))
            lists = lists or [[] for _ in targets]
            for n, (dst, columns) in enumerate(targets):
                other = far.at[k, :, columns] if j == 0 else pieces[3 + k // half].at[k % half, :, columns]
                first = pltpu.make_async_copy(mine.at[k, :, columns], dst, sems.at[at])
                second = pltpu.make_async_copy(other, dst, sems.at[at])
                at += 1

                @pl.when(home)
                def _():
                    first.start()

                @pl.when(jnp.logical_not(home))
                def _():
                    second.start()

                lists[n].append(first)
    return lists


def wait_all(waits):
    for made in waits:
        made.wait()


def load_a(meta, pieces, w_a, sems):
    width = w_a.shape[2]
    return load_weights(meta, pieces, lambda j, rows: [(w_a.at[j, rows, :], pl.ds(0, width))], sems)[0]


def load_b(meta, pieces, w_i, w_f, sems):
    one = w_i.shape[1] // 2
    return load_weights(
        meta,
        pieces,
        lambda j, rows: [
            (w_i.at[rows, pl.ds(j * one, one)], pl.ds(0, one)),
            (w_f.at[rows, pl.ds(j * one, one)], pl.ds(one, one)),
        ],
        sems,
    )


def attn_forward(level, meta, x_or_mid, parts, norms, pieces, bias, seg_col, seg_row):
    nz, rz, four = pieces[0].shape
    length, width = x_or_mid.shape
    cols = four // 4
    three = 3 * cols
    heads = 2 * cols // HD

    def body(meta, *refs):
        refs = list(refs)
        src = refs.pop(0)
        if level:
            own, other, gain, shift = (refs.pop(0) for _ in range(4))
        pieces = [refs.pop(0) for _ in range(5)]
        bias, sc, sr = (refs.pop(0) for _ in range(3))
        part_out, qkv_out, probs_out, ctx_out = (refs.pop(0) for _ in range(4))
        if level:
            x_out, xhat_out, scale_out = (refs.pop(0) for _ in range(3))
        w_a, sems = refs
        waits = load_a(meta, pieces, w_a, sems)
        if level:
            for rows in chunks(length):
                z = src[rows, :] + (own[rows, :].astype(F32) + other[rows, :].astype(F32)) + shift[2:3, :]
                xhat, scale = norm_rows(z)
                x_out[rows, :] = (xhat * gain[1:2, :] + shift[3:4, :]).astype(BF16)
                xhat_out[rows, :] = xhat.astype(BF16)
                scale_out[rows, :] = scale
            x_ref = x_out
        else:
            x_ref = src
        wait_all(waits)
        for j in range(2):
            c = slice(j * three, (j + 1) * three)
            for rows in chunks(length, 256):
                qkv_out[rows, c] = (nn(x_ref[rows, :], w_a[j, :, :three]) + bias[:, c]).astype(BF16)
        v_t = jnp.concatenate(
            [qkv_out[:, j * three + 2 * cols : (j + 1) * three].astype(F32) for j in range(2)], 1
        ).T.astype(BF16)
        for queries in chunks(length, 256):
            same = sc[...] == sr[:, queries]
            outs = []
            for h in range(heads):
                j, i = divmod(h, cols // HD)
                at = j * three + i * HD
                q = qkv_out[queries, at : at + HD]
                k = qkv_out[:, at + cols : at + cols + HD]
                st = jnp.where(same, nt(k, q) * 0.125, -1e30)
                p = jnp.exp(st - jnp.max(st, 0, keepdims=True))
                p = (p * (1.0 / jnp.sum(p, 0, keepdims=True))).astype(BF16)
                probs_out[h, :, queries] = p
                outs.append(nn(v_t[h * HD : (h + 1) * HD], p))
            ctx = jnp.concatenate(outs, 0).T.astype(BF16)
            ctx_out[queries, :] = ctx
            part_out[queries, :] = (
                nt(ctx[:, :cols], w_a[0, :, three:]) + nt(ctx[:, cols:], w_a[1, :, three:])
            ).astype(BF16)

    outs = [
        sds((length, width), BF16), sds((length, 2 * three), BF16),
        sds((heads, length, length), BF16), sds((length, 2 * cols), BF16),
    ]
    args = [meta, x_or_mid]
    if level:
        args += [*parts, *norms]
        outs += [sds((length, width), BF16), sds((length, width), BF16), sds((length, 1), F32)]
    specs = [SM] + [VM] * (len(args) - 1) + [ANY] * 5 + [VM] * 3
    args += [*pieces, bias, seg_col, seg_row]
    return pl.pallas_call(
        body,
        out_shape=outs,
        in_specs=specs,
        out_specs=[VM] * len(outs),
        scratch_shapes=[pltpu.VMEM((2, width, four), BF16), pltpu.SemaphoreType.DMA((2 * nz,))],
        compiler_params=params(),
        cost_estimate=takes(13),
        name="attn_forward",
    )(*args)


def ffn_forward(meta, x, parts, gains, shifts, pieces, bias_in):
    nz, rz, units = pieces[0].shape
    length, width = x.shape

    def body(meta, x, own, other, gain, shift, p0, p1, p2, p3, p4, bias,
             part_out, mid_out, xhat_out, scale_out, act_out, slope_out, w_i, w_f, low, sems):
        first, second = load_b(meta, (p0, p1, p2, p3, p4), w_i, w_f, sems)
        for rows in chunks(length):
            z = x[rows, :].astype(F32) + (own[rows, :].astype(F32) + other[rows, :].astype(F32)) + shift[0:1, :]
            xhat, scale = norm_rows(z)
            mid = xhat * gain[0:1, :] + shift[1:2, :]
            mid_out[rows, :] = mid
            low[rows, :] = mid.astype(BF16)
            xhat_out[rows, :] = xhat.astype(BF16)
            scale_out[rows, :] = scale
        wait_all(first)
        for rows in chunks(length, 256):
            for c in chunks(units, 512):
                pre = nn(low[rows, :], w_i[:, c]) + bias[:, c]
                act, slope = gelu_parts(pre)
                act_out[rows, c] = act.astype(BF16)
                slope_out[rows, c] = slope.astype(BF16)
        wait_all(second)
        for rows in chunks(length, 256):
            part_out[rows, :] = nt(act_out[rows, :], w_f[...]).astype(BF16)

    return pl.pallas_call(
        body,
        out_shape=[
            sds((length, width), BF16), sds((length, width), F32), sds((length, width), BF16),
            sds((length, 1), F32), sds((length, units), BF16), sds((length, units), BF16),
        ],
        in_specs=[SM] + [VM] * 5 + [ANY] * 5 + [VM],
        out_specs=[VM] * 6,
        scratch_shapes=[
            pltpu.VMEM((width, units), BF16), pltpu.VMEM((width, units), BF16),
            pltpu.VMEM((length, width), BF16), pltpu.SemaphoreType.DMA((4 * nz,)),
        ],
        compiler_params=params(),
        cost_estimate=takes(9),
        name="ffn_forward",
    )(meta, x, *parts, gains, shifts, *pieces, bias_in)


def last_norm(mid, parts, gains, shifts, tok_row, cls_pos):
    length, width = mid.shape
    n_cls = cls_pos.shape[0]

    def body(cls, mid, own, other, gain, shift, tok, y_out, xhat_out, scale_out, cls_out):
        for rows in chunks(length):
            z = mid[rows, :] + (own[rows, :].astype(F32) + other[rows, :].astype(F32)) + shift[2:3, :]
            xhat, scale = norm_rows(z)
            y_out[rows, :] = (xhat * gain[1:2, :] + shift[3:4, :]).astype(BF16)
            xhat_out[rows, :] = xhat.astype(BF16)
            scale_out[rows, :] = scale
        which = lax.broadcasted_iota(jnp.int32, (16, length), 0)
        hot = jnp.zeros((16, length), F32)
        for p in range(n_cls):
            hot = jnp.where(jnp.logical_and(which == p, tok[...] == cls[p]), 1.0, hot)
        cls_out[...] = nn(hot.astype(BF16), y_out[...])[:n_cls].astype(BF16)

    return pl.pallas_call(
        body,
        out_shape=[
            sds((length, width), BF16), sds((length, width), BF16), sds((length, 1), F32),
            sds((n_cls, width), BF16),
        ],
        in_specs=[SM] + [VM] * 6,
        out_specs=[VM] * 4,
        compiler_params=params(),
        cost_estimate=takes(2),
        name="last_norm",
    )(cls_pos, mid, *parts, gains, shifts, tok_row)


def ffn_backward(level, meta, sources, xhat, scale, gains, slope, pieces):
    nz, rz, units = pieces[0].shape
    length, width = xhat.shape
    n_cls = sources[3].shape[0] if level else 0

    def body(meta, *refs):
        refs = list(refs)
        if level:
            cls, grad, d_cls, tok = (refs.pop(0) for _ in range(4))
        else:
            d_above, own, other = (refs.pop(0) for _ in range(3))
        xhat, scale, gain, slope = (refs.pop(0) for _ in range(4))
        pieces = [refs.pop(0) for _ in range(5)]
        part_out, second_out, low_out, pre_out, vec_out, inb_out, w_i, w_f, sems = refs
        first, second = load_b(meta, pieces, w_i, w_f, sems)
        sums = [jnp.zeros((1, width), F32) for _ in range(3)]
        for rows in chunks(length):
            if level:
                d_out = grad[rows, :].astype(F32)
                for p in range(n_cls):
                    d_out = d_out + jnp.where(tok[rows, :] == cls[p], 1.0, 0.0) * d_cls[p : p + 1, :]
            else:
                d_out = d_above[rows, :] + (own[rows, :].astype(F32) + other[rows, :].astype(F32))
                d_out = d_out.astype(BF16).astype(F32)
            hat = xhat[rows, :].astype(F32)
            d_second = norm_back_rows(d_out, gain[1:2, :], hat, scale[rows, :])
            second_out[rows, :] = d_second
            low_out[rows, :] = d_second.astype(BF16)
            for n, item in enumerate((d_out * hat, d_out, d_second)):
                sums[n] = sums[n] + jnp.sum(item, 0, keepdims=True)
        for n in range(3):
            vec_out[n : n + 1, :] = sums[n]
        wait_all(second)
        for n, rows in enumerate(chunks(length, 256)):
            for c in chunks(units, units // 4):
                d_act = nn(low_out[rows, :], w_f[:, c])
                d_pre = (slope[rows, c].astype(F32) * d_act).astype(BF16)
                pre_out[rows, c] = d_pre
                j, at = divmod(c.start, units // 2)
                at = slice(at, at + c.stop - c.start)
                total = jnp.sum(d_pre.astype(F32), 0, keepdims=True)
                inb_out[j : j + 1, at] = total if n == 0 else inb_out[j : j + 1, at] + total
        wait_all(first)
        for rows in chunks(length, 256):
            part_out[rows, :] = nt(pre_out[rows, :], w_i[...]).astype(BF16)

    if level:
        token_grad, d_cls, tok_col, cls_pos = sources
        args, specs = [meta, cls_pos, token_grad, d_cls, tok_col], [SM, SM, VM, VM, VM]
    else:
        args, specs = [meta, *sources], [SM, VM, VM, VM]
    args += [xhat, scale, gains, slope, *pieces]
    specs += [VM] * 4 + [ANY] * 5
    return pl.pallas_call(
        body,
        out_shape=[
            sds((length, width), BF16), sds((length, width), F32), sds((length, width), BF16),
            sds((length, units), BF16), sds((3, width), F32), sds((2, units // 2), F32),
        ],
        in_specs=specs,
        out_specs=[VM] * 6,
        scratch_shapes=[
            pltpu.VMEM((width, units), BF16), pltpu.VMEM((width, units), BF16),
            pltpu.SemaphoreType.DMA((4 * nz,)),
        ],
        compiler_params=params(),
        cost_estimate=takes(9),
        name="ffn_backward",
    )(*args)


def halves_of(nz, rz, width):
    half = nz // 2
    return [sds((nz, rz, width), BF16), sds((half, rz, width), BF16), sds((half, rz, width), BF16)]


def place_half(outs, j, k, nz):
    half = nz // 2
    if k < half:
        return outs[0], k + (half if j == 0 else 0)
    return outs[2 if j == 0 else 1], k - half


def ffn_grads(meta, mid, d_pre, d_ffn, act, nz):
    length, width = mid.shape
    units = d_pre.shape[1]
    one = units // 2
    rz = width // nz

    def body(meta, mid, d_pre, d_ffn, act, *refs):
        outs, (mid_t, ffn_t) = refs[:3], refs[3:]
        mid_t[...] = mid[...].T.astype(BF16)
        ffn_t[...] = d_ffn[...].astype(F32).T.astype(BF16)
        for j in range(2):
            c = slice(j * one, (j + 1) * one)
            for k in range(nz):
                rows = zrows(meta, k, rz)
                out, at = place_half(outs, j, k, nz)
                out[at, :, :one] = nn(mid_t[rows, :], d_pre[:, c]).astype(BF16)
                out[at, :, one:] = nn(ffn_t[rows, :], act[:, c]).astype(BF16)

    return pl.pallas_call(
        body,
        out_shape=halves_of(nz, rz, units),
        in_specs=[SM] + [VM] * 4,
        out_specs=[VM] * 3,
        scratch_shapes=[pltpu.VMEM((width, length), BF16)] * 2,
        compiler_params=params(),
        cost_estimate=takes(7),
        name="ffn_grads",
    )(meta, mid, d_pre, d_ffn, act)


def attn_backward(meta, d_second, parts, xhat, scale, gains, qkv, probs, pieces):
    nz, rz, four = pieces[0].shape
    length, width = d_second.shape
    cols = four // 4
    three = 3 * cols
    heads = 2 * cols // HD

    def body(meta, d_second, own, other, xhat, scale, gain, qkv, probs, p0, p1, p2, p3, p4,
             part_out, first_out, low_out, dqkv_out, vec_out, sum_out,
             w_a, d_ctx, acc_v, acc_k, sems):
        waits = load_a(meta, (p0, p1, p2, p3, p4), w_a, sems)
        sums = [jnp.zeros((1, width), F32) for _ in range(3)]
        for rows in chunks(length):
            d_mid = d_second[rows, :] + (own[rows, :].astype(F32) + other[rows, :].astype(F32))
            hat = xhat[rows, :].astype(F32)
            d_first = norm_back_rows(d_mid, gain[0:1, :], hat, scale[rows, :])
            first_out[rows, :] = d_first
            low_out[rows, :] = d_first.astype(BF16)
            for n, item in enumerate((d_mid * hat, d_mid, d_first)):
                sums[n] = sums[n] + jnp.sum(item, 0, keepdims=True)
        for n in range(3):
            vec_out[n : n + 1, :] = sums[n]
        wait_all(waits)
        for j in range(2):
            for rows in chunks(length, 256):
                d_ctx[rows, j * cols : (j + 1) * cols] = nn(low_out[rows, :], w_a[j, :, three:]).astype(BF16)
        k_t = jnp.concatenate(
            [qkv[:, j * three + cols : j * three + 2 * cols].astype(F32) for j in range(2)], 1
        ).T.astype(BF16)
        for h in range(heads):
            j, i = divmod(h, cols // HD)
            at = j * three + i * HD
            q_cols, k_cols, v_cols = (slice(at + n * cols, at + n * cols + HD) for n in range(3))
            for n, queries in enumerate(chunks(length, 256)):
                d_o = d_ctx[queries, h * HD : (h + 1) * HD]
                d_p = nt(qkv[:, v_cols], d_o)
                p = probs[h, :, queries]
                wide = p.astype(F32)
                d_s = (wide * (d_p - jnp.sum(wide * d_p, 0, keepdims=True))).astype(BF16)
                d_v = nn(p, d_o)
                d_k = nn(d_s, qkv[queries, q_cols])
                acc_v[...] = d_v if n == 0 else acc_v[...] + d_v
                acc_k[...] = d_k if n == 0 else acc_k[...] + d_k
                d_q = nn(k_t[h * HD : (h + 1) * HD], d_s)
                dqkv_out[queries, q_cols] = (d_q.T * 0.125).astype(BF16)
            dqkv_out[:, v_cols] = acc_v[...].astype(BF16)
            dqkv_out[:, k_cols] = (acc_k[...] * 0.125).astype(BF16)
        for j in range(2):
            sum_out[j : j + 1, :] = jnp.sum(
                dqkv_out[:, j * three : (j + 1) * three].astype(F32), 0, keepdims=True
            )
        for rows in chunks(length, 256):
            part_out[rows, :] = (
                nt(dqkv_out[rows, :three], w_a[0, :, :three]) + nt(dqkv_out[rows, three:], w_a[1, :, :three])
            ).astype(BF16)

    return pl.pallas_call(
        body,
        out_shape=[
            sds((length, width), BF16), sds((length, width), F32), sds((length, width), BF16),
            sds((length, 2 * three), BF16), sds((3, width), F32), sds((2, three), F32),
        ],
        in_specs=[SM] + [VM] * 8 + [ANY] * 5,
        out_specs=[VM] * 6,
        scratch_shapes=[
            pltpu.VMEM((2, width, four), BF16), pltpu.VMEM((length, 2 * cols), BF16),
            pltpu.VMEM((length, HD), F32), pltpu.VMEM((length, HD), F32),
            pltpu.SemaphoreType.DMA((2 * nz,)),
        ],
        compiler_params=params(),
        cost_estimate=takes(15),
        name="attn_backward",
    )(meta, d_second, *parts, xhat, scale, gains, qkv, probs, *pieces)


def attn_grads(meta, x, d_attn, d_qkv, ctx, nz):
    length, width = x.shape
    three = d_qkv.shape[1] // 2
    cols = ctx.shape[1] // 2
    rz = width // nz

    def body(meta, x, d_attn, d_qkv, ctx, *refs):
        outs, (x_t, a_t) = refs[:3], refs[3:]
        x_t[...] = x[...].astype(F32).T.astype(BF16)
        a_t[...] = d_attn[...].astype(F32).T.astype(BF16)
        for j in range(2):
            for k in range(nz):
                rows = zrows(meta, k, rz)
                out, at = place_half(outs, j, k, nz)
                out[at, :, :three] = nn(x_t[rows, :], d_qkv[:, j * three : (j + 1) * three]).astype(BF16)
                out[at, :, three:] = nn(a_t[rows, :], ctx[:, j * cols : (j + 1) * cols]).astype(BF16)

    return pl.pallas_call(
        body,
        out_shape=halves_of(nz, rz, three + cols),
        in_specs=[SM] + [VM] * 4,
        out_specs=[VM] * 3,
        scratch_shapes=[pltpu.VMEM((width, length), BF16)] * 2,
        compiler_params=params(),
        cost_estimate=takes(4),
        name="attn_grads",
    )(meta, x, d_attn, d_qkv, ctx)


def loss_kernel(own, perm, slots, queries, positive_col, n_own):
    n_q, width = queries.shape
    n_p = slots.shape[0]

    def body(own, perm, slots, queries, pos, loss_out, d_out):
        passages = nn(perm[...], slots[...]).astype(BF16)
        logits = nt(queries[...], passages)
        top = jnp.max(logits, -1, keepdims=True)
        log_total = top + jnp.log(jnp.sum(jnp.exp(logits - top), -1, keepdims=True))
        index = lax.broadcasted_iota(jnp.int32, (n_q, n_p), 1)
        hits = pos[...] == index
        chosen = jnp.sum(jnp.where(hits, logits, 0.0), -1, keepdims=True)
        loss_out[...] = jnp.sum(log_total - chosen, 0, keepdims=True) / n_q
        d_logits = (16.0 * (jnp.exp(logits - log_total) - jnp.where(hits, 1.0, 0.0))).astype(BF16)
        pick = jnp.where(
            lax.broadcasted_iota(jnp.int32, (n_p, 128), 0)
            == lax.broadcasted_iota(jnp.int32, (n_p, 128), 1) + own[0],
            1.0, 0.0,
        ).astype(BF16)
        cols = nn(d_logits, pick)
        d_out[...] = nn(cols.T.astype(BF16), queries[...])[:n_own]

    return pl.pallas_call(
        body,
        out_shape=[sds((1, 1), F32), sds((n_own, width), F32)],
        in_specs=[SM] + [VM] * 4,
        out_specs=[VM] * 2,
        compiler_params=params(),
        cost_estimate=takes(1),
        name="contrast",
    )(own, perm, slots, queries, positive_col)


def on_device(
    inputs, cls_pos, w_qkv, qv_bias, w_out, w_in, in_bias, w_ffn_out,
    layer_gains, shifts, queries, positive, token_grad,
):
    core = lax.axis_index("section")
    dp = lax.axis_index("dp")
    me = lax.axis_index("tensor")
    n_dp = lax.axis_size("dp")
    n_t = lax.axis_size("tensor")
    first_core = core == 0
    rows_dev, share, width = inputs.shape
    cols = w_qkv.shape[3]
    units = w_in.shape[2]
    length = n_t * share
    n_chips = n_dp * n_t
    piece = width // n_chips
    order = dp_order()
    direct = direct_dp()
    nz = 4 if direct else 2
    t_ids = jnp.arange(n_t, dtype=jnp.int32)

    vec = jnp.concatenate(
        [layer_gains.reshape(-1), shifts.reshape(-1), qv_bias.reshape(-1), in_bias.reshape(-1)]
    )
    n_gain, n_shift, n_qv, n_inb = layer_gains.size, shifts.size, qv_bias.size, in_bias.size
    n_vec = vec.shape[0]
    flat = jnp.concatenate(
        [vec, queries.reshape(-1), (positive // 16).astype(BF16), (positive % 16).astype(BF16)]
    )
    flat = jnp.pad(flat, (0, -flat.shape[0] % 2048)).reshape(-1, 128)

    both = jnp.concatenate([inputs, token_grad], 1)
    both = [lax.dynamic_index_in_dim(both, me ^ k, 0, keepdims=False) for k in range(n_t)]
    both = [both[0]] + [hop(both[k], "tensor", k) for k in range(1, n_t)]
    x_low = jnp.concatenate([b[:share] for b in both], 0)
    tokens = jnp.concatenate([b[share:] for b in both], 0)

    pack_a = jnp.concatenate([w_qkv[0, :, 0], w_qkv[0, :, 1], w_qkv[0, :, 2], w_out[0].T], 1)
    pack_b = jnp.concatenate([w_in[0], w_ffn_out[0].T], 1)
    z_a0 = stack_dp(gather_dp(pack_a, 0))
    message = gather_small(after(flat, z_a0))
    z_b0 = stack_dp(gather_dp(after(pack_b, z_a0, message), 0))
    near_a0 = gather_near(after(z_a0, x_low, tokens), 0)
    a0 = [z_a0, *near_a0, *gather_both(*near_a0, 0)]
    near_b0 = gather_near(after(z_b0, a0), 0)
    dp_a1 = gather_dp(after(pack_a, z_b0), 1)

    zrow = order * (width // n_dp) if direct else jnp.arange(2, dtype=jnp.int32) * (width // 2)
    metas = [
        jnp.concatenate([(core == level)[None].astype(jnp.int32), zrow.astype(jnp.int32)])
        for level in range(2)
    ]
    slots = [me ^ (2 * (core != level) + jnp.arange(2, dtype=jnp.int32)) for level in range(2)]
    hots = [(s[:, None] == t_ids[None, :]).astype(F32) for s in slots]

    positions = jnp.concatenate(
        [(me ^ k) * share + jnp.arange(share, dtype=jnp.int32) for k in range(n_t)]
    )
    cls_row = lax.dynamic_index_in_dim(cls_pos, me, 0, keepdims=False)
    segments = jnp.sum((positions[:, None] >= cls_row[None, :]).astype(jnp.int32), -1)
    seg_col, seg_row = segments[:, None], segments[None, :]
    tok_col, tok_row = positions[:, None], positions[None, :]

    slot_ids = (order[None, :] * n_t + (me ^ t_ids)[:, None]).reshape(-1)
    to_natural = (jnp.arange(n_chips, dtype=jnp.int32)[:, None] == slot_ids[None, :]).astype(BF16)
    table = nn(to_natural, message.reshape(n_chips, -1))
    own_table = table[:, :n_vec].astype(BF16)
    other_table = swap_cores(own_table)
    tables = jnp.where(
        first_core, jnp.stack([own_table, other_table]), jnp.stack([other_table, own_table])
    ).astype(F32)
    at = 0
    gains = tables[:, :, at : at + n_gain].reshape(2, n_chips, 2, piece).transpose(0, 2, 1, 3).reshape(2, 2, width)
    at += n_gain
    shift = tables[:, :, at : at + n_shift].reshape(2, n_chips, 4, piece).transpose(0, 2, 1, 3).reshape(2, 4, width)
    at += n_shift
    qv = tables[:, :, at : at + n_qv].reshape(2, n_dp, n_t, 2, cols // n_dp)
    qv = qv.transpose(0, 3, 2, 1, 4).reshape(2, 2, n_t, cols)
    at += n_qv
    inb = tables[:, :, at : at + n_inb].reshape(2, n_dp, n_t, n_inb).transpose(0, 2, 1, 3).reshape(2, n_t, units)
    vectors = []
    for level in range(2):
        bias = jnp.sum(hots[level][None, :, :, None] * qv[level][:, None], 2)
        bias = jnp.stack([bias[0], jnp.zeros_like(bias[0]), bias[1]], 1).reshape(1, -1)
        bias_in = jnp.sum(hots[level][:, :, None] * inb[level][None], 1).reshape(1, -1)
        vectors.append((gains[level], shift[level], bias, bias_in))
    at = n_vec
    q_dev = queries.shape[0]
    all_q = table[:, at : at + q_dev * width].reshape(-1, width).astype(BF16)
    at += q_dev * width
    all_pos = table[:, at : at + q_dev] * 16.0 + table[:, at + q_dev : at + 2 * q_dev]
    all_pos = all_pos.astype(jnp.int32).reshape(-1, 1)
    n_cls = cls_row.shape[0]
    perm = jnp.repeat(jnp.repeat(to_natural, n_cls, 0), n_cls, 1)
    perm = perm * jnp.tile(jnp.eye(n_cls, dtype=BF16), (n_chips, n_chips))

    vectors, all_q, all_pos, perm, x_low = lax.optimization_barrier(
        (vectors, all_q, all_pos, perm, x_low)
    )
    saved = []
    source, parts, norms = after(x_low, z_b0), None, None
    pieces_a, pieces_b = [a0, None], [None, None]
    for level in range(2):
        gain, shift, bias, bias_in = vectors[level]
        outs = attn_forward(
            level, metas[level], source, parts, norms, pieces_a[level], bias, seg_col, seg_row
        )
        part, qkv, probs, ctx = outs[:4]
        if level == 0:
            z_a1 = stack_dp(dp_a1, part)
            near_a1 = gather_near(after(z_a1, near_b0), 1)
            dp_b1 = gather_dp(after(pack_b, z_a1), 1)
        z_b, near_b = (z_b0, near_b0) if level == 0 else (z_b1, near_b1)
        pieces_b[level] = [z_b, *near_b, *gather_both(*after(near_b, part), level)]
        if level:
            x, xhat2, scale2 = outs[4:]
            saved[0]["second"] = (xhat2, scale2)
        else:
            x = x_low
        part, mid, xhat1, scale1, act, slope = ffn_forward(
            metas[level], x, (part, swap_cores(part)), gain, shift, pieces_b[level], bias_in
        )
        saved.append(
            dict(x=x, qkv=qkv, probs=probs, ctx=ctx, mid=mid, xhat1=xhat1, scale1=scale1, act=act, slope=slope)
        )
        source, parts, norms = mid, (part, swap_cores(part)), (gain, shift)
        if level == 0:
            z_b1 = stack_dp(dp_b1, part)
            pieces_a[1] = [z_a1, *near_a1, *gather_both(*after(near_a1, part), 1)]
            near_b1 = gather_near(after(z_b1, pieces_a[1]), 1)
            source = after(source, z_b1)
    y, xhat2, scale2, cls_own = last_norm(source, parts, *norms, tok_row, cls_row)
    saved[1]["second"] = (xhat2, scale2)

    cls_slots = gather_small(cls_own).reshape(n_chips * n_cls, width)
    first_own = ((dp * n_t + me) * n_cls).astype(jnp.int32)[None]
    mean_loss, d_cls = loss_kernel(first_own, perm, cls_slots, all_q, all_pos, n_cls)

    vector_rows = [None, None]
    sources = (tokens, d_cls, tok_col, cls_row)
    sums_a, sums_b = [None, None], [None, None]
    for level in (1, 0):
        gain = vectors[level][0]
        kept = saved[level]
        meta = metas[level]
        xhat2, scale2 = kept["second"]
        if level == 0:
            sources = (after(sources[0], *sums_b[1].first(grads_a[1])), *sources[1:])
        part, d_second, d_ffn, d_pre, vec2, sum_inb = ffn_backward(
            level, meta, sources, xhat2, scale2, gain, kept["slope"], pieces_b[level]
        )
        other = swap_cores(part)
        grads_b = ffn_grads(meta, kept["mid"], d_pre, d_ffn, kept["act"], nz)
        sums_b[level] = Reduction(grads_b, level)
        d_second = after(d_second, grads_b[1])
        if level == 0:
            d_second = after(d_second, *sums_b[1].second(grads_b[1]), *sums_a[1].first(grads_b[1]))
        part, d_first, d_attn, d_qkv, vec1, sum_qkv = attn_backward(
            meta, d_second, (part, other), kept["xhat1"], kept["scale1"], gain,
            kept["qkv"], kept["probs"], pieces_a[level],
        )
        other = swap_cores(part)
        if level == 0:
            d_attn = after(d_attn, *sums_a[1].second(part), *sums_b[0].first(part))
        grads_a = attn_grads(meta, kept["x"], d_attn, d_qkv, kept["ctx"], nz)
        sums_a[level] = Reduction(grads_a, level)
        vector_rows[level] = (vec1, vec2, sum_qkv, sum_inb)
        sources = (d_first, part, other)
    sums_b[1].third(grads_a[1])
    sums_b[0].second(grads_a[1], sums_b[1].total)
    sums_a[1].third(*sums_b[0].sums)
    sums_a[0].first(*sums_b[0].sums)
    sums_a[0].second(sums_a[1].total)
    sums_b[0].third(*sums_a[0].sums)
    sums_a[0].third(sums_b[0].total)
    d_hidden = d_first + (part.astype(F32) + other.astype(F32))
    outgoing = jnp.where(first_core, d_hidden, y.astype(F32))
    low = outgoing.astype(BF16).reshape(n_t, share, width)
    incoming = [outgoing[:share]] + [hop(low[k], "tensor", k).astype(F32) for k in range(1, n_t)]
    boundary = jnp.zeros((n_t, share, width), F32)
    for k in range(n_t):
        boundary = lax.dynamic_update_index_in_dim(boundary, incoming[k], me ^ k, 0)
    tot_b = jnp.where(first_core, sums_b[0].total, sums_b[1].total)
    tot_a = jnp.where(first_core, sums_a[0].total, sums_a[1].total)

    vector_rows, _ = lax.optimization_barrier((vector_rows, sums_a[0].sums))
    wide = 3 * cols + units

    def vector_table(level):
        vec1, vec2, sum_qkv, sum_inb = vector_rows[level]
        by_t = lax.dot_general(
            hots[level], jnp.concatenate([sum_qkv, sum_inb], 1), (((0,), (0,)), ((), ())),
            precision=lax.Precision.HIGHEST,
        )
        whole = 0.5 * jnp.concatenate([vec1, vec2])
        return jnp.concatenate([jnp.pad(whole, ((0, 2), (0, wide - width))), by_t, jnp.zeros((4, wide), F32)])

    rows0, rows1 = vector_table(0), vector_table(1)
    flat = jnp.where(first_core, rows0, rows1) + swap_cores(jnp.where(first_core, rows1, rows0))
    flat = flat + sum(hop(flat, "tensor", k) for k in range(1, n_t))
    if direct:
        flat = flat + sum(hop(flat, "dp", k) for k in range(1, 4))
    else:
        flat = lax.psum(flat, "dp")
    own = lax.dynamic_slice_in_dim(flat[:6, :width], (dp * n_t + me) * piece, piece, 1)
    grad_gains = jnp.concatenate([own[0:1], own[3:4]]).reshape(layer_gains.shape)
    grad_shifts = jnp.concatenate([own[2:3], own[1:2], own[5:6], own[4:5]]).reshape(shifts.shape)
    by_t = lax.dynamic_slice_in_dim(flat, 8 + me, 1, 0)
    qv = jnp.concatenate([by_t[:, :cols], by_t[:, 2 * cols : 3 * cols]])
    grad_qv = lax.dynamic_slice_in_dim(qv, dp * qv_bias.shape[3], qv_bias.shape[3], 1).reshape(qv_bias.shape)
    grad_inb = lax.dynamic_slice_in_dim(by_t[:, 3 * cols :], dp * n_inb, n_inb, 1).reshape(in_bias.shape)

    grad_qkv = jnp.stack([tot_a[:, n * cols : (n + 1) * cols] for n in range(3)], 1)[None]
    grad_out = tot_a[:, 3 * cols :].T[None]
    grad_in = tot_b[:, :units][None]
    grad_ffn = tot_b[:, units:].T[None]
    return (
        grad_qkv, grad_qv, grad_out, grad_in, grad_inb, grad_ffn,
        grad_gains, grad_shifts, boundary[None], mean_loss.reshape(()),
    )


def solution(mesh):
    return jax.shard_map(
        on_device,
        mesh=mesh,
        in_specs=(
            P("dp", "tensor", None),
            P("dp", None),
            P("section", "dp", None, "tensor"),
            P("section", None, "tensor", "dp"),
            P("section", "tensor", "dp"),
            P("section", "dp", "tensor"),
            P("section", "tensor", "dp"),
            P("section", "tensor", "dp"),
            P("section", None, ("dp", "tensor")),
            P("section", None, ("dp", "tensor")),
            P(("dp", "tensor"), None),
            P(("dp", "tensor")),
            P("dp", "tensor", None),
        ),
        out_specs=(
            P("section", "dp", None, "tensor"),
            P("section", None, "tensor", "dp"),
            P("section", "tensor", "dp"),
            P("section", "dp", "tensor"),
            P("section", "tensor", "dp"),
            P("section", "tensor", "dp"),
            P("section", None, ("dp", "tensor")),
            P("section", None, ("dp", "tensor")),
            P("section", "dp", "tensor", None),
            P(),
        ),
        check_vma=False,
    )
```

```python
import jax
import jax.numpy as jnp
from jax import lax
from jax.experimental import pallas as pl
from jax.experimental.pallas import tpu as pltpu
from jax.sharding import PartitionSpec as P

HD = 64
PARTNER = 1
CROSS = 2
BF16 = jnp.bfloat16
F32 = jnp.float32


def mm(left, right, dims):
    return lax.dot_general(left, right, (dims, ((), ())), preferred_element_type=F32)


def nn(left, right):
    return mm(left, right, ((1,), (0,)))


def nt(left, right):
    return mm(left, right, ((1,), (1,)))


def after(block, *earlier):
    return lax.optimization_barrier((block, *earlier))[0]


def swap_cores(block):
    return lax.ppermute(block, "section", [(0, 1), (1, 0)])


def hop(block, axis, flip):
    return lax.ppermute(block, axis, [(i, i ^ flip) for i in range(lax.axis_size(axis))])


def core_hop(block, axis, flip, core):
    size = lax.axis_size(axis)
    route = [(core * size + i, core * size + (i ^ flip)) for i in range(size)]
    return lax.ppermute(block, ("section", axis), route)


def cross_hop(block, source):
    size = lax.axis_size("tensor")
    route = [(source * size + i, (1 - source) * size + (i ^ CROSS)) for i in range(size)]
    return lax.ppermute(block, ("section", "tensor"), route)


def direct_dp():
    return lax.axis_size("dp") == 4


def dp_order():
    size = lax.axis_size("dp")
    if direct_dp():
        return lax.axis_index("dp") ^ jnp.arange(size, dtype=jnp.int32)
    return jnp.arange(size, dtype=jnp.int32)


def gather_small(block):
    if direct_dp():
        block = jnp.stack([block] + [hop(block, "dp", k) for k in range(1, 4)])
    else:
        block = lax.all_gather(block, "dp", axis=0, tiled=False)
    return jnp.stack([block] + [hop(block, "tensor", k) for k in range(1, lax.axis_size("tensor"))])


def gather_dp(block, core):
    if direct_dp():
        return [block] + [core_hop(block, "dp", k, core) for k in range(1, 4)]
    return [lax.all_gather(block, "dp", axis=0, tiled=True)]


def stack_dp(blocks, *earlier):
    blocks = after(blocks, *earlier)
    if len(blocks) > 1:
        return jnp.stack(blocks)
    return blocks[0].reshape(2, blocks[0].shape[0] // 2, blocks[0].shape[1])


def gather_near(own, core):
    return core_hop(own, "tensor", PARTNER, core), cross_hop(own, core)


def gather_both(near, far, core):
    half = near.shape[0] // 2
    return cross_hop(near[:half], core), core_hop(far[half:], "tensor", PARTNER, 1 - core)


def add_low(*items):
    total = items[0].astype(F32)
    for item in items[1:]:
        total = total + item.astype(F32)
    return total.astype(BF16)


class Reduction:
    def __init__(self, grads, core):
        self.core = core
        self.pair, self.next_b, self.own_b = grads
        self.got = cross_hop(self.pair, 1 - core)
        self.near_b = hop(self.next_b, "tensor", PARTNER)

    def first(self, *earlier):
        half = self.next_b.shape[0]
        pair, own_b, got, near_b = after((self.pair, self.own_b, self.got, self.near_b), *earlier)
        self.parts = (pair[half:], got[half:]), (own_b, near_b)
        self.added = add_low(pair[:half], got[:half]), add_low(own_b, near_b)
        self.near_a = core_hop(self.added[0], "tensor", PARTNER, self.core)
        self.far_b = cross_hop(self.added[1], 1 - self.core)
        return self.added

    def second(self, *earlier):
        near_a, far_b, (parts_a, parts_b) = after((self.near_a, self.far_b, self.parts), *earlier)
        a, b = self.sums = add_low(*parts_a, near_a), add_low(*parts_b, far_b)
        if direct_dp():
            self.pieces = [a[0]] + [
                core_hop(block, "dp", k, self.core) for k, block in ((1, a[1]), (2, b[0]), (3, b[1]))
            ]
        else:
            whole = jnp.concatenate([a, b]).reshape(-1, a.shape[2])
            self.pieces = [lax.psum_scatter(whole, "dp", scatter_dimension=0, tiled=True)]
        return self.sums

    def third(self, *earlier):
        self.total = sum(block.astype(F32) for block in after(self.pieces, *earlier))
        return self.total


VMEM_LIMIT = 48 * 1024 * 1024
CHUNK = 128


def takes(micros):
    return pl.CostEstimate(flops=int(micros * 1.1e9), bytes_accessed=0, transcendentals=0)


def params():
    return pltpu.CompilerParams(vmem_limit_bytes=VMEM_LIMIT)


ANY = pl.BlockSpec(memory_space=pl.ANY)
VM = pl.BlockSpec(memory_space=pltpu.VMEM)
SM = pl.BlockSpec(memory_space=pltpu.SMEM)


def sds(shape, dtype):
    return jax.ShapeDtypeStruct(shape, dtype)


def chunks(length, step=CHUNK):
    return [slice(i, i + step) for i in range(0, length, step)]


def norm_rows(z):
    centre = z - jnp.mean(z, -1, keepdims=True)
    spread = jnp.mean(centre * centre, -1, keepdims=True)
    scale = lax.rsqrt(spread + 1e-05)
    return centre * scale, scale


def norm_back_rows(d_out, gain, xhat, scale):
    g = d_out * gain
    m1 = jnp.mean(g, -1, keepdims=True)
    m2 = jnp.mean(g * xhat, -1, keepdims=True)
    return scale * (g - m1 - xhat * m2)


def gelu_parts(x):
    e = jnp.exp(-0.5 * x * x)
    t = 1.0 / (1.0 + 0.2316418882 * jnp.abs(x))
    poly = t * (
        0.127414796 + t * (-0.142248368 + t * (0.7107068705 + t * (-0.7265760135 + t * 0.5307027145)))
    )
    tail = poly * e
    cdf = jnp.where(x < 0.0, tail, 1.0 - tail)
    return x * cdf, cdf + x * e * 0.3989422804014327


def zrows(meta, k, rz):
    return pl.ds(pl.multiple_of(meta[1 + k], 64), rz)


def load_weights(meta, pieces, place, sems):
    own, near, far = pieces[:3]
    nz, rz, _ = own.shape
    half = nz // 2
    home = meta[0] == 1
    lists = None
    at = 0
    for j, mine in enumerate((own, near)):
        for k in range(nz):
            targets = place(j, zrows(meta, k, rz))
            lists = lists or [[] for _ in targets]
            for n, (dst, columns) in enumerate(targets):
                other = far.at[k, :, columns] if j == 0 else pieces[3 + k // half].at[k % half, :, columns]
                first = pltpu.make_async_copy(mine.at[k, :, columns], dst, sems.at[at])
                second = pltpu.make_async_copy(other, dst, sems.at[at])
                at += 1

                @pl.when(home)
                def _():
                    first.start()

                @pl.when(jnp.logical_not(home))
                def _():
                    second.start()

                lists[n].append(first)
    return lists


def wait_all(waits):
    for made in waits:
        made.wait()


def load_a(meta, pieces, w_a, sems):
    width = w_a.shape[2]
    return load_weights(meta, pieces, lambda j, rows: [(w_a.at[j, rows, :], pl.ds(0, width))], sems)[0]


def load_b(meta, pieces, w_i, w_f, sems):
    one = w_i.shape[1] // 2
    return load_weights(
        meta,
        pieces,
        lambda j, rows: [
            (w_i.at[rows, pl.ds(j * one, one)], pl.ds(0, one)),
            (w_f.at[rows, pl.ds(j * one, one)], pl.ds(one, one)),
        ],
        sems,
    )


def attn_forward(level, meta, x_or_mid, parts, norms, pieces, bias, seg_col, seg_row):
    nz, rz, four = pieces[0].shape
    length, width = x_or_mid.shape
    cols = four // 4
    three = 3 * cols
    heads = 2 * cols // HD

    def body(meta, *refs):
        refs = list(refs)
        src = refs.pop(0)
        if level:
            own, other, gain, shift = (refs.pop(0) for _ in range(4))
        pieces = [refs.pop(0) for _ in range(5)]
        bias, sc, sr = (refs.pop(0) for _ in range(3))
        part_out, qkv_out, probs_out, ctx_out = (refs.pop(0) for _ in range(4))
        if level:
            x_out, xhat_out, scale_out = (refs.pop(0) for _ in range(3))
        w_a, sems = refs
        waits = load_a(meta, pieces, w_a, sems)
        if level:
            for rows in chunks(length):
                z = src[rows, :] + (own[rows, :].astype(F32) + other[rows, :].astype(F32)) + shift[2:3, :]
                xhat, scale = norm_rows(z)
                x_out[rows, :] = (xhat * gain[1:2, :] + shift[3:4, :]).astype(BF16)
                xhat_out[rows, :] = xhat.astype(BF16)
                scale_out[rows, :] = scale
            x_ref = x_out
        else:
            x_ref = src
        wait_all(waits)
        for j in range(2):
            c = slice(j * three, (j + 1) * three)
            for rows in chunks(length, 256):
                qkv_out[rows, c] = (nn(x_ref[rows, :], w_a[j, :, :three]) + bias[:, c]).astype(BF16)
        v_t = jnp.concatenate(
            [qkv_out[:, j * three + 2 * cols : (j + 1) * three].astype(F32) for j in range(2)], 1
        ).T.astype(BF16)
        for queries in chunks(length, 256):
            same = sc[...] == sr[:, queries]
            outs = []
            for h in range(heads):
                j, i = divmod(h, cols // HD)
                at = j * three + i * HD
                q = qkv_out[queries, at : at + HD]
                k = qkv_out[:, at + cols : at + cols + HD]
                st = jnp.where(same, nt(k, q) * 0.125, -1e30)
                p = jnp.exp(st - jnp.max(st, 0, keepdims=True))
                p = (p * (1.0 / jnp.sum(p, 0, keepdims=True))).astype(BF16)
                probs_out[h, :, queries] = p
                outs.append(nn(v_t[h * HD : (h + 1) * HD], p))
            ctx = jnp.concatenate(outs, 0).T.astype(BF16)
            ctx_out[queries, :] = ctx
            part_out[queries, :] = (
                nt(ctx[:, :cols], w_a[0, :, three:]) + nt(ctx[:, cols:], w_a[1, :, three:])
            ).astype(BF16)

    outs = [
        sds((length, width), BF16), sds((length, 2 * three), BF16),
        sds((heads, length, length), BF16), sds((length, 2 * cols), BF16),
    ]
    args = [meta, x_or_mid]
    if level:
        args += [*parts, *norms]
        outs += [sds((length, width), BF16), sds((length, width), BF16), sds((length, 1), F32)]
    specs = [SM] + [VM] * (len(args) - 1) + [ANY] * 5 + [VM] * 3
    args += [*pieces, bias, seg_col, seg_row]
    return pl.pallas_call(
        body,
        out_shape=outs,
        in_specs=specs,
        out_specs=[VM] * len(outs),
        scratch_shapes=[pltpu.VMEM((2, width, four), BF16), pltpu.SemaphoreType.DMA((2 * nz,))],
        compiler_params=params(),
        cost_estimate=takes(13),
        name="attn_forward",
    )(*args)


def ffn_forward(meta, x, parts, gains, shifts, pieces, bias_in):
    nz, rz, units = pieces[0].shape
    length, width = x.shape

    def body(meta, x, own, other, gain, shift, p0, p1, p2, p3, p4, bias,
             part_out, mid_out, xhat_out, scale_out, act_out, slope_out, w_i, w_f, low, sems):
        first, second = load_b(meta, (p0, p1, p2, p3, p4), w_i, w_f, sems)
        for rows in chunks(length):
            z = x[rows, :].astype(F32) + (own[rows, :].astype(F32) + other[rows, :].astype(F32)) + shift[0:1, :]
            xhat, scale = norm_rows(z)
            mid = xhat * gain[0:1, :] + shift[1:2, :]
            mid_out[rows, :] = mid
            low[rows, :] = mid.astype(BF16)
            xhat_out[rows, :] = xhat.astype(BF16)
            scale_out[rows, :] = scale
        wait_all(first)
        for rows in chunks(length, 256):
            for c in chunks(units, 512):
                pre = nn(low[rows, :], w_i[:, c]) + bias[:, c]
                act, slope = gelu_parts(pre)
                act_out[rows, c] = act.astype(BF16)
                slope_out[rows, c] = slope.astype(BF16)
        wait_all(second)
        for rows in chunks(length, 256):
            part_out[rows, :] = nt(act_out[rows, :], w_f[...]).astype(BF16)

    return pl.pallas_call(
        body,
        out_shape=[
            sds((length, width), BF16), sds((length, width), F32), sds((length, width), BF16),
            sds((length, 1), F32), sds((length, units), BF16), sds((length, units), BF16),
        ],
        in_specs=[SM] + [VM] * 5 + [ANY] * 5 + [VM],
        out_specs=[VM] * 6,
        scratch_shapes=[
            pltpu.VMEM((width, units), BF16), pltpu.VMEM((width, units), BF16),
            pltpu.VMEM((length, width), BF16), pltpu.SemaphoreType.DMA((4 * nz,)),
        ],
        compiler_params=params(),
        cost_estimate=takes(9),
        name="ffn_forward",
    )(meta, x, *parts, gains, shifts, *pieces, bias_in)


def last_norm(mid, parts, gains, shifts, tok_row, cls_pos):
    length, width = mid.shape
    n_cls = cls_pos.shape[0]

    def body(cls, mid, own, other, gain, shift, tok, y_out, xhat_out, scale_out, cls_out):
        for rows in chunks(length):
            z = mid[rows, :] + (own[rows, :].astype(F32) + other[rows, :].astype(F32)) + shift[2:3, :]
            xhat, scale = norm_rows(z)
            y_out[rows, :] = (xhat * gain[1:2, :] + shift[3:4, :]).astype(BF16)
            xhat_out[rows, :] = xhat.astype(BF16)
            scale_out[rows, :] = scale
        which = lax.broadcasted_iota(jnp.int32, (16, length), 0)
        hot = jnp.zeros((16, length), F32)
        for p in range(n_cls):
            hot = jnp.where(jnp.logical_and(which == p, tok[...] == cls[p]), 1.0, hot)
        cls_out[...] = nn(hot.astype(BF16), y_out[...])[:n_cls].astype(BF16)

    return pl.pallas_call(
        body,
        out_shape=[
            sds((length, width), BF16), sds((length, width), BF16), sds((length, 1), F32),
            sds((n_cls, width), BF16),
        ],
        in_specs=[SM] + [VM] * 6,
        out_specs=[VM] * 4,
        compiler_params=params(),
        cost_estimate=takes(2),
        name="last_norm",
    )(cls_pos, mid, *parts, gains, shifts, tok_row)


def ffn_backward(level, meta, sources, xhat, scale, gains, slope, pieces):
    nz, rz, units = pieces[0].shape
    length, width = xhat.shape
    n_cls = sources[3].shape[0] if level else 0

    def body(meta, *refs):
        refs = list(refs)
        if level:
            cls, grad, d_cls, tok = (refs.pop(0) for _ in range(4))
        else:
            d_above, own, other = (refs.pop(0) for _ in range(3))
        xhat, scale, gain, slope = (refs.pop(0) for _ in range(4))
        pieces = [refs.pop(0) for _ in range(5)]
        part_out, second_out, low_out, pre_out, vec_out, inb_out, w_i, w_f, sems = refs
        first, second = load_b(meta, pieces, w_i, w_f, sems)
        sums = [jnp.zeros((1, width), F32) for _ in range(3)]
        for rows in chunks(length):
            if level:
                d_out = grad[rows, :].astype(F32)
                for p in range(n_cls):
                    d_out = d_out + jnp.where(tok[rows, :] == cls[p], 1.0, 0.0) * d_cls[p : p + 1, :]
            else:
                d_out = d_above[rows, :] + (own[rows, :].astype(F32) + other[rows, :].astype(F32))
                d_out = d_out.astype(BF16).astype(F32)
            hat = xhat[rows, :].astype(F32)
            d_second = norm_back_rows(d_out, gain[1:2, :], hat, scale[rows, :])
            second_out[rows, :] = d_second
            low_out[rows, :] = d_second.astype(BF16)
            for n, item in enumerate((d_out * hat, d_out, d_second)):
                sums[n] = sums[n] + jnp.sum(item, 0, keepdims=True)
        for n in range(3):
            vec_out[n : n + 1, :] = sums[n]
        wait_all(second)
        for n, rows in enumerate(chunks(length, 256)):
            for c in chunks(units, units // 4):
                d_act = nn(low_out[rows, :], w_f[:, c])
                d_pre = (slope[rows, c].astype(F32) * d_act).astype(BF16)
                pre_out[rows, c] = d_pre
                j, at = divmod(c.start, units // 2)
                at = slice(at, at + c.stop - c.start)
                total = jnp.sum(d_pre.astype(F32), 0, keepdims=True)
                inb_out[j : j + 1, at] = total if n == 0 else inb_out[j : j + 1, at] + total
        wait_all(first)
        for rows in chunks(length, 256):
            part_out[rows, :] = nt(pre_out[rows, :], w_i[...]).astype(BF16)

    if level:
        token_grad, d_cls, tok_col, cls_pos = sources
        args, specs = [meta, cls_pos, token_grad, d_cls, tok_col], [SM, SM, VM, VM, VM]
    else:
        args, specs = [meta, *sources], [SM, VM, VM, VM]
    args += [xhat, scale, gains, slope, *pieces]
    specs += [VM] * 4 + [ANY] * 5
    return pl.pallas_call(
        body,
        out_shape=[
            sds((length, width), BF16), sds((length, width), F32), sds((length, width), BF16),
            sds((length, units), BF16), sds((3, width), F32), sds((2, units // 2), F32),
        ],
        in_specs=specs,
        out_specs=[VM] * 6,
        scratch_shapes=[
            pltpu.VMEM((width, units), BF16), pltpu.VMEM((width, units), BF16),
            pltpu.SemaphoreType.DMA((4 * nz,)),
        ],
        compiler_params=params(),
        cost_estimate=takes(9),
        name="ffn_backward",
    )(*args)


def halves_of(nz, rz, width):
    half = nz // 2
    return [sds((nz, rz, width), BF16), sds((half, rz, width), BF16), sds((half, rz, width), BF16)]


def place_half(outs, j, k, nz):
    half = nz // 2
    if k < half:
        return outs[0], k + (half if j == 0 else 0)
    return outs[2 if j == 0 else 1], k - half


def ffn_grads(meta, mid, d_pre, d_ffn, act, nz):
    length, width = mid.shape
    units = d_pre.shape[1]
    one = units // 2
    rz = width // nz

    def body(meta, mid, d_pre, d_ffn, act, *refs):
        outs, (mid_t, ffn_t) = refs[:3], refs[3:]
        mid_t[...] = mid[...].T.astype(BF16)
        ffn_t[...] = d_ffn[...].astype(F32).T.astype(BF16)
        for j in range(2):
            c = slice(j * one, (j + 1) * one)
            for k in range(nz):
                rows = zrows(meta, k, rz)
                out, at = place_half(outs, j, k, nz)
                out[at, :, :one] = nn(mid_t[rows, :], d_pre[:, c]).astype(BF16)
                out[at, :, one:] = nn(ffn_t[rows, :], act[:, c]).astype(BF16)

    return pl.pallas_call(
        body,
        out_shape=halves_of(nz, rz, units),
        in_specs=[SM] + [VM] * 4,
        out_specs=[VM] * 3,
        scratch_shapes=[pltpu.VMEM((width, length), BF16)] * 2,
        compiler_params=params(),
        cost_estimate=takes(7),
        name="ffn_grads",
    )(meta, mid, d_pre, d_ffn, act)


def attn_backward(meta, d_second, parts, xhat, scale, gains, qkv, probs, pieces):
    nz, rz, four = pieces[0].shape
    length, width = d_second.shape
    cols = four // 4
    three = 3 * cols
    heads = 2 * cols // HD

    def body(meta, d_second, own, other, xhat, scale, gain, qkv, probs, p0, p1, p2, p3, p4,
             part_out, first_out, low_out, dqkv_out, vec_out, sum_out,
             w_a, d_ctx, acc_v, acc_k, sems):
        waits = load_a(meta, (p0, p1, p2, p3, p4), w_a, sems)
        sums = [jnp.zeros((1, width), F32) for _ in range(3)]
        for rows in chunks(length):
            d_mid = d_second[rows, :] + (own[rows, :].astype(F32) + other[rows, :].astype(F32))
            hat = xhat[rows, :].astype(F32)
            d_first = norm_back_rows(d_mid, gain[0:1, :], hat, scale[rows, :])
            first_out[rows, :] = d_first
            low_out[rows, :] = d_first.astype(BF16)
            for n, item in enumerate((d_mid * hat, d_mid, d_first)):
                sums[n] = sums[n] + jnp.sum(item, 0, keepdims=True)
        for n in range(3):
            vec_out[n : n + 1, :] = sums[n]
        wait_all(waits)
        for j in range(2):
            for rows in chunks(length, 256):
                d_ctx[rows, j * cols : (j + 1) * cols] = nn(low_out[rows, :], w_a[j, :, three:]).astype(BF16)
        k_t = jnp.concatenate(
            [qkv[:, j * three + cols : j * three + 2 * cols].astype(F32) for j in range(2)], 1
        ).T.astype(BF16)
        for h in range(heads):
            j, i = divmod(h, cols // HD)
            at = j * three + i * HD
            q_cols, k_cols, v_cols = (slice(at + n * cols, at + n * cols + HD) for n in range(3))
            for n, queries in enumerate(chunks(length, 256)):
                d_o = d_ctx[queries, h * HD : (h + 1) * HD]
                d_p = nt(qkv[:, v_cols], d_o)
                p = probs[h, :, queries]
                wide = p.astype(F32)
                d_s = (wide * (d_p - jnp.sum(wide * d_p, 0, keepdims=True))).astype(BF16)
                d_v = nn(p, d_o)
                d_k = nn(d_s, qkv[queries, q_cols])
                acc_v[...] = d_v if n == 0 else acc_v[...] + d_v
                acc_k[...] = d_k if n == 0 else acc_k[...] + d_k
                d_q = nn(k_t[h * HD : (h + 1) * HD], d_s)
                dqkv_out[queries, q_cols] = (d_q.T * 0.125).astype(BF16)
            dqkv_out[:, v_cols] = acc_v[...].astype(BF16)
            dqkv_out[:, k_cols] = (acc_k[...] * 0.125).astype(BF16)
        for j in range(2):
            sum_out[j : j + 1, :] = jnp.sum(
                dqkv_out[:, j * three : (j + 1) * three].astype(F32), 0, keepdims=True
            )
        for rows in chunks(length, 256):
            part_out[rows, :] = (
                nt(dqkv_out[rows, :three], w_a[0, :, :three]) + nt(dqkv_out[rows, three:], w_a[1, :, :three])
            ).astype(BF16)

    return pl.pallas_call(
        body,
        out_shape=[
            sds((length, width), BF16), sds((length, width), F32), sds((length, width), BF16),
            sds((length, 2 * three), BF16), sds((3, width), F32), sds((2, three), F32),
        ],
        in_specs=[SM] + [VM] * 8 + [ANY] * 5,
        out_specs=[VM] * 6,
        scratch_shapes=[
            pltpu.VMEM((2, width, four), BF16), pltpu.VMEM((length, 2 * cols), BF16),
            pltpu.VMEM((length, HD), F32), pltpu.VMEM((length, HD), F32),
            pltpu.SemaphoreType.DMA((2 * nz,)),
        ],
        compiler_params=params(),
        cost_estimate=takes(15),
        name="attn_backward",
    )(meta, d_second, *parts, xhat, scale, gains, qkv, probs, *pieces)


def attn_grads(meta, x, d_attn, d_qkv, ctx, nz):
    length, width = x.shape
    three = d_qkv.shape[1] // 2
    cols = ctx.shape[1] // 2
    rz = width // nz

    def body(meta, x, d_attn, d_qkv, ctx, *refs):
        outs, (x_t, a_t) = refs[:3], refs[3:]
        x_t[...] = x[...].astype(F32).T.astype(BF16)
        a_t[...] = d_attn[...].astype(F32).T.astype(BF16)
        for j in range(2):
            for k in range(nz):
                rows = zrows(meta, k, rz)
                out, at = place_half(outs, j, k, nz)
                out[at, :, :three] = nn(x_t[rows, :], d_qkv[:, j * three : (j + 1) * three]).astype(BF16)
                out[at, :, three:] = nn(a_t[rows, :], ctx[:, j * cols : (j + 1) * cols]).astype(BF16)

    return pl.pallas_call(
        body,
        out_shape=halves_of(nz, rz, three + cols),
        in_specs=[SM] + [VM] * 4,
        out_specs=[VM] * 3,
        scratch_shapes=[pltpu.VMEM((width, length), BF16)] * 2,
        compiler_params=params(),
        cost_estimate=takes(4),
        name="attn_grads",
    )(meta, x, d_attn, d_qkv, ctx)


def loss_kernel(own, perm, slots, queries, positive_col, n_own):
    n_q, width = queries.shape
    n_p = slots.shape[0]

    def body(own, perm, slots, queries, pos, loss_out, d_out):
        passages = nn(perm[...], slots[...]).astype(BF16)
        logits = nt(queries[...], passages)
        top = jnp.max(logits, -1, keepdims=True)
        log_total = top + jnp.log(jnp.sum(jnp.exp(logits - top), -1, keepdims=True))
        index = lax.broadcasted_iota(jnp.int32, (n_q, n_p), 1)
        hits = pos[...] == index
        chosen = jnp.sum(jnp.where(hits, logits, 0.0), -1, keepdims=True)
        loss_out[...] = jnp.sum(log_total - chosen, 0, keepdims=True) / n_q
        d_logits = (16.0 * (jnp.exp(logits - log_total) - jnp.where(hits, 1.0, 0.0))).astype(BF16)
        pick = jnp.where(
            lax.broadcasted_iota(jnp.int32, (n_p, 128), 0)
            == lax.broadcasted_iota(jnp.int32, (n_p, 128), 1) + own[0],
            1.0, 0.0,
        ).astype(BF16)
        cols = nn(d_logits, pick)
        d_out[...] = nn(cols.T.astype(BF16), queries[...])[:n_own]

    return pl.pallas_call(
        body,
        out_shape=[sds((1, 1), F32), sds((n_own, width), F32)],
        in_specs=[SM] + [VM] * 4,
        out_specs=[VM] * 2,
        compiler_params=params(),
        cost_estimate=takes(1),
        name="contrast",
    )(own, perm, slots, queries, positive_col)


def on_device(
    inputs, cls_pos, w_qkv, qv_bias, w_out, w_in, in_bias, w_ffn_out,
    layer_gains, shifts, queries, positive, token_grad,
):
    core = lax.axis_index("section")
    dp = lax.axis_index("dp")
    me = lax.axis_index("tensor")
    n_dp = lax.axis_size("dp")
    n_t = lax.axis_size("tensor")
    first_core = core == 0
    rows_dev, share, width = inputs.shape
    cols = w_qkv.shape[3]
    units = w_in.shape[2]
    length = n_t * share
    n_chips = n_dp * n_t
    piece = width // n_chips
    order = dp_order()
    direct = direct_dp()
    nz = 4 if direct else 2
    t_ids = jnp.arange(n_t, dtype=jnp.int32)

    vec = jnp.concatenate(
        [layer_gains.reshape(-1), shifts.reshape(-1), qv_bias.reshape(-1), in_bias.reshape(-1)]
    )
    n_gain, n_shift, n_qv, n_inb = layer_gains.size, shifts.size, qv_bias.size, in_bias.size
    n_vec = vec.shape[0]
    flat = jnp.concatenate(
        [vec, queries.reshape(-1), (positive // 16).astype(BF16), (positive % 16).astype(BF16)]
    )
    flat = jnp.pad(flat, (0, -flat.shape[0] % 2048)).reshape(-1, 128)

    both = jnp.concatenate([inputs, token_grad], 1)
    both = [lax.dynamic_index_in_dim(both, me ^ k, 0, keepdims=False) for k in range(n_t)]
    both = [both[0]] + [hop(both[k], "tensor", k) for k in range(1, n_t)]
    x_low = jnp.concatenate([b[:share] for b in both], 0)
    tokens = jnp.concatenate([b[share:] for b in both], 0)

    pack_a = jnp.concatenate([w_qkv[0, :, 0], w_qkv[0, :, 1], w_qkv[0, :, 2], w_out[0].T], 1)
    pack_b = jnp.concatenate([w_in[0], w_ffn_out[0].T], 1)
    z_a0 = stack_dp(gather_dp(pack_a, 0))
    message = gather_small(after(flat, z_a0))
    z_b0 = stack_dp(gather_dp(after(pack_b, z_a0, message), 0))
    near_a0 = gather_near(after(z_a0, x_low, tokens), 0)
    a0 = [z_a0, *near_a0, *gather_both(*near_a0, 0)]
    near_b0 = gather_near(after(z_b0, a0), 0)
    dp_a1 = gather_dp(after(pack_a, z_b0), 1)

    zrow = order * (width // n_dp) if direct else jnp.arange(2, dtype=jnp.int32) * (width // 2)
    metas = [
        jnp.concatenate([(core == level)[None].astype(jnp.int32), zrow.astype(jnp.int32)])
        for level in range(2)
    ]
    slots = [me ^ (2 * (core != level) + jnp.arange(2, dtype=jnp.int32)) for level in range(2)]
    hots = [(s[:, None] == t_ids[None, :]).astype(F32) for s in slots]

    positions = jnp.concatenate(
        [(me ^ k) * share + jnp.arange(share, dtype=jnp.int32) for k in range(n_t)]
    )
    cls_row = lax.dynamic_index_in_dim(cls_pos, me, 0, keepdims=False)
    segments = jnp.sum((positions[:, None] >= cls_row[None, :]).astype(jnp.int32), -1)
    seg_col, seg_row = segments[:, None], segments[None, :]
    tok_col, tok_row = positions[:, None], positions[None, :]

    slot_ids = (order[None, :] * n_t + (me ^ t_ids)[:, None]).reshape(-1)
    to_natural = (jnp.arange(n_chips, dtype=jnp.int32)[:, None] == slot_ids[None, :]).astype(BF16)
    table = nn(to_natural, message.reshape(n_chips, -1))
    own_table = table[:, :n_vec].astype(BF16)
    other_table = swap_cores(own_table)
    tables = jnp.where(
        first_core, jnp.stack([own_table, other_table]), jnp.stack([other_table, own_table])
    ).astype(F32)
    at = 0
    gains = tables[:, :, at : at + n_gain].reshape(2, n_chips, 2, piece).transpose(0, 2, 1, 3).reshape(2, 2, width)
    at += n_gain
    shift = tables[:, :, at : at + n_shift].reshape(2, n_chips, 4, piece).transpose(0, 2, 1, 3).reshape(2, 4, width)
    at += n_shift
    qv = tables[:, :, at : at + n_qv].reshape(2, n_dp, n_t, 2, cols // n_dp)
    qv = qv.transpose(0, 3, 2, 1, 4).reshape(2, 2, n_t, cols)
    at += n_qv
    inb = tables[:, :, at : at + n_inb].reshape(2, n_dp, n_t, n_inb).transpose(0, 2, 1, 3).reshape(2, n_t, units)
    vectors = []
    for level in range(2):
        bias = jnp.sum(hots[level][None, :, :, None] * qv[level][:, None], 2)
        bias = jnp.stack([bias[0], jnp.zeros_like(bias[0]), bias[1]], 1).reshape(1, -1)
        bias_in = jnp.sum(hots[level][:, :, None] * inb[level][None], 1).reshape(1, -1)
        vectors.append((gains[level], shift[level], bias, bias_in))
    at = n_vec
    q_dev = queries.shape[0]
    all_q = table[:, at : at + q_dev * width].reshape(-1, width).astype(BF16)
    at += q_dev * width
    all_pos = table[:, at : at + q_dev] * 16.0 + table[:, at + q_dev : at + 2 * q_dev]
    all_pos = all_pos.astype(jnp.int32).reshape(-1, 1)
    n_cls = cls_row.shape[0]
    perm = jnp.repeat(jnp.repeat(to_natural, n_cls, 0), n_cls, 1)
    perm = perm * jnp.tile(jnp.eye(n_cls, dtype=BF16), (n_chips, n_chips))

    vectors, all_q, all_pos, perm, x_low = lax.optimization_barrier(
        (vectors, all_q, all_pos, perm, x_low)
    )
    saved = []
    source, parts, norms = after(x_low, z_b0), None, None
    pieces_a, pieces_b = [a0, None], [None, None]
    for level in range(2):
        gain, shift, bias, bias_in = vectors[level]
        outs = attn_forward(
            level, metas[level], source, parts, norms, pieces_a[level], bias, seg_col, seg_row
        )
        part, qkv, probs, ctx = outs[:4]
        if level == 0:
            z_a1 = stack_dp(dp_a1, part)
            near_a1 = gather_near(after(z_a1, near_b0), 1)
            dp_b1 = gather_dp(after(pack_b, z_a1), 1)
        z_b, near_b = (z_b0, near_b0) if level == 0 else (z_b1, near_b1)
        pieces_b[level] = [z_b, *near_b, *gather_both(*after(near_b, part), level)]
        if level:
            x, xhat2, scale2 = outs[4:]
            saved[0]["second"] = (xhat2, scale2)
        else:
            x = x_low
        part, mid, xhat1, scale1, act, slope = ffn_forward(
            metas[level], x, (part, swap_cores(part)), gain, shift, pieces_b[level], bias_in
        )
        saved.append(
            dict(x=x, qkv=qkv, probs=probs, ctx=ctx, mid=mid, xhat1=xhat1, scale1=scale1, act=act, slope=slope)
        )
        source, parts, norms = mid, (part, swap_cores(part)), (gain, shift)
        if level == 0:
            z_b1 = stack_dp(dp_b1, part)
            pieces_a[1] = [z_a1, *near_a1, *gather_both(*after(near_a1, part), 1)]
            near_b1 = gather_near(after(z_b1, pieces_a[1]), 1)
            source = after(source, z_b1)
    y, xhat2, scale2, cls_own = last_norm(source, parts, *norms, tok_row, cls_row)
    saved[1]["second"] = (xhat2, scale2)

    cls_slots = gather_small(cls_own).reshape(n_chips * n_cls, width)
    first_own = ((dp * n_t + me) * n_cls).astype(jnp.int32)[None]
    mean_loss, d_cls = loss_kernel(first_own, perm, cls_slots, all_q, all_pos, n_cls)

    vector_rows = [None, None]
    sources = (tokens, d_cls, tok_col, cls_row)
    sums_a, sums_b = [None, None], [None, None]
    for level in (1, 0):
        gain = vectors[level][0]
        kept = saved[level]
        meta = metas[level]
        xhat2, scale2 = kept["second"]
        if level == 0:
            sources = (after(sources[0], *sums_b[1].first(grads_a[1])), *sources[1:])
        part, d_second, d_ffn, d_pre, vec2, sum_inb = ffn_backward(
            level, meta, sources, xhat2, scale2, gain, kept["slope"], pieces_b[level]
        )
        other = swap_cores(part)
        grads_b = ffn_grads(meta, kept["mid"], d_pre, d_ffn, kept["act"], nz)
        sums_b[level] = Reduction(grads_b, level)
        d_second = after(d_second, grads_b[1])
        if level == 0:
            d_second = after(d_second, *sums_b[1].second(grads_b[1]), *sums_a[1].first(grads_b[1]))
        part, d_first, d_attn, d_qkv, vec1, sum_qkv = attn_backward(
            meta, d_second, (part, other), kept["xhat1"], kept["scale1"], gain,
            kept["qkv"], kept["probs"], pieces_a[level],
        )
        other = swap_cores(part)
        if level == 0:
            d_attn = after(d_attn, *sums_a[1].second(part), *sums_b[0].first(part))
        grads_a = attn_grads(meta, kept["x"], d_attn, d_qkv, kept["ctx"], nz)
        sums_a[level] = Reduction(grads_a, level)
        vector_rows[level] = (vec1, vec2, sum_qkv, sum_inb)
        sources = (d_first, part, other)
    sums_b[1].third(grads_a[1])
    sums_b[0].second(grads_a[1], sums_b[1].total)
    sums_a[1].third(*sums_b[0].sums)
    sums_a[0].first(*sums_b[0].sums)
    sums_a[0].second(sums_a[1].total)
    sums_b[0].third(*sums_a[0].sums)
    sums_a[0].third(sums_b[0].total)
    d_hidden = d_first + (part.astype(F32) + other.astype(F32))
    outgoing = jnp.where(first_core, d_hidden, y.astype(F32))
    low = outgoing.astype(BF16).reshape(n_t, share, width)
    incoming = [outgoing[:share]] + [hop(low[k], "tensor", k).astype(F32) for k in range(1, n_t)]
    boundary = jnp.zeros((n_t, share, width), F32)
    for k in range(n_t):
        boundary = lax.dynamic_update_index_in_dim(boundary, incoming[k], me ^ k, 0)
    tot_b = jnp.where(first_core, sums_b[0].total, sums_b[1].total)
    tot_a = jnp.where(first_core, sums_a[0].total, sums_a[1].total)

    vector_rows, _ = lax.optimization_barrier((vector_rows, sums_a[0].sums))
    wide = 3 * cols + units

    def vector_table(level):
        vec1, vec2, sum_qkv, sum_inb = vector_rows[level]
        by_t = lax.dot_general(
            hots[level], jnp.concatenate([sum_qkv, sum_inb], 1), (((0,), (0,)), ((), ())),
            precision=lax.Precision.HIGHEST,
        )
        whole = 0.5 * jnp.concatenate([vec1, vec2])
        return jnp.concatenate([jnp.pad(whole, ((0, 2), (0, wide - width))), by_t, jnp.zeros((4, wide), F32)])

    rows0, rows1 = vector_table(0), vector_table(1)
    flat = jnp.where(first_core, rows0, rows1) + swap_cores(jnp.where(first_core, rows1, rows0))
    flat = flat + sum(hop(flat, "tensor", k) for k in range(1, n_t))
    if direct:
        flat = flat + sum(hop(flat, "dp", k) for k in range(1, 4))
    else:
        flat = lax.psum(flat, "dp")
    own = lax.dynamic_slice_in_dim(flat[:6, :width], (dp * n_t + me) * piece, piece, 1)
    grad_gains = jnp.concatenate([own[0:1], own[3:4]]).reshape(layer_gains.shape)
    grad_shifts = jnp.concatenate([own[2:3], own[1:2], own[5:6], own[4:5]]).reshape(shifts.shape)
    by_t = lax.dynamic_slice_in_dim(flat, 8 + me, 1, 0)
    qv = jnp.concatenate([by_t[:, :cols], by_t[:, 2 * cols : 3 * cols]])
    grad_qv = lax.dynamic_slice_in_dim(qv, dp * qv_bias.shape[3], qv_bias.shape[3], 1).reshape(qv_bias.shape)
    grad_inb = lax.dynamic_slice_in_dim(by_t[:, 3 * cols :], dp * n_inb, n_inb, 1).reshape(in_bias.shape)

    grad_qkv = jnp.stack([tot_a[:, n * cols : (n + 1) * cols] for n in range(3)], 1)[None]
    grad_out = tot_a[:, 3 * cols :].T[None]
    grad_in = tot_b[:, :units][None]
    grad_ffn = tot_b[:, units:].T[None]
    return (
        grad_qkv, grad_qv, grad_out, grad_in, grad_inb, grad_ffn,
        grad_gains, grad_shifts, boundary[None], mean_loss.reshape(()),
    )


def solution(mesh):
    return jax.shard_map(
        on_device,
        mesh=mesh,
        in_specs=(
            P("dp", "tensor", None),
            P("dp", None),
            P("section", "dp", None, "tensor"),
            P("section", None, "tensor", "dp"),
            P("section", "tensor", "dp"),
            P("section", "dp", "tensor"),
            P("section", "tensor", "dp"),
            P("section", "tensor", "dp"),
            P("section", None, ("dp", "tensor")),
            P("section", None, ("dp", "tensor")),
            P(("dp", "tensor"), None),
            P(("dp", "tensor")),
            P("dp", "tensor", None),
        ),
        out_specs=(
            P("section", "dp", None, "tensor"),
            P("section", None, "tensor", "dp"),
            P("section", "tensor", "dp"),
            P("section", "dp", "tensor"),
            P("section", "tensor", "dp"),
            P("section", "tensor", "dp"),
            P("section", None, ("dp", "tensor")),
            P("section", None, ("dp", "tensor")),
            P("section", "dp", "tensor", None),
            P(),
        ),
        check_vma=False,
    )
```

```python
import jax
import jax.numpy as jnp
from jax import lax
from jax.experimental import pallas as pl
from jax.experimental.pallas import tpu as pltpu
from jax.sharding import PartitionSpec as P

HD = 64
PARTNER = 1
CROSS = 2
BF16 = jnp.bfloat16
F32 = jnp.float32


def mm(left, right, dims):
    return lax.dot_general(left, right, (dims, ((), ())), preferred_element_type=F32)


def nn(left, right):
    return mm(left, right, ((1,), (0,)))


def nt(left, right):
    return mm(left, right, ((1,), (1,)))


def after(block, *earlier):
    return lax.optimization_barrier((block, *earlier))[0]


def swap_cores(block):
    return lax.ppermute(block, "section", [(0, 1), (1, 0)])


def hop(block, axis, flip):
    return lax.ppermute(block, axis, [(i, i ^ flip) for i in range(lax.axis_size(axis))])


def core_hop(block, axis, flip, core):
    size = lax.axis_size(axis)
    route = [(core * size + i, core * size + (i ^ flip)) for i in range(size)]
    return lax.ppermute(block, ("section", axis), route)


def cross_hop(block, source):
    size = lax.axis_size("tensor")
    route = [(source * size + i, (1 - source) * size + (i ^ CROSS)) for i in range(size)]
    return lax.ppermute(block, ("section", "tensor"), route)


def direct_dp():
    return lax.axis_size("dp") == 4


def dp_order():
    size = lax.axis_size("dp")
    if direct_dp():
        return lax.axis_index("dp") ^ jnp.arange(size, dtype=jnp.int32)
    return jnp.arange(size, dtype=jnp.int32)


def spread_dp(block):
    if direct_dp():
        return jnp.stack([block] + [hop(block, "dp", k) for k in range(1, 4)])
    return lax.all_gather(block, "dp", axis=0, tiled=False)


def spread_tensor(block):
    return jnp.stack([block] + [hop(block, "tensor", k) for k in range(1, lax.axis_size("tensor"))])


def gather_dp(block, core):
    if direct_dp():
        return [block] + [core_hop(block, "dp", k, core) for k in range(1, 4)]
    return [lax.all_gather(block, "dp", axis=0, tiled=True)]


def stack_dp(blocks, *earlier):
    blocks = after(blocks, *earlier)
    if len(blocks) > 1:
        return jnp.stack(blocks)
    return blocks[0].reshape(2, blocks[0].shape[0] // 2, blocks[0].shape[1])


def gather_near(own, core):
    return core_hop(own, "tensor", PARTNER, core), cross_hop(own, core)


def gather_both(near, far, core):
    half = near.shape[0] // 2
    return cross_hop(near[:half], core), core_hop(far[half:], "tensor", PARTNER, 1 - core)


def add_low(*items):
    total = items[0].astype(F32)
    for item in items[1:]:
        total = total + item.astype(F32)
    return total.astype(BF16)


class Reduction:
    def __init__(self, grads, core):
        self.core = core
        self.pair, self.next_b, self.own_b = grads
        self.got = cross_hop(self.pair, 1 - core)
        self.near_b = hop(self.next_b, "tensor", PARTNER)

    def first(self, *earlier):
        half = self.next_b.shape[0]
        pair, own_b, got, near_b = after((self.pair, self.own_b, self.got, self.near_b), *earlier)
        self.parts = (pair[half:], got[half:]), (own_b, near_b)
        self.added = add_low(pair[:half], got[:half]), add_low(own_b, near_b)
        self.near_a = core_hop(self.added[0], "tensor", PARTNER, self.core)
        self.far_b = cross_hop(self.added[1], 1 - self.core)
        return self.added

    def second(self, *earlier):
        near_a, far_b, (parts_a, parts_b) = after((self.near_a, self.far_b, self.parts), *earlier)
        a, b = self.sums = add_low(*parts_a, near_a), add_low(*parts_b, far_b)
        if direct_dp():
            self.pieces = [a[0]] + [
                core_hop(block, "dp", k, self.core) for k, block in ((1, a[1]), (2, b[0]), (3, b[1]))
            ]
        else:
            whole = jnp.concatenate([a, b]).reshape(-1, a.shape[2])
            self.pieces = [lax.psum_scatter(whole, "dp", scatter_dimension=0, tiled=True)]
        return self.sums

    def third(self, *earlier):
        self.total = sum(block.astype(F32) for block in after(self.pieces, *earlier))
        return self.total


VMEM_LIMIT = 48 * 1024 * 1024
CHUNK = 128


def takes(micros):
    return pl.CostEstimate(flops=int(micros * 1.1e9), bytes_accessed=0, transcendentals=0)


def params():
    return pltpu.CompilerParams(vmem_limit_bytes=VMEM_LIMIT)


ANY = pl.BlockSpec(memory_space=pl.ANY)
VM = pl.BlockSpec(memory_space=pltpu.VMEM)
SM = pl.BlockSpec(memory_space=pltpu.SMEM)


def sds(shape, dtype):
    return jax.ShapeDtypeStruct(shape, dtype)


def chunks(length, step=CHUNK):
    return [slice(i, i + step) for i in range(0, length, step)]


def norm_rows(z):
    centre = z - jnp.mean(z, -1, keepdims=True)
    spread = jnp.mean(centre * centre, -1, keepdims=True)
    scale = lax.rsqrt(spread + 1e-05)
    return centre * scale, scale


def norm_back_rows(d_out, gain, xhat, scale):
    g = d_out * gain
    m1 = jnp.mean(g, -1, keepdims=True)
    m2 = jnp.mean(g * xhat, -1, keepdims=True)
    return scale * (g - m1 - xhat * m2)


def gelu_parts(x):
    e = jnp.exp(-0.5 * x * x)
    t = 1.0 / (1.0 + 0.2316418882 * jnp.abs(x))
    poly = t * (
        0.127414796 + t * (-0.142248368 + t * (0.7107068705 + t * (-0.7265760135 + t * 0.5307027145)))
    )
    tail = poly * e
    cdf = jnp.where(x < 0.0, tail, 1.0 - tail)
    return x * cdf, cdf + x * e * 0.3989422804014327


def zrows(meta, k, rz):
    return pl.ds(pl.multiple_of(meta[1 + k], 64), rz)


def load_weights(meta, pieces, place, sems):
    own, near, far = pieces[:3]
    nz, rz, _ = own.shape
    half = nz // 2
    home = meta[0] == 1
    lists = None
    at = 0
    for j, mine in enumerate((own, near)):
        for k in range(nz):
            targets = place(j, zrows(meta, k, rz))
            lists = lists or [[] for _ in targets]
            for n, (dst, columns) in enumerate(targets):
                other = far.at[k, :, columns] if j == 0 else pieces[3 + k // half].at[k % half, :, columns]
                first = pltpu.make_async_copy(mine.at[k, :, columns], dst, sems.at[at])
                second = pltpu.make_async_copy(other, dst, sems.at[at])
                at += 1

                @pl.when(home)
                def _():
                    first.start()

                @pl.when(jnp.logical_not(home))
                def _():
                    second.start()

                lists[n].append(first)
    return lists


def wait_all(waits):
    for made in waits:
        made.wait()


def load_a(meta, pieces, w_a, sems):
    width = w_a.shape[2]
    return load_weights(meta, pieces, lambda j, rows: [(w_a.at[j, rows, :], pl.ds(0, width))], sems)[0]


def load_b(meta, pieces, w_i, w_f, sems):
    one = w_i.shape[1] // 2
    return load_weights(
        meta,
        pieces,
        lambda j, rows: [
            (w_i.at[rows, pl.ds(j * one, one)], pl.ds(0, one)),
            (w_f.at[rows, pl.ds(j * one, one)], pl.ds(one, one)),
        ],
        sems,
    )


def attn_forward(level, meta, x_or_mid, parts, norms, pieces, bias, seg_col, seg_row):
    nz, rz, four = pieces[0].shape
    length, width = x_or_mid.shape
    cols = four // 4
    three = 3 * cols
    heads = 2 * cols // HD

    def body(meta, *refs):
        refs = list(refs)
        src = refs.pop(0)
        if level:
            own, other, gain, shift = (refs.pop(0) for _ in range(4))
        pieces = [refs.pop(0) for _ in range(5)]
        bias, sc, sr = (refs.pop(0) for _ in range(3))
        part_out, qkv_out, probs_out, ctx_out = (refs.pop(0) for _ in range(4))
        if level:
            x_out, xhat_out, scale_out = (refs.pop(0) for _ in range(3))
        w_a, sems = refs
        waits = load_a(meta, pieces, w_a, sems)
        if level:
            for rows in chunks(length):
                z = src[rows, :] + (own[rows, :].astype(F32) + other[rows, :].astype(F32)) + shift[2:3, :]
                xhat, scale = norm_rows(z)
                x_out[rows, :] = (xhat * gain[1:2, :] + shift[3:4, :]).astype(BF16)
                xhat_out[rows, :] = xhat.astype(BF16)
                scale_out[rows, :] = scale
            x_ref = x_out
        else:
            x_ref = src
        wait_all(waits)
        for j in range(2):
            c = slice(j * three, (j + 1) * three)
            for rows in chunks(length, 256):
                qkv_out[rows, c] = (nn(x_ref[rows, :], w_a[j, :, :three]) + bias[:, c]).astype(BF16)
        v_t = jnp.concatenate(
            [qkv_out[:, j * three + 2 * cols : (j + 1) * three].astype(F32) for j in range(2)], 1
        ).T.astype(BF16)
        for queries in chunks(length, 256):
            same = sc[...] == sr[:, queries]
            outs = []
            for h in range(heads):
                j, i = divmod(h, cols // HD)
                at = j * three + i * HD
                q = qkv_out[queries, at : at + HD]
                k = qkv_out[:, at + cols : at + cols + HD]
                st = jnp.where(same, nt(k, q) * 0.125, -1e30)
                p = jnp.exp(st - jnp.max(st, 0, keepdims=True))
                p = (p * (1.0 / jnp.sum(p, 0, keepdims=True))).astype(BF16)
                probs_out[h, :, queries] = p
                outs.append(nn(v_t[h * HD : (h + 1) * HD], p))
            ctx = jnp.concatenate(outs, 0).T.astype(BF16)
            ctx_out[queries, :] = ctx
            part_out[queries, :] = (
                nt(ctx[:, :cols], w_a[0, :, three:]) + nt(ctx[:, cols:], w_a[1, :, three:])
            ).astype(BF16)

    outs = [
        sds((length, width), BF16), sds((length, 2 * three), BF16),
        sds((heads, length, length), BF16), sds((length, 2 * cols), BF16),
    ]
    args = [meta, x_or_mid]
    if level:
        args += [*parts, *norms]
        outs += [sds((length, width), BF16), sds((length, width), BF16), sds((length, 1), F32)]
    specs = [SM] + [VM] * (len(args) - 1) + [ANY] * 5 + [VM] * 3
    args += [*pieces, bias, seg_col, seg_row]
    return pl.pallas_call(
        body,
        out_shape=outs,
        in_specs=specs,
        out_specs=[VM] * len(outs),
        scratch_shapes=[pltpu.VMEM((2, width, four), BF16), pltpu.SemaphoreType.DMA((2 * nz,))],
        compiler_params=params(),
        cost_estimate=takes(13),
        name="attn_forward",
    )(*args)


def ffn_forward(meta, x, parts, gains, shifts, pieces, bias_in):
    nz, rz, units = pieces[0].shape
    length, width = x.shape

    def body(meta, x, own, other, gain, shift, p0, p1, p2, p3, p4, bias,
             part_out, mid_out, xhat_out, scale_out, act_out, slope_out, w_i, w_f, low, sems):
        first, second = load_b(meta, (p0, p1, p2, p3, p4), w_i, w_f, sems)
        for rows in chunks(length):
            z = x[rows, :].astype(F32) + (own[rows, :].astype(F32) + other[rows, :].astype(F32)) + shift[0:1, :]
            xhat, scale = norm_rows(z)
            mid = xhat * gain[0:1, :] + shift[1:2, :]
            mid_out[rows, :] = mid
            low[rows, :] = mid.astype(BF16)
            xhat_out[rows, :] = xhat.astype(BF16)
            scale_out[rows, :] = scale
        wait_all(first)
        for rows in chunks(length, 256):
            for c in chunks(units, 512):
                pre = nn(low[rows, :], w_i[:, c]) + bias[:, c]
                act, slope = gelu_parts(pre)
                act_out[rows, c] = act.astype(BF16)
                slope_out[rows, c] = slope.astype(BF16)
        wait_all(second)
        for rows in chunks(length, 256):
            part_out[rows, :] = nt(act_out[rows, :], w_f[...]).astype(BF16)

    return pl.pallas_call(
        body,
        out_shape=[
            sds((length, width), BF16), sds((length, width), F32), sds((length, width), BF16),
            sds((length, 1), F32), sds((length, units), BF16), sds((length, units), BF16),
        ],
        in_specs=[SM] + [VM] * 5 + [ANY] * 5 + [VM],
        out_specs=[VM] * 6,
        scratch_shapes=[
            pltpu.VMEM((width, units), BF16), pltpu.VMEM((width, units), BF16),
            pltpu.VMEM((length, width), BF16), pltpu.SemaphoreType.DMA((4 * nz,)),
        ],
        compiler_params=params(),
        cost_estimate=takes(9),
        name="ffn_forward",
    )(meta, x, *parts, gains, shifts, *pieces, bias_in)


def last_norm(mid, parts, gains, shifts, tok_row, cls_pos):
    length, width = mid.shape
    n_cls = cls_pos.shape[0]

    def body(cls, mid, own, other, gain, shift, tok, y_out, xhat_out, scale_out, cls_out):
        for rows in chunks(length):
            z = mid[rows, :] + (own[rows, :].astype(F32) + other[rows, :].astype(F32)) + shift[2:3, :]
            xhat, scale = norm_rows(z)
            y_out[rows, :] = (xhat * gain[1:2, :] + shift[3:4, :]).astype(BF16)
            xhat_out[rows, :] = xhat.astype(BF16)
            scale_out[rows, :] = scale
        which = lax.broadcasted_iota(jnp.int32, (16, length), 0)
        hot = jnp.zeros((16, length), F32)
        for p in range(n_cls):
            hot = jnp.where(jnp.logical_and(which == p, tok[...] == cls[p]), 1.0, hot)
        cls_out[...] = nn(hot.astype(BF16), y_out[...])[:n_cls].astype(BF16)

    return pl.pallas_call(
        body,
        out_shape=[
            sds((length, width), BF16), sds((length, width), BF16), sds((length, 1), F32),
            sds((n_cls, width), BF16),
        ],
        in_specs=[SM] + [VM] * 6,
        out_specs=[VM] * 4,
        compiler_params=params(),
        cost_estimate=takes(2),
        name="last_norm",
    )(cls_pos, mid, *parts, gains, shifts, tok_row)


def ffn_backward(level, meta, sources, xhat, scale, gains, slope, pieces):
    nz, rz, units = pieces[0].shape
    length, width = xhat.shape
    n_cls = sources[3].shape[0] if level else 0

    def body(meta, *refs):
        refs = list(refs)
        if level:
            cls, grad, d_cls, tok = (refs.pop(0) for _ in range(4))
        else:
            d_above, own, other = (refs.pop(0) for _ in range(3))
        xhat, scale, gain, slope = (refs.pop(0) for _ in range(4))
        pieces = [refs.pop(0) for _ in range(5)]
        part_out, second_out, low_out, pre_out, vec_out, inb_out, w_i, w_f, sems = refs
        first, second = load_b(meta, pieces, w_i, w_f, sems)
        sums = [jnp.zeros((1, width), F32) for _ in range(3)]
        for rows in chunks(length):
            if level:
                d_out = grad[rows, :].astype(F32)
                for p in range(n_cls):
                    d_out = d_out + jnp.where(tok[rows, :] == cls[p], 1.0, 0.0) * d_cls[p : p + 1, :]
            else:
                d_out = d_above[rows, :] + (own[rows, :].astype(F32) + other[rows, :].astype(F32))
                d_out = d_out.astype(BF16).astype(F32)
            hat = xhat[rows, :].astype(F32)
            d_second = norm_back_rows(d_out, gain[1:2, :], hat, scale[rows, :])
            second_out[rows, :] = d_second
            low_out[rows, :] = d_second.astype(BF16)
            for n, item in enumerate((d_out * hat, d_out, d_second)):
                sums[n] = sums[n] + jnp.sum(item, 0, keepdims=True)
        for n in range(3):
            vec_out[n : n + 1, :] = sums[n]
        wait_all(second)
        for n, rows in enumerate(chunks(length, 256)):
            for c in chunks(units, units // 4):
                d_act = nn(low_out[rows, :], w_f[:, c])
                d_pre = (slope[rows, c].astype(F32) * d_act).astype(BF16)
                pre_out[rows, c] = d_pre
                j, at = divmod(c.start, units // 2)
                at = slice(at, at + c.stop - c.start)
                total = jnp.sum(d_pre.astype(F32), 0, keepdims=True)
                inb_out[j : j + 1, at] = total if n == 0 else inb_out[j : j + 1, at] + total
        wait_all(first)
        for rows in chunks(length, 256):
            part_out[rows, :] = nt(pre_out[rows, :], w_i[...]).astype(BF16)

    if level:
        token_grad, d_cls, tok_col, cls_pos = sources
        args, specs = [meta, cls_pos, token_grad, d_cls, tok_col], [SM, SM, VM, VM, VM]
    else:
        args, specs = [meta, *sources], [SM, VM, VM, VM]
    args += [xhat, scale, gains, slope, *pieces]
    specs += [VM] * 4 + [ANY] * 5
    return pl.pallas_call(
        body,
        out_shape=[
            sds((length, width), BF16), sds((length, width), F32), sds((length, width), BF16),
            sds((length, units), BF16), sds((3, width), F32), sds((2, units // 2), F32),
        ],
        in_specs=specs,
        out_specs=[VM] * 6,
        scratch_shapes=[
            pltpu.VMEM((width, units), BF16), pltpu.VMEM((width, units), BF16),
            pltpu.SemaphoreType.DMA((4 * nz,)),
        ],
        compiler_params=params(),
        cost_estimate=takes(9),
        name="ffn_backward",
    )(*args)


def halves_of(nz, rz, width):
    half = nz // 2
    return [sds((nz, rz, width), BF16), sds((half, rz, width), BF16), sds((half, rz, width), BF16)]


def place_half(outs, j, k, nz):
    half = nz // 2
    if k < half:
        return outs[0], k + (half if j == 0 else 0)
    return outs[2 if j == 0 else 1], k - half


def ffn_grads(meta, mid, d_pre, d_ffn, act, nz):
    length, width = mid.shape
    units = d_pre.shape[1]
    one = units // 2
    rz = width // nz

    def body(meta, mid, d_pre, d_ffn, act, *refs):
        outs, (mid_t, ffn_t) = refs[:3], refs[3:]
        mid_t[...] = mid[...].T.astype(BF16)
        ffn_t[...] = d_ffn[...].astype(F32).T.astype(BF16)
        for j in range(2):
            c = slice(j * one, (j + 1) * one)
            for k in range(nz):
                rows = zrows(meta, k, rz)
                out, at = place_half(outs, j, k, nz)
                out[at, :, :one] = nn(mid_t[rows, :], d_pre[:, c]).astype(BF16)
                out[at, :, one:] = nn(ffn_t[rows, :], act[:, c]).astype(BF16)

    return pl.pallas_call(
        body,
        out_shape=halves_of(nz, rz, units),
        in_specs=[SM] + [VM] * 4,
        out_specs=[VM] * 3,
        scratch_shapes=[pltpu.VMEM((width, length), BF16)] * 2,
        compiler_params=params(),
        cost_estimate=takes(7),
        name="ffn_grads",
    )(meta, mid, d_pre, d_ffn, act)


def attn_backward(meta, d_second, parts, xhat, scale, gains, qkv, probs, pieces):
    nz, rz, four = pieces[0].shape
    length, width = d_second.shape
    cols = four // 4
    three = 3 * cols
    heads = 2 * cols // HD

    def body(meta, d_second, own, other, xhat, scale, gain, qkv, probs, p0, p1, p2, p3, p4,
             part_out, first_out, low_out, dqkv_out, vec_out, sum_out,
             w_a, d_ctx, acc_v, acc_k, sems):
        waits = load_a(meta, (p0, p1, p2, p3, p4), w_a, sems)
        sums = [jnp.zeros((1, width), F32) for _ in range(3)]
        for rows in chunks(length):
            d_mid = d_second[rows, :] + (own[rows, :].astype(F32) + other[rows, :].astype(F32))
            hat = xhat[rows, :].astype(F32)
            d_first = norm_back_rows(d_mid, gain[0:1, :], hat, scale[rows, :])
            first_out[rows, :] = d_first
            low_out[rows, :] = d_first.astype(BF16)
            for n, item in enumerate((d_mid * hat, d_mid, d_first)):
                sums[n] = sums[n] + jnp.sum(item, 0, keepdims=True)
        for n in range(3):
            vec_out[n : n + 1, :] = sums[n]
        wait_all(waits)
        for j in range(2):
            for rows in chunks(length, 256):
                d_ctx[rows, j * cols : (j + 1) * cols] = nn(low_out[rows, :], w_a[j, :, three:]).astype(BF16)
        k_t = jnp.concatenate(
            [qkv[:, j * three + cols : j * three + 2 * cols].astype(F32) for j in range(2)], 1
        ).T.astype(BF16)
        for h in range(heads):
            j, i = divmod(h, cols // HD)
            at = j * three + i * HD
            q_cols, k_cols, v_cols = (slice(at + n * cols, at + n * cols + HD) for n in range(3))
            for n, queries in enumerate(chunks(length, 256)):
                d_o = d_ctx[queries, h * HD : (h + 1) * HD]
                d_p = nt(qkv[:, v_cols], d_o)
                p = probs[h, :, queries]
                wide = p.astype(F32)
                d_s = (wide * (d_p - jnp.sum(wide * d_p, 0, keepdims=True))).astype(BF16)
                d_v = nn(p, d_o)
                d_k = nn(d_s, qkv[queries, q_cols])
                acc_v[...] = d_v if n == 0 else acc_v[...] + d_v
                acc_k[...] = d_k if n == 0 else acc_k[...] + d_k
                d_q = nn(k_t[h * HD : (h + 1) * HD], d_s)
                dqkv_out[queries, q_cols] = (d_q.T * 0.125).astype(BF16)
            dqkv_out[:, v_cols] = acc_v[...].astype(BF16)
            dqkv_out[:, k_cols] = (acc_k[...] * 0.125).astype(BF16)
        for j in range(2):
            sum_out[j : j + 1, :] = jnp.sum(
                dqkv_out[:, j * three : (j + 1) * three].astype(F32), 0, keepdims=True
            )
        for rows in chunks(length, 256):
            part_out[rows, :] = (
                nt(dqkv_out[rows, :three], w_a[0, :, :three]) + nt(dqkv_out[rows, three:], w_a[1, :, :three])
            ).astype(BF16)

    return pl.pallas_call(
        body,
        out_shape=[
            sds((length, width), BF16), sds((length, width), F32), sds((length, width), BF16),
            sds((length, 2 * three), BF16), sds((3, width), F32), sds((2, three), F32),
        ],
        in_specs=[SM] + [VM] * 8 + [ANY] * 5,
        out_specs=[VM] * 6,
        scratch_shapes=[
            pltpu.VMEM((2, width, four), BF16), pltpu.VMEM((length, 2 * cols), BF16),
            pltpu.VMEM((length, HD), F32), pltpu.VMEM((length, HD), F32),
            pltpu.SemaphoreType.DMA((2 * nz,)),
        ],
        compiler_params=params(),
        cost_estimate=takes(15),
        name="attn_backward",
    )(meta, d_second, *parts, xhat, scale, gains, qkv, probs, *pieces)


def attn_grads(meta, x, d_attn, d_qkv, ctx, nz):
    length, width = x.shape
    three = d_qkv.shape[1] // 2
    cols = ctx.shape[1] // 2
    rz = width // nz

    def body(meta, x, d_attn, d_qkv, ctx, *refs):
        outs, (x_t, a_t) = refs[:3], refs[3:]
        x_t[...] = x[...].astype(F32).T.astype(BF16)
        a_t[...] = d_attn[...].astype(F32).T.astype(BF16)
        for j in range(2):
            for k in range(nz):
                rows = zrows(meta, k, rz)
                out, at = place_half(outs, j, k, nz)
                out[at, :, :three] = nn(x_t[rows, :], d_qkv[:, j * three : (j + 1) * three]).astype(BF16)
                out[at, :, three:] = nn(a_t[rows, :], ctx[:, j * cols : (j + 1) * cols]).astype(BF16)

    return pl.pallas_call(
        body,
        out_shape=halves_of(nz, rz, three + cols),
        in_specs=[SM] + [VM] * 4,
        out_specs=[VM] * 3,
        scratch_shapes=[pltpu.VMEM((width, length), BF16)] * 2,
        compiler_params=params(),
        cost_estimate=takes(4),
        name="attn_grads",
    )(meta, x, d_attn, d_qkv, ctx)


def loss_kernel(own, perm, slots, queries, positive_col, n_own):
    n_q, width = queries.shape
    n_p = slots.shape[0]

    def body(own, perm, slots, queries, pos, loss_out, d_out):
        passages = nn(perm[...], slots[...]).astype(BF16)
        logits = nt(queries[...], passages)
        top = jnp.max(logits, -1, keepdims=True)
        log_total = top + jnp.log(jnp.sum(jnp.exp(logits - top), -1, keepdims=True))
        index = lax.broadcasted_iota(jnp.int32, (n_q, n_p), 1)
        hits = pos[...] == index
        chosen = jnp.sum(jnp.where(hits, logits, 0.0), -1, keepdims=True)
        loss_out[...] = jnp.sum(log_total - chosen, 0, keepdims=True) / n_q
        d_logits = (16.0 * (jnp.exp(logits - log_total) - jnp.where(hits, 1.0, 0.0))).astype(BF16)
        pick = jnp.where(
            lax.broadcasted_iota(jnp.int32, (n_p, 128), 0)
            == lax.broadcasted_iota(jnp.int32, (n_p, 128), 1) + own[0],
            1.0, 0.0,
        ).astype(BF16)
        cols = nn(d_logits, pick)
        d_out[...] = nn(cols.T.astype(BF16), queries[...])[:n_own]

    return pl.pallas_call(
        body,
        out_shape=[sds((1, 1), F32), sds((n_own, width), F32)],
        in_specs=[SM] + [VM] * 4,
        out_specs=[VM] * 2,
        compiler_params=params(),
        cost_estimate=takes(1),
        name="contrast",
    )(own, perm, slots, queries, positive_col)


def on_device(
    inputs, cls_pos, w_qkv, qv_bias, w_out, w_in, in_bias, w_ffn_out,
    layer_gains, shifts, queries, positive, token_grad,
):
    core = lax.axis_index("section")
    dp = lax.axis_index("dp")
    me = lax.axis_index("tensor")
    n_dp = lax.axis_size("dp")
    n_t = lax.axis_size("tensor")
    first_core = core == 0
    rows_dev, share, width = inputs.shape
    cols = w_qkv.shape[3]
    units = w_in.shape[2]
    length = n_t * share
    n_chips = n_dp * n_t
    piece = width // n_chips
    order = dp_order()
    direct = direct_dp()
    nz = 4 if direct else 2
    t_ids = jnp.arange(n_t, dtype=jnp.int32)

    vec = jnp.concatenate(
        [layer_gains.reshape(-1), shifts.reshape(-1), qv_bias.reshape(-1), in_bias.reshape(-1)]
    )
    n_gain, n_shift, n_qv, n_inb = layer_gains.size, shifts.size, qv_bias.size, in_bias.size
    n_vec = vec.shape[0]
    flat = jnp.concatenate(
        [vec, queries.reshape(-1), (positive // 16).astype(BF16), (positive % 16).astype(BF16)]
    )
    flat = jnp.pad(flat, (0, -flat.shape[0] % 2048)).reshape(-1, 128)

    def spread_rows(block):
        parts = [lax.dynamic_index_in_dim(block, me ^ k, 0, keepdims=False) for k in range(n_t)]
        return jnp.concatenate([parts[0]] + [hop(parts[k], "tensor", k) for k in range(1, n_t)], 0)

    x_low = spread_rows(inputs)

    pack_a = jnp.concatenate([w_qkv[0, :, 0], w_qkv[0, :, 1], w_qkv[0, :, 2], w_out[0].T], 1)
    pack_b = jnp.concatenate([w_in[0], w_ffn_out[0].T], 1)
    dp_a0 = gather_dp(pack_a, 0)
    message = spread_dp(flat)
    z_a0 = stack_dp(dp_a0, x_low, message)
    near_a0 = gather_near(z_a0, 0)
    message = spread_tensor(after(message, z_a0))
    dp_b0 = gather_dp(after(pack_b, z_a0), 0)
    both_a0 = gather_both(*near_a0, 0)
    a0 = [z_a0, *near_a0, *both_a0]

    zrow = order * (width // n_dp) if direct else jnp.arange(2, dtype=jnp.int32) * (width // 2)
    metas = [
        jnp.concatenate([(core == level)[None].astype(jnp.int32), zrow.astype(jnp.int32)])
        for level in range(2)
    ]
    slots = [me ^ (2 * (core != level) + jnp.arange(2, dtype=jnp.int32)) for level in range(2)]
    hots = [(s[:, None] == t_ids[None, :]).astype(F32) for s in slots]

    positions = jnp.concatenate(
        [(me ^ k) * share + jnp.arange(share, dtype=jnp.int32) for k in range(n_t)]
    )
    cls_row = lax.dynamic_index_in_dim(cls_pos, me, 0, keepdims=False)
    segments = jnp.sum((positions[:, None] >= cls_row[None, :]).astype(jnp.int32), -1)
    seg_col, seg_row = segments[:, None], segments[None, :]
    tok_col, tok_row = positions[:, None], positions[None, :]

    slot_ids = (order[None, :] * n_t + (me ^ t_ids)[:, None]).reshape(-1)
    to_natural = (jnp.arange(n_chips, dtype=jnp.int32)[:, None] == slot_ids[None, :]).astype(BF16)
    table = nn(to_natural, message.reshape(n_chips, -1))
    own_table = table[:, :n_vec].astype(BF16)
    other_table = swap_cores(own_table)
    tables = jnp.where(
        first_core, jnp.stack([own_table, other_table]), jnp.stack([other_table, own_table])
    ).astype(F32)
    at = 0
    gains = tables[:, :, at : at + n_gain].reshape(2, n_chips, 2, piece).transpose(0, 2, 1, 3).reshape(2, 2, width)
    at += n_gain
    shift = tables[:, :, at : at + n_shift].reshape(2, n_chips, 4, piece).transpose(0, 2, 1, 3).reshape(2, 4, width)
    at += n_shift
    qv = tables[:, :, at : at + n_qv].reshape(2, n_dp, n_t, 2, cols // n_dp)
    qv = qv.transpose(0, 3, 2, 1, 4).reshape(2, 2, n_t, cols)
    at += n_qv
    inb = tables[:, :, at : at + n_inb].reshape(2, n_dp, n_t, n_inb).transpose(0, 2, 1, 3).reshape(2, n_t, units)
    vectors = []
    for level in range(2):
        bias = jnp.sum(hots[level][None, :, :, None] * qv[level][:, None], 2)
        bias = jnp.stack([bias[0], jnp.zeros_like(bias[0]), bias[1]], 1).reshape(1, -1)
        bias_in = jnp.sum(hots[level][:, :, None] * inb[level][None], 1).reshape(1, -1)
        vectors.append((gains[level], shift[level], bias, bias_in))
    at = n_vec
    q_dev = queries.shape[0]
    all_q = table[:, at : at + q_dev * width].reshape(-1, width).astype(BF16)
    at += q_dev * width
    all_pos = table[:, at : at + q_dev] * 16.0 + table[:, at + q_dev : at + 2 * q_dev]
    all_pos = all_pos.astype(jnp.int32).reshape(-1, 1)
    n_cls = cls_row.shape[0]
    perm = jnp.repeat(jnp.repeat(to_natural, n_cls, 0), n_cls, 1)
    perm = perm * jnp.tile(jnp.eye(n_cls, dtype=BF16), (n_chips, n_chips))

    vectors, all_q, all_pos, perm, x_low = lax.optimization_barrier(
        (vectors, all_q, all_pos, perm, x_low)
    )
    saved = []
    z_b0 = stack_dp(dp_b0, both_a0)
    near_b0 = gather_near(z_b0, 0)
    dp_a1 = gather_dp(after(pack_a, z_b0), 1)
    source, parts, norms = after(x_low, z_b0), None, None
    pieces_a, pieces_b = [a0, None], [None, None]
    for level in range(2):
        gain, shift, bias, bias_in = vectors[level]
        outs = attn_forward(
            level, metas[level], source, parts, norms, pieces_a[level], bias, seg_col, seg_row
        )
        part, qkv, probs, ctx = outs[:4]
        if level == 0:
            z_a1 = stack_dp(dp_a1, part)
            dp_b1 = gather_dp(after(pack_b, z_a1), 1)
            both_b0 = gather_both(*after(near_b0, z_a1), 0)
            near_a1 = gather_near(after(z_a1, near_b0), 1)
            pieces_b[0] = [z_b0, *near_b0, *both_b0]
        else:
            near_b1, part = lax.optimization_barrier((near_b1, part))
            both_b1 = gather_both(*near_b1, 1)
            tokens = spread_rows(after(token_grad, near_b1))
            pieces_b[1] = [z_b1, *near_b1, *both_b1]
        if level:
            x, xhat2, scale2 = outs[4:]
            saved[0]["second"] = (xhat2, scale2)
        else:
            x = x_low
        part, mid, xhat1, scale1, act, slope = ffn_forward(
            metas[level], x, (part, swap_cores(part)), gain, shift, pieces_b[level], bias_in
        )
        saved.append(
            dict(x=x, qkv=qkv, probs=probs, ctx=ctx, mid=mid, xhat1=xhat1, scale1=scale1, act=act, slope=slope)
        )
        source, parts, norms = mid, (part, swap_cores(part)), (gain, shift)
        if level == 0:
            z_b1 = stack_dp(dp_b1, part)
            near_a1, z_b1 = lax.optimization_barrier((near_a1, z_b1))
            both_a1 = gather_both(*near_a1, 1)
            near_b1 = gather_near(after(z_b1, near_a1), 1)
            pieces_a[1] = [z_a1, *near_a1, *both_a1]
    source = after(source, tokens)
    y, xhat2, scale2, cls_own = last_norm(source, parts, *norms, tok_row, cls_row)
    saved[1]["second"] = (xhat2, scale2)

    cls_slots = spread_tensor(spread_dp(cls_own)).reshape(n_chips * n_cls, width)
    first_own = ((dp * n_t + me) * n_cls).astype(jnp.int32)[None]
    mean_loss, d_cls = loss_kernel(first_own, perm, cls_slots, all_q, all_pos, n_cls)

    vector_rows = [None, None]
    sources = (tokens, d_cls, tok_col, cls_row)
    sums_a, sums_b = [None, None], [None, None]
    for level in (1, 0):
        gain = vectors[level][0]
        kept = saved[level]
        meta = metas[level]
        xhat2, scale2 = kept["second"]
        if level == 0:
            sources = (after(sources[0], sums_b[1].first(grads_a[1])), *sources[1:])
        part, d_second, d_ffn, d_pre, vec2, sum_inb = ffn_backward(
            level, meta, sources, xhat2, scale2, gain, kept["slope"], pieces_b[level]
        )
        other = swap_cores(part)
        if level == 0:
            d_ffn = after(d_ffn, sums_a[1].first(part))
        grads_b = ffn_grads(meta, kept["mid"], d_pre, d_ffn, kept["act"], nz)
        sums_b[level] = Reduction(grads_b, level)
        d_second = after(d_second, grads_b[1])
        if level == 0:
            d_second = after(d_second, sums_b[1].second(grads_b[1]))
        part, d_first, d_attn, d_qkv, vec1, sum_qkv = attn_backward(
            meta, d_second, (part, other), kept["xhat1"], kept["scale1"], gain,
            kept["qkv"], kept["probs"], pieces_a[level],
        )
        other = swap_cores(part)
        if level == 0:
            d_attn = after(d_attn, sums_b[1].third(sums_a[1].second(part)))
        grads_a = attn_grads(meta, kept["x"], d_attn, d_qkv, kept["ctx"], nz)
        sums_a[level] = Reduction(grads_a, level)
        vector_rows[level] = (vec1, vec2, sum_qkv, sum_inb)
        sources = (d_first, part, other)
    sums_b[0].first(grads_a[1])
    sums_a[1].third(sums_b[0].added)
    sums_a[0].first(sums_a[1].total)
    sums_b[0].second(sums_a[0].added)
    sums_a[0].second(sums_b[0].sums)
    sums_b[0].third(sums_a[0].sums)
    sums_a[0].third(sums_b[0].total)
    d_hidden = d_first + (part.astype(F32) + other.astype(F32))
    outgoing = jnp.where(first_core, d_hidden, y.astype(F32))
    low = after(outgoing.astype(BF16), sums_b[0].added).reshape(n_t, share, width)
    incoming = [outgoing[:share]] + [hop(low[k], "tensor", k).astype(F32) for k in range(1, n_t)]
    boundary = jnp.zeros((n_t, share, width), F32)
    for k in range(n_t):
        boundary = lax.dynamic_update_index_in_dim(boundary, incoming[k], me ^ k, 0)
    tot_b = jnp.where(first_core, sums_b[0].total, sums_b[1].total)
    tot_a = jnp.where(first_core, sums_a[0].total, sums_a[1].total)

    vector_rows, _ = lax.optimization_barrier((vector_rows, sums_a[0].added))
    wide = 3 * cols + units

    def vector_table(level):
        vec1, vec2, sum_qkv, sum_inb = vector_rows[level]
        by_t = lax.dot_general(
            hots[level], jnp.concatenate([sum_qkv, sum_inb], 1), (((0,), (0,)), ((), ())),
            precision=lax.Precision.HIGHEST,
        )
        whole = 0.5 * jnp.concatenate([vec1, vec2])
        return jnp.concatenate([jnp.pad(whole, ((0, 2), (0, wide - width))), by_t, jnp.zeros((4, wide), F32)])

    rows0, rows1 = vector_table(0), vector_table(1)
    flat = jnp.where(first_core, rows0, rows1) + swap_cores(jnp.where(first_core, rows1, rows0))
    flat = flat + sum(hop(flat, "tensor", k) for k in range(1, n_t))
    if direct:
        flat = flat + sum(hop(flat, "dp", k) for k in range(1, 4))
    else:
        flat = lax.psum(flat, "dp")
    own = lax.dynamic_slice_in_dim(flat[:6, :width], (dp * n_t + me) * piece, piece, 1)
    grad_gains = jnp.concatenate([own[0:1], own[3:4]]).reshape(layer_gains.shape)
    grad_shifts = jnp.concatenate([own[2:3], own[1:2], own[5:6], own[4:5]]).reshape(shifts.shape)
    by_t = lax.dynamic_slice_in_dim(flat, 8 + me, 1, 0)
    qv = jnp.concatenate([by_t[:, :cols], by_t[:, 2 * cols : 3 * cols]])
    grad_qv = lax.dynamic_slice_in_dim(qv, dp * qv_bias.shape[3], qv_bias.shape[3], 1).reshape(qv_bias.shape)
    grad_inb = lax.dynamic_slice_in_dim(by_t[:, 3 * cols :], dp * n_inb, n_inb, 1).reshape(in_bias.shape)

    grad_qkv = jnp.stack([tot_a[:, n * cols : (n + 1) * cols] for n in range(3)], 1)[None]
    grad_out = tot_a[:, 3 * cols :].T[None]
    grad_in = tot_b[:, :units][None]
    grad_ffn = tot_b[:, units:].T[None]
    return (
        grad_qkv, grad_qv, grad_out, grad_in, grad_inb, grad_ffn,
        grad_gains, grad_shifts, boundary[None], mean_loss.reshape(()),
    )


def solution(mesh):
    return jax.shard_map(
        on_device,
        mesh=mesh,
        in_specs=(
            P("dp", "tensor", None),
            P("dp", None),
            P("section", "dp", None, "tensor"),
            P("section", None, "tensor", "dp"),
            P("section", "tensor", "dp"),
            P("section", "dp", "tensor"),
            P("section", "tensor", "dp"),
            P("section", "tensor", "dp"),
            P("section", None, ("dp", "tensor")),
            P("section", None, ("dp", "tensor")),
            P(("dp", "tensor"), None),
            P(("dp", "tensor")),
            P("dp", "tensor", None),
        ),
        out_specs=(
            P("section", "dp", None, "tensor"),
            P("section", None, "tensor", "dp"),
            P("section", "tensor", "dp"),
            P("section", "dp", "tensor"),
            P("section", "tensor", "dp"),
            P("section", "tensor", "dp"),
            P("section", None, ("dp", "tensor")),
            P("section", None, ("dp", "tensor")),
            P("section", "dp", "tensor", None),
            P(),
        ),
        check_vma=False,
    )
```

```python
import jax
import jax.numpy as jnp
from jax import lax
from jax.experimental import pallas as pl
from jax.experimental.pallas import tpu as pltpu
from jax.sharding import PartitionSpec as P

HD = 64
PARTNER = 1
CROSS = 2
BF16 = jnp.bfloat16
F32 = jnp.float32


def mm(left, right, dims):
    return lax.dot_general(left, right, (dims, ((), ())), preferred_element_type=F32)


def nn(left, right):
    return mm(left, right, ((1,), (0,)))


def nt(left, right):
    return mm(left, right, ((1,), (1,)))


def after(block, *earlier):
    return lax.optimization_barrier((block, *earlier))[0]


def swap_cores(block):
    return lax.ppermute(block, "section", [(0, 1), (1, 0)])


def hop(block, axis, flip):
    return lax.ppermute(block, axis, [(i, i ^ flip) for i in range(lax.axis_size(axis))])


def core_hop(block, axis, flip, core):
    size = lax.axis_size(axis)
    route = [(core * size + i, core * size + (i ^ flip)) for i in range(size)]
    return lax.ppermute(block, ("section", axis), route)


def cross_hop(block, source):
    size = lax.axis_size("tensor")
    route = [(source * size + i, (1 - source) * size + (i ^ CROSS)) for i in range(size)]
    return lax.ppermute(block, ("section", "tensor"), route)


def direct_dp():
    return lax.axis_size("dp") == 4


def dp_order():
    size = lax.axis_size("dp")
    if direct_dp():
        return lax.axis_index("dp") ^ jnp.arange(size, dtype=jnp.int32)
    return jnp.arange(size, dtype=jnp.int32)


def spread_dp(block):
    if direct_dp():
        return jnp.stack([block] + [hop(block, "dp", k) for k in range(1, 4)])
    return lax.all_gather(block, "dp", axis=0, tiled=False)


def spread_tensor(block):
    return jnp.stack([block] + [hop(block, "tensor", k) for k in range(1, 4)])


def double(block, axis):
    pair = jnp.stack([block, hop(block, axis, 1)])
    return jnp.concatenate([pair, hop(pair, axis, 2)])


def exchange_rows(blocks):
    first = hop(jnp.stack([blocks[1], blocks[3]]), "tensor", 1)
    second = hop(jnp.stack([blocks[2], first[1]]), "tensor", 2)
    return [blocks[0], first[0], second[0], second[1]]


def first_dp(block, core):
    return core_hop(block, "dp", 1, core) if direct_dp() else block


def second_dp(block, one, core):
    if not direct_dp():
        return [lax.all_gather(block, "dp", axis=0, tiled=True)]
    pair = jnp.stack([block, one])
    return [pair, core_hop(pair, "dp", 2, core)]


def all_dp(block, core):
    if not direct_dp():
        return [lax.all_gather(block, "dp", axis=0, tiled=True)]
    return [block[None]] + [core_hop(block, "dp", k, core)[None] for k in range(1, 4)]


def whole_dp(blocks, *earlier):
    blocks = after(blocks, *earlier)
    if len(blocks) > 1:
        return jnp.concatenate(blocks)
    return blocks[0].reshape(2, blocks[0].shape[0] // 2, blocks[0].shape[1])


def gather_near(own, core):
    return core_hop(own, "tensor", PARTNER, core), cross_hop(own, core)


def gather_both(near, far, core):
    half = near.shape[0] // 2
    return cross_hop(near[:half], core), core_hop(far[half:], "tensor", PARTNER, 1 - core)


def add_low(*items):
    total = items[0].astype(F32)
    for item in items[1:]:
        total = total + item.astype(F32)
    return total.astype(BF16)


class Reduction:
    def __init__(self, grads, core):
        self.core = core
        self.pair, self.next_b, self.own_b = grads
        self.got = cross_hop(self.pair, 1 - core)
        self.near_b = hop(self.next_b, "tensor", PARTNER)

    def first(self, *earlier):
        half = self.next_b.shape[0]
        self.parts = pair, own_b, got, near_b = after((self.pair, self.own_b, self.got, self.near_b), *earlier)
        self.added = add_low(pair[:half], got[:half]), add_low(own_b, near_b)
        self.near_a = core_hop(self.added[0], "tensor", PARTNER, self.core)
        self.far_b = cross_hop(self.added[1], 1 - self.core)
        return self.added

    def sum_halves(self, *earlier):
        half = self.next_b.shape[0]
        near_a, far_b, (pair, own_b, got, near_b) = after((self.near_a, self.far_b, self.parts), *earlier)
        return add_low(pair[half:], got[half:], near_a), add_low(own_b, near_b, far_b)

    def scatter(self):
        whole = jnp.concatenate(self.sums).reshape(-1, self.own_b.shape[2])
        return [lax.psum_scatter(whole, "dp", scatter_dimension=0, tiled=True)]

    def second(self, *earlier):
        self.sums = self.sum_halves(*earlier)
        if direct_dp():
            self.across = core_hop(self.sums[1], "dp", 2, self.core)
        return self.sums

    def third(self, *earlier):
        if not direct_dp():
            self.pieces = self.scatter()
            return self.pieces
        a, across = after((self.sums[0], self.across), *earlier)
        self.pieces = [add_low(a[k], across[k]) for k in range(2)]
        return self.pieces


def last_dp(reductions, *earlier):
    if not direct_dp():
        return [r.pieces for r in reductions]
    block = after(jnp.concatenate([r.pieces[1] for r in reductions], 1), *earlier)
    got = core_hop(block, "dp", 1, reductions[0].core)
    at, out = 0, []
    for r in reductions:
        width = r.pieces[0].shape[1]
        out.append([r.pieces[0], got[:, at : at + width]])
        at += width
    return out

VMEM_LIMIT = 48 * 1024 * 1024
CHUNK = 128


def takes(micros):
    return pl.CostEstimate(flops=int(micros * 1.1e9), bytes_accessed=0, transcendentals=0)


def params():
    return pltpu.CompilerParams(vmem_limit_bytes=VMEM_LIMIT)


ANY = pl.BlockSpec(memory_space=pl.ANY)
VM = pl.BlockSpec(memory_space=pltpu.VMEM)
SM = pl.BlockSpec(memory_space=pltpu.SMEM)


def sds(shape, dtype):
    return jax.ShapeDtypeStruct(shape, dtype)


def chunks(length, step=CHUNK):
    return [slice(i, i + step) for i in range(0, length, step)]


def norm_rows(z):
    centre = z - jnp.mean(z, -1, keepdims=True)
    spread = jnp.mean(centre * centre, -1, keepdims=True)
    scale = lax.rsqrt(spread + 1e-05)
    return centre * scale, scale


def norm_back_rows(d_out, gain, xhat, scale):
    g = d_out * gain
    m1 = jnp.mean(g, -1, keepdims=True)
    m2 = jnp.mean(g * xhat, -1, keepdims=True)
    return scale * (g - m1 - xhat * m2)


def gelu_parts(x):
    e = jnp.exp(-0.5 * x * x)
    t = 1.0 / (1.0 + 0.2316418882 * jnp.abs(x))
    poly = t * (
        0.127414796 + t * (-0.142248368 + t * (0.7107068705 + t * (-0.7265760135 + t * 0.5307027145)))
    )
    tail = poly * e
    cdf = jnp.where(x < 0.0, tail, 1.0 - tail)
    return x * cdf, cdf + x * e * 0.3989422804014327


def zrows(meta, k, rz):
    return pl.ds(pl.multiple_of(meta[1 + k], 64), rz)


def load_weights(meta, pieces, place, sems):
    own, near, far = pieces[:3]
    nz, rz, _ = own.shape
    half = nz // 2
    home = meta[0] == 1
    lists = None
    at = 0
    for j, mine in enumerate((own, near)):
        for k in range(nz):
            targets = place(j, zrows(meta, k, rz))
            lists = lists or [[] for _ in targets]
            for n, (dst, columns) in enumerate(targets):
                other = far.at[k, :, columns] if j == 0 else pieces[3 + k // half].at[k % half, :, columns]
                first = pltpu.make_async_copy(mine.at[k, :, columns], dst, sems.at[at])
                second = pltpu.make_async_copy(other, dst, sems.at[at])
                at += 1

                @pl.when(home)
                def _():
                    first.start()

                @pl.when(jnp.logical_not(home))
                def _():
                    second.start()

                lists[n].append(first)
    return lists


def wait_all(waits):
    for made in waits:
        made.wait()


def load_a(meta, pieces, w_a, sems):
    width = w_a.shape[2]
    return load_weights(meta, pieces, lambda j, rows: [(w_a.at[j, rows, :], pl.ds(0, width))], sems)[0]


def load_b(meta, pieces, w_i, w_f, sems):
    one = w_i.shape[1] // 2
    return load_weights(
        meta,
        pieces,
        lambda j, rows: [
            (w_i.at[rows, pl.ds(j * one, one)], pl.ds(0, one)),
            (w_f.at[rows, pl.ds(j * one, one)], pl.ds(one, one)),
        ],
        sems,
    )


def attn_forward(level, meta, x_or_mid, parts, norms, pieces, bias, seg_col, seg_row):
    nz, rz, four = pieces[0].shape
    length, width = x_or_mid.shape
    cols = four // 4
    three = 3 * cols
    heads = 2 * cols // HD

    def body(meta, *refs):
        refs = list(refs)
        src = refs.pop(0)
        if level:
            own, other, gain, shift = (refs.pop(0) for _ in range(4))
        pieces = [refs.pop(0) for _ in range(5)]
        bias, sc, sr = (refs.pop(0) for _ in range(3))
        part_out, qkv_out, probs_out, ctx_out = (refs.pop(0) for _ in range(4))
        if level:
            x_out, xhat_out, scale_out = (refs.pop(0) for _ in range(3))
        w_a, sems = refs
        waits = load_a(meta, pieces, w_a, sems)
        if level:
            for rows in chunks(length):
                z = src[rows, :] + (own[rows, :].astype(F32) + other[rows, :].astype(F32)) + shift[2:3, :]
                xhat, scale = norm_rows(z)
                x_out[rows, :] = (xhat * gain[1:2, :] + shift[3:4, :]).astype(BF16)
                xhat_out[rows, :] = xhat.astype(BF16)
                scale_out[rows, :] = scale
            x_ref = x_out
        else:
            x_ref = src
        wait_all(waits)
        for j in range(2):
            c = slice(j * three, (j + 1) * three)
            for rows in chunks(length, 256):
                qkv_out[rows, c] = (nn(x_ref[rows, :], w_a[j, :, :three]) + bias[:, c]).astype(BF16)
        v_t = jnp.concatenate(
            [qkv_out[:, j * three + 2 * cols : (j + 1) * three].astype(F32) for j in range(2)], 1
        ).T.astype(BF16)
        for queries in chunks(length, 256):
            same = sc[...] == sr[:, queries]
            outs = []
            for h in range(heads):
                j, i = divmod(h, cols // HD)
                at = j * three + i * HD
                q = qkv_out[queries, at : at + HD]
                k = qkv_out[:, at + cols : at + cols + HD]
                st = jnp.where(same, nt(k, q) * 0.125, -1e30)
                p = jnp.exp(st - jnp.max(st, 0, keepdims=True))
                p = (p * (1.0 / jnp.sum(p, 0, keepdims=True))).astype(BF16)
                probs_out[h, :, queries] = p
                outs.append(nn(v_t[h * HD : (h + 1) * HD], p))
            ctx = jnp.concatenate(outs, 0).T.astype(BF16)
            ctx_out[queries, :] = ctx
            part_out[queries, :] = (
                nt(ctx[:, :cols], w_a[0, :, three:]) + nt(ctx[:, cols:], w_a[1, :, three:])
            ).astype(BF16)

    outs = [
        sds((length, width), BF16), sds((length, 2 * three), BF16),
        sds((heads, length, length), BF16), sds((length, 2 * cols), BF16),
    ]
    args = [meta, x_or_mid]
    if level:
        args += [*parts, *norms]
        outs += [sds((length, width), BF16), sds((length, width), BF16), sds((length, 1), F32)]
    specs = [SM] + [VM] * (len(args) - 1) + [ANY] * 5 + [VM] * 3
    args += [*pieces, bias, seg_col, seg_row]
    return pl.pallas_call(
        body,
        out_shape=outs,
        in_specs=specs,
        out_specs=[VM] * len(outs),
        scratch_shapes=[pltpu.VMEM((2, width, four), BF16), pltpu.SemaphoreType.DMA((2 * nz,))],
        compiler_params=params(),
        cost_estimate=takes(13),
        name="attn_forward",
    )(*args)


def ffn_forward(meta, x, parts, gains, shifts, pieces, bias_in):
    nz, rz, units = pieces[0].shape
    length, width = x.shape

    def body(meta, x, own, other, gain, shift, p0, p1, p2, p3, p4, bias,
             part_out, mid_out, xhat_out, scale_out, act_out, slope_out, w_i, w_f, low, sems):
        first, second = load_b(meta, (p0, p1, p2, p3, p4), w_i, w_f, sems)
        for rows in chunks(length):
            z = x[rows, :].astype(F32) + (own[rows, :].astype(F32) + other[rows, :].astype(F32)) + shift[0:1, :]
            xhat, scale = norm_rows(z)
            mid = xhat * gain[0:1, :] + shift[1:2, :]
            mid_out[rows, :] = mid
            low[rows, :] = mid.astype(BF16)
            xhat_out[rows, :] = xhat.astype(BF16)
            scale_out[rows, :] = scale
        wait_all(first)
        for rows in chunks(length, 256):
            for c in chunks(units, 512):
                pre = nn(low[rows, :], w_i[:, c]) + bias[:, c]
                act, slope = gelu_parts(pre)
                act_out[rows, c] = act.astype(BF16)
                slope_out[rows, c] = slope.astype(BF16)
        wait_all(second)
        for rows in chunks(length, 256):
            part_out[rows, :] = nt(act_out[rows, :], w_f[...]).astype(BF16)

    return pl.pallas_call(
        body,
        out_shape=[
            sds((length, width), BF16), sds((length, width), F32), sds((length, width), BF16),
            sds((length, 1), F32), sds((length, units), BF16), sds((length, units), BF16),
        ],
        in_specs=[SM] + [VM] * 5 + [ANY] * 5 + [VM],
        out_specs=[VM] * 6,
        scratch_shapes=[
            pltpu.VMEM((width, units), BF16), pltpu.VMEM((width, units), BF16),
            pltpu.VMEM((length, width), BF16), pltpu.SemaphoreType.DMA((4 * nz,)),
        ],
        compiler_params=params(),
        cost_estimate=takes(9),
        name="ffn_forward",
    )(meta, x, *parts, gains, shifts, *pieces, bias_in)


def last_norm(mid, parts, gains, shifts, tok_row, cls_pos):
    length, width = mid.shape
    n_cls = cls_pos.shape[0]

    def body(cls, mid, own, other, gain, shift, tok, y_out, xhat_out, scale_out, cls_out):
        for rows in chunks(length):
            z = mid[rows, :] + (own[rows, :].astype(F32) + other[rows, :].astype(F32)) + shift[2:3, :]
            xhat, scale = norm_rows(z)
            y_out[rows, :] = (xhat * gain[1:2, :] + shift[3:4, :]).astype(BF16)
            xhat_out[rows, :] = xhat.astype(BF16)
            scale_out[rows, :] = scale
        which = lax.broadcasted_iota(jnp.int32, (16, length), 0)
        hot = jnp.zeros((16, length), F32)
        for p in range(n_cls):
            hot = jnp.where(jnp.logical_and(which == p, tok[...] == cls[p]), 1.0, hot)
        cls_out[...] = nn(hot.astype(BF16), y_out[...])[:n_cls].astype(BF16)

    return pl.pallas_call(
        body,
        out_shape=[
            sds((length, width), BF16), sds((length, width), BF16), sds((length, 1), F32),
            sds((n_cls, width), BF16),
        ],
        in_specs=[SM] + [VM] * 6,
        out_specs=[VM] * 4,
        compiler_params=params(),
        cost_estimate=takes(2),
        name="last_norm",
    )(cls_pos, mid, *parts, gains, shifts, tok_row)


def ffn_backward(level, meta, sources, xhat, scale, gains, slope, pieces):
    nz, rz, units = pieces[0].shape
    length, width = xhat.shape
    n_cls = sources[3].shape[0] if level else 0

    def body(meta, *refs):
        refs = list(refs)
        if level:
            cls, grad, d_cls, tok = (refs.pop(0) for _ in range(4))
        else:
            d_above, own, other = (refs.pop(0) for _ in range(3))
        xhat, scale, gain, slope = (refs.pop(0) for _ in range(4))
        pieces = [refs.pop(0) for _ in range(5)]
        part_out, second_out, low_out, pre_out, vec_out, inb_out, w_i, w_f, sems = refs
        first, second = load_b(meta, pieces, w_i, w_f, sems)
        sums = [jnp.zeros((1, width), F32) for _ in range(3)]
        for rows in chunks(length):
            if level:
                d_out = grad[rows, :].astype(F32)
                for p in range(n_cls):
                    d_out = d_out + jnp.where(tok[rows, :] == cls[p], 1.0, 0.0) * d_cls[p : p + 1, :]
            else:
                d_out = d_above[rows, :] + (own[rows, :].astype(F32) + other[rows, :].astype(F32))
                d_out = d_out.astype(BF16).astype(F32)
            hat = xhat[rows, :].astype(F32)
            d_second = norm_back_rows(d_out, gain[1:2, :], hat, scale[rows, :])
            second_out[rows, :] = d_second
            low_out[rows, :] = d_second.astype(BF16)
            for n, item in enumerate((d_out * hat, d_out, d_second)):
                sums[n] = sums[n] + jnp.sum(item, 0, keepdims=True)
        for n in range(3):
            vec_out[n : n + 1, :] = sums[n]
        wait_all(second)
        for n, rows in enumerate(chunks(length, 256)):
            for c in chunks(units, units // 4):
                d_act = nn(low_out[rows, :], w_f[:, c])
                d_pre = (slope[rows, c].astype(F32) * d_act).astype(BF16)
                pre_out[rows, c] = d_pre
                j, at = divmod(c.start, units // 2)
                at = slice(at, at + c.stop - c.start)
                total = jnp.sum(d_pre.astype(F32), 0, keepdims=True)
                inb_out[j : j + 1, at] = total if n == 0 else inb_out[j : j + 1, at] + total
        wait_all(first)
        for rows in chunks(length, 256):
            part_out[rows, :] = nt(pre_out[rows, :], w_i[...]).astype(BF16)

    if level:
        token_grad, d_cls, tok_col, cls_pos = sources
        args, specs = [meta, cls_pos, token_grad, d_cls, tok_col], [SM, SM, VM, VM, VM]
    else:
        args, specs = [meta, *sources], [SM, VM, VM, VM]
    args += [xhat, scale, gains, slope, *pieces]
    specs += [VM] * 4 + [ANY] * 5
    return pl.pallas_call(
        body,
        out_shape=[
            sds((length, width), BF16), sds((length, width), F32), sds((length, width), BF16),
            sds((length, units), BF16), sds((3, width), F32), sds((2, units // 2), F32),
        ],
        in_specs=specs,
        out_specs=[VM] * 6,
        scratch_shapes=[
            pltpu.VMEM((width, units), BF16), pltpu.VMEM((width, units), BF16),
            pltpu.SemaphoreType.DMA((4 * nz,)),
        ],
        compiler_params=params(),
        cost_estimate=takes(9),
        name="ffn_backward",
    )(*args)


def halves_of(nz, rz, width):
    half = nz // 2
    return [sds((nz, rz, width), BF16), sds((half, rz, width), BF16), sds((half, rz, width), BF16)]


def place_half(outs, j, k, nz):
    half = nz // 2
    if k < half:
        return outs[0], k + (half if j == 0 else 0)
    return outs[2 if j == 0 else 1], k - half


def ffn_grads(meta, mid, d_pre, d_ffn, act, nz):
    length, width = mid.shape
    units = d_pre.shape[1]
    one = units // 2
    rz = width // nz

    def body(meta, mid, d_pre, d_ffn, act, *refs):
        outs, (mid_t, ffn_t) = refs[:3], refs[3:]
        mid_t[...] = mid[...].T.astype(BF16)
        ffn_t[...] = d_ffn[...].astype(F32).T.astype(BF16)
        for j in range(2):
            c = slice(j * one, (j + 1) * one)
            for k in range(nz):
                rows = zrows(meta, k, rz)
                out, at = place_half(outs, j, k, nz)
                out[at, :, :one] = nn(mid_t[rows, :], d_pre[:, c]).astype(BF16)
                out[at, :, one:] = nn(ffn_t[rows, :], act[:, c]).astype(BF16)

    return pl.pallas_call(
        body,
        out_shape=halves_of(nz, rz, units),
        in_specs=[SM] + [VM] * 4,
        out_specs=[VM] * 3,
        scratch_shapes=[pltpu.VMEM((width, length), BF16)] * 2,
        compiler_params=params(),
        cost_estimate=takes(7),
        name="ffn_grads",
    )(meta, mid, d_pre, d_ffn, act)


def attn_backward(meta, d_second, parts, xhat, scale, gains, qkv, probs, pieces):
    nz, rz, four = pieces[0].shape
    length, width = d_second.shape
    cols = four // 4
    three = 3 * cols
    heads = 2 * cols // HD

    def body(meta, d_second, own, other, xhat, scale, gain, qkv, probs, p0, p1, p2, p3, p4,
             part_out, first_out, low_out, dqkv_out, vec_out, sum_out,
             w_a, d_ctx, acc_v, acc_k, sems):
        waits = load_a(meta, (p0, p1, p2, p3, p4), w_a, sems)
        sums = [jnp.zeros((1, width), F32) for _ in range(3)]
        for rows in chunks(length):
            d_mid = d_second[rows, :] + (own[rows, :].astype(F32) + other[rows, :].astype(F32))
            hat = xhat[rows, :].astype(F32)
            d_first = norm_back_rows(d_mid, gain[0:1, :], hat, scale[rows, :])
            first_out[rows, :] = d_first
            low_out[rows, :] = d_first.astype(BF16)
            for n, item in enumerate((d_mid * hat, d_mid, d_first)):
                sums[n] = sums[n] + jnp.sum(item, 0, keepdims=True)
        for n in range(3):
            vec_out[n : n + 1, :] = sums[n]
        wait_all(waits)
        for j in range(2):
            for rows in chunks(length, 256):
                d_ctx[rows, j * cols : (j + 1) * cols] = nn(low_out[rows, :], w_a[j, :, three:]).astype(BF16)
        k_t = jnp.concatenate(
            [qkv[:, j * three + cols : j * three + 2 * cols].astype(F32) for j in range(2)], 1
        ).T.astype(BF16)
        for h in range(heads):
            j, i = divmod(h, cols // HD)
            at = j * three + i * HD
            q_cols, k_cols, v_cols = (slice(at + n * cols, at + n * cols + HD) for n in range(3))
            for n, queries in enumerate(chunks(length, 256)):
                d_o = d_ctx[queries, h * HD : (h + 1) * HD]
                d_p = nt(qkv[:, v_cols], d_o)
                p = probs[h, :, queries]
                wide = p.astype(F32)
                d_s = (wide * (d_p - jnp.sum(wide * d_p, 0, keepdims=True))).astype(BF16)
                d_v = nn(p, d_o)
                d_k = nn(d_s, qkv[queries, q_cols])
                acc_v[...] = d_v if n == 0 else acc_v[...] + d_v
                acc_k[...] = d_k if n == 0 else acc_k[...] + d_k
                d_q = nn(k_t[h * HD : (h + 1) * HD], d_s)
                dqkv_out[queries, q_cols] = (d_q.T * 0.125).astype(BF16)
            dqkv_out[:, v_cols] = acc_v[...].astype(BF16)
            dqkv_out[:, k_cols] = (acc_k[...] * 0.125).astype(BF16)
        for j in range(2):
            sum_out[j : j + 1, :] = jnp.sum(
                dqkv_out[:, j * three : (j + 1) * three].astype(F32), 0, keepdims=True
            )
        for rows in chunks(length, 256):
            part_out[rows, :] = (
                nt(dqkv_out[rows, :three], w_a[0, :, :three]) + nt(dqkv_out[rows, three:], w_a[1, :, :three])
            ).astype(BF16)

    return pl.pallas_call(
        body,
        out_shape=[
            sds((length, width), BF16), sds((length, width), F32), sds((length, width), BF16),
            sds((length, 2 * three), BF16), sds((3, width), F32), sds((2, three), F32),
        ],
        in_specs=[SM] + [VM] * 8 + [ANY] * 5,
        out_specs=[VM] * 6,
        scratch_shapes=[
            pltpu.VMEM((2, width, four), BF16), pltpu.VMEM((length, 2 * cols), BF16),
            pltpu.VMEM((length, HD), F32), pltpu.VMEM((length, HD), F32),
            pltpu.SemaphoreType.DMA((2 * nz,)),
        ],
        compiler_params=params(),
        cost_estimate=takes(15),
        name="attn_backward",
    )(meta, d_second, *parts, xhat, scale, gains, qkv, probs, *pieces)


def attn_grads(meta, x, d_attn, d_qkv, ctx, nz):
    length, width = x.shape
    three = d_qkv.shape[1] // 2
    cols = ctx.shape[1] // 2
    rz = width // nz

    def body(meta, x, d_attn, d_qkv, ctx, *refs):
        outs, (x_t, a_t) = refs[:3], refs[3:]
        x_t[...] = x[...].astype(F32).T.astype(BF16)
        a_t[...] = d_attn[...].astype(F32).T.astype(BF16)
        for j in range(2):
            for k in range(nz):
                rows = zrows(meta, k, rz)
                out, at = place_half(outs, j, k, nz)
                out[at, :, :three] = nn(x_t[rows, :], d_qkv[:, j * three : (j + 1) * three]).astype(BF16)
                out[at, :, three:] = nn(a_t[rows, :], ctx[:, j * cols : (j + 1) * cols]).astype(BF16)

    return pl.pallas_call(
        body,
        out_shape=halves_of(nz, rz, three + cols),
        in_specs=[SM] + [VM] * 4,
        out_specs=[VM] * 3,
        scratch_shapes=[pltpu.VMEM((width, length), BF16)] * 2,
        compiler_params=params(),
        cost_estimate=takes(4),
        name="attn_grads",
    )(meta, x, d_attn, d_qkv, ctx)


def loss_kernel(own, perm, slots, queries, positive_col, n_own):
    n_q, width = queries.shape
    n_p = slots.shape[0]

    def body(own, perm, slots, queries, pos, loss_out, d_out):
        passages = nn(perm[...], slots[...]).astype(BF16)
        logits = nt(queries[...], passages)
        top = jnp.max(logits, -1, keepdims=True)
        log_total = top + jnp.log(jnp.sum(jnp.exp(logits - top), -1, keepdims=True))
        index = lax.broadcasted_iota(jnp.int32, (n_q, n_p), 1)
        hits = pos[...] == index
        chosen = jnp.sum(jnp.where(hits, logits, 0.0), -1, keepdims=True)
        loss_out[...] = jnp.sum(log_total - chosen, 0, keepdims=True) / n_q
        d_logits = (16.0 * (jnp.exp(logits - log_total) - jnp.where(hits, 1.0, 0.0))).astype(BF16)
        pick = jnp.where(
            lax.broadcasted_iota(jnp.int32, (n_p, 128), 0)
            == lax.broadcasted_iota(jnp.int32, (n_p, 128), 1) + own[0],
            1.0, 0.0,
        ).astype(BF16)
        cols = nn(d_logits, pick)
        d_out[...] = nn(cols.T.astype(BF16), queries[...])[:n_own]

    return pl.pallas_call(
        body,
        out_shape=[sds((1, 1), F32), sds((n_own, width), F32)],
        in_specs=[SM] + [VM] * 4,
        out_specs=[VM] * 2,
        compiler_params=params(),
        cost_estimate=takes(1),
        name="contrast",
    )(own, perm, slots, queries, positive_col)


def on_device(
    inputs, cls_pos, w_qkv, qv_bias, w_out, w_in, in_bias, w_ffn_out,
    layer_gains, shifts, queries, positive, token_grad,
):
    core = lax.axis_index("section")
    dp = lax.axis_index("dp")
    me = lax.axis_index("tensor")
    n_dp = lax.axis_size("dp")
    n_t = lax.axis_size("tensor")
    first_core = core == 0
    rows_dev, share, width = inputs.shape
    cols = w_qkv.shape[3]
    units = w_in.shape[2]
    length = n_t * share
    n_chips = n_dp * n_t
    piece = width // n_chips
    order = dp_order()
    direct = direct_dp()
    nz = 4 if direct else 2
    t_ids = jnp.arange(n_t, dtype=jnp.int32)

    vec = jnp.concatenate(
        [layer_gains.reshape(-1), shifts.reshape(-1), qv_bias.reshape(-1), in_bias.reshape(-1)]
    )
    n_gain, n_shift, n_qv, n_inb = layer_gains.size, shifts.size, qv_bias.size, in_bias.size
    n_vec = vec.shape[0]
    flat = jnp.concatenate(
        [vec, queries.reshape(-1), (positive // 16).astype(BF16), (positive % 16).astype(BF16)]
    )
    flat = jnp.pad(flat, (0, -flat.shape[0] % 2048)).reshape(-1, 128)

    both = jnp.concatenate([inputs, token_grad], 1)
    both = [lax.dynamic_index_in_dim(both, me ^ k, 0, keepdims=False) for k in range(n_t)]
    both = exchange_rows(both)
    x_low = jnp.concatenate([b[:share] for b in both], 0)
    tokens = jnp.concatenate([b[share:] for b in both], 0)

    pack_a = jnp.concatenate([w_qkv[0, :, 0], w_qkv[0, :, 1], w_qkv[0, :, 2], w_out[0].T], 1)
    pack_b = jnp.concatenate([w_in[0], w_ffn_out[0].T], 1)
    dp_a0 = all_dp(pack_a, 0)
    one_b0 = first_dp(pack_b, 0)
    z_a0 = whole_dp(dp_a0, x_low, tokens)
    near_a0 = gather_near(z_a0, 0)
    dp_b0 = second_dp(after(pack_b, z_a0), one_b0, 0)
    message = after(flat, z_a0)
    message = double(message, "dp") if direct else spread_dp(message)
    message = double(after(message, near_a0), "tensor")
    one_1 = first_dp(after(jnp.concatenate([pack_a, pack_b], 1), z_a0), 1)
    both_a0 = gather_both(*near_a0, 0)
    a0 = [z_a0, *near_a0, *both_a0]

    zrow = order * (width // n_dp) if direct else jnp.arange(2, dtype=jnp.int32) * (width // 2)
    metas = [
        jnp.concatenate([(core == level)[None].astype(jnp.int32), zrow.astype(jnp.int32)])
        for level in range(2)
    ]
    slots = [me ^ (2 * (core != level) + jnp.arange(2, dtype=jnp.int32)) for level in range(2)]
    hots = [(s[:, None] == t_ids[None, :]).astype(F32) for s in slots]

    positions = jnp.concatenate(
        [(me ^ k) * share + jnp.arange(share, dtype=jnp.int32) for k in range(n_t)]
    )
    cls_row = lax.dynamic_index_in_dim(cls_pos, me, 0, keepdims=False)
    segments = jnp.sum((positions[:, None] >= cls_row[None, :]).astype(jnp.int32), -1)
    seg_col, seg_row = segments[:, None], segments[None, :]
    tok_col, tok_row = positions[:, None], positions[None, :]

    slot_ids = (order[None, :] * n_t + (me ^ t_ids)[:, None]).reshape(-1)
    to_natural = (jnp.arange(n_chips, dtype=jnp.int32)[:, None] == slot_ids[None, :]).astype(BF16)
    table = nn(to_natural, message.reshape(n_chips, -1))
    own_table = table[:, :n_vec].astype(BF16)
    other_table = swap_cores(own_table)
    tables = jnp.where(
        first_core, jnp.stack([own_table, other_table]), jnp.stack([other_table, own_table])
    ).astype(F32)
    at = 0
    gains = tables[:, :, at : at + n_gain].reshape(2, n_chips, 2, piece).transpose(0, 2, 1, 3).reshape(2, 2, width)
    at += n_gain
    shift = tables[:, :, at : at + n_shift].reshape(2, n_chips, 4, piece).transpose(0, 2, 1, 3).reshape(2, 4, width)
    at += n_shift
    qv = tables[:, :, at : at + n_qv].reshape(2, n_dp, n_t, 2, cols // n_dp)
    qv = qv.transpose(0, 3, 2, 1, 4).reshape(2, 2, n_t, cols)
    at += n_qv
    inb = tables[:, :, at : at + n_inb].reshape(2, n_dp, n_t, n_inb).transpose(0, 2, 1, 3).reshape(2, n_t, units)
    vectors = []
    for level in range(2):
        bias = jnp.sum(hots[level][None, :, :, None] * qv[level][:, None], 2)
        bias = jnp.stack([bias[0], jnp.zeros_like(bias[0]), bias[1]], 1).reshape(1, -1)
        bias_in = jnp.sum(hots[level][:, :, None] * inb[level][None], 1).reshape(1, -1)
        vectors.append((gains[level], shift[level], bias, bias_in))
    at = n_vec
    q_dev = queries.shape[0]
    all_q = table[:, at : at + q_dev * width].reshape(-1, width).astype(BF16)
    at += q_dev * width
    all_pos = table[:, at : at + q_dev] * 16.0 + table[:, at + q_dev : at + 2 * q_dev]
    all_pos = all_pos.astype(jnp.int32).reshape(-1, 1)
    n_cls = cls_row.shape[0]
    perm = jnp.repeat(jnp.repeat(to_natural, n_cls, 0), n_cls, 1)
    perm = perm * jnp.tile(jnp.eye(n_cls, dtype=BF16), (n_chips, n_chips))

    vectors, all_q, all_pos, perm, x_low = lax.optimization_barrier(
        (vectors, all_q, all_pos, perm, x_low)
    )
    saved = []
    z_b0 = whole_dp(dp_b0, both_a0)
    near_b0 = gather_near(z_b0, 0)
    one_a1, one_b1 = one_1[:, :width], one_1[:, width:]
    dp_a1 = second_dp(after(pack_a, z_b0), one_a1, 1)
    source, parts, norms = after(x_low, z_b0), None, None
    pieces_a, pieces_b = [a0, None], [None, None]
    for level in range(2):
        gain, shift, bias, bias_in = vectors[level]
        outs = attn_forward(
            level, metas[level], source, parts, norms, pieces_a[level], bias, seg_col, seg_row
        )
        part, qkv, probs, ctx = outs[:4]
        if level == 0:
            z_a1 = whole_dp(dp_a1, part)
            dp_b1 = second_dp(after(pack_b, z_a1), one_b1, 1)
            both_b0 = gather_both(*after(near_b0, z_a1), 0)
            near_a1 = gather_near(after(z_a1, near_b0), 1)
            pieces_b[0] = [z_b0, *near_b0, *both_b0]
        else:
            near_b1, part = lax.optimization_barrier((near_b1, part))
            both_b1 = gather_both(*near_b1, 1)
            pieces_b[1] = [z_b1, *near_b1, *both_b1]
        if level:
            x, xhat2, scale2 = outs[4:]
            saved[0]["second"] = (xhat2, scale2)
        else:
            x = x_low
        part, mid, xhat1, scale1, act, slope = ffn_forward(
            metas[level], x, (part, swap_cores(part)), gain, shift, pieces_b[level], bias_in
        )
        saved.append(
            dict(x=x, qkv=qkv, probs=probs, ctx=ctx, mid=mid, xhat1=xhat1, scale1=scale1, act=act, slope=slope)
        )
        source, parts, norms = mid, (part, swap_cores(part)), (gain, shift)
        if level == 0:
            z_b1 = whole_dp(dp_b1, part)
            near_a1, z_b1 = lax.optimization_barrier((near_a1, z_b1))
            both_a1 = gather_both(*near_a1, 1)
            near_b1 = gather_near(after(z_b1, both_a1), 1)
            pieces_a[1] = [z_a1, *near_a1, *both_a1]
    y, xhat2, scale2, cls_own = last_norm(source, parts, *norms, tok_row, cls_row)
    saved[1]["second"] = (xhat2, scale2)

    cls_slots = spread_tensor(spread_dp(cls_own)).reshape(n_chips * n_cls, width)
    first_own = ((dp * n_t + me) * n_cls).astype(jnp.int32)[None]
    mean_loss, d_cls = loss_kernel(first_own, perm, cls_slots, all_q, all_pos, n_cls)

    vector_rows = [None, None]
    sources = (tokens, d_cls, tok_col, cls_row)
    sums_a, sums_b = [None, None], [None, None]
    for level in (1, 0):
        gain = vectors[level][0]
        kept = saved[level]
        meta = metas[level]
        xhat2, scale2 = kept["second"]
        if level == 0:
            sources = (after(sources[0], sums_b[1].first(grads_a[1])), *sources[1:])
        part, d_second, d_ffn, d_pre, vec2, sum_inb = ffn_backward(
            level, meta, sources, xhat2, scale2, gain, kept["slope"], pieces_b[level]
        )
        other = swap_cores(part)
        if level == 0:
            d_ffn = after(d_ffn, sums_a[1].first(part))
        grads_b = ffn_grads(meta, kept["mid"], d_pre, d_ffn, kept["act"], nz)
        sums_b[level] = Reduction(grads_b, level)
        d_second = after(d_second, grads_b[1])
        if level == 0:
            d_second = after(d_second, sums_b[1].second(grads_b[1]))
        part, d_first, d_attn, d_qkv, vec1, sum_qkv = attn_backward(
            meta, d_second, (part, other), kept["xhat1"], kept["scale1"], gain,
            kept["qkv"], kept["probs"], pieces_a[level],
        )
        other = swap_cores(part)
        if level == 0:
            d_attn = after(d_attn, sums_a[1].second(part))
        grads_a = attn_grads(meta, kept["x"], d_attn, d_qkv, kept["ctx"], nz)
        sums_a[level] = Reduction(grads_a, level)
        vector_rows[level] = (vec1, vec2, sum_qkv, sum_inb)
        sources = (d_first, part, other)
    sums_b[0].first(grads_a[1])
    sums_b[1].third(sums_b[0].added)
    sums_a[0].first(sums_b[1].pieces)
    sums_a[1].third(sums_a[0].added)
    last_b1, last_a1 = last_dp([sums_b[1], sums_a[1]])
    sums_b[0].second(sums_a[1].pieces)
    sums_a[0].second(sums_b[0].sums)
    sums_b[0].third(sums_a[0].sums)
    d_hidden = d_first + (part.astype(F32) + other.astype(F32))
    outgoing = jnp.where(first_core, d_hidden, y.astype(F32))
    low = after(outgoing.astype(BF16), sums_a[0].sums).reshape(n_t, share, width)
    incoming = [outgoing[:share]] + [b.astype(F32) for b in exchange_rows([low[k] for k in range(n_t)])[1:]]
    boundary = jnp.zeros((n_t, share, width), F32)
    for k in range(n_t):
        boundary = lax.dynamic_update_index_in_dim(boundary, incoming[k], me ^ k, 0)
    vector_rows, _ = lax.optimization_barrier((vector_rows, sums_a[0].sums))
    wide = 3 * cols + units

    def vector_table(level):
        vec1, vec2, sum_qkv, sum_inb = vector_rows[level]
        by_t = lax.dot_general(
            hots[level], jnp.concatenate([sum_qkv, sum_inb], 1), (((0,), (0,)), ((), ())),
            precision=lax.Precision.HIGHEST,
        )
        whole = 0.5 * jnp.concatenate([vec1, vec2])
        return jnp.concatenate([jnp.pad(whole, ((0, 2), (0, wide - width))), by_t, jnp.zeros((4, wide), F32)])

    rows0, rows1 = vector_table(0), vector_table(1)
    flat = jnp.where(first_core, rows0, rows1) + swap_cores(jnp.where(first_core, rows1, rows0))
    flat = flat + hop(flat, "tensor", 1)
    flat = flat + hop(flat, "tensor", 2)
    if direct:
        flat = flat + hop(flat, "dp", 1)
        flat = flat + hop(flat, "dp", 2)
    else:
        flat = lax.psum(flat, "dp")
    sums_a[0].third(flat, sums_b[0].pieces)
    last_b0, last_a0 = last_dp([sums_b[0], sums_a[0]])
    tot_b, tot_a = (
        jnp.where(first_core, sum(p.astype(F32) for p in low), sum(p.astype(F32) for p in high))
        for low, high in ((last_b0, last_b1), (last_a0, last_a1))
    )
    own = lax.dynamic_slice_in_dim(flat[:6, :width], (dp * n_t + me) * piece, piece, 1)
    grad_gains = jnp.concatenate([own[0:1], own[3:4]]).reshape(layer_gains.shape)
    grad_shifts = jnp.concatenate([own[2:3], own[1:2], own[5:6], own[4:5]]).reshape(shifts.shape)
    by_t = lax.dynamic_slice_in_dim(flat, 8 + me, 1, 0)
    qv = jnp.concatenate([by_t[:, :cols], by_t[:, 2 * cols : 3 * cols]])
    grad_qv = lax.dynamic_slice_in_dim(qv, dp * qv_bias.shape[3], qv_bias.shape[3], 1).reshape(qv_bias.shape)
    grad_inb = lax.dynamic_slice_in_dim(by_t[:, 3 * cols :], dp * n_inb, n_inb, 1).reshape(in_bias.shape)

    grad_qkv = jnp.stack([tot_a[:, n * cols : (n + 1) * cols] for n in range(3)], 1)[None]
    grad_out = tot_a[:, 3 * cols :].T[None]
    grad_in = tot_b[:, :units][None]
    grad_ffn = tot_b[:, units:].T[None]
    return (
        grad_qkv, grad_qv, grad_out, grad_in, grad_inb, grad_ffn,
        grad_gains, grad_shifts, boundary[None], mean_loss.reshape(()),
    )


def solution(mesh):
    return jax.shard_map(
        on_device,
        mesh=mesh,
        in_specs=(
            P("dp", "tensor", None),
            P("dp", None),
            P("section", "dp", None, "tensor"),
            P("section", None, "tensor", "dp"),
            P("section", "tensor", "dp"),
            P("section", "dp", "tensor"),
            P("section", "tensor", "dp"),
            P("section", "tensor", "dp"),
            P("section", None, ("dp", "tensor")),
            P("section", None, ("dp", "tensor")),
            P(("dp", "tensor"), None),
            P(("dp", "tensor")),
            P("dp", "tensor", None),
        ),
        out_specs=(
            P("section", "dp", None, "tensor"),
            P("section", None, "tensor", "dp"),
            P("section", "tensor", "dp"),
            P("section", "dp", "tensor"),
            P("section", "tensor", "dp"),
            P("section", "tensor", "dp"),
            P("section", None, ("dp", "tensor")),
            P("section", None, ("dp", "tensor")),
            P("section", "dp", "tensor", None),
            P(),
        ),
        check_vma=False,
    )
```

```python
import jax
import jax.numpy as jnp
from jax import lax
from jax.experimental import pallas as pl
from jax.experimental.pallas import tpu as pltpu
from jax.sharding import PartitionSpec as P

HD = 64
PARTNER = 1
CROSS = 2
BF16 = jnp.bfloat16
F32 = jnp.float32


def mm(left, right, dims):
    return lax.dot_general(left, right, (dims, ((), ())), preferred_element_type=F32)


def nn(left, right):
    return mm(left, right, ((1,), (0,)))


def nt(left, right):
    return mm(left, right, ((1,), (1,)))


def after(block, *earlier):
    return lax.optimization_barrier((block, *earlier))[0]


def swap_cores(block):
    return lax.ppermute(block, "section", [(0, 1), (1, 0)])


def hop(block, axis, flip):
    return lax.ppermute(block, axis, [(i, i ^ flip) for i in range(lax.axis_size(axis))])


def core_hop(block, axis, flip, core):
    size = lax.axis_size(axis)
    route = [(core * size + i, core * size + (i ^ flip)) for i in range(size)]
    return lax.ppermute(block, ("section", axis), route)


def cross_hop(block, source):
    size = lax.axis_size("tensor")
    route = [(source * size + i, (1 - source) * size + (i ^ CROSS)) for i in range(size)]
    return lax.ppermute(block, ("section", "tensor"), route)


def direct_dp():
    return lax.axis_size("dp") == 4


def dp_order():
    size = lax.axis_size("dp")
    if direct_dp():
        return lax.axis_index("dp") ^ jnp.arange(size, dtype=jnp.int32)
    return jnp.arange(size, dtype=jnp.int32)


def spread_dp(block):
    if direct_dp():
        return jnp.stack([block] + [hop(block, "dp", k) for k in range(1, 4)])
    return lax.all_gather(block, "dp", axis=0, tiled=False)


def spread_tensor(block):
    return jnp.stack([block] + [hop(block, "tensor", k) for k in range(1, 4)])


def double(block, axis):
    pair = jnp.stack([block, hop(block, axis, 1)])
    return jnp.concatenate([pair, hop(pair, axis, 2)])


def exchange_rows(blocks):
    first = hop(jnp.stack([blocks[1], blocks[3]]), "tensor", 1)
    second = hop(jnp.stack([blocks[2], first[1]]), "tensor", 2)
    return [blocks[0], first[0], second[0], second[1]]


def cross_all(block):
    size = lax.axis_size("tensor")
    route = [(s * size + i, (1 - s) * size + (i ^ CROSS)) for s in range(2) for i in range(size)]
    return lax.ppermute(block, ("section", "tensor"), route)


def rest_dp(own, one, core, *earlier):
    pair = after(jnp.stack([own, one]), *earlier)
    return one, core_hop(pair, "dp", 2, core)


def stack_rest(rest, *earlier):
    one, two = after(rest, *earlier)
    return jnp.concatenate([one[None], two])


def gather_own(own):
    near, far = hop(own, "tensor", PARTNER), cross_all(own)
    return near, far


def gather_own_both(near, far):
    half = near.shape[1] // 2
    return cross_all(near[:, :half]), hop(far[:, half:], "tensor", PARTNER)


def gather_near(rest, core):
    return core_hop(rest, "tensor", PARTNER, core), cross_hop(rest, core)


def gather_both(near, far, core):
    half = near.shape[2] // 2
    return cross_hop(near[:, :, :half], core), core_hop(far[:, :, half:], "tensor", PARTNER, 1 - core)


def add_low(*items):
    total = items[0].astype(F32)
    for item in items[1:]:
        total = total + item.astype(F32)
    return total.astype(BF16)


class Reduction:
    def __init__(self, grads, core):
        self.core = core
        self.pair, self.next_b, self.own_b = grads
        self.got = cross_hop(self.pair, 1 - core)
        self.near_b = hop(self.next_b, "tensor", PARTNER)

    def first(self, *earlier):
        self.parts = pair, own_b, got, near_b = after((self.pair, self.own_b, self.got, self.near_b), *earlier)
        self.added = add_low(pair[0], got[0]), add_low(own_b, near_b)
        self.near_a = core_hop(self.added[0], "tensor", PARTNER, self.core)
        self.far_b = cross_hop(self.added[1], 1 - self.core)
        return self.added

    def second(self, *earlier):
        near_a, far_b, (pair, own_b, got, near_b) = after((self.near_a, self.far_b, self.parts), *earlier)

        def both(k):
            return jnp.concatenate(
                [add_low(pair[1][k], got[1][k], near_a[k]), add_low(own_b[k], near_b[k], far_b[k])], -1
            )

        if not direct_dp():
            self.sums = [both(slice(None))]
            return self.sums
        self.sums = both(slice(1, None)), both(0)
        self.across = core_hop(self.sums[0], "dp", 2, self.core)
        return self.sums

    def third(self, *earlier):
        if not direct_dp():
            self.pieces = self.sums
            return self.pieces
        one, across = after((self.sums[1], self.across), *earlier)
        self.pieces = [across[0], add_low(one, across[1])]
        return self.pieces


def last_dp(reductions, *earlier):
    if not direct_dp():
        return jnp.concatenate([r.pieces[0][0].astype(F32) for r in reductions], 1)
    block = after(jnp.concatenate([r.pieces[1] for r in reductions], 1), *earlier)
    got = core_hop(block, "dp", 1, reductions[0].core)
    here = jnp.concatenate([r.pieces[0] for r in reductions], 1)
    return here, got


class OwnReduction:
    def __init__(self, slots, *earlier):
        first_core = lax.axis_index("section") == 0
        low, high = after(slots, *earlier)
        self.here, self.away = jnp.where(first_core, low, high), jnp.where(first_core, high, low)
        self.half = half = low.shape[2] // 2
        self.got = cross_all(jnp.stack([self.away[1][:, :half], self.away[0][:, :half]]))
        self.near_b = hop(jnp.stack([self.here[1][:, half:], self.away[1][:, half:]]), "tensor", PARTNER)

    def first(self, *earlier):
        here, away, got, near_b = after((self.here, self.away, self.got, self.near_b), *earlier)
        half = self.half
        self.parts = here, got, near_b
        self.added = add_low(here[1][:, :half], got[0]), add_low(away[0][:, half:], near_b[1])
        self.near_a = hop(self.added[0], "tensor", PARTNER)
        self.far_b = cross_all(self.added[1])
        return self.added

    def second(self, *earlier):
        near_a, far_b, (here, got, near_b) = after((self.near_a, self.far_b, self.parts), *earlier)
        here, got, near_b, near_a, far_b = (v.astype(F32) for v in (here, got, near_b, near_a, far_b))
        half = self.half
        return jnp.concatenate(
            [here[0][:, :half] + got[1] + near_a, here[0][:, half:] + near_b[0] + far_b], 1
        )


VMEM_LIMIT = 48 * 1024 * 1024
CHUNK = 128


def takes(micros):
    return pl.CostEstimate(flops=int(micros * 1.1e9), bytes_accessed=0, transcendentals=0)


def params():
    return pltpu.CompilerParams(vmem_limit_bytes=VMEM_LIMIT)


ANY = pl.BlockSpec(memory_space=pl.ANY)
VM = pl.BlockSpec(memory_space=pltpu.VMEM)
SM = pl.BlockSpec(memory_space=pltpu.SMEM)


def sds(shape, dtype):
    return jax.ShapeDtypeStruct(shape, dtype)


def chunks(length, step=CHUNK):
    return [slice(i, i + step) for i in range(0, length, step)]


def norm_rows(z):
    centre = z - jnp.mean(z, -1, keepdims=True)
    spread = jnp.mean(centre * centre, -1, keepdims=True)
    scale = lax.rsqrt(spread + 1e-05)
    return centre * scale, scale


def norm_back_rows(d_out, gain, xhat, scale):
    g = d_out * gain
    m1 = jnp.mean(g, -1, keepdims=True)
    m2 = jnp.mean(g * xhat, -1, keepdims=True)
    return scale * (g - m1 - xhat * m2)


def gelu_parts(x):
    e = jnp.exp(-0.5 * x * x)
    t = 1.0 / (1.0 + 0.2316418882 * jnp.abs(x))
    poly = t * (
        0.127414796 + t * (-0.142248368 + t * (0.7107068705 + t * (-0.7265760135 + t * 0.5307027145)))
    )
    tail = poly * e
    cdf = jnp.where(x < 0.0, tail, 1.0 - tail)
    return x * cdf, cdf + x * e * 0.3989422804014327


def zrows(meta, k, rz):
    return pl.ds(pl.multiple_of(meta[1 + k], 64), rz)


def cut(start, width, at):
    if start < at < start + width:
        return [(start, at - start), (at, start + width - at)]
    return [(start, width)]


def load_weights(meta, pieces, base, places, sems):
    own, near0, far0, a0, b0, rest, near, far, a, b = pieces
    rz, split0, count = own.shape[0], a0.shape[1], rest.shape[0]
    split = rest.shape[2] // 2
    home = meta[0] == 1
    lists = [[] for _ in places]
    at = 0
    for j in range(2):
        for k in range(count + 1):
            rows = zrows(meta, k, rz)
            for n, (start, width, place) in enumerate(places):
                for c, w in cut(start, width, split if k else split0 - base):
                    g = base + c
                    if k == 0:
                        mine = (near0 if j else own).at[:, pl.ds(g, w)]
                        if j == 0:
                            other = far0.at[:, pl.ds(g, w)]
                        else:
                            other = a0.at[:, pl.ds(g, w)] if g < split0 else b0.at[:, pl.ds(g - split0, w)]
                    else:
                        mine = (near if j else rest).at[k - 1, :, pl.ds(c, w)]
                        if j == 0:
                            other = far.at[k - 1, :, pl.ds(c, w)]
                        else:
                            other = (
                                a.at[k - 1, :, pl.ds(c, w)] if c < split else b.at[k - 1, :, pl.ds(c - split, w)]
                            )
                    dst = place(j, rows, c - start, w)
                    first = pltpu.make_async_copy(mine, dst, sems.at[at])
                    second = pltpu.make_async_copy(other, dst, sems.at[at])
                    at += 1

                    @pl.when(home)
                    def _():
                        first.start()

                    @pl.when(jnp.logical_not(home))
                    def _():
                        second.start()

                    lists[n].append(first)
    return lists


def copies_of(rest):
    return 2 * (3 + 2 * rest.shape[0])


def wait_all(waits):
    for made in waits:
        made.wait()


def load_a(meta, pieces, w_a, sems):
    width = w_a.shape[2]
    return load_weights(
        meta, pieces, 0, [(0, width, lambda j, rows, c, w: w_a.at[j, rows, pl.ds(c, w)])], sems
    )[0]


def load_b(meta, pieces, w_i, w_f, sems):
    one = w_i.shape[1] // 2
    base = pieces[0].shape[1] - 2 * one
    return load_weights(
        meta,
        pieces,
        base,
        [
            (0, one, lambda j, rows, c, w: w_i.at[rows, pl.ds(j * one + c, w)]),
            (one, one, lambda j, rows, c, w: w_f.at[rows, pl.ds(j * one + c, w)]),
        ],
        sems,
    )


def attn_forward(level, meta, x_or_mid, parts, norms, pieces, bias, seg_col, seg_row):
    four = pieces[5].shape[2]
    length, width = x_or_mid.shape
    cols = four // 4
    three = 3 * cols
    heads = 2 * cols // HD

    def body(meta, *refs):
        refs = list(refs)
        src = refs.pop(0)
        if level:
            own, other, gain, shift = (refs.pop(0) for _ in range(4))
        pieces = [refs.pop(0) for _ in range(10)]
        bias, sc, sr = (refs.pop(0) for _ in range(3))
        part_out, qkv_out, probs_out, ctx_out = (refs.pop(0) for _ in range(4))
        if level:
            x_out, xhat_out, scale_out = (refs.pop(0) for _ in range(3))
        w_a, sems = refs
        waits = load_a(meta, pieces, w_a, sems)
        if level:
            for rows in chunks(length):
                z = src[rows, :] + (own[rows, :].astype(F32) + other[rows, :].astype(F32)) + shift[2:3, :]
                xhat, scale = norm_rows(z)
                x_out[rows, :] = (xhat * gain[1:2, :] + shift[3:4, :]).astype(BF16)
                xhat_out[rows, :] = xhat.astype(BF16)
                scale_out[rows, :] = scale
            x_ref = x_out
        else:
            x_ref = src
        wait_all(waits)
        for j in range(2):
            c = slice(j * three, (j + 1) * three)
            for rows in chunks(length, 256):
                qkv_out[rows, c] = (nn(x_ref[rows, :], w_a[j, :, :three]) + bias[:, c]).astype(BF16)
        v_t = jnp.concatenate(
            [qkv_out[:, j * three + 2 * cols : (j + 1) * three].astype(F32) for j in range(2)], 1
        ).T.astype(BF16)
        for queries in chunks(length, 256):
            same = sc[...] == sr[:, queries]
            outs = []
            for h in range(heads):
                j, i = divmod(h, cols // HD)
                at = j * three + i * HD
                q = qkv_out[queries, at : at + HD]
                k = qkv_out[:, at + cols : at + cols + HD]
                st = jnp.where(same, nt(k, q) * 0.125, -1e30)
                p = jnp.exp(st - jnp.max(st, 0, keepdims=True))
                p = (p * (1.0 / jnp.sum(p, 0, keepdims=True))).astype(BF16)
                probs_out[h, :, queries] = p
                outs.append(nn(v_t[h * HD : (h + 1) * HD], p))
            ctx = jnp.concatenate(outs, 0).T.astype(BF16)
            ctx_out[queries, :] = ctx
            part_out[queries, :] = (
                nt(ctx[:, :cols], w_a[0, :, three:]) + nt(ctx[:, cols:], w_a[1, :, three:])
            ).astype(BF16)

    outs = [
        sds((length, width), BF16), sds((length, 2 * three), BF16),
        sds((heads, length, length), BF16), sds((length, 2 * cols), BF16),
    ]
    args = [meta, x_or_mid]
    if level:
        args += [*parts, *norms]
        outs += [sds((length, width), BF16), sds((length, width), BF16), sds((length, 1), F32)]
    specs = [SM] + [VM] * (len(args) - 1) + [ANY] * 10 + [VM] * 3
    args += [*pieces, bias, seg_col, seg_row]
    return pl.pallas_call(
        body,
        out_shape=outs,
        in_specs=specs,
        out_specs=[VM] * len(outs),
        scratch_shapes=[pltpu.VMEM((2, width, four), BF16), pltpu.SemaphoreType.DMA((copies_of(pieces[5]),))],
        compiler_params=params(),
        cost_estimate=takes(13),
        name="attn_forward",
    )(*args)


def ffn_forward(meta, x, parts, gains, shifts, pieces, bias_in):
    units = pieces[5].shape[2]
    length, width = x.shape

    def body(meta, x, own, other, gain, shift, p0, p1, p2, p3, p4, p5, p6, p7, p8, p9, bias,
             part_out, mid_out, xhat_out, scale_out, act_out, slope_out, w_i, w_f, low, sems):
        first, second = load_b(meta, (p0, p1, p2, p3, p4, p5, p6, p7, p8, p9), w_i, w_f, sems)
        for rows in chunks(length):
            z = x[rows, :].astype(F32) + (own[rows, :].astype(F32) + other[rows, :].astype(F32)) + shift[0:1, :]
            xhat, scale = norm_rows(z)
            mid = xhat * gain[0:1, :] + shift[1:2, :]
            mid_out[rows, :] = mid
            low[rows, :] = mid.astype(BF16)
            xhat_out[rows, :] = xhat.astype(BF16)
            scale_out[rows, :] = scale
        wait_all(first)
        for rows in chunks(length, 256):
            for c in chunks(units, 512):
                pre = nn(low[rows, :], w_i[:, c]) + bias[:, c]
                act, slope = gelu_parts(pre)
                act_out[rows, c] = act.astype(BF16)
                slope_out[rows, c] = slope.astype(BF16)
        wait_all(second)
        for rows in chunks(length, 256):
            part_out[rows, :] = nt(act_out[rows, :], w_f[...]).astype(BF16)

    return pl.pallas_call(
        body,
        out_shape=[
            sds((length, width), BF16), sds((length, width), F32), sds((length, width), BF16),
            sds((length, 1), F32), sds((length, units), BF16), sds((length, units), BF16),
        ],
        in_specs=[SM] + [VM] * 5 + [ANY] * 10 + [VM],
        out_specs=[VM] * 6,
        scratch_shapes=[
            pltpu.VMEM((width, units), BF16), pltpu.VMEM((width, units), BF16),
            pltpu.VMEM((length, width), BF16), pltpu.SemaphoreType.DMA((copies_of(pieces[5]),)),
        ],
        compiler_params=params(),
        cost_estimate=takes(9),
        name="ffn_forward",
    )(meta, x, *parts, gains, shifts, *pieces, bias_in)


def last_norm(mid, parts, gains, shifts, tok_row, cls_pos):
    length, width = mid.shape
    n_cls = cls_pos.shape[0]

    def body(cls, mid, own, other, gain, shift, tok, y_out, xhat_out, scale_out, cls_out):
        for rows in chunks(length):
            z = mid[rows, :] + (own[rows, :].astype(F32) + other[rows, :].astype(F32)) + shift[2:3, :]
            xhat, scale = norm_rows(z)
            y_out[rows, :] = (xhat * gain[1:2, :] + shift[3:4, :]).astype(BF16)
            xhat_out[rows, :] = xhat.astype(BF16)
            scale_out[rows, :] = scale
        which = lax.broadcasted_iota(jnp.int32, (16, length), 0)
        hot = jnp.zeros((16, length), F32)
        for p in range(n_cls):
            hot = jnp.where(jnp.logical_and(which == p, tok[...] == cls[p]), 1.0, hot)
        cls_out[...] = nn(hot.astype(BF16), y_out[...])[:n_cls].astype(BF16)

    return pl.pallas_call(
        body,
        out_shape=[
            sds((length, width), BF16), sds((length, width), BF16), sds((length, 1), F32),
            sds((n_cls, width), BF16),
        ],
        in_specs=[SM] + [VM] * 6,
        out_specs=[VM] * 4,
        compiler_params=params(),
        cost_estimate=takes(2),
        name="last_norm",
    )(cls_pos, mid, *parts, gains, shifts, tok_row)


def ffn_backward(level, meta, sources, xhat, scale, gains, slope, pieces):
    units = pieces[5].shape[2]
    length, width = xhat.shape
    n_cls = sources[3].shape[0] if level else 0

    def body(meta, *refs):
        refs = list(refs)
        if level:
            cls, grad, d_cls, tok = (refs.pop(0) for _ in range(4))
        else:
            d_above, own, other = (refs.pop(0) for _ in range(3))
        xhat, scale, gain, slope = (refs.pop(0) for _ in range(4))
        pieces = [refs.pop(0) for _ in range(10)]
        part_out, second_out, low_out, pre_out, vec_out, inb_out, w_i, w_f, sems = refs
        first, second = load_b(meta, pieces, w_i, w_f, sems)
        sums = [jnp.zeros((1, width), F32) for _ in range(3)]
        for rows in chunks(length):
            if level:
                d_out = grad[rows, :].astype(F32)
                for p in range(n_cls):
                    d_out = d_out + jnp.where(tok[rows, :] == cls[p], 1.0, 0.0) * d_cls[p : p + 1, :]
            else:
                d_out = d_above[rows, :] + (own[rows, :].astype(F32) + other[rows, :].astype(F32))
                d_out = d_out.astype(BF16).astype(F32)
            hat = xhat[rows, :].astype(F32)
            d_second = norm_back_rows(d_out, gain[1:2, :], hat, scale[rows, :])
            second_out[rows, :] = d_second
            low_out[rows, :] = d_second.astype(BF16)
            for n, item in enumerate((d_out * hat, d_out, d_second)):
                sums[n] = sums[n] + jnp.sum(item, 0, keepdims=True)
        for n in range(3):
            vec_out[n : n + 1, :] = sums[n]
        wait_all(second)
        for n, rows in enumerate(chunks(length, 256)):
            for c in chunks(units, units // 4):
                d_act = nn(low_out[rows, :], w_f[:, c])
                d_pre = (slope[rows, c].astype(F32) * d_act).astype(BF16)
                pre_out[rows, c] = d_pre
                j, at = divmod(c.start, units // 2)
                at = slice(at, at + c.stop - c.start)
                total = jnp.sum(d_pre.astype(F32), 0, keepdims=True)
                inb_out[j : j + 1, at] = total if n == 0 else inb_out[j : j + 1, at] + total
        wait_all(first)
        for rows in chunks(length, 256):
            part_out[rows, :] = nt(pre_out[rows, :], w_i[...]).astype(BF16)

    if level:
        token_grad, d_cls, tok_col, cls_pos = sources
        args, specs = [meta, cls_pos, token_grad, d_cls, tok_col], [SM, SM, VM, VM, VM]
    else:
        args, specs = [meta, *sources], [SM, VM, VM, VM]
    args += [xhat, scale, gains, slope, *pieces]
    specs += [VM] * 4 + [ANY] * 10
    return pl.pallas_call(
        body,
        out_shape=[
            sds((length, width), BF16), sds((length, width), F32), sds((length, width), BF16),
            sds((length, units), BF16), sds((3, width), F32), sds((2, units // 2), F32),
        ],
        in_specs=specs,
        out_specs=[VM] * 6,
        scratch_shapes=[
            pltpu.VMEM((width, units), BF16), pltpu.VMEM((width, units), BF16),
            pltpu.SemaphoreType.DMA((copies_of(pieces[5]),)),
        ],
        compiler_params=params(),
        cost_estimate=takes(9),
        name="ffn_backward",
    )(*args)


def grads_of(nz, rz, width):
    half = width // 2
    return [
        sds((2, rz, width), BF16), sds((2, nz - 1, rz, half), BF16),
        sds((nz - 1, rz, half), BF16), sds((nz - 1, rz, half), BF16),
    ]


def put_grad(outs, j, k, column, value):
    own, pair, next_b, own_b = outs
    value = value.astype(BF16)
    half, width = own_b.shape[2], value.shape[1]
    if k == 0:
        own[j, :, column : column + width] = value
    elif column < half:
        pair[1 - j, k - 1, :, column : column + width] = value
    else:
        (next_b if j else own_b)[k - 1, :, column - half : column - half + width] = value


def ffn_grads(meta, mid, d_pre, d_ffn, act, nz):
    length, width = mid.shape
    units = d_pre.shape[1]
    one = units // 2
    rz = width // nz

    def body(meta, mid, d_pre, d_ffn, act, *refs):
        outs, (mid_t, ffn_t) = refs[:4], refs[4:]
        mid_t[...] = mid[...].T.astype(BF16)
        ffn_t[...] = d_ffn[...].astype(F32).T.astype(BF16)
        for j in range(2):
            c = slice(j * one, (j + 1) * one)
            for k in range(nz):
                rows = zrows(meta, k, rz)
                put_grad(outs, j, k, 0, nn(mid_t[rows, :], d_pre[:, c]))
                put_grad(outs, j, k, one, nn(ffn_t[rows, :], act[:, c]))

    return pl.pallas_call(
        body,
        out_shape=grads_of(nz, rz, units),
        in_specs=[SM] + [VM] * 4,
        out_specs=[VM] * 4,
        scratch_shapes=[pltpu.VMEM((width, length), BF16)] * 2,
        compiler_params=params(),
        cost_estimate=takes(7),
        name="ffn_grads",
    )(meta, mid, d_pre, d_ffn, act)


def attn_backward(meta, d_second, parts, xhat, scale, gains, qkv, probs, pieces):
    four = pieces[5].shape[2]
    length, width = d_second.shape
    cols = four // 4
    three = 3 * cols
    heads = 2 * cols // HD

    def body(meta, d_second, own, other, xhat, scale, gain, qkv, probs, p0, p1, p2, p3, p4, p5, p6, p7, p8, p9,
             part_out, first_out, low_out, dqkv_out, vec_out, sum_out,
             w_a, d_ctx, acc_v, acc_k, sems):
        waits = load_a(meta, (p0, p1, p2, p3, p4, p5, p6, p7, p8, p9), w_a, sems)
        sums = [jnp.zeros((1, width), F32) for _ in range(3)]
        for rows in chunks(length):
            d_mid = d_second[rows, :] + (own[rows, :].astype(F32) + other[rows, :].astype(F32))
            hat = xhat[rows, :].astype(F32)
            d_first = norm_back_rows(d_mid, gain[0:1, :], hat, scale[rows, :])
            first_out[rows, :] = d_first
            low_out[rows, :] = d_first.astype(BF16)
            for n, item in enumerate((d_mid * hat, d_mid, d_first)):
                sums[n] = sums[n] + jnp.sum(item, 0, keepdims=True)
        for n in range(3):
            vec_out[n : n + 1, :] = sums[n]
        wait_all(waits)
        for j in range(2):
            for rows in chunks(length, 256):
                d_ctx[rows, j * cols : (j + 1) * cols] = nn(low_out[rows, :], w_a[j, :, three:]).astype(BF16)
        k_t = jnp.concatenate(
            [qkv[:, j * three + cols : j * three + 2 * cols].astype(F32) for j in range(2)], 1
        ).T.astype(BF16)
        for h in range(heads):
            j, i = divmod(h, cols // HD)
            at = j * three + i * HD
            q_cols, k_cols, v_cols = (slice(at + n * cols, at + n * cols + HD) for n in range(3))
            for n, queries in enumerate(chunks(length, 256)):
                d_o = d_ctx[queries, h * HD : (h + 1) * HD]
                d_p = nt(qkv[:, v_cols], d_o)
                p = probs[h, :, queries]
                wide = p.astype(F32)
                d_s = (wide * (d_p - jnp.sum(wide * d_p, 0, keepdims=True))).astype(BF16)
                d_v = nn(p, d_o)
                d_k = nn(d_s, qkv[queries, q_cols])
                acc_v[...] = d_v if n == 0 else acc_v[...] + d_v
                acc_k[...] = d_k if n == 0 else acc_k[...] + d_k
                d_q = nn(k_t[h * HD : (h + 1) * HD], d_s)
                dqkv_out[queries, q_cols] = (d_q.T * 0.125).astype(BF16)
            dqkv_out[:, v_cols] = acc_v[...].astype(BF16)
            dqkv_out[:, k_cols] = (acc_k[...] * 0.125).astype(BF16)
        for j in range(2):
            sum_out[j : j + 1, :] = jnp.sum(
                dqkv_out[:, j * three : (j + 1) * three].astype(F32), 0, keepdims=True
            )
        for rows in chunks(length, 256):
            part_out[rows, :] = (
                nt(dqkv_out[rows, :three], w_a[0, :, :three]) + nt(dqkv_out[rows, three:], w_a[1, :, :three])
            ).astype(BF16)

    return pl.pallas_call(
        body,
        out_shape=[
            sds((length, width), BF16), sds((length, width), F32), sds((length, width), BF16),
            sds((length, 2 * three), BF16), sds((3, width), F32), sds((2, three), F32),
        ],
        in_specs=[SM] + [VM] * 8 + [ANY] * 10,
        out_specs=[VM] * 6,
        scratch_shapes=[
            pltpu.VMEM((2, width, four), BF16), pltpu.VMEM((length, 2 * cols), BF16),
            pltpu.VMEM((length, HD), F32), pltpu.VMEM((length, HD), F32),
            pltpu.SemaphoreType.DMA((copies_of(pieces[5]),)),
        ],
        compiler_params=params(),
        cost_estimate=takes(15),
        name="attn_backward",
    )(meta, d_second, *parts, xhat, scale, gains, qkv, probs, *pieces)


def attn_grads(meta, x, d_attn, d_qkv, ctx, nz):
    length, width = x.shape
    three = d_qkv.shape[1] // 2
    cols = ctx.shape[1] // 2
    rz = width // nz

    def body(meta, x, d_attn, d_qkv, ctx, *refs):
        outs, (x_t, a_t) = refs[:4], refs[4:]
        x_t[...] = x[...].astype(F32).T.astype(BF16)
        a_t[...] = d_attn[...].astype(F32).T.astype(BF16)
        for j in range(2):
            for k in range(nz):
                rows = zrows(meta, k, rz)
                grad = nn(x_t[rows, :], d_qkv[:, j * three : (j + 1) * three])
                put_grad(outs, j, k, 0, grad[:, : 2 * cols])
                put_grad(outs, j, k, 2 * cols, grad[:, 2 * cols :])
                put_grad(outs, j, k, three, nn(a_t[rows, :], ctx[:, j * cols : (j + 1) * cols]))

    return pl.pallas_call(
        body,
        out_shape=grads_of(nz, rz, three + cols),
        in_specs=[SM] + [VM] * 4,
        out_specs=[VM] * 4,
        scratch_shapes=[pltpu.VMEM((width, length), BF16)] * 2,
        compiler_params=params(),
        cost_estimate=takes(4),
        name="attn_grads",
    )(meta, x, d_attn, d_qkv, ctx)


def loss_kernel(own, perm, slots, queries, positive_col, n_own):
    n_q, width = queries.shape
    n_p = slots.shape[0]

    def body(own, perm, slots, queries, pos, loss_out, d_out):
        passages = nn(perm[...], slots[...]).astype(BF16)
        logits = nt(queries[...], passages)
        top = jnp.max(logits, -1, keepdims=True)
        log_total = top + jnp.log(jnp.sum(jnp.exp(logits - top), -1, keepdims=True))
        index = lax.broadcasted_iota(jnp.int32, (n_q, n_p), 1)
        hits = pos[...] == index
        chosen = jnp.sum(jnp.where(hits, logits, 0.0), -1, keepdims=True)
        loss_out[...] = jnp.sum(log_total - chosen, 0, keepdims=True) / n_q
        d_logits = (16.0 * (jnp.exp(logits - log_total) - jnp.where(hits, 1.0, 0.0))).astype(BF16)
        pick = jnp.where(
            lax.broadcasted_iota(jnp.int32, (n_p, 128), 0)
            == lax.broadcasted_iota(jnp.int32, (n_p, 128), 1) + own[0],
            1.0, 0.0,
        ).astype(BF16)
        cols = nn(d_logits, pick)
        d_out[...] = nn(cols.T.astype(BF16), queries[...])[:n_own]

    return pl.pallas_call(
        body,
        out_shape=[sds((1, 1), F32), sds((n_own, width), F32)],
        in_specs=[SM] + [VM] * 4,
        out_specs=[VM] * 2,
        compiler_params=params(),
        cost_estimate=takes(1),
        name="contrast",
    )(own, perm, slots, queries, positive_col)


def on_device(
    inputs, cls_pos, w_qkv, qv_bias, w_out, w_in, in_bias, w_ffn_out,
    layer_gains, shifts, queries, positive, token_grad,
):
    core = lax.axis_index("section")
    dp = lax.axis_index("dp")
    me = lax.axis_index("tensor")
    n_dp = lax.axis_size("dp")
    n_t = lax.axis_size("tensor")
    first_core = core == 0
    rows_dev, share, width = inputs.shape
    cols = w_qkv.shape[3]
    units = w_in.shape[2]
    length = n_t * share
    n_chips = n_dp * n_t
    piece = width // n_chips
    order = dp_order()
    direct = direct_dp()
    nz = 4 if direct else 2
    t_ids = jnp.arange(n_t, dtype=jnp.int32)

    vec = jnp.concatenate(
        [layer_gains.reshape(-1), shifts.reshape(-1), qv_bias.reshape(-1), in_bias.reshape(-1)]
    )
    n_gain, n_shift, n_qv, n_inb = layer_gains.size, shifts.size, qv_bias.size, in_bias.size
    n_vec = vec.shape[0]
    flat = jnp.concatenate(
        [vec, queries.reshape(-1), (positive // 16).astype(BF16), (positive % 16).astype(BF16)]
    )
    flat = jnp.pad(flat, (0, -flat.shape[0] % 2048)).reshape(-1, 128)

    def spread_rows(block):
        blocks = [lax.dynamic_index_in_dim(block, me ^ k, 0, keepdims=False) for k in range(n_t)]
        return jnp.concatenate(exchange_rows(blocks), 0)

    pack = jnp.concatenate(
        [w_qkv[0, :, 0], w_qkv[0, :, 1], w_qkv[0, :, 2], w_out[0].T, w_in[0], w_ffn_out[0].T], 1
    )
    if direct:
        own = pack
        one = hop(pack, "dp", 1)
        one_a, one_b = one[:, :width], one[:, width:]
        own_a, own_b = pack[:, :width], pack[:, width:]
    else:
        pack = lax.all_gather(pack, "dp", axis=0, tiled=True)
        own, other_rows = pack[: width // 2], pack[width // 2 :][None]
    near0, far0 = gather_own(own)
    both0 = gather_own_both(near0, far0)
    owns = [own, near0, far0, *both0]

    def rest_of(a_part, core, *earlier):
        if not direct:
            return other_rows[:, :, :width] if a_part else other_rows[:, :, width:]
        return rest_dp(own_a if a_part else own_b, one_a if a_part else one_b, core, *earlier)

    def stacked(rest, *earlier):
        return stack_rest(rest, *earlier) if direct else after(rest, *earlier)

    x_low = spread_rows(inputs)
    message = double(flat, "dp") if direct else spread_dp(flat)
    z_a0 = rest_of(True, 0)
    rest_a0 = stacked(z_a0, both0, x_low)
    z_b0 = rest_of(False, 0, rest_a0)
    near_a0 = gather_near(rest_a0, 0)
    message = double(after(message, rest_a0), "tensor")
    both_a0 = gather_both(*near_a0, 0)
    pieces_a0 = [*owns, rest_a0, *near_a0, *both_a0]

    zrow = order * (width // n_dp) if direct else jnp.arange(2, dtype=jnp.int32) * (width // 2)
    metas = [
        jnp.concatenate([(core == level)[None].astype(jnp.int32), zrow.astype(jnp.int32)])
        for level in range(2)
    ]
    slots = [me ^ (2 * (core != level) + jnp.arange(2, dtype=jnp.int32)) for level in range(2)]
    hots = [(s[:, None] == t_ids[None, :]).astype(F32) for s in slots]

    positions = jnp.concatenate(
        [(me ^ k) * share + jnp.arange(share, dtype=jnp.int32) for k in range(n_t)]
    )
    cls_row = lax.dynamic_index_in_dim(cls_pos, me, 0, keepdims=False)
    segments = jnp.sum((positions[:, None] >= cls_row[None, :]).astype(jnp.int32), -1)
    seg_col, seg_row = segments[:, None], segments[None, :]
    tok_col, tok_row = positions[:, None], positions[None, :]

    slot_ids = (order[None, :] * n_t + (me ^ t_ids)[:, None]).reshape(-1)
    to_natural = (jnp.arange(n_chips, dtype=jnp.int32)[:, None] == slot_ids[None, :]).astype(BF16)
    table = nn(to_natural, message.reshape(n_chips, -1))
    own_table = table[:, :n_vec].astype(BF16)
    other_table = swap_cores(own_table)
    tables = jnp.where(
        first_core, jnp.stack([own_table, other_table]), jnp.stack([other_table, own_table])
    ).astype(F32)
    at = 0
    gains = tables[:, :, at : at + n_gain].reshape(2, n_chips, 2, piece).transpose(0, 2, 1, 3).reshape(2, 2, width)
    at += n_gain
    shift = tables[:, :, at : at + n_shift].reshape(2, n_chips, 4, piece).transpose(0, 2, 1, 3).reshape(2, 4, width)
    at += n_shift
    qv = tables[:, :, at : at + n_qv].reshape(2, n_dp, n_t, 2, cols // n_dp)
    qv = qv.transpose(0, 3, 2, 1, 4).reshape(2, 2, n_t, cols)
    at += n_qv
    inb = tables[:, :, at : at + n_inb].reshape(2, n_dp, n_t, n_inb).transpose(0, 2, 1, 3).reshape(2, n_t, units)
    vectors = []
    for level in range(2):
        bias = jnp.sum(hots[level][None, :, :, None] * qv[level][:, None], 2)
        bias = jnp.stack([bias[0], jnp.zeros_like(bias[0]), bias[1]], 1).reshape(1, -1)
        bias_in = jnp.sum(hots[level][:, :, None] * inb[level][None], 1).reshape(1, -1)
        vectors.append((gains[level], shift[level], bias, bias_in))
    at = n_vec
    q_dev = queries.shape[0]
    all_q = table[:, at : at + q_dev * width].reshape(-1, width).astype(BF16)
    at += q_dev * width
    all_pos = table[:, at : at + q_dev] * 16.0 + table[:, at + q_dev : at + 2 * q_dev]
    all_pos = all_pos.astype(jnp.int32).reshape(-1, 1)
    n_cls = cls_row.shape[0]
    perm = jnp.repeat(jnp.repeat(to_natural, n_cls, 0), n_cls, 1)
    perm = perm * jnp.tile(jnp.eye(n_cls, dtype=BF16), (n_chips, n_chips))

    vectors, all_q, all_pos, perm, x_low = lax.optimization_barrier(
        (vectors, all_q, all_pos, perm, x_low)
    )
    saved = []
    rest_b0 = stacked(z_b0, both_a0)
    near_b0 = gather_near(rest_b0, 0)
    z_a1 = rest_of(True, 1, rest_b0)
    source, parts, norms = after(x_low, rest_b0), None, None
    pieces_a, pieces_b = [pieces_a0, None], [None, None]
    for level in range(2):
        gain, shift, bias, bias_in = vectors[level]
        outs = attn_forward(
            level, metas[level], source, parts, norms, pieces_a[level], bias, seg_col, seg_row
        )
        part, qkv, probs, ctx = outs[:4]
        if level == 0:
            rest_a1 = stacked(z_a1, part)
            z_b1 = rest_of(False, 1, rest_a1)
            both_b0 = gather_both(*after(near_b0, rest_a1), 0)
            near_a1 = gather_near(after(rest_a1, near_b0), 1)
            pieces_b[0] = [*owns, rest_b0, *near_b0, *both_b0]
        else:
            near_b1, part = lax.optimization_barrier((near_b1, part))
            both_b1 = gather_both(*near_b1, 1)
            pieces_b[1] = [*owns, rest_b1, *near_b1, *both_b1]
        if level:
            x, xhat2, scale2 = outs[4:]
            saved[0]["second"] = (xhat2, scale2)
        else:
            x = x_low
        part, mid, xhat1, scale1, act, slope = ffn_forward(
            metas[level], x, (part, swap_cores(part)), gain, shift, pieces_b[level], bias_in
        )
        saved.append(
            dict(x=x, qkv=qkv, probs=probs, ctx=ctx, mid=mid, xhat1=xhat1, scale1=scale1, act=act, slope=slope)
        )
        source, parts, norms = mid, (part, swap_cores(part)), (gain, shift)
        if level == 0:
            rest_b1 = stacked(z_b1, part)
            near_a1, rest_b1 = lax.optimization_barrier((near_a1, rest_b1))
            both_a1 = gather_both(*near_a1, 1)
            near_b1 = gather_near(after(rest_b1, both_a1), 1)
            pieces_a[1] = [*owns, rest_a1, *near_a1, *both_a1]
            source = after(source, rest_b1)
    tokens = spread_rows(after(token_grad, part))
    y, xhat2, scale2, cls_own = last_norm(source, parts, *norms, tok_row, cls_row)
    saved[1]["second"] = (xhat2, scale2)

    cls_slots = spread_tensor(spread_dp(cls_own)).reshape(n_chips * n_cls, width)
    first_own = ((dp * n_t + me) * n_cls).astype(jnp.int32)[None]
    mean_loss, d_cls = loss_kernel(first_own, perm, cls_slots, all_q, all_pos, n_cls)

    vector_rows = [None, None]
    sources = (tokens, d_cls, tok_col, cls_row)
    sums_a, sums_b, own_grads = [None, None], [None, None], [None, None]
    for level in (1, 0):
        gain = vectors[level][0]
        kept = saved[level]
        meta = metas[level]
        xhat2, scale2 = kept["second"]
        if level == 0:
            sources = (after(sources[0], sums_b[1].first(grads_a[1])), *sources[1:])
        part, d_second, d_ffn, d_pre, vec2, sum_inb = ffn_backward(
            level, meta, sources, xhat2, scale2, gain, kept["slope"], pieces_b[level]
        )
        other = swap_cores(part)
        if level == 0:
            d_ffn = after(d_ffn, sums_a[1].first(part))
        grads_b = ffn_grads(meta, kept["mid"], d_pre, d_ffn, kept["act"], nz)
        own_b, *grads_b = grads_b
        sums_b[level] = Reduction(grads_b, level)
        d_second = after(d_second, grads_b[1])
        if level == 0:
            d_second = after(d_second, sums_b[1].second(grads_b[1]))
        part, d_first, d_attn, d_qkv, vec1, sum_qkv = attn_backward(
            meta, d_second, (part, other), kept["xhat1"], kept["scale1"], gain,
            kept["qkv"], kept["probs"], pieces_a[level],
        )
        other = swap_cores(part)
        if level == 0:
            d_attn = after(d_attn, sums_a[1].second(part))
        own_a, *grads_a = attn_grads(meta, kept["x"], d_attn, d_qkv, kept["ctx"], nz)
        own_grads[level] = jnp.concatenate([own_a, own_b], 2)
        sums_a[level] = Reduction(grads_a, level)
        vector_rows[level] = (vec1, vec2, sum_qkv, sum_inb)
        sources = (d_first, part, other)
    sums_b[0].first(grads_a[1])
    sums_b[1].third(sums_b[0].added)
    sums_a[0].first(sums_b[1].pieces)
    sums_a[1].third(sums_a[0].added)
    last_1 = last_dp([sums_a[1], sums_b[1]])
    own_sum = OwnReduction(own_grads, sums_a[0].added)
    sums_b[0].second(sums_a[1].pieces)
    sums_a[0].second(sums_b[0].sums)
    own_sum.first(sums_a[0].sums)
    sums_b[0].third(own_sum.added)
    d_hidden = d_first + (part.astype(F32) + other.astype(F32))
    outgoing = jnp.where(first_core, d_hidden, y.astype(F32))
    low = after(outgoing.astype(BF16), own_sum.added).reshape(n_t, share, width)
    incoming = [outgoing[:share]] + [b.astype(F32) for b in exchange_rows([low[k] for k in range(n_t)])[1:]]
    boundary = jnp.zeros((n_t, share, width), F32)
    for k in range(n_t):
        boundary = lax.dynamic_update_index_in_dim(boundary, incoming[k], me ^ k, 0)
    vector_rows, _ = lax.optimization_barrier((vector_rows, sums_b[0].pieces))
    wide = 3 * cols + units

    def vector_table(level):
        vec1, vec2, sum_qkv, sum_inb = vector_rows[level]
        by_t = lax.dot_general(
            hots[level], jnp.concatenate([sum_qkv, sum_inb], 1), (((0,), (0,)), ((), ())),
            precision=lax.Precision.HIGHEST,
        )
        whole = 0.5 * jnp.concatenate([vec1, vec2])
        return jnp.concatenate([jnp.pad(whole, ((0, 2), (0, wide - width))), by_t, jnp.zeros((4, wide), F32)])

    rows0, rows1 = vector_table(0), vector_table(1)
    flat = jnp.where(first_core, rows0, rows1) + swap_cores(jnp.where(first_core, rows1, rows0))
    flat = flat + hop(flat, "tensor", 1)
    flat = flat + hop(flat, "tensor", 2)
    if direct:
        flat = flat + hop(flat, "dp", 1)
        flat = flat + hop(flat, "dp", 2)
    else:
        flat = lax.psum(flat, "dp")
    sums_a[0].third(flat)
    last_0 = last_dp([sums_a[0], sums_b[0]])
    total = own_sum.second()
    if direct:
        here, got = (jnp.where(first_core, low, high).astype(F32) for low, high in zip(last_0, last_1))
        total = total + here + got
    else:
        whole = jnp.concatenate([total, jnp.where(first_core, last_0, last_1)]).astype(BF16)
        total = lax.psum_scatter(whole, "dp", scatter_dimension=0, tiled=True).astype(F32)
    tot_a, tot_b = total[:, :width], total[:, width:]
    own = lax.dynamic_slice_in_dim(flat[:6, :width], (dp * n_t + me) * piece, piece, 1)
    grad_gains = jnp.concatenate([own[0:1], own[3:4]]).reshape(layer_gains.shape)
    grad_shifts = jnp.concatenate([own[2:3], own[1:2], own[5:6], own[4:5]]).reshape(shifts.shape)
    by_t = lax.dynamic_slice_in_dim(flat, 8 + me, 1, 0)
    qv = jnp.concatenate([by_t[:, :cols], by_t[:, 2 * cols : 3 * cols]])
    grad_qv = lax.dynamic_slice_in_dim(qv, dp * qv_bias.shape[3], qv_bias.shape[3], 1).reshape(qv_bias.shape)
    grad_inb = lax.dynamic_slice_in_dim(by_t[:, 3 * cols :], dp * n_inb, n_inb, 1).reshape(in_bias.shape)

    grad_qkv = jnp.stack([tot_a[:, n * cols : (n + 1) * cols] for n in range(3)], 1)[None]
    grad_out = tot_a[:, 3 * cols :].T[None]
    grad_in = tot_b[:, :units][None]
    grad_ffn = tot_b[:, units:].T[None]
    return (
        grad_qkv, grad_qv, grad_out, grad_in, grad_inb, grad_ffn,
        grad_gains, grad_shifts, boundary[None], mean_loss.reshape(()),
    )


def solution(mesh):
    return jax.shard_map(
        on_device,
        mesh=mesh,
        in_specs=(
            P("dp", "tensor", None),
            P("dp", None),
            P("section", "dp", None, "tensor"),
            P("section", None, "tensor", "dp"),
            P("section", "tensor", "dp"),
            P("section", "dp", "tensor"),
            P("section", "tensor", "dp"),
            P("section", "tensor", "dp"),
            P("section", None, ("dp", "tensor")),
            P("section", None, ("dp", "tensor")),
            P(("dp", "tensor"), None),
            P(("dp", "tensor")),
            P("dp", "tensor", None),
        ),
        out_specs=(
            P("section", "dp", None, "tensor"),
            P("section", None, "tensor", "dp"),
            P("section", "tensor", "dp"),
            P("section", "dp", "tensor"),
            P("section", "tensor", "dp"),
            P("section", "tensor", "dp"),
            P("section", None, ("dp", "tensor")),
            P("section", None, ("dp", "tensor")),
            P("section", "dp", "tensor", None),
            P(),
        ),
        check_vma=False,
    )
```

```python
import jax
import jax.numpy as jnp
from jax import lax
from jax.experimental import pallas as pl
from jax.experimental.pallas import tpu as pltpu
from jax.sharding import PartitionSpec as P

HD = 64
PARTNER = 1
CROSS = 2
BF16 = jnp.bfloat16
F32 = jnp.float32


def mm(left, right, dims):
    return lax.dot_general(left, right, (dims, ((), ())), preferred_element_type=F32)


def nn(left, right):
    return mm(left, right, ((1,), (0,)))


def nt(left, right):
    return mm(left, right, ((1,), (1,)))


def after(block, *earlier):
    return lax.optimization_barrier((block, *earlier))[0]


def swap_cores(block):
    return lax.ppermute(block, "section", [(0, 1), (1, 0)])


def hop(block, axis, flip):
    return lax.ppermute(block, axis, [(i, i ^ flip) for i in range(lax.axis_size(axis))])


def core_hop(block, axis, flip, core):
    size = lax.axis_size(axis)
    route = [(core * size + i, core * size + (i ^ flip)) for i in range(size)]
    return lax.ppermute(block, ("section", axis), route)


def cross_hop(block, source):
    size = lax.axis_size("tensor")
    route = [(source * size + i, (1 - source) * size + (i ^ CROSS)) for i in range(size)]
    return lax.ppermute(block, ("section", "tensor"), route)


def direct_dp():
    return lax.axis_size("dp") == 4


def dp_order():
    size = lax.axis_size("dp")
    if direct_dp():
        return lax.axis_index("dp") ^ jnp.arange(size, dtype=jnp.int32)
    return jnp.arange(size, dtype=jnp.int32)


def spread_dp(block):
    if direct_dp():
        return jnp.stack([block] + [hop(block, "dp", k) for k in range(1, 4)])
    return lax.all_gather(block, "dp", axis=0, tiled=False)


def spread_tensor(block):
    return jnp.stack([block] + [hop(block, "tensor", k) for k in range(1, 4)])


def double(block, axis):
    pair = jnp.stack([block, hop(block, axis, 1)])
    return jnp.concatenate([pair, hop(pair, axis, 2)])


def exchange_rows(blocks):
    first = hop(jnp.stack([blocks[1], blocks[3]]), "tensor", 1)
    second = hop(jnp.stack([blocks[2], first[1]]), "tensor", 2)
    return [blocks[0], first[0], second[0], second[1]]


def cross_all(block):
    size = lax.axis_size("tensor")
    route = [(s * size + i, (1 - s) * size + (i ^ CROSS)) for s in range(2) for i in range(size)]
    return lax.ppermute(block, ("section", "tensor"), route)


def rest_dp(own, one, core, *earlier):
    pair = after(jnp.stack([own, one]), *earlier)
    return one, core_hop(pair, "dp", 2, core)


def rest_direct(own, core):
    return [core_hop(own, "dp", k, core)[None] for k in range(1, 4)]


def stack_rest(rest, *earlier):
    rest = after(list(rest), *earlier)
    if len(rest) == 2:
        rest = [rest[0][None], rest[1]]
    return jnp.concatenate(rest)


def gather_own(own):
    near, far = hop(own, "tensor", PARTNER), cross_all(own)
    return near, far


def gather_own_both(near, far):
    half = near.shape[1] // 2
    return cross_all(near[:, :half]), hop(far[:, half:], "tensor", PARTNER)


def gather_near(rest, core):
    return core_hop(rest, "tensor", PARTNER, core), cross_hop(rest, core)


def gather_both(near, far, core):
    half = near.shape[2] // 2
    return cross_hop(near[:, :, :half], core), core_hop(far[:, :, half:], "tensor", PARTNER, 1 - core)


def add_low(*items):
    total = items[0].astype(F32)
    for item in items[1:]:
        total = total + item.astype(F32)
    return total.astype(BF16)


class Reduction:
    def __init__(self, grads, core):
        self.core = core
        self.pair, self.next_b, self.own_b = grads
        self.got = cross_hop(self.pair, 1 - core)
        self.near_b = hop(self.next_b, "tensor", PARTNER)

    def first(self, *earlier):
        self.parts = pair, own_b, got, near_b = after((self.pair, self.own_b, self.got, self.near_b), *earlier)
        self.added = add_low(pair[0], got[0]), add_low(own_b, near_b)
        self.near_a = core_hop(self.added[0], "tensor", PARTNER, self.core)
        self.far_b = cross_hop(self.added[1], 1 - self.core)
        return self.added

    def second(self, *earlier):
        near_a, far_b, (pair, own_b, got, near_b) = after((self.near_a, self.far_b, self.parts), *earlier)

        def both(k):
            return jnp.concatenate(
                [add_low(pair[1][k], got[1][k], near_a[k]), add_low(own_b[k], near_b[k], far_b[k])], -1
            )

        if not direct_dp():
            self.sums = [both(slice(None))]
            return self.sums
        self.sums = both(slice(1, None)), both(0)
        self.across = core_hop(self.sums[0], "dp", 2, self.core)
        return self.sums

    def third(self, *earlier):
        if not direct_dp():
            self.pieces = self.sums
            return self.pieces
        one, across = after((self.sums[1], self.across), *earlier)
        self.pieces = [across[0], add_low(one, across[1])]
        return self.pieces


def last_dp(reductions, *earlier):
    if not direct_dp():
        return jnp.concatenate([r.pieces[0][0].astype(F32) for r in reductions], 1)
    high = max(r.pieces[0].shape[0] for r in reductions)

    def side_by_side(n):
        return jnp.concatenate(
            [jnp.pad(r.pieces[n], ((0, high - r.pieces[n].shape[0]), (0, 0))) for r in reductions], 1
        )

    return side_by_side(0), core_hop(after(side_by_side(1), *earlier), "dp", 1, reductions[0].core)


class OwnReduction:
    def __init__(self, slots, *earlier):
        first_core = lax.axis_index("section") == 0
        low, high = after(slots, *earlier)
        self.here, self.away = jnp.where(first_core, low, high), jnp.where(first_core, high, low)
        self.half = half = low.shape[2] // 2
        self.got = cross_all(jnp.stack([self.away[1][:, :half], self.away[0][:, :half]]))
        self.near_b = hop(jnp.stack([self.here[1][:, half:], self.away[1][:, half:]]), "tensor", PARTNER)

    def first(self, *earlier):
        here, away, got, near_b = after((self.here, self.away, self.got, self.near_b), *earlier)
        half = self.half
        self.parts = here, got, near_b
        self.added = add_low(here[1][:, :half], got[0]), add_low(away[0][:, half:], near_b[1])
        self.near_a = hop(self.added[0], "tensor", PARTNER)
        self.far_b = cross_all(self.added[1])
        return self.added

    def second(self, *earlier):
        near_a, far_b, (here, got, near_b) = after((self.near_a, self.far_b, self.parts), *earlier)
        here, got, near_b, near_a, far_b = (v.astype(F32) for v in (here, got, near_b, near_a, far_b))
        half = self.half
        return jnp.concatenate(
            [here[0][:, :half] + got[1] + near_a, here[0][:, half:] + near_b[0] + far_b], 1
        )


VMEM_LIMIT = 48 * 1024 * 1024
CHUNK = 128


def takes(micros):
    return pl.CostEstimate(flops=int(micros * 1.1e9), bytes_accessed=0, transcendentals=0)


def params():
    return pltpu.CompilerParams(vmem_limit_bytes=VMEM_LIMIT)


ANY = pl.BlockSpec(memory_space=pl.ANY)
VM = pl.BlockSpec(memory_space=pltpu.VMEM)
SM = pl.BlockSpec(memory_space=pltpu.SMEM)


def sds(shape, dtype):
    return jax.ShapeDtypeStruct(shape, dtype)


def chunks(length, step=CHUNK):
    return [slice(i, i + step) for i in range(0, length, step)]


def norm_rows(z):
    centre = z - jnp.mean(z, -1, keepdims=True)
    spread = jnp.mean(centre * centre, -1, keepdims=True)
    scale = lax.rsqrt(spread + 1e-05)
    return centre * scale, scale


def norm_back_rows(d_out, gain, xhat, scale):
    g = d_out * gain
    m1 = jnp.mean(g, -1, keepdims=True)
    m2 = jnp.mean(g * xhat, -1, keepdims=True)
    return scale * (g - m1 - xhat * m2)


def gelu_parts(x):
    e = jnp.exp(-0.5 * x * x)
    t = 1.0 / (1.0 + 0.2316418882 * jnp.abs(x))
    poly = t * (
        0.127414796 + t * (-0.142248368 + t * (0.7107068705 + t * (-0.7265760135 + t * 0.5307027145)))
    )
    tail = poly * e
    cdf = jnp.where(x < 0.0, tail, 1.0 - tail)
    return x * cdf, cdf + x * e * 0.3989422804014327


def zrows(meta, k, rz):
    return pl.ds(pl.multiple_of(meta[1 + k], 64), rz)


def cut(start, width, at):
    if start < at < start + width:
        return [(start, at - start), (at, start + width - at)]
    return [(start, width)]


def load_weights(meta, pieces, base, places, sems):
    own, near0, far0, a0, b0, rest, near, far, a, b = pieces
    rz, split0, count = own.shape[0], a0.shape[1], rest.shape[0]
    split = rest.shape[2] // 2
    home = meta[0] == 1
    lists = [[] for _ in places]
    at = 0
    for j in range(2):
        for k in range(count + 1):
            rows = zrows(meta, k, rz)
            for n, (start, width, place) in enumerate(places):
                for c, w in cut(start, width, split if k else split0 - base):
                    g = base + c
                    if k == 0:
                        mine = (near0 if j else own).at[:, pl.ds(g, w)]
                        if j == 0:
                            other = far0.at[:, pl.ds(g, w)]
                        else:
                            other = a0.at[:, pl.ds(g, w)] if g < split0 else b0.at[:, pl.ds(g - split0, w)]
                    else:
                        mine = (near if j else rest).at[k - 1, :, pl.ds(c, w)]
                        if j == 0:
                            other = far.at[k - 1, :, pl.ds(c, w)]
                        else:
                            other = (
                                a.at[k - 1, :, pl.ds(c, w)] if c < split else b.at[k - 1, :, pl.ds(c - split, w)]
                            )
                    dst = place(j, rows, c - start, w)
                    first = pltpu.make_async_copy(mine, dst, sems.at[at])
                    second = pltpu.make_async_copy(other, dst, sems.at[at])
                    at += 1

                    @pl.when(home)
                    def _():
                        first.start()

                    @pl.when(jnp.logical_not(home))
                    def _():
                        second.start()

                    lists[n].append(first)
    return lists


def copies_of(rest):
    return 2 * (3 + 2 * rest.shape[0])


def wait_all(waits):
    for made in waits:
        made.wait()


def load_a(meta, pieces, w_a, sems):
    width = w_a.shape[2]
    return load_weights(
        meta, pieces, 0, [(0, width, lambda j, rows, c, w: w_a.at[j, rows, pl.ds(c, w)])], sems
    )[0]


def load_b(meta, pieces, w_i, w_f, sems):
    one = w_i.shape[1] // 2
    base = pieces[0].shape[1] - 2 * one
    return load_weights(
        meta,
        pieces,
        base,
        [
            (0, one, lambda j, rows, c, w: w_i.at[rows, pl.ds(j * one + c, w)]),
            (one, one, lambda j, rows, c, w: w_f.at[rows, pl.ds(j * one + c, w)]),
        ],
        sems,
    )


def attn_forward(level, meta, x_or_mid, parts, norms, pieces, bias, seg_col, seg_row):
    four = pieces[5].shape[2]
    length, width = x_or_mid.shape
    cols = four // 4
    three = 3 * cols
    heads = 2 * cols // HD

    def body(meta, *refs):
        refs = list(refs)
        src = refs.pop(0)
        if level:
            own, other, gain, shift = (refs.pop(0) for _ in range(4))
        pieces = [refs.pop(0) for _ in range(10)]
        bias, sc, sr = (refs.pop(0) for _ in range(3))
        part_out, qkv_out, probs_out, ctx_out = (refs.pop(0) for _ in range(4))
        if level:
            x_out, xhat_out, scale_out = (refs.pop(0) for _ in range(3))
        w_a, sems = refs
        waits = load_a(meta, pieces, w_a, sems)
        if level:
            for rows in chunks(length):
                z = src[rows, :] + (own[rows, :].astype(F32) + other[rows, :].astype(F32)) + shift[2:3, :]
                xhat, scale = norm_rows(z)
                x_out[rows, :] = (xhat * gain[1:2, :] + shift[3:4, :]).astype(BF16)
                xhat_out[rows, :] = xhat.astype(BF16)
                scale_out[rows, :] = scale
            x_ref = x_out
        else:
            x_ref = src
        wait_all(waits)
        for j in range(2):
            c = slice(j * three, (j + 1) * three)
            for rows in chunks(length, 256):
                qkv_out[rows, c] = (nn(x_ref[rows, :], w_a[j, :, :three]) + bias[:, c]).astype(BF16)
        v_t = jnp.concatenate(
            [qkv_out[:, j * three + 2 * cols : (j + 1) * three].astype(F32) for j in range(2)], 1
        ).T.astype(BF16)
        for queries in chunks(length, 256):
            same = sc[...] == sr[:, queries]
            outs = []
            for h in range(heads):
                j, i = divmod(h, cols // HD)
                at = j * three + i * HD
                q = qkv_out[queries, at : at + HD]
                k = qkv_out[:, at + cols : at + cols + HD]
                st = jnp.where(same, nt(k, q) * 0.125, -1e30)
                p = jnp.exp(st - jnp.max(st, 0, keepdims=True))
                p = (p * (1.0 / jnp.sum(p, 0, keepdims=True))).astype(BF16)
                probs_out[h, :, queries] = p
                outs.append(nn(v_t[h * HD : (h + 1) * HD], p))
            ctx = jnp.concatenate(outs, 0).T.astype(BF16)
            ctx_out[queries, :] = ctx
            part_out[queries, :] = (
                nt(ctx[:, :cols], w_a[0, :, three:]) + nt(ctx[:, cols:], w_a[1, :, three:])
            ).astype(BF16)

    outs = [
        sds((length, width), BF16), sds((length, 2 * three), BF16),
        sds((heads, length, length), BF16), sds((length, 2 * cols), BF16),
    ]
    args = [meta, x_or_mid]
    if level:
        args += [*parts, *norms]
        outs += [sds((length, width), BF16), sds((length, width), BF16), sds((length, 1), F32)]
    specs = [SM] + [VM] * (len(args) - 1) + [ANY] * 10 + [VM] * 3
    args += [*pieces, bias, seg_col, seg_row]
    return pl.pallas_call(
        body,
        out_shape=outs,
        in_specs=specs,
        out_specs=[VM] * len(outs),
        scratch_shapes=[pltpu.VMEM((2, width, four), BF16), pltpu.SemaphoreType.DMA((copies_of(pieces[5]),))],
        compiler_params=params(),
        cost_estimate=takes(13),
        name="attn_forward",
    )(*args)


def ffn_forward(meta, x, parts, gains, shifts, pieces, bias_in):
    units = pieces[5].shape[2]
    length, width = x.shape

    def body(meta, x, own, other, gain, shift, p0, p1, p2, p3, p4, p5, p6, p7, p8, p9, bias,
             part_out, mid_out, xhat_out, scale_out, act_out, slope_out, w_i, w_f, low, sems):
        first, second = load_b(meta, (p0, p1, p2, p3, p4, p5, p6, p7, p8, p9), w_i, w_f, sems)
        for rows in chunks(length):
            z = x[rows, :].astype(F32) + (own[rows, :].astype(F32) + other[rows, :].astype(F32)) + shift[0:1, :]
            xhat, scale = norm_rows(z)
            mid = xhat * gain[0:1, :] + shift[1:2, :]
            mid_out[rows, :] = mid
            low[rows, :] = mid.astype(BF16)
            xhat_out[rows, :] = xhat.astype(BF16)
            scale_out[rows, :] = scale
        wait_all(first)
        for rows in chunks(length, 256):
            for c in chunks(units, 512):
                pre = nn(low[rows, :], w_i[:, c]) + bias[:, c]
                act, slope = gelu_parts(pre)
                act_out[rows, c] = act.astype(BF16)
                slope_out[rows, c] = slope.astype(BF16)
        wait_all(second)
        for rows in chunks(length, 256):
            part_out[rows, :] = nt(act_out[rows, :], w_f[...]).astype(BF16)

    return pl.pallas_call(
        body,
        out_shape=[
            sds((length, width), BF16), sds((length, width), F32), sds((length, width), BF16),
            sds((length, 1), F32), sds((length, units), BF16), sds((length, units), BF16),
        ],
        in_specs=[SM] + [VM] * 5 + [ANY] * 10 + [VM],
        out_specs=[VM] * 6,
        scratch_shapes=[
            pltpu.VMEM((width, units), BF16), pltpu.VMEM((width, units), BF16),
            pltpu.VMEM((length, width), BF16), pltpu.SemaphoreType.DMA((copies_of(pieces[5]),)),
        ],
        compiler_params=params(),
        cost_estimate=takes(9),
        name="ffn_forward",
    )(meta, x, *parts, gains, shifts, *pieces, bias_in)


def last_norm(mid, parts, gains, shifts, tok_row, cls_pos):
    length, width = mid.shape
    n_cls = cls_pos.shape[0]

    def body(cls, mid, own, other, gain, shift, tok, y_out, xhat_out, scale_out, cls_out):
        for rows in chunks(length):
            z = mid[rows, :] + (own[rows, :].astype(F32) + other[rows, :].astype(F32)) + shift[2:3, :]
            xhat, scale = norm_rows(z)
            y_out[rows, :] = (xhat * gain[1:2, :] + shift[3:4, :]).astype(BF16)
            xhat_out[rows, :] = xhat.astype(BF16)
            scale_out[rows, :] = scale
        which = lax.broadcasted_iota(jnp.int32, (16, length), 0)
        hot = jnp.zeros((16, length), F32)
        for p in range(n_cls):
            hot = jnp.where(jnp.logical_and(which == p, tok[...] == cls[p]), 1.0, hot)
        cls_out[...] = nn(hot.astype(BF16), y_out[...])[:n_cls].astype(BF16)

    return pl.pallas_call(
        body,
        out_shape=[
            sds((length, width), BF16), sds((length, width), BF16), sds((length, 1), F32),
            sds((n_cls, width), BF16),
        ],
        in_specs=[SM] + [VM] * 6,
        out_specs=[VM] * 4,
        compiler_params=params(),
        cost_estimate=takes(2),
        name="last_norm",
    )(cls_pos, mid, *parts, gains, shifts, tok_row)


def ffn_backward(level, meta, sources, xhat, scale, gains, slope, pieces):
    units = pieces[5].shape[2]
    length, width = xhat.shape
    n_cls = sources[3].shape[0] if level else 0

    def body(meta, *refs):
        refs = list(refs)
        if level:
            cls, grad, d_cls, tok = (refs.pop(0) for _ in range(4))
        else:
            d_above, own, other = (refs.pop(0) for _ in range(3))
        xhat, scale, gain, slope = (refs.pop(0) for _ in range(4))
        pieces = [refs.pop(0) for _ in range(10)]
        part_out, second_out, low_out, pre_out, vec_out, inb_out, w_i, w_f, sems = refs
        first, second = load_b(meta, pieces, w_i, w_f, sems)
        sums = [jnp.zeros((1, width), F32) for _ in range(3)]
        for rows in chunks(length):
            if level:
                d_out = grad[rows, :].astype(F32)
                for p in range(n_cls):
                    d_out = d_out + jnp.where(tok[rows, :] == cls[p], 1.0, 0.0) * d_cls[p : p + 1, :]
            else:
                d_out = d_above[rows, :] + (own[rows, :].astype(F32) + other[rows, :].astype(F32))
                d_out = d_out.astype(BF16).astype(F32)
            hat = xhat[rows, :].astype(F32)
            d_second = norm_back_rows(d_out, gain[1:2, :], hat, scale[rows, :])
            second_out[rows, :] = d_second
            low_out[rows, :] = d_second.astype(BF16)
            for n, item in enumerate((d_out * hat, d_out, d_second)):
                sums[n] = sums[n] + jnp.sum(item, 0, keepdims=True)
        for n in range(3):
            vec_out[n : n + 1, :] = sums[n]
        wait_all(second)
        for n, rows in enumerate(chunks(length, 256)):
            for c in chunks(units, units // 4):
                d_act = nn(low_out[rows, :], w_f[:, c])
                d_pre = (slope[rows, c].astype(F32) * d_act).astype(BF16)
                pre_out[rows, c] = d_pre
                j, at = divmod(c.start, units // 2)
                at = slice(at, at + c.stop - c.start)
                total = jnp.sum(d_pre.astype(F32), 0, keepdims=True)
                inb_out[j : j + 1, at] = total if n == 0 else inb_out[j : j + 1, at] + total
        wait_all(first)
        for rows in chunks(length, 256):
            part_out[rows, :] = nt(pre_out[rows, :], w_i[...]).astype(BF16)

    if level:
        token_grad, d_cls, tok_col, cls_pos = sources
        args, specs = [meta, cls_pos, token_grad, d_cls, tok_col], [SM, SM, VM, VM, VM]
    else:
        args, specs = [meta, *sources], [SM, VM, VM, VM]
    args += [xhat, scale, gains, slope, *pieces]
    specs += [VM] * 4 + [ANY] * 10
    return pl.pallas_call(
        body,
        out_shape=[
            sds((length, width), BF16), sds((length, width), F32), sds((length, width), BF16),
            sds((length, units), BF16), sds((3, width), F32), sds((2, units // 2), F32),
        ],
        in_specs=specs,
        out_specs=[VM] * 6,
        scratch_shapes=[
            pltpu.VMEM((width, units), BF16), pltpu.VMEM((width, units), BF16),
            pltpu.SemaphoreType.DMA((copies_of(pieces[5]),)),
        ],
        compiler_params=params(),
        cost_estimate=takes(9),
        name="ffn_backward",
    )(*args)


def grads_of(nz, own_rows, rz, width):
    half = width // 2
    return [
        sds((2, own_rows, width), BF16), sds((2, nz - 1, rz, half), BF16),
        sds((nz - 1, rz, half), BF16), sds((nz - 1, rz, half), BF16),
    ]


def put_grad(outs, j, k, column, value, first=0):
    own, pair, next_b, own_b = outs
    value = value.astype(BF16)
    half, (height, width) = own_b.shape[2], value.shape
    rows = slice(first, first + height)
    if k == 0:
        own[j, rows, column : column + width] = value
    elif column < half:
        pair[1 - j, k - 1, rows, column : column + width] = value
    else:
        (next_b if j else own_b)[k - 1, rows, column - half : column - half + width] = value


def ffn_grads(meta, mid, d_pre, d_ffn, act, nz, extra):
    length, width = mid.shape
    units = d_pre.shape[1]
    one = units // 2
    rz = width // nz

    def body(meta, mid, d_pre, d_ffn, act, *refs):
        outs, (mid_t, ffn_t) = refs[:4], refs[4:]
        mid_t[...] = mid[...].T.astype(BF16)
        ffn_t[...] = d_ffn[...].astype(F32).T.astype(BF16)
        for j in range(2):
            c = slice(j * one, (j + 1) * one)
            for k in range(nz):
                rows = zrows(meta, k, rz)
                put_grad(outs, j, k, 0, nn(mid_t[rows, :], d_pre[:, c]))
                put_grad(outs, j, k, one, nn(ffn_t[rows, :], act[:, c]))
            if extra:
                put_grad(outs, j, 0, 0, jnp.zeros((extra, units), F32), rz)

    return pl.pallas_call(
        body,
        out_shape=grads_of(nz, rz + extra, rz, units),
        in_specs=[SM] + [VM] * 4,
        out_specs=[VM] * 4,
        scratch_shapes=[pltpu.VMEM((width, length), BF16)] * 2,
        compiler_params=params(),
        cost_estimate=takes(7),
        name="ffn_grads",
    )(meta, mid, d_pre, d_ffn, act)


def attn_backward(meta, d_second, parts, xhat, scale, gains, qkv, probs, pieces):
    four = pieces[5].shape[2]
    length, width = d_second.shape
    cols = four // 4
    three = 3 * cols
    heads = 2 * cols // HD

    def body(meta, d_second, own, other, xhat, scale, gain, qkv, probs, p0, p1, p2, p3, p4, p5, p6, p7, p8, p9,
             part_out, first_out, low_out, dqkv_out, vec_out, sum_out,
             w_a, d_ctx, acc_v, acc_k, sems):
        waits = load_a(meta, (p0, p1, p2, p3, p4, p5, p6, p7, p8, p9), w_a, sems)
        sums = [jnp.zeros((1, width), F32) for _ in range(3)]
        for rows in chunks(length):
            d_mid = d_second[rows, :] + (own[rows, :].astype(F32) + other[rows, :].astype(F32))
            hat = xhat[rows, :].astype(F32)
            d_first = norm_back_rows(d_mid, gain[0:1, :], hat, scale[rows, :])
            first_out[rows, :] = d_first
            low_out[rows, :] = d_first.astype(BF16)
            for n, item in enumerate((d_mid * hat, d_mid, d_first)):
                sums[n] = sums[n] + jnp.sum(item, 0, keepdims=True)
        for n in range(3):
            vec_out[n : n + 1, :] = sums[n]
        wait_all(waits)
        for j in range(2):
            for rows in chunks(length, 256):
                d_ctx[rows, j * cols : (j + 1) * cols] = nn(low_out[rows, :], w_a[j, :, three:]).astype(BF16)
        k_t = jnp.concatenate(
            [qkv[:, j * three + cols : j * three + 2 * cols].astype(F32) for j in range(2)], 1
        ).T.astype(BF16)
        for h in range(heads):
            j, i = divmod(h, cols // HD)
            at = j * three + i * HD
            q_cols, k_cols, v_cols = (slice(at + n * cols, at + n * cols + HD) for n in range(3))
            for n, queries in enumerate(chunks(length, 256)):
                d_o = d_ctx[queries, h * HD : (h + 1) * HD]
                d_p = nt(qkv[:, v_cols], d_o)
                p = probs[h, :, queries]
                wide = p.astype(F32)
                d_s = (wide * (d_p - jnp.sum(wide * d_p, 0, keepdims=True))).astype(BF16)
                d_v = nn(p, d_o)
                d_k = nn(d_s, qkv[queries, q_cols])
                acc_v[...] = d_v if n == 0 else acc_v[...] + d_v
                acc_k[...] = d_k if n == 0 else acc_k[...] + d_k
                d_q = nn(k_t[h * HD : (h + 1) * HD], d_s)
                dqkv_out[queries, q_cols] = (d_q.T * 0.125).astype(BF16)
            dqkv_out[:, v_cols] = acc_v[...].astype(BF16)
            dqkv_out[:, k_cols] = (acc_k[...] * 0.125).astype(BF16)
        for j in range(2):
            sum_out[j : j + 1, :] = jnp.sum(
                dqkv_out[:, j * three : (j + 1) * three].astype(F32), 0, keepdims=True
            )
        for rows in chunks(length, 256):
            part_out[rows, :] = (
                nt(dqkv_out[rows, :three], w_a[0, :, :three]) + nt(dqkv_out[rows, three:], w_a[1, :, :three])
            ).astype(BF16)

    return pl.pallas_call(
        body,
        out_shape=[
            sds((length, width), BF16), sds((length, width), F32), sds((length, width), BF16),
            sds((length, 2 * three), BF16), sds((3, width), F32), sds((2, three), F32),
        ],
        in_specs=[SM] + [VM] * 8 + [ANY] * 10,
        out_specs=[VM] * 6,
        scratch_shapes=[
            pltpu.VMEM((2, width, four), BF16), pltpu.VMEM((length, 2 * cols), BF16),
            pltpu.VMEM((length, HD), F32), pltpu.VMEM((length, HD), F32),
            pltpu.SemaphoreType.DMA((copies_of(pieces[5]),)),
        ],
        compiler_params=params(),
        cost_estimate=takes(15),
        name="attn_backward",
    )(meta, d_second, *parts, xhat, scale, gains, qkv, probs, *pieces)


def attn_grads(meta, places, x, d_attn, d_qkv, ctx, vectors, nz, extra):
    length, width = x.shape
    three = d_qkv.shape[1] // 2
    cols = ctx.shape[1] // 2
    rz = width // nz

    def body(meta, places, x, d_attn, d_qkv, ctx, vec1, vec2, sum_qkv, sum_inb, *refs):
        outs, (x_t, a_t, norm_rows_, qv_rows, inb_rows) = refs[:4], refs[4:]
        x_t[...] = x[...].astype(F32).T.astype(BF16)
        a_t[...] = d_attn[...].astype(F32).T.astype(BF16)
        for j in range(2):
            for k in range(nz):
                rows = zrows(meta, k, rz)
                grad = nn(x_t[rows, :], d_qkv[:, j * three : (j + 1) * three])
                put_grad(outs, j, k, 0, grad[:, : 2 * cols])
                put_grad(outs, j, k, 2 * cols, grad[:, 2 * cols :])
                put_grad(outs, j, k, three, nn(a_t[rows, :], ctx[:, j * cols : (j + 1) * cols]))
        if not extra:
            return
        piece, part = width // (4 * nz), cols // nz
        units = sum_inb.shape[1] // nz
        norm_rows_[...] = jnp.zeros_like(norm_rows_)
        norm_rows_[0:3, :] = vec1[...]
        norm_rows_[3:6, :] = vec2[...]
        for j in range(2):
            qv_rows[...] = jnp.zeros_like(qv_rows)
            qv_rows[0:1, :cols] = sum_qkv[j : j + 1, :cols]
            qv_rows[1:2, :cols] = sum_qkv[j : j + 1, 2 * cols : three]
            inb_rows[...] = jnp.zeros_like(inb_rows)
            inb_rows[0:1, :] = sum_inb[j : j + 1, :]
            for k in range(nz):
                d = places[2 + k]
                from_norm = pltpu.roll(norm_rows_[...], width - (d * 4 + places[j]) * piece, 1)
                from_qv = pltpu.roll(qv_rows[...], width - d * part, 1)
                from_inb = pltpu.roll(inb_rows[...], width - d * units, 1)
                lane = lax.broadcasted_iota(jnp.int32, (8, 2 * cols), 1)
                upper = jnp.where(lane < piece, from_norm[:, : 2 * cols], 0.0)
                lower = jnp.where(lane < part, from_qv[:, : 2 * cols], 0.0)
                shifted = pltpu.roll(from_inb, 128, 1)[:, : 2 * cols]
                inside = jnp.logical_and(lane >= 128, lane < 128 + units)
                lower = jnp.where(inside, shifted, lower)
                put_grad(outs, j, k, 0, jnp.concatenate([upper, lower], 0), rz)
                put_grad(outs, j, k, 2 * cols, jnp.zeros((extra, 2 * cols), F32), rz)

    return pl.pallas_call(
        body,
        out_shape=grads_of(nz, rz + extra, rz + extra, three + cols),
        in_specs=[SM, SM] + [VM] * 8,
        out_specs=[VM] * 4,
        scratch_shapes=[pltpu.VMEM((width, length), BF16)] * 2 + [pltpu.VMEM((8, width), F32)] * 3,
        compiler_params=params(),
        cost_estimate=takes(4),
        name="attn_grads",
    )(meta, places, x, d_attn, d_qkv, ctx, *vectors)


def loss_kernel(own, perm, slots, queries, positive_col, n_own):
    n_q, width = queries.shape
    n_p = slots.shape[0]

    def body(own, perm, slots, queries, pos, loss_out, d_out):
        passages = nn(perm[...], slots[...]).astype(BF16)
        logits = nt(queries[...], passages)
        top = jnp.max(logits, -1, keepdims=True)
        log_total = top + jnp.log(jnp.sum(jnp.exp(logits - top), -1, keepdims=True))
        index = lax.broadcasted_iota(jnp.int32, (n_q, n_p), 1)
        hits = pos[...] == index
        chosen = jnp.sum(jnp.where(hits, logits, 0.0), -1, keepdims=True)
        loss_out[...] = jnp.sum(log_total - chosen, 0, keepdims=True) / n_q
        d_logits = (16.0 * (jnp.exp(logits - log_total) - jnp.where(hits, 1.0, 0.0))).astype(BF16)
        pick = jnp.where(
            lax.broadcasted_iota(jnp.int32, (n_p, 128), 0)
            == lax.broadcasted_iota(jnp.int32, (n_p, 128), 1) + own[0],
            1.0, 0.0,
        ).astype(BF16)
        cols = nn(d_logits, pick)
        d_out[...] = nn(cols.T.astype(BF16), queries[...])[:n_own]

    return pl.pallas_call(
        body,
        out_shape=[sds((1, 1), F32), sds((n_own, width), F32)],
        in_specs=[SM] + [VM] * 4,
        out_specs=[VM] * 2,
        compiler_params=params(),
        cost_estimate=takes(1),
        name="contrast",
    )(own, perm, slots, queries, positive_col)


def on_device(
    inputs, cls_pos, w_qkv, qv_bias, w_out, w_in, in_bias, w_ffn_out,
    layer_gains, shifts, queries, positive, token_grad,
):
    core = lax.axis_index("section")
    dp = lax.axis_index("dp")
    me = lax.axis_index("tensor")
    n_dp = lax.axis_size("dp")
    n_t = lax.axis_size("tensor")
    first_core = core == 0
    rows_dev, share, width = inputs.shape
    cols = w_qkv.shape[3]
    units = w_in.shape[2]
    length = n_t * share
    n_chips = n_dp * n_t
    piece = width // n_chips
    order = dp_order()
    direct = direct_dp()
    nz, extra = (4, 16) if direct else (2, 0)
    t_ids = jnp.arange(n_t, dtype=jnp.int32)

    vec = jnp.concatenate(
        [layer_gains.reshape(-1), shifts.reshape(-1), qv_bias.reshape(-1), in_bias.reshape(-1)]
    )
    n_gain, n_shift, n_qv, n_inb = layer_gains.size, shifts.size, qv_bias.size, in_bias.size
    n_vec = vec.shape[0]
    flat = jnp.concatenate(
        [vec, queries.reshape(-1), (positive // 16).astype(BF16), (positive % 16).astype(BF16)]
    )
    flat = jnp.pad(flat, (0, -flat.shape[0] % 2048)).reshape(-1, 128)

    def spread_rows(block):
        blocks = [lax.dynamic_index_in_dim(block, me ^ k, 0, keepdims=False) for k in range(n_t)]
        return jnp.concatenate(exchange_rows(blocks), 0)

    pack = jnp.concatenate(
        [w_qkv[0, :, 0], w_qkv[0, :, 1], w_qkv[0, :, 2], w_out[0].T, w_in[0], w_ffn_out[0].T], 1
    )
    own_a, own_b = pack[:, :width], pack[:, width:]
    if direct:
        own = pack
        z_a0 = rest_direct(own_a, 0)
    else:
        pack = lax.all_gather(pack, "dp", axis=0, tiled=True)
        own, other_rows = pack[: width // 2], pack[width // 2 :][None]
    near0, far0 = gather_own(own)
    x_low = spread_rows(inputs)
    if direct:
        rest_a0 = stack_rest(z_a0)
        one_b0 = core_hop(after(own_b, rest_a0), "dp", 1, 0)
        z_b0 = rest_dp(own_b, one_b0, 0)
    else:
        rest_a0 = other_rows[:, :, :width]
    near_a0 = gather_near(rest_a0, 0)
    both0 = gather_own_both(near0, far0)
    owns = [own, near0, far0, *both0]
    message = after(flat, near0)
    message = double(message, "dp") if direct else spread_dp(message)
    message = double(after(message, near_a0), "tensor")
    both_a0 = gather_both(*after(near_a0, both0), 0)
    if direct:
        rest_b0 = stack_rest(z_b0, near_a0)
        one = core_hop(after(pack, rest_b0), "dp", 1, 1)
        one_a1, one_b1 = one[:, :width], one[:, width:]
        z_a1 = rest_dp(own_a, one_a1, 1)
    else:
        rest_b0 = other_rows[:, :, width:]
    near_b0 = gather_near(after(rest_b0, near_a0), 0)

    zrow = order * (width // n_dp) if direct else jnp.arange(2, dtype=jnp.int32) * (width // 2)
    metas = [
        jnp.concatenate([(core == level)[None].astype(jnp.int32), zrow.astype(jnp.int32)])
        for level in range(2)
    ]
    slots = [me ^ (2 * (core != level) + jnp.arange(2, dtype=jnp.int32)) for level in range(2)]
    places = [jnp.concatenate([s, order[:nz]]).astype(jnp.int32) for s in slots]
    hots = [(s[:, None] == t_ids[None, :]).astype(F32) for s in slots]

    positions = jnp.concatenate(
        [(me ^ k) * share + jnp.arange(share, dtype=jnp.int32) for k in range(n_t)]
    )
    cls_row = lax.dynamic_index_in_dim(cls_pos, me, 0, keepdims=False)
    segments = jnp.sum((positions[:, None] >= cls_row[None, :]).astype(jnp.int32), -1)
    seg_col, seg_row = segments[:, None], segments[None, :]
    tok_col, tok_row = positions[:, None], positions[None, :]

    slot_ids = (order[None, :] * n_t + (me ^ t_ids)[:, None]).reshape(-1)
    to_natural = (jnp.arange(n_chips, dtype=jnp.int32)[:, None] == slot_ids[None, :]).astype(BF16)
    table = nn(to_natural, message.reshape(n_chips, -1))
    own_table = table[:, :n_vec].astype(BF16)
    other_table = swap_cores(own_table)
    tables = jnp.where(
        first_core, jnp.stack([own_table, other_table]), jnp.stack([other_table, own_table])
    ).astype(F32)
    at = 0
    gains = tables[:, :, at : at + n_gain].reshape(2, n_chips, 2, piece).transpose(0, 2, 1, 3).reshape(2, 2, width)
    at += n_gain
    shift = tables[:, :, at : at + n_shift].reshape(2, n_chips, 4, piece).transpose(0, 2, 1, 3).reshape(2, 4, width)
    at += n_shift
    qv = tables[:, :, at : at + n_qv].reshape(2, n_dp, n_t, 2, cols // n_dp)
    qv = qv.transpose(0, 3, 2, 1, 4).reshape(2, 2, n_t, cols)
    at += n_qv
    inb = tables[:, :, at : at + n_inb].reshape(2, n_dp, n_t, n_inb).transpose(0, 2, 1, 3).reshape(2, n_t, units)
    vectors = []
    for level in range(2):
        bias = jnp.sum(hots[level][None, :, :, None] * qv[level][:, None], 2)
        bias = jnp.stack([bias[0], jnp.zeros_like(bias[0]), bias[1]], 1).reshape(1, -1)
        bias_in = jnp.sum(hots[level][:, :, None] * inb[level][None], 1).reshape(1, -1)
        vectors.append((gains[level], shift[level], bias, bias_in))
    at = n_vec
    q_dev = queries.shape[0]
    all_q = table[:, at : at + q_dev * width].reshape(-1, width).astype(BF16)
    at += q_dev * width
    all_pos = table[:, at : at + q_dev] * 16.0 + table[:, at + q_dev : at + 2 * q_dev]
    all_pos = all_pos.astype(jnp.int32).reshape(-1, 1)
    n_cls = cls_row.shape[0]
    perm = jnp.repeat(jnp.repeat(to_natural, n_cls, 0), n_cls, 1)
    perm = perm * jnp.tile(jnp.eye(n_cls, dtype=BF16), (n_chips, n_chips))

    vectors, all_q, all_pos, perm, x_low = lax.optimization_barrier(
        (vectors, all_q, all_pos, perm, x_low)
    )
    saved = []
    source, parts, norms = after(x_low, rest_b0), None, None
    pieces_a, pieces_b = [[*owns, rest_a0, *near_a0, *both_a0], None], [None, None]
    for level in range(2):
        gain, shift, bias, bias_in = vectors[level]
        outs = attn_forward(
            level, metas[level], source, parts, norms, pieces_a[level], bias, seg_col, seg_row
        )
        part, qkv, probs, ctx = outs[:4]
        if level == 0:
            if direct:
                rest_a1 = stack_rest(z_a1, near_b0)
                z_b1 = rest_dp(own_b, one_b1, 1, rest_a1)
            else:
                rest_a1 = other_rows[:, :, :width]
            near_a1 = gather_near(after(rest_a1, near_b0), 1)
            both_b0 = gather_both(*after(near_b0, both_a0, part), 0)
            pieces_b[0] = [*owns, rest_b0, *near_b0, *both_b0]
        else:
            pieces_b[1] = [*owns, rest_b1, *near_b1, *both_b1]
        if level:
            x, xhat2, scale2 = outs[4:]
            saved[0]["second"] = (xhat2, scale2)
        else:
            x = x_low
        part, mid, xhat1, scale1, act, slope = ffn_forward(
            metas[level], x, (part, swap_cores(part)), gain, shift, pieces_b[level], bias_in
        )
        saved.append(
            dict(x=x, qkv=qkv, probs=probs, ctx=ctx, mid=mid, xhat1=xhat1, scale1=scale1, act=act, slope=slope)
        )
        source, parts, norms = mid, (part, swap_cores(part)), (gain, shift)
        if level == 0:
            rest_b1 = stack_rest(z_b1, near_a1) if direct else other_rows[:, :, width:]
            near_b1 = gather_near(after(rest_b1, near_a1), 1)
            both_a1 = gather_both(*after(near_a1, both_b0), 1)
            both_b1 = gather_both(*after(near_b1, both_a1, part), 1)
            pieces_a[1] = [*owns, rest_a1, *near_a1, *both_a1]
    y, xhat2, scale2, cls_own = last_norm(source, parts, *norms, tok_row, cls_row)
    saved[1]["second"] = (xhat2, scale2)
    tokens = spread_rows(after(token_grad, cls_own))

    cls_slots = spread_tensor(spread_dp(cls_own)).reshape(n_chips * n_cls, width)
    first_own = ((dp * n_t + me) * n_cls).astype(jnp.int32)[None]
    mean_loss, d_cls = loss_kernel(first_own, perm, cls_slots, all_q, all_pos, n_cls)

    vector_rows = [None, None]
    sources = (tokens, d_cls, tok_col, cls_row)
    sums_a, sums_b, own_grads = [None, None], [None, None], [None, None]
    for level in (1, 0):
        gain = vectors[level][0]
        kept = saved[level]
        meta = metas[level]
        xhat2, scale2 = kept["second"]
        if level == 0:
            sources = (after(sources[0], sums_b[1].first(grads_a[1])), *sources[1:])
        part, d_second, d_ffn, d_pre, vec2, sum_inb = ffn_backward(
            level, meta, sources, xhat2, scale2, gain, kept["slope"], pieces_b[level]
        )
        other = swap_cores(part)
        if level == 0:
            d_ffn = after(d_ffn, sums_a[1].first(part))
        grads_b = ffn_grads(meta, kept["mid"], d_pre, d_ffn, kept["act"], nz, extra)
        own_b, *grads_b = grads_b
        sums_b[level] = Reduction(grads_b, level)
        d_second = after(d_second, grads_b[1])
        if level == 0:
            d_second = after(d_second, sums_b[1].second(grads_b[1]))
        part, d_first, d_attn, d_qkv, vec1, sum_qkv = attn_backward(
            meta, d_second, (part, other), kept["xhat1"], kept["scale1"], gain,
            kept["qkv"], kept["probs"], pieces_a[level],
        )
        other = swap_cores(part)
        if level == 0:
            d_attn = after(d_attn, sums_a[1].second(part))
        own_a, *grads_a = attn_grads(
            meta, places[level], kept["x"], d_attn, d_qkv, kept["ctx"], (vec1, vec2, sum_qkv, sum_inb), nz, extra
        )
        own_grads[level] = jnp.concatenate([own_a, own_b], 2)
        sums_a[level] = Reduction(grads_a, level)
        vector_rows[level] = (vec1, vec2, sum_qkv, sum_inb)
        sources = (d_first, part, other)
    sums_b[0].first(grads_a[1])
    sums_b[1].third(sums_b[0].added)
    sums_a[0].first(sums_b[1].pieces)
    sums_a[1].third(sums_a[0].added)
    last_1 = last_dp([sums_a[1], sums_b[1]])
    own_sum = OwnReduction(own_grads, sums_a[0].added)
    sums_b[0].second(sums_a[1].pieces)
    sums_a[0].second(sums_b[0].sums)
    sums_b[0].third(sums_a[0].sums)
    own_sum.first(sums_b[0].pieces)
    d_hidden = d_first + (part.astype(F32) + other.astype(F32))
    outgoing = jnp.where(first_core, d_hidden, y.astype(F32))
    low = after(outgoing.astype(BF16), own_sum.added).reshape(n_t, share, width)
    incoming = [outgoing[:share]] + [b.astype(F32) for b in exchange_rows([low[k] for k in range(n_t)])[1:]]
    boundary = jnp.zeros((n_t, share, width), F32)
    for k in range(n_t):
        boundary = lax.dynamic_update_index_in_dim(boundary, incoming[k], me ^ k, 0)
    sums_a[0].third(own_sum.added)
    last_0 = last_dp([sums_a[0], sums_b[0]])
    total = own_sum.second()
    if direct:
        here, got = (jnp.where(first_core, low, high).astype(F32) for low, high in zip(last_0, last_1))
        total = total + here + got
        end = width // n_dp
        own = total[end : end + 6, :piece]
        qv = total[end + 8 : end + 10, : qv_bias.shape[3]]
        grad_inb = total[end + 8 : end + 9, 128 : 128 + n_inb]
        total = total[:end]
    else:
        whole = jnp.concatenate([total, jnp.where(first_core, last_0, last_1)]).astype(BF16)
        total = lax.psum_scatter(whole, "dp", scatter_dimension=0, tiled=True).astype(F32)
        tables = []
        for level in range(2):
            vec1, vec2, sum_qkv, sum_inb = vector_rows[level]
            by_t = lax.dot_general(
                hots[level], jnp.concatenate([sum_qkv, sum_inb], 1), (((0,), (0,)), ((), ())),
                precision=lax.Precision.HIGHEST,
            )
            whole = 0.5 * jnp.concatenate([vec1, vec2])
            whole = jnp.pad(whole, ((0, 0), (0, by_t.shape[1] - width)))
            tables.append(jnp.concatenate([whole, by_t]))
        tables = lax.psum(jnp.stack(tables), ("section", "dp", "tensor"))
        flat = jnp.where(first_core, tables[0], tables[1])
        own = lax.dynamic_slice_in_dim(flat[:6, :width], (dp * n_t + me) * piece, piece, 1)
        by_t = lax.dynamic_slice_in_dim(flat, 6 + me, 1, 0)
        qv = jnp.concatenate([by_t[:, :cols], by_t[:, 2 * cols : 3 * cols]])
        qv = lax.dynamic_slice_in_dim(qv, dp * qv_bias.shape[3], qv_bias.shape[3], 1)
        grad_inb = lax.dynamic_slice_in_dim(by_t[:, 3 * cols :], dp * n_inb, n_inb, 1)
    tot_a, tot_b = total[:, :width], total[:, width:]
    grad_gains = jnp.concatenate([own[0:1], own[3:4]]).reshape(layer_gains.shape)
    grad_shifts = jnp.concatenate([own[2:3], own[1:2], own[5:6], own[4:5]]).reshape(shifts.shape)
    grad_qv, grad_inb = qv.reshape(qv_bias.shape), grad_inb.reshape(in_bias.shape)

    grad_qkv = jnp.stack([tot_a[:, n * cols : (n + 1) * cols] for n in range(3)], 1)[None]
    grad_out = tot_a[:, 3 * cols :].T[None]
    grad_in = tot_b[:, :units][None]
    grad_ffn = tot_b[:, units:].T[None]
    return (
        grad_qkv, grad_qv, grad_out, grad_in, grad_inb, grad_ffn,
        grad_gains, grad_shifts, boundary[None], mean_loss.reshape(()),
    )


def solution(mesh):
    return jax.shard_map(
        on_device,
        mesh=mesh,
        in_specs=(
            P("dp", "tensor", None),
            P("dp", None),
            P("section", "dp", None, "tensor"),
            P("section", None, "tensor", "dp"),
            P("section", "tensor", "dp"),
            P("section", "dp", "tensor"),
            P("section", "tensor", "dp"),
            P("section", "tensor", "dp"),
            P("section", None, ("dp", "tensor")),
            P("section", None, ("dp", "tensor")),
            P(("dp", "tensor"), None),
            P(("dp", "tensor")),
            P("dp", "tensor", None),
        ),
        out_specs=(
            P("section", "dp", None, "tensor"),
            P("section", None, "tensor", "dp"),
            P("section", "tensor", "dp"),
            P("section", "dp", "tensor"),
            P("section", "tensor", "dp"),
            P("section", "tensor", "dp"),
            P("section", None, ("dp", "tensor")),
            P("section", None, ("dp", "tensor")),
            P("section", "dp", "tensor", None),
            P(),
        ),
        check_vma=False,
    )
```

```python
import jax
import jax.numpy as jnp
from jax import lax
from jax.experimental import pallas as pl
from jax.experimental.pallas import tpu as pltpu
from jax.sharding import PartitionSpec as P

HD = 64
PARTNER = 1
CROSS = 2
BF16 = jnp.bfloat16
F32 = jnp.float32


def mm(left, right, dims):
    return lax.dot_general(left, right, (dims, ((), ())), preferred_element_type=F32)


def nn(left, right):
    return mm(left, right, ((1,), (0,)))


def nt(left, right):
    return mm(left, right, ((1,), (1,)))


def after(block, *earlier):
    return lax.optimization_barrier((block, *earlier))[0]


def swap_cores(block):
    return lax.ppermute(block, "section", [(0, 1), (1, 0)])


def hop(block, axis, flip):
    return lax.ppermute(block, axis, [(i, i ^ flip) for i in range(lax.axis_size(axis))])


def core_hop(block, axis, flip, core):
    size = lax.axis_size(axis)
    route = [(core * size + i, core * size + (i ^ flip)) for i in range(size)]
    return lax.ppermute(block, ("section", axis), route)


def cross_hop(block, source):
    size = lax.axis_size("tensor")
    route = [(source * size + i, (1 - source) * size + (i ^ CROSS)) for i in range(size)]
    return lax.ppermute(block, ("section", "tensor"), route)


def direct_dp():
    return lax.axis_size("dp") == 4


def dp_order():
    size = lax.axis_size("dp")
    if direct_dp():
        return lax.axis_index("dp") ^ jnp.arange(size, dtype=jnp.int32)
    return jnp.arange(size, dtype=jnp.int32)


def spread_dp(block):
    if direct_dp():
        return jnp.stack([block] + [hop(block, "dp", k) for k in range(1, 4)])
    return lax.all_gather(block, "dp", axis=0, tiled=False)


def spread_tensor(block):
    return jnp.stack([block] + [hop(block, "tensor", k) for k in range(1, 4)])


def double(block, axis):
    pair = jnp.stack([block, hop(block, axis, 1)])
    return jnp.concatenate([pair, hop(pair, axis, 2)])


def exchange_rows(blocks):
    first = hop(jnp.stack([blocks[1], blocks[3]]), "tensor", 1)
    second = hop(jnp.stack([blocks[2], first[1]]), "tensor", 2)
    return [blocks[0], first[0], second[0], second[1]]


def cross_all(block):
    size = lax.axis_size("tensor")
    route = [(s * size + i, (1 - s) * size + (i ^ CROSS)) for s in range(2) for i in range(size)]
    return lax.ppermute(block, ("section", "tensor"), route)


def rest_dp(own, core):
    return [core_hop(own, "dp", k, core) for k in range(1, 4)]


def gather_own(own):
    near, far = hop(own, "tensor", PARTNER), cross_all(own)
    return near, far


def gather_own_both(near, far):
    half = near.shape[1] // 2
    return cross_all(near[:, :half]), hop(far[:, half:], "tensor", PARTNER)


def gather_near(rest, core):
    return core_hop(rest, "tensor", PARTNER, core), cross_hop(rest, core)


def gather_both(near, far, core):
    half = near.shape[2] // 2
    return cross_hop(near[:, :, :half], core), core_hop(far[:, :, half:], "tensor", PARTNER, 1 - core)


def add_low(*items):
    total = items[0].astype(F32)
    for item in items[1:]:
        total = total + item.astype(F32)
    return total.astype(BF16)


class Reduction:
    def __init__(self, grads, core):
        self.core = core
        self.pair, self.next_b, self.own_b = grads
        self.got = cross_hop(self.pair, 1 - core)
        self.near_b = hop(self.next_b, "tensor", PARTNER)

    def first(self, *earlier):
        half = self.next_b.shape[0]
        self.parts = pair, own_b, got, near_b = after((self.pair, self.own_b, self.got, self.near_b), *earlier)
        self.added = add_low(pair[:half], got[:half]), add_low(own_b, near_b)
        self.near_a = core_hop(self.added[0], "tensor", PARTNER, self.core)
        self.far_b = cross_hop(self.added[1], 1 - self.core)
        return self.added

    def sum_halves(self, *earlier):
        half = self.next_b.shape[0]
        near_a, far_b, (pair, own_b, got, near_b) = after((self.near_a, self.far_b, self.parts), *earlier)
        return add_low(pair[half:], got[half:], near_a), add_low(own_b, near_b, far_b)

    def scatter(self):
        whole = jnp.concatenate(self.sums).reshape(-1, self.own_b.shape[2])
        return [lax.psum_scatter(whole, "dp", scatter_dimension=0, tiled=True)]

    def second_direct(self, *earlier):
        a, b = self.sums = self.sum_halves(*earlier)
        if direct_dp():
            self.hops = [
                core_hop(block, "dp", k, self.core) for k, block in ((1, a[1]), (2, b[0]), (3, b[1]))
            ]
        return self.sums

    def third_direct(self, *earlier):
        if not direct_dp():
            return sum(p.astype(F32) for p in self.scatter())
        return sum(p.astype(F32) for p in after([self.sums[0][0], *self.hops], *earlier))

    def second(self, *earlier):
        self.sums = self.sum_halves(*earlier)
        if direct_dp():
            self.across = core_hop(self.sums[1], "dp", 2, self.core)
        return self.sums

    def third(self, *earlier):
        if not direct_dp():
            self.pieces = self.scatter()
            return self.pieces
        a, across = after((self.sums[0], self.across), *earlier)
        self.pieces = [add_low(a[k], across[k]) for k in range(2)]
        return self.pieces


def last_dp(reductions, *earlier):
    if not direct_dp():
        return [r.pieces for r in reductions]
    high = max(r.pieces[0].shape[0] for r in reductions)
    block = [jnp.pad(r.pieces[1], ((0, high - r.pieces[1].shape[0]), (0, 0))) for r in reductions]
    got = core_hop(after(jnp.concatenate(block, 1), *earlier), "dp", 1, reductions[0].core)
    at, out = 0, []
    for r in reductions:
        rows, width = r.pieces[0].shape
        out.append([r.pieces[0], got[:rows, at : at + width]])
        at += width
    return out


VMEM_LIMIT = 48 * 1024 * 1024
CHUNK = 128


def takes(micros):
    return pl.CostEstimate(flops=int(micros * 1.1e9), bytes_accessed=0, transcendentals=0)


def params():
    return pltpu.CompilerParams(vmem_limit_bytes=VMEM_LIMIT)


ANY = pl.BlockSpec(memory_space=pl.ANY)
VM = pl.BlockSpec(memory_space=pltpu.VMEM)
SM = pl.BlockSpec(memory_space=pltpu.SMEM)


def sds(shape, dtype):
    return jax.ShapeDtypeStruct(shape, dtype)


def chunks(length, step=CHUNK):
    return [slice(i, i + step) for i in range(0, length, step)]


def norm_rows(z):
    centre = z - jnp.mean(z, -1, keepdims=True)
    spread = jnp.mean(centre * centre, -1, keepdims=True)
    scale = lax.rsqrt(spread + 1e-05)
    return centre * scale, scale


def norm_back_rows(d_out, gain, xhat, scale):
    g = d_out * gain
    m1 = jnp.mean(g, -1, keepdims=True)
    m2 = jnp.mean(g * xhat, -1, keepdims=True)
    return scale * (g - m1 - xhat * m2)


def gelu_parts(x):
    e = jnp.exp(-0.5 * x * x)
    t = 1.0 / (1.0 + 0.2316418882 * jnp.abs(x))
    poly = t * (
        0.127414796 + t * (-0.142248368 + t * (0.7107068705 + t * (-0.7265760135 + t * 0.5307027145)))
    )
    tail = poly * e
    cdf = jnp.where(x < 0.0, tail, 1.0 - tail)
    return x * cdf, cdf + x * e * 0.3989422804014327


def zrows(meta, k, rz):
    return pl.ds(pl.multiple_of(meta[1 + k], 64), rz)


def cut(start, width, at):
    if start < at < start + width:
        return [(start, at - start), (at, start + width - at)]
    return [(start, width)]


def load_weights(meta, pieces, base, places, sems):
    own, near0, far0, a0, b0, rest, near, far, a, b = pieces
    split, count = a0.shape[1], rest.shape[0]
    home = meta[0] == 1
    lists = [[] for _ in places]
    at = 0
    for j in range(2):
        for k in range(count + 1):
            rows = zrows(meta, k, own.shape[0])
            for n, (start, width, place) in enumerate(places):
                for g, w in cut(base + start, width, split):
                    upper, column = (g < split, g if g < split else g - split)
                    if k == 0:
                        mine = (near0 if j else own).at[:, pl.ds(g, w)]
                        other = (a0 if upper else b0).at[:, pl.ds(column, w)] if j else far0.at[:, pl.ds(g, w)]
                    else:
                        mine = (near if j else rest).at[k - 1, :, pl.ds(g, w)]
                        other = (
                            (a if upper else b).at[k - 1, :, pl.ds(column, w)] if j
                            else far.at[k - 1, :, pl.ds(g, w)]
                        )
                    dst = place(j, rows, g - base - start, w)
                    first = pltpu.make_async_copy(mine, dst, sems.at[at])
                    second = pltpu.make_async_copy(other, dst, sems.at[at])
                    at += 1

                    @pl.when(home)
                    def _():
                        first.start()

                    @pl.when(jnp.logical_not(home))
                    def _():
                        second.start()

                    lists[n].append(first)
    return lists


def copies_of(rest):
    return 2 * 3 * (1 + rest.shape[0])


def wait_all(waits):
    for made in waits:
        made.wait()


def load_a(meta, pieces, w_a, sems):
    width = w_a.shape[2]
    return load_weights(
        meta, pieces, 0, [(0, width, lambda j, rows, c, w: w_a.at[j, rows, pl.ds(c, w)])], sems
    )[0]


def load_b(meta, pieces, w_i, w_f, sems):
    one = w_i.shape[1] // 2
    base = pieces[0].shape[1] - 2 * one
    return load_weights(
        meta,
        pieces,
        base,
        [
            (0, one, lambda j, rows, c, w: w_i.at[rows, pl.ds(j * one + c, w)]),
            (one, one, lambda j, rows, c, w: w_f.at[rows, pl.ds(j * one + c, w)]),
        ],
        sems,
    )


def attn_forward(level, meta, x_or_mid, parts, norms, pieces, bias, seg_col, seg_row, cols):
    four = 4 * cols
    length, width = x_or_mid.shape
    three = 3 * cols
    heads = 2 * cols // HD

    def body(meta, *refs):
        refs = list(refs)
        src = refs.pop(0)
        if level:
            own, other, gain, shift = (refs.pop(0) for _ in range(4))
        pieces = [refs.pop(0) for _ in range(10)]
        bias, sc, sr = (refs.pop(0) for _ in range(3))
        part_out, qkv_out, probs_out, ctx_out = (refs.pop(0) for _ in range(4))
        if level:
            x_out, xhat_out, scale_out = (refs.pop(0) for _ in range(3))
        w_a, sems = refs
        waits = load_a(meta, pieces, w_a, sems)
        if level:
            for rows in chunks(length):
                z = src[rows, :] + (own[rows, :].astype(F32) + other[rows, :].astype(F32)) + shift[2:3, :]
                xhat, scale = norm_rows(z)
                x_out[rows, :] = (xhat * gain[1:2, :] + shift[3:4, :]).astype(BF16)
                xhat_out[rows, :] = xhat.astype(BF16)
                scale_out[rows, :] = scale
            x_ref = x_out
        else:
            x_ref = src
        wait_all(waits)
        for j in range(2):
            c = slice(j * three, (j + 1) * three)
            for rows in chunks(length, 256):
                qkv_out[rows, c] = (nn(x_ref[rows, :], w_a[j, :, :three]) + bias[:, c]).astype(BF16)
        v_t = jnp.concatenate(
            [qkv_out[:, j * three + 2 * cols : (j + 1) * three].astype(F32) for j in range(2)], 1
        ).T.astype(BF16)
        for queries in chunks(length, 256):
            same = sc[...] == sr[:, queries]
            outs = []
            for h in range(heads):
                j, i = divmod(h, cols // HD)
                at = j * three + i * HD
                q = qkv_out[queries, at : at + HD]
                k = qkv_out[:, at + cols : at + cols + HD]
                st = jnp.where(same, nt(k, q) * 0.125, -1e30)
                p = jnp.exp(st - jnp.max(st, 0, keepdims=True))
                p = (p * (1.0 / jnp.sum(p, 0, keepdims=True))).astype(BF16)
                probs_out[h, :, queries] = p
                outs.append(nn(v_t[h * HD : (h + 1) * HD], p))
            ctx = jnp.concatenate(outs, 0).T.astype(BF16)
            ctx_out[queries, :] = ctx
            part_out[queries, :] = (
                nt(ctx[:, :cols], w_a[0, :, three:]) + nt(ctx[:, cols:], w_a[1, :, three:])
            ).astype(BF16)

    outs = [
        sds((length, width), BF16), sds((length, 2 * three), BF16),
        sds((heads, length, length), BF16), sds((length, 2 * cols), BF16),
    ]
    args = [meta, x_or_mid]
    if level:
        args += [*parts, *norms]
        outs += [sds((length, width), BF16), sds((length, width), BF16), sds((length, 1), F32)]
    specs = [SM] + [VM] * (len(args) - 1) + [ANY] * 10 + [VM] * 3
    args += [*pieces, bias, seg_col, seg_row]
    return pl.pallas_call(
        body,
        out_shape=outs,
        in_specs=specs,
        out_specs=[VM] * len(outs),
        scratch_shapes=[pltpu.VMEM((2, width, four), BF16), pltpu.SemaphoreType.DMA((copies_of(pieces[5]),))],
        compiler_params=params(),
        cost_estimate=takes(13),
        name="attn_forward",
    )(*args)


def ffn_forward(meta, x, parts, gains, shifts, pieces, bias_in, half):
    units = 2 * half
    length, width = x.shape

    def body(meta, x, own, other, gain, shift, p0, p1, p2, p3, p4, p5, p6, p7, p8, p9, bias,
             part_out, mid_out, xhat_out, scale_out, act_out, slope_out, w_i, w_f, low, sems):
        first, second = load_b(meta, (p0, p1, p2, p3, p4, p5, p6, p7, p8, p9), w_i, w_f, sems)
        for rows in chunks(length):
            z = x[rows, :].astype(F32) + (own[rows, :].astype(F32) + other[rows, :].astype(F32)) + shift[0:1, :]
            xhat, scale = norm_rows(z)
            mid = xhat * gain[0:1, :] + shift[1:2, :]
            mid_out[rows, :] = mid
            low[rows, :] = mid.astype(BF16)
            xhat_out[rows, :] = xhat.astype(BF16)
            scale_out[rows, :] = scale
        wait_all(first)
        for rows in chunks(length, 256):
            for c in chunks(units, 512):
                pre = nn(low[rows, :], w_i[:, c]) + bias[:, c]
                act, slope = gelu_parts(pre)
                act_out[rows, c] = act.astype(BF16)
                slope_out[rows, c] = slope.astype(BF16)
        wait_all(second)
        for rows in chunks(length, 256):
            part_out[rows, :] = nt(act_out[rows, :], w_f[...]).astype(BF16)

    return pl.pallas_call(
        body,
        out_shape=[
            sds((length, width), BF16), sds((length, width), F32), sds((length, width), BF16),
            sds((length, 1), F32), sds((length, units), BF16), sds((length, units), BF16),
        ],
        in_specs=[SM] + [VM] * 5 + [ANY] * 10 + [VM],
        out_specs=[VM] * 6,
        scratch_shapes=[
            pltpu.VMEM((width, units), BF16), pltpu.VMEM((width, units), BF16),
            pltpu.VMEM((length, width), BF16), pltpu.SemaphoreType.DMA((copies_of(pieces[5]),)),
        ],
        compiler_params=params(),
        cost_estimate=takes(9),
        name="ffn_forward",
    )(meta, x, *parts, gains, shifts, *pieces, bias_in)


def last_norm(mid, parts, gains, shifts, tok_row, cls_pos):
    length, width = mid.shape
    n_cls = cls_pos.shape[0]

    def body(cls, mid, own, other, gain, shift, tok, y_out, xhat_out, scale_out, cls_out):
        for rows in chunks(length):
            z = mid[rows, :] + (own[rows, :].astype(F32) + other[rows, :].astype(F32)) + shift[2:3, :]
            xhat, scale = norm_rows(z)
            y_out[rows, :] = (xhat * gain[1:2, :] + shift[3:4, :]).astype(BF16)
            xhat_out[rows, :] = xhat.astype(BF16)
            scale_out[rows, :] = scale
        which = lax.broadcasted_iota(jnp.int32, (16, length), 0)
        hot = jnp.zeros((16, length), F32)
        for p in range(n_cls):
            hot = jnp.where(jnp.logical_and(which == p, tok[...] == cls[p]), 1.0, hot)
        cls_out[...] = nn(hot.astype(BF16), y_out[...])[:n_cls].astype(BF16)

    return pl.pallas_call(
        body,
        out_shape=[
            sds((length, width), BF16), sds((length, width), BF16), sds((length, 1), F32),
            sds((n_cls, width), BF16),
        ],
        in_specs=[SM] + [VM] * 6,
        out_specs=[VM] * 4,
        compiler_params=params(),
        cost_estimate=takes(2),
        name="last_norm",
    )(cls_pos, mid, *parts, gains, shifts, tok_row)


def ffn_backward(level, meta, sources, xhat, scale, gains, slope, pieces, half):
    units = 2 * half
    length, width = xhat.shape
    n_cls = sources[3].shape[0] if level else 0

    def body(meta, *refs):
        refs = list(refs)
        if level:
            cls, grad, d_cls, tok = (refs.pop(0) for _ in range(4))
        else:
            d_above, own, other = (refs.pop(0) for _ in range(3))
        xhat, scale, gain, slope = (refs.pop(0) for _ in range(4))
        pieces = [refs.pop(0) for _ in range(10)]
        part_out, second_out, low_out, pre_out, vec_out, inb_out, w_i, w_f, sems = refs
        first, second = load_b(meta, pieces, w_i, w_f, sems)
        sums = [jnp.zeros((1, width), F32) for _ in range(3)]
        for rows in chunks(length):
            if level:
                d_out = grad[rows, :].astype(F32)
                for p in range(n_cls):
                    d_out = d_out + jnp.where(tok[rows, :] == cls[p], 1.0, 0.0) * d_cls[p : p + 1, :]
            else:
                d_out = d_above[rows, :] + (own[rows, :].astype(F32) + other[rows, :].astype(F32))
                d_out = d_out.astype(BF16).astype(F32)
            hat = xhat[rows, :].astype(F32)
            d_second = norm_back_rows(d_out, gain[1:2, :], hat, scale[rows, :])
            second_out[rows, :] = d_second
            low_out[rows, :] = d_second.astype(BF16)
            for n, item in enumerate((d_out * hat, d_out, d_second)):
                sums[n] = sums[n] + jnp.sum(item, 0, keepdims=True)
        for n in range(3):
            vec_out[n : n + 1, :] = sums[n]
        wait_all(second)
        for n, rows in enumerate(chunks(length, 256)):
            for c in chunks(units, units // 4):
                d_act = nn(low_out[rows, :], w_f[:, c])
                d_pre = (slope[rows, c].astype(F32) * d_act).astype(BF16)
                pre_out[rows, c] = d_pre
                j, at = divmod(c.start, units // 2)
                at = slice(at, at + c.stop - c.start)
                total = jnp.sum(d_pre.astype(F32), 0, keepdims=True)
                inb_out[j : j + 1, at] = total if n == 0 else inb_out[j : j + 1, at] + total
        wait_all(first)
        for rows in chunks(length, 256):
            part_out[rows, :] = nt(pre_out[rows, :], w_i[...]).astype(BF16)

    if level:
        token_grad, d_cls, tok_col, cls_pos = sources
        args, specs = [meta, cls_pos, token_grad, d_cls, tok_col], [SM, SM, VM, VM, VM]
    else:
        args, specs = [meta, *sources], [SM, VM, VM, VM]
    args += [xhat, scale, gains, slope, *pieces]
    specs += [VM] * 4 + [ANY] * 10
    return pl.pallas_call(
        body,
        out_shape=[
            sds((length, width), BF16), sds((length, width), F32), sds((length, width), BF16),
            sds((length, units), BF16), sds((3, width), F32), sds((2, units // 2), F32),
        ],
        in_specs=specs,
        out_specs=[VM] * 6,
        scratch_shapes=[
            pltpu.VMEM((width, units), BF16), pltpu.VMEM((width, units), BF16),
            pltpu.SemaphoreType.DMA((copies_of(pieces[5]),)),
        ],
        compiler_params=params(),
        cost_estimate=takes(9),
        name="ffn_backward",
    )(*args)


def grads_of(nz, rz, width):
    half = nz // 2
    return [sds((nz, rz, width), BF16), sds((half, rz, width), BF16), sds((half, rz, width), BF16)]


def put_grad(outs, j, k, nz, column, value, first=0):
    half, (height, width) = nz // 2, value.shape
    if k < half:
        out, at = outs[0], k + (half if j == 0 else 0)
    else:
        out, at = outs[2 if j == 0 else 1], k - half
    out[at, first : first + height, column : column + width] = value.astype(BF16)


def ffn_grads(meta, mid, d_pre, d_ffn, act, nz):
    length, width = mid.shape
    units = d_pre.shape[1]
    one = units // 2
    rz = width // nz

    def body(meta, mid, d_pre, d_ffn, act, *refs):
        outs, (mid_t, ffn_t) = refs[:3], refs[3:]
        mid_t[...] = mid[...].T.astype(BF16)
        ffn_t[...] = d_ffn[...].astype(F32).T.astype(BF16)
        for j in range(2):
            c = slice(j * one, (j + 1) * one)
            for k in range(nz):
                rows = zrows(meta, k, rz)
                put_grad(outs, j, k, nz, 0, nn(mid_t[rows, :], d_pre[:, c]))
                put_grad(outs, j, k, nz, one, nn(ffn_t[rows, :], act[:, c]))

    return pl.pallas_call(
        body,
        out_shape=grads_of(nz, rz, units),
        in_specs=[SM] + [VM] * 4,
        out_specs=[VM] * 3,
        scratch_shapes=[pltpu.VMEM((width, length), BF16)] * 2,
        compiler_params=params(),
        cost_estimate=takes(7),
        name="ffn_grads",
    )(meta, mid, d_pre, d_ffn, act)


def attn_backward(meta, d_second, parts, xhat, scale, gains, qkv, probs, pieces, cols):
    four = 4 * cols
    length, width = d_second.shape
    three = 3 * cols
    heads = 2 * cols // HD

    def body(meta, d_second, own, other, xhat, scale, gain, qkv, probs, p0, p1, p2, p3, p4, p5, p6, p7, p8, p9,
             part_out, first_out, low_out, dqkv_out, vec_out, sum_out,
             w_a, d_ctx, acc_v, acc_k, sems):
        waits = load_a(meta, (p0, p1, p2, p3, p4, p5, p6, p7, p8, p9), w_a, sems)
        sums = [jnp.zeros((1, width), F32) for _ in range(3)]
        for rows in chunks(length):
            d_mid = d_second[rows, :] + (own[rows, :].astype(F32) + other[rows, :].astype(F32))
            hat = xhat[rows, :].astype(F32)
            d_first = norm_back_rows(d_mid, gain[0:1, :], hat, scale[rows, :])
            first_out[rows, :] = d_first
            low_out[rows, :] = d_first.astype(BF16)
            for n, item in enumerate((d_mid * hat, d_mid, d_first)):
                sums[n] = sums[n] + jnp.sum(item, 0, keepdims=True)
        for n in range(3):
            vec_out[n : n + 1, :] = sums[n]
        wait_all(waits)
        for j in range(2):
            for rows in chunks(length, 256):
                d_ctx[rows, j * cols : (j + 1) * cols] = nn(low_out[rows, :], w_a[j, :, three:]).astype(BF16)
        k_t = jnp.concatenate(
            [qkv[:, j * three + cols : j * three + 2 * cols].astype(F32) for j in range(2)], 1
        ).T.astype(BF16)
        for h in range(heads):
            j, i = divmod(h, cols // HD)
            at = j * three + i * HD
            q_cols, k_cols, v_cols = (slice(at + n * cols, at + n * cols + HD) for n in range(3))
            for n, queries in enumerate(chunks(length, 256)):
                d_o = d_ctx[queries, h * HD : (h + 1) * HD]
                d_p = nt(qkv[:, v_cols], d_o)
                p = probs[h, :, queries]
                wide = p.astype(F32)
                d_s = (wide * (d_p - jnp.sum(wide * d_p, 0, keepdims=True))).astype(BF16)
                d_v = nn(p, d_o)
                d_k = nn(d_s, qkv[queries, q_cols])
                acc_v[...] = d_v if n == 0 else acc_v[...] + d_v
                acc_k[...] = d_k if n == 0 else acc_k[...] + d_k
                d_q = nn(k_t[h * HD : (h + 1) * HD], d_s)
                dqkv_out[queries, q_cols] = (d_q.T * 0.125).astype(BF16)
            dqkv_out[:, v_cols] = acc_v[...].astype(BF16)
            dqkv_out[:, k_cols] = (acc_k[...] * 0.125).astype(BF16)
        for j in range(2):
            sum_out[j : j + 1, :] = jnp.sum(
                dqkv_out[:, j * three : (j + 1) * three].astype(F32), 0, keepdims=True
            )
        for rows in chunks(length, 256):
            part_out[rows, :] = (
                nt(dqkv_out[rows, :three], w_a[0, :, :three]) + nt(dqkv_out[rows, three:], w_a[1, :, :three])
            ).astype(BF16)

    return pl.pallas_call(
        body,
        out_shape=[
            sds((length, width), BF16), sds((length, width), F32), sds((length, width), BF16),
            sds((length, 2 * three), BF16), sds((3, width), F32), sds((2, three), F32),
        ],
        in_specs=[SM] + [VM] * 8 + [ANY] * 10,
        out_specs=[VM] * 6,
        scratch_shapes=[
            pltpu.VMEM((2, width, four), BF16), pltpu.VMEM((length, 2 * cols), BF16),
            pltpu.VMEM((length, HD), F32), pltpu.VMEM((length, HD), F32),
            pltpu.SemaphoreType.DMA((copies_of(pieces[5]),)),
        ],
        compiler_params=params(),
        cost_estimate=takes(15),
        name="attn_backward",
    )(meta, d_second, *parts, xhat, scale, gains, qkv, probs, *pieces)


def attn_grads(meta, places, x, d_attn, d_qkv, ctx, vectors, nz, extra):
    length, width = x.shape
    three = d_qkv.shape[1] // 2
    cols = ctx.shape[1] // 2
    rz = width // nz

    def body(meta, places, x, d_attn, d_qkv, ctx, vec1, vec2, sum_qkv, sum_inb, *refs):
        outs, (x_t, a_t, norm_rows_, qv_rows, inb_rows) = refs[:3], refs[3:]
        x_t[...] = x[...].astype(F32).T.astype(BF16)
        a_t[...] = d_attn[...].astype(F32).T.astype(BF16)
        for j in range(2):
            for k in range(nz):
                rows = zrows(meta, k, rz)
                grad = nn(x_t[rows, :], d_qkv[:, j * three : (j + 1) * three])
                put_grad(outs, j, k, nz, 0, grad)
                put_grad(outs, j, k, nz, three, nn(a_t[rows, :], ctx[:, j * cols : (j + 1) * cols]))
        if not extra:
            return
        piece, part = width // (4 * nz), cols // nz
        units = sum_inb.shape[1] // nz
        norm_rows_[...] = jnp.zeros_like(norm_rows_)
        norm_rows_[0:3, :] = vec1[...]
        norm_rows_[3:6, :] = vec2[...]
        for j in range(2):
            qv_rows[...] = jnp.zeros_like(qv_rows)
            qv_rows[0:1, :cols] = sum_qkv[j : j + 1, :cols]
            qv_rows[1:2, :cols] = sum_qkv[j : j + 1, 2 * cols : three]
            inb_rows[...] = jnp.zeros_like(inb_rows)
            inb_rows[0:1, :] = sum_inb[j : j + 1, :]
            for k in range(nz):
                d = places[2 + k]
                from_norm = pltpu.roll(norm_rows_[...], width - (d * 4 + places[j]) * piece, 1)
                from_qv = pltpu.roll(qv_rows[...], width - d * part, 1)
                from_inb = pltpu.roll(inb_rows[...], width - d * units, 1)
                lane = lax.broadcasted_iota(jnp.int32, (8, 2 * cols), 1)
                upper = jnp.where(lane < piece, from_norm[:, : 2 * cols], 0.0)
                lower = jnp.where(lane < part, from_qv[:, : 2 * cols], 0.0)
                shifted = pltpu.roll(from_inb, 128, 1)[:, : 2 * cols]
                inside = jnp.logical_and(lane >= 128, lane < 128 + units)
                lower = jnp.where(inside, shifted, lower)
                put_grad(outs, j, k, nz, 0, jnp.concatenate([upper, lower], 0), rz)
                put_grad(outs, j, k, nz, 2 * cols, jnp.zeros((extra, 2 * cols), F32), rz)

    return pl.pallas_call(
        body,
        out_shape=grads_of(nz, rz + extra, three + cols),
        in_specs=[SM, SM] + [VM] * 8,
        out_specs=[VM] * 3,
        scratch_shapes=[pltpu.VMEM((width, length), BF16)] * 2 + [pltpu.VMEM((8, width), F32)] * 3,
        compiler_params=params(),
        cost_estimate=takes(4),
        name="attn_grads",
    )(meta, places, x, d_attn, d_qkv, ctx, *vectors)


def loss_kernel(own, perm, slots, queries, positive_col, n_own):
    n_q, width = queries.shape
    n_p = slots.shape[0]

    def body(own, perm, slots, queries, pos, loss_out, d_out):
        passages = nn(perm[...], slots[...]).astype(BF16)
        logits = nt(queries[...], passages)
        top = jnp.max(logits, -1, keepdims=True)
        log_total = top + jnp.log(jnp.sum(jnp.exp(logits - top), -1, keepdims=True))
        index = lax.broadcasted_iota(jnp.int32, (n_q, n_p), 1)
        hits = pos[...] == index
        chosen = jnp.sum(jnp.where(hits, logits, 0.0), -1, keepdims=True)
        loss_out[...] = jnp.sum(log_total - chosen, 0, keepdims=True) / n_q
        d_logits = (16.0 * (jnp.exp(logits - log_total) - jnp.where(hits, 1.0, 0.0))).astype(BF16)
        pick = jnp.where(
            lax.broadcasted_iota(jnp.int32, (n_p, 128), 0)
            == lax.broadcasted_iota(jnp.int32, (n_p, 128), 1) + own[0],
            1.0, 0.0,
        ).astype(BF16)
        cols = nn(d_logits, pick)
        d_out[...] = nn(cols.T.astype(BF16), queries[...])[:n_own]

    return pl.pallas_call(
        body,
        out_shape=[sds((1, 1), F32), sds((n_own, width), F32)],
        in_specs=[SM] + [VM] * 4,
        out_specs=[VM] * 2,
        compiler_params=params(),
        cost_estimate=takes(1),
        name="contrast",
    )(own, perm, slots, queries, positive_col)


def on_device(
    inputs, cls_pos, w_qkv, qv_bias, w_out, w_in, in_bias, w_ffn_out,
    layer_gains, shifts, queries, positive, token_grad,
):
    core = lax.axis_index("section")
    dp = lax.axis_index("dp")
    me = lax.axis_index("tensor")
    n_dp = lax.axis_size("dp")
    n_t = lax.axis_size("tensor")
    first_core = core == 0
    rows_dev, share, width = inputs.shape
    cols = w_qkv.shape[3]
    units = w_in.shape[2]
    length = n_t * share
    n_chips = n_dp * n_t
    piece = width // n_chips
    order = dp_order()
    direct = direct_dp()
    nz, extra = (4, 16) if direct else (2, 0)
    t_ids = jnp.arange(n_t, dtype=jnp.int32)

    vec = jnp.concatenate(
        [layer_gains.reshape(-1), shifts.reshape(-1), qv_bias.reshape(-1), in_bias.reshape(-1)]
    )
    n_gain, n_shift, n_qv, n_inb = layer_gains.size, shifts.size, qv_bias.size, in_bias.size
    n_vec = vec.shape[0]
    flat = jnp.concatenate(
        [vec, queries.reshape(-1), (positive // 16).astype(BF16), (positive % 16).astype(BF16)]
    )
    flat = jnp.pad(flat, (0, -flat.shape[0] % 2048)).reshape(-1, 128)

    def spread_rows(block):
        blocks = [lax.dynamic_index_in_dim(block, me ^ k, 0, keepdims=False) for k in range(n_t)]
        return jnp.concatenate(exchange_rows(blocks), 0)

    pack = jnp.concatenate(
        [w_qkv[0, :, 0], w_qkv[0, :, 1], w_qkv[0, :, 2], w_out[0].T, w_in[0], w_ffn_out[0].T], 1
    )
    if direct:
        own = pack
        z_0 = rest_dp(pack, 0)
    else:
        pack = lax.all_gather(pack, "dp", axis=0, tiled=True)
        own, other_rows = pack[: width // 2], pack[width // 2 :][None]
    near0, far0 = gather_own(own)
    x_low = spread_rows(inputs)
    message = after(flat, near0)
    message = double(message, "dp") if direct else spread_dp(message)
    both0 = gather_own_both(near0, far0)
    owns = [own, near0, far0, *both0]
    rest_0 = jnp.stack(after(z_0, near0)) if direct else other_rows
    near_0 = gather_near(rest_0, 0)
    if direct:
        z_1 = rest_dp(after(pack, rest_0), 1)
    message = double(after(message, both0), "tensor")
    both_0 = gather_both(*near_0, 0)

    zrow = order * (width // n_dp) if direct else jnp.arange(2, dtype=jnp.int32) * (width // 2)
    metas = [
        jnp.concatenate([(core == level)[None].astype(jnp.int32), zrow.astype(jnp.int32)])
        for level in range(2)
    ]
    slots = [me ^ (2 * (core != level) + jnp.arange(2, dtype=jnp.int32)) for level in range(2)]
    places = [jnp.concatenate([s, order[:nz]]).astype(jnp.int32) for s in slots]
    hots = [(s[:, None] == t_ids[None, :]).astype(F32) for s in slots]

    positions = jnp.concatenate(
        [(me ^ k) * share + jnp.arange(share, dtype=jnp.int32) for k in range(n_t)]
    )
    cls_row = lax.dynamic_index_in_dim(cls_pos, me, 0, keepdims=False)
    segments = jnp.sum((positions[:, None] >= cls_row[None, :]).astype(jnp.int32), -1)
    seg_col, seg_row = segments[:, None], segments[None, :]
    tok_col, tok_row = positions[:, None], positions[None, :]

    slot_ids = (order[None, :] * n_t + (me ^ t_ids)[:, None]).reshape(-1)
    to_natural = (jnp.arange(n_chips, dtype=jnp.int32)[:, None] == slot_ids[None, :]).astype(BF16)
    table = nn(to_natural, message.reshape(n_chips, -1))
    own_table = table[:, :n_vec].astype(BF16)
    other_table = swap_cores(own_table)
    tables = jnp.where(
        first_core, jnp.stack([own_table, other_table]), jnp.stack([other_table, own_table])
    ).astype(F32)
    at = 0
    gains = tables[:, :, at : at + n_gain].reshape(2, n_chips, 2, piece).transpose(0, 2, 1, 3).reshape(2, 2, width)
    at += n_gain
    shift = tables[:, :, at : at + n_shift].reshape(2, n_chips, 4, piece).transpose(0, 2, 1, 3).reshape(2, 4, width)
    at += n_shift
    qv = tables[:, :, at : at + n_qv].reshape(2, n_dp, n_t, 2, cols // n_dp)
    qv = qv.transpose(0, 3, 2, 1, 4).reshape(2, 2, n_t, cols)
    at += n_qv
    inb = tables[:, :, at : at + n_inb].reshape(2, n_dp, n_t, n_inb).transpose(0, 2, 1, 3).reshape(2, n_t, units)
    vectors = []
    for level in range(2):
        bias = jnp.sum(hots[level][None, :, :, None] * qv[level][:, None], 2)
        bias = jnp.stack([bias[0], jnp.zeros_like(bias[0]), bias[1]], 1).reshape(1, -1)
        bias_in = jnp.sum(hots[level][:, :, None] * inb[level][None], 1).reshape(1, -1)
        vectors.append((gains[level], shift[level], bias, bias_in))
    at = n_vec
    q_dev = queries.shape[0]
    all_q = table[:, at : at + q_dev * width].reshape(-1, width).astype(BF16)
    at += q_dev * width
    all_pos = table[:, at : at + q_dev] * 16.0 + table[:, at + q_dev : at + 2 * q_dev]
    all_pos = all_pos.astype(jnp.int32).reshape(-1, 1)
    n_cls = cls_row.shape[0]
    perm = jnp.repeat(jnp.repeat(to_natural, n_cls, 0), n_cls, 1)
    perm = perm * jnp.tile(jnp.eye(n_cls, dtype=BF16), (n_chips, n_chips))

    vectors, all_q, all_pos, perm, x_low = lax.optimization_barrier(
        (vectors, all_q, all_pos, perm, x_low)
    )
    saved = []
    source, parts, norms = x_low, None, None
    rest_1 = jnp.stack(after(z_1, near_0)) if direct else other_rows
    near_1 = gather_near(after(rest_1, both_0), 1)
    pieces = [[*owns, rest_0, *near_0, *both_0], None]
    for level in range(2):
        gain, shift, bias, bias_in = vectors[level]
        outs = attn_forward(
            level, metas[level], source, parts, norms, pieces[level], bias, seg_col, seg_row, cols
        )
        part, qkv, probs, ctx = outs[:4]
        if level:
            x, xhat2, scale2 = outs[4:]
            saved[0]["second"] = (xhat2, scale2)
        else:
            x = x_low
        part, mid, xhat1, scale1, act, slope = ffn_forward(
            metas[level], x, (part, swap_cores(part)), gain, shift, pieces[level], bias_in, units
        )
        saved.append(
            dict(x=x, qkv=qkv, probs=probs, ctx=ctx, mid=mid, xhat1=xhat1, scale1=scale1, act=act, slope=slope)
        )
        source, parts, norms = mid, (part, swap_cores(part)), (gain, shift)
        if level == 0:
            near_1, part = lax.optimization_barrier((near_1, part))
            pieces[1] = [*owns, rest_1, *near_1, *gather_both(*near_1, 1)]
    y, xhat2, scale2, cls_own = last_norm(source, parts, *norms, tok_row, cls_row)
    saved[1]["second"] = (xhat2, scale2)
    tokens = spread_rows(after(token_grad, cls_own))

    cls_slots = spread_tensor(spread_dp(cls_own)).reshape(n_chips * n_cls, width)
    first_own = ((dp * n_t + me) * n_cls).astype(jnp.int32)[None]
    mean_loss, d_cls = loss_kernel(first_own, perm, cls_slots, all_q, all_pos, n_cls)

    vector_rows = [None, None]
    sources = (tokens, d_cls, tok_col, cls_row)
    sums_a, sums_b = [None, None], [None, None]
    for level in (1, 0):
        gain = vectors[level][0]
        kept = saved[level]
        meta = metas[level]
        xhat2, scale2 = kept["second"]
        if level == 0:
            sources = (after(sources[0], sums_b[1].first(grads_a[1])), *sources[1:])
        part, d_second, d_ffn, d_pre, vec2, sum_inb = ffn_backward(
            level, meta, sources, xhat2, scale2, gain, kept["slope"], pieces[level], units
        )
        other = swap_cores(part)
        if level == 0:
            d_ffn = after(d_ffn, sums_a[1].first(part))
        grads_b = ffn_grads(meta, kept["mid"], d_pre, d_ffn, kept["act"], nz)
        sums_b[level] = Reduction(grads_b, level)
        d_second = after(d_second, grads_b[1])
        if level == 0:
            d_second = after(d_second, sums_b[1].second(grads_b[1]))
        part, d_first, d_attn, d_qkv, vec1, sum_qkv = attn_backward(
            meta, d_second, (part, other), kept["xhat1"], kept["scale1"], gain,
            kept["qkv"], kept["probs"], pieces[level], cols,
        )
        other = swap_cores(part)
        if level == 0:
            d_attn = after(d_attn, sums_b[0].first(sums_a[1].second(part)))
        grads_a = attn_grads(
            meta, places[level], kept["x"], d_attn, d_qkv, kept["ctx"], (vec1, vec2, sum_qkv, sum_inb), nz, extra
        )
        sums_a[level] = Reduction(grads_a, level)
        vector_rows[level] = (vec1, vec2, sum_qkv, sum_inb)
        sources = (d_first, part, other)
    sums_b[1].third(grads_a[1])
    sums_b[0].second_direct(sums_b[1].pieces)
    sums_a[1].third(sums_b[0].sums)
    last_a1, last_b1 = last_dp([sums_a[1], sums_b[1]])
    sums_a[0].first(sums_a[1].pieces)
    sums_a[0].second_direct(sums_a[0].added)
    d_hidden = d_first + (part.astype(F32) + other.astype(F32))
    outgoing = jnp.where(first_core, d_hidden, y.astype(F32))
    low = after(outgoing.astype(BF16), sums_a[0].added).reshape(n_t, share, width)
    incoming = [outgoing[:share]] + [b.astype(F32) for b in exchange_rows([low[k] for k in range(n_t)])[1:]]
    boundary = jnp.zeros((n_t, share, width), F32)
    for k in range(n_t):
        boundary = lax.dynamic_update_index_in_dim(boundary, incoming[k], me ^ k, 0)
    tot_b, tot_a = (
        jnp.where(first_core, low, sum(p.astype(F32) for p in high))
        for low, high in ((sums_b[0].third_direct(), last_b1), (sums_a[0].third_direct(), last_a1))
    )
    if direct:
        end = width // n_dp
        own = tot_a[end : end + 6, :piece]
        qv = tot_a[end + 8 : end + 10, : qv_bias.shape[3]]
        grad_inb = tot_a[end + 8 : end + 9, 128 : 128 + n_inb]
        tot_a = tot_a[:end]
    else:
        tables = []
        for level in range(2):
            vec1, vec2, sum_qkv, sum_inb = vector_rows[level]
            by_t = lax.dot_general(
                hots[level], jnp.concatenate([sum_qkv, sum_inb], 1), (((0,), (0,)), ((), ())),
                precision=lax.Precision.HIGHEST,
            )
            whole = 0.5 * jnp.concatenate([vec1, vec2])
            whole = jnp.pad(whole, ((0, 0), (0, by_t.shape[1] - width)))
            tables.append(jnp.concatenate([whole, by_t]))
        tables = lax.psum(jnp.stack(tables), ("section", "dp", "tensor"))
        flat = jnp.where(first_core, tables[0], tables[1])
        own = lax.dynamic_slice_in_dim(flat[:6, :width], (dp * n_t + me) * piece, piece, 1)
        by_t = lax.dynamic_slice_in_dim(flat, 6 + me, 1, 0)
        qv = jnp.concatenate([by_t[:, :cols], by_t[:, 2 * cols : 3 * cols]])
        qv = lax.dynamic_slice_in_dim(qv, dp * qv_bias.shape[3], qv_bias.shape[3], 1)
        grad_inb = lax.dynamic_slice_in_dim(by_t[:, 3 * cols :], dp * n_inb, n_inb, 1)
    grad_gains = jnp.concatenate([own[0:1], own[3:4]]).reshape(layer_gains.shape)
    grad_shifts = jnp.concatenate([own[2:3], own[1:2], own[5:6], own[4:5]]).reshape(shifts.shape)
    grad_qv, grad_inb = qv.reshape(qv_bias.shape), grad_inb.reshape(in_bias.shape)

    grad_qkv = jnp.stack([tot_a[:, n * cols : (n + 1) * cols] for n in range(3)], 1)[None]
    grad_out = tot_a[:, 3 * cols :].T[None]
    grad_in = tot_b[:, :units][None]
    grad_ffn = tot_b[:, units:].T[None]
    return (
        grad_qkv, grad_qv, grad_out, grad_in, grad_inb, grad_ffn,
        grad_gains, grad_shifts, boundary[None], mean_loss.reshape(()),
    )


def solution(mesh):
    return jax.shard_map(
        on_device,
        mesh=mesh,
        in_specs=(
            P("dp", "tensor", None),
            P("dp", None),
            P("section", "dp", None, "tensor"),
            P("section", None, "tensor", "dp"),
            P("section", "tensor", "dp"),
            P("section", "dp", "tensor"),
            P("section", "tensor", "dp"),
            P("section", "tensor", "dp"),
            P("section", None, ("dp", "tensor")),
            P("section", None, ("dp", "tensor")),
            P(("dp", "tensor"), None),
            P(("dp", "tensor")),
            P("dp", "tensor", None),
        ),
        out_specs=(
            P("section", "dp", None, "tensor"),
            P("section", None, "tensor", "dp"),
            P("section", "tensor", "dp"),
            P("section", "dp", "tensor"),
            P("section", "tensor", "dp"),
            P("section", "tensor", "dp"),
            P("section", None, ("dp", "tensor")),
            P("section", None, ("dp", "tensor")),
            P("section", "dp", "tensor", None),
            P(),
        ),
        check_vma=False,
    )
```

```python
import jax
import jax.numpy as jnp
from jax import lax
from jax.experimental import pallas as pl
from jax.experimental.pallas import tpu as pltpu
from jax.sharding import PartitionSpec as P

HD = 64
PARTNER = 1
CROSS = 2
BF16 = jnp.bfloat16
F32 = jnp.float32


def mm(left, right, dims):
    return lax.dot_general(left, right, (dims, ((), ())), preferred_element_type=F32)


def nn(left, right):
    return mm(left, right, ((1,), (0,)))


def nt(left, right):
    return mm(left, right, ((1,), (1,)))


def after(block, *earlier):
    return lax.optimization_barrier((block, *earlier))[0]


def swap_cores(block):
    return lax.ppermute(block, "section", [(0, 1), (1, 0)])


def hop(block, axis, flip):
    return lax.ppermute(block, axis, [(i, i ^ flip) for i in range(lax.axis_size(axis))])


def core_hop(block, axis, flip, core):
    size = lax.axis_size(axis)
    route = [(core * size + i, core * size + (i ^ flip)) for i in range(size)]
    return lax.ppermute(block, ("section", axis), route)


def cross_hop(block, source):
    size = lax.axis_size("tensor")
    route = [(source * size + i, (1 - source) * size + (i ^ CROSS)) for i in range(size)]
    return lax.ppermute(block, ("section", "tensor"), route)


def direct_dp():
    return lax.axis_size("dp") == 4


def dp_order():
    size = lax.axis_size("dp")
    if direct_dp():
        return lax.axis_index("dp") ^ jnp.arange(size, dtype=jnp.int32)
    return jnp.arange(size, dtype=jnp.int32)


def spread_dp(block):
    if direct_dp():
        return jnp.stack([block] + [hop(block, "dp", k) for k in range(1, 4)])
    return lax.all_gather(block, "dp", axis=0, tiled=False)


def spread_tensor(block):
    return jnp.stack([block] + [hop(block, "tensor", k) for k in range(1, 4)])


def double(block, axis):
    pair = jnp.stack([block, hop(block, axis, 1)])
    return jnp.concatenate([pair, hop(pair, axis, 2)])


def exchange_rows(blocks):
    first = hop(jnp.stack([blocks[1], blocks[3]]), "tensor", 1)
    second = hop(jnp.stack([blocks[2], first[1]]), "tensor", 2)
    return [blocks[0], first[0], second[0], second[1]]


def cross_all(block):
    size = lax.axis_size("tensor")
    route = [(s * size + i, (1 - s) * size + (i ^ CROSS)) for s in range(2) for i in range(size)]
    return lax.ppermute(block, ("section", "tensor"), route)


def rest_dp(own, core):
    return [core_hop(own, "dp", k, core) for k in range(1, 4)]


def gather_own(own):
    near, far = hop(own, "tensor", PARTNER), cross_all(own)
    return near, far


def gather_own_both(near, far):
    half = near.shape[1] // 2
    return cross_all(near[:, :half]), hop(far[:, half:], "tensor", PARTNER)


def gather_near(rest, core):
    a, b = rest
    near_a, far_b = core_hop(a, "tensor", PARTNER, core), cross_hop(b, core)
    near_b, far_a = core_hop(b, "tensor", PARTNER, core), cross_hop(a, core)
    return near_a, near_b, far_a, far_b


def gather_both(near, core):
    return cross_hop(near[0], core), core_hop(near[3], "tensor", PARTNER, 1 - core)


def add_low(*items):
    total = items[0].astype(F32)
    for item in items[1:]:
        total = total + item.astype(F32)
    return total.astype(BF16)


class Reduction:
    def __init__(self, grads, core):
        self.core = core
        self.pair, self.next_b, self.own_b = grads
        self.got = cross_hop(self.pair, 1 - core)
        self.near_b = hop(self.next_b, "tensor", PARTNER)

    def first(self, *earlier):
        half = self.next_b.shape[0]
        self.parts = pair, own_b, got, near_b = after((self.pair, self.own_b, self.got, self.near_b), *earlier)
        self.added = add_low(pair[:half], got[:half]), add_low(own_b, near_b)
        self.near_a = core_hop(self.added[0], "tensor", PARTNER, self.core)
        self.far_b = cross_hop(self.added[1], 1 - self.core)
        return self.added

    def sum_halves(self, *earlier):
        half = self.next_b.shape[0]
        near_a, far_b, (pair, own_b, got, near_b) = after((self.near_a, self.far_b, self.parts), *earlier)
        return add_low(pair[half:], got[half:], near_a), add_low(own_b, near_b, far_b)

    def scatter(self):
        whole = jnp.concatenate(self.sums).reshape(-1, self.own_b.shape[2])
        return [lax.psum_scatter(whole, "dp", scatter_dimension=0, tiled=True)]

    def second_direct(self, *earlier):
        a, b = self.sums = self.sum_halves(*earlier)
        if direct_dp():
            self.hops = [
                core_hop(block, "dp", k, self.core) for k, block in ((1, a[1]), (2, b[0]), (3, b[1]))
            ]
        return self.sums

    def third_direct(self, *earlier):
        if not direct_dp():
            return sum(p.astype(F32) for p in self.scatter())
        return sum(p.astype(F32) for p in after([self.sums[0][0], *self.hops], *earlier))

    def second(self, *earlier):
        self.sums = self.sum_halves(*earlier)
        if direct_dp():
            self.across = core_hop(self.sums[1], "dp", 2, self.core)
        return self.sums

    def third(self, *earlier):
        if not direct_dp():
            self.pieces = self.scatter()
            return self.pieces
        a, across = after((self.sums[0], self.across), *earlier)
        self.pieces = [add_low(a[k], across[k]) for k in range(2)]
        return self.pieces


def last_dp(reductions, *earlier):
    if not direct_dp():
        return [r.pieces for r in reductions]
    high = max(r.pieces[0].shape[0] for r in reductions)
    block = [jnp.pad(r.pieces[1], ((0, high - r.pieces[1].shape[0]), (0, 0))) for r in reductions]
    got = core_hop(after(jnp.concatenate(block, 1), *earlier), "dp", 1, reductions[0].core)
    at, out = 0, []
    for r in reductions:
        rows, width = r.pieces[0].shape
        out.append([r.pieces[0], got[:rows, at : at + width]])
        at += width
    return out


VMEM_LIMIT = 48 * 1024 * 1024
CHUNK = 128


def takes(micros):
    return pl.CostEstimate(flops=int(micros * 1.1e9), bytes_accessed=0, transcendentals=0)


def params():
    return pltpu.CompilerParams(vmem_limit_bytes=VMEM_LIMIT)


ANY = pl.BlockSpec(memory_space=pl.ANY)
VM = pl.BlockSpec(memory_space=pltpu.VMEM)
SM = pl.BlockSpec(memory_space=pltpu.SMEM)


def sds(shape, dtype):
    return jax.ShapeDtypeStruct(shape, dtype)


def chunks(length, step=CHUNK):
    return [slice(i, i + step) for i in range(0, length, step)]


def norm_rows(z):
    centre = z - jnp.mean(z, -1, keepdims=True)
    spread = jnp.mean(centre * centre, -1, keepdims=True)
    scale = lax.rsqrt(spread + 1e-05)
    return centre * scale, scale


def norm_back_rows(d_out, gain, xhat, scale):
    g = d_out * gain
    m1 = jnp.mean(g, -1, keepdims=True)
    m2 = jnp.mean(g * xhat, -1, keepdims=True)
    return scale * (g - m1 - xhat * m2)


def gelu_parts(x):
    e = jnp.exp(-0.5 * x * x)
    t = 1.0 / (1.0 + 0.2316418882 * jnp.abs(x))
    poly = t * (
        0.127414796 + t * (-0.142248368 + t * (0.7107068705 + t * (-0.7265760135 + t * 0.5307027145)))
    )
    tail = poly * e
    cdf = jnp.where(x < 0.0, tail, 1.0 - tail)
    return x * cdf, cdf + x * e * 0.3989422804014327


def zrows(meta, k, rz):
    return pl.ds(pl.multiple_of(meta[1 + k], 64), rz)


def cut(start, width, at):
    if start < at < start + width:
        return [(start, at - start), (at, start + width - at)]
    return [(start, width)]


def load_weights(meta, pieces, base, places, sems):
    own, near0, far0, a0, b0, *halves = pieces
    rest, near, far, both = halves[0:2], halves[2:4], halves[4:6], halves[6:8]
    split, count = a0.shape[1], rest[0].shape[0]
    home = meta[0] == 1
    lists = [[] for _ in places]
    at = 0
    for j in range(2):
        for k in range(count + 1):
            rows = zrows(meta, k, own.shape[0])
            for n, (start, width, place) in enumerate(places):
                for g, w in cut(base + start, width, split):
                    side, column = divmod(g, split)
                    if k == 0:
                        mine = (near0 if j else own).at[:, pl.ds(g, w)]
                        other = (a0, b0)[side].at[:, pl.ds(column, w)] if j else far0.at[:, pl.ds(g, w)]
                    else:
                        mine, other = (
                            v[side].at[k - 1, :, pl.ds(column, w)] for v in ((near, both) if j else (rest, far))
                        )
                    dst = place(j, rows, g - base - start, w)
                    first = pltpu.make_async_copy(mine, dst, sems.at[at])
                    second = pltpu.make_async_copy(other, dst, sems.at[at])
                    at += 1

                    @pl.when(home)
                    def _():
                        first.start()

                    @pl.when(jnp.logical_not(home))
                    def _():
                        second.start()

                    lists[n].append(first)
    return lists


def copies_of(rest):
    return 2 * 3 * (1 + rest.shape[0])


def wait_all(waits):
    for made in waits:
        made.wait()


def load_a(meta, pieces, w_a, sems):
    width = w_a.shape[2]
    return load_weights(
        meta, pieces, 0, [(0, width, lambda j, rows, c, w: w_a.at[j, rows, pl.ds(c, w)])], sems
    )[0]


def load_b(meta, pieces, w_i, w_f, sems):
    one = w_i.shape[1] // 2
    base = pieces[0].shape[1] - 2 * one
    return load_weights(
        meta,
        pieces,
        base,
        [
            (0, one, lambda j, rows, c, w: w_i.at[rows, pl.ds(j * one + c, w)]),
            (one, one, lambda j, rows, c, w: w_f.at[rows, pl.ds(j * one + c, w)]),
        ],
        sems,
    )


def attn_forward(level, meta, x_or_mid, parts, norms, pieces, bias, seg_col, seg_row, cols):
    four = 4 * cols
    length, width = x_or_mid.shape
    three = 3 * cols
    heads = 2 * cols // HD

    def body(meta, *refs):
        refs = list(refs)
        src = refs.pop(0)
        if level:
            own, other, gain, shift = (refs.pop(0) for _ in range(4))
        pieces = [refs.pop(0) for _ in range(13)]
        bias, sc, sr = (refs.pop(0) for _ in range(3))
        part_out, qkv_out, probs_out, ctx_out = (refs.pop(0) for _ in range(4))
        if level:
            x_out, xhat_out, scale_out = (refs.pop(0) for _ in range(3))
        w_a, sems = refs
        waits = load_a(meta, pieces, w_a, sems)
        if level:
            for rows in chunks(length):
                z = src[rows, :] + (own[rows, :].astype(F32) + other[rows, :].astype(F32)) + shift[2:3, :]
                xhat, scale = norm_rows(z)
                x_out[rows, :] = (xhat * gain[1:2, :] + shift[3:4, :]).astype(BF16)
                xhat_out[rows, :] = xhat.astype(BF16)
                scale_out[rows, :] = scale
            x_ref = x_out
        else:
            x_ref = src
        wait_all(waits)
        for j in range(2):
            c = slice(j * three, (j + 1) * three)
            for rows in chunks(length, 256):
                qkv_out[rows, c] = (nn(x_ref[rows, :], w_a[j, :, :three]) + bias[:, c]).astype(BF16)
        v_t = jnp.concatenate(
            [qkv_out[:, j * three + 2 * cols : (j + 1) * three].astype(F32) for j in range(2)], 1
        ).T.astype(BF16)
        for queries in chunks(length, 256):
            same = sc[...] == sr[:, queries]
            outs = []
            for h in range(heads):
                j, i = divmod(h, cols // HD)
                at = j * three + i * HD
                q = qkv_out[queries, at : at + HD]
                k = qkv_out[:, at + cols : at + cols + HD]
                st = jnp.where(same, nt(k, q) * 0.125, -1e30)
                p = jnp.exp(st - jnp.max(st, 0, keepdims=True))
                p = (p * (1.0 / jnp.sum(p, 0, keepdims=True))).astype(BF16)
                probs_out[h, :, queries] = p
                outs.append(nn(v_t[h * HD : (h + 1) * HD], p))
            ctx = jnp.concatenate(outs, 0).T.astype(BF16)
            ctx_out[queries, :] = ctx
            part_out[queries, :] = (
                nt(ctx[:, :cols], w_a[0, :, three:]) + nt(ctx[:, cols:], w_a[1, :, three:])
            ).astype(BF16)

    outs = [
        sds((length, width), BF16), sds((length, 2 * three), BF16),
        sds((heads, length, length), BF16), sds((length, 2 * cols), BF16),
    ]
    args = [meta, x_or_mid]
    if level:
        args += [*parts, *norms]
        outs += [sds((length, width), BF16), sds((length, width), BF16), sds((length, 1), F32)]
    specs = [SM] + [VM] * (len(args) - 1) + [ANY] * 13 + [VM] * 3
    args += [*pieces, bias, seg_col, seg_row]
    return pl.pallas_call(
        body,
        out_shape=outs,
        in_specs=specs,
        out_specs=[VM] * len(outs),
        scratch_shapes=[pltpu.VMEM((2, width, four), BF16), pltpu.SemaphoreType.DMA((copies_of(pieces[5]),))],
        compiler_params=params(),
        cost_estimate=takes(13),
        name="attn_forward",
    )(*args)


def ffn_forward(meta, x, parts, gains, shifts, pieces, bias_in, half):
    units = 2 * half
    length, width = x.shape

    def body(meta, x, own, other, gain, shift, p0, p1, p2, p3, p4, p5, p6, p7, p8, p9, p10, p11, p12, bias,
             part_out, mid_out, xhat_out, scale_out, act_out, slope_out, w_i, w_f, low, sems):
        first, second = load_b(meta, (p0, p1, p2, p3, p4, p5, p6, p7, p8, p9, p10, p11, p12), w_i, w_f, sems)
        for rows in chunks(length):
            z = x[rows, :].astype(F32) + (own[rows, :].astype(F32) + other[rows, :].astype(F32)) + shift[0:1, :]
            xhat, scale = norm_rows(z)
            mid = xhat * gain[0:1, :] + shift[1:2, :]
            mid_out[rows, :] = mid
            low[rows, :] = mid.astype(BF16)
            xhat_out[rows, :] = xhat.astype(BF16)
            scale_out[rows, :] = scale
        wait_all(first)
        for rows in chunks(length, 256):
            for c in chunks(units, 512):
                pre = nn(low[rows, :], w_i[:, c]) + bias[:, c]
                act, slope = gelu_parts(pre)
                act_out[rows, c] = act.astype(BF16)
                slope_out[rows, c] = slope.astype(BF16)
        wait_all(second)
        for rows in chunks(length, 256):
            part_out[rows, :] = nt(act_out[rows, :], w_f[...]).astype(BF16)

    return pl.pallas_call(
        body,
        out_shape=[
            sds((length, width), BF16), sds((length, width), F32), sds((length, width), BF16),
            sds((length, 1), F32), sds((length, units), BF16), sds((length, units), BF16),
        ],
        in_specs=[SM] + [VM] * 5 + [ANY] * 13 + [VM],
        out_specs=[VM] * 6,
        scratch_shapes=[
            pltpu.VMEM((width, units), BF16), pltpu.VMEM((width, units), BF16),
            pltpu.VMEM((length, width), BF16), pltpu.SemaphoreType.DMA((copies_of(pieces[5]),)),
        ],
        compiler_params=params(),
        cost_estimate=takes(9),
        name="ffn_forward",
    )(meta, x, *parts, gains, shifts, *pieces, bias_in)


def last_norm(mid, parts, gains, shifts, tok_row, cls_pos):
    length, width = mid.shape
    n_cls = cls_pos.shape[0]

    def body(cls, mid, own, other, gain, shift, tok, y_out, xhat_out, scale_out, cls_out):
        for rows in chunks(length):
            z = mid[rows, :] + (own[rows, :].astype(F32) + other[rows, :].astype(F32)) + shift[2:3, :]
            xhat, scale = norm_rows(z)
            y_out[rows, :] = (xhat * gain[1:2, :] + shift[3:4, :]).astype(BF16)
            xhat_out[rows, :] = xhat.astype(BF16)
            scale_out[rows, :] = scale
        which = lax.broadcasted_iota(jnp.int32, (16, length), 0)
        hot = jnp.zeros((16, length), F32)
        for p in range(n_cls):
            hot = jnp.where(jnp.logical_and(which == p, tok[...] == cls[p]), 1.0, hot)
        cls_out[...] = nn(hot.astype(BF16), y_out[...])[:n_cls].astype(BF16)

    return pl.pallas_call(
        body,
        out_shape=[
            sds((length, width), BF16), sds((length, width), BF16), sds((length, 1), F32),
            sds((n_cls, width), BF16),
        ],
        in_specs=[SM] + [VM] * 6,
        out_specs=[VM] * 4,
        compiler_params=params(),
        cost_estimate=takes(2),
        name="last_norm",
    )(cls_pos, mid, *parts, gains, shifts, tok_row)


def ffn_backward(level, meta, sources, xhat, scale, gains, slope, pieces, half):
    units = 2 * half
    length, width = xhat.shape
    n_cls = sources[3].shape[0] if level else 0

    def body(meta, *refs):
        refs = list(refs)
        if level:
            cls, grad, d_cls, tok = (refs.pop(0) for _ in range(4))
        else:
            d_above, own, other = (refs.pop(0) for _ in range(3))
        xhat, scale, gain, slope = (refs.pop(0) for _ in range(4))
        pieces = [refs.pop(0) for _ in range(13)]
        part_out, second_out, low_out, pre_out, vec_out, inb_out, w_i, w_f, sems = refs
        first, second = load_b(meta, pieces, w_i, w_f, sems)
        sums = [jnp.zeros((1, width), F32) for _ in range(3)]
        for rows in chunks(length):
            if level:
                d_out = grad[rows, :].astype(F32)
                for p in range(n_cls):
                    d_out = d_out + jnp.where(tok[rows, :] == cls[p], 1.0, 0.0) * d_cls[p : p + 1, :]
            else:
                d_out = d_above[rows, :] + (own[rows, :].astype(F32) + other[rows, :].astype(F32))
                d_out = d_out.astype(BF16).astype(F32)
            hat = xhat[rows, :].astype(F32)
            d_second = norm_back_rows(d_out, gain[1:2, :], hat, scale[rows, :])
            second_out[rows, :] = d_second
            low_out[rows, :] = d_second.astype(BF16)
            for n, item in enumerate((d_out * hat, d_out, d_second)):
                sums[n] = sums[n] + jnp.sum(item, 0, keepdims=True)
        for n in range(3):
            vec_out[n : n + 1, :] = sums[n]
        wait_all(second)
        for n, rows in enumerate(chunks(length, 256)):
            for c in chunks(units, units // 4):
                d_act = nn(low_out[rows, :], w_f[:, c])
                d_pre = (slope[rows, c].astype(F32) * d_act).astype(BF16)
                pre_out[rows, c] = d_pre
                j, at = divmod(c.start, units // 2)
                at = slice(at, at + c.stop - c.start)
                total = jnp.sum(d_pre.astype(F32), 0, keepdims=True)
                inb_out[j : j + 1, at] = total if n == 0 else inb_out[j : j + 1, at] + total
        wait_all(first)
        for rows in chunks(length, 256):
            part_out[rows, :] = nt(pre_out[rows, :], w_i[...]).astype(BF16)

    if level:
        token_grad, d_cls, tok_col, cls_pos = sources
        args, specs = [meta, cls_pos, token_grad, d_cls, tok_col], [SM, SM, VM, VM, VM]
    else:
        args, specs = [meta, *sources], [SM, VM, VM, VM]
    args += [xhat, scale, gains, slope, *pieces]
    specs += [VM] * 4 + [ANY] * 13
    return pl.pallas_call(
        body,
        out_shape=[
            sds((length, width), BF16), sds((length, width), F32), sds((length, width), BF16),
            sds((length, units), BF16), sds((3, width), F32), sds((2, units // 2), F32),
        ],
        in_specs=specs,
        out_specs=[VM] * 6,
        scratch_shapes=[
            pltpu.VMEM((width, units), BF16), pltpu.VMEM((width, units), BF16),
            pltpu.SemaphoreType.DMA((copies_of(pieces[5]),)),
        ],
        compiler_params=params(),
        cost_estimate=takes(9),
        name="ffn_backward",
    )(*args)


def grads_of(nz, rz, width):
    half = nz // 2
    return [sds((nz, rz, width), BF16), sds((half, rz, width), BF16), sds((half, rz, width), BF16)]


def put_grad(outs, j, k, nz, column, value, first=0):
    half, (height, width) = nz // 2, value.shape
    if k < half:
        out, at = outs[0], k + (half if j == 0 else 0)
    else:
        out, at = outs[2 if j == 0 else 1], k - half
    out[at, first : first + height, column : column + width] = value.astype(BF16)


def ffn_grads(meta, mid, d_pre, d_ffn, act, nz):
    length, width = mid.shape
    units = d_pre.shape[1]
    one = units // 2
    rz = width // nz

    def body(meta, mid, d_pre, d_ffn, act, *refs):
        outs, (mid_t, ffn_t) = refs[:3], refs[3:]
        mid_t[...] = mid[...].T.astype(BF16)
        ffn_t[...] = d_ffn[...].astype(F32).T.astype(BF16)
        for j in range(2):
            c = slice(j * one, (j + 1) * one)
            for k in range(nz):
                rows = zrows(meta, k, rz)
                put_grad(outs, j, k, nz, 0, nn(mid_t[rows, :], d_pre[:, c]))
                put_grad(outs, j, k, nz, one, nn(ffn_t[rows, :], act[:, c]))

    return pl.pallas_call(
        body,
        out_shape=grads_of(nz, rz, units),
        in_specs=[SM] + [VM] * 4,
        out_specs=[VM] * 3,
        scratch_shapes=[pltpu.VMEM((width, length), BF16)] * 2,
        compiler_params=params(),
        cost_estimate=takes(7),
        name="ffn_grads",
    )(meta, mid, d_pre, d_ffn, act)


def attn_backward(meta, d_second, parts, xhat, scale, gains, qkv, probs, pieces, cols):
    four = 4 * cols
    length, width = d_second.shape
    three = 3 * cols
    heads = 2 * cols // HD

    def body(meta, d_second, own, other, xhat, scale, gain, qkv, probs, p0, p1, p2, p3, p4, p5, p6, p7, p8, p9, p10, p11, p12,
             part_out, first_out, low_out, dqkv_out, vec_out, sum_out,
             w_a, d_ctx, acc_v, acc_k, sems):
        waits = load_a(meta, (p0, p1, p2, p3, p4, p5, p6, p7, p8, p9, p10, p11, p12), w_a, sems)
        sums = [jnp.zeros((1, width), F32) for _ in range(3)]
        for rows in chunks(length):
            d_mid = d_second[rows, :] + (own[rows, :].astype(F32) + other[rows, :].astype(F32))
            hat = xhat[rows, :].astype(F32)
            d_first = norm_back_rows(d_mid, gain[0:1, :], hat, scale[rows, :])
            first_out[rows, :] = d_first
            low_out[rows, :] = d_first.astype(BF16)
            for n, item in enumerate((d_mid * hat, d_mid, d_first)):
                sums[n] = sums[n] + jnp.sum(item, 0, keepdims=True)
        for n in range(3):
            vec_out[n : n + 1, :] = sums[n]
        wait_all(waits)
        for j in range(2):
            for rows in chunks(length, 256):
                d_ctx[rows, j * cols : (j + 1) * cols] = nn(low_out[rows, :], w_a[j, :, three:]).astype(BF16)
        k_t = jnp.concatenate(
            [qkv[:, j * three + cols : j * three + 2 * cols].astype(F32) for j in range(2)], 1
        ).T.astype(BF16)
        for h in range(heads):
            j, i = divmod(h, cols // HD)
            at = j * three + i * HD
            q_cols, k_cols, v_cols = (slice(at + n * cols, at + n * cols + HD) for n in range(3))
            for n, queries in enumerate(chunks(length, 256)):
                d_o = d_ctx[queries, h * HD : (h + 1) * HD]
                d_p = nt(qkv[:, v_cols], d_o)
                p = probs[h, :, queries]
                wide = p.astype(F32)
                d_s = (wide * (d_p - jnp.sum(wide * d_p, 0, keepdims=True))).astype(BF16)
                d_v = nn(p, d_o)
                d_k = nn(d_s, qkv[queries, q_cols])
                acc_v[...] = d_v if n == 0 else acc_v[...] + d_v
                acc_k[...] = d_k if n == 0 else acc_k[...] + d_k
                d_q = nn(k_t[h * HD : (h + 1) * HD], d_s)
                dqkv_out[queries, q_cols] = (d_q.T * 0.125).astype(BF16)
            dqkv_out[:, v_cols] = acc_v[...].astype(BF16)
            dqkv_out[:, k_cols] = (acc_k[...] * 0.125).astype(BF16)
        for j in range(2):
            sum_out[j : j + 1, :] = jnp.sum(
                dqkv_out[:, j * three : (j + 1) * three].astype(F32), 0, keepdims=True
            )
        for rows in chunks(length, 256):
            part_out[rows, :] = (
                nt(dqkv_out[rows, :three], w_a[0, :, :three]) + nt(dqkv_out[rows, three:], w_a[1, :, :three])
            ).astype(BF16)

    return pl.pallas_call(
        body,
        out_shape=[
            sds((length, width), BF16), sds((length, width), F32), sds((length, width), BF16),
            sds((length, 2 * three), BF16), sds((3, width), F32), sds((2, three), F32),
        ],
        in_specs=[SM] + [VM] * 8 + [ANY] * 13,
        out_specs=[VM] * 6,
        scratch_shapes=[
            pltpu.VMEM((2, width, four), BF16), pltpu.VMEM((length, 2 * cols), BF16),
            pltpu.VMEM((length, HD), F32), pltpu.VMEM((length, HD), F32),
            pltpu.SemaphoreType.DMA((copies_of(pieces[5]),)),
        ],
        compiler_params=params(),
        cost_estimate=takes(15),
        name="attn_backward",
    )(meta, d_second, *parts, xhat, scale, gains, qkv, probs, *pieces)


def attn_grads(meta, places, x, d_attn, d_qkv, ctx, vectors, nz, extra):
    length, width = x.shape
    three = d_qkv.shape[1] // 2
    cols = ctx.shape[1] // 2
    rz = width // nz

    def body(meta, places, x, d_attn, d_qkv, ctx, vec1, vec2, sum_qkv, sum_inb, *refs):
        outs, (x_t, a_t, norm_rows_, qv_rows, inb_rows) = refs[:3], refs[3:]
        x_t[...] = x[...].astype(F32).T.astype(BF16)
        a_t[...] = d_attn[...].astype(F32).T.astype(BF16)
        for j in range(2):
            for k in range(nz):
                rows = zrows(meta, k, rz)
                grad = nn(x_t[rows, :], d_qkv[:, j * three : (j + 1) * three])
                put_grad(outs, j, k, nz, 0, grad)
                put_grad(outs, j, k, nz, three, nn(a_t[rows, :], ctx[:, j * cols : (j + 1) * cols]))
        if not extra:
            return
        piece, part = width // (4 * nz), cols // nz
        units = sum_inb.shape[1] // nz
        norm_rows_[...] = jnp.zeros_like(norm_rows_)
        norm_rows_[0:3, :] = vec1[...]
        norm_rows_[3:6, :] = vec2[...]
        for j in range(2):
            qv_rows[...] = jnp.zeros_like(qv_rows)
            qv_rows[0:1, :cols] = sum_qkv[j : j + 1, :cols]
            qv_rows[1:2, :cols] = sum_qkv[j : j + 1, 2 * cols : three]
            inb_rows[...] = jnp.zeros_like(inb_rows)
            inb_rows[0:1, :] = sum_inb[j : j + 1, :]
            for k in range(nz):
                d = places[2 + k]
                from_norm = pltpu.roll(norm_rows_[...], width - (d * 4 + places[j]) * piece, 1)
                from_qv = pltpu.roll(qv_rows[...], width - d * part, 1)
                from_inb = pltpu.roll(inb_rows[...], width - d * units, 1)
                lane = lax.broadcasted_iota(jnp.int32, (8, 2 * cols), 1)
                upper = jnp.where(lane < piece, from_norm[:, : 2 * cols], 0.0)
                lower = jnp.where(lane < part, from_qv[:, : 2 * cols], 0.0)
                shifted = pltpu.roll(from_inb, 128, 1)[:, : 2 * cols]
                inside = jnp.logical_and(lane >= 128, lane < 128 + units)
                lower = jnp.where(inside, shifted, lower)
                put_grad(outs, j, k, nz, 0, jnp.concatenate([upper, lower], 0), rz)
                put_grad(outs, j, k, nz, 2 * cols, jnp.zeros((extra, 2 * cols), F32), rz)

    return pl.pallas_call(
        body,
        out_shape=grads_of(nz, rz + extra, three + cols),
        in_specs=[SM, SM] + [VM] * 8,
        out_specs=[VM] * 3,
        scratch_shapes=[pltpu.VMEM((width, length), BF16)] * 2 + [pltpu.VMEM((8, width), F32)] * 3,
        compiler_params=params(),
        cost_estimate=takes(4),
        name="attn_grads",
    )(meta, places, x, d_attn, d_qkv, ctx, *vectors)


def loss_kernel(own, perm, slots, queries, positive_col, n_own):
    n_q, width = queries.shape
    n_p = slots.shape[0]

    def body(own, perm, slots, queries, pos, loss_out, d_out):
        passages = nn(perm[...], slots[...]).astype(BF16)
        logits = nt(queries[...], passages)
        top = jnp.max(logits, -1, keepdims=True)
        log_total = top + jnp.log(jnp.sum(jnp.exp(logits - top), -1, keepdims=True))
        index = lax.broadcasted_iota(jnp.int32, (n_q, n_p), 1)
        hits = pos[...] == index
        chosen = jnp.sum(jnp.where(hits, logits, 0.0), -1, keepdims=True)
        loss_out[...] = jnp.sum(log_total - chosen, 0, keepdims=True) / n_q
        d_logits = (16.0 * (jnp.exp(logits - log_total) - jnp.where(hits, 1.0, 0.0))).astype(BF16)
        pick = jnp.where(
            lax.broadcasted_iota(jnp.int32, (n_p, 128), 0)
            == lax.broadcasted_iota(jnp.int32, (n_p, 128), 1) + own[0],
            1.0, 0.0,
        ).astype(BF16)
        cols = nn(d_logits, pick)
        d_out[...] = nn(cols.T.astype(BF16), queries[...])[:n_own]

    return pl.pallas_call(
        body,
        out_shape=[sds((1, 1), F32), sds((n_own, width), F32)],
        in_specs=[SM] + [VM] * 4,
        out_specs=[VM] * 2,
        compiler_params=params(),
        cost_estimate=takes(1),
        name="contrast",
    )(own, perm, slots, queries, positive_col)


def on_device(
    inputs, cls_pos, w_qkv, qv_bias, w_out, w_in, in_bias, w_ffn_out,
    layer_gains, shifts, queries, positive, token_grad,
):
    core = lax.axis_index("section")
    dp = lax.axis_index("dp")
    me = lax.axis_index("tensor")
    n_dp = lax.axis_size("dp")
    n_t = lax.axis_size("tensor")
    first_core = core == 0
    rows_dev, share, width = inputs.shape
    cols = w_qkv.shape[3]
    units = w_in.shape[2]
    length = n_t * share
    n_chips = n_dp * n_t
    piece = width // n_chips
    order = dp_order()
    direct = direct_dp()
    nz, extra = (4, 16) if direct else (2, 0)
    t_ids = jnp.arange(n_t, dtype=jnp.int32)

    vec = jnp.concatenate(
        [layer_gains.reshape(-1), shifts.reshape(-1), qv_bias.reshape(-1), in_bias.reshape(-1)]
    )
    n_gain, n_shift, n_qv, n_inb = layer_gains.size, shifts.size, qv_bias.size, in_bias.size
    n_vec = vec.shape[0]
    flat = jnp.concatenate(
        [vec, queries.reshape(-1), (positive // 16).astype(BF16), (positive % 16).astype(BF16)]
    )
    flat = jnp.pad(flat, (0, -flat.shape[0] % 2048)).reshape(-1, 128)

    def spread_rows(block):
        blocks = [lax.dynamic_index_in_dim(block, me ^ k, 0, keepdims=False) for k in range(n_t)]
        return jnp.concatenate(exchange_rows(blocks), 0)

    pack = jnp.concatenate(
        [w_qkv[0, :, 0], w_qkv[0, :, 1], w_qkv[0, :, 2], w_out[0].T, w_in[0], w_ffn_out[0].T], 1
    )
    if direct:
        own = pack
        z_0 = rest_dp(pack, 0)
    else:
        pack = lax.all_gather(pack, "dp", axis=0, tiled=True)
        own, other_rows = pack[: width // 2], pack[width // 2 :][None]
    near0, far0 = gather_own(own)
    both0 = gather_own_both(near0, far0)
    owns = [own, near0, far0, *both0]
    half = pack.shape[1] // 2

    def halves_of(blocks, *earlier):
        if not direct:
            return other_rows[:, :, :half], other_rows[:, :, half:]
        blocks = after(blocks, *earlier)
        return jnp.stack([b[:, :half] for b in blocks]), jnp.stack([b[:, half:] for b in blocks])

    rest_0 = halves_of(z_0 if direct else None, near0)
    near_0 = gather_near(rest_0, 0)
    message = after(flat, rest_0)
    message = double(message, "dp") if direct else spread_dp(message)
    if direct:
        z_1 = rest_dp(after(pack, message), 1)
    rows_in = spread_rows(after(jnp.where(first_core, inputs, token_grad), near_0[0]))
    rows_got = swap_cores(rows_in)
    x_low = jnp.where(first_core, rows_in, rows_got)
    tokens = jnp.where(first_core, rows_got, rows_in)
    both_0 = gather_both(near_0, 0)
    message = double(after(message, near_0), "tensor")

    zrow = order * (width // n_dp) if direct else jnp.arange(2, dtype=jnp.int32) * (width // 2)
    metas = [
        jnp.concatenate([(core == level)[None].astype(jnp.int32), zrow.astype(jnp.int32)])
        for level in range(2)
    ]
    slots = [me ^ (2 * (core != level) + jnp.arange(2, dtype=jnp.int32)) for level in range(2)]
    places = [jnp.concatenate([s, order[:nz]]).astype(jnp.int32) for s in slots]
    hots = [(s[:, None] == t_ids[None, :]).astype(F32) for s in slots]

    positions = jnp.concatenate(
        [(me ^ k) * share + jnp.arange(share, dtype=jnp.int32) for k in range(n_t)]
    )
    cls_row = lax.dynamic_index_in_dim(cls_pos, me, 0, keepdims=False)
    segments = jnp.sum((positions[:, None] >= cls_row[None, :]).astype(jnp.int32), -1)
    seg_col, seg_row = segments[:, None], segments[None, :]
    tok_col, tok_row = positions[:, None], positions[None, :]

    slot_ids = (order[None, :] * n_t + (me ^ t_ids)[:, None]).reshape(-1)
    to_natural = (jnp.arange(n_chips, dtype=jnp.int32)[:, None] == slot_ids[None, :]).astype(BF16)
    table = nn(to_natural, message.reshape(n_chips, -1))
    own_table = table[:, :n_vec].astype(BF16)
    other_table = swap_cores(own_table)
    tables = jnp.where(
        first_core, jnp.stack([own_table, other_table]), jnp.stack([other_table, own_table])
    ).astype(F32)
    at = 0
    gains = tables[:, :, at : at + n_gain].reshape(2, n_chips, 2, piece).transpose(0, 2, 1, 3).reshape(2, 2, width)
    at += n_gain
    shift = tables[:, :, at : at + n_shift].reshape(2, n_chips, 4, piece).transpose(0, 2, 1, 3).reshape(2, 4, width)
    at += n_shift
    qv = tables[:, :, at : at + n_qv].reshape(2, n_dp, n_t, 2, cols // n_dp)
    qv = qv.transpose(0, 3, 2, 1, 4).reshape(2, 2, n_t, cols)
    at += n_qv
    inb = tables[:, :, at : at + n_inb].reshape(2, n_dp, n_t, n_inb).transpose(0, 2, 1, 3).reshape(2, n_t, units)
    vectors = []
    for level in range(2):
        bias = jnp.sum(hots[level][None, :, :, None] * qv[level][:, None], 2)
        bias = jnp.stack([bias[0], jnp.zeros_like(bias[0]), bias[1]], 1).reshape(1, -1)
        bias_in = jnp.sum(hots[level][:, :, None] * inb[level][None], 1).reshape(1, -1)
        vectors.append((gains[level], shift[level], bias, bias_in))
    at = n_vec
    q_dev = queries.shape[0]
    all_q = table[:, at : at + q_dev * width].reshape(-1, width).astype(BF16)
    at += q_dev * width
    all_pos = table[:, at : at + q_dev] * 16.0 + table[:, at + q_dev : at + 2 * q_dev]
    all_pos = all_pos.astype(jnp.int32).reshape(-1, 1)
    n_cls = cls_row.shape[0]
    perm = jnp.repeat(jnp.repeat(to_natural, n_cls, 0), n_cls, 1)
    perm = perm * jnp.tile(jnp.eye(n_cls, dtype=BF16), (n_chips, n_chips))

    vectors, all_q, all_pos, perm, x_low = lax.optimization_barrier(
        (vectors, all_q, all_pos, perm, x_low)
    )
    saved = []
    source, parts, norms = x_low, None, None
    rest_1 = halves_of(z_1 if direct else None, near_0)
    near_1 = gather_near(after(rest_1, both_0), 1)
    pieces = [[*owns, *rest_0, *near_0, *both_0], None]
    for level in range(2):
        gain, shift, bias, bias_in = vectors[level]
        outs = attn_forward(
            level, metas[level], source, parts, norms, pieces[level], bias, seg_col, seg_row, cols
        )
        part, qkv, probs, ctx = outs[:4]
        if level:
            x, xhat2, scale2 = outs[4:]
            saved[0]["second"] = (xhat2, scale2)
        else:
            x = x_low
        part, mid, xhat1, scale1, act, slope = ffn_forward(
            metas[level], x, (part, swap_cores(part)), gain, shift, pieces[level], bias_in, units
        )
        saved.append(
            dict(x=x, qkv=qkv, probs=probs, ctx=ctx, mid=mid, xhat1=xhat1, scale1=scale1, act=act, slope=slope)
        )
        source, parts, norms = mid, (part, swap_cores(part)), (gain, shift)
        if level == 0:
            pieces[1] = [*owns, *rest_1, *near_1, *gather_both(near_1, 1)]
    y, xhat2, scale2, cls_own = last_norm(source, parts, *norms, tok_row, cls_row)
    saved[1]["second"] = (xhat2, scale2)

    cls_slots = spread_tensor(spread_dp(cls_own)).reshape(n_chips * n_cls, width)
    first_own = ((dp * n_t + me) * n_cls).astype(jnp.int32)[None]
    mean_loss, d_cls = loss_kernel(first_own, perm, cls_slots, all_q, all_pos, n_cls)

    vector_rows = [None, None]
    sources = (tokens, d_cls, tok_col, cls_row)
    sums_a, sums_b = [None, None], [None, None]
    for level in (1, 0):
        gain = vectors[level][0]
        kept = saved[level]
        meta = metas[level]
        xhat2, scale2 = kept["second"]
        if level == 0:
            sources = (after(sources[0], sums_b[1].first(grads_a[1])), *sources[1:])
        part, d_second, d_ffn, d_pre, vec2, sum_inb = ffn_backward(
            level, meta, sources, xhat2, scale2, gain, kept["slope"], pieces[level], units
        )
        other = swap_cores(part)
        if level == 0:
            d_ffn = after(d_ffn, sums_a[1].first(part))
        grads_b = ffn_grads(meta, kept["mid"], d_pre, d_ffn, kept["act"], nz)
        sums_b[level] = Reduction(grads_b, level)
        d_second = after(d_second, grads_b[1])
        if level == 0:
            d_second = after(d_second, sums_b[1].second(grads_b[1]))
        part, d_first, d_attn, d_qkv, vec1, sum_qkv = attn_backward(
            meta, d_second, (part, other), kept["xhat1"], kept["scale1"], gain,
            kept["qkv"], kept["probs"], pieces[level], cols,
        )
        other = swap_cores(part)
        if level == 0:
            d_attn = after(d_attn, sums_b[0].first(sums_a[1].second(part)))
        grads_a = attn_grads(
            meta, places[level], kept["x"], d_attn, d_qkv, kept["ctx"], (vec1, vec2, sum_qkv, sum_inb), nz, extra
        )
        sums_a[level] = Reduction(grads_a, level)
        vector_rows[level] = (vec1, vec2, sum_qkv, sum_inb)
        sources = (d_first, part, other)
    sums_b[1].third(grads_a[1])
    sums_b[0].second_direct(sums_b[1].pieces)
    sums_a[1].third(sums_b[0].sums)
    last_a1, last_b1 = last_dp([sums_a[1], sums_b[1]])
    sums_a[0].first(sums_a[1].pieces)
    sums_a[0].second_direct(sums_a[0].added)
    total_b0 = sums_b[0].third_direct(sums_a[0].sums)
    d_hidden = d_first + (part.astype(F32) + other.astype(F32))
    outgoing = jnp.where(first_core, d_hidden, y.astype(F32))
    low = after(outgoing.astype(BF16), total_b0).reshape(n_t, share, width)
    incoming = [outgoing[:share]] + [b.astype(F32) for b in exchange_rows([low[k] for k in range(n_t)])[1:]]
    boundary = jnp.zeros((n_t, share, width), F32)
    for k in range(n_t):
        boundary = lax.dynamic_update_index_in_dim(boundary, incoming[k], me ^ k, 0)
    tot_b, tot_a = (
        jnp.where(first_core, low, sum(p.astype(F32) for p in high))
        for low, high in ((total_b0, last_b1), (sums_a[0].third_direct(), last_a1))
    )
    if direct:
        end = width // n_dp
        own = tot_a[end : end + 6, :piece]
        qv = tot_a[end + 8 : end + 10, : qv_bias.shape[3]]
        grad_inb = tot_a[end + 8 : end + 9, 128 : 128 + n_inb]
        tot_a = tot_a[:end]
    else:
        tables = []
        for level in range(2):
            vec1, vec2, sum_qkv, sum_inb = vector_rows[level]
            by_t = lax.dot_general(
                hots[level], jnp.concatenate([sum_qkv, sum_inb], 1), (((0,), (0,)), ((), ())),
                precision=lax.Precision.HIGHEST,
            )
            whole = 0.5 * jnp.concatenate([vec1, vec2])
            whole = jnp.pad(whole, ((0, 0), (0, by_t.shape[1] - width)))
            tables.append(jnp.concatenate([whole, by_t]))
        tables = lax.psum(jnp.stack(tables), ("section", "dp", "tensor"))
        flat = jnp.where(first_core, tables[0], tables[1])
        own = lax.dynamic_slice_in_dim(flat[:6, :width], (dp * n_t + me) * piece, piece, 1)
        by_t = lax.dynamic_slice_in_dim(flat, 6 + me, 1, 0)
        qv = jnp.concatenate([by_t[:, :cols], by_t[:, 2 * cols : 3 * cols]])
        qv = lax.dynamic_slice_in_dim(qv, dp * qv_bias.shape[3], qv_bias.shape[3], 1)
        grad_inb = lax.dynamic_slice_in_dim(by_t[:, 3 * cols :], dp * n_inb, n_inb, 1)
    grad_gains = jnp.concatenate([own[0:1], own[3:4]]).reshape(layer_gains.shape)
    grad_shifts = jnp.concatenate([own[2:3], own[1:2], own[5:6], own[4:5]]).reshape(shifts.shape)
    grad_qv, grad_inb = qv.reshape(qv_bias.shape), grad_inb.reshape(in_bias.shape)

    grad_qkv = jnp.stack([tot_a[:, n * cols : (n + 1) * cols] for n in range(3)], 1)[None]
    grad_out = tot_a[:, 3 * cols :].T[None]
    grad_in = tot_b[:, :units][None]
    grad_ffn = tot_b[:, units:].T[None]
    return (
        grad_qkv, grad_qv, grad_out, grad_in, grad_inb, grad_ffn,
        grad_gains, grad_shifts, boundary[None], mean_loss.reshape(()),
    )


def solution(mesh):
    return jax.shard_map(
        on_device,
        mesh=mesh,
        in_specs=(
            P("dp", "tensor", None),
            P("dp", None),
            P("section", "dp", None, "tensor"),
            P("section", None, "tensor", "dp"),
            P("section", "tensor", "dp"),
            P("section", "dp", "tensor"),
            P("section", "tensor", "dp"),
            P("section", "tensor", "dp"),
            P("section", None, ("dp", "tensor")),
            P("section", None, ("dp", "tensor")),
            P(("dp", "tensor"), None),
            P(("dp", "tensor")),
            P("dp", "tensor", None),
        ),
        out_specs=(
            P("section", "dp", None, "tensor"),
            P("section", None, "tensor", "dp"),
            P("section", "tensor", "dp"),
            P("section", "dp", "tensor"),
            P("section", "tensor", "dp"),
            P("section", "tensor", "dp"),
            P("section", None, ("dp", "tensor")),
            P("section", None, ("dp", "tensor")),
            P("section", "dp", "tensor", None),
            P(),
        ),
        check_vma=False,
    )
```

```python
import jax
import jax.numpy as jnp
from jax import lax
from jax.experimental import pallas as pl
from jax.experimental.pallas import tpu as pltpu
from jax.sharding import PartitionSpec as P

HD = 64
PARTNER = 1
CROSS = 2
BF16 = jnp.bfloat16
F32 = jnp.float32


def mm(left, right, dims):
    return lax.dot_general(left, right, (dims, ((), ())), preferred_element_type=F32)


def nn(left, right):
    return mm(left, right, ((1,), (0,)))


def nt(left, right):
    return mm(left, right, ((1,), (1,)))


def after(block, *earlier):
    return lax.optimization_barrier((block, *earlier))[0]


def swap_cores(block):
    return lax.ppermute(block, "section", [(0, 1), (1, 0)])


def hop(block, axis, flip):
    return lax.ppermute(block, axis, [(i, i ^ flip) for i in range(lax.axis_size(axis))])


def core_hop(block, axis, flip, core):
    size = lax.axis_size(axis)
    route = [(core * size + i, core * size + (i ^ flip)) for i in range(size)]
    return lax.ppermute(block, ("section", axis), route)


def cross_hop(block, source):
    size = lax.axis_size("tensor")
    route = [(source * size + i, (1 - source) * size + (i ^ CROSS)) for i in range(size)]
    return lax.ppermute(block, ("section", "tensor"), route)


def direct_dp():
    return lax.axis_size("dp") == 4


def dp_order():
    size = lax.axis_size("dp")
    if direct_dp():
        return lax.axis_index("dp") ^ jnp.arange(size, dtype=jnp.int32)
    return jnp.arange(size, dtype=jnp.int32)


def spread_dp(block):
    if direct_dp():
        return jnp.stack([block] + [hop(block, "dp", k) for k in range(1, 4)])
    return lax.all_gather(block, "dp", axis=0, tiled=False)


def spread_tensor(block):
    return jnp.stack([block] + [hop(block, "tensor", k) for k in range(1, 4)])


def double(block, axis):
    pair = jnp.stack([block, hop(block, axis, 1)])
    return jnp.concatenate([pair, hop(pair, axis, 2)])


def exchange_rows(blocks):
    first = hop(jnp.stack([blocks[1], blocks[3]]), "tensor", 1)
    second = hop(jnp.stack([blocks[2], first[1]]), "tensor", 2)
    return [blocks[0], first[0], second[0], second[1]]


def cross_all(block):
    size = lax.axis_size("tensor")
    route = [(s * size + i, (1 - s) * size + (i ^ CROSS)) for s in range(2) for i in range(size)]
    return lax.ppermute(block, ("section", "tensor"), route)


def rest_dp(own, core):
    return [core_hop(own, "dp", k, core) for k in range(1, 4)]


def gather_own(own):
    near, far = hop(own, "tensor", PARTNER), cross_all(own)
    return near, far


def gather_own_both(near, far):
    half = near.shape[1] // 2
    return cross_all(near[:, :half]), hop(far[:, half:], "tensor", PARTNER)


def gather_near(rest, core):
    a, b = rest
    near_a, far_b = core_hop(a, "tensor", PARTNER, core), cross_hop(b, core)
    near_b, far_a = core_hop(b, "tensor", PARTNER, core), cross_hop(a, core)
    return near_a, near_b, far_a, far_b


def gather_both(near, core):
    return cross_hop(near[0], core), core_hop(near[3], "tensor", PARTNER, 1 - core)


def add_low(*items):
    total = items[0].astype(F32)
    for item in items[1:]:
        total = total + item.astype(F32)
    return total.astype(BF16)


class Reduction:
    def __init__(self, grads, core):
        self.core = core
        self.pair, self.next_b, self.own_b = grads
        self.got = cross_hop(self.pair, 1 - core)
        self.near_b = hop(self.next_b, "tensor", PARTNER)

    def first(self, *earlier):
        half = self.next_b.shape[0]
        self.parts = pair, own_b, got, near_b = after((self.pair, self.own_b, self.got, self.near_b), *earlier)
        self.added = add_low(pair[:half], got[:half]), add_low(own_b, near_b)
        self.near_a = core_hop(self.added[0], "tensor", PARTNER, self.core)
        self.far_b = cross_hop(self.added[1], 1 - self.core)
        return self.added

    def sum_halves(self, *earlier):
        half = self.next_b.shape[0]
        near_a, far_b, (pair, own_b, got, near_b) = after((self.near_a, self.far_b, self.parts), *earlier)
        return add_low(pair[half:], got[half:], near_a), add_low(own_b, near_b, far_b)

    def scatter(self):
        whole = jnp.concatenate(self.sums).reshape(-1, self.own_b.shape[2])
        return [lax.psum_scatter(whole, "dp", scatter_dimension=0, tiled=True)]

    def second_direct(self, *earlier):
        a, b = self.sums = self.sum_halves(*earlier)
        if direct_dp():
            self.hops = [
                core_hop(block, "dp", k, self.core) for k, block in ((1, a[1]), (2, b[0]), (3, b[1]))
            ]
        return self.sums

    def third_direct(self, *earlier):
        if not direct_dp():
            return sum(p.astype(F32) for p in self.scatter())
        return sum(p.astype(F32) for p in after([self.sums[0][0], *self.hops], *earlier))

    def second(self, *earlier):
        self.sums = self.sum_halves(*earlier)
        if direct_dp():
            self.across = core_hop(self.sums[1], "dp", 2, self.core)
        return self.sums

    def third(self, *earlier):
        if not direct_dp():
            self.pieces = self.scatter()
            return self.pieces
        a, across = after((self.sums[0], self.across), *earlier)
        self.pieces = [add_low(a[k], across[k]) for k in range(2)]
        return self.pieces


def last_dp(reductions, *earlier):
    if not direct_dp():
        return [r.pieces for r in reductions]
    high = max(r.pieces[0].shape[0] for r in reductions)
    block = [jnp.pad(r.pieces[1], ((0, high - r.pieces[1].shape[0]), (0, 0))) for r in reductions]
    got = core_hop(after(jnp.concatenate(block, 1), *earlier), "dp", 1, reductions[0].core)
    at, out = 0, []
    for r in reductions:
        rows, width = r.pieces[0].shape
        out.append([r.pieces[0], got[:rows, at : at + width]])
        at += width
    return out


VMEM_LIMIT = 48 * 1024 * 1024
CHUNK = 128


def takes(micros):
    return pl.CostEstimate(flops=int(micros * 1.1e9), bytes_accessed=0, transcendentals=0)


def params():
    return pltpu.CompilerParams(vmem_limit_bytes=VMEM_LIMIT)


ANY = pl.BlockSpec(memory_space=pl.ANY)
VM = pl.BlockSpec(memory_space=pltpu.VMEM)
SM = pl.BlockSpec(memory_space=pltpu.SMEM)


def sds(shape, dtype):
    return jax.ShapeDtypeStruct(shape, dtype)


def chunks(length, step=CHUNK):
    return [slice(i, i + step) for i in range(0, length, step)]


def norm_rows(z):
    centre = z - jnp.mean(z, -1, keepdims=True)
    spread = jnp.mean(centre * centre, -1, keepdims=True)
    scale = lax.rsqrt(spread + 1e-05)
    return centre * scale, scale


def norm_back_rows(d_out, gain, xhat, scale):
    g = d_out * gain
    m1 = jnp.mean(g, -1, keepdims=True)
    m2 = jnp.mean(g * xhat, -1, keepdims=True)
    return scale * (g - m1 - xhat * m2)


def gelu_parts(x):
    e = jnp.exp(-0.5 * x * x)
    t = 1.0 / (1.0 + 0.2316418882 * jnp.abs(x))
    poly = t * (
        0.127414796 + t * (-0.142248368 + t * (0.7107068705 + t * (-0.7265760135 + t * 0.5307027145)))
    )
    tail = poly * e
    cdf = jnp.where(x < 0.0, tail, 1.0 - tail)
    return x * cdf, cdf + x * e * 0.3989422804014327


def zrows(meta, k, rz):
    return pl.ds(pl.multiple_of(meta[1 + k], 64), rz)


def cut(start, width, at):
    if start < at < start + width:
        return [(start, at - start), (at, start + width - at)]
    return [(start, width)]


def load_weights(meta, pieces, base, places, sems):
    own, near0, far0, a0, b0, *halves = pieces
    rest, near, far, both = halves[0:2], halves[2:4], halves[4:6], halves[6:8]
    split, count = a0.shape[1], rest[0].shape[0]
    home = meta[0] == 1
    lists = [[] for _ in places]
    at = 0
    for j in range(2):
        for k in range(count + 1):
            rows = zrows(meta, k, own.shape[0])
            for n, (start, width, place) in enumerate(places):
                for g, w in cut(base + start, width, split):
                    side, column = divmod(g, split)
                    if k == 0:
                        mine = (near0 if j else own).at[:, pl.ds(g, w)]
                        other = (a0, b0)[side].at[:, pl.ds(column, w)] if j else far0.at[:, pl.ds(g, w)]
                    else:
                        mine, other = (
                            v[side].at[k - 1, :, pl.ds(column, w)] for v in ((near, both) if j else (rest, far))
                        )
                    dst = place(j, rows, g - base - start, w)
                    first = pltpu.make_async_copy(mine, dst, sems.at[at])
                    second = pltpu.make_async_copy(other, dst, sems.at[at])
                    at += 1

                    @pl.when(home)
                    def _():
                        first.start()

                    @pl.when(jnp.logical_not(home))
                    def _():
                        second.start()

                    lists[n].append(first)
    return lists


def copies_of(rest):
    return 2 * 3 * (1 + rest.shape[0])


def wait_all(waits):
    for made in waits:
        made.wait()


def load_a(meta, pieces, w_a, sems):
    width = w_a.shape[2]
    return load_weights(
        meta, pieces, 0, [(0, width, lambda j, rows, c, w: w_a.at[j, rows, pl.ds(c, w)])], sems
    )[0]


def load_b(meta, pieces, w_i, w_f, sems):
    one = w_i.shape[1] // 2
    base = pieces[0].shape[1] - 2 * one
    return load_weights(
        meta,
        pieces,
        base,
        [
            (0, one, lambda j, rows, c, w: w_i.at[rows, pl.ds(j * one + c, w)]),
            (one, one, lambda j, rows, c, w: w_f.at[rows, pl.ds(j * one + c, w)]),
        ],
        sems,
    )


def attn_forward(level, meta, x_or_mid, parts, norms, pieces, bias, seg_col, seg_row, cols):
    four = 4 * cols
    length, width = x_or_mid.shape
    three = 3 * cols
    heads = 2 * cols // HD

    def body(meta, *refs):
        refs = list(refs)
        src = refs.pop(0)
        if level:
            own, other, gain, shift = (refs.pop(0) for _ in range(4))
        pieces = [refs.pop(0) for _ in range(13)]
        bias, sc, sr = (refs.pop(0) for _ in range(3))
        part_out, qkv_out, probs_out, ctx_out = (refs.pop(0) for _ in range(4))
        if level:
            x_out, xhat_out, scale_out = (refs.pop(0) for _ in range(3))
        w_a, sems = refs
        waits = load_a(meta, pieces, w_a, sems)
        if level:
            for rows in chunks(length):
                z = src[rows, :] + (own[rows, :].astype(F32) + other[rows, :].astype(F32)) + shift[2:3, :]
                xhat, scale = norm_rows(z)
                x_out[rows, :] = (xhat * gain[1:2, :] + shift[3:4, :]).astype(BF16)
                xhat_out[rows, :] = xhat.astype(BF16)
                scale_out[rows, :] = scale
            x_ref = x_out
        else:
            x_ref = src
        wait_all(waits)
        for j in range(2):
            c = slice(j * three, (j + 1) * three)
            for rows in chunks(length, 256):
                qkv_out[rows, c] = (nn(x_ref[rows, :], w_a[j, :, :three]) + bias[:, c]).astype(BF16)
        v_t = jnp.concatenate(
            [qkv_out[:, j * three + 2 * cols : (j + 1) * three].astype(F32) for j in range(2)], 1
        ).T.astype(BF16)
        for queries in chunks(length, 256):
            same = sc[...] == sr[:, queries]
            outs = []
            for h in range(heads):
                j, i = divmod(h, cols // HD)
                at = j * three + i * HD
                q = qkv_out[queries, at : at + HD]
                k = qkv_out[:, at + cols : at + cols + HD]
                st = jnp.where(same, nt(k, q) * 0.125, -1e30)
                p = jnp.exp(st - jnp.max(st, 0, keepdims=True))
                p = (p * (1.0 / jnp.sum(p, 0, keepdims=True))).astype(BF16)
                probs_out[h, :, queries] = p
                outs.append(nn(v_t[h * HD : (h + 1) * HD], p))
            ctx = jnp.concatenate(outs, 0).T.astype(BF16)
            ctx_out[queries, :] = ctx
            part_out[queries, :] = (
                nt(ctx[:, :cols], w_a[0, :, three:]) + nt(ctx[:, cols:], w_a[1, :, three:])
            ).astype(BF16)

    outs = [
        sds((length, width), BF16), sds((length, 2 * three), BF16),
        sds((heads, length, length), BF16), sds((length, 2 * cols), BF16),
    ]
    args = [meta, x_or_mid]
    if level:
        args += [*parts, *norms]
        outs += [sds((length, width), BF16), sds((length, width), BF16), sds((length, 1), F32)]
    specs = [SM] + [VM] * (len(args) - 1) + [ANY] * 13 + [VM] * 3
    args += [*pieces, bias, seg_col, seg_row]
    return pl.pallas_call(
        body,
        out_shape=outs,
        in_specs=specs,
        out_specs=[VM] * len(outs),
        scratch_shapes=[pltpu.VMEM((2, width, four), BF16), pltpu.SemaphoreType.DMA((copies_of(pieces[5]),))],
        compiler_params=params(),
        cost_estimate=takes(13),
        name="attn_forward",
    )(*args)


def ffn_forward(meta, x, parts, gains, shifts, pieces, bias_in, half):
    units = 2 * half
    length, width = x.shape

    def body(meta, x, own, other, gain, shift, p0, p1, p2, p3, p4, p5, p6, p7, p8, p9, p10, p11, p12, bias,
             part_out, mid_out, xhat_out, scale_out, act_out, slope_out, w_i, w_f, low, sems):
        first, second = load_b(meta, (p0, p1, p2, p3, p4, p5, p6, p7, p8, p9, p10, p11, p12), w_i, w_f, sems)
        for rows in chunks(length):
            z = x[rows, :].astype(F32) + (own[rows, :].astype(F32) + other[rows, :].astype(F32)) + shift[0:1, :]
            xhat, scale = norm_rows(z)
            mid = xhat * gain[0:1, :] + shift[1:2, :]
            mid_out[rows, :] = mid
            low[rows, :] = mid.astype(BF16)
            xhat_out[rows, :] = xhat.astype(BF16)
            scale_out[rows, :] = scale
        wait_all(first)
        for rows in chunks(length, 256):
            for c in chunks(units, 512):
                pre = nn(low[rows, :], w_i[:, c]) + bias[:, c]
                act, slope = gelu_parts(pre)
                act_out[rows, c] = act.astype(BF16)
                slope_out[rows, c] = slope.astype(BF16)
        wait_all(second)
        for rows in chunks(length, 256):
            part_out[rows, :] = nt(act_out[rows, :], w_f[...]).astype(BF16)

    return pl.pallas_call(
        body,
        out_shape=[
            sds((length, width), BF16), sds((length, width), F32), sds((length, width), BF16),
            sds((length, 1), F32), sds((length, units), BF16), sds((length, units), BF16),
        ],
        in_specs=[SM] + [VM] * 5 + [ANY] * 13 + [VM],
        out_specs=[VM] * 6,
        scratch_shapes=[
            pltpu.VMEM((width, units), BF16), pltpu.VMEM((width, units), BF16),
            pltpu.VMEM((length, width), BF16), pltpu.SemaphoreType.DMA((copies_of(pieces[5]),)),
        ],
        compiler_params=params(),
        cost_estimate=takes(9),
        name="ffn_forward",
    )(meta, x, *parts, gains, shifts, *pieces, bias_in)


def last_norm(mid, parts, gains, shifts, tok_row, cls_pos):
    length, width = mid.shape
    n_cls = cls_pos.shape[0]

    def body(cls, mid, own, other, gain, shift, tok, y_out, xhat_out, scale_out, cls_out):
        for rows in chunks(length):
            z = mid[rows, :] + (own[rows, :].astype(F32) + other[rows, :].astype(F32)) + shift[2:3, :]
            xhat, scale = norm_rows(z)
            y_out[rows, :] = (xhat * gain[1:2, :] + shift[3:4, :]).astype(BF16)
            xhat_out[rows, :] = xhat.astype(BF16)
            scale_out[rows, :] = scale
        which = lax.broadcasted_iota(jnp.int32, (16, length), 0)
        hot = jnp.zeros((16, length), F32)
        for p in range(n_cls):
            hot = jnp.where(jnp.logical_and(which == p, tok[...] == cls[p]), 1.0, hot)
        cls_out[...] = nn(hot.astype(BF16), y_out[...])[:n_cls].astype(BF16)

    return pl.pallas_call(
        body,
        out_shape=[
            sds((length, width), BF16), sds((length, width), BF16), sds((length, 1), F32),
            sds((n_cls, width), BF16),
        ],
        in_specs=[SM] + [VM] * 6,
        out_specs=[VM] * 4,
        compiler_params=params(),
        cost_estimate=takes(2),
        name="last_norm",
    )(cls_pos, mid, *parts, gains, shifts, tok_row)


def ffn_backward(level, meta, sources, xhat, scale, gains, slope, pieces, half):
    units = 2 * half
    length, width = xhat.shape
    n_cls = sources[3].shape[0] if level else 0

    def body(meta, *refs):
        refs = list(refs)
        if level:
            cls, grad, d_cls, tok = (refs.pop(0) for _ in range(4))
        else:
            d_above, own, other = (refs.pop(0) for _ in range(3))
        xhat, scale, gain, slope = (refs.pop(0) for _ in range(4))
        pieces = [refs.pop(0) for _ in range(13)]
        part_out, second_out, low_out, pre_out, vec_out, inb_out, w_i, w_f, sems = refs
        first, second = load_b(meta, pieces, w_i, w_f, sems)
        sums = [jnp.zeros((1, width), F32) for _ in range(3)]
        for rows in chunks(length):
            if level:
                d_out = grad[rows, :].astype(F32)
                for p in range(n_cls):
                    d_out = d_out + jnp.where(tok[rows, :] == cls[p], 1.0, 0.0) * d_cls[p : p + 1, :]
            else:
                d_out = d_above[rows, :] + (own[rows, :].astype(F32) + other[rows, :].astype(F32))
                d_out = d_out.astype(BF16).astype(F32)
            hat = xhat[rows, :].astype(F32)
            d_second = norm_back_rows(d_out, gain[1:2, :], hat, scale[rows, :])
            second_out[rows, :] = d_second
            low_out[rows, :] = d_second.astype(BF16)
            for n, item in enumerate((d_out * hat, d_out, d_second)):
                sums[n] = sums[n] + jnp.sum(item, 0, keepdims=True)
        for n in range(3):
            vec_out[n : n + 1, :] = sums[n]
        wait_all(second)
        for n, rows in enumerate(chunks(length, 256)):
            for c in chunks(units, units // 4):
                d_act = nn(low_out[rows, :], w_f[:, c])
                d_pre = (slope[rows, c].astype(F32) * d_act).astype(BF16)
                pre_out[rows, c] = d_pre
                j, at = divmod(c.start, units // 2)
                at = slice(at, at + c.stop - c.start)
                total = jnp.sum(d_pre.astype(F32), 0, keepdims=True)
                inb_out[j : j + 1, at] = total if n == 0 else inb_out[j : j + 1, at] + total
        wait_all(first)
        for rows in chunks(length, 256):
            part_out[rows, :] = nt(pre_out[rows, :], w_i[...]).astype(BF16)

    if level:
        token_grad, d_cls, tok_col, cls_pos = sources
        args, specs = [meta, cls_pos, token_grad, d_cls, tok_col], [SM, SM, VM, VM, VM]
    else:
        args, specs = [meta, *sources], [SM, VM, VM, VM]
    args += [xhat, scale, gains, slope, *pieces]
    specs += [VM] * 4 + [ANY] * 13
    return pl.pallas_call(
        body,
        out_shape=[
            sds((length, width), BF16), sds((length, width), F32), sds((length, width), BF16),
            sds((length, units), BF16), sds((3, width), F32), sds((2, units // 2), F32),
        ],
        in_specs=specs,
        out_specs=[VM] * 6,
        scratch_shapes=[
            pltpu.VMEM((width, units), BF16), pltpu.VMEM((width, units), BF16),
            pltpu.SemaphoreType.DMA((copies_of(pieces[5]),)),
        ],
        compiler_params=params(),
        cost_estimate=takes(9),
        name="ffn_backward",
    )(*args)


def grads_of(nz, rz, width):
    half = nz // 2
    return [sds((nz, rz, width), BF16), sds((half, rz, width), BF16), sds((half, rz, width), BF16)]


def put_grad(outs, j, k, nz, column, value, first=0):
    half, (height, width) = nz // 2, value.shape
    if k < half:
        out, at = outs[0], k + (half if j == 0 else 0)
    else:
        out, at = outs[2 if j == 0 else 1], k - half
    out[at, first : first + height, column : column + width] = value.astype(BF16)


def ffn_grads(meta, mid, d_pre, d_ffn, act, nz):
    length, width = mid.shape
    units = d_pre.shape[1]
    one = units // 2
    rz = width // nz

    def body(meta, mid, d_pre, d_ffn, act, *refs):
        outs, (mid_t, ffn_t) = refs[:3], refs[3:]
        mid_t[...] = mid[...].T.astype(BF16)
        ffn_t[...] = d_ffn[...].astype(F32).T.astype(BF16)
        for j in range(2):
            c = slice(j * one, (j + 1) * one)
            for k in range(nz):
                rows = zrows(meta, k, rz)
                put_grad(outs, j, k, nz, 0, nn(mid_t[rows, :], d_pre[:, c]))
                put_grad(outs, j, k, nz, one, nn(ffn_t[rows, :], act[:, c]))

    return pl.pallas_call(
        body,
        out_shape=grads_of(nz, rz, units),
        in_specs=[SM] + [VM] * 4,
        out_specs=[VM] * 3,
        scratch_shapes=[pltpu.VMEM((width, length), BF16)] * 2,
        compiler_params=params(),
        cost_estimate=takes(7),
        name="ffn_grads",
    )(meta, mid, d_pre, d_ffn, act)


def attn_backward(meta, d_second, parts, xhat, scale, gains, qkv, probs, pieces, cols):
    four = 4 * cols
    length, width = d_second.shape
    three = 3 * cols
    heads = 2 * cols // HD

    def body(meta, d_second, own, other, xhat, scale, gain, qkv, probs, p0, p1, p2, p3, p4, p5, p6, p7, p8, p9, p10, p11, p12,
             part_out, first_out, low_out, dqkv_out, vec_out, sum_out,
             w_a, d_ctx, acc_v, acc_k, sems):
        waits = load_a(meta, (p0, p1, p2, p3, p4, p5, p6, p7, p8, p9, p10, p11, p12), w_a, sems)
        sums = [jnp.zeros((1, width), F32) for _ in range(3)]
        for rows in chunks(length):
            d_mid = d_second[rows, :] + (own[rows, :].astype(F32) + other[rows, :].astype(F32))
            hat = xhat[rows, :].astype(F32)
            d_first = norm_back_rows(d_mid, gain[0:1, :], hat, scale[rows, :])
            first_out[rows, :] = d_first
            low_out[rows, :] = d_first.astype(BF16)
            for n, item in enumerate((d_mid * hat, d_mid, d_first)):
                sums[n] = sums[n] + jnp.sum(item, 0, keepdims=True)
        for n in range(3):
            vec_out[n : n + 1, :] = sums[n]
        wait_all(waits)
        for j in range(2):
            for rows in chunks(length, 256):
                d_ctx[rows, j * cols : (j + 1) * cols] = nn(low_out[rows, :], w_a[j, :, three:]).astype(BF16)
        k_t = jnp.concatenate(
            [qkv[:, j * three + cols : j * three + 2 * cols].astype(F32) for j in range(2)], 1
        ).T.astype(BF16)
        for h in range(heads):
            j, i = divmod(h, cols // HD)
            at = j * three + i * HD
            q_cols, k_cols, v_cols = (slice(at + n * cols, at + n * cols + HD) for n in range(3))
            for n, queries in enumerate(chunks(length, 256)):
                d_o = d_ctx[queries, h * HD : (h + 1) * HD]
                d_p = nt(qkv[:, v_cols], d_o)
                p = probs[h, :, queries]
                wide = p.astype(F32)
                d_s = (wide * (d_p - jnp.sum(wide * d_p, 0, keepdims=True))).astype(BF16)
                d_v = nn(p, d_o)
                d_k = nn(d_s, qkv[queries, q_cols])
                acc_v[...] = d_v if n == 0 else acc_v[...] + d_v
                acc_k[...] = d_k if n == 0 else acc_k[...] + d_k
                d_q = nn(k_t[h * HD : (h + 1) * HD], d_s)
                dqkv_out[queries, q_cols] = (d_q.T * 0.125).astype(BF16)
            dqkv_out[:, v_cols] = acc_v[...].astype(BF16)
            dqkv_out[:, k_cols] = (acc_k[...] * 0.125).astype(BF16)
        for j in range(2):
            sum_out[j : j + 1, :] = jnp.sum(
                dqkv_out[:, j * three : (j + 1) * three].astype(F32), 0, keepdims=True
            )
        for rows in chunks(length, 256):
            part_out[rows, :] = (
                nt(dqkv_out[rows, :three], w_a[0, :, :three]) + nt(dqkv_out[rows, three:], w_a[1, :, :three])
            ).astype(BF16)

    return pl.pallas_call(
        body,
        out_shape=[
            sds((length, width), BF16), sds((length, width), F32), sds((length, width), BF16),
            sds((length, 2 * three), BF16), sds((3, width), F32), sds((2, three), F32),
        ],
        in_specs=[SM] + [VM] * 8 + [ANY] * 13,
        out_specs=[VM] * 6,
        scratch_shapes=[
            pltpu.VMEM((2, width, four), BF16), pltpu.VMEM((length, 2 * cols), BF16),
            pltpu.VMEM((length, HD), F32), pltpu.VMEM((length, HD), F32),
            pltpu.SemaphoreType.DMA((copies_of(pieces[5]),)),
        ],
        compiler_params=params(),
        cost_estimate=takes(15),
        name="attn_backward",
    )(meta, d_second, *parts, xhat, scale, gains, qkv, probs, *pieces)


def attn_grads(meta, places, x, d_attn, d_qkv, ctx, vectors, nz, extra):
    length, width = x.shape
    three = d_qkv.shape[1] // 2
    cols = ctx.shape[1] // 2
    rz = width // nz

    def body(meta, places, x, d_attn, d_qkv, ctx, vec1, vec2, sum_qkv, sum_inb, *refs):
        outs, (x_t, a_t, norm_rows_, qv_rows, inb_rows) = refs[:3], refs[3:]
        x_t[...] = x[...].astype(F32).T.astype(BF16)
        a_t[...] = d_attn[...].astype(F32).T.astype(BF16)
        for j in range(2):
            for k in range(nz):
                rows = zrows(meta, k, rz)
                grad = nn(x_t[rows, :], d_qkv[:, j * three : (j + 1) * three])
                put_grad(outs, j, k, nz, 0, grad)
                put_grad(outs, j, k, nz, three, nn(a_t[rows, :], ctx[:, j * cols : (j + 1) * cols]))
        if not extra:
            return
        piece, part = width // (4 * nz), cols // nz
        units = sum_inb.shape[1] // nz
        norm_rows_[...] = jnp.zeros_like(norm_rows_)
        norm_rows_[0:3, :] = vec1[...]
        norm_rows_[3:6, :] = vec2[...]
        for j in range(2):
            qv_rows[...] = jnp.zeros_like(qv_rows)
            qv_rows[0:1, :cols] = sum_qkv[j : j + 1, :cols]
            qv_rows[1:2, :cols] = sum_qkv[j : j + 1, 2 * cols : three]
            inb_rows[...] = jnp.zeros_like(inb_rows)
            inb_rows[0:1, :] = sum_inb[j : j + 1, :]
            for k in range(nz):
                d = places[2 + k]
                from_norm = pltpu.roll(norm_rows_[...], width - (d * 4 + places[j]) * piece, 1)
                from_qv = pltpu.roll(qv_rows[...], width - d * part, 1)
                from_inb = pltpu.roll(inb_rows[...], width - d * units, 1)
                lane = lax.broadcasted_iota(jnp.int32, (8, 2 * cols), 1)
                upper = jnp.where(lane < piece, from_norm[:, : 2 * cols], 0.0)
                lower = jnp.where(lane < part, from_qv[:, : 2 * cols], 0.0)
                shifted = pltpu.roll(from_inb, 128, 1)[:, : 2 * cols]
                inside = jnp.logical_and(lane >= 128, lane < 128 + units)
                lower = jnp.where(inside, shifted, lower)
                put_grad(outs, j, k, nz, 0, jnp.concatenate([upper, lower], 0), rz)
                put_grad(outs, j, k, nz, 2 * cols, jnp.zeros((extra, 2 * cols), F32), rz)

    return pl.pallas_call(
        body,
        out_shape=grads_of(nz, rz + extra, three + cols),
        in_specs=[SM, SM] + [VM] * 8,
        out_specs=[VM] * 3,
        scratch_shapes=[pltpu.VMEM((width, length), BF16)] * 2 + [pltpu.VMEM((8, width), F32)] * 3,
        compiler_params=params(),
        cost_estimate=takes(4),
        name="attn_grads",
    )(meta, places, x, d_attn, d_qkv, ctx, *vectors)


def loss_kernel(own, perm, slots, queries, positive_col, n_own):
    n_q, width = queries.shape
    n_p = slots.shape[0]

    def body(own, perm, slots, queries, pos, loss_out, d_out):
        passages = nn(perm[...], slots[...]).astype(BF16)
        logits = nt(queries[...], passages)
        top = jnp.max(logits, -1, keepdims=True)
        log_total = top + jnp.log(jnp.sum(jnp.exp(logits - top), -1, keepdims=True))
        index = lax.broadcasted_iota(jnp.int32, (n_q, n_p), 1)
        hits = pos[...] == index
        chosen = jnp.sum(jnp.where(hits, logits, 0.0), -1, keepdims=True)
        loss_out[...] = jnp.sum(log_total - chosen, 0, keepdims=True) / n_q
        d_logits = (16.0 * (jnp.exp(logits - log_total) - jnp.where(hits, 1.0, 0.0))).astype(BF16)
        pick = jnp.where(
            lax.broadcasted_iota(jnp.int32, (n_p, 128), 0)
            == lax.broadcasted_iota(jnp.int32, (n_p, 128), 1) + own[0],
            1.0, 0.0,
        ).astype(BF16)
        cols = nn(d_logits, pick)
        d_out[...] = nn(cols.T.astype(BF16), queries[...])[:n_own]

    return pl.pallas_call(
        body,
        out_shape=[sds((1, 1), F32), sds((n_own, width), F32)],
        in_specs=[SM] + [VM] * 4,
        out_specs=[VM] * 2,
        compiler_params=params(),
        cost_estimate=takes(1),
        name="contrast",
    )(own, perm, slots, queries, positive_col)


def on_device(
    inputs, cls_pos, w_qkv, qv_bias, w_out, w_in, in_bias, w_ffn_out,
    layer_gains, shifts, queries, positive, token_grad,
):
    core = lax.axis_index("section")
    dp = lax.axis_index("dp")
    me = lax.axis_index("tensor")
    n_dp = lax.axis_size("dp")
    n_t = lax.axis_size("tensor")
    first_core = core == 0
    rows_dev, share, width = inputs.shape
    cols = w_qkv.shape[3]
    units = w_in.shape[2]
    length = n_t * share
    n_chips = n_dp * n_t
    piece = width // n_chips
    order = dp_order()
    direct = direct_dp()
    nz, extra = (4, 16) if direct else (2, 0)
    t_ids = jnp.arange(n_t, dtype=jnp.int32)

    vec = jnp.concatenate(
        [layer_gains.reshape(-1), shifts.reshape(-1), qv_bias.reshape(-1), in_bias.reshape(-1)]
    )
    n_gain, n_shift, n_qv, n_inb = layer_gains.size, shifts.size, qv_bias.size, in_bias.size
    n_vec = vec.shape[0]
    flat = jnp.concatenate(
        [vec, queries.reshape(-1), (positive // 16).astype(BF16), (positive % 16).astype(BF16)]
    )
    flat = jnp.pad(flat, (0, -flat.shape[0] % 2048)).reshape(-1, 128)

    def spread_rows(block):
        blocks = [lax.dynamic_index_in_dim(block, me ^ k, 0, keepdims=False) for k in range(n_t)]
        return jnp.concatenate(exchange_rows(blocks), 0)

    pack = jnp.concatenate(
        [w_qkv[0, :, 0], w_qkv[0, :, 1], w_qkv[0, :, 2], w_out[0].T, w_in[0], w_ffn_out[0].T], 1
    )
    half = pack.shape[1] // 2
    message = spread_dp(flat)
    if direct:
        own = pack
        z_0 = rest_dp(after(pack, message), 0)
    else:
        pack = lax.all_gather(pack, "dp", axis=0, tiled=True)
        own, other_rows = pack[: width // 2], pack[width // 2 :][None]
    message = spread_tensor(message)
    near0, far0 = gather_own(after(own, message))
    both0 = gather_own_both(near0, far0)
    owns = [own, near0, far0, *both0]
    rows_in = spread_rows(after(jnp.where(first_core, inputs, token_grad), near0, far0))

    def halves_of(blocks, *earlier):
        if not direct:
            return other_rows[:, :, :half], other_rows[:, :, half:]
        blocks = after(blocks, *earlier)
        return jnp.stack([b[:, :half] for b in blocks]), jnp.stack([b[:, half:] for b in blocks])

    rest_0 = halves_of(z_0 if direct else None, rows_in)
    near_0 = gather_near(rest_0, 0)
    if direct:
        z_1 = rest_dp(after(pack, rest_0), 1)
    rows_got = swap_cores(after(rows_in, rest_0))
    x_low = jnp.where(first_core, rows_in, rows_got)
    tokens = jnp.where(first_core, rows_got, rows_in)
    both_0 = gather_both(near_0, 0)

    zrow = order * (width // n_dp) if direct else jnp.arange(2, dtype=jnp.int32) * (width // 2)
    metas = [
        jnp.concatenate([(core == level)[None].astype(jnp.int32), zrow.astype(jnp.int32)])
        for level in range(2)
    ]
    slots = [me ^ (2 * (core != level) + jnp.arange(2, dtype=jnp.int32)) for level in range(2)]
    places = [jnp.concatenate([s, order[:nz]]).astype(jnp.int32) for s in slots]
    hots = [(s[:, None] == t_ids[None, :]).astype(F32) for s in slots]

    positions = jnp.concatenate(
        [(me ^ k) * share + jnp.arange(share, dtype=jnp.int32) for k in range(n_t)]
    )
    cls_row = lax.dynamic_index_in_dim(cls_pos, me, 0, keepdims=False)
    segments = jnp.sum((positions[:, None] >= cls_row[None, :]).astype(jnp.int32), -1)
    seg_col, seg_row = segments[:, None], segments[None, :]
    tok_col, tok_row = positions[:, None], positions[None, :]

    slot_ids = (order[None, :] * n_t + (me ^ t_ids)[:, None]).reshape(-1)
    to_natural = (jnp.arange(n_chips, dtype=jnp.int32)[:, None] == slot_ids[None, :]).astype(BF16)
    table = nn(to_natural, message.reshape(n_chips, -1))
    own_table = table[:, :n_vec].astype(BF16)
    other_table = swap_cores(own_table)
    tables = jnp.where(
        first_core, jnp.stack([own_table, other_table]), jnp.stack([other_table, own_table])
    ).astype(F32)
    at = 0
    gains = tables[:, :, at : at + n_gain].reshape(2, n_chips, 2, piece).transpose(0, 2, 1, 3).reshape(2, 2, width)
    at += n_gain
    shift = tables[:, :, at : at + n_shift].reshape(2, n_chips, 4, piece).transpose(0, 2, 1, 3).reshape(2, 4, width)
    at += n_shift
    qv = tables[:, :, at : at + n_qv].reshape(2, n_dp, n_t, 2, cols // n_dp)
    qv = qv.transpose(0, 3, 2, 1, 4).reshape(2, 2, n_t, cols)
    at += n_qv
    inb = tables[:, :, at : at + n_inb].reshape(2, n_dp, n_t, n_inb).transpose(0, 2, 1, 3).reshape(2, n_t, units)
    vectors = []
    for level in range(2):
        bias = jnp.sum(hots[level][None, :, :, None] * qv[level][:, None], 2)
        bias = jnp.stack([bias[0], jnp.zeros_like(bias[0]), bias[1]], 1).reshape(1, -1)
        bias_in = jnp.sum(hots[level][:, :, None] * inb[level][None], 1).reshape(1, -1)
        vectors.append((gains[level], shift[level], bias, bias_in))
    at = n_vec
    q_dev = queries.shape[0]
    all_q = table[:, at : at + q_dev * width].reshape(-1, width).astype(BF16)
    at += q_dev * width
    all_pos = table[:, at : at + q_dev] * 16.0 + table[:, at + q_dev : at + 2 * q_dev]
    all_pos = all_pos.astype(jnp.int32).reshape(-1, 1)
    n_cls = cls_row.shape[0]
    perm = jnp.repeat(jnp.repeat(to_natural, n_cls, 0), n_cls, 1)
    perm = perm * jnp.tile(jnp.eye(n_cls, dtype=BF16), (n_chips, n_chips))

    vectors, all_q, all_pos, perm, x_low = lax.optimization_barrier(
        (vectors, all_q, all_pos, perm, x_low)
    )
    saved = []
    source, parts, norms = x_low, None, None
    rest_1 = halves_of(z_1 if direct else None, near_0)
    near_1 = gather_near(after(rest_1, both_0), 1)
    pieces = [[*owns, *rest_0, *near_0, *both_0], None]
    for level in range(2):
        gain, shift, bias, bias_in = vectors[level]
        outs = attn_forward(
            level, metas[level], source, parts, norms, pieces[level], bias, seg_col, seg_row, cols
        )
        part, qkv, probs, ctx = outs[:4]
        if level:
            x, xhat2, scale2 = outs[4:]
            saved[0]["second"] = (xhat2, scale2)
        else:
            x = x_low
        part, mid, xhat1, scale1, act, slope = ffn_forward(
            metas[level], x, (part, swap_cores(part)), gain, shift, pieces[level], bias_in, units
        )
        saved.append(
            dict(x=x, qkv=qkv, probs=probs, ctx=ctx, mid=mid, xhat1=xhat1, scale1=scale1, act=act, slope=slope)
        )
        source, parts, norms = mid, (part, swap_cores(part)), (gain, shift)
        if level == 0:
            pieces[1] = [*owns, *rest_1, *near_1, *gather_both(near_1, 1)]
    y, xhat2, scale2, cls_own = last_norm(source, parts, *norms, tok_row, cls_row)
    saved[1]["second"] = (xhat2, scale2)

    cls_slots = spread_tensor(spread_dp(cls_own)).reshape(n_chips * n_cls, width)
    first_own = ((dp * n_t + me) * n_cls).astype(jnp.int32)[None]
    mean_loss, d_cls = loss_kernel(first_own, perm, cls_slots, all_q, all_pos, n_cls)

    vector_rows = [None, None]
    sources = (tokens, d_cls, tok_col, cls_row)
    sums_a, sums_b = [None, None], [None, None]
    for level in (1, 0):
        gain = vectors[level][0]
        kept = saved[level]
        meta = metas[level]
        xhat2, scale2 = kept["second"]
        if level == 0:
            sources = (after(sources[0], sums_b[1].first(grads_a[1])), *sources[1:])
        part, d_second, d_ffn, d_pre, vec2, sum_inb = ffn_backward(
            level, meta, sources, xhat2, scale2, gain, kept["slope"], pieces[level], units
        )
        other = swap_cores(part)
        if level == 0:
            d_ffn = after(d_ffn, sums_a[1].first(part))
        grads_b = ffn_grads(meta, kept["mid"], d_pre, d_ffn, kept["act"], nz)
        sums_b[level] = Reduction(grads_b, level)
        d_second = after(d_second, grads_b[1])
        if level == 0:
            d_second = after(d_second, sums_b[1].second(grads_b[1]))
        part, d_first, d_attn, d_qkv, vec1, sum_qkv = attn_backward(
            meta, d_second, (part, other), kept["xhat1"], kept["scale1"], gain,
            kept["qkv"], kept["probs"], pieces[level], cols,
        )
        other = swap_cores(part)
        if level == 0:
            d_attn = after(d_attn, sums_b[0].first(sums_a[1].second(part)))
        grads_a = attn_grads(
            meta, places[level], kept["x"], d_attn, d_qkv, kept["ctx"], (vec1, vec2, sum_qkv, sum_inb), nz, extra
        )
        sums_a[level] = Reduction(grads_a, level)
        vector_rows[level] = (vec1, vec2, sum_qkv, sum_inb)
        sources = (d_first, part, other)
    sums_b[1].third(grads_a[1])
    sums_b[0].second_direct(sums_b[1].pieces)
    sums_a[1].third(sums_b[0].sums)
    sums_a[0].first(sums_a[1].pieces, sums_b[0].hops[1:2] if direct else sums_b[0].sums)
    last_a1, last_b1 = last_dp([sums_a[1], sums_b[1]], sums_a[0].added)
    sums_a[0].second_direct(sums_a[0].added)
    total_b0 = sums_b[0].third_direct()
    d_hidden = d_first + (part.astype(F32) + other.astype(F32))
    outgoing = jnp.where(first_core, d_hidden, y.astype(F32))
    low = after(outgoing.astype(BF16), sums_a[0].sums).reshape(n_t, share, width)
    incoming = [outgoing[:share]] + [b.astype(F32) for b in exchange_rows([low[k] for k in range(n_t)])[1:]]
    boundary = jnp.zeros((n_t, share, width), F32)
    for k in range(n_t):
        boundary = lax.dynamic_update_index_in_dim(boundary, incoming[k], me ^ k, 0)
    tot_b, tot_a = (
        jnp.where(first_core, low, sum(p.astype(F32) for p in high))
        for low, high in ((total_b0, last_b1), (sums_a[0].third_direct(), last_a1))
    )
    if direct:
        end = width // n_dp
        own = tot_a[end : end + 6, :piece]
        qv = tot_a[end + 8 : end + 10, : qv_bias.shape[3]]
        grad_inb = tot_a[end + 8 : end + 9, 128 : 128 + n_inb]
        tot_a = tot_a[:end]
    else:
        tables = []
        for level in range(2):
            vec1, vec2, sum_qkv, sum_inb = vector_rows[level]
            by_t = lax.dot_general(
                hots[level], jnp.concatenate([sum_qkv, sum_inb], 1), (((0,), (0,)), ((), ())),
                precision=lax.Precision.HIGHEST,
            )
            whole = 0.5 * jnp.concatenate([vec1, vec2])
            whole = jnp.pad(whole, ((0, 0), (0, by_t.shape[1] - width)))
            tables.append(jnp.concatenate([whole, by_t]))
        tables = lax.psum(jnp.stack(tables), ("section", "dp", "tensor"))
        flat = jnp.where(first_core, tables[0], tables[1])
        own = lax.dynamic_slice_in_dim(flat[:6, :width], (dp * n_t + me) * piece, piece, 1)
        by_t = lax.dynamic_slice_in_dim(flat, 6 + me, 1, 0)
        qv = jnp.concatenate([by_t[:, :cols], by_t[:, 2 * cols : 3 * cols]])
        qv = lax.dynamic_slice_in_dim(qv, dp * qv_bias.shape[3], qv_bias.shape[3], 1)
        grad_inb = lax.dynamic_slice_in_dim(by_t[:, 3 * cols :], dp * n_inb, n_inb, 1)
    grad_gains = jnp.concatenate([own[0:1], own[3:4]]).reshape(layer_gains.shape)
    grad_shifts = jnp.concatenate([own[2:3], own[1:2], own[5:6], own[4:5]]).reshape(shifts.shape)
    grad_qv, grad_inb = qv.reshape(qv_bias.shape), grad_inb.reshape(in_bias.shape)

    grad_qkv = jnp.stack([tot_a[:, n * cols : (n + 1) * cols] for n in range(3)], 1)[None]
    grad_out = tot_a[:, 3 * cols :].T[None]
    grad_in = tot_b[:, :units][None]
    grad_ffn = tot_b[:, units:].T[None]
    return (
        grad_qkv, grad_qv, grad_out, grad_in, grad_inb, grad_ffn,
        grad_gains, grad_shifts, boundary[None], mean_loss.reshape(()),
    )


def solution(mesh):
    return jax.shard_map(
        on_device,
        mesh=mesh,
        in_specs=(
            P("dp", "tensor", None),
            P("dp", None),
            P("section", "dp", None, "tensor"),
            P("section", None, "tensor", "dp"),
            P("section", "tensor", "dp"),
            P("section", "dp", "tensor"),
            P("section", "tensor", "dp"),
            P("section", "tensor", "dp"),
            P("section", None, ("dp", "tensor")),
            P("section", None, ("dp", "tensor")),
            P(("dp", "tensor"), None),
            P(("dp", "tensor")),
            P("dp", "tensor", None),
        ),
        out_specs=(
            P("section", "dp", None, "tensor"),
            P("section", None, "tensor", "dp"),
            P("section", "tensor", "dp"),
            P("section", "dp", "tensor"),
            P("section", "tensor", "dp"),
            P("section", "tensor", "dp"),
            P("section", None, ("dp", "tensor")),
            P("section", None, ("dp", "tensor")),
            P("section", "dp", "tensor", None),
            P(),
        ),
        check_vma=False,
    )
```

```python
import jax
import jax.numpy as jnp
from jax import lax
from jax.experimental import pallas as pl
from jax.experimental.pallas import tpu as pltpu
from jax.sharding import PartitionSpec as P

HD = 64
PARTNER = 1
CROSS = 2
BF16 = jnp.bfloat16
F32 = jnp.float32


def mm(left, right, dims):
    return lax.dot_general(left, right, (dims, ((), ())), preferred_element_type=F32)


def nn(left, right):
    return mm(left, right, ((1,), (0,)))


def nt(left, right):
    return mm(left, right, ((1,), (1,)))


def after(block, *earlier):
    return lax.optimization_barrier((block, *earlier))[0]


def swap_cores(block):
    return lax.ppermute(block, "section", [(0, 1), (1, 0)])


def hop(block, axis, flip):
    return lax.ppermute(block, axis, [(i, i ^ flip) for i in range(lax.axis_size(axis))])


def core_hop(block, axis, flip, core):
    size = lax.axis_size(axis)
    route = [(core * size + i, core * size + (i ^ flip)) for i in range(size)]
    return lax.ppermute(block, ("section", axis), route)


def cross_hop(block, source):
    size = lax.axis_size("tensor")
    route = [(source * size + i, (1 - source) * size + (i ^ CROSS)) for i in range(size)]
    return lax.ppermute(block, ("section", "tensor"), route)


def direct_dp():
    return lax.axis_size("dp") == 4


def dp_order():
    size = lax.axis_size("dp")
    if direct_dp():
        return lax.axis_index("dp") ^ jnp.arange(size, dtype=jnp.int32)
    return jnp.arange(size, dtype=jnp.int32)


def spread_dp(block):
    if direct_dp():
        return jnp.stack([block] + [hop(block, "dp", k) for k in range(1, 4)])
    return lax.all_gather(block, "dp", axis=0, tiled=False)


def spread_tensor(block):
    return jnp.stack([block] + [hop(block, "tensor", k) for k in range(1, 4)])


def double(block, axis):
    pair = jnp.stack([block, hop(block, axis, 1)])
    return jnp.concatenate([pair, hop(pair, axis, 2)])


def exchange_rows(blocks):
    first = hop(jnp.stack([blocks[1], blocks[3]]), "tensor", 1)
    second = hop(jnp.stack([blocks[2], first[1]]), "tensor", 2)
    return [blocks[0], first[0], second[0], second[1]]


def cross_all(block):
    size = lax.axis_size("tensor")
    route = [(s * size + i, (1 - s) * size + (i ^ CROSS)) for s in range(2) for i in range(size)]
    return lax.ppermute(block, ("section", "tensor"), route)


def rest_dp(own, core):
    return [core_hop(own, "dp", k, core) for k in range(1, 4)]


def gather_own(own):
    near, far = hop(own, "tensor", PARTNER), cross_all(own)
    return near, far


def gather_own_both(near, far):
    half = near.shape[1] // 2
    return cross_all(near[:, :half]), hop(far[:, half:], "tensor", PARTNER)


def gather_near(rest, core):
    a, b = rest
    near_a, far_b = core_hop(a, "tensor", PARTNER, core), cross_hop(b, core)
    near_b, far_a = core_hop(b, "tensor", PARTNER, core), cross_hop(a, core)
    return near_a, near_b, far_a, far_b


def gather_both(near, core):
    return cross_hop(near[0], core), core_hop(near[3], "tensor", PARTNER, 1 - core)


def add_low(*items):
    total = items[0].astype(F32)
    for item in items[1:]:
        total = total + item.astype(F32)
    return total.astype(BF16)


class Reduction:
    def __init__(self, grads, core):
        self.core = core
        self.pair, self.next_b, self.own_b = grads
        self.got = cross_hop(self.pair, 1 - core)
        self.near_b = hop(self.next_b, "tensor", PARTNER)

    def first(self, *earlier):
        half = self.next_b.shape[0]
        self.parts = pair, own_b, got, near_b = after((self.pair, self.own_b, self.got, self.near_b), *earlier)
        self.added = add_low(pair[:half], got[:half]), add_low(own_b, near_b)
        self.near_a = core_hop(self.added[0], "tensor", PARTNER, self.core)
        self.far_b = cross_hop(self.added[1], 1 - self.core)
        return self.added

    def sum_halves(self, *earlier):
        half = self.next_b.shape[0]
        near_a, far_b, (pair, own_b, got, near_b) = after((self.near_a, self.far_b, self.parts), *earlier)
        return add_low(pair[half:], got[half:], near_a), add_low(own_b, near_b, far_b)

    def scatter(self):
        whole = jnp.concatenate(self.sums).reshape(-1, self.own_b.shape[2])
        return [lax.psum_scatter(whole, "dp", scatter_dimension=0, tiled=True)]

    def second_direct(self, *earlier):
        a, b = self.sums = self.sum_halves(*earlier)
        if direct_dp():
            self.hops = [
                core_hop(block, "dp", k, self.core) for k, block in ((1, a[1]), (2, b[0]), (3, b[1]))
            ]
        return self.sums

    def third_direct(self, *earlier):
        if not direct_dp():
            return sum(p.astype(F32) for p in self.scatter())
        return sum(p.astype(F32) for p in after([self.sums[0][0], *self.hops], *earlier))

    def second(self, *earlier):
        self.sums = self.sum_halves(*earlier)
        if direct_dp():
            self.across = core_hop(self.sums[1], "dp", 2, self.core)
        return self.sums

    def third(self, *earlier):
        if not direct_dp():
            self.pieces = self.scatter()
            return self.pieces
        a, across = after((self.sums[0], self.across), *earlier)
        self.pieces = [add_low(a[k], across[k]) for k in range(2)]
        return self.pieces


def last_dp(reductions, *earlier):
    if not direct_dp():
        return [r.pieces for r in reductions]
    high = max(r.pieces[0].shape[0] for r in reductions)
    block = [jnp.pad(r.pieces[1], ((0, high - r.pieces[1].shape[0]), (0, 0))) for r in reductions]
    got = core_hop(after(jnp.concatenate(block, 1), *earlier), "dp", 1, reductions[0].core)
    at, out = 0, []
    for r in reductions:
        rows, width = r.pieces[0].shape
        out.append([r.pieces[0], got[:rows, at : at + width]])
        at += width
    return out


VMEM_LIMIT = 48 * 1024 * 1024
CHUNK = 128


def takes(micros):
    return pl.CostEstimate(flops=int(micros * 1.1e9), bytes_accessed=0, transcendentals=0)


def params():
    return pltpu.CompilerParams(vmem_limit_bytes=VMEM_LIMIT)


ANY = pl.BlockSpec(memory_space=pl.ANY)
VM = pl.BlockSpec(memory_space=pltpu.VMEM)
SM = pl.BlockSpec(memory_space=pltpu.SMEM)


def sds(shape, dtype):
    return jax.ShapeDtypeStruct(shape, dtype)


def chunks(length, step=CHUNK):
    return [slice(i, i + step) for i in range(0, length, step)]


def norm_rows(z):
    centre = z - jnp.mean(z, -1, keepdims=True)
    spread = jnp.mean(centre * centre, -1, keepdims=True)
    scale = lax.rsqrt(spread + 1e-05)
    return centre * scale, scale


def norm_back_rows(d_out, gain, xhat, scale):
    g = d_out * gain
    m1 = jnp.mean(g, -1, keepdims=True)
    m2 = jnp.mean(g * xhat, -1, keepdims=True)
    return scale * (g - m1 - xhat * m2)


def gelu_parts(x):
    e = jnp.exp(-0.5 * x * x)
    t = 1.0 / (1.0 + 0.2316418882 * jnp.abs(x))
    poly = t * (
        0.127414796 + t * (-0.142248368 + t * (0.7107068705 + t * (-0.7265760135 + t * 0.5307027145)))
    )
    tail = poly * e
    cdf = jnp.where(x < 0.0, tail, 1.0 - tail)
    return x * cdf, cdf + x * e * 0.3989422804014327


def zrows(meta, k, rz):
    return pl.ds(pl.multiple_of(meta[1 + k], 64), rz)


def cut(start, width, at):
    if start < at < start + width:
        return [(start, at - start), (at, start + width - at)]
    return [(start, width)]


def load_weights(meta, pieces, base, places, sems):
    own, near0, far0, a0, b0, *halves = pieces
    rest, near, far, both = halves[0:2], halves[2:4], halves[4:6], halves[6:8]
    split, count = a0.shape[1], rest[0].shape[0]
    home = meta[0] == 1
    lists = [[] for _ in places]
    at = 0
    for j in range(2):
        for k in range(count + 1):
            rows = zrows(meta, k, own.shape[0])
            for n, (start, width, place) in enumerate(places):
                for g, w in cut(base + start, width, split):
                    side, column = divmod(g, split)
                    if k == 0:
                        mine = (near0 if j else own).at[:, pl.ds(g, w)]
                        other = (a0, b0)[side].at[:, pl.ds(column, w)] if j else far0.at[:, pl.ds(g, w)]
                    else:
                        mine, other = (
                            v[side].at[k - 1, :, pl.ds(column, w)] for v in ((near, both) if j else (rest, far))
                        )
                    dst = place(j, rows, g - base - start, w)
                    first = pltpu.make_async_copy(mine, dst, sems.at[at])
                    second = pltpu.make_async_copy(other, dst, sems.at[at])
                    at += 1

                    @pl.when(home)
                    def _():
                        first.start()

                    @pl.when(jnp.logical_not(home))
                    def _():
                        second.start()

                    lists[n].append(first)
    return lists


def copies_of(rest):
    return 2 * 3 * (1 + rest.shape[0])


def wait_all(waits):
    for made in waits:
        made.wait()


def load_a(meta, pieces, w_a, sems):
    width = w_a.shape[2]
    return load_weights(
        meta, pieces, 0, [(0, width, lambda j, rows, c, w: w_a.at[j, rows, pl.ds(c, w)])], sems
    )[0]


def load_b(meta, pieces, w_i, w_f, sems):
    one = w_i.shape[1] // 2
    base = pieces[0].shape[1] - 2 * one
    return load_weights(
        meta,
        pieces,
        base,
        [
            (0, one, lambda j, rows, c, w: w_i.at[rows, pl.ds(j * one + c, w)]),
            (one, one, lambda j, rows, c, w: w_f.at[rows, pl.ds(j * one + c, w)]),
        ],
        sems,
    )


def attn_forward(level, meta, x_or_mid, parts, norms, pieces, bias, seg_col, seg_row, cols):
    four = 4 * cols
    length, width = x_or_mid.shape
    three = 3 * cols
    heads = 2 * cols // HD

    def body(meta, *refs):
        refs = list(refs)
        src = refs.pop(0)
        if level:
            own, other, gain, shift = (refs.pop(0) for _ in range(4))
        pieces = [refs.pop(0) for _ in range(13)]
        bias, sc, sr = (refs.pop(0) for _ in range(3))
        part_out, qkv_out, probs_out, ctx_out = (refs.pop(0) for _ in range(4))
        if level:
            x_out, xhat_out, scale_out = (refs.pop(0) for _ in range(3))
        w_a, sems = refs
        waits = load_a(meta, pieces, w_a, sems)
        if level:
            for rows in chunks(length):
                z = src[rows, :] + (own[rows, :].astype(F32) + other[rows, :].astype(F32)) + shift[2:3, :]
                xhat, scale = norm_rows(z)
                x_out[rows, :] = (xhat * gain[1:2, :] + shift[3:4, :]).astype(BF16)
                xhat_out[rows, :] = xhat.astype(BF16)
                scale_out[rows, :] = scale
            x_ref = x_out
        else:
            x_ref = src
        wait_all(waits)
        for j in range(2):
            c = slice(j * three, (j + 1) * three)
            for rows in chunks(length, 256):
                qkv_out[rows, c] = (nn(x_ref[rows, :], w_a[j, :, :three]) + bias[:, c]).astype(BF16)
        v_t = jnp.concatenate(
            [qkv_out[:, j * three + 2 * cols : (j + 1) * three].astype(F32) for j in range(2)], 1
        ).T.astype(BF16)
        for queries in chunks(length, 256):
            same = sc[...] == sr[:, queries]
            outs = []
            for h in range(heads):
                j, i = divmod(h, cols // HD)
                at = j * three + i * HD
                q = qkv_out[queries, at : at + HD]
                k = qkv_out[:, at + cols : at + cols + HD]
                st = jnp.where(same, nt(k, q) * 0.125, -1e30)
                p = jnp.exp(st - jnp.max(st, 0, keepdims=True))
                p = (p * (1.0 / jnp.sum(p, 0, keepdims=True))).astype(BF16)
                probs_out[h, :, queries] = p
                outs.append(nn(v_t[h * HD : (h + 1) * HD], p))
            ctx = jnp.concatenate(outs, 0).T.astype(BF16)
            ctx_out[queries, :] = ctx
            part_out[queries, :] = (
                nt(ctx[:, :cols], w_a[0, :, three:]) + nt(ctx[:, cols:], w_a[1, :, three:])
            ).astype(BF16)

    outs = [
        sds((length, width), BF16), sds((length, 2 * three), BF16),
        sds((heads, length, length), BF16), sds((length, 2 * cols), BF16),
    ]
    args = [meta, x_or_mid]
    if level:
        args += [*parts, *norms]
        outs += [sds((length, width), BF16), sds((length, width), BF16), sds((length, 1), F32)]
    specs = [SM] + [VM] * (len(args) - 1) + [ANY] * 13 + [VM] * 3
    args += [*pieces, bias, seg_col, seg_row]
    return pl.pallas_call(
        body,
        out_shape=outs,
        in_specs=specs,
        out_specs=[VM] * len(outs),
        scratch_shapes=[pltpu.VMEM((2, width, four), BF16), pltpu.SemaphoreType.DMA((copies_of(pieces[5]),))],
        compiler_params=params(),
        cost_estimate=takes(13),
        name="attn_forward",
    )(*args)


def ffn_forward(meta, x, parts, gains, shifts, pieces, bias_in, half):
    units = 2 * half
    length, width = x.shape

    def body(meta, x, own, other, gain, shift, p0, p1, p2, p3, p4, p5, p6, p7, p8, p9, p10, p11, p12, bias,
             part_out, mid_out, xhat_out, scale_out, act_out, slope_out, w_i, w_f, low, sems):
        first, second = load_b(meta, (p0, p1, p2, p3, p4, p5, p6, p7, p8, p9, p10, p11, p12), w_i, w_f, sems)
        for rows in chunks(length):
            z = x[rows, :].astype(F32) + (own[rows, :].astype(F32) + other[rows, :].astype(F32)) + shift[0:1, :]
            xhat, scale = norm_rows(z)
            mid = xhat * gain[0:1, :] + shift[1:2, :]
            mid_out[rows, :] = mid
            low[rows, :] = mid.astype(BF16)
            xhat_out[rows, :] = xhat.astype(BF16)
            scale_out[rows, :] = scale
        wait_all(first)
        for rows in chunks(length, 256):
            for c in chunks(units, 512):
                pre = nn(low[rows, :], w_i[:, c]) + bias[:, c]
                act, slope = gelu_parts(pre)
                act_out[rows, c] = act.astype(BF16)
                slope_out[rows, c] = slope.astype(BF16)
        wait_all(second)
        for rows in chunks(length, 256):
            part_out[rows, :] = nt(act_out[rows, :], w_f[...]).astype(BF16)

    return pl.pallas_call(
        body,
        out_shape=[
            sds((length, width), BF16), sds((length, width), F32), sds((length, width), BF16),
            sds((length, 1), F32), sds((length, units), BF16), sds((length, units), BF16),
        ],
        in_specs=[SM] + [VM] * 5 + [ANY] * 13 + [VM],
        out_specs=[VM] * 6,
        scratch_shapes=[
            pltpu.VMEM((width, units), BF16), pltpu.VMEM((width, units), BF16),
            pltpu.VMEM((length, width), BF16), pltpu.SemaphoreType.DMA((copies_of(pieces[5]),)),
        ],
        compiler_params=params(),
        cost_estimate=takes(9),
        name="ffn_forward",
    )(meta, x, *parts, gains, shifts, *pieces, bias_in)


def last_norm(mid, parts, gains, shifts, tok_row, cls_pos):
    length, width = mid.shape
    n_cls = cls_pos.shape[0]

    def body(cls, mid, own, other, gain, shift, tok, y_out, xhat_out, scale_out, cls_out):
        for rows in chunks(length):
            z = mid[rows, :] + (own[rows, :].astype(F32) + other[rows, :].astype(F32)) + shift[2:3, :]
            xhat, scale = norm_rows(z)
            y_out[rows, :] = (xhat * gain[1:2, :] + shift[3:4, :]).astype(BF16)
            xhat_out[rows, :] = xhat.astype(BF16)
            scale_out[rows, :] = scale
        which = lax.broadcasted_iota(jnp.int32, (16, length), 0)
        hot = jnp.zeros((16, length), F32)
        for p in range(n_cls):
            hot = jnp.where(jnp.logical_and(which == p, tok[...] == cls[p]), 1.0, hot)
        cls_out[...] = nn(hot.astype(BF16), y_out[...])[:n_cls].astype(BF16)

    return pl.pallas_call(
        body,
        out_shape=[
            sds((length, width), BF16), sds((length, width), BF16), sds((length, 1), F32),
            sds((n_cls, width), BF16),
        ],
        in_specs=[SM] + [VM] * 6,
        out_specs=[VM] * 4,
        compiler_params=params(),
        cost_estimate=takes(2),
        name="last_norm",
    )(cls_pos, mid, *parts, gains, shifts, tok_row)


def ffn_backward(level, meta, sources, xhat, scale, gains, slope, pieces, half):
    units = 2 * half
    length, width = xhat.shape
    n_cls = sources[3].shape[0] if level else 0

    def body(meta, *refs):
        refs = list(refs)
        if level:
            cls, grad, d_cls, tok = (refs.pop(0) for _ in range(4))
        else:
            d_above, own, other = (refs.pop(0) for _ in range(3))
        xhat, scale, gain, slope = (refs.pop(0) for _ in range(4))
        pieces = [refs.pop(0) for _ in range(13)]
        part_out, second_out, low_out, pre_out, vec_out, inb_out, w_i, w_f, sems = refs
        first, second = load_b(meta, pieces, w_i, w_f, sems)
        sums = [jnp.zeros((1, width), F32) for _ in range(3)]
        for rows in chunks(length):
            if level:
                d_out = grad[rows, :].astype(F32)
                for p in range(n_cls):
                    d_out = d_out + jnp.where(tok[rows, :] == cls[p], 1.0, 0.0) * d_cls[p : p + 1, :]
            else:
                d_out = d_above[rows, :] + (own[rows, :].astype(F32) + other[rows, :].astype(F32))
                d_out = d_out.astype(BF16).astype(F32)
            hat = xhat[rows, :].astype(F32)
            d_second = norm_back_rows(d_out, gain[1:2, :], hat, scale[rows, :])
            second_out[rows, :] = d_second
            low_out[rows, :] = d_second.astype(BF16)
            for n, item in enumerate((d_out * hat, d_out, d_second)):
                sums[n] = sums[n] + jnp.sum(item, 0, keepdims=True)
        for n in range(3):
            vec_out[n : n + 1, :] = sums[n]
        wait_all(second)
        for n, rows in enumerate(chunks(length, 256)):
            for c in chunks(units, units // 4):
                d_act = nn(low_out[rows, :], w_f[:, c])
                d_pre = (slope[rows, c].astype(F32) * d_act).astype(BF16)
                pre_out[rows, c] = d_pre
                j, at = divmod(c.start, units // 2)
                at = slice(at, at + c.stop - c.start)
                total = jnp.sum(d_pre.astype(F32), 0, keepdims=True)
                inb_out[j : j + 1, at] = total if n == 0 else inb_out[j : j + 1, at] + total
        wait_all(first)
        for rows in chunks(length, 256):
            part_out[rows, :] = nt(pre_out[rows, :], w_i[...]).astype(BF16)

    if level:
        token_grad, d_cls, tok_col, cls_pos = sources
        args, specs = [meta, cls_pos, token_grad, d_cls, tok_col], [SM, SM, VM, VM, VM]
    else:
        args, specs = [meta, *sources], [SM, VM, VM, VM]
    args += [xhat, scale, gains, slope, *pieces]
    specs += [VM] * 4 + [ANY] * 13
    return pl.pallas_call(
        body,
        out_shape=[
            sds((length, width), BF16), sds((length, width), F32), sds((length, width), BF16),
            sds((length, units), BF16), sds((3, width), F32), sds((2, units // 2), F32),
        ],
        in_specs=specs,
        out_specs=[VM] * 6,
        scratch_shapes=[
            pltpu.VMEM((width, units), BF16), pltpu.VMEM((width, units), BF16),
            pltpu.SemaphoreType.DMA((copies_of(pieces[5]),)),
        ],
        compiler_params=params(),
        cost_estimate=takes(9),
        name="ffn_backward",
    )(*args)


def grads_of(nz, rz, width):
    half = nz // 2
    return [sds((nz, rz, width), BF16), sds((half, rz, width), BF16), sds((half, rz, width), BF16)]


def put_grad(outs, j, k, nz, column, value, first=0):
    half, (height, width) = nz // 2, value.shape
    if k < half:
        out, at = outs[0], k + (half if j == 0 else 0)
    else:
        out, at = outs[2 if j == 0 else 1], k - half
    out[at, first : first + height, column : column + width] = value.astype(BF16)


def ffn_grads(meta, mid, d_pre, d_ffn, act, nz):
    length, width = mid.shape
    units = d_pre.shape[1]
    one = units // 2
    rz = width // nz

    def body(meta, mid, d_pre, d_ffn, act, *refs):
        outs, (mid_t, ffn_t) = refs[:3], refs[3:]
        mid_t[...] = mid[...].T.astype(BF16)
        ffn_t[...] = d_ffn[...].astype(F32).T.astype(BF16)
        for j in range(2):
            c = slice(j * one, (j + 1) * one)
            for k in range(nz):
                rows = zrows(meta, k, rz)
                put_grad(outs, j, k, nz, 0, nn(mid_t[rows, :], d_pre[:, c]))
                put_grad(outs, j, k, nz, one, nn(ffn_t[rows, :], act[:, c]))

    return pl.pallas_call(
        body,
        out_shape=grads_of(nz, rz, units),
        in_specs=[SM] + [VM] * 4,
        out_specs=[VM] * 3,
        scratch_shapes=[pltpu.VMEM((width, length), BF16)] * 2,
        compiler_params=params(),
        cost_estimate=takes(7),
        name="ffn_grads",
    )(meta, mid, d_pre, d_ffn, act)


def attn_backward(meta, d_second, parts, xhat, scale, gains, qkv, probs, pieces, cols):
    four = 4 * cols
    length, width = d_second.shape
    three = 3 * cols
    heads = 2 * cols // HD

    def body(meta, d_second, own, other, xhat, scale, gain, qkv, probs, p0, p1, p2, p3, p4, p5, p6, p7, p8, p9, p10, p11, p12,
             part_out, first_out, low_out, dqkv_out, vec_out, sum_out,
             w_a, d_ctx, acc_v, acc_k, sems):
        waits = load_a(meta, (p0, p1, p2, p3, p4, p5, p6, p7, p8, p9, p10, p11, p12), w_a, sems)
        sums = [jnp.zeros((1, width), F32) for _ in range(3)]
        for rows in chunks(length):
            d_mid = d_second[rows, :] + (own[rows, :].astype(F32) + other[rows, :].astype(F32))
            hat = xhat[rows, :].astype(F32)
            d_first = norm_back_rows(d_mid, gain[0:1, :], hat, scale[rows, :])
            first_out[rows, :] = d_first
            low_out[rows, :] = d_first.astype(BF16)
            for n, item in enumerate((d_mid * hat, d_mid, d_first)):
                sums[n] = sums[n] + jnp.sum(item, 0, keepdims=True)
        for n in range(3):
            vec_out[n : n + 1, :] = sums[n]
        wait_all(waits)
        for j in range(2):
            for rows in chunks(length, 256):
                d_ctx[rows, j * cols : (j + 1) * cols] = nn(low_out[rows, :], w_a[j, :, three:]).astype(BF16)
        k_t = jnp.concatenate(
            [qkv[:, j * three + cols : j * three + 2 * cols].astype(F32) for j in range(2)], 1
        ).T.astype(BF16)
        for h in range(heads):
            j, i = divmod(h, cols // HD)
            at = j * three + i * HD
            q_cols, k_cols, v_cols = (slice(at + n * cols, at + n * cols + HD) for n in range(3))
            for n, queries in enumerate(chunks(length, 256)):
                d_o = d_ctx[queries, h * HD : (h + 1) * HD]
                d_p = nt(qkv[:, v_cols], d_o)
                p = probs[h, :, queries]
                wide = p.astype(F32)
                d_s = (wide * (d_p - jnp.sum(wide * d_p, 0, keepdims=True))).astype(BF16)
                d_v = nn(p, d_o)
                d_k = nn(d_s, qkv[queries, q_cols])
                acc_v[...] = d_v if n == 0 else acc_v[...] + d_v
                acc_k[...] = d_k if n == 0 else acc_k[...] + d_k
                d_q = nn(k_t[h * HD : (h + 1) * HD], d_s)
                dqkv_out[queries, q_cols] = (d_q.T * 0.125).astype(BF16)
            dqkv_out[:, v_cols] = acc_v[...].astype(BF16)
            dqkv_out[:, k_cols] = (acc_k[...] * 0.125).astype(BF16)
        for j in range(2):
            sum_out[j : j + 1, :] = jnp.sum(
                dqkv_out[:, j * three : (j + 1) * three].astype(F32), 0, keepdims=True
            )
        for rows in chunks(length, 256):
            part_out[rows, :] = (
                nt(dqkv_out[rows, :three], w_a[0, :, :three]) + nt(dqkv_out[rows, three:], w_a[1, :, :three])
            ).astype(BF16)

    return pl.pallas_call(
        body,
        out_shape=[
            sds((length, width), BF16), sds((length, width), F32), sds((length, width), BF16),
            sds((length, 2 * three), BF16), sds((3, width), F32), sds((2, three), F32),
        ],
        in_specs=[SM] + [VM] * 8 + [ANY] * 13,
        out_specs=[VM] * 6,
        scratch_shapes=[
            pltpu.VMEM((2, width, four), BF16), pltpu.VMEM((length, 2 * cols), BF16),
            pltpu.VMEM((length, HD), F32), pltpu.VMEM((length, HD), F32),
            pltpu.SemaphoreType.DMA((copies_of(pieces[5]),)),
        ],
        compiler_params=params(),
        cost_estimate=takes(15),
        name="attn_backward",
    )(meta, d_second, *parts, xhat, scale, gains, qkv, probs, *pieces)


def attn_grads(meta, places, x, d_attn, d_qkv, ctx, vectors, nz, extra):
    length, width = x.shape
    three = d_qkv.shape[1] // 2
    cols = ctx.shape[1] // 2
    rz = width // nz

    def body(meta, places, x, d_attn, d_qkv, ctx, vec1, vec2, sum_qkv, sum_inb, *refs):
        outs, (x_t, a_t, norm_rows_, qv_rows, inb_rows) = refs[:3], refs[3:]
        x_t[...] = x[...].astype(F32).T.astype(BF16)
        a_t[...] = d_attn[...].astype(F32).T.astype(BF16)
        for j in range(2):
            for k in range(nz):
                rows = zrows(meta, k, rz)
                grad = nn(x_t[rows, :], d_qkv[:, j * three : (j + 1) * three])
                put_grad(outs, j, k, nz, 0, grad)
                put_grad(outs, j, k, nz, three, nn(a_t[rows, :], ctx[:, j * cols : (j + 1) * cols]))
        if not extra:
            return
        piece, part = width // (4 * nz), cols // nz
        units = sum_inb.shape[1] // nz
        norm_rows_[...] = jnp.zeros_like(norm_rows_)
        norm_rows_[0:3, :] = vec1[...]
        norm_rows_[3:6, :] = vec2[...]
        for j in range(2):
            qv_rows[...] = jnp.zeros_like(qv_rows)
            qv_rows[0:1, :cols] = sum_qkv[j : j + 1, :cols]
            qv_rows[1:2, :cols] = sum_qkv[j : j + 1, 2 * cols : three]
            inb_rows[...] = jnp.zeros_like(inb_rows)
            inb_rows[0:1, :] = sum_inb[j : j + 1, :]
            for k in range(nz):
                d = places[2 + k]
                from_norm = pltpu.roll(norm_rows_[...], width - (d * 4 + places[j]) * piece, 1)
                from_qv = pltpu.roll(qv_rows[...], width - d * part, 1)
                from_inb = pltpu.roll(inb_rows[...], width - d * units, 1)
                lane = lax.broadcasted_iota(jnp.int32, (8, 2 * cols), 1)
                upper = jnp.where(lane < piece, from_norm[:, : 2 * cols], 0.0)
                lower = jnp.where(lane < part, from_qv[:, : 2 * cols], 0.0)
                shifted = pltpu.roll(from_inb, 128, 1)[:, : 2 * cols]
                inside = jnp.logical_and(lane >= 128, lane < 128 + units)
                lower = jnp.where(inside, shifted, lower)
                put_grad(outs, j, k, nz, 0, jnp.concatenate([upper, lower], 0), rz)
                put_grad(outs, j, k, nz, 2 * cols, jnp.zeros((extra, 2 * cols), F32), rz)

    return pl.pallas_call(
        body,
        out_shape=grads_of(nz, rz + extra, three + cols),
        in_specs=[SM, SM] + [VM] * 8,
        out_specs=[VM] * 3,
        scratch_shapes=[pltpu.VMEM((width, length), BF16)] * 2 + [pltpu.VMEM((8, width), F32)] * 3,
        compiler_params=params(),
        cost_estimate=takes(4),
        name="attn_grads",
    )(meta, places, x, d_attn, d_qkv, ctx, *vectors)


def loss_kernel(own, perm, slots, queries, positive_col, n_own):
    n_q, width = queries.shape
    n_p = slots.shape[0]

    def body(own, perm, slots, queries, pos, loss_out, d_out):
        passages = nn(perm[...], slots[...]).astype(BF16)
        logits = nt(queries[...], passages)
        top = jnp.max(logits, -1, keepdims=True)
        log_total = top + jnp.log(jnp.sum(jnp.exp(logits - top), -1, keepdims=True))
        index = lax.broadcasted_iota(jnp.int32, (n_q, n_p), 1)
        hits = pos[...] == index
        chosen = jnp.sum(jnp.where(hits, logits, 0.0), -1, keepdims=True)
        loss_out[...] = jnp.sum(log_total - chosen, 0, keepdims=True) / n_q
        d_logits = (16.0 * (jnp.exp(logits - log_total) - jnp.where(hits, 1.0, 0.0))).astype(BF16)
        pick = jnp.where(
            lax.broadcasted_iota(jnp.int32, (n_p, 128), 0)
            == lax.broadcasted_iota(jnp.int32, (n_p, 128), 1) + own[0],
            1.0, 0.0,
        ).astype(BF16)
        cols = nn(d_logits, pick)
        d_out[...] = nn(cols.T.astype(BF16), queries[...])[:n_own]

    return pl.pallas_call(
        body,
        out_shape=[sds((1, 1), F32), sds((n_own, width), F32)],
        in_specs=[SM] + [VM] * 4,
        out_specs=[VM] * 2,
        compiler_params=params(),
        cost_estimate=takes(1),
        name="contrast",
    )(own, perm, slots, queries, positive_col)


def on_device(
    inputs, cls_pos, w_qkv, qv_bias, w_out, w_in, in_bias, w_ffn_out,
    layer_gains, shifts, queries, positive, token_grad,
):
    core = lax.axis_index("section")
    dp = lax.axis_index("dp")
    me = lax.axis_index("tensor")
    n_dp = lax.axis_size("dp")
    n_t = lax.axis_size("tensor")
    first_core = core == 0
    rows_dev, share, width = inputs.shape
    cols = w_qkv.shape[3]
    units = w_in.shape[2]
    length = n_t * share
    n_chips = n_dp * n_t
    piece = width // n_chips
    order = dp_order()
    direct = direct_dp()
    nz, extra = (4, 16) if direct else (2, 0)
    t_ids = jnp.arange(n_t, dtype=jnp.int32)

    vec = jnp.concatenate(
        [layer_gains.reshape(-1), shifts.reshape(-1), qv_bias.reshape(-1), in_bias.reshape(-1)]
    )
    n_gain, n_shift, n_qv, n_inb = layer_gains.size, shifts.size, qv_bias.size, in_bias.size
    n_vec = vec.shape[0]
    flat = jnp.concatenate(
        [vec, queries.reshape(-1), (positive // 16).astype(BF16), (positive % 16).astype(BF16)]
    )
    flat = jnp.pad(flat, (0, -flat.shape[0] % 2048)).reshape(-1, 128)

    def spread_rows(block):
        blocks = [lax.dynamic_index_in_dim(block, me ^ k, 0, keepdims=False) for k in range(n_t)]
        return jnp.concatenate(exchange_rows(blocks), 0)

    pack = jnp.concatenate(
        [w_qkv[0, :, 0], w_qkv[0, :, 1], w_qkv[0, :, 2], w_out[0].T, w_in[0], w_ffn_out[0].T], 1
    )
    half = pack.shape[1] // 2
    message = spread_dp(flat)
    if direct:
        own = pack
        z_0 = rest_dp(after(pack, message), 0)
    else:
        pack = lax.all_gather(pack, "dp", axis=0, tiled=True)
        own, other_rows = pack[: width // 2], pack[width // 2 :][None]
    message = spread_tensor(message)
    near0, far0 = gather_own(after(own, message))
    near0, far0 = after((near0, far0), z_0[:2] if direct else near0)
    both0 = gather_own_both(near0, far0)
    owns = [own, near0, far0, *both0]
    rows_in = spread_rows(after(jnp.where(first_core, inputs, token_grad), near0, far0))

    def halves_of(blocks, *earlier):
        if not direct:
            return other_rows[:, :, :half], other_rows[:, :, half:]
        blocks = after(blocks, *earlier)
        return jnp.stack([b[:, :half] for b in blocks]), jnp.stack([b[:, half:] for b in blocks])

    rest_0 = halves_of(z_0 if direct else None, rows_in, both0)
    near_0 = gather_near(rest_0, 0)
    if direct:
        z_1 = rest_dp(after(pack, rest_0), 1)
    rows_got = swap_cores(after(rows_in, rest_0))
    x_low = jnp.where(first_core, rows_in, rows_got)
    tokens = jnp.where(first_core, rows_got, rows_in)
    both_0 = gather_both(near_0, 0)
    message = after(message, near_0[0])

    zrow = order * (width // n_dp) if direct else jnp.arange(2, dtype=jnp.int32) * (width // 2)
    metas = [
        jnp.concatenate([(core == level)[None].astype(jnp.int32), zrow.astype(jnp.int32)])
        for level in range(2)
    ]
    slots = [me ^ (2 * (core != level) + jnp.arange(2, dtype=jnp.int32)) for level in range(2)]
    places = [jnp.concatenate([s, order[:nz]]).astype(jnp.int32) for s in slots]
    hots = [(s[:, None] == t_ids[None, :]).astype(F32) for s in slots]

    positions = jnp.concatenate(
        [(me ^ k) * share + jnp.arange(share, dtype=jnp.int32) for k in range(n_t)]
    )
    cls_row = lax.dynamic_index_in_dim(cls_pos, me, 0, keepdims=False)
    segments = jnp.sum((positions[:, None] >= cls_row[None, :]).astype(jnp.int32), -1)
    seg_col, seg_row = segments[:, None], segments[None, :]
    tok_col, tok_row = positions[:, None], positions[None, :]

    slot_ids = (order[None, :] * n_t + (me ^ t_ids)[:, None]).reshape(-1)
    to_natural = (jnp.arange(n_chips, dtype=jnp.int32)[:, None] == slot_ids[None, :]).astype(BF16)
    table = nn(to_natural, message.reshape(n_chips, -1))
    own_table = table[:, :n_vec].astype(BF16)
    other_table = swap_cores(own_table)
    tables = jnp.where(
        first_core, jnp.stack([own_table, other_table]), jnp.stack([other_table, own_table])
    ).astype(F32)
    at = 0
    gains = tables[:, :, at : at + n_gain].reshape(2, n_chips, 2, piece).transpose(0, 2, 1, 3).reshape(2, 2, width)
    at += n_gain
    shift = tables[:, :, at : at + n_shift].reshape(2, n_chips, 4, piece).transpose(0, 2, 1, 3).reshape(2, 4, width)
    at += n_shift
    qv = tables[:, :, at : at + n_qv].reshape(2, n_dp, n_t, 2, cols // n_dp)
    qv = qv.transpose(0, 3, 2, 1, 4).reshape(2, 2, n_t, cols)
    at += n_qv
    inb = tables[:, :, at : at + n_inb].reshape(2, n_dp, n_t, n_inb).transpose(0, 2, 1, 3).reshape(2, n_t, units)
    vectors = []
    for level in range(2):
        bias = jnp.sum(hots[level][None, :, :, None] * qv[level][:, None], 2)
        bias = jnp.stack([bias[0], jnp.zeros_like(bias[0]), bias[1]], 1).reshape(1, -1)
        bias_in = jnp.sum(hots[level][:, :, None] * inb[level][None], 1).reshape(1, -1)
        vectors.append((gains[level], shift[level], bias, bias_in))
    at = n_vec
    q_dev = queries.shape[0]
    all_q = table[:, at : at + q_dev * width].reshape(-1, width).astype(BF16)
    at += q_dev * width
    all_pos = table[:, at : at + q_dev] * 16.0 + table[:, at + q_dev : at + 2 * q_dev]
    all_pos = all_pos.astype(jnp.int32).reshape(-1, 1)
    n_cls = cls_row.shape[0]
    perm = jnp.repeat(jnp.repeat(to_natural, n_cls, 0), n_cls, 1)
    perm = perm * jnp.tile(jnp.eye(n_cls, dtype=BF16), (n_chips, n_chips))

    vectors, all_q, all_pos, perm, x_low = lax.optimization_barrier(
        (vectors, all_q, all_pos, perm, x_low)
    )
    saved = []
    source, parts, norms = x_low, None, None
    rest_1 = halves_of(z_1 if direct else None, near_0)
    near_1 = gather_near(after(rest_1, both_0), 1)
    pieces = [[*owns, *rest_0, *near_0, *both_0], None]
    for level in range(2):
        gain, shift, bias, bias_in = vectors[level]
        outs = attn_forward(
            level, metas[level], source, parts, norms, pieces[level], bias, seg_col, seg_row, cols
        )
        part, qkv, probs, ctx = outs[:4]
        if level:
            x, xhat2, scale2 = outs[4:]
            saved[0]["second"] = (xhat2, scale2)
        else:
            x = x_low
        part, mid, xhat1, scale1, act, slope = ffn_forward(
            metas[level], x, (part, swap_cores(part)), gain, shift, pieces[level], bias_in, units
        )
        saved.append(
            dict(x=x, qkv=qkv, probs=probs, ctx=ctx, mid=mid, xhat1=xhat1, scale1=scale1, act=act, slope=slope)
        )
        source, parts, norms = mid, (part, swap_cores(part)), (gain, shift)
        if level == 0:
            pieces[1] = [*owns, *rest_1, *near_1, *gather_both(near_1, 1)]
    y, xhat2, scale2, cls_own = last_norm(source, parts, *norms, tok_row, cls_row)
    saved[1]["second"] = (xhat2, scale2)

    cls_slots = spread_tensor(spread_dp(cls_own)).reshape(n_chips * n_cls, width)
    first_own = ((dp * n_t + me) * n_cls).astype(jnp.int32)[None]
    mean_loss, d_cls = loss_kernel(first_own, perm, cls_slots, all_q, all_pos, n_cls)

    vector_rows = [None, None]
    sources = (tokens, d_cls, tok_col, cls_row)
    sums_a, sums_b = [None, None], [None, None]
    for level in (1, 0):
        gain = vectors[level][0]
        kept = saved[level]
        meta = metas[level]
        xhat2, scale2 = kept["second"]
        if level == 0:
            sources = (after(sources[0], sums_b[1].first(grads_a[1])), *sources[1:])
        part, d_second, d_ffn, d_pre, vec2, sum_inb = ffn_backward(
            level, meta, sources, xhat2, scale2, gain, kept["slope"], pieces[level], units
        )
        other = swap_cores(part)
        if level == 0:
            d_ffn = after(d_ffn, sums_a[1].first(part))
        grads_b = ffn_grads(meta, kept["mid"], d_pre, d_ffn, kept["act"], nz)
        sums_b[level] = Reduction(grads_b, level)
        d_second = after(d_second, grads_b[1])
        if level == 0:
            d_second = after(d_second, sums_b[1].second(grads_b[1]))
        part, d_first, d_attn, d_qkv, vec1, sum_qkv = attn_backward(
            meta, d_second, (part, other), kept["xhat1"], kept["scale1"], gain,
            kept["qkv"], kept["probs"], pieces[level], cols,
        )
        other = swap_cores(part)
        if level == 0:
            d_attn = after(d_attn, sums_b[0].first(sums_a[1].second(part)))
        grads_a = attn_grads(
            meta, places[level], kept["x"], d_attn, d_qkv, kept["ctx"], (vec1, vec2, sum_qkv, sum_inb), nz, extra
        )
        sums_a[level] = Reduction(grads_a, level)
        vector_rows[level] = (vec1, vec2, sum_qkv, sum_inb)
        sources = (d_first, part, other)
    sums_b[1].third(grads_a[1])
    sums_b[0].second_direct(sums_b[1].pieces)
    sums_a[1].third(sums_b[0].sums)
    sums_a[0].first(sums_a[1].pieces, sums_b[0].hops[1:2] if direct else sums_b[0].sums)
    sums_a[0].second_direct(sums_a[0].added)
    last_a1, last_b1 = last_dp([sums_a[1], sums_b[1]], sums_a[0].sums)
    total_b0 = sums_b[0].third_direct()
    d_hidden = d_first + (part.astype(F32) + other.astype(F32))
    outgoing = jnp.where(first_core, d_hidden, y.astype(F32))
    low = after(outgoing.astype(BF16), sums_a[0].added).reshape(n_t, share, width)
    incoming = [outgoing[:share]] + [b.astype(F32) for b in exchange_rows([low[k] for k in range(n_t)])[1:]]
    boundary = jnp.zeros((n_t, share, width), F32)
    for k in range(n_t):
        boundary = lax.dynamic_update_index_in_dim(boundary, incoming[k], me ^ k, 0)
    tot_b, tot_a = (
        jnp.where(first_core, low, sum(p.astype(F32) for p in high))
        for low, high in ((total_b0, last_b1), (sums_a[0].third_direct(), last_a1))
    )
    if direct:
        end = width // n_dp
        own = tot_a[end : end + 6, :piece]
        qv = tot_a[end + 8 : end + 10, : qv_bias.shape[3]]
        grad_inb = tot_a[end + 8 : end + 9, 128 : 128 + n_inb]
        tot_a = tot_a[:end]
    else:
        tables = []
        for level in range(2):
            vec1, vec2, sum_qkv, sum_inb = vector_rows[level]
            by_t = lax.dot_general(
                hots[level], jnp.concatenate([sum_qkv, sum_inb], 1), (((0,), (0,)), ((), ())),
                precision=lax.Precision.HIGHEST,
            )
            whole = 0.5 * jnp.concatenate([vec1, vec2])
            whole = jnp.pad(whole, ((0, 0), (0, by_t.shape[1] - width)))
            tables.append(jnp.concatenate([whole, by_t]))
        tables = lax.psum(jnp.stack(tables), ("section", "dp", "tensor"))
        flat = jnp.where(first_core, tables[0], tables[1])
        own = lax.dynamic_slice_in_dim(flat[:6, :width], (dp * n_t + me) * piece, piece, 1)
        by_t = lax.dynamic_slice_in_dim(flat, 6 + me, 1, 0)
        qv = jnp.concatenate([by_t[:, :cols], by_t[:, 2 * cols : 3 * cols]])
        qv = lax.dynamic_slice_in_dim(qv, dp * qv_bias.shape[3], qv_bias.shape[3], 1)
        grad_inb = lax.dynamic_slice_in_dim(by_t[:, 3 * cols :], dp * n_inb, n_inb, 1)
    grad_gains = jnp.concatenate([own[0:1], own[3:4]]).reshape(layer_gains.shape)
    grad_shifts = jnp.concatenate([own[2:3], own[1:2], own[5:6], own[4:5]]).reshape(shifts.shape)
    grad_qv, grad_inb = qv.reshape(qv_bias.shape), grad_inb.reshape(in_bias.shape)

    grad_qkv = jnp.stack([tot_a[:, n * cols : (n + 1) * cols] for n in range(3)], 1)[None]
    grad_out = tot_a[:, 3 * cols :].T[None]
    grad_in = tot_b[:, :units][None]
    grad_ffn = tot_b[:, units:].T[None]
    return (
        grad_qkv, grad_qv, grad_out, grad_in, grad_inb, grad_ffn,
        grad_gains, grad_shifts, boundary[None], mean_loss.reshape(()),
    )


def solution(mesh):
    return jax.shard_map(
        on_device,
        mesh=mesh,
        in_specs=(
            P("dp", "tensor", None),
            P("dp", None),
            P("section", "dp", None, "tensor"),
            P("section", None, "tensor", "dp"),
            P("section", "tensor", "dp"),
            P("section", "dp", "tensor"),
            P("section", "tensor", "dp"),
            P("section", "tensor", "dp"),
            P("section", None, ("dp", "tensor")),
            P("section", None, ("dp", "tensor")),
            P(("dp", "tensor"), None),
            P(("dp", "tensor")),
            P("dp", "tensor", None),
        ),
        out_specs=(
            P("section", "dp", None, "tensor"),
            P("section", None, "tensor", "dp"),
            P("section", "tensor", "dp"),
            P("section", "dp", "tensor"),
            P("section", "tensor", "dp"),
            P("section", "tensor", "dp"),
            P("section", None, ("dp", "tensor")),
            P("section", None, ("dp", "tensor")),
            P("section", "dp", "tensor", None),
            P(),
        ),
        check_vma=False,
    )
```

```python
import jax
import jax.numpy as jnp
from jax import lax
from jax.experimental import pallas as pl
from jax.experimental.pallas import tpu as pltpu
from jax.sharding import PartitionSpec as P

HD = 64
PARTNER = 1
CROSS = 2
BF16 = jnp.bfloat16
F32 = jnp.float32


def mm(left, right, dims):
    return lax.dot_general(left, right, (dims, ((), ())), preferred_element_type=F32)


def nn(left, right):
    return mm(left, right, ((1,), (0,)))


def nt(left, right):
    return mm(left, right, ((1,), (1,)))


def after(block, *earlier):
    return lax.optimization_barrier((block, *earlier))[0]


def swap_cores(block):
    return lax.ppermute(block, "section", [(0, 1), (1, 0)])


def hop(block, axis, flip):
    return lax.ppermute(block, axis, [(i, i ^ flip) for i in range(lax.axis_size(axis))])


def core_hop(block, axis, flip, core):
    size = lax.axis_size(axis)
    route = [(core * size + i, core * size + (i ^ flip)) for i in range(size)]
    return lax.ppermute(block, ("section", axis), route)


def cross_hop(block, source):
    size = lax.axis_size("tensor")
    route = [(source * size + i, (1 - source) * size + (i ^ CROSS)) for i in range(size)]
    return lax.ppermute(block, ("section", "tensor"), route)


def direct_dp():
    return lax.axis_size("dp") == 4


def dp_order():
    size = lax.axis_size("dp")
    if direct_dp():
        return lax.axis_index("dp") ^ jnp.arange(size, dtype=jnp.int32)
    return jnp.arange(size, dtype=jnp.int32)


def spread_dp(block):
    if direct_dp():
        return jnp.stack([block] + [hop(block, "dp", k) for k in range(1, 4)])
    return lax.all_gather(block, "dp", axis=0, tiled=False)


def spread_tensor(block):
    return jnp.stack([block] + [hop(block, "tensor", k) for k in range(1, 4)])


def double(block, axis):
    pair = jnp.stack([block, hop(block, axis, 1)])
    return jnp.concatenate([pair, hop(pair, axis, 2)])


def exchange_rows(blocks):
    first = hop(jnp.stack([blocks[1], blocks[3]]), "tensor", 1)
    second = hop(jnp.stack([blocks[2], first[1]]), "tensor", 2)
    return [blocks[0], first[0], second[0], second[1]]


def cross_all(block):
    size = lax.axis_size("tensor")
    route = [(s * size + i, (1 - s) * size + (i ^ CROSS)) for s in range(2) for i in range(size)]
    return lax.ppermute(block, ("section", "tensor"), route)


def rest_dp(own):
    return [hop(own, "dp", k) for k in range(1, 4)]


def gather_own(own):
    near, far = hop(own, "tensor", PARTNER), cross_all(own)
    return near, far


def gather_own_both(near, far):
    half = near.shape[1] // 2
    return cross_all(near[:, :half]), hop(far[:, half:], "tensor", PARTNER)


def gather_near(rest):
    a, b = rest
    near_a, far_b = hop(a, "tensor", PARTNER), cross_all(b)
    near_b, far_a = hop(b, "tensor", PARTNER), cross_all(a)
    return near_a, near_b, far_a, far_b


def gather_both(near):
    return cross_all(near[0]), hop(near[3], "tensor", PARTNER)


def add_low(*items):
    total = items[0].astype(F32)
    for item in items[1:]:
        total = total + item.astype(F32)
    return total.astype(BF16)


class Reduction:
    def __init__(self, grads, core):
        self.core = core
        self.pair, self.next_b, self.own_b = grads
        self.got = cross_hop(self.pair, 1 - core)
        self.near_b = hop(self.next_b, "tensor", PARTNER)

    def first(self, *earlier):
        half = self.next_b.shape[0]
        self.parts = pair, own_b, got, near_b = after((self.pair, self.own_b, self.got, self.near_b), *earlier)
        self.added = add_low(pair[:half], got[:half]), add_low(own_b, near_b)
        self.near_a = core_hop(self.added[0], "tensor", PARTNER, self.core)
        self.far_b = cross_hop(self.added[1], 1 - self.core)
        return self.added

    def sum_halves(self, *earlier):
        half = self.next_b.shape[0]
        near_a, far_b, (pair, own_b, got, near_b) = after((self.near_a, self.far_b, self.parts), *earlier)
        return add_low(pair[half:], got[half:], near_a), add_low(own_b, near_b, far_b)

    def scatter(self):
        whole = jnp.concatenate(self.sums).reshape(-1, self.own_b.shape[2])
        return [lax.psum_scatter(whole, "dp", scatter_dimension=0, tiled=True)]

    def second_direct(self, *earlier):
        a, b = self.sums = self.sum_halves(*earlier)
        if direct_dp():
            self.hops = [
                core_hop(block, "dp", k, self.core) for k, block in ((1, a[1]), (2, b[0]), (3, b[1]))
            ]
        return self.sums

    def third_direct(self, *earlier):
        if not direct_dp():
            return sum(p.astype(F32) for p in self.scatter())
        return sum(p.astype(F32) for p in after([self.sums[0][0], *self.hops], *earlier))

    def second(self, *earlier):
        self.sums = self.sum_halves(*earlier)
        if direct_dp():
            self.across = core_hop(self.sums[1], "dp", 2, self.core)
        return self.sums

    def third(self, *earlier):
        if not direct_dp():
            self.pieces = self.scatter()
            return self.pieces
        a, across = after((self.sums[0], self.across), *earlier)
        self.pieces = [add_low(a[k], across[k]) for k in range(2)]
        return self.pieces


def last_dp(reductions, *earlier):
    if not direct_dp():
        return [r.pieces for r in reductions]
    high = max(r.pieces[0].shape[0] for r in reductions)
    block = [jnp.pad(r.pieces[1], ((0, high - r.pieces[1].shape[0]), (0, 0))) for r in reductions]
    got = core_hop(after(jnp.concatenate(block, 1), *earlier), "dp", 1, reductions[0].core)
    at, out = 0, []
    for r in reductions:
        rows, width = r.pieces[0].shape
        out.append([r.pieces[0], got[:rows, at : at + width]])
        at += width
    return out


VMEM_LIMIT = 48 * 1024 * 1024
CHUNK = 128


def takes(micros):
    return pl.CostEstimate(flops=int(micros * 1.1e9), bytes_accessed=0, transcendentals=0)


def params():
    return pltpu.CompilerParams(vmem_limit_bytes=VMEM_LIMIT)


ANY = pl.BlockSpec(memory_space=pl.ANY)
VM = pl.BlockSpec(memory_space=pltpu.VMEM)
SM = pl.BlockSpec(memory_space=pltpu.SMEM)


def sds(shape, dtype):
    return jax.ShapeDtypeStruct(shape, dtype)


def chunks(length, step=CHUNK):
    return [slice(i, i + step) for i in range(0, length, step)]


def norm_rows(z):
    centre = z - jnp.mean(z, -1, keepdims=True)
    spread = jnp.mean(centre * centre, -1, keepdims=True)
    scale = lax.rsqrt(spread + 1e-05)
    return centre * scale, scale


def norm_back_rows(d_out, gain, xhat, scale):
    g = d_out * gain
    m1 = jnp.mean(g, -1, keepdims=True)
    m2 = jnp.mean(g * xhat, -1, keepdims=True)
    return scale * (g - m1 - xhat * m2)


def gelu_parts(x):
    e = jnp.exp(-0.5 * x * x)
    t = 1.0 / (1.0 + 0.2316418882 * jnp.abs(x))
    poly = t * (
        0.127414796 + t * (-0.142248368 + t * (0.7107068705 + t * (-0.7265760135 + t * 0.5307027145)))
    )
    tail = poly * e
    cdf = jnp.where(x < 0.0, tail, 1.0 - tail)
    return x * cdf, cdf + x * e * 0.3989422804014327


def zrows(meta, k, rz):
    return pl.ds(pl.multiple_of(meta[1 + k], 64), rz)


def cut(start, width, at):
    if start < at < start + width:
        return [(start, at - start), (at, start + width - at)]
    return [(start, width)]


def load_weights(meta, pieces, base, places, sems):
    own, near0, far0, a0, b0, *halves = pieces
    rest, near, far, both = halves[0:2], halves[2:4], halves[4:6], halves[6:8]
    split0, split, count = a0.shape[1], rest[0].shape[2], rest[0].shape[0]
    home = meta[0] == 1
    lists = [[] for _ in places]
    at = 0
    for j in range(2):
        for k in range(count + 1):
            rows = zrows(meta, k, own.shape[0])
            for n, (start, width, place) in enumerate(places):
                offset = 0 if k else base
                for g, w in cut(offset + start, width, split if k else split0):
                    side, column = divmod(g, split if k else split0)
                    if k == 0:
                        mine = (near0 if j else own).at[:, pl.ds(g, w)]
                        other = (a0, b0)[side].at[:, pl.ds(column, w)] if j else far0.at[:, pl.ds(g, w)]
                    else:
                        mine, other = (
                            v[side].at[k - 1, :, pl.ds(column, w)] for v in ((near, both) if j else (rest, far))
                        )
                    dst = place(j, rows, g - offset - start, w)
                    first = pltpu.make_async_copy(mine, dst, sems.at[at])
                    second = pltpu.make_async_copy(other, dst, sems.at[at])
                    at += 1

                    @pl.when(home)
                    def _():
                        first.start()

                    @pl.when(jnp.logical_not(home))
                    def _():
                        second.start()

                    lists[n].append(first)
    return lists


def copies_of(rest):
    return 2 * 3 * (1 + rest.shape[0])


def wait_all(waits):
    for made in waits:
        made.wait()


def load_a(meta, pieces, w_a, sems):
    width = w_a.shape[2]
    return load_weights(
        meta, pieces, 0, [(0, width, lambda j, rows, c, w: w_a.at[j, rows, pl.ds(c, w)])], sems
    )[0]


def load_b(meta, pieces, w_i, w_f, sems):
    one = w_i.shape[1] // 2
    base = pieces[0].shape[1] - 2 * one
    return load_weights(
        meta,
        pieces,
        base,
        [
            (0, one, lambda j, rows, c, w: w_i.at[rows, pl.ds(j * one + c, w)]),
            (one, one, lambda j, rows, c, w: w_f.at[rows, pl.ds(j * one + c, w)]),
        ],
        sems,
    )


def attn_forward(level, meta, x_or_mid, parts, norms, pieces, bias, seg_col, seg_row, cols):
    four = 4 * cols
    length, width = x_or_mid.shape
    three = 3 * cols
    heads = 2 * cols // HD

    def body(meta, *refs):
        refs = list(refs)
        src = refs.pop(0)
        if level:
            own, other, gain, shift = (refs.pop(0) for _ in range(4))
        pieces = [refs.pop(0) for _ in range(13)]
        bias, sc, sr = (refs.pop(0) for _ in range(3))
        part_out, qkv_out, probs_out, ctx_out = (refs.pop(0) for _ in range(4))
        if level:
            x_out, xhat_out, scale_out = (refs.pop(0) for _ in range(3))
        w_a, sems = refs
        waits = load_a(meta, pieces, w_a, sems)
        if level:
            for rows in chunks(length):
                z = src[rows, :] + (own[rows, :].astype(F32) + other[rows, :].astype(F32)) + shift[2:3, :]
                xhat, scale = norm_rows(z)
                x_out[rows, :] = (xhat * gain[1:2, :] + shift[3:4, :]).astype(BF16)
                xhat_out[rows, :] = xhat.astype(BF16)
                scale_out[rows, :] = scale
            x_ref = x_out
        else:
            x_ref = src
        wait_all(waits)
        for j in range(2):
            c = slice(j * three, (j + 1) * three)
            for rows in chunks(length, 256):
                qkv_out[rows, c] = (nn(x_ref[rows, :], w_a[j, :, :three]) + bias[:, c]).astype(BF16)
        v_t = jnp.concatenate(
            [qkv_out[:, j * three + 2 * cols : (j + 1) * three].astype(F32) for j in range(2)], 1
        ).T.astype(BF16)
        for queries in chunks(length, 256):
            same = sc[...] == sr[:, queries]
            outs = []
            for h in range(heads):
                j, i = divmod(h, cols // HD)
                at = j * three + i * HD
                q = qkv_out[queries, at : at + HD]
                k = qkv_out[:, at + cols : at + cols + HD]
                st = jnp.where(same, nt(k, q) * 0.125, -1e30)
                p = jnp.exp(st - jnp.max(st, 0, keepdims=True))
                p = (p * (1.0 / jnp.sum(p, 0, keepdims=True))).astype(BF16)
                probs_out[h, :, queries] = p
                outs.append(nn(v_t[h * HD : (h + 1) * HD], p))
            ctx = jnp.concatenate(outs, 0).T.astype(BF16)
            ctx_out[queries, :] = ctx
            part_out[queries, :] = (
                nt(ctx[:, :cols], w_a[0, :, three:]) + nt(ctx[:, cols:], w_a[1, :, three:])
            ).astype(BF16)

    outs = [
        sds((length, width), BF16), sds((length, 2 * three), BF16),
        sds((heads, length, length), BF16), sds((length, 2 * cols), BF16),
    ]
    args = [meta, x_or_mid]
    if level:
        args += [*parts, *norms]
        outs += [sds((length, width), BF16), sds((length, width), BF16), sds((length, 1), F32)]
    specs = [SM] + [VM] * (len(args) - 1) + [ANY] * 13 + [VM] * 3
    args += [*pieces, bias, seg_col, seg_row]
    return pl.pallas_call(
        body,
        out_shape=outs,
        in_specs=specs,
        out_specs=[VM] * len(outs),
        scratch_shapes=[pltpu.VMEM((2, width, four), BF16), pltpu.SemaphoreType.DMA((copies_of(pieces[5]),))],
        compiler_params=params(),
        cost_estimate=takes(13),
        name="attn_forward",
    )(*args)


def ffn_forward(meta, x, parts, gains, shifts, pieces, bias_in, half):
    units = 2 * half
    length, width = x.shape

    def body(meta, x, own, other, gain, shift, p0, p1, p2, p3, p4, p5, p6, p7, p8, p9, p10, p11, p12, bias,
             part_out, mid_out, xhat_out, scale_out, act_out, slope_out, w_i, w_f, low, sems):
        first, second = load_b(meta, (p0, p1, p2, p3, p4, p5, p6, p7, p8, p9, p10, p11, p12), w_i, w_f, sems)
        for rows in chunks(length):
            z = x[rows, :].astype(F32) + (own[rows, :].astype(F32) + other[rows, :].astype(F32)) + shift[0:1, :]
            xhat, scale = norm_rows(z)
            mid = xhat * gain[0:1, :] + shift[1:2, :]
            mid_out[rows, :] = mid
            low[rows, :] = mid.astype(BF16)
            xhat_out[rows, :] = xhat.astype(BF16)
            scale_out[rows, :] = scale
        wait_all(first)
        for rows in chunks(length, 256):
            for c in chunks(units, 512):
                pre = nn(low[rows, :], w_i[:, c]) + bias[:, c]
                act, slope = gelu_parts(pre)
                act_out[rows, c] = act.astype(BF16)
                slope_out[rows, c] = slope.astype(BF16)
        wait_all(second)
        for rows in chunks(length, 256):
            part_out[rows, :] = nt(act_out[rows, :], w_f[...]).astype(BF16)

    return pl.pallas_call(
        body,
        out_shape=[
            sds((length, width), BF16), sds((length, width), F32), sds((length, width), BF16),
            sds((length, 1), F32), sds((length, units), BF16), sds((length, units), BF16),
        ],
        in_specs=[SM] + [VM] * 5 + [ANY] * 13 + [VM],
        out_specs=[VM] * 6,
        scratch_shapes=[
            pltpu.VMEM((width, units), BF16), pltpu.VMEM((width, units), BF16),
            pltpu.VMEM((length, width), BF16), pltpu.SemaphoreType.DMA((copies_of(pieces[5]),)),
        ],
        compiler_params=params(),
        cost_estimate=takes(9),
        name="ffn_forward",
    )(meta, x, *parts, gains, shifts, *pieces, bias_in)


def last_norm(mid, parts, gains, shifts, tok_row, cls_pos):
    length, width = mid.shape
    n_cls = cls_pos.shape[0]

    def body(cls, mid, own, other, gain, shift, tok, y_out, xhat_out, scale_out, cls_out):
        for rows in chunks(length):
            z = mid[rows, :] + (own[rows, :].astype(F32) + other[rows, :].astype(F32)) + shift[2:3, :]
            xhat, scale = norm_rows(z)
            y_out[rows, :] = (xhat * gain[1:2, :] + shift[3:4, :]).astype(BF16)
            xhat_out[rows, :] = xhat.astype(BF16)
            scale_out[rows, :] = scale
        which = lax.broadcasted_iota(jnp.int32, (16, length), 0)
        hot = jnp.zeros((16, length), F32)
        for p in range(n_cls):
            hot = jnp.where(jnp.logical_and(which == p, tok[...] == cls[p]), 1.0, hot)
        cls_out[...] = nn(hot.astype(BF16), y_out[...])[:n_cls].astype(BF16)

    return pl.pallas_call(
        body,
        out_shape=[
            sds((length, width), BF16), sds((length, width), BF16), sds((length, 1), F32),
            sds((n_cls, width), BF16),
        ],
        in_specs=[SM] + [VM] * 6,
        out_specs=[VM] * 4,
        compiler_params=params(),
        cost_estimate=takes(2),
        name="last_norm",
    )(cls_pos, mid, *parts, gains, shifts, tok_row)


def ffn_backward(level, meta, sources, xhat, scale, gains, slope, pieces, half):
    units = 2 * half
    length, width = xhat.shape
    n_cls = sources[3].shape[0] if level else 0

    def body(meta, *refs):
        refs = list(refs)
        if level:
            cls, grad, d_cls, tok = (refs.pop(0) for _ in range(4))
        else:
            d_above, own, other = (refs.pop(0) for _ in range(3))
        xhat, scale, gain, slope = (refs.pop(0) for _ in range(4))
        pieces = [refs.pop(0) for _ in range(13)]
        part_out, second_out, low_out, pre_out, vec_out, inb_out, w_i, w_f, sems = refs
        first, second = load_b(meta, pieces, w_i, w_f, sems)
        sums = [jnp.zeros((1, width), F32) for _ in range(3)]
        for rows in chunks(length):
            if level:
                d_out = grad[rows, :].astype(F32)
                for p in range(n_cls):
                    d_out = d_out + jnp.where(tok[rows, :] == cls[p], 1.0, 0.0) * d_cls[p : p + 1, :]
            else:
                d_out = d_above[rows, :] + (own[rows, :].astype(F32) + other[rows, :].astype(F32))
                d_out = d_out.astype(BF16).astype(F32)
            hat = xhat[rows, :].astype(F32)
            d_second = norm_back_rows(d_out, gain[1:2, :], hat, scale[rows, :])
            second_out[rows, :] = d_second
            low_out[rows, :] = d_second.astype(BF16)
            for n, item in enumerate((d_out * hat, d_out, d_second)):
                sums[n] = sums[n] + jnp.sum(item, 0, keepdims=True)
        for n in range(3):
            vec_out[n : n + 1, :] = sums[n]
        wait_all(second)
        for n, rows in enumerate(chunks(length, 256)):
            for c in chunks(units, units // 4):
                d_act = nn(low_out[rows, :], w_f[:, c])
                d_pre = (slope[rows, c].astype(F32) * d_act).astype(BF16)
                pre_out[rows, c] = d_pre
                j, at = divmod(c.start, units // 2)
                at = slice(at, at + c.stop - c.start)
                total = jnp.sum(d_pre.astype(F32), 0, keepdims=True)
                inb_out[j : j + 1, at] = total if n == 0 else inb_out[j : j + 1, at] + total
        wait_all(first)
        for rows in chunks(length, 256):
            part_out[rows, :] = nt(pre_out[rows, :], w_i[...]).astype(BF16)

    if level:
        token_grad, d_cls, tok_col, cls_pos = sources
        args, specs = [meta, cls_pos, token_grad, d_cls, tok_col], [SM, SM, VM, VM, VM]
    else:
        args, specs = [meta, *sources], [SM, VM, VM, VM]
    args += [xhat, scale, gains, slope, *pieces]
    specs += [VM] * 4 + [ANY] * 13
    return pl.pallas_call(
        body,
        out_shape=[
            sds((length, width), BF16), sds((length, width), F32), sds((length, width), BF16),
            sds((length, units), BF16), sds((3, width), F32), sds((2, units // 2), F32),
        ],
        in_specs=specs,
        out_specs=[VM] * 6,
        scratch_shapes=[
            pltpu.VMEM((width, units), BF16), pltpu.VMEM((width, units), BF16),
            pltpu.SemaphoreType.DMA((copies_of(pieces[5]),)),
        ],
        compiler_params=params(),
        cost_estimate=takes(9),
        name="ffn_backward",
    )(*args)


def grads_of(nz, rz, width):
    half = nz // 2
    return [sds((nz, rz, width), BF16), sds((half, rz, width), BF16), sds((half, rz, width), BF16)]


def put_grad(outs, j, k, nz, column, value, first=0):
    half, (height, width) = nz // 2, value.shape
    if k < half:
        out, at = outs[0], k + (half if j == 0 else 0)
    else:
        out, at = outs[2 if j == 0 else 1], k - half
    out[at, first : first + height, column : column + width] = value.astype(BF16)


def ffn_grads(meta, mid, d_pre, d_ffn, act, nz):
    length, width = mid.shape
    units = d_pre.shape[1]
    one = units // 2
    rz = width // nz

    def body(meta, mid, d_pre, d_ffn, act, *refs):
        outs, (mid_t, ffn_t) = refs[:3], refs[3:]
        mid_t[...] = mid[...].T.astype(BF16)
        ffn_t[...] = d_ffn[...].astype(F32).T.astype(BF16)
        for j in range(2):
            c = slice(j * one, (j + 1) * one)
            for k in range(nz):
                rows = zrows(meta, k, rz)
                put_grad(outs, j, k, nz, 0, nn(mid_t[rows, :], d_pre[:, c]))
                put_grad(outs, j, k, nz, one, nn(ffn_t[rows, :], act[:, c]))

    return pl.pallas_call(
        body,
        out_shape=grads_of(nz, rz, units),
        in_specs=[SM] + [VM] * 4,
        out_specs=[VM] * 3,
        scratch_shapes=[pltpu.VMEM((width, length), BF16)] * 2,
        compiler_params=params(),
        cost_estimate=takes(7),
        name="ffn_grads",
    )(meta, mid, d_pre, d_ffn, act)


def attn_backward(meta, d_second, parts, xhat, scale, gains, qkv, probs, pieces, cols):
    four = 4 * cols
    length, width = d_second.shape
    three = 3 * cols
    heads = 2 * cols // HD

    def body(meta, d_second, own, other, xhat, scale, gain, qkv, probs, p0, p1, p2, p3, p4, p5, p6, p7, p8, p9, p10, p11, p12,
             part_out, first_out, low_out, dqkv_out, vec_out, sum_out,
             w_a, d_ctx, acc_v, acc_k, sems):
        waits = load_a(meta, (p0, p1, p2, p3, p4, p5, p6, p7, p8, p9, p10, p11, p12), w_a, sems)
        sums = [jnp.zeros((1, width), F32) for _ in range(3)]
        for rows in chunks(length):
            d_mid = d_second[rows, :] + (own[rows, :].astype(F32) + other[rows, :].astype(F32))
            hat = xhat[rows, :].astype(F32)
            d_first = norm_back_rows(d_mid, gain[0:1, :], hat, scale[rows, :])
            first_out[rows, :] = d_first
            low_out[rows, :] = d_first.astype(BF16)
            for n, item in enumerate((d_mid * hat, d_mid, d_first)):
                sums[n] = sums[n] + jnp.sum(item, 0, keepdims=True)
        for n in range(3):
            vec_out[n : n + 1, :] = sums[n]
        wait_all(waits)
        for j in range(2):
            for rows in chunks(length, 256):
                d_ctx[rows, j * cols : (j + 1) * cols] = nn(low_out[rows, :], w_a[j, :, three:]).astype(BF16)
        k_t = jnp.concatenate(
            [qkv[:, j * three + cols : j * three + 2 * cols].astype(F32) for j in range(2)], 1
        ).T.astype(BF16)
        for h in range(heads):
            j, i = divmod(h, cols // HD)
            at = j * three + i * HD
            q_cols, k_cols, v_cols = (slice(at + n * cols, at + n * cols + HD) for n in range(3))
            for n, queries in enumerate(chunks(length, 256)):
                d_o = d_ctx[queries, h * HD : (h + 1) * HD]
                d_p = nt(qkv[:, v_cols], d_o)
                p = probs[h, :, queries]
                wide = p.astype(F32)
                d_s = (wide * (d_p - jnp.sum(wide * d_p, 0, keepdims=True))).astype(BF16)
                d_v = nn(p, d_o)
                d_k = nn(d_s, qkv[queries, q_cols])
                acc_v[...] = d_v if n == 0 else acc_v[...] + d_v
                acc_k[...] = d_k if n == 0 else acc_k[...] + d_k
                d_q = nn(k_t[h * HD : (h + 1) * HD], d_s)
                dqkv_out[queries, q_cols] = (d_q.T * 0.125).astype(BF16)
            dqkv_out[:, v_cols] = acc_v[...].astype(BF16)
            dqkv_out[:, k_cols] = (acc_k[...] * 0.125).astype(BF16)
        for j in range(2):
            sum_out[j : j + 1, :] = jnp.sum(
                dqkv_out[:, j * three : (j + 1) * three].astype(F32), 0, keepdims=True
            )
        for rows in chunks(length, 256):
            part_out[rows, :] = (
                nt(dqkv_out[rows, :three], w_a[0, :, :three]) + nt(dqkv_out[rows, three:], w_a[1, :, :three])
            ).astype(BF16)

    return pl.pallas_call(
        body,
        out_shape=[
            sds((length, width), BF16), sds((length, width), F32), sds((length, width), BF16),
            sds((length, 2 * three), BF16), sds((3, width), F32), sds((2, three), F32),
        ],
        in_specs=[SM] + [VM] * 8 + [ANY] * 13,
        out_specs=[VM] * 6,
        scratch_shapes=[
            pltpu.VMEM((2, width, four), BF16), pltpu.VMEM((length, 2 * cols), BF16),
            pltpu.VMEM((length, HD), F32), pltpu.VMEM((length, HD), F32),
            pltpu.SemaphoreType.DMA((copies_of(pieces[5]),)),
        ],
        compiler_params=params(),
        cost_estimate=takes(15),
        name="attn_backward",
    )(meta, d_second, *parts, xhat, scale, gains, qkv, probs, *pieces)


def attn_grads(meta, places, x, d_attn, d_qkv, ctx, vectors, nz, extra):
    length, width = x.shape
    three = d_qkv.shape[1] // 2
    cols = ctx.shape[1] // 2
    rz = width // nz

    def body(meta, places, x, d_attn, d_qkv, ctx, vec1, vec2, sum_qkv, sum_inb, *refs):
        outs, (x_t, a_t, norm_rows_, qv_rows, inb_rows) = refs[:3], refs[3:]
        x_t[...] = x[...].astype(F32).T.astype(BF16)
        a_t[...] = d_attn[...].astype(F32).T.astype(BF16)
        for j in range(2):
            for k in range(nz):
                rows = zrows(meta, k, rz)
                grad = nn(x_t[rows, :], d_qkv[:, j * three : (j + 1) * three])
                put_grad(outs, j, k, nz, 0, grad)
                put_grad(outs, j, k, nz, three, nn(a_t[rows, :], ctx[:, j * cols : (j + 1) * cols]))
        if not extra:
            return
        piece, part = width // (4 * nz), cols // nz
        units = sum_inb.shape[1] // nz
        norm_rows_[...] = jnp.zeros_like(norm_rows_)
        norm_rows_[0:3, :] = vec1[...]
        norm_rows_[3:6, :] = vec2[...]
        for j in range(2):
            qv_rows[...] = jnp.zeros_like(qv_rows)
            qv_rows[0:1, :cols] = sum_qkv[j : j + 1, :cols]
            qv_rows[1:2, :cols] = sum_qkv[j : j + 1, 2 * cols : three]
            inb_rows[...] = jnp.zeros_like(inb_rows)
            inb_rows[0:1, :] = sum_inb[j : j + 1, :]
            for k in range(nz):
                d = places[2 + k]
                from_norm = pltpu.roll(norm_rows_[...], width - (d * 4 + places[j]) * piece, 1)
                from_qv = pltpu.roll(qv_rows[...], width - d * part, 1)
                from_inb = pltpu.roll(inb_rows[...], width - d * units, 1)
                lane = lax.broadcasted_iota(jnp.int32, (8, 2 * cols), 1)
                upper = jnp.where(lane < piece, from_norm[:, : 2 * cols], 0.0)
                lower = jnp.where(lane < part, from_qv[:, : 2 * cols], 0.0)
                shifted = pltpu.roll(from_inb, 128, 1)[:, : 2 * cols]
                inside = jnp.logical_and(lane >= 128, lane < 128 + units)
                lower = jnp.where(inside, shifted, lower)
                put_grad(outs, j, k, nz, 0, jnp.concatenate([upper, lower], 0), rz)
                put_grad(outs, j, k, nz, 2 * cols, jnp.zeros((extra, 2 * cols), F32), rz)

    return pl.pallas_call(
        body,
        out_shape=grads_of(nz, rz + extra, three + cols),
        in_specs=[SM, SM] + [VM] * 8,
        out_specs=[VM] * 3,
        scratch_shapes=[pltpu.VMEM((width, length), BF16)] * 2 + [pltpu.VMEM((8, width), F32)] * 3,
        compiler_params=params(),
        cost_estimate=takes(4),
        name="attn_grads",
    )(meta, places, x, d_attn, d_qkv, ctx, *vectors)


def loss_kernel(own, perm, slots, queries, positive_col, n_own):
    n_q, width = queries.shape
    n_p = slots.shape[0]

    def body(own, perm, slots, queries, pos, loss_out, d_out):
        passages = nn(perm[...], slots[...]).astype(BF16)
        logits = nt(queries[...], passages)
        top = jnp.max(logits, -1, keepdims=True)
        log_total = top + jnp.log(jnp.sum(jnp.exp(logits - top), -1, keepdims=True))
        index = lax.broadcasted_iota(jnp.int32, (n_q, n_p), 1)
        hits = pos[...] == index
        chosen = jnp.sum(jnp.where(hits, logits, 0.0), -1, keepdims=True)
        loss_out[...] = jnp.sum(log_total - chosen, 0, keepdims=True) / n_q
        d_logits = (16.0 * (jnp.exp(logits - log_total) - jnp.where(hits, 1.0, 0.0))).astype(BF16)
        pick = jnp.where(
            lax.broadcasted_iota(jnp.int32, (n_p, 128), 0)
            == lax.broadcasted_iota(jnp.int32, (n_p, 128), 1) + own[0],
            1.0, 0.0,
        ).astype(BF16)
        cols = nn(d_logits, pick)
        d_out[...] = nn(cols.T.astype(BF16), queries[...])[:n_own]

    return pl.pallas_call(
        body,
        out_shape=[sds((1, 1), F32), sds((n_own, width), F32)],
        in_specs=[SM] + [VM] * 4,
        out_specs=[VM] * 2,
        compiler_params=params(),
        cost_estimate=takes(1),
        name="contrast",
    )(own, perm, slots, queries, positive_col)


def on_device(
    inputs, cls_pos, w_qkv, qv_bias, w_out, w_in, in_bias, w_ffn_out,
    layer_gains, shifts, queries, positive, token_grad,
):
    core = lax.axis_index("section")
    dp = lax.axis_index("dp")
    me = lax.axis_index("tensor")
    n_dp = lax.axis_size("dp")
    n_t = lax.axis_size("tensor")
    first_core = core == 0
    rows_dev, share, width = inputs.shape
    cols = w_qkv.shape[3]
    units = w_in.shape[2]
    length = n_t * share
    n_chips = n_dp * n_t
    piece = width // n_chips
    order = dp_order()
    direct = direct_dp()
    nz, extra = (4, 16) if direct else (2, 0)
    t_ids = jnp.arange(n_t, dtype=jnp.int32)

    vec = jnp.concatenate(
        [layer_gains.reshape(-1), shifts.reshape(-1), qv_bias.reshape(-1), in_bias.reshape(-1)]
    )
    n_gain, n_shift, n_qv, n_inb = layer_gains.size, shifts.size, qv_bias.size, in_bias.size
    n_vec = vec.shape[0]
    flat = jnp.concatenate(
        [vec, queries.reshape(-1), (positive // 16).astype(BF16), (positive % 16).astype(BF16)]
    )
    flat = jnp.pad(flat, (0, -flat.shape[0] % 2048)).reshape(-1, 128)

    def spread_rows(block):
        blocks = [lax.dynamic_index_in_dim(block, me ^ k, 0, keepdims=False) for k in range(n_t)]
        return jnp.concatenate(exchange_rows(blocks), 0)

    pack = jnp.concatenate(
        [w_qkv[0, :, 0], w_qkv[0, :, 1], w_qkv[0, :, 2], w_out[0].T, w_in[0], w_ffn_out[0].T], 1
    )
    message = spread_dp(flat)
    if direct:
        own = pack
        z_a = rest_dp(after(pack[:, :width], message))
    else:
        pack = lax.all_gather(pack, "dp", axis=0, tiled=True)
        own, other_rows = pack[: width // 2], pack[width // 2 :][None]
    message = spread_tensor(message)
    near0, far0 = gather_own(after(own, message))
    both0 = gather_own_both(near0, far0)
    owns = [own, near0, far0, *both0]
    rows_in = spread_rows(after(jnp.where(first_core, inputs, token_grad), near0, far0))

    def halves_of(blocks, first, size, *earlier):
        half = size // 2
        if not direct:
            blocks = other_rows[:, :, first : first + size]
            return blocks[:, :, :half], blocks[:, :, half:]
        blocks = after(blocks, *earlier)
        return jnp.stack([b[:, :half] for b in blocks]), jnp.stack([b[:, half:] for b in blocks])

    rest_a = halves_of(z_a if direct else None, 0, width, near0)
    near_a = gather_near(rest_a)
    if direct:
        z_b = rest_dp(after(pack[:, width:], rest_a))
    both_a = gather_both(after(near_a, both0, z_b[:1] if direct else both0))
    rows_got = swap_cores(after(rows_in, near_a))
    x_low = jnp.where(first_core, rows_in, rows_got)
    tokens = jnp.where(first_core, rows_got, rows_in)
    rest_b = halves_of(z_b if direct else None, width, 2 * units, both_a)
    near_b = gather_near(rest_b)
    pieces_a = [*owns, *rest_a, *near_a, *both_a]

    zrow = order * (width // n_dp) if direct else jnp.arange(2, dtype=jnp.int32) * (width // 2)
    metas = [
        jnp.concatenate([(core == level)[None].astype(jnp.int32), zrow.astype(jnp.int32)])
        for level in range(2)
    ]
    slots = [me ^ (2 * (core != level) + jnp.arange(2, dtype=jnp.int32)) for level in range(2)]
    places = [jnp.concatenate([s, order[:nz]]).astype(jnp.int32) for s in slots]
    hots = [(s[:, None] == t_ids[None, :]).astype(F32) for s in slots]

    positions = jnp.concatenate(
        [(me ^ k) * share + jnp.arange(share, dtype=jnp.int32) for k in range(n_t)]
    )
    cls_row = lax.dynamic_index_in_dim(cls_pos, me, 0, keepdims=False)
    segments = jnp.sum((positions[:, None] >= cls_row[None, :]).astype(jnp.int32), -1)
    seg_col, seg_row = segments[:, None], segments[None, :]
    tok_col, tok_row = positions[:, None], positions[None, :]

    slot_ids = (order[None, :] * n_t + (me ^ t_ids)[:, None]).reshape(-1)
    to_natural = (jnp.arange(n_chips, dtype=jnp.int32)[:, None] == slot_ids[None, :]).astype(BF16)
    table = nn(to_natural, message.reshape(n_chips, -1))
    own_table = table[:, :n_vec].astype(BF16)
    other_table = swap_cores(own_table)
    tables = jnp.where(
        first_core, jnp.stack([own_table, other_table]), jnp.stack([other_table, own_table])
    ).astype(F32)
    at = 0
    gains = tables[:, :, at : at + n_gain].reshape(2, n_chips, 2, piece).transpose(0, 2, 1, 3).reshape(2, 2, width)
    at += n_gain
    shift = tables[:, :, at : at + n_shift].reshape(2, n_chips, 4, piece).transpose(0, 2, 1, 3).reshape(2, 4, width)
    at += n_shift
    qv = tables[:, :, at : at + n_qv].reshape(2, n_dp, n_t, 2, cols // n_dp)
    qv = qv.transpose(0, 3, 2, 1, 4).reshape(2, 2, n_t, cols)
    at += n_qv
    inb = tables[:, :, at : at + n_inb].reshape(2, n_dp, n_t, n_inb).transpose(0, 2, 1, 3).reshape(2, n_t, units)
    vectors = []
    for level in range(2):
        bias = jnp.sum(hots[level][None, :, :, None] * qv[level][:, None], 2)
        bias = jnp.stack([bias[0], jnp.zeros_like(bias[0]), bias[1]], 1).reshape(1, -1)
        bias_in = jnp.sum(hots[level][:, :, None] * inb[level][None], 1).reshape(1, -1)
        vectors.append((gains[level], shift[level], bias, bias_in))
    at = n_vec
    q_dev = queries.shape[0]
    all_q = table[:, at : at + q_dev * width].reshape(-1, width).astype(BF16)
    at += q_dev * width
    all_pos = table[:, at : at + q_dev] * 16.0 + table[:, at + q_dev : at + 2 * q_dev]
    all_pos = all_pos.astype(jnp.int32).reshape(-1, 1)
    n_cls = cls_row.shape[0]
    perm = jnp.repeat(jnp.repeat(to_natural, n_cls, 0), n_cls, 1)
    perm = perm * jnp.tile(jnp.eye(n_cls, dtype=BF16), (n_chips, n_chips))

    vectors, all_q, all_pos, perm, x_low = lax.optimization_barrier(
        (vectors, all_q, all_pos, perm, x_low)
    )
    saved = []
    source, parts, norms = x_low, None, None
    for level in range(2):
        gain, shift, bias, bias_in = vectors[level]
        outs = attn_forward(
            level, metas[level], source, parts, norms, pieces_a, bias, seg_col, seg_row, cols
        )
        part, qkv, probs, ctx = outs[:4]
        if level == 0:
            pieces_b = [*owns, *rest_b, *near_b, *gather_both(after(near_b, part))]
        if level:
            x, xhat2, scale2 = outs[4:]
            saved[0]["second"] = (xhat2, scale2)
        else:
            x = x_low
        part, mid, xhat1, scale1, act, slope = ffn_forward(
            metas[level], x, (part, swap_cores(part)), gain, shift, pieces_b, bias_in, units
        )
        saved.append(
            dict(x=x, qkv=qkv, probs=probs, ctx=ctx, mid=mid, xhat1=xhat1, scale1=scale1, act=act, slope=slope)
        )
        source, parts, norms = mid, (part, swap_cores(part)), (gain, shift)
    y, xhat2, scale2, cls_own = last_norm(source, parts, *norms, tok_row, cls_row)
    saved[1]["second"] = (xhat2, scale2)

    cls_slots = spread_tensor(spread_dp(cls_own)).reshape(n_chips * n_cls, width)
    first_own = ((dp * n_t + me) * n_cls).astype(jnp.int32)[None]
    mean_loss, d_cls = loss_kernel(first_own, perm, cls_slots, all_q, all_pos, n_cls)

    vector_rows = [None, None]
    sources = (tokens, d_cls, tok_col, cls_row)
    sums_a, sums_b = [None, None], [None, None]
    for level in (1, 0):
        gain = vectors[level][0]
        kept = saved[level]
        meta = metas[level]
        xhat2, scale2 = kept["second"]
        if level == 0:
            sources = (after(sources[0], sums_b[1].first(grads_a[1])), *sources[1:])
        part, d_second, d_ffn, d_pre, vec2, sum_inb = ffn_backward(
            level, meta, sources, xhat2, scale2, gain, kept["slope"], pieces_b, units
        )
        other = swap_cores(part)
        if level == 0:
            d_ffn = after(d_ffn, sums_a[1].first(part))
        grads_b = ffn_grads(meta, kept["mid"], d_pre, d_ffn, kept["act"], nz)
        sums_b[level] = Reduction(grads_b, level)
        d_second = after(d_second, grads_b[1])
        if level == 0:
            d_second = after(d_second, sums_b[1].second(grads_b[1]))
        part, d_first, d_attn, d_qkv, vec1, sum_qkv = attn_backward(
            meta, d_second, (part, other), kept["xhat1"], kept["scale1"], gain,
            kept["qkv"], kept["probs"], pieces_a, cols,
        )
        other = swap_cores(part)
        if level == 0:
            d_attn = after(d_attn, sums_b[0].first(sums_a[1].second(part)))
        grads_a = attn_grads(
            meta, places[level], kept["x"], d_attn, d_qkv, kept["ctx"], (vec1, vec2, sum_qkv, sum_inb), nz, extra
        )
        sums_a[level] = Reduction(grads_a, level)
        vector_rows[level] = (vec1, vec2, sum_qkv, sum_inb)
        sources = (d_first, part, other)
    sums_b[1].third(grads_a[1])
    sums_b[0].second_direct(sums_b[1].pieces)
    sums_a[1].third(sums_b[0].sums)
    sums_a[0].first(sums_a[1].pieces, sums_b[0].hops[1:2] if direct else sums_b[0].sums)
    sums_a[0].second_direct(sums_a[0].added)
    last_a1, last_b1 = last_dp([sums_a[1], sums_b[1]], sums_a[0].sums)
    total_b0 = sums_b[0].third_direct()
    d_hidden = d_first + (part.astype(F32) + other.astype(F32))
    outgoing = jnp.where(first_core, d_hidden, y.astype(F32))
    low = after(outgoing.astype(BF16), sums_a[0].added).reshape(n_t, share, width)
    incoming = [outgoing[:share]] + [b.astype(F32) for b in exchange_rows([low[k] for k in range(n_t)])[1:]]
    boundary = jnp.zeros((n_t, share, width), F32)
    for k in range(n_t):
        boundary = lax.dynamic_update_index_in_dim(boundary, incoming[k], me ^ k, 0)
    tot_b, tot_a = (
        jnp.where(first_core, low, sum(p.astype(F32) for p in high))
        for low, high in ((total_b0, last_b1), (sums_a[0].third_direct(), last_a1))
    )
    if direct:
        end = width // n_dp
        own = tot_a[end : end + 6, :piece]
        qv = tot_a[end + 8 : end + 10, : qv_bias.shape[3]]
        grad_inb = tot_a[end + 8 : end + 9, 128 : 128 + n_inb]
        tot_a = tot_a[:end]
    else:
        tables = []
        for level in range(2):
            vec1, vec2, sum_qkv, sum_inb = vector_rows[level]
            by_t = lax.dot_general(
                hots[level], jnp.concatenate([sum_qkv, sum_inb], 1), (((0,), (0,)), ((), ())),
                precision=lax.Precision.HIGHEST,
            )
            whole = 0.5 * jnp.concatenate([vec1, vec2])
            whole = jnp.pad(whole, ((0, 0), (0, by_t.shape[1] - width)))
            tables.append(jnp.concatenate([whole, by_t]))
        tables = lax.psum(jnp.stack(tables), ("section", "dp", "tensor"))
        flat = jnp.where(first_core, tables[0], tables[1])
        own = lax.dynamic_slice_in_dim(flat[:6, :width], (dp * n_t + me) * piece, piece, 1)
        by_t = lax.dynamic_slice_in_dim(flat, 6 + me, 1, 0)
        qv = jnp.concatenate([by_t[:, :cols], by_t[:, 2 * cols : 3 * cols]])
        qv = lax.dynamic_slice_in_dim(qv, dp * qv_bias.shape[3], qv_bias.shape[3], 1)
        grad_inb = lax.dynamic_slice_in_dim(by_t[:, 3 * cols :], dp * n_inb, n_inb, 1)
    grad_gains = jnp.concatenate([own[0:1], own[3:4]]).reshape(layer_gains.shape)
    grad_shifts = jnp.concatenate([own[2:3], own[1:2], own[5:6], own[4:5]]).reshape(shifts.shape)
    grad_qv, grad_inb = qv.reshape(qv_bias.shape), grad_inb.reshape(in_bias.shape)

    grad_qkv = jnp.stack([tot_a[:, n * cols : (n + 1) * cols] for n in range(3)], 1)[None]
    grad_out = tot_a[:, 3 * cols :].T[None]
    grad_in = tot_b[:, :units][None]
    grad_ffn = tot_b[:, units:].T[None]
    return (
        grad_qkv, grad_qv, grad_out, grad_in, grad_inb, grad_ffn,
        grad_gains, grad_shifts, boundary[None], mean_loss.reshape(()),
    )


def solution(mesh):
    return jax.shard_map(
        on_device,
        mesh=mesh,
        in_specs=(
            P("dp", "tensor", None),
            P("dp", None),
            P("section", "dp", None, "tensor"),
            P("section", None, "tensor", "dp"),
            P("section", "tensor", "dp"),
            P("section", "dp", "tensor"),
            P("section", "tensor", "dp"),
            P("section", "tensor", "dp"),
            P("section", None, ("dp", "tensor")),
            P("section", None, ("dp", "tensor")),
            P(("dp", "tensor"), None),
            P(("dp", "tensor")),
            P("dp", "tensor", None),
        ),
        out_specs=(
            P("section", "dp", None, "tensor"),
            P("section", None, "tensor", "dp"),
            P("section", "tensor", "dp"),
            P("section", "dp", "tensor"),
            P("section", "tensor", "dp"),
            P("section", "tensor", "dp"),
            P("section", None, ("dp", "tensor")),
            P("section", None, ("dp", "tensor")),
            P("section", "dp", "tensor", None),
            P(),
        ),
        check_vma=False,
    )
```

```python
import jax
import jax.numpy as jnp
from jax import lax
from jax.experimental import pallas as pl
from jax.experimental.pallas import tpu as pltpu
from jax.sharding import PartitionSpec as P

HD = 64
PARTNER = 1
CROSS = 2
BF16 = jnp.bfloat16
F32 = jnp.float32


def mm(left, right, dims):
    return lax.dot_general(left, right, (dims, ((), ())), preferred_element_type=F32)


def nn(left, right):
    return mm(left, right, ((1,), (0,)))


def nt(left, right):
    return mm(left, right, ((1,), (1,)))


def after(block, *earlier):
    return lax.optimization_barrier((block, *earlier))[0]


def swap_cores(block):
    return lax.ppermute(block, "section", [(0, 1), (1, 0)])


def hop(block, axis, flip):
    return lax.ppermute(block, axis, [(i, i ^ flip) for i in range(lax.axis_size(axis))])


def core_hop(block, axis, flip, core):
    size = lax.axis_size(axis)
    route = [(core * size + i, core * size + (i ^ flip)) for i in range(size)]
    return lax.ppermute(block, ("section", axis), route)


def cross_hop(block, source):
    size = lax.axis_size("tensor")
    route = [(source * size + i, (1 - source) * size + (i ^ CROSS)) for i in range(size)]
    return lax.ppermute(block, ("section", "tensor"), route)


def direct_dp():
    return lax.axis_size("dp") == 4


def dp_order():
    size = lax.axis_size("dp")
    if direct_dp():
        return lax.axis_index("dp") ^ jnp.arange(size, dtype=jnp.int32)
    return jnp.arange(size, dtype=jnp.int32)


def spread_dp(block):
    if direct_dp():
        return jnp.stack([block] + [hop(block, "dp", k) for k in range(1, 4)])
    return lax.all_gather(block, "dp", axis=0, tiled=False)


def spread_tensor(block):
    return jnp.stack([block] + [hop(block, "tensor", k) for k in range(1, 4)])


def double(block, axis):
    pair = jnp.stack([block, hop(block, axis, 1)])
    return jnp.concatenate([pair, hop(pair, axis, 2)])


def exchange_rows(blocks):
    first = hop(jnp.stack([blocks[1], blocks[3]]), "tensor", 1)
    second = hop(jnp.stack([blocks[2], first[1]]), "tensor", 2)
    return [blocks[0], first[0], second[0], second[1]]


def cross_all(block):
    size = lax.axis_size("tensor")
    route = [(s * size + i, (1 - s) * size + (i ^ CROSS)) for s in range(2) for i in range(size)]
    return lax.ppermute(block, ("section", "tensor"), route)


def rest_dp(own):
    return [hop(own, "dp", k) for k in range(1, 4)]


def gather_own(own):
    near, far = hop(own, "tensor", PARTNER), cross_all(own)
    return near, far


def gather_own_both(near, far):
    half = near.shape[1] // 2
    return cross_all(near[:, :half]), hop(far[:, half:], "tensor", PARTNER)


def gather_near(rest):
    a, b = rest
    near_a, far_b = hop(a, "tensor", PARTNER), cross_all(b)
    near_b, far_a = hop(b, "tensor", PARTNER), cross_all(a)
    return near_a, near_b, far_a, far_b


def gather_both(near_a, far_b):
    return cross_all(near_a), hop(far_b, "tensor", PARTNER)


def add_low(*items):
    total = items[0].astype(F32)
    for item in items[1:]:
        total = total + item.astype(F32)
    return total.astype(BF16)


class Reduction:
    def __init__(self, grads, core):
        self.core = core
        self.pair, self.next_b, self.own_b = grads
        self.got = cross_hop(self.pair, 1 - core)
        self.near_b = hop(self.next_b, "tensor", PARTNER)

    def first(self, *earlier):
        half = self.next_b.shape[0]
        self.parts = pair, own_b, got, near_b = after((self.pair, self.own_b, self.got, self.near_b), *earlier)
        self.added = add_low(pair[:half], got[:half]), add_low(own_b, near_b)
        self.near_a = core_hop(self.added[0], "tensor", PARTNER, self.core)
        self.far_b = cross_hop(self.added[1], 1 - self.core)
        return self.added

    def sum_halves(self, *earlier):
        half = self.next_b.shape[0]
        near_a, far_b, (pair, own_b, got, near_b) = after((self.near_a, self.far_b, self.parts), *earlier)
        return add_low(pair[half:], got[half:], near_a), add_low(own_b, near_b, far_b)

    def scatter(self):
        whole = jnp.concatenate(self.sums).reshape(-1, self.own_b.shape[2])
        return [lax.psum_scatter(whole, "dp", scatter_dimension=0, tiled=True)]

    def second_direct(self, *earlier):
        a, b = self.sums = self.sum_halves(*earlier)
        if direct_dp():
            self.hops = [
                core_hop(block, "dp", k, self.core) for k, block in ((1, a[1]), (2, b[0]), (3, b[1]))
            ]
        return self.sums

    def third_direct(self, *earlier):
        if not direct_dp():
            return sum(p.astype(F32) for p in self.scatter())
        return sum(p.astype(F32) for p in after([self.sums[0][0], *self.hops], *earlier))

    def second(self, *earlier):
        self.sums = self.sum_halves(*earlier)
        if direct_dp():
            self.across = core_hop(self.sums[1], "dp", 2, self.core)
        return self.sums

    def third(self, *earlier):
        if not direct_dp():
            self.pieces = self.scatter()
            return self.pieces
        a, across = after((self.sums[0], self.across), *earlier)
        self.pieces = [add_low(a[k], across[k]) for k in range(2)]
        return self.pieces


def last_dp(reductions, *earlier):
    if not direct_dp():
        return [r.pieces for r in reductions]
    high = max(r.pieces[0].shape[0] for r in reductions)
    block = [jnp.pad(r.pieces[1], ((0, high - r.pieces[1].shape[0]), (0, 0))) for r in reductions]
    got = core_hop(after(jnp.concatenate(block, 1), *earlier), "dp", 1, reductions[0].core)
    at, out = 0, []
    for r in reductions:
        rows, width = r.pieces[0].shape
        out.append([r.pieces[0], got[:rows, at : at + width]])
        at += width
    return out


VMEM_LIMIT = 48 * 1024 * 1024
CHUNK = 128


def takes(micros):
    return pl.CostEstimate(flops=int(micros * 1.1e9), bytes_accessed=0, transcendentals=0)


def params():
    return pltpu.CompilerParams(vmem_limit_bytes=VMEM_LIMIT)


ANY = pl.BlockSpec(memory_space=pl.ANY)
VM = pl.BlockSpec(memory_space=pltpu.VMEM)
SM = pl.BlockSpec(memory_space=pltpu.SMEM)


def sds(shape, dtype):
    return jax.ShapeDtypeStruct(shape, dtype)


def chunks(length, step=CHUNK):
    return [slice(i, i + step) for i in range(0, length, step)]


def norm_rows(z):
    centre = z - jnp.mean(z, -1, keepdims=True)
    spread = jnp.mean(centre * centre, -1, keepdims=True)
    scale = lax.rsqrt(spread + 1e-05)
    return centre * scale, scale


def norm_back_rows(d_out, gain, xhat, scale):
    g = d_out * gain
    m1 = jnp.mean(g, -1, keepdims=True)
    m2 = jnp.mean(g * xhat, -1, keepdims=True)
    return scale * (g - m1 - xhat * m2)


def gelu_parts(x):
    e = jnp.exp(-0.5 * x * x)
    t = 1.0 / (1.0 + 0.2316418882 * jnp.abs(x))
    poly = t * (
        0.127414796 + t * (-0.142248368 + t * (0.7107068705 + t * (-0.7265760135 + t * 0.5307027145)))
    )
    tail = poly * e
    cdf = jnp.where(x < 0.0, tail, 1.0 - tail)
    return x * cdf, cdf + x * e * 0.3989422804014327


def zrows(meta, k, rz):
    return pl.ds(pl.multiple_of(meta[1 + k], 64), rz)


def cut(start, width, at):
    if start < at < start + width:
        return [(start, at - start), (at, start + width - at)]
    return [(start, width)]


def load_weights(meta, pieces, base, places, sems):
    own, near0, far0, a0, b0, *halves = pieces
    rest, near, far, both = halves[0:2], halves[2:4], halves[4:6], halves[6:8]
    split0, split, count = a0.shape[1], both[0].shape[2], rest[0].shape[0]
    home = meta[0] == 1
    lists = [[] for _ in places]
    at = 0
    for j in range(2):
        for k in range(count + 1):
            rows = zrows(meta, k, own.shape[0])
            for n, (start, width, place) in enumerate(places):
                offset = 0 if k else base
                for g, w in cut(offset + start, width, split if k else split0):
                    side, column = divmod(g, split if k else split0)
                    if k == 0:
                        mine = (near0 if j else own).at[:, pl.ds(g, w)]
                        other = (a0, b0)[side].at[:, pl.ds(column, w)] if j else far0.at[:, pl.ds(g, w)]
                    else:
                        mine, other = (
                            v[side].at[k - 1, :, pl.ds(g if v[0].shape[2] > split else column, w)]
                            for v in ((near, both) if j else (rest, far))
                        )
                    dst = place(j, rows, g - offset - start, w)
                    first = pltpu.make_async_copy(mine, dst, sems.at[at])
                    second = pltpu.make_async_copy(other, dst, sems.at[at])
                    at += 1

                    @pl.when(home)
                    def _():
                        first.start()

                    @pl.when(jnp.logical_not(home))
                    def _():
                        second.start()

                    lists[n].append(first)
    return lists


def copies_of(rest):
    return 2 * 3 * (1 + rest.shape[0])


def wait_all(waits):
    for made in waits:
        made.wait()


def load_a(meta, pieces, w_a, sems):
    width = w_a.shape[2]
    return load_weights(
        meta, pieces, 0, [(0, width, lambda j, rows, c, w: w_a.at[j, rows, pl.ds(c, w)])], sems
    )[0]


def load_b(meta, pieces, w_i, w_f, sems):
    one = w_i.shape[1] // 2
    base = pieces[0].shape[1] - 2 * one
    return load_weights(
        meta,
        pieces,
        base,
        [
            (0, one, lambda j, rows, c, w: w_i.at[rows, pl.ds(j * one + c, w)]),
            (one, one, lambda j, rows, c, w: w_f.at[rows, pl.ds(j * one + c, w)]),
        ],
        sems,
    )


def attn_forward(level, meta, x_or_mid, parts, norms, pieces, bias, seg_col, seg_row, cols):
    four = 4 * cols
    length, width = x_or_mid.shape
    three = 3 * cols
    heads = 2 * cols // HD

    def body(meta, *refs):
        refs = list(refs)
        src = refs.pop(0)
        if level:
            own, other, gain, shift = (refs.pop(0) for _ in range(4))
        pieces = [refs.pop(0) for _ in range(13)]
        bias, sc, sr = (refs.pop(0) for _ in range(3))
        part_out, qkv_out, probs_out, ctx_out = (refs.pop(0) for _ in range(4))
        if level:
            x_out, xhat_out, scale_out = (refs.pop(0) for _ in range(3))
        w_a, sems = refs
        waits = load_a(meta, pieces, w_a, sems)
        if level:
            for rows in chunks(length):
                z = src[rows, :] + (own[rows, :].astype(F32) + other[rows, :].astype(F32)) + shift[2:3, :]
                xhat, scale = norm_rows(z)
                x_out[rows, :] = (xhat * gain[1:2, :] + shift[3:4, :]).astype(BF16)
                xhat_out[rows, :] = xhat.astype(BF16)
                scale_out[rows, :] = scale
            x_ref = x_out
        else:
            x_ref = src
        wait_all(waits)
        for j in range(2):
            c = slice(j * three, (j + 1) * three)
            for rows in chunks(length, 256):
                qkv_out[rows, c] = (nn(x_ref[rows, :], w_a[j, :, :three]) + bias[:, c]).astype(BF16)
        v_t = jnp.concatenate(
            [qkv_out[:, j * three + 2 * cols : (j + 1) * three].astype(F32) for j in range(2)], 1
        ).T.astype(BF16)
        for queries in chunks(length, 256):
            same = sc[...] == sr[:, queries]
            outs = []
            for h in range(heads):
                j, i = divmod(h, cols // HD)
                at = j * three + i * HD
                q = qkv_out[queries, at : at + HD]
                k = qkv_out[:, at + cols : at + cols + HD]
                st = jnp.where(same, nt(k, q) * 0.125, -1e30)
                p = jnp.exp(st - jnp.max(st, 0, keepdims=True))
                p = (p * (1.0 / jnp.sum(p, 0, keepdims=True))).astype(BF16)
                probs_out[h, :, queries] = p
                outs.append(nn(v_t[h * HD : (h + 1) * HD], p))
            ctx = jnp.concatenate(outs, 0).T.astype(BF16)
            ctx_out[queries, :] = ctx
            part_out[queries, :] = (
                nt(ctx[:, :cols], w_a[0, :, three:]) + nt(ctx[:, cols:], w_a[1, :, three:])
            ).astype(BF16)

    outs = [
        sds((length, width), BF16), sds((length, 2 * three), BF16),
        sds((heads, length, length), BF16), sds((length, 2 * cols), BF16),
    ]
    args = [meta, x_or_mid]
    if level:
        args += [*parts, *norms]
        outs += [sds((length, width), BF16), sds((length, width), BF16), sds((length, 1), F32)]
    specs = [SM] + [VM] * (len(args) - 1) + [ANY] * 13 + [VM] * 3
    args += [*pieces, bias, seg_col, seg_row]
    return pl.pallas_call(
        body,
        out_shape=outs,
        in_specs=specs,
        out_specs=[VM] * len(outs),
        scratch_shapes=[pltpu.VMEM((2, width, four), BF16), pltpu.SemaphoreType.DMA((copies_of(pieces[5]),))],
        compiler_params=params(),
        cost_estimate=takes(13),
        name="attn_forward",
    )(*args)


def ffn_forward(meta, x, parts, gains, shifts, pieces, bias_in, half):
    units = 2 * half
    length, width = x.shape

    def body(meta, x, own, other, gain, shift, p0, p1, p2, p3, p4, p5, p6, p7, p8, p9, p10, p11, p12, bias,
             part_out, mid_out, xhat_out, scale_out, act_out, slope_out, w_i, w_f, low, sems):
        first, second = load_b(meta, (p0, p1, p2, p3, p4, p5, p6, p7, p8, p9, p10, p11, p12), w_i, w_f, sems)
        for rows in chunks(length):
            z = x[rows, :].astype(F32) + (own[rows, :].astype(F32) + other[rows, :].astype(F32)) + shift[0:1, :]
            xhat, scale = norm_rows(z)
            mid = xhat * gain[0:1, :] + shift[1:2, :]
            mid_out[rows, :] = mid
            low[rows, :] = mid.astype(BF16)
            xhat_out[rows, :] = xhat.astype(BF16)
            scale_out[rows, :] = scale
        wait_all(first)
        for rows in chunks(length, 256):
            for c in chunks(units, 512):
                pre = nn(low[rows, :], w_i[:, c]) + bias[:, c]
                act, slope = gelu_parts(pre)
                act_out[rows, c] = act.astype(BF16)
                slope_out[rows, c] = slope.astype(BF16)
        wait_all(second)
        for rows in chunks(length, 256):
            part_out[rows, :] = nt(act_out[rows, :], w_f[...]).astype(BF16)

    return pl.pallas_call(
        body,
        out_shape=[
            sds((length, width), BF16), sds((length, width), F32), sds((length, width), BF16),
            sds((length, 1), F32), sds((length, units), BF16), sds((length, units), BF16),
        ],
        in_specs=[SM] + [VM] * 5 + [ANY] * 13 + [VM],
        out_specs=[VM] * 6,
        scratch_shapes=[
            pltpu.VMEM((width, units), BF16), pltpu.VMEM((width, units), BF16),
            pltpu.VMEM((length, width), BF16), pltpu.SemaphoreType.DMA((copies_of(pieces[5]),)),
        ],
        compiler_params=params(),
        cost_estimate=takes(9),
        name="ffn_forward",
    )(meta, x, *parts, gains, shifts, *pieces, bias_in)


def last_norm(mid, parts, gains, shifts, tok_row, cls_pos):
    length, width = mid.shape
    n_cls = cls_pos.shape[0]

    def body(cls, mid, own, other, gain, shift, tok, y_out, xhat_out, scale_out, cls_out):
        for rows in chunks(length):
            z = mid[rows, :] + (own[rows, :].astype(F32) + other[rows, :].astype(F32)) + shift[2:3, :]
            xhat, scale = norm_rows(z)
            y_out[rows, :] = (xhat * gain[1:2, :] + shift[3:4, :]).astype(BF16)
            xhat_out[rows, :] = xhat.astype(BF16)
            scale_out[rows, :] = scale
        which = lax.broadcasted_iota(jnp.int32, (16, length), 0)
        hot = jnp.zeros((16, length), F32)
        for p in range(n_cls):
            hot = jnp.where(jnp.logical_and(which == p, tok[...] == cls[p]), 1.0, hot)
        cls_out[...] = nn(hot.astype(BF16), y_out[...])[:n_cls].astype(BF16)

    return pl.pallas_call(
        body,
        out_shape=[
            sds((length, width), BF16), sds((length, width), BF16), sds((length, 1), F32),
            sds((n_cls, width), BF16),
        ],
        in_specs=[SM] + [VM] * 6,
        out_specs=[VM] * 4,
        compiler_params=params(),
        cost_estimate=takes(2),
        name="last_norm",
    )(cls_pos, mid, *parts, gains, shifts, tok_row)


def ffn_backward(level, meta, sources, xhat, scale, gains, slope, pieces, half):
    units = 2 * half
    length, width = xhat.shape
    n_cls = sources[3].shape[0] if level else 0

    def body(meta, *refs):
        refs = list(refs)
        if level:
            cls, grad, d_cls, tok = (refs.pop(0) for _ in range(4))
        else:
            d_above, own, other = (refs.pop(0) for _ in range(3))
        xhat, scale, gain, slope = (refs.pop(0) for _ in range(4))
        pieces = [refs.pop(0) for _ in range(13)]
        part_out, second_out, low_out, pre_out, vec_out, inb_out, w_i, w_f, sems = refs
        first, second = load_b(meta, pieces, w_i, w_f, sems)
        sums = [jnp.zeros((1, width), F32) for _ in range(3)]
        for rows in chunks(length):
            if level:
                d_out = grad[rows, :].astype(F32)
                for p in range(n_cls):
                    d_out = d_out + jnp.where(tok[rows, :] == cls[p], 1.0, 0.0) * d_cls[p : p + 1, :]
            else:
                d_out = d_above[rows, :] + (own[rows, :].astype(F32) + other[rows, :].astype(F32))
                d_out = d_out.astype(BF16).astype(F32)
            hat = xhat[rows, :].astype(F32)
            d_second = norm_back_rows(d_out, gain[1:2, :], hat, scale[rows, :])
            second_out[rows, :] = d_second
            low_out[rows, :] = d_second.astype(BF16)
            for n, item in enumerate((d_out * hat, d_out, d_second)):
                sums[n] = sums[n] + jnp.sum(item, 0, keepdims=True)
        for n in range(3):
            vec_out[n : n + 1, :] = sums[n]
        wait_all(second)
        for n, rows in enumerate(chunks(length, 256)):
            for c in chunks(units, units // 4):
                d_act = nn(low_out[rows, :], w_f[:, c])
                d_pre = (slope[rows, c].astype(F32) * d_act).astype(BF16)
                pre_out[rows, c] = d_pre
                j, at = divmod(c.start, units // 2)
                at = slice(at, at + c.stop - c.start)
                total = jnp.sum(d_pre.astype(F32), 0, keepdims=True)
                inb_out[j : j + 1, at] = total if n == 0 else inb_out[j : j + 1, at] + total
        wait_all(first)
        for rows in chunks(length, 256):
            part_out[rows, :] = nt(pre_out[rows, :], w_i[...]).astype(BF16)

    if level:
        token_grad, d_cls, tok_col, cls_pos = sources
        args, specs = [meta, cls_pos, token_grad, d_cls, tok_col], [SM, SM, VM, VM, VM]
    else:
        args, specs = [meta, *sources], [SM, VM, VM, VM]
    args += [xhat, scale, gains, slope, *pieces]
    specs += [VM] * 4 + [ANY] * 13
    return pl.pallas_call(
        body,
        out_shape=[
            sds((length, width), BF16), sds((length, width), F32), sds((length, width), BF16),
            sds((length, units), BF16), sds((3, width), F32), sds((2, units // 2), F32),
        ],
        in_specs=specs,
        out_specs=[VM] * 6,
        scratch_shapes=[
            pltpu.VMEM((width, units), BF16), pltpu.VMEM((width, units), BF16),
            pltpu.SemaphoreType.DMA((copies_of(pieces[5]),)),
        ],
        compiler_params=params(),
        cost_estimate=takes(9),
        name="ffn_backward",
    )(*args)


def grads_of(nz, rz, width):
    half = nz // 2
    return [sds((nz, rz, width), BF16), sds((half, rz, width), BF16), sds((half, rz, width), BF16)]


def put_grad(outs, j, k, nz, column, value, first=0):
    half, (height, width) = nz // 2, value.shape
    if k < half:
        out, at = outs[0], k + (half if j == 0 else 0)
    else:
        out, at = outs[2 if j == 0 else 1], k - half
    out[at, first : first + height, column : column + width] = value.astype(BF16)


def ffn_grads(meta, mid, d_pre, d_ffn, act, nz):
    length, width = mid.shape
    units = d_pre.shape[1]
    one = units // 2
    rz = width // nz

    def body(meta, mid, d_pre, d_ffn, act, *refs):
        outs, (mid_t, ffn_t) = refs[:3], refs[3:]
        mid_t[...] = mid[...].T.astype(BF16)
        ffn_t[...] = d_ffn[...].astype(F32).T.astype(BF16)
        for j in range(2):
            c = slice(j * one, (j + 1) * one)
            for k in range(nz):
                rows = zrows(meta, k, rz)
                put_grad(outs, j, k, nz, 0, nn(mid_t[rows, :], d_pre[:, c]))
                put_grad(outs, j, k, nz, one, nn(ffn_t[rows, :], act[:, c]))

    return pl.pallas_call(
        body,
        out_shape=grads_of(nz, rz, units),
        in_specs=[SM] + [VM] * 4,
        out_specs=[VM] * 3,
        scratch_shapes=[pltpu.VMEM((width, length), BF16)] * 2,
        compiler_params=params(),
        cost_estimate=takes(7),
        name="ffn_grads",
    )(meta, mid, d_pre, d_ffn, act)


def attn_backward(meta, d_second, parts, xhat, scale, gains, qkv, probs, pieces, cols):
    four = 4 * cols
    length, width = d_second.shape
    three = 3 * cols
    heads = 2 * cols // HD

    def body(meta, d_second, own, other, xhat, scale, gain, qkv, probs, p0, p1, p2, p3, p4, p5, p6, p7, p8, p9, p10, p11, p12,
             part_out, first_out, low_out, dqkv_out, vec_out, sum_out,
             w_a, d_ctx, acc_v, acc_k, sems):
        waits = load_a(meta, (p0, p1, p2, p3, p4, p5, p6, p7, p8, p9, p10, p11, p12), w_a, sems)
        sums = [jnp.zeros((1, width), F32) for _ in range(3)]
        for rows in chunks(length):
            d_mid = d_second[rows, :] + (own[rows, :].astype(F32) + other[rows, :].astype(F32))
            hat = xhat[rows, :].astype(F32)
            d_first = norm_back_rows(d_mid, gain[0:1, :], hat, scale[rows, :])
            first_out[rows, :] = d_first
            low_out[rows, :] = d_first.astype(BF16)
            for n, item in enumerate((d_mid * hat, d_mid, d_first)):
                sums[n] = sums[n] + jnp.sum(item, 0, keepdims=True)
        for n in range(3):
            vec_out[n : n + 1, :] = sums[n]
        wait_all(waits)
        for j in range(2):
            for rows in chunks(length, 256):
                d_ctx[rows, j * cols : (j + 1) * cols] = nn(low_out[rows, :], w_a[j, :, three:]).astype(BF16)
        k_t = jnp.concatenate(
            [qkv[:, j * three + cols : j * three + 2 * cols].astype(F32) for j in range(2)], 1
        ).T.astype(BF16)
        for h in range(heads):
            j, i = divmod(h, cols // HD)
            at = j * three + i * HD
            q_cols, k_cols, v_cols = (slice(at + n * cols, at + n * cols + HD) for n in range(3))
            for n, queries in enumerate(chunks(length, 256)):
                d_o = d_ctx[queries, h * HD : (h + 1) * HD]
                d_p = nt(qkv[:, v_cols], d_o)
                p = probs[h, :, queries]
                wide = p.astype(F32)
                d_s = (wide * (d_p - jnp.sum(wide * d_p, 0, keepdims=True))).astype(BF16)
                d_v = nn(p, d_o)
                d_k = nn(d_s, qkv[queries, q_cols])
                acc_v[...] = d_v if n == 0 else acc_v[...] + d_v
                acc_k[...] = d_k if n == 0 else acc_k[...] + d_k
                d_q = nn(k_t[h * HD : (h + 1) * HD], d_s)
                dqkv_out[queries, q_cols] = (d_q.T * 0.125).astype(BF16)
            dqkv_out[:, v_cols] = acc_v[...].astype(BF16)
            dqkv_out[:, k_cols] = (acc_k[...] * 0.125).astype(BF16)
        for j in range(2):
            sum_out[j : j + 1, :] = jnp.sum(
                dqkv_out[:, j * three : (j + 1) * three].astype(F32), 0, keepdims=True
            )
        for rows in chunks(length, 256):
            part_out[rows, :] = (
                nt(dqkv_out[rows, :three], w_a[0, :, :three]) + nt(dqkv_out[rows, three:], w_a[1, :, :three])
            ).astype(BF16)

    return pl.pallas_call(
        body,
        out_shape=[
            sds((length, width), BF16), sds((length, width), F32), sds((length, width), BF16),
            sds((length, 2 * three), BF16), sds((3, width), F32), sds((2, three), F32),
        ],
        in_specs=[SM] + [VM] * 8 + [ANY] * 13,
        out_specs=[VM] * 6,
        scratch_shapes=[
            pltpu.VMEM((2, width, four), BF16), pltpu.VMEM((length, 2 * cols), BF16),
            pltpu.VMEM((length, HD), F32), pltpu.VMEM((length, HD), F32),
            pltpu.SemaphoreType.DMA((copies_of(pieces[5]),)),
        ],
        compiler_params=params(),
        cost_estimate=takes(15),
        name="attn_backward",
    )(meta, d_second, *parts, xhat, scale, gains, qkv, probs, *pieces)


def attn_grads(meta, places, x, d_attn, d_qkv, ctx, vectors, nz, extra):
    length, width = x.shape
    three = d_qkv.shape[1] // 2
    cols = ctx.shape[1] // 2
    rz = width // nz

    def body(meta, places, x, d_attn, d_qkv, ctx, vec1, vec2, sum_qkv, sum_inb, *refs):
        outs, (x_t, a_t, norm_rows_, qv_rows, inb_rows) = refs[:3], refs[3:]
        x_t[...] = x[...].astype(F32).T.astype(BF16)
        a_t[...] = d_attn[...].astype(F32).T.astype(BF16)
        for j in range(2):
            for k in range(nz):
                rows = zrows(meta, k, rz)
                grad = nn(x_t[rows, :], d_qkv[:, j * three : (j + 1) * three])
                put_grad(outs, j, k, nz, 0, grad)
                put_grad(outs, j, k, nz, three, nn(a_t[rows, :], ctx[:, j * cols : (j + 1) * cols]))
        if not extra:
            return
        piece, part = width // (4 * nz), cols // nz
        units = sum_inb.shape[1] // nz
        norm_rows_[...] = jnp.zeros_like(norm_rows_)
        norm_rows_[0:3, :] = vec1[...]
        norm_rows_[3:6, :] = vec2[...]
        for j in range(2):
            qv_rows[...] = jnp.zeros_like(qv_rows)
            qv_rows[0:1, :cols] = sum_qkv[j : j + 1, :cols]
            qv_rows[1:2, :cols] = sum_qkv[j : j + 1, 2 * cols : three]
            inb_rows[...] = jnp.zeros_like(inb_rows)
            inb_rows[0:1, :] = sum_inb[j : j + 1, :]
            for k in range(nz):
                d = places[2 + k]
                from_norm = pltpu.roll(norm_rows_[...], width - (d * 4 + places[j]) * piece, 1)
                from_qv = pltpu.roll(qv_rows[...], width - d * part, 1)
                from_inb = pltpu.roll(inb_rows[...], width - d * units, 1)
                lane = lax.broadcasted_iota(jnp.int32, (8, 2 * cols), 1)
                upper = jnp.where(lane < piece, from_norm[:, : 2 * cols], 0.0)
                lower = jnp.where(lane < part, from_qv[:, : 2 * cols], 0.0)
                shifted = pltpu.roll(from_inb, 128, 1)[:, : 2 * cols]
                inside = jnp.logical_and(lane >= 128, lane < 128 + units)
                lower = jnp.where(inside, shifted, lower)
                put_grad(outs, j, k, nz, 0, jnp.concatenate([upper, lower], 0), rz)
                put_grad(outs, j, k, nz, 2 * cols, jnp.zeros((extra, 2 * cols), F32), rz)

    return pl.pallas_call(
        body,
        out_shape=grads_of(nz, rz + extra, three + cols),
        in_specs=[SM, SM] + [VM] * 8,
        out_specs=[VM] * 3,
        scratch_shapes=[pltpu.VMEM((width, length), BF16)] * 2 + [pltpu.VMEM((8, width), F32)] * 3,
        compiler_params=params(),
        cost_estimate=takes(4),
        name="attn_grads",
    )(meta, places, x, d_attn, d_qkv, ctx, *vectors)


def loss_kernel(own, perm, slots, queries, positive_col, n_own):
    n_q, width = queries.shape
    n_p = slots.shape[0]

    def body(own, perm, slots, queries, pos, loss_out, d_out):
        passages = nn(perm[...], slots[...]).astype(BF16)
        logits = nt(queries[...], passages)
        top = jnp.max(logits, -1, keepdims=True)
        log_total = top + jnp.log(jnp.sum(jnp.exp(logits - top), -1, keepdims=True))
        index = lax.broadcasted_iota(jnp.int32, (n_q, n_p), 1)
        hits = pos[...] == index
        chosen = jnp.sum(jnp.where(hits, logits, 0.0), -1, keepdims=True)
        loss_out[...] = jnp.sum(log_total - chosen, 0, keepdims=True) / n_q
        d_logits = (16.0 * (jnp.exp(logits - log_total) - jnp.where(hits, 1.0, 0.0))).astype(BF16)
        pick = jnp.where(
            lax.broadcasted_iota(jnp.int32, (n_p, 128), 0)
            == lax.broadcasted_iota(jnp.int32, (n_p, 128), 1) + own[0],
            1.0, 0.0,
        ).astype(BF16)
        cols = nn(d_logits, pick)
        d_out[...] = nn(cols.T.astype(BF16), queries[...])[:n_own]

    return pl.pallas_call(
        body,
        out_shape=[sds((1, 1), F32), sds((n_own, width), F32)],
        in_specs=[SM] + [VM] * 4,
        out_specs=[VM] * 2,
        compiler_params=params(),
        cost_estimate=takes(1),
        name="contrast",
    )(own, perm, slots, queries, positive_col)


def on_device(
    inputs, cls_pos, w_qkv, qv_bias, w_out, w_in, in_bias, w_ffn_out,
    layer_gains, shifts, queries, positive, token_grad,
):
    core = lax.axis_index("section")
    dp = lax.axis_index("dp")
    me = lax.axis_index("tensor")
    n_dp = lax.axis_size("dp")
    n_t = lax.axis_size("tensor")
    first_core = core == 0
    rows_dev, share, width = inputs.shape
    cols = w_qkv.shape[3]
    units = w_in.shape[2]
    length = n_t * share
    n_chips = n_dp * n_t
    piece = width // n_chips
    order = dp_order()
    direct = direct_dp()
    nz, extra = (4, 16) if direct else (2, 0)
    t_ids = jnp.arange(n_t, dtype=jnp.int32)

    vec = jnp.concatenate(
        [layer_gains.reshape(-1), shifts.reshape(-1), qv_bias.reshape(-1), in_bias.reshape(-1)]
    )
    n_gain, n_shift, n_qv, n_inb = layer_gains.size, shifts.size, qv_bias.size, in_bias.size
    n_vec = vec.shape[0]
    flat = jnp.concatenate(
        [vec, queries.reshape(-1), (positive // 16).astype(BF16), (positive % 16).astype(BF16)]
    )
    flat = jnp.pad(flat, (0, -flat.shape[0] % 2048)).reshape(-1, 128)

    def spread_rows(block):
        blocks = [lax.dynamic_index_in_dim(block, me ^ k, 0, keepdims=False) for k in range(n_t)]
        return jnp.concatenate(exchange_rows(blocks), 0)

    pack = jnp.concatenate(
        [w_qkv[0, :, 0], w_qkv[0, :, 1], w_qkv[0, :, 2], w_out[0].T, w_in[0], w_ffn_out[0].T], 1
    )
    message = spread_dp(flat)
    if direct:
        own = pack
        z_a = rest_dp(after(pack[:, :width], message))
    else:
        pack = lax.all_gather(pack, "dp", axis=0, tiled=True)
        own, other_rows = pack[: width // 2], pack[width // 2 :][None]
    message = spread_tensor(message)
    near0, far0 = gather_own(after(own, message))
    both0 = gather_own_both(near0, far0)
    owns = [own, near0, far0, *both0]

    def halves_of(blocks, first, size, *earlier):
        half = size // 2
        if not direct:
            blocks = other_rows[:, :, first : first + size]
            return blocks[:, :, :half], blocks[:, :, half:]
        blocks = after(blocks, *earlier)
        return jnp.stack([b[:, :half] for b in blocks]), jnp.stack([b[:, half:] for b in blocks])

    rest_a = jnp.stack(after(z_a, near0, far0)) if direct else other_rows[:, :, :width]
    near_a, far_a = gather_own(rest_a)
    if direct:
        z_b = rest_dp(after(pack[:, width:], rest_a))
    rows_in = spread_rows(after(jnp.where(first_core, inputs, token_grad), near_a))
    near_a, far_a = after((near_a, far_a), both0, z_b[:2] if direct else near_a)
    both_a = gather_both(near_a[:, :, : width // 2], far_a[:, :, width // 2 :])
    rows_got = swap_cores(rows_in)
    x_low = jnp.where(first_core, rows_in, rows_got)
    tokens = jnp.where(first_core, rows_got, rows_in)
    rest_b = halves_of(z_b if direct else None, width, 2 * units, both_a)
    near_b = gather_near(rest_b)
    pieces_a = [*owns, rest_a, rest_a, near_a, near_a, far_a, far_a, *both_a]

    zrow = order * (width // n_dp) if direct else jnp.arange(2, dtype=jnp.int32) * (width // 2)
    metas = [
        jnp.concatenate([(core == level)[None].astype(jnp.int32), zrow.astype(jnp.int32)])
        for level in range(2)
    ]
    slots = [me ^ (2 * (core != level) + jnp.arange(2, dtype=jnp.int32)) for level in range(2)]
    places = [jnp.concatenate([s, order[:nz]]).astype(jnp.int32) for s in slots]
    hots = [(s[:, None] == t_ids[None, :]).astype(F32) for s in slots]

    positions = jnp.concatenate(
        [(me ^ k) * share + jnp.arange(share, dtype=jnp.int32) for k in range(n_t)]
    )
    cls_row = lax.dynamic_index_in_dim(cls_pos, me, 0, keepdims=False)
    segments = jnp.sum((positions[:, None] >= cls_row[None, :]).astype(jnp.int32), -1)
    seg_col, seg_row = segments[:, None], segments[None, :]
    tok_col, tok_row = positions[:, None], positions[None, :]

    slot_ids = (order[None, :] * n_t + (me ^ t_ids)[:, None]).reshape(-1)
    to_natural = (jnp.arange(n_chips, dtype=jnp.int32)[:, None] == slot_ids[None, :]).astype(BF16)
    table = nn(to_natural, message.reshape(n_chips, -1))
    own_table = table[:, :n_vec].astype(BF16)
    other_table = swap_cores(own_table)
    tables = jnp.where(
        first_core, jnp.stack([own_table, other_table]), jnp.stack([other_table, own_table])
    ).astype(F32)
    at = 0
    gains = tables[:, :, at : at + n_gain].reshape(2, n_chips, 2, piece).transpose(0, 2, 1, 3).reshape(2, 2, width)
    at += n_gain
    shift = tables[:, :, at : at + n_shift].reshape(2, n_chips, 4, piece).transpose(0, 2, 1, 3).reshape(2, 4, width)
    at += n_shift
    qv = tables[:, :, at : at + n_qv].reshape(2, n_dp, n_t, 2, cols // n_dp)
    qv = qv.transpose(0, 3, 2, 1, 4).reshape(2, 2, n_t, cols)
    at += n_qv
    inb = tables[:, :, at : at + n_inb].reshape(2, n_dp, n_t, n_inb).transpose(0, 2, 1, 3).reshape(2, n_t, units)
    vectors = []
    for level in range(2):
        bias = jnp.sum(hots[level][None, :, :, None] * qv[level][:, None], 2)
        bias = jnp.stack([bias[0], jnp.zeros_like(bias[0]), bias[1]], 1).reshape(1, -1)
        bias_in = jnp.sum(hots[level][:, :, None] * inb[level][None], 1).reshape(1, -1)
        vectors.append((gains[level], shift[level], bias, bias_in))
    at = n_vec
    q_dev = queries.shape[0]
    all_q = table[:, at : at + q_dev * width].reshape(-1, width).astype(BF16)
    at += q_dev * width
    all_pos = table[:, at : at + q_dev] * 16.0 + table[:, at + q_dev : at + 2 * q_dev]
    all_pos = all_pos.astype(jnp.int32).reshape(-1, 1)
    n_cls = cls_row.shape[0]
    perm = jnp.repeat(jnp.repeat(to_natural, n_cls, 0), n_cls, 1)
    perm = perm * jnp.tile(jnp.eye(n_cls, dtype=BF16), (n_chips, n_chips))

    vectors, all_q, all_pos, perm, x_low = lax.optimization_barrier(
        (vectors, all_q, all_pos, perm, x_low)
    )
    saved = []
    source, parts, norms = x_low, None, None
    for level in range(2):
        gain, shift, bias, bias_in = vectors[level]
        outs = attn_forward(
            level, metas[level], source, parts, norms, pieces_a, bias, seg_col, seg_row, cols
        )
        part, qkv, probs, ctx = outs[:4]
        if level == 0:
            pieces_b = [*owns, *rest_b, *near_b, *gather_both(near_b[0], after(near_b[3], part))]
        if level:
            x, xhat2, scale2 = outs[4:]
            saved[0]["second"] = (xhat2, scale2)
        else:
            x = x_low
        part, mid, xhat1, scale1, act, slope = ffn_forward(
            metas[level], x, (part, swap_cores(part)), gain, shift, pieces_b, bias_in, units
        )
        saved.append(
            dict(x=x, qkv=qkv, probs=probs, ctx=ctx, mid=mid, xhat1=xhat1, scale1=scale1, act=act, slope=slope)
        )
        source, parts, norms = mid, (part, swap_cores(part)), (gain, shift)
    y, xhat2, scale2, cls_own = last_norm(source, parts, *norms, tok_row, cls_row)
    saved[1]["second"] = (xhat2, scale2)

    cls_slots = spread_tensor(spread_dp(cls_own)).reshape(n_chips * n_cls, width)
    first_own = ((dp * n_t + me) * n_cls).astype(jnp.int32)[None]
    mean_loss, d_cls = loss_kernel(first_own, perm, cls_slots, all_q, all_pos, n_cls)

    vector_rows = [None, None]
    sources = (tokens, d_cls, tok_col, cls_row)
    sums_a, sums_b = [None, None], [None, None]
    for level in (1, 0):
        gain = vectors[level][0]
        kept = saved[level]
        meta = metas[level]
        xhat2, scale2 = kept["second"]
        if level == 0:
            sources = (after(sources[0], sums_b[1].first(grads_a[1])), *sources[1:])
        part, d_second, d_ffn, d_pre, vec2, sum_inb = ffn_backward(
            level, meta, sources, xhat2, scale2, gain, kept["slope"], pieces_b, units
        )
        other = swap_cores(part)
        if level == 0:
            d_ffn = after(d_ffn, sums_a[1].first(part))
        grads_b = ffn_grads(meta, kept["mid"], d_pre, d_ffn, kept["act"], nz)
        sums_b[level] = Reduction(grads_b, level)
        d_second = after(d_second, grads_b[1])
        if level == 0:
            d_second = after(d_second, sums_b[1].second(grads_b[1]))
        part, d_first, d_attn, d_qkv, vec1, sum_qkv = attn_backward(
            meta, d_second, (part, other), kept["xhat1"], kept["scale1"], gain,
            kept["qkv"], kept["probs"], pieces_a, cols,
        )
        other = swap_cores(part)
        if level == 0:
            d_attn = after(d_attn, sums_b[0].first(sums_a[1].second(part)))
        grads_a = attn_grads(
            meta, places[level], kept["x"], d_attn, d_qkv, kept["ctx"], (vec1, vec2, sum_qkv, sum_inb), nz, extra
        )
        sums_a[level] = Reduction(grads_a, level)
        vector_rows[level] = (vec1, vec2, sum_qkv, sum_inb)
        sources = (d_first, part, other)
    sums_b[1].third(grads_a[1])
    sums_b[0].second_direct(sums_b[1].pieces)
    sums_a[1].third(sums_b[0].sums)
    sums_a[0].first(sums_a[1].pieces, sums_b[0].hops[1:2] if direct else sums_b[0].sums)
    sums_a[0].second_direct(sums_a[0].added)
    last_a1, last_b1 = last_dp([sums_a[1], sums_b[1]], sums_a[0].sums)
    total_b0 = sums_b[0].third_direct()
    d_hidden = d_first + (part.astype(F32) + other.astype(F32))
    outgoing = jnp.where(first_core, d_hidden, y.astype(F32))
    low = after(outgoing.astype(BF16), sums_a[0].added).reshape(n_t, share, width)
    incoming = [outgoing[:share]] + [b.astype(F32) for b in exchange_rows([low[k] for k in range(n_t)])[1:]]
    boundary = jnp.zeros((n_t, share, width), F32)
    for k in range(n_t):
        boundary = lax.dynamic_update_index_in_dim(boundary, incoming[k], me ^ k, 0)
    tot_b, tot_a = (
        jnp.where(first_core, low, sum(p.astype(F32) for p in high))
        for low, high in ((total_b0, last_b1), (sums_a[0].third_direct(), last_a1))
    )
    if direct:
        end = width // n_dp
        own = tot_a[end : end + 6, :piece]
        qv = tot_a[end + 8 : end + 10, : qv_bias.shape[3]]
        grad_inb = tot_a[end + 8 : end + 9, 128 : 128 + n_inb]
        tot_a = tot_a[:end]
    else:
        tables = []
        for level in range(2):
            vec1, vec2, sum_qkv, sum_inb = vector_rows[level]
            by_t = lax.dot_general(
                hots[level], jnp.concatenate([sum_qkv, sum_inb], 1), (((0,), (0,)), ((), ())),
                precision=lax.Precision.HIGHEST,
            )
            whole = 0.5 * jnp.concatenate([vec1, vec2])
            whole = jnp.pad(whole, ((0, 0), (0, by_t.shape[1] - width)))
            tables.append(jnp.concatenate([whole, by_t]))
        tables = lax.psum(jnp.stack(tables), ("section", "dp", "tensor"))
        flat = jnp.where(first_core, tables[0], tables[1])
        own = lax.dynamic_slice_in_dim(flat[:6, :width], (dp * n_t + me) * piece, piece, 1)
        by_t = lax.dynamic_slice_in_dim(flat, 6 + me, 1, 0)
        qv = jnp.concatenate([by_t[:, :cols], by_t[:, 2 * cols : 3 * cols]])
        qv = lax.dynamic_slice_in_dim(qv, dp * qv_bias.shape[3], qv_bias.shape[3], 1)
        grad_inb = lax.dynamic_slice_in_dim(by_t[:, 3 * cols :], dp * n_inb, n_inb, 1)
    grad_gains = jnp.concatenate([own[0:1], own[3:4]]).reshape(layer_gains.shape)
    grad_shifts = jnp.concatenate([own[2:3], own[1:2], own[5:6], own[4:5]]).reshape(shifts.shape)
    grad_qv, grad_inb = qv.reshape(qv_bias.shape), grad_inb.reshape(in_bias.shape)

    grad_qkv = jnp.stack([tot_a[:, n * cols : (n + 1) * cols] for n in range(3)], 1)[None]
    grad_out = tot_a[:, 3 * cols :].T[None]
    grad_in = tot_b[:, :units][None]
    grad_ffn = tot_b[:, units:].T[None]
    return (
        grad_qkv, grad_qv, grad_out, grad_in, grad_inb, grad_ffn,
        grad_gains, grad_shifts, boundary[None], mean_loss.reshape(()),
    )


def solution(mesh):
    return jax.shard_map(
        on_device,
        mesh=mesh,
        in_specs=(
            P("dp", "tensor", None),
            P("dp", None),
            P("section", "dp", None, "tensor"),
            P("section", None, "tensor", "dp"),
            P("section", "tensor", "dp"),
            P("section", "dp", "tensor"),
            P("section", "tensor", "dp"),
            P("section", "tensor", "dp"),
            P("section", None, ("dp", "tensor")),
            P("section", None, ("dp", "tensor")),
            P(("dp", "tensor"), None),
            P(("dp", "tensor")),
            P("dp", "tensor", None),
        ),
        out_specs=(
            P("section", "dp", None, "tensor"),
            P("section", None, "tensor", "dp"),
            P("section", "tensor", "dp"),
            P("section", "dp", "tensor"),
            P("section", "tensor", "dp"),
            P("section", "tensor", "dp"),
            P("section", None, ("dp", "tensor")),
            P("section", None, ("dp", "tensor")),
            P("section", "dp", "tensor", None),
            P(),
        ),
        check_vma=False,
    )
```

```python
import jax
import jax.numpy as jnp
from jax import lax
from jax.experimental import pallas as pl
from jax.experimental.pallas import tpu as pltpu
from jax.sharding import PartitionSpec as P

HD = 64
PARTNER = 1
CROSS = 2
BF16 = jnp.bfloat16
F32 = jnp.float32


def mm(left, right, dims):
    return lax.dot_general(left, right, (dims, ((), ())), preferred_element_type=F32)


def nn(left, right):
    return mm(left, right, ((1,), (0,)))


def nt(left, right):
    return mm(left, right, ((1,), (1,)))


def after(block, *earlier):
    return lax.optimization_barrier((block, *earlier))[0]


def swap_cores(block):
    return lax.ppermute(block, "section", [(0, 1), (1, 0)])


def hop(block, axis, flip):
    return lax.ppermute(block, axis, [(i, i ^ flip) for i in range(lax.axis_size(axis))])


def core_hop(block, axis, flip, core):
    size = lax.axis_size(axis)
    route = [(core * size + i, core * size + (i ^ flip)) for i in range(size)]
    return lax.ppermute(block, ("section", axis), route)


def cross_hop(block, source):
    size = lax.axis_size("tensor")
    route = [(source * size + i, (1 - source) * size + (i ^ CROSS)) for i in range(size)]
    return lax.ppermute(block, ("section", "tensor"), route)


def direct_dp():
    return lax.axis_size("dp") == 4


def dp_order():
    size = lax.axis_size("dp")
    if direct_dp():
        return lax.axis_index("dp") ^ jnp.arange(size, dtype=jnp.int32)
    return jnp.arange(size, dtype=jnp.int32)


def spread_dp(block):
    if direct_dp():
        return jnp.stack([block] + [hop(block, "dp", k) for k in range(1, 4)])
    return lax.all_gather(block, "dp", axis=0, tiled=False)


def spread_tensor(block):
    return jnp.stack([block] + [hop(block, "tensor", k) for k in range(1, 4)])


def double(block, axis):
    pair = jnp.stack([block, hop(block, axis, 1)])
    return jnp.concatenate([pair, hop(pair, axis, 2)])


def exchange_rows(blocks):
    first = hop(jnp.stack([blocks[1], blocks[3]]), "tensor", 1)
    second = hop(jnp.stack([blocks[2], first[1]]), "tensor", 2)
    return [blocks[0], first[0], second[0], second[1]]


def cross_all(block):
    size = lax.axis_size("tensor")
    route = [(s * size + i, (1 - s) * size + (i ^ CROSS)) for s in range(2) for i in range(size)]
    return lax.ppermute(block, ("section", "tensor"), route)


def rest_dp(own):
    return [hop(own, "dp", k) for k in range(1, 4)]


def gather_own(own):
    near, far = hop(own, "tensor", PARTNER), cross_all(own)
    return near, far


def gather_own_both(near, far):
    half = near.shape[1] // 2
    return cross_all(near[:, :half]), hop(far[:, half:], "tensor", PARTNER)


def gather_near(rest):
    a, b = rest
    near_a, far_b = hop(a, "tensor", PARTNER), cross_all(b)
    near_b, far_a = hop(b, "tensor", PARTNER), cross_all(a)
    return near_a, near_b, far_a, far_b


def gather_both(near_a, far_b):
    return cross_all(near_a), hop(far_b, "tensor", PARTNER)


def add_low(*items):
    total = items[0].astype(F32)
    for item in items[1:]:
        total = total + item.astype(F32)
    return total.astype(BF16)


class Reduction:
    def __init__(self, grads, core):
        self.core = core
        self.pair, self.next_b, self.own_b = grads
        self.got = cross_hop(self.pair, 1 - core)
        self.near_b = hop(self.next_b, "tensor", PARTNER)

    def first(self, *earlier):
        half = self.next_b.shape[0]
        self.parts = pair, own_b, got, near_b = after((self.pair, self.own_b, self.got, self.near_b), *earlier)
        self.added = add_low(pair[:half], got[:half]), add_low(own_b, near_b)
        self.near_a = core_hop(self.added[0], "tensor", PARTNER, self.core)
        self.far_b = cross_hop(self.added[1], 1 - self.core)
        return self.added

    def sum_halves(self, *earlier):
        half = self.next_b.shape[0]
        near_a, far_b, (pair, own_b, got, near_b) = after((self.near_a, self.far_b, self.parts), *earlier)
        return add_low(pair[half:], got[half:], near_a), add_low(own_b, near_b, far_b)

    def scatter(self):
        whole = jnp.concatenate(self.sums).reshape(-1, self.own_b.shape[2])
        return [lax.psum_scatter(whole, "dp", scatter_dimension=0, tiled=True)]

    def second_direct(self, *earlier):
        a, b = self.sums = self.sum_halves(*earlier)
        if direct_dp():
            self.hops = [
                core_hop(block, "dp", k, self.core) for k, block in ((1, a[1]), (2, b[0]), (3, b[1]))
            ]
        return self.sums

    def third_direct(self, *earlier):
        if not direct_dp():
            return sum(p.astype(F32) for p in self.scatter())
        return sum(p.astype(F32) for p in after([self.sums[0][0], *self.hops], *earlier))

    def second(self, *earlier):
        self.sums = self.sum_halves(*earlier)
        if direct_dp():
            self.across = core_hop(self.sums[1], "dp", 2, self.core)
        return self.sums

    def third(self, *earlier):
        if not direct_dp():
            self.pieces = self.scatter()
            return self.pieces
        a, across = after((self.sums[0], self.across), *earlier)
        self.pieces = [add_low(a[k], across[k]) for k in range(2)]
        return self.pieces


def last_dp(reductions, *earlier):
    if not direct_dp():
        return [r.pieces for r in reductions]
    high = max(r.pieces[0].shape[0] for r in reductions)
    block = [jnp.pad(r.pieces[1], ((0, high - r.pieces[1].shape[0]), (0, 0))) for r in reductions]
    got = core_hop(after(jnp.concatenate(block, 1), *earlier), "dp", 1, reductions[0].core)
    at, out = 0, []
    for r in reductions:
        rows, width = r.pieces[0].shape
        out.append([r.pieces[0], got[:rows, at : at + width]])
        at += width
    return out


VMEM_LIMIT = 48 * 1024 * 1024
CHUNK = 128


def takes(micros):
    return pl.CostEstimate(flops=int(micros * 1.1e9), bytes_accessed=0, transcendentals=0)


def params():
    return pltpu.CompilerParams(vmem_limit_bytes=VMEM_LIMIT)


ANY = pl.BlockSpec(memory_space=pl.ANY)
VM = pl.BlockSpec(memory_space=pltpu.VMEM)
SM = pl.BlockSpec(memory_space=pltpu.SMEM)


def sds(shape, dtype):
    return jax.ShapeDtypeStruct(shape, dtype)


def chunks(length, step=CHUNK):
    return [slice(i, i + step) for i in range(0, length, step)]


def norm_rows(z):
    centre = z - jnp.mean(z, -1, keepdims=True)
    spread = jnp.mean(centre * centre, -1, keepdims=True)
    scale = lax.rsqrt(spread + 1e-05)
    return centre * scale, scale


def norm_back_rows(d_out, gain, xhat, scale):
    g = d_out * gain
    m1 = jnp.mean(g, -1, keepdims=True)
    m2 = jnp.mean(g * xhat, -1, keepdims=True)
    return scale * (g - m1 - xhat * m2)


def gelu_parts(x):
    e = jnp.exp(-0.5 * x * x)
    t = 1.0 / (1.0 + 0.2316418882 * jnp.abs(x))
    poly = t * (
        0.127414796 + t * (-0.142248368 + t * (0.7107068705 + t * (-0.7265760135 + t * 0.5307027145)))
    )
    tail = poly * e
    cdf = jnp.where(x < 0.0, tail, 1.0 - tail)
    return x * cdf, cdf + x * e * 0.3989422804014327


def zrows(meta, k, rz):
    return pl.ds(pl.multiple_of(meta[1 + k], 64), rz)


def cut(start, width, at):
    if start < at < start + width:
        return [(start, at - start), (at, start + width - at)]
    return [(start, width)]


def load_weights(meta, pieces, base, places, sems):
    own, near0, far0, a0, b0, *halves = pieces
    rest, near, far, both = halves[0:2], halves[2:4], halves[4:6], halves[6:8]
    split0, split, count = a0.shape[1], both[0].shape[2], rest[0].shape[0]
    home = meta[0] == 1
    lists = [[] for _ in places]
    at = 0
    for j in range(2):
        for k in range(count + 1):
            rows = zrows(meta, k, own.shape[0])
            for n, (start, width, place) in enumerate(places):
                offset = 0 if k else base
                for g, w in cut(offset + start, width, split if k else split0):
                    side, column = divmod(g, split if k else split0)
                    if k == 0:
                        mine = (near0 if j else own).at[:, pl.ds(g, w)]
                        other = (a0, b0)[side].at[:, pl.ds(column, w)] if j else far0.at[:, pl.ds(g, w)]
                    else:
                        mine, other = (
                            v[side].at[k - 1, :, pl.ds(g if v[0].shape[2] > split else column, w)]
                            for v in ((near, both) if j else (rest, far))
                        )
                    dst = place(j, rows, g - offset - start, w)
                    first = pltpu.make_async_copy(mine, dst, sems.at[at])
                    second = pltpu.make_async_copy(other, dst, sems.at[at])
                    at += 1

                    @pl.when(home)
                    def _():
                        first.start()

                    @pl.when(jnp.logical_not(home))
                    def _():
                        second.start()

                    lists[n].append(first)
    return lists


def copies_of(rest):
    return 2 * 3 * (1 + rest.shape[0])


def wait_all(waits):
    for made in waits:
        made.wait()


def load_a(meta, pieces, w_a, sems):
    width = w_a.shape[2]
    return load_weights(
        meta, pieces, 0, [(0, width, lambda j, rows, c, w: w_a.at[j, rows, pl.ds(c, w)])], sems
    )[0]


def load_b(meta, pieces, w_i, w_f, sems):
    one = w_i.shape[1] // 2
    base = pieces[0].shape[1] - 2 * one
    return load_weights(
        meta,
        pieces,
        base,
        [
            (0, one, lambda j, rows, c, w: w_i.at[rows, pl.ds(j * one + c, w)]),
            (one, one, lambda j, rows, c, w: w_f.at[rows, pl.ds(j * one + c, w)]),
        ],
        sems,
    )


def attn_forward(level, meta, x_or_mid, parts, norms, pieces, bias, seg_col, seg_row, cols):
    four = 4 * cols
    length, width = x_or_mid.shape
    three = 3 * cols
    heads = 2 * cols // HD

    def body(meta, *refs):
        refs = list(refs)
        src = refs.pop(0)
        if level:
            own, other, gain, shift = (refs.pop(0) for _ in range(4))
        pieces = [refs.pop(0) for _ in range(13)]
        bias, sc, sr = (refs.pop(0) for _ in range(3))
        part_out, qkv_out, probs_out, ctx_out = (refs.pop(0) for _ in range(4))
        if level:
            x_out, xhat_out, scale_out = (refs.pop(0) for _ in range(3))
        w_a, sems = refs
        waits = load_a(meta, pieces, w_a, sems)
        if level:
            for rows in chunks(length):
                z = src[rows, :] + (own[rows, :].astype(F32) + other[rows, :].astype(F32)) + shift[2:3, :]
                xhat, scale = norm_rows(z)
                x_out[rows, :] = (xhat * gain[1:2, :] + shift[3:4, :]).astype(BF16)
                xhat_out[rows, :] = xhat.astype(BF16)
                scale_out[rows, :] = scale
            x_ref = x_out
        else:
            x_ref = src
        wait_all(waits)
        for j in range(2):
            c = slice(j * three, (j + 1) * three)
            for rows in chunks(length, 256):
                qkv_out[rows, c] = (nn(x_ref[rows, :], w_a[j, :, :three]) + bias[:, c]).astype(BF16)
        v_t = jnp.concatenate(
            [qkv_out[:, j * three + 2 * cols : (j + 1) * three].astype(F32) for j in range(2)], 1
        ).T.astype(BF16)
        for queries in chunks(length, 256):
            same = sc[...] == sr[:, queries]
            outs = []
            for h in range(heads):
                j, i = divmod(h, cols // HD)
                at = j * three + i * HD
                q = qkv_out[queries, at : at + HD]
                k = qkv_out[:, at + cols : at + cols + HD]
                st = jnp.where(same, nt(k, q) * 0.125, -1e30)
                p = jnp.exp(st - jnp.max(st, 0, keepdims=True))
                p = (p * (1.0 / jnp.sum(p, 0, keepdims=True))).astype(BF16)
                probs_out[h, :, queries] = p
                outs.append(nn(v_t[h * HD : (h + 1) * HD], p))
            ctx = jnp.concatenate(outs, 0).T.astype(BF16)
            ctx_out[queries, :] = ctx
            part_out[queries, :] = (
                nt(ctx[:, :cols], w_a[0, :, three:]) + nt(ctx[:, cols:], w_a[1, :, three:])
            ).astype(BF16)

    outs = [
        sds((length, width), BF16), sds((length, 2 * three), BF16),
        sds((heads, length, length), BF16), sds((length, 2 * cols), BF16),
    ]
    args = [meta, x_or_mid]
    if level:
        args += [*parts, *norms]
        outs += [sds((length, width), BF16), sds((length, width), BF16), sds((length, 1), F32)]
    specs = [SM] + [VM] * (len(args) - 1) + [ANY] * 13 + [VM] * 3
    args += [*pieces, bias, seg_col, seg_row]
    return pl.pallas_call(
        body,
        out_shape=outs,
        in_specs=specs,
        out_specs=[VM] * len(outs),
        scratch_shapes=[pltpu.VMEM((2, width, four), BF16), pltpu.SemaphoreType.DMA((copies_of(pieces[5]),))],
        compiler_params=params(),
        cost_estimate=takes(13),
        name="attn_forward",
    )(*args)


def ffn_forward(meta, x, parts, gains, shifts, pieces, bias_in, half):
    units = 2 * half
    length, width = x.shape

    def body(meta, x, own, other, gain, shift, p0, p1, p2, p3, p4, p5, p6, p7, p8, p9, p10, p11, p12, bias,
             part_out, mid_out, xhat_out, scale_out, act_out, slope_out, w_i, w_f, low, sems):
        first, second = load_b(meta, (p0, p1, p2, p3, p4, p5, p6, p7, p8, p9, p10, p11, p12), w_i, w_f, sems)
        for rows in chunks(length):
            z = x[rows, :].astype(F32) + (own[rows, :].astype(F32) + other[rows, :].astype(F32)) + shift[0:1, :]
            xhat, scale = norm_rows(z)
            mid = xhat * gain[0:1, :] + shift[1:2, :]
            mid_out[rows, :] = mid
            low[rows, :] = mid.astype(BF16)
            xhat_out[rows, :] = xhat.astype(BF16)
            scale_out[rows, :] = scale
        wait_all(first)
        for rows in chunks(length, 256):
            for c in chunks(units, 512):
                pre = nn(low[rows, :], w_i[:, c]) + bias[:, c]
                act, slope = gelu_parts(pre)
                act_out[rows, c] = act.astype(BF16)
                slope_out[rows, c] = slope.astype(BF16)
        wait_all(second)
        for rows in chunks(length, 256):
            part_out[rows, :] = nt(act_out[rows, :], w_f[...]).astype(BF16)

    return pl.pallas_call(
        body,
        out_shape=[
            sds((length, width), BF16), sds((length, width), F32), sds((length, width), BF16),
            sds((length, 1), F32), sds((length, units), BF16), sds((length, units), BF16),
        ],
        in_specs=[SM] + [VM] * 5 + [ANY] * 13 + [VM],
        out_specs=[VM] * 6,
        scratch_shapes=[
            pltpu.VMEM((width, units), BF16), pltpu.VMEM((width, units), BF16),
            pltpu.VMEM((length, width), BF16), pltpu.SemaphoreType.DMA((copies_of(pieces[5]),)),
        ],
        compiler_params=params(),
        cost_estimate=takes(9),
        name="ffn_forward",
    )(meta, x, *parts, gains, shifts, *pieces, bias_in)


def last_norm(mid, parts, gains, shifts, tok_row, cls_pos):
    length, width = mid.shape
    n_cls = cls_pos.shape[0]

    def body(cls, mid, own, other, gain, shift, tok, y_out, xhat_out, scale_out, cls_out):
        for rows in chunks(length):
            z = mid[rows, :] + (own[rows, :].astype(F32) + other[rows, :].astype(F32)) + shift[2:3, :]
            xhat, scale = norm_rows(z)
            y_out[rows, :] = (xhat * gain[1:2, :] + shift[3:4, :]).astype(BF16)
            xhat_out[rows, :] = xhat.astype(BF16)
            scale_out[rows, :] = scale
        which = lax.broadcasted_iota(jnp.int32, (16, length), 0)
        hot = jnp.zeros((16, length), F32)
        for p in range(n_cls):
            hot = jnp.where(jnp.logical_and(which == p, tok[...] == cls[p]), 1.0, hot)
        cls_out[...] = nn(hot.astype(BF16), y_out[...])[:n_cls].astype(BF16)

    return pl.pallas_call(
        body,
        out_shape=[
            sds((length, width), BF16), sds((length, width), BF16), sds((length, 1), F32),
            sds((n_cls, width), BF16),
        ],
        in_specs=[SM] + [VM] * 6,
        out_specs=[VM] * 4,
        compiler_params=params(),
        cost_estimate=takes(2),
        name="last_norm",
    )(cls_pos, mid, *parts, gains, shifts, tok_row)


def ffn_backward(level, meta, sources, xhat, scale, gains, slope, pieces, half):
    units = 2 * half
    length, width = xhat.shape
    n_cls = sources[3].shape[0] if level else 0

    def body(meta, *refs):
        refs = list(refs)
        if level:
            cls, grad, d_cls, tok = (refs.pop(0) for _ in range(4))
        else:
            d_above, own, other = (refs.pop(0) for _ in range(3))
        xhat_from, scale, gain, slope_from = (refs.pop(0) for _ in range(4))
        pieces = [refs.pop(0) for _ in range(13)]
        part_out, second_out, low_out, pre_out, vec_out, inb_out, w_i, w_f, sems, xhat, slope, kept_sems = refs
        get_hat = pltpu.make_async_copy(xhat_from, xhat, kept_sems.at[0])
        get_slope = pltpu.make_async_copy(slope_from, slope, kept_sems.at[1])
        get_hat.start()
        get_slope.start()
        first, second = load_b(meta, pieces, w_i, w_f, sems)
        sums = [jnp.zeros((1, width), F32) for _ in range(3)]
        get_hat.wait()
        for rows in chunks(length):
            if level:
                d_out = grad[rows, :].astype(F32)
                for p in range(n_cls):
                    d_out = d_out + jnp.where(tok[rows, :] == cls[p], 1.0, 0.0) * d_cls[p : p + 1, :]
            else:
                d_out = d_above[rows, :] + (own[rows, :].astype(F32) + other[rows, :].astype(F32))
                d_out = d_out.astype(BF16).astype(F32)
            hat = xhat[rows, :].astype(F32)
            d_second = norm_back_rows(d_out, gain[1:2, :], hat, scale[rows, :])
            second_out[rows, :] = d_second
            low_out[rows, :] = d_second.astype(BF16)
            for n, item in enumerate((d_out * hat, d_out, d_second)):
                sums[n] = sums[n] + jnp.sum(item, 0, keepdims=True)
        for n in range(3):
            vec_out[n : n + 1, :] = sums[n]
        wait_all(second)
        get_slope.wait()
        for n, rows in enumerate(chunks(length, 256)):
            for c in chunks(units, units // 4):
                d_act = nn(low_out[rows, :], w_f[:, c])
                d_pre = (slope[rows, c].astype(F32) * d_act).astype(BF16)
                pre_out[rows, c] = d_pre
                j, at = divmod(c.start, units // 2)
                at = slice(at, at + c.stop - c.start)
                total = jnp.sum(d_pre.astype(F32), 0, keepdims=True)
                inb_out[j : j + 1, at] = total if n == 0 else inb_out[j : j + 1, at] + total
        wait_all(first)
        for rows in chunks(length, 256):
            part_out[rows, :] = nt(pre_out[rows, :], w_i[...]).astype(BF16)

    if level:
        token_grad, d_cls, tok_col, cls_pos = sources
        args, specs = [meta, cls_pos, token_grad, d_cls, tok_col], [SM, SM, VM, VM, VM]
    else:
        args, specs = [meta, *sources], [SM, VM, VM, VM]
    args += [xhat, scale, gains, slope, *pieces]
    specs += [ANY, VM, VM, ANY] + [ANY] * 13
    return pl.pallas_call(
        body,
        out_shape=[
            sds((length, width), BF16), sds((length, width), F32), sds((length, width), BF16),
            sds((length, units), BF16), sds((3, width), F32), sds((2, units // 2), F32),
        ],
        in_specs=specs,
        out_specs=[VM] * 6,
        scratch_shapes=[
            pltpu.VMEM((width, units), BF16), pltpu.VMEM((width, units), BF16),
            pltpu.SemaphoreType.DMA((copies_of(pieces[5]),)),
            pltpu.VMEM((length, width), BF16), pltpu.VMEM((length, units), BF16),
            pltpu.SemaphoreType.DMA((2,)),
        ],
        compiler_params=params(),
        cost_estimate=takes(9),
        name="ffn_backward",
    )(*args)


def grads_of(nz, rz, width):
    half = nz // 2
    return [sds((nz, rz, width), BF16), sds((half, rz, width), BF16), sds((half, rz, width), BF16)]


def put_grad(outs, j, k, nz, column, value, first=0):
    half, (height, width) = nz // 2, value.shape
    if k < half:
        out, at = outs[0], k + (half if j == 0 else 0)
    else:
        out, at = outs[2 if j == 0 else 1], k - half
    out[at, first : first + height, column : column + width] = value.astype(BF16)


def ffn_grads(meta, mid, d_pre, d_ffn, act, nz):
    length, width = mid.shape
    units = d_pre.shape[1]
    one = units // 2
    rz = width // nz

    def body(meta, mid, d_pre, d_ffn, act, *refs):
        outs, (mid_t, ffn_t) = refs[:3], refs[3:]
        mid_t[...] = mid[...].T.astype(BF16)
        ffn_t[...] = d_ffn[...].astype(F32).T.astype(BF16)
        for j in range(2):
            c = slice(j * one, (j + 1) * one)
            for k in range(nz):
                rows = zrows(meta, k, rz)
                put_grad(outs, j, k, nz, 0, nn(mid_t[rows, :], d_pre[:, c]))
                put_grad(outs, j, k, nz, one, nn(ffn_t[rows, :], act[:, c]))

    return pl.pallas_call(
        body,
        out_shape=grads_of(nz, rz, units),
        in_specs=[SM] + [VM] * 4,
        out_specs=[VM] * 3,
        scratch_shapes=[pltpu.VMEM((width, length), BF16)] * 2,
        compiler_params=params(),
        cost_estimate=takes(7),
        name="ffn_grads",
    )(meta, mid, d_pre, d_ffn, act)


def attn_backward(meta, d_second, parts, xhat, scale, gains, qkv, probs, pieces, cols):
    four = 4 * cols
    length, width = d_second.shape
    three = 3 * cols
    heads = 2 * cols // HD

    def body(meta, d_second, own, other, xhat, scale, gain, qkv, probs, p0, p1, p2, p3, p4, p5, p6, p7, p8, p9, p10, p11, p12,
             part_out, first_out, low_out, dqkv_out, vec_out, sum_out,
             w_a, d_ctx, acc_v, acc_k, sems):
        waits = load_a(meta, (p0, p1, p2, p3, p4, p5, p6, p7, p8, p9, p10, p11, p12), w_a, sems)
        sums = [jnp.zeros((1, width), F32) for _ in range(3)]
        for rows in chunks(length):
            d_mid = d_second[rows, :] + (own[rows, :].astype(F32) + other[rows, :].astype(F32))
            hat = xhat[rows, :].astype(F32)
            d_first = norm_back_rows(d_mid, gain[0:1, :], hat, scale[rows, :])
            first_out[rows, :] = d_first
            low_out[rows, :] = d_first.astype(BF16)
            for n, item in enumerate((d_mid * hat, d_mid, d_first)):
                sums[n] = sums[n] + jnp.sum(item, 0, keepdims=True)
        for n in range(3):
            vec_out[n : n + 1, :] = sums[n]
        wait_all(waits)
        for j in range(2):
            for rows in chunks(length, 256):
                d_ctx[rows, j * cols : (j + 1) * cols] = nn(low_out[rows, :], w_a[j, :, three:]).astype(BF16)
        k_t = jnp.concatenate(
            [qkv[:, j * three + cols : j * three + 2 * cols].astype(F32) for j in range(2)], 1
        ).T.astype(BF16)
        for h in range(heads):
            j, i = divmod(h, cols // HD)
            at = j * three + i * HD
            q_cols, k_cols, v_cols = (slice(at + n * cols, at + n * cols + HD) for n in range(3))
            for n, queries in enumerate(chunks(length, 256)):
                d_o = d_ctx[queries, h * HD : (h + 1) * HD]
                d_p = nt(qkv[:, v_cols], d_o)
                p = probs[h, :, queries]
                wide = p.astype(F32)
                d_s = (wide * (d_p - jnp.sum(wide * d_p, 0, keepdims=True))).astype(BF16)
                d_v = nn(p, d_o)
                d_k = nn(d_s, qkv[queries, q_cols])
                acc_v[...] = d_v if n == 0 else acc_v[...] + d_v
                acc_k[...] = d_k if n == 0 else acc_k[...] + d_k
                d_q = nn(k_t[h * HD : (h + 1) * HD], d_s)
                dqkv_out[queries, q_cols] = (d_q.T * 0.125).astype(BF16)
            dqkv_out[:, v_cols] = acc_v[...].astype(BF16)
            dqkv_out[:, k_cols] = (acc_k[...] * 0.125).astype(BF16)
        for j in range(2):
            sum_out[j : j + 1, :] = jnp.sum(
                dqkv_out[:, j * three : (j + 1) * three].astype(F32), 0, keepdims=True
            )
        for rows in chunks(length, 256):
            part_out[rows, :] = (
                nt(dqkv_out[rows, :three], w_a[0, :, :three]) + nt(dqkv_out[rows, three:], w_a[1, :, :three])
            ).astype(BF16)

    return pl.pallas_call(
        body,
        out_shape=[
            sds((length, width), BF16), sds((length, width), F32), sds((length, width), BF16),
            sds((length, 2 * three), BF16), sds((3, width), F32), sds((2, three), F32),
        ],
        in_specs=[SM] + [VM] * 8 + [ANY] * 13,
        out_specs=[VM] * 6,
        scratch_shapes=[
            pltpu.VMEM((2, width, four), BF16), pltpu.VMEM((length, 2 * cols), BF16),
            pltpu.VMEM((length, HD), F32), pltpu.VMEM((length, HD), F32),
            pltpu.SemaphoreType.DMA((copies_of(pieces[5]),)),
        ],
        compiler_params=params(),
        cost_estimate=takes(15),
        name="attn_backward",
    )(meta, d_second, *parts, xhat, scale, gains, qkv, probs, *pieces)


def attn_grads(meta, places, x, d_attn, d_qkv, ctx, vectors, nz, extra):
    length, width = x.shape
    three = d_qkv.shape[1] // 2
    cols = ctx.shape[1] // 2
    rz = width // nz

    def body(meta, places, x, d_attn, d_qkv, ctx, vec1, vec2, sum_qkv, sum_inb, *refs):
        outs, (x_t, a_t, norm_rows_, qv_rows, inb_rows) = refs[:3], refs[3:]
        x_t[...] = x[...].astype(F32).T.astype(BF16)
        a_t[...] = d_attn[...].astype(F32).T.astype(BF16)
        for j in range(2):
            for k in range(nz):
                rows = zrows(meta, k, rz)
                grad = nn(x_t[rows, :], d_qkv[:, j * three : (j + 1) * three])
                put_grad(outs, j, k, nz, 0, grad)
                put_grad(outs, j, k, nz, three, nn(a_t[rows, :], ctx[:, j * cols : (j + 1) * cols]))
        if not extra:
            return
        piece, part = width // (4 * nz), cols // nz
        units = sum_inb.shape[1] // nz
        norm_rows_[...] = jnp.zeros_like(norm_rows_)
        norm_rows_[0:3, :] = vec1[...]
        norm_rows_[3:6, :] = vec2[...]
        for j in range(2):
            qv_rows[...] = jnp.zeros_like(qv_rows)
            qv_rows[0:1, :cols] = sum_qkv[j : j + 1, :cols]
            qv_rows[1:2, :cols] = sum_qkv[j : j + 1, 2 * cols : three]
            inb_rows[...] = jnp.zeros_like(inb_rows)
            inb_rows[0:1, :] = sum_inb[j : j + 1, :]
            for k in range(nz):
                d = places[2 + k]
                from_norm = pltpu.roll(norm_rows_[...], width - (d * 4 + places[j]) * piece, 1)
                from_qv = pltpu.roll(qv_rows[...], width - d * part, 1)
                from_inb = pltpu.roll(inb_rows[...], width - d * units, 1)
                lane = lax.broadcasted_iota(jnp.int32, (8, 2 * cols), 1)
                upper = jnp.where(lane < piece, from_norm[:, : 2 * cols], 0.0)
                lower = jnp.where(lane < part, from_qv[:, : 2 * cols], 0.0)
                shifted = pltpu.roll(from_inb, 128, 1)[:, : 2 * cols]
                inside = jnp.logical_and(lane >= 128, lane < 128 + units)
                lower = jnp.where(inside, shifted, lower)
                put_grad(outs, j, k, nz, 0, jnp.concatenate([upper, lower], 0), rz)
                put_grad(outs, j, k, nz, 2 * cols, jnp.zeros((extra, 2 * cols), F32), rz)

    return pl.pallas_call(
        body,
        out_shape=grads_of(nz, rz + extra, three + cols),
        in_specs=[SM, SM] + [VM] * 8,
        out_specs=[VM] * 3,
        scratch_shapes=[pltpu.VMEM((width, length), BF16)] * 2 + [pltpu.VMEM((8, width), F32)] * 3,
        compiler_params=params(),
        cost_estimate=takes(4),
        name="attn_grads",
    )(meta, places, x, d_attn, d_qkv, ctx, *vectors)


def loss_kernel(own, perm, slots, queries, positive_col, n_own):
    n_q, width = queries.shape
    n_p = slots.shape[0]

    def body(own, perm, slots, queries, pos, loss_out, d_out):
        passages = nn(perm[...], slots[...]).astype(BF16)
        logits = nt(queries[...], passages)
        top = jnp.max(logits, -1, keepdims=True)
        log_total = top + jnp.log(jnp.sum(jnp.exp(logits - top), -1, keepdims=True))
        index = lax.broadcasted_iota(jnp.int32, (n_q, n_p), 1)
        hits = pos[...] == index
        chosen = jnp.sum(jnp.where(hits, logits, 0.0), -1, keepdims=True)
        loss_out[...] = jnp.sum(log_total - chosen, 0, keepdims=True) / n_q
        d_logits = (16.0 * (jnp.exp(logits - log_total) - jnp.where(hits, 1.0, 0.0))).astype(BF16)
        pick = jnp.where(
            lax.broadcasted_iota(jnp.int32, (n_p, 128), 0)
            == lax.broadcasted_iota(jnp.int32, (n_p, 128), 1) + own[0],
            1.0, 0.0,
        ).astype(BF16)
        cols = nn(d_logits, pick)
        d_out[...] = nn(cols.T.astype(BF16), queries[...])[:n_own]

    return pl.pallas_call(
        body,
        out_shape=[sds((1, 1), F32), sds((n_own, width), F32)],
        in_specs=[SM] + [VM] * 4,
        out_specs=[VM] * 2,
        compiler_params=params(),
        cost_estimate=takes(1),
        name="contrast",
    )(own, perm, slots, queries, positive_col)


def on_device(
    inputs, cls_pos, w_qkv, qv_bias, w_out, w_in, in_bias, w_ffn_out,
    layer_gains, shifts, queries, positive, token_grad,
):
    core = lax.axis_index("section")
    dp = lax.axis_index("dp")
    me = lax.axis_index("tensor")
    n_dp = lax.axis_size("dp")
    n_t = lax.axis_size("tensor")
    first_core = core == 0
    rows_dev, share, width = inputs.shape
    cols = w_qkv.shape[3]
    units = w_in.shape[2]
    length = n_t * share
    n_chips = n_dp * n_t
    piece = width // n_chips
    order = dp_order()
    direct = direct_dp()
    nz, extra = (4, 16) if direct else (2, 0)
    t_ids = jnp.arange(n_t, dtype=jnp.int32)

    vec = jnp.concatenate(
        [layer_gains.reshape(-1), shifts.reshape(-1), qv_bias.reshape(-1), in_bias.reshape(-1)]
    )
    n_gain, n_shift, n_qv, n_inb = layer_gains.size, shifts.size, qv_bias.size, in_bias.size
    n_vec = vec.shape[0]
    flat = jnp.concatenate(
        [vec, queries.reshape(-1), (positive // 16).astype(BF16), (positive % 16).astype(BF16)]
    )
    flat = jnp.pad(flat, (0, -flat.shape[0] % 2048)).reshape(-1, 128)

    def spread_rows(block):
        blocks = [lax.dynamic_index_in_dim(block, me ^ k, 0, keepdims=False) for k in range(n_t)]
        return jnp.concatenate(exchange_rows(blocks), 0)

    pack = jnp.concatenate(
        [w_qkv[0, :, 0], w_qkv[0, :, 1], w_qkv[0, :, 2], w_out[0].T, w_in[0], w_ffn_out[0].T], 1
    )
    message = spread_dp(flat)
    if direct:
        own = pack
        z_a = rest_dp(after(pack[:, :width], message))
    else:
        pack = lax.all_gather(pack, "dp", axis=0, tiled=True)
        own, other_rows = pack[: width // 2], pack[width // 2 :][None]
    message = spread_tensor(message)
    near0, far0 = gather_own(after(own, message))
    both0 = gather_own_both(near0, far0)
    owns = [own, near0, far0, *both0]

    def halves_of(blocks, first, size, *earlier):
        half = size // 2
        if not direct:
            blocks = other_rows[:, :, first : first + size]
            return blocks[:, :, :half], blocks[:, :, half:]
        blocks = after(blocks, *earlier)
        return jnp.stack([b[:, :half] for b in blocks]), jnp.stack([b[:, half:] for b in blocks])

    rest_a = jnp.stack(after(z_a, near0, far0)) if direct else other_rows[:, :, :width]
    near_a, far_a = gather_own(rest_a)
    if direct:
        z_b = rest_dp(after(pack[:, width:], rest_a))
    rows_in = spread_rows(after(jnp.where(first_core, inputs, token_grad), near_a))
    near_a, far_a = after((near_a, far_a), both0, z_b[:2] if direct else near_a)
    both_a = gather_both(near_a[:, :, : width // 2], far_a[:, :, width // 2 :])
    rows_got = swap_cores(rows_in)
    x_low = jnp.where(first_core, rows_in, rows_got)
    tokens = jnp.where(first_core, rows_got, rows_in)
    rest_b = halves_of(z_b if direct else None, width, 2 * units, both_a)
    near_b = gather_near(rest_b)
    pieces_a = [*owns, rest_a, rest_a, near_a, near_a, far_a, far_a, *both_a]

    zrow = order * (width // n_dp) if direct else jnp.arange(2, dtype=jnp.int32) * (width // 2)
    metas = [
        jnp.concatenate([(core == level)[None].astype(jnp.int32), zrow.astype(jnp.int32)])
        for level in range(2)
    ]
    slots = [me ^ (2 * (core != level) + jnp.arange(2, dtype=jnp.int32)) for level in range(2)]
    places = [jnp.concatenate([s, order[:nz]]).astype(jnp.int32) for s in slots]
    hots = [(s[:, None] == t_ids[None, :]).astype(F32) for s in slots]

    positions = jnp.concatenate(
        [(me ^ k) * share + jnp.arange(share, dtype=jnp.int32) for k in range(n_t)]
    )
    cls_row = lax.dynamic_index_in_dim(cls_pos, me, 0, keepdims=False)
    segments = jnp.sum((positions[:, None] >= cls_row[None, :]).astype(jnp.int32), -1)
    seg_col, seg_row = segments[:, None], segments[None, :]
    tok_col, tok_row = positions[:, None], positions[None, :]

    slot_ids = (order[None, :] * n_t + (me ^ t_ids)[:, None]).reshape(-1)
    to_natural = (jnp.arange(n_chips, dtype=jnp.int32)[:, None] == slot_ids[None, :]).astype(BF16)
    table = nn(to_natural, message.reshape(n_chips, -1))
    own_table = table[:, :n_vec].astype(BF16)
    other_table = swap_cores(own_table)
    tables = jnp.where(
        first_core, jnp.stack([own_table, other_table]), jnp.stack([other_table, own_table])
    ).astype(F32)
    at = 0
    gains = tables[:, :, at : at + n_gain].reshape(2, n_chips, 2, piece).transpose(0, 2, 1, 3).reshape(2, 2, width)
    at += n_gain
    shift = tables[:, :, at : at + n_shift].reshape(2, n_chips, 4, piece).transpose(0, 2, 1, 3).reshape(2, 4, width)
    at += n_shift
    qv = tables[:, :, at : at + n_qv].reshape(2, n_dp, n_t, 2, cols // n_dp)
    qv = qv.transpose(0, 3, 2, 1, 4).reshape(2, 2, n_t, cols)
    at += n_qv
    inb = tables[:, :, at : at + n_inb].reshape(2, n_dp, n_t, n_inb).transpose(0, 2, 1, 3).reshape(2, n_t, units)
    vectors = []
    for level in range(2):
        bias = jnp.sum(hots[level][None, :, :, None] * qv[level][:, None], 2)
        bias = jnp.stack([bias[0], jnp.zeros_like(bias[0]), bias[1]], 1).reshape(1, -1)
        bias_in = jnp.sum(hots[level][:, :, None] * inb[level][None], 1).reshape(1, -1)
        vectors.append((gains[level], shift[level], bias, bias_in))
    at = n_vec
    q_dev = queries.shape[0]
    all_q = table[:, at : at + q_dev * width].reshape(-1, width).astype(BF16)
    at += q_dev * width
    all_pos = table[:, at : at + q_dev] * 16.0 + table[:, at + q_dev : at + 2 * q_dev]
    all_pos = all_pos.astype(jnp.int32).reshape(-1, 1)
    n_cls = cls_row.shape[0]
    perm = jnp.repeat(jnp.repeat(to_natural, n_cls, 0), n_cls, 1)
    perm = perm * jnp.tile(jnp.eye(n_cls, dtype=BF16), (n_chips, n_chips))

    vectors, all_q, all_pos, perm, x_low = lax.optimization_barrier(
        (vectors, all_q, all_pos, perm, x_low)
    )
    saved = []
    source, parts, norms = x_low, None, None
    for level in range(2):
        gain, shift, bias, bias_in = vectors[level]
        outs = attn_forward(
            level, metas[level], source, parts, norms, pieces_a, bias, seg_col, seg_row, cols
        )
        part, qkv, probs, ctx = outs[:4]
        if level == 0:
            pieces_b = [*owns, *rest_b, *near_b, *gather_both(near_b[0], after(near_b[3], part))]
        if level:
            x, xhat2, scale2 = outs[4:]
            saved[0]["second"] = (xhat2, scale2)
        else:
            x = x_low
        part, mid, xhat1, scale1, act, slope = ffn_forward(
            metas[level], x, (part, swap_cores(part)), gain, shift, pieces_b, bias_in, units
        )
        saved.append(
            dict(x=x, qkv=qkv, probs=probs, ctx=ctx, mid=mid, xhat1=xhat1, scale1=scale1, act=act, slope=slope)
        )
        source, parts, norms = mid, (part, swap_cores(part)), (gain, shift)
    y, xhat2, scale2, cls_own = last_norm(source, parts, *norms, tok_row, cls_row)
    saved[1]["second"] = (xhat2, scale2)

    cls_slots = spread_tensor(spread_dp(cls_own)).reshape(n_chips * n_cls, width)
    first_own = ((dp * n_t + me) * n_cls).astype(jnp.int32)[None]
    mean_loss, d_cls = loss_kernel(first_own, perm, cls_slots, all_q, all_pos, n_cls)

    vector_rows = [None, None]
    sources = (tokens, d_cls, tok_col, cls_row)
    sums_a, sums_b = [None, None], [None, None]
    for level in (1, 0):
        gain = vectors[level][0]
        kept = saved[level]
        meta = metas[level]
        xhat2, scale2 = kept["second"]
        if level == 0:
            sources = (after(sources[0], sums_b[1].first(grads_a[1])), *sources[1:])
        part, d_second, d_ffn, d_pre, vec2, sum_inb = ffn_backward(
            level, meta, sources, xhat2, scale2, gain, kept["slope"], pieces_b, units
        )
        other = swap_cores(part)
        if level == 0:
            d_ffn = after(d_ffn, sums_a[1].first(part))
        grads_b = ffn_grads(meta, kept["mid"], d_pre, d_ffn, kept["act"], nz)
        sums_b[level] = Reduction(grads_b, level)
        d_second = after(d_second, grads_b[1])
        if level == 0:
            d_second = after(d_second, sums_b[1].second(grads_b[1]))
        part, d_first, d_attn, d_qkv, vec1, sum_qkv = attn_backward(
            meta, d_second, (part, other), kept["xhat1"], kept["scale1"], gain,
            kept["qkv"], kept["probs"], pieces_a, cols,
        )
        other = swap_cores(part)
        if level == 0:
            d_attn = after(d_attn, sums_b[0].first(sums_a[1].second(part)))
        grads_a = attn_grads(
            meta, places[level], kept["x"], d_attn, d_qkv, kept["ctx"], (vec1, vec2, sum_qkv, sum_inb), nz, extra
        )
        sums_a[level] = Reduction(grads_a, level)
        vector_rows[level] = (vec1, vec2, sum_qkv, sum_inb)
        sources = (d_first, part, other)
    sums_b[1].third(grads_a[1])
    sums_b[0].second_direct(sums_b[1].pieces)
    sums_a[1].third(sums_b[0].sums)
    sums_a[0].first(sums_a[1].pieces, sums_b[0].hops[:1] if direct else sums_b[0].sums)
    sums_a[0].second_direct(sums_a[0].added)
    last_a1, last_b1 = last_dp([sums_a[1], sums_b[1]], sums_a[0].sums)
    total_b0 = sums_b[0].third_direct()
    d_hidden = d_first + (part.astype(F32) + other.astype(F32))
    outgoing = jnp.where(first_core, d_hidden, y.astype(F32))
    low = after(outgoing.astype(BF16), sums_a[0].added).reshape(n_t, share, width)
    incoming = [outgoing[:share]] + [b.astype(F32) for b in exchange_rows([low[k] for k in range(n_t)])[1:]]
    boundary = jnp.zeros((n_t, share, width), F32)
    for k in range(n_t):
        boundary = lax.dynamic_update_index_in_dim(boundary, incoming[k], me ^ k, 0)
    tot_b, tot_a = (
        jnp.where(first_core, low, sum(p.astype(F32) for p in high))
        for low, high in ((total_b0, last_b1), (sums_a[0].third_direct(), last_a1))
    )
    if direct:
        end = width // n_dp
        own = tot_a[end : end + 6, :piece]
        qv = tot_a[end + 8 : end + 10, : qv_bias.shape[3]]
        grad_inb = tot_a[end + 8 : end + 9, 128 : 128 + n_inb]
        tot_a = tot_a[:end]
    else:
        tables = []
        for level in range(2):
            vec1, vec2, sum_qkv, sum_inb = vector_rows[level]
            by_t = lax.dot_general(
                hots[level], jnp.concatenate([sum_qkv, sum_inb], 1), (((0,), (0,)), ((), ())),
                precision=lax.Precision.HIGHEST,
            )
            whole = 0.5 * jnp.concatenate([vec1, vec2])
            whole = jnp.pad(whole, ((0, 0), (0, by_t.shape[1] - width)))
            tables.append(jnp.concatenate([whole, by_t]))
        tables = lax.psum(jnp.stack(tables), ("section", "dp", "tensor"))
        flat = jnp.where(first_core, tables[0], tables[1])
        own = lax.dynamic_slice_in_dim(flat[:6, :width], (dp * n_t + me) * piece, piece, 1)
        by_t = lax.dynamic_slice_in_dim(flat, 6 + me, 1, 0)
        qv = jnp.concatenate([by_t[:, :cols], by_t[:, 2 * cols : 3 * cols]])
        qv = lax.dynamic_slice_in_dim(qv, dp * qv_bias.shape[3], qv_bias.shape[3], 1)
        grad_inb = lax.dynamic_slice_in_dim(by_t[:, 3 * cols :], dp * n_inb, n_inb, 1)
    grad_gains = jnp.concatenate([own[0:1], own[3:4]]).reshape(layer_gains.shape)
    grad_shifts = jnp.concatenate([own[2:3], own[1:2], own[5:6], own[4:5]]).reshape(shifts.shape)
    grad_qv, grad_inb = qv.reshape(qv_bias.shape), grad_inb.reshape(in_bias.shape)

    grad_qkv = jnp.stack([tot_a[:, n * cols : (n + 1) * cols] for n in range(3)], 1)[None]
    grad_out = tot_a[:, 3 * cols :].T[None]
    grad_in = tot_b[:, :units][None]
    grad_ffn = tot_b[:, units:].T[None]
    return (
        grad_qkv, grad_qv, grad_out, grad_in, grad_inb, grad_ffn,
        grad_gains, grad_shifts, boundary[None], mean_loss.reshape(()),
    )


def solution(mesh):
    return jax.shard_map(
        on_device,
        mesh=mesh,
        in_specs=(
            P("dp", "tensor", None),
            P("dp", None),
            P("section", "dp", None, "tensor"),
            P("section", None, "tensor", "dp"),
            P("section", "tensor", "dp"),
            P("section", "dp", "tensor"),
            P("section", "tensor", "dp"),
            P("section", "tensor", "dp"),
            P("section", None, ("dp", "tensor")),
            P("section", None, ("dp", "tensor")),
            P(("dp", "tensor"), None),
            P(("dp", "tensor")),
            P("dp", "tensor", None),
        ),
        out_specs=(
            P("section", "dp", None, "tensor"),
            P("section", None, "tensor", "dp"),
            P("section", "tensor", "dp"),
            P("section", "dp", "tensor"),
            P("section", "tensor", "dp"),
            P("section", "tensor", "dp"),
            P("section", None, ("dp", "tensor")),
            P("section", None, ("dp", "tensor")),
            P("section", "dp", "tensor", None),
            P(),
        ),
        check_vma=False,
    )
```

```python
import jax
import jax.numpy as jnp
from jax import lax
from jax.experimental import pallas as pl
from jax.experimental.pallas import tpu as pltpu
from jax.sharding import PartitionSpec as P

HD = 64
PARTNER = 1
CROSS = 2
BF16 = jnp.bfloat16
F32 = jnp.float32


def mm(left, right, dims):
    return lax.dot_general(left, right, (dims, ((), ())), preferred_element_type=F32)


def nn(left, right):
    return mm(left, right, ((1,), (0,)))


def nt(left, right):
    return mm(left, right, ((1,), (1,)))


def after(block, *earlier):
    return lax.optimization_barrier((block, *earlier))[0]


def swap_cores(block):
    return lax.ppermute(block, "section", [(0, 1), (1, 0)])


def hop(block, axis, flip):
    return lax.ppermute(block, axis, [(i, i ^ flip) for i in range(lax.axis_size(axis))])


def core_hop(block, axis, flip, core):
    size = lax.axis_size(axis)
    route = [(core * size + i, core * size + (i ^ flip)) for i in range(size)]
    return lax.ppermute(block, ("section", axis), route)


def cross_hop(block, source):
    size = lax.axis_size("tensor")
    route = [(source * size + i, (1 - source) * size + (i ^ CROSS)) for i in range(size)]
    return lax.ppermute(block, ("section", "tensor"), route)


def direct_dp():
    return lax.axis_size("dp") == 4


def dp_order():
    size = lax.axis_size("dp")
    if direct_dp():
        return lax.axis_index("dp") ^ jnp.arange(size, dtype=jnp.int32)
    return jnp.arange(size, dtype=jnp.int32)


def spread_dp(block):
    if direct_dp():
        return jnp.stack([block] + [hop(block, "dp", k) for k in range(1, 4)])
    return lax.all_gather(block, "dp", axis=0, tiled=False)


def spread_tensor(block):
    return jnp.stack([block] + [hop(block, "tensor", k) for k in range(1, 4)])


def double(block, axis):
    pair = jnp.stack([block, hop(block, axis, 1)])
    return jnp.concatenate([pair, hop(pair, axis, 2)])


def exchange_rows(blocks):
    first = hop(jnp.stack([blocks[1], blocks[3]]), "tensor", 1)
    second = hop(jnp.stack([blocks[2], first[1]]), "tensor", 2)
    return [blocks[0], first[0], second[0], second[1]]


def cross_all(block):
    size = lax.axis_size("tensor")
    route = [(s * size + i, (1 - s) * size + (i ^ CROSS)) for s in range(2) for i in range(size)]
    return lax.ppermute(block, ("section", "tensor"), route)


def rest_dp(own):
    return [hop(own, "dp", k) for k in range(1, 4)]


def gather_own(own):
    near, far = hop(own, "tensor", PARTNER), cross_all(own)
    return near, far


def gather_own_both(near, far):
    half = near.shape[1] // 2
    return cross_all(near[:, :half]), hop(far[:, half:], "tensor", PARTNER)


def gather_near(rest):
    a, b = rest
    near_a, far_b = hop(a, "tensor", PARTNER), cross_all(b)
    near_b, far_a = hop(b, "tensor", PARTNER), cross_all(a)
    return near_a, near_b, far_a, far_b


def gather_both(near_a, far_b):
    return cross_all(near_a), hop(far_b, "tensor", PARTNER)


def add_low(*items):
    total = items[0].astype(F32)
    for item in items[1:]:
        total = total + item.astype(F32)
    return total.astype(BF16)


class Reduction:
    def __init__(self, grads, core):
        self.core = core
        self.pair, self.next_b, self.own_b = grads
        self.got = cross_hop(self.pair, 1 - core)
        self.near_b = hop(self.next_b, "tensor", PARTNER)

    def first(self, *earlier):
        half = self.next_b.shape[0]
        self.parts = pair, own_b, got, near_b = after((self.pair, self.own_b, self.got, self.near_b), *earlier)
        self.added = add_low(pair[:half], got[:half]), add_low(own_b, near_b)
        self.near_a = core_hop(self.added[0], "tensor", PARTNER, self.core)
        self.far_b = cross_hop(self.added[1], 1 - self.core)
        return self.added

    def sum_halves(self, *earlier):
        half = self.next_b.shape[0]
        near_a, far_b, (pair, own_b, got, near_b) = after((self.near_a, self.far_b, self.parts), *earlier)
        return add_low(pair[half:], got[half:], near_a), add_low(own_b, near_b, far_b)

    def scatter(self):
        whole = jnp.concatenate(self.sums).reshape(-1, self.own_b.shape[2])
        return [lax.psum_scatter(whole, "dp", scatter_dimension=0, tiled=True)]

    def second_direct(self, *earlier):
        a, b = self.sums = self.sum_halves(*earlier)
        if direct_dp():
            self.hops = [
                core_hop(block, "dp", k, self.core) for k, block in ((1, a[1]), (2, b[0]), (3, b[1]))
            ]
        return self.sums

    def third_direct(self, *earlier):
        if not direct_dp():
            return sum(p.astype(F32) for p in self.scatter())
        return sum(p.astype(F32) for p in after([self.sums[0][0], *self.hops], *earlier))

    def second(self, *earlier):
        self.sums = self.sum_halves(*earlier)
        if direct_dp():
            self.across = core_hop(self.sums[1], "dp", 2, self.core)
        return self.sums

    def third(self, *earlier):
        if not direct_dp():
            self.pieces = self.scatter()
            return self.pieces
        a, across = after((self.sums[0], self.across), *earlier)
        self.pieces = [add_low(a[k], across[k]) for k in range(2)]
        return self.pieces


def last_dp(reductions, *earlier):
    if not direct_dp():
        return [r.pieces for r in reductions]
    high = max(r.pieces[0].shape[0] for r in reductions)
    block = [jnp.pad(r.pieces[1], ((0, high - r.pieces[1].shape[0]), (0, 0))) for r in reductions]
    got = core_hop(after(jnp.concatenate(block, 1), *earlier), "dp", 1, reductions[0].core)
    at, out = 0, []
    for r in reductions:
        rows, width = r.pieces[0].shape
        out.append([r.pieces[0], got[:rows, at : at + width]])
        at += width
    return out


VMEM_LIMIT = 48 * 1024 * 1024
CHUNK = 128


def takes(micros):
    return pl.CostEstimate(flops=int(micros * 1.1e9), bytes_accessed=0, transcendentals=0)


def params():
    return pltpu.CompilerParams(vmem_limit_bytes=VMEM_LIMIT)


ANY = pl.BlockSpec(memory_space=pl.ANY)
VM = pl.BlockSpec(memory_space=pltpu.VMEM)
SM = pl.BlockSpec(memory_space=pltpu.SMEM)


def sds(shape, dtype):
    return jax.ShapeDtypeStruct(shape, dtype)


def chunks(length, step=CHUNK):
    return [slice(i, i + step) for i in range(0, length, step)]


def norm_rows(z):
    centre = z - jnp.mean(z, -1, keepdims=True)
    spread = jnp.mean(centre * centre, -1, keepdims=True)
    scale = lax.rsqrt(spread + 1e-05)
    return centre * scale, scale


def norm_back_rows(d_out, gain, xhat, scale):
    g = d_out * gain
    m1 = jnp.mean(g, -1, keepdims=True)
    m2 = jnp.mean(g * xhat, -1, keepdims=True)
    return scale * (g - m1 - xhat * m2)


def gelu_parts(x):
    e = jnp.exp(-0.5 * x * x)
    t = 1.0 / (1.0 + 0.2316418882 * jnp.abs(x))
    poly = t * (
        0.127414796 + t * (-0.142248368 + t * (0.7107068705 + t * (-0.7265760135 + t * 0.5307027145)))
    )
    tail = poly * e
    cdf = jnp.where(x < 0.0, tail, 1.0 - tail)
    return x * cdf, cdf + x * e * 0.3989422804014327


def zrows(meta, k, rz):
    return pl.ds(pl.multiple_of(meta[1 + k], 64), rz)


def cut(start, width, at):
    if start < at < start + width:
        return [(start, at - start), (at, start + width - at)]
    return [(start, width)]


def load_weights(meta, pieces, base, places, sems):
    own, near0, far0, a0, b0, *halves = pieces
    rest, near, far, both = halves[0:2], halves[2:4], halves[4:6], halves[6:8]
    split0, split, count = a0.shape[1], both[0].shape[2], rest[0].shape[0]
    home = meta[0] == 1
    lists = [[] for _ in places]
    at = 0
    for j in range(2):
        for k in range(count + 1):
            rows = zrows(meta, k, own.shape[0])
            for n, (start, width, place) in enumerate(places):
                offset = 0 if k else base
                for g, w in cut(offset + start, width, split if k else split0):
                    side, column = divmod(g, split if k else split0)
                    if k == 0:
                        mine = (near0 if j else own).at[:, pl.ds(g, w)]
                        other = (a0, b0)[side].at[:, pl.ds(column, w)] if j else far0.at[:, pl.ds(g, w)]
                    else:
                        mine, other = (
                            v[side].at[k - 1, :, pl.ds(g if v[0].shape[2] > split else column, w)]
                            for v in ((near, both) if j else (rest, far))
                        )
                    dst = place(j, rows, g - offset - start, w)
                    first = pltpu.make_async_copy(mine, dst, sems.at[at])
                    second = pltpu.make_async_copy(other, dst, sems.at[at])
                    at += 1

                    @pl.when(home)
                    def _():
                        first.start()

                    @pl.when(jnp.logical_not(home))
                    def _():
                        second.start()

                    lists[n].append(first)
    return lists


def copies_of(rest):
    return 2 * 3 * (1 + rest.shape[0])


def wait_all(waits):
    for made in waits:
        made.wait()


def load_a(meta, pieces, w_a, sems):
    width = w_a.shape[2]
    return load_weights(
        meta, pieces, 0, [(0, width, lambda j, rows, c, w: w_a.at[j, rows, pl.ds(c, w)])], sems
    )[0]


def load_b(meta, pieces, w_i, w_f, sems):
    one = w_i.shape[1] // 2
    base = pieces[0].shape[1] - 2 * one
    return load_weights(
        meta,
        pieces,
        base,
        [
            (0, one, lambda j, rows, c, w: w_i.at[rows, pl.ds(j * one + c, w)]),
            (one, one, lambda j, rows, c, w: w_f.at[rows, pl.ds(j * one + c, w)]),
        ],
        sems,
    )


def attn_forward(level, meta, x_or_mid, parts, norms, pieces, bias, seg_col, seg_row, cols):
    four = 4 * cols
    length, width = x_or_mid.shape
    three = 3 * cols
    heads = 2 * cols // HD

    def body(meta, *refs):
        refs = list(refs)
        src = refs.pop(0)
        if level:
            own, other, gain, shift = (refs.pop(0) for _ in range(4))
        pieces = [refs.pop(0) for _ in range(13)]
        bias, sc, sr = (refs.pop(0) for _ in range(3))
        part_out, qkv_out, probs_out, ctx_out = (refs.pop(0) for _ in range(4))
        if level:
            x_out, xhat_out, scale_out = (refs.pop(0) for _ in range(3))
        w_a, sems = refs
        waits = load_a(meta, pieces, w_a, sems)
        if level:
            for rows in chunks(length):
                z = src[rows, :] + (own[rows, :].astype(F32) + other[rows, :].astype(F32)) + shift[2:3, :]
                xhat, scale = norm_rows(z)
                x_out[rows, :] = (xhat * gain[1:2, :] + shift[3:4, :]).astype(BF16)
                xhat_out[rows, :] = xhat.astype(BF16)
                scale_out[rows, :] = scale
            x_ref = x_out
        else:
            x_ref = src
        wait_all(waits)
        for j in range(2):
            c = slice(j * three, (j + 1) * three)
            for rows in chunks(length, 256):
                qkv_out[rows, c] = (nn(x_ref[rows, :], w_a[j, :, :three]) + bias[:, c]).astype(BF16)
        v_t = jnp.concatenate(
            [qkv_out[:, j * three + 2 * cols : (j + 1) * three].astype(F32) for j in range(2)], 1
        ).T.astype(BF16)
        for queries in chunks(length, 256):
            same = sc[...] == sr[:, queries]
            outs = []
            for h in range(heads):
                j, i = divmod(h, cols // HD)
                at = j * three + i * HD
                q = qkv_out[queries, at : at + HD]
                k = qkv_out[:, at + cols : at + cols + HD]
                st = jnp.where(same, nt(k, q) * 0.125, -1e30)
                p = jnp.exp(st - jnp.max(st, 0, keepdims=True))
                p = (p * (1.0 / jnp.sum(p, 0, keepdims=True))).astype(BF16)
                probs_out[h, :, queries] = p
                outs.append(nn(v_t[h * HD : (h + 1) * HD], p))
            ctx = jnp.concatenate(outs, 0).T.astype(BF16)
            ctx_out[queries, :] = ctx
            part_out[queries, :] = (
                nt(ctx[:, :cols], w_a[0, :, three:]) + nt(ctx[:, cols:], w_a[1, :, three:])
            ).astype(BF16)

    outs = [
        sds((length, width), BF16), sds((length, 2 * three), BF16),
        sds((heads, length, length), BF16), sds((length, 2 * cols), BF16),
    ]
    args = [meta, x_or_mid]
    if level:
        args += [*parts, *norms]
        outs += [sds((length, width), BF16), sds((length, width), BF16), sds((length, 1), F32)]
    specs = [SM] + [VM] * (len(args) - 1) + [ANY] * 13 + [VM] * 3
    args += [*pieces, bias, seg_col, seg_row]
    return pl.pallas_call(
        body,
        out_shape=outs,
        in_specs=specs,
        out_specs=[VM] * len(outs),
        scratch_shapes=[pltpu.VMEM((2, width, four), BF16), pltpu.SemaphoreType.DMA((copies_of(pieces[5]),))],
        compiler_params=params(),
        cost_estimate=takes(13),
        name="attn_forward",
    )(*args)


def ffn_forward(meta, x, parts, gains, shifts, pieces, bias_in, half):
    units = 2 * half
    length, width = x.shape

    def body(meta, x, own, other, gain, shift, p0, p1, p2, p3, p4, p5, p6, p7, p8, p9, p10, p11, p12, bias,
             part_out, mid_out, xhat_out, scale_out, act_out, slope_out, w_i, w_f, low, sems):
        first, second = load_b(meta, (p0, p1, p2, p3, p4, p5, p6, p7, p8, p9, p10, p11, p12), w_i, w_f, sems)
        for rows in chunks(length):
            z = x[rows, :].astype(F32) + (own[rows, :].astype(F32) + other[rows, :].astype(F32)) + shift[0:1, :]
            xhat, scale = norm_rows(z)
            mid = xhat * gain[0:1, :] + shift[1:2, :]
            mid_out[rows, :] = mid
            low[rows, :] = mid.astype(BF16)
            xhat_out[rows, :] = xhat.astype(BF16)
            scale_out[rows, :] = scale
        wait_all(first)
        for rows in chunks(length, 256):
            for c in chunks(units, 512):
                pre = nn(low[rows, :], w_i[:, c]) + bias[:, c]
                act, slope = gelu_parts(pre)
                act_out[rows, c] = act.astype(BF16)
                slope_out[rows, c] = slope.astype(BF16)
        wait_all(second)
        for rows in chunks(length, 256):
            part_out[rows, :] = nt(act_out[rows, :], w_f[...]).astype(BF16)

    return pl.pallas_call(
        body,
        out_shape=[
            sds((length, width), BF16), sds((length, width), F32), sds((length, width), BF16),
            sds((length, 1), F32), sds((length, units), BF16), sds((length, units), BF16),
        ],
        in_specs=[SM] + [VM] * 5 + [ANY] * 13 + [VM],
        out_specs=[VM] * 6,
        scratch_shapes=[
            pltpu.VMEM((width, units), BF16), pltpu.VMEM((width, units), BF16),
            pltpu.VMEM((length, width), BF16), pltpu.SemaphoreType.DMA((copies_of(pieces[5]),)),
        ],
        compiler_params=params(),
        cost_estimate=takes(9),
        name="ffn_forward",
    )(meta, x, *parts, gains, shifts, *pieces, bias_in)


def last_norm(mid, parts, gains, shifts, tok_row, cls_pos):
    length, width = mid.shape
    n_cls = cls_pos.shape[0]

    def body(cls, mid_from, own, other, gain, shift, tok, y_out, xhat_out, scale_out, cls_out, mid, sem):
        get_mid = pltpu.make_async_copy(mid_from, mid, sem.at[0])
        get_mid.start()
        get_mid.wait()
        for rows in chunks(length):
            z = mid[rows, :] + (own[rows, :].astype(F32) + other[rows, :].astype(F32)) + shift[2:3, :]
            xhat, scale = norm_rows(z)
            y_out[rows, :] = (xhat * gain[1:2, :] + shift[3:4, :]).astype(BF16)
            xhat_out[rows, :] = xhat.astype(BF16)
            scale_out[rows, :] = scale
        which = lax.broadcasted_iota(jnp.int32, (16, length), 0)
        hot = jnp.zeros((16, length), F32)
        for p in range(n_cls):
            hot = jnp.where(jnp.logical_and(which == p, tok[...] == cls[p]), 1.0, hot)
        cls_out[...] = nn(hot.astype(BF16), y_out[...])[:n_cls].astype(BF16)

    return pl.pallas_call(
        body,
        out_shape=[
            sds((length, width), BF16), sds((length, width), BF16), sds((length, 1), F32),
            sds((n_cls, width), BF16),
        ],
        in_specs=[SM, ANY] + [VM] * 5,
        out_specs=[VM] * 4,
        scratch_shapes=[pltpu.VMEM((length, width), F32), pltpu.SemaphoreType.DMA((1,))],
        compiler_params=params(),
        cost_estimate=takes(2),
        name="last_norm",
    )(cls_pos, mid, *parts, gains, shifts, tok_row)


def ffn_backward(level, meta, sources, xhat, scale, gains, slope, pieces, half):
    units = 2 * half
    length, width = xhat.shape
    n_cls = sources[3].shape[0] if level else 0

    def body(meta, *refs):
        refs = list(refs)
        if level:
            cls, grad, d_cls, tok = (refs.pop(0) for _ in range(4))
        else:
            d_above, own, other = (refs.pop(0) for _ in range(3))
        xhat_from, scale, gain, slope_from = (refs.pop(0) for _ in range(4))
        pieces = [refs.pop(0) for _ in range(13)]
        part_out, second_out, low_out, pre_out, vec_out, inb_out, w_i, w_f, sems, xhat, slope, kept_sems = refs
        get_hat = pltpu.make_async_copy(xhat_from, xhat, kept_sems.at[0])
        get_slope = pltpu.make_async_copy(slope_from, slope, kept_sems.at[1])
        get_hat.start()
        get_slope.start()
        first, second = load_b(meta, pieces, w_i, w_f, sems)
        sums = [jnp.zeros((1, width), F32) for _ in range(3)]
        get_hat.wait()
        for rows in chunks(length):
            if level:
                d_out = grad[rows, :].astype(F32)
                for p in range(n_cls):
                    d_out = d_out + jnp.where(tok[rows, :] == cls[p], 1.0, 0.0) * d_cls[p : p + 1, :]
            else:
                d_out = d_above[rows, :] + (own[rows, :].astype(F32) + other[rows, :].astype(F32))
                d_out = d_out.astype(BF16).astype(F32)
            hat = xhat[rows, :].astype(F32)
            d_second = norm_back_rows(d_out, gain[1:2, :], hat, scale[rows, :])
            second_out[rows, :] = d_second
            low_out[rows, :] = d_second.astype(BF16)
            for n, item in enumerate((d_out * hat, d_out, d_second)):
                sums[n] = sums[n] + jnp.sum(item, 0, keepdims=True)
        for n in range(3):
            vec_out[n : n + 1, :] = sums[n]
        wait_all(second)
        get_slope.wait()
        for n, rows in enumerate(chunks(length, 256)):
            for c in chunks(units, units // 4):
                d_act = nn(low_out[rows, :], w_f[:, c])
                d_pre = (slope[rows, c].astype(F32) * d_act).astype(BF16)
                pre_out[rows, c] = d_pre
                j, at = divmod(c.start, units // 2)
                at = slice(at, at + c.stop - c.start)
                total = jnp.sum(d_pre.astype(F32), 0, keepdims=True)
                inb_out[j : j + 1, at] = total if n == 0 else inb_out[j : j + 1, at] + total
        wait_all(first)
        for rows in chunks(length, 256):
            part_out[rows, :] = nt(pre_out[rows, :], w_i[...]).astype(BF16)

    if level:
        token_grad, d_cls, tok_col, cls_pos = sources
        args, specs = [meta, cls_pos, token_grad, d_cls, tok_col], [SM, SM, VM, VM, VM]
    else:
        args, specs = [meta, *sources], [SM, VM, VM, VM]
    args += [xhat, scale, gains, slope, *pieces]
    specs += [ANY, VM, VM, ANY] + [ANY] * 13
    return pl.pallas_call(
        body,
        out_shape=[
            sds((length, width), BF16), sds((length, width), F32), sds((length, width), BF16),
            sds((length, units), BF16), sds((3, width), F32), sds((2, units // 2), F32),
        ],
        in_specs=specs,
        out_specs=[VM] * 6,
        scratch_shapes=[
            pltpu.VMEM((width, units), BF16), pltpu.VMEM((width, units), BF16),
            pltpu.SemaphoreType.DMA((copies_of(pieces[5]),)),
            pltpu.VMEM((length, width), BF16), pltpu.VMEM((length, units), BF16),
            pltpu.SemaphoreType.DMA((2,)),
        ],
        compiler_params=params(),
        cost_estimate=takes(9),
        name="ffn_backward",
    )(*args)


def grads_of(nz, rz, width):
    half = nz // 2
    return [sds((nz, rz, width), BF16), sds((half, rz, width), BF16), sds((half, rz, width), BF16)]


def put_grad(outs, j, k, nz, column, value, first=0):
    half, (height, width) = nz // 2, value.shape
    if k < half:
        out, at = outs[0], k + (half if j == 0 else 0)
    else:
        out, at = outs[2 if j == 0 else 1], k - half
    out[at, first : first + height, column : column + width] = value.astype(BF16)


def ffn_grads(meta, mid, d_pre, d_ffn, act, nz):
    length, width = mid.shape
    units = d_pre.shape[1]
    one = units // 2
    rz = width // nz

    def body(meta, mid, d_pre, d_ffn, act, *refs):
        outs, (mid_t, ffn_t) = refs[:3], refs[3:]
        mid_t[...] = mid[...].T.astype(BF16)
        ffn_t[...] = d_ffn[...].astype(F32).T.astype(BF16)
        for j in range(2):
            c = slice(j * one, (j + 1) * one)
            for k in range(nz):
                rows = zrows(meta, k, rz)
                put_grad(outs, j, k, nz, 0, nn(mid_t[rows, :], d_pre[:, c]))
                put_grad(outs, j, k, nz, one, nn(ffn_t[rows, :], act[:, c]))

    return pl.pallas_call(
        body,
        out_shape=grads_of(nz, rz, units),
        in_specs=[SM] + [VM] * 4,
        out_specs=[VM] * 3,
        scratch_shapes=[pltpu.VMEM((width, length), BF16)] * 2,
        compiler_params=params(),
        cost_estimate=takes(7),
        name="ffn_grads",
    )(meta, mid, d_pre, d_ffn, act)


def attn_backward(meta, d_second, parts, xhat, scale, gains, qkv, probs, pieces, cols):
    four = 4 * cols
    length, width = d_second.shape
    three = 3 * cols
    heads = 2 * cols // HD

    def body(meta, d_second, own, other, xhat, scale, gain, qkv, probs, p0, p1, p2, p3, p4, p5, p6, p7, p8, p9, p10, p11, p12,
             part_out, first_out, low_out, dqkv_out, vec_out, sum_out,
             w_a, d_ctx, acc_v, acc_k, sems):
        waits = load_a(meta, (p0, p1, p2, p3, p4, p5, p6, p7, p8, p9, p10, p11, p12), w_a, sems)
        sums = [jnp.zeros((1, width), F32) for _ in range(3)]
        for rows in chunks(length):
            d_mid = d_second[rows, :] + (own[rows, :].astype(F32) + other[rows, :].astype(F32))
            hat = xhat[rows, :].astype(F32)
            d_first = norm_back_rows(d_mid, gain[0:1, :], hat, scale[rows, :])
            first_out[rows, :] = d_first
            low_out[rows, :] = d_first.astype(BF16)
            for n, item in enumerate((d_mid * hat, d_mid, d_first)):
                sums[n] = sums[n] + jnp.sum(item, 0, keepdims=True)
        for n in range(3):
            vec_out[n : n + 1, :] = sums[n]
        wait_all(waits)
        for j in range(2):
            for rows in chunks(length, 256):
                d_ctx[rows, j * cols : (j + 1) * cols] = nn(low_out[rows, :], w_a[j, :, three:]).astype(BF16)
        k_t = jnp.concatenate(
            [qkv[:, j * three + cols : j * three + 2 * cols].astype(F32) for j in range(2)], 1
        ).T.astype(BF16)
        for h in range(heads):
            j, i = divmod(h, cols // HD)
            at = j * three + i * HD
            q_cols, k_cols, v_cols = (slice(at + n * cols, at + n * cols + HD) for n in range(3))
            for n, queries in enumerate(chunks(length, 256)):
                d_o = d_ctx[queries, h * HD : (h + 1) * HD]
                d_p = nt(qkv[:, v_cols], d_o)
                p = probs[h, :, queries]
                wide = p.astype(F32)
                d_s = (wide * (d_p - jnp.sum(wide * d_p, 0, keepdims=True))).astype(BF16)
                d_v = nn(p, d_o)
                d_k = nn(d_s, qkv[queries, q_cols])
                acc_v[...] = d_v if n == 0 else acc_v[...] + d_v
                acc_k[...] = d_k if n == 0 else acc_k[...] + d_k
                d_q = nn(k_t[h * HD : (h + 1) * HD], d_s)
                dqkv_out[queries, q_cols] = (d_q.T * 0.125).astype(BF16)
            dqkv_out[:, v_cols] = acc_v[...].astype(BF16)
            dqkv_out[:, k_cols] = (acc_k[...] * 0.125).astype(BF16)
        for j in range(2):
            sum_out[j : j + 1, :] = jnp.sum(
                dqkv_out[:, j * three : (j + 1) * three].astype(F32), 0, keepdims=True
            )
        for rows in chunks(length, 256):
            part_out[rows, :] = (
                nt(dqkv_out[rows, :three], w_a[0, :, :three]) + nt(dqkv_out[rows, three:], w_a[1, :, :three])
            ).astype(BF16)

    return pl.pallas_call(
        body,
        out_shape=[
            sds((length, width), BF16), sds((length, width), F32), sds((length, width), BF16),
            sds((length, 2 * three), BF16), sds((3, width), F32), sds((2, three), F32),
        ],
        in_specs=[SM] + [VM] * 8 + [ANY] * 13,
        out_specs=[VM] * 6,
        scratch_shapes=[
            pltpu.VMEM((2, width, four), BF16), pltpu.VMEM((length, 2 * cols), BF16),
            pltpu.VMEM((length, HD), F32), pltpu.VMEM((length, HD), F32),
            pltpu.SemaphoreType.DMA((copies_of(pieces[5]),)),
        ],
        compiler_params=params(),
        cost_estimate=takes(15),
        name="attn_backward",
    )(meta, d_second, *parts, xhat, scale, gains, qkv, probs, *pieces)


def attn_grads(meta, places, x, d_attn, d_qkv, ctx, vectors, nz, extra):
    length, width = x.shape
    three = d_qkv.shape[1] // 2
    cols = ctx.shape[1] // 2
    rz = width // nz

    def body(meta, places, x, d_attn, d_qkv, ctx, vec1, vec2, sum_qkv, sum_inb, *refs):
        outs, (x_t, a_t, norm_rows_, qv_rows, inb_rows) = refs[:3], refs[3:]
        x_t[...] = x[...].astype(F32).T.astype(BF16)
        a_t[...] = d_attn[...].astype(F32).T.astype(BF16)
        for j in range(2):
            for k in range(nz):
                rows = zrows(meta, k, rz)
                grad = nn(x_t[rows, :], d_qkv[:, j * three : (j + 1) * three])
                put_grad(outs, j, k, nz, 0, grad)
                put_grad(outs, j, k, nz, three, nn(a_t[rows, :], ctx[:, j * cols : (j + 1) * cols]))
        if not extra:
            return
        piece, part = width // (4 * nz), cols // nz
        units = sum_inb.shape[1] // nz
        norm_rows_[...] = jnp.zeros_like(norm_rows_)
        norm_rows_[0:3, :] = vec1[...]
        norm_rows_[3:6, :] = vec2[...]
        for j in range(2):
            qv_rows[...] = jnp.zeros_like(qv_rows)
            qv_rows[0:1, :cols] = sum_qkv[j : j + 1, :cols]
            qv_rows[1:2, :cols] = sum_qkv[j : j + 1, 2 * cols : three]
            inb_rows[...] = jnp.zeros_like(inb_rows)
            inb_rows[0:1, :] = sum_inb[j : j + 1, :]
            for k in range(nz):
                d = places[2 + k]
                from_norm = pltpu.roll(norm_rows_[...], width - (d * 4 + places[j]) * piece, 1)
                from_qv = pltpu.roll(qv_rows[...], width - d * part, 1)
                from_inb = pltpu.roll(inb_rows[...], width - d * units, 1)
                lane = lax.broadcasted_iota(jnp.int32, (8, 2 * cols), 1)
                upper = jnp.where(lane < piece, from_norm[:, : 2 * cols], 0.0)
                lower = jnp.where(lane < part, from_qv[:, : 2 * cols], 0.0)
                shifted = pltpu.roll(from_inb, 128, 1)[:, : 2 * cols]
                inside = jnp.logical_and(lane >= 128, lane < 128 + units)
                lower = jnp.where(inside, shifted, lower)
                put_grad(outs, j, k, nz, 0, jnp.concatenate([upper, lower], 0), rz)
                put_grad(outs, j, k, nz, 2 * cols, jnp.zeros((extra, 2 * cols), F32), rz)

    return pl.pallas_call(
        body,
        out_shape=grads_of(nz, rz + extra, three + cols),
        in_specs=[SM, SM] + [VM] * 8,
        out_specs=[VM] * 3,
        scratch_shapes=[pltpu.VMEM((width, length), BF16)] * 2 + [pltpu.VMEM((8, width), F32)] * 3,
        compiler_params=params(),
        cost_estimate=takes(4),
        name="attn_grads",
    )(meta, places, x, d_attn, d_qkv, ctx, *vectors)


def loss_kernel(own, perm, slots, queries, positive_col, n_own):
    n_q, width = queries.shape
    n_p = slots.shape[0]

    def body(own, perm_from, slots, queries_from, pos, loss_out, d_out, perm, queries, sems):
        get_perm = pltpu.make_async_copy(perm_from, perm, sems.at[0])
        get_queries = pltpu.make_async_copy(queries_from, queries, sems.at[1])
        get_perm.start()
        get_queries.start()
        get_perm.wait()
        get_queries.wait()
        passages = nn(perm[...], slots[...]).astype(BF16)
        logits = nt(queries[...], passages)
        top = jnp.max(logits, -1, keepdims=True)
        log_total = top + jnp.log(jnp.sum(jnp.exp(logits - top), -1, keepdims=True))
        index = lax.broadcasted_iota(jnp.int32, (n_q, n_p), 1)
        hits = pos[...] == index
        chosen = jnp.sum(jnp.where(hits, logits, 0.0), -1, keepdims=True)
        loss_out[...] = jnp.sum(log_total - chosen, 0, keepdims=True) / n_q
        d_logits = (16.0 * (jnp.exp(logits - log_total) - jnp.where(hits, 1.0, 0.0))).astype(BF16)
        pick = jnp.where(
            lax.broadcasted_iota(jnp.int32, (n_p, 128), 0)
            == lax.broadcasted_iota(jnp.int32, (n_p, 128), 1) + own[0],
            1.0, 0.0,
        ).astype(BF16)
        cols = nn(d_logits, pick)
        d_out[...] = nn(cols.T.astype(BF16), queries[...])[:n_own]

    return pl.pallas_call(
        body,
        out_shape=[sds((1, 1), F32), sds((n_own, width), F32)],
        in_specs=[SM, ANY, VM, ANY, VM],
        out_specs=[VM] * 2,
        scratch_shapes=[
            pltpu.VMEM(perm.shape, BF16), pltpu.VMEM(queries.shape, BF16), pltpu.SemaphoreType.DMA((2,)),
        ],
        compiler_params=params(),
        cost_estimate=takes(1),
        name="contrast",
    )(own, perm, slots, queries, positive_col)


def on_device(
    inputs, cls_pos, w_qkv, qv_bias, w_out, w_in, in_bias, w_ffn_out,
    layer_gains, shifts, queries, positive, token_grad,
):
    core = lax.axis_index("section")
    dp = lax.axis_index("dp")
    me = lax.axis_index("tensor")
    n_dp = lax.axis_size("dp")
    n_t = lax.axis_size("tensor")
    first_core = core == 0
    rows_dev, share, width = inputs.shape
    cols = w_qkv.shape[3]
    units = w_in.shape[2]
    length = n_t * share
    n_chips = n_dp * n_t
    piece = width // n_chips
    order = dp_order()
    direct = direct_dp()
    nz, extra = (4, 16) if direct else (2, 0)
    t_ids = jnp.arange(n_t, dtype=jnp.int32)

    vec = jnp.concatenate(
        [layer_gains.reshape(-1), shifts.reshape(-1), qv_bias.reshape(-1), in_bias.reshape(-1)]
    )
    n_gain, n_shift, n_qv, n_inb = layer_gains.size, shifts.size, qv_bias.size, in_bias.size
    n_vec = vec.shape[0]
    flat = jnp.concatenate(
        [vec, queries.reshape(-1), (positive // 16).astype(BF16), (positive % 16).astype(BF16)]
    )
    flat = jnp.pad(flat, (0, -flat.shape[0] % 2048)).reshape(-1, 128)

    def spread_rows(block):
        blocks = [lax.dynamic_index_in_dim(block, me ^ k, 0, keepdims=False) for k in range(n_t)]
        return jnp.concatenate(exchange_rows(blocks), 0)

    pack = jnp.concatenate(
        [w_qkv[0, :, 0], w_qkv[0, :, 1], w_qkv[0, :, 2], w_out[0].T, w_in[0], w_ffn_out[0].T], 1
    )
    message = spread_dp(flat)
    if direct:
        own = pack
        z_a = rest_dp(after(pack[:, :width], message))
    else:
        pack = lax.all_gather(pack, "dp", axis=0, tiled=True)
        own, other_rows = pack[: width // 2], pack[width // 2 :][None]
    near0, far0 = gather_own(after(own, message))
    message = spread_tensor(message)
    both0 = gather_own_both(near0, far0)
    owns = [own, near0, far0, *both0]

    def halves_of(blocks, first, size, *earlier):
        half = size // 2
        if not direct:
            blocks = other_rows[:, :, first : first + size]
            return blocks[:, :, :half], blocks[:, :, half:]
        blocks = after(blocks, *earlier)
        return jnp.stack([b[:, :half] for b in blocks]), jnp.stack([b[:, half:] for b in blocks])

    rest_a = jnp.stack(after(z_a, near0, far0)) if direct else other_rows[:, :, :width]
    near_a, far_a = gather_own(rest_a)
    if direct:
        z_b = rest_dp(after(pack[:, width:], rest_a))
    rows_in = spread_rows(after(jnp.where(first_core, inputs, token_grad), near_a))
    near_a, far_a = after((near_a, far_a), both0, z_b[:2] if direct else near_a)
    both_a = gather_both(near_a[:, :, : width // 2], far_a[:, :, width // 2 :])
    rows_got = swap_cores(rows_in)
    x_low = jnp.where(first_core, rows_in, rows_got)
    tokens = jnp.where(first_core, rows_got, rows_in)
    rest_b = halves_of(z_b if direct else None, width, 2 * units, both_a)
    near_b = gather_near(rest_b)
    pieces_a = [*owns, rest_a, rest_a, near_a, near_a, far_a, far_a, *both_a]

    zrow = order * (width // n_dp) if direct else jnp.arange(2, dtype=jnp.int32) * (width // 2)
    metas = [
        jnp.concatenate([(core == level)[None].astype(jnp.int32), zrow.astype(jnp.int32)])
        for level in range(2)
    ]
    slots = [me ^ (2 * (core != level) + jnp.arange(2, dtype=jnp.int32)) for level in range(2)]
    places = [jnp.concatenate([s, order[:nz]]).astype(jnp.int32) for s in slots]
    hots = [(s[:, None] == t_ids[None, :]).astype(F32) for s in slots]

    positions = jnp.concatenate(
        [(me ^ k) * share + jnp.arange(share, dtype=jnp.int32) for k in range(n_t)]
    )
    cls_row = lax.dynamic_index_in_dim(cls_pos, me, 0, keepdims=False)
    segments = jnp.sum((positions[:, None] >= cls_row[None, :]).astype(jnp.int32), -1)
    seg_col, seg_row = segments[:, None], segments[None, :]
    tok_col, tok_row = positions[:, None], positions[None, :]

    slot_ids = (order[None, :] * n_t + (me ^ t_ids)[:, None]).reshape(-1)
    to_natural = (jnp.arange(n_chips, dtype=jnp.int32)[:, None] == slot_ids[None, :]).astype(BF16)
    table = nn(to_natural, message.reshape(n_chips, -1))
    own_table = table[:, :n_vec].astype(BF16)
    other_table = swap_cores(own_table)
    tables = jnp.where(
        first_core, jnp.stack([own_table, other_table]), jnp.stack([other_table, own_table])
    ).astype(F32)
    at = 0
    gains = tables[:, :, at : at + n_gain].reshape(2, n_chips, 2, piece).transpose(0, 2, 1, 3).reshape(2, 2, width)
    at += n_gain
    shift = tables[:, :, at : at + n_shift].reshape(2, n_chips, 4, piece).transpose(0, 2, 1, 3).reshape(2, 4, width)
    at += n_shift
    qv = tables[:, :, at : at + n_qv].reshape(2, n_dp, n_t, 2, cols // n_dp)
    qv = qv.transpose(0, 3, 2, 1, 4).reshape(2, 2, n_t, cols)
    at += n_qv
    inb = tables[:, :, at : at + n_inb].reshape(2, n_dp, n_t, n_inb).transpose(0, 2, 1, 3).reshape(2, n_t, units)
    vectors = []
    for level in range(2):
        bias = jnp.sum(hots[level][None, :, :, None] * qv[level][:, None], 2)
        bias = jnp.stack([bias[0], jnp.zeros_like(bias[0]), bias[1]], 1).reshape(1, -1)
        bias_in = jnp.sum(hots[level][:, :, None] * inb[level][None], 1).reshape(1, -1)
        vectors.append((gains[level], shift[level], bias, bias_in))
    at = n_vec
    q_dev = queries.shape[0]
    all_q = table[:, at : at + q_dev * width].reshape(-1, width).astype(BF16)
    at += q_dev * width
    all_pos = table[:, at : at + q_dev] * 16.0 + table[:, at + q_dev : at + 2 * q_dev]
    all_pos = all_pos.astype(jnp.int32).reshape(-1, 1)
    n_cls = cls_row.shape[0]
    perm = jnp.repeat(jnp.repeat(to_natural, n_cls, 0), n_cls, 1)
    perm = perm * jnp.tile(jnp.eye(n_cls, dtype=BF16), (n_chips, n_chips))

    vectors, all_q, all_pos, perm, x_low = lax.optimization_barrier(
        (vectors, all_q, all_pos, perm, x_low)
    )
    saved = []
    source, parts, norms = x_low, None, None
    for level in range(2):
        gain, shift, bias, bias_in = vectors[level]
        outs = attn_forward(
            level, metas[level], source, parts, norms, pieces_a, bias, seg_col, seg_row, cols
        )
        part, qkv, probs, ctx = outs[:4]
        if level == 0:
            pieces_b = [*owns, *rest_b, *near_b, *gather_both(near_b[0], after(near_b[3], part))]
        if level:
            x, xhat2, scale2 = outs[4:]
            saved[0]["second"] = (xhat2, scale2)
        else:
            x = x_low
        part, mid, xhat1, scale1, act, slope = ffn_forward(
            metas[level], x, (part, swap_cores(part)), gain, shift, pieces_b, bias_in, units
        )
        saved.append(
            dict(x=x, qkv=qkv, probs=probs, ctx=ctx, mid=mid, xhat1=xhat1, scale1=scale1, act=act, slope=slope)
        )
        source, parts, norms = mid, (part, swap_cores(part)), (gain, shift)
    y, xhat2, scale2, cls_own = last_norm(source, parts, *norms, tok_row, cls_row)
    saved[1]["second"] = (xhat2, scale2)

    cls_slots = spread_tensor(spread_dp(cls_own)).reshape(n_chips * n_cls, width)
    first_own = ((dp * n_t + me) * n_cls).astype(jnp.int32)[None]
    mean_loss, d_cls = loss_kernel(first_own, perm, cls_slots, all_q, all_pos, n_cls)

    vector_rows = [None, None]
    sources = (tokens, d_cls, tok_col, cls_row)
    sums_a, sums_b = [None, None], [None, None]
    for level in (1, 0):
        gain = vectors[level][0]
        kept = saved[level]
        meta = metas[level]
        xhat2, scale2 = kept["second"]
        if level == 0:
            sources = (after(sources[0], sums_b[1].first(grads_a[1])), *sources[1:])
        part, d_second, d_ffn, d_pre, vec2, sum_inb = ffn_backward(
            level, meta, sources, xhat2, scale2, gain, kept["slope"], pieces_b, units
        )
        other = swap_cores(part)
        if level == 0:
            d_ffn = after(d_ffn, sums_a[1].first(part))
        grads_b = ffn_grads(meta, kept["mid"], d_pre, d_ffn, kept["act"], nz)
        sums_b[level] = Reduction(grads_b, level)
        d_second = after(d_second, grads_b[1])
        if level == 0:
            d_second = after(d_second, sums_b[1].second(grads_b[1]))
        part, d_first, d_attn, d_qkv, vec1, sum_qkv = attn_backward(
            meta, d_second, (part, other), kept["xhat1"], kept["scale1"], gain,
            kept["qkv"], kept["probs"], pieces_a, cols,
        )
        other = swap_cores(part)
        if level == 0:
            d_attn = after(d_attn, sums_b[0].first(sums_a[1].second(part)))
        grads_a = attn_grads(
            meta, places[level], kept["x"], d_attn, d_qkv, kept["ctx"], (vec1, vec2, sum_qkv, sum_inb), nz, extra
        )
        sums_a[level] = Reduction(grads_a, level)
        vector_rows[level] = (vec1, vec2, sum_qkv, sum_inb)
        sources = (d_first, part, other)
    sums_b[1].third(grads_a[1])
    sums_b[0].second_direct(sums_b[1].pieces)
    sums_a[1].third(sums_b[0].sums)
    sums_a[0].first(sums_a[1].pieces, sums_b[0].hops[:1] if direct else sums_b[0].sums)
    sums_a[0].second_direct(sums_a[0].added)
    last_a1, last_b1 = last_dp([sums_a[1], sums_b[1]], sums_a[0].sums)
    total_b0 = sums_b[0].third_direct()
    d_hidden = d_first + (part.astype(F32) + other.astype(F32))
    outgoing = jnp.where(first_core, d_hidden, y.astype(F32))
    low = after(outgoing.astype(BF16), sums_a[0].added).reshape(n_t, share, width)
    incoming = [outgoing[:share]] + [b.astype(F32) for b in exchange_rows([low[k] for k in range(n_t)])[1:]]
    boundary = jnp.zeros((n_t, share, width), F32)
    for k in range(n_t):
        boundary = lax.dynamic_update_index_in_dim(boundary, incoming[k], me ^ k, 0)
    tot_b, tot_a = (
        jnp.where(first_core, low, sum(p.astype(F32) for p in high))
        for low, high in ((total_b0, last_b1), (sums_a[0].third_direct(), last_a1))
    )
    if direct:
        end = width // n_dp
        own = tot_a[end : end + 6, :piece]
        qv = tot_a[end + 8 : end + 10, : qv_bias.shape[3]]
        grad_inb = tot_a[end + 8 : end + 9, 128 : 128 + n_inb]
        tot_a = tot_a[:end]
    else:
        tables = []
        for level in range(2):
            vec1, vec2, sum_qkv, sum_inb = vector_rows[level]
            by_t = lax.dot_general(
                hots[level], jnp.concatenate([sum_qkv, sum_inb], 1), (((0,), (0,)), ((), ())),
                precision=lax.Precision.HIGHEST,
            )
            whole = 0.5 * jnp.concatenate([vec1, vec2])
            whole = jnp.pad(whole, ((0, 0), (0, by_t.shape[1] - width)))
            tables.append(jnp.concatenate([whole, by_t]))
        tables = lax.psum(jnp.stack(tables), ("section", "dp", "tensor"))
        flat = jnp.where(first_core, tables[0], tables[1])
        own = lax.dynamic_slice_in_dim(flat[:6, :width], (dp * n_t + me) * piece, piece, 1)
        by_t = lax.dynamic_slice_in_dim(flat, 6 + me, 1, 0)
        qv = jnp.concatenate([by_t[:, :cols], by_t[:, 2 * cols : 3 * cols]])
        qv = lax.dynamic_slice_in_dim(qv, dp * qv_bias.shape[3], qv_bias.shape[3], 1)
        grad_inb = lax.dynamic_slice_in_dim(by_t[:, 3 * cols :], dp * n_inb, n_inb, 1)
    grad_gains = jnp.concatenate([own[0:1], own[3:4]]).reshape(layer_gains.shape)
    grad_shifts = jnp.concatenate([own[2:3], own[1:2], own[5:6], own[4:5]]).reshape(shifts.shape)
    grad_qv, grad_inb = qv.reshape(qv_bias.shape), grad_inb.reshape(in_bias.shape)

    grad_qkv = jnp.stack([tot_a[:, n * cols : (n + 1) * cols] for n in range(3)], 1)[None]
    grad_out = tot_a[:, 3 * cols :].T[None]
    grad_in = tot_b[:, :units][None]
    grad_ffn = tot_b[:, units:].T[None]
    return (
        grad_qkv, grad_qv, grad_out, grad_in, grad_inb, grad_ffn,
        grad_gains, grad_shifts, boundary[None], mean_loss.reshape(()),
    )


def solution(mesh):
    return jax.shard_map(
        on_device,
        mesh=mesh,
        in_specs=(
            P("dp", "tensor", None),
            P("dp", None),
            P("section", "dp", None, "tensor"),
            P("section", None, "tensor", "dp"),
            P("section", "tensor", "dp"),
            P("section", "dp", "tensor"),
            P("section", "tensor", "dp"),
            P("section", "tensor", "dp"),
            P("section", None, ("dp", "tensor")),
            P("section", None, ("dp", "tensor")),
            P(("dp", "tensor"), None),
            P(("dp", "tensor")),
            P("dp", "tensor", None),
        ),
        out_specs=(
            P("section", "dp", None, "tensor"),
            P("section", None, "tensor", "dp"),
            P("section", "tensor", "dp"),
            P("section", "dp", "tensor"),
            P("section", "tensor", "dp"),
            P("section", "tensor", "dp"),
            P("section", None, ("dp", "tensor")),
            P("section", None, ("dp", "tensor")),
            P("section", "dp", "tensor", None),
            P(),
        ),
        check_vma=False,
    )
```

```python
import jax
import jax.numpy as jnp
from jax import lax
from jax.experimental import pallas as pl
from jax.experimental.pallas import tpu as pltpu
from jax.sharding import PartitionSpec as P

HD = 64
PARTNER = 1
CROSS = 2
BF16 = jnp.bfloat16
F32 = jnp.float32


def mm(left, right, dims):
    return lax.dot_general(left, right, (dims, ((), ())), preferred_element_type=F32)


def nn(left, right):
    return mm(left, right, ((1,), (0,)))


def nt(left, right):
    return mm(left, right, ((1,), (1,)))


def after(block, *earlier):
    return lax.optimization_barrier((block, *earlier))[0]


def swap_cores(block):
    return lax.ppermute(block, "section", [(0, 1), (1, 0)])


def hop(block, axis, flip):
    return lax.ppermute(block, axis, [(i, i ^ flip) for i in range(lax.axis_size(axis))])


def core_hop(block, axis, flip, core):
    size = lax.axis_size(axis)
    route = [(core * size + i, core * size + (i ^ flip)) for i in range(size)]
    return lax.ppermute(block, ("section", axis), route)


def cross_hop(block, source):
    size = lax.axis_size("tensor")
    route = [(source * size + i, (1 - source) * size + (i ^ CROSS)) for i in range(size)]
    return lax.ppermute(block, ("section", "tensor"), route)


def direct_dp():
    return lax.axis_size("dp") == 4


def dp_order():
    size = lax.axis_size("dp")
    if direct_dp():
        return lax.axis_index("dp") ^ jnp.arange(size, dtype=jnp.int32)
    return jnp.arange(size, dtype=jnp.int32)


def spread_dp(block):
    if direct_dp():
        return jnp.stack([block] + [hop(block, "dp", k) for k in range(1, 4)])
    return lax.all_gather(block, "dp", axis=0, tiled=False)


def spread_tensor(block):
    return jnp.stack([block] + [hop(block, "tensor", k) for k in range(1, 4)])


def double(block, axis):
    pair = jnp.stack([block, hop(block, axis, 1)])
    return jnp.concatenate([pair, hop(pair, axis, 2)])


def exchange_rows(blocks):
    first = hop(jnp.stack([blocks[1], blocks[3]]), "tensor", 1)
    second = hop(jnp.stack([blocks[2], first[1]]), "tensor", 2)
    return [blocks[0], first[0], second[0], second[1]]


def cross_all(block):
    size = lax.axis_size("tensor")
    route = [(s * size + i, (1 - s) * size + (i ^ CROSS)) for s in range(2) for i in range(size)]
    return lax.ppermute(block, ("section", "tensor"), route)


def rest_dp(own):
    return [hop(own, "dp", k) for k in range(1, 4)]


def gather_own(own):
    near, far = hop(own, "tensor", PARTNER), cross_all(own)
    return near, far


def gather_own_both(near, far):
    half = near.shape[1] // 2
    return cross_all(near[:, :half]), hop(far[:, half:], "tensor", PARTNER)


def gather_near(rest):
    a, b = rest
    near_a, far_b = hop(a, "tensor", PARTNER), cross_all(b)
    near_b, far_a = hop(b, "tensor", PARTNER), cross_all(a)
    return near_a, near_b, far_a, far_b


def gather_both(near_a, far_b):
    return cross_all(near_a), hop(far_b, "tensor", PARTNER)


def add_low(*items):
    total = items[0].astype(F32)
    for item in items[1:]:
        total = total + item.astype(F32)
    return total.astype(BF16)


class Reduction:
    def __init__(self, grads, core):
        self.core = core
        self.pair, self.next_b, self.own_b = grads
        self.got = cross_hop(self.pair, 1 - core)
        self.near_b = hop(self.next_b, "tensor", PARTNER)

    def first(self, *earlier):
        half = self.next_b.shape[0]
        self.parts = pair, own_b, got, near_b = after((self.pair, self.own_b, self.got, self.near_b), *earlier)
        self.added = add_low(pair[:half], got[:half]), add_low(own_b, near_b)
        self.near_a = core_hop(self.added[0], "tensor", PARTNER, self.core)
        self.far_b = cross_hop(self.added[1], 1 - self.core)
        return self.added

    def sum_halves(self, *earlier):
        half = self.next_b.shape[0]
        near_a, far_b, (pair, own_b, got, near_b) = after((self.near_a, self.far_b, self.parts), *earlier)
        return add_low(pair[half:], got[half:], near_a), add_low(own_b, near_b, far_b)

    def scatter(self):
        whole = jnp.concatenate(self.sums).reshape(-1, self.own_b.shape[2])
        return [lax.psum_scatter(whole, "dp", scatter_dimension=0, tiled=True)]

    def second_direct(self, *earlier):
        a, b = self.sums = self.sum_halves(*earlier)
        if direct_dp():
            self.hops = [
                core_hop(block, "dp", k, self.core) for k, block in ((1, a[1]), (2, b[0]), (3, b[1]))
            ]
        return self.sums

    def third_direct(self, *earlier):
        if not direct_dp():
            return sum(p.astype(F32) for p in self.scatter())
        return sum(p.astype(F32) for p in after([self.sums[0][0], *self.hops], *earlier))

    def second(self, *earlier):
        self.sums = self.sum_halves(*earlier)
        if direct_dp():
            self.across = core_hop(self.sums[1], "dp", 2, self.core)
        return self.sums

    def third(self, *earlier):
        if not direct_dp():
            self.pieces = self.scatter()
            return self.pieces
        a, across = after((self.sums[0], self.across), *earlier)
        self.pieces = [add_low(a[k], across[k]) for k in range(2)]
        return self.pieces


def last_dp(reductions, *earlier):
    if not direct_dp():
        return [r.pieces for r in reductions]
    high = max(r.pieces[0].shape[0] for r in reductions)
    block = [jnp.pad(r.pieces[1], ((0, high - r.pieces[1].shape[0]), (0, 0))) for r in reductions]
    got = core_hop(after(jnp.concatenate(block, 1), *earlier), "dp", 1, reductions[0].core)
    at, out = 0, []
    for r in reductions:
        rows, width = r.pieces[0].shape
        out.append([r.pieces[0], got[:rows, at : at + width]])
        at += width
    return out


VMEM_LIMIT = 48 * 1024 * 1024
CHUNK = 128


def takes(micros):
    return pl.CostEstimate(flops=int(micros * 1.1e9), bytes_accessed=0, transcendentals=0)


def params():
    return pltpu.CompilerParams(vmem_limit_bytes=VMEM_LIMIT)


ANY = pl.BlockSpec(memory_space=pl.ANY)
VM = pl.BlockSpec(memory_space=pltpu.VMEM)
SM = pl.BlockSpec(memory_space=pltpu.SMEM)


def sds(shape, dtype):
    return jax.ShapeDtypeStruct(shape, dtype)


def chunks(length, step=CHUNK):
    return [slice(i, i + step) for i in range(0, length, step)]


def norm_rows(z):
    centre = z - jnp.mean(z, -1, keepdims=True)
    spread = jnp.mean(centre * centre, -1, keepdims=True)
    scale = lax.rsqrt(spread + 1e-05)
    return centre * scale, scale


def norm_back_rows(d_out, gain, xhat, scale):
    g = d_out * gain
    m1 = jnp.mean(g, -1, keepdims=True)
    m2 = jnp.mean(g * xhat, -1, keepdims=True)
    return scale * (g - m1 - xhat * m2)


def gelu_parts(x):
    e = jnp.exp(-0.5 * x * x)
    t = 1.0 / (1.0 + 0.2316418882 * jnp.abs(x))
    poly = t * (
        0.127414796 + t * (-0.142248368 + t * (0.7107068705 + t * (-0.7265760135 + t * 0.5307027145)))
    )
    tail = poly * e
    cdf = jnp.where(x < 0.0, tail, 1.0 - tail)
    return x * cdf, cdf + x * e * 0.3989422804014327


def zrows(meta, k, rz):
    return pl.ds(pl.multiple_of(meta[1 + k], 64), rz)


def cut(start, width, at):
    if start < at < start + width:
        return [(start, at - start), (at, start + width - at)]
    return [(start, width)]


def load_weights(meta, pieces, base, places, sems):
    own, near0, far0, a0, b0, *halves = pieces
    rest, near, far, both = halves[0:2], halves[2:4], halves[4:6], halves[6:8]
    split0, split, count = a0.shape[1], both[0].shape[2], rest[0].shape[0]
    home = meta[0] == 1
    lists = [[] for _ in places]
    at = 0
    for j in range(2):
        for k in range(count + 1):
            rows = zrows(meta, k, own.shape[0])
            for n, (start, width, place) in enumerate(places):
                offset = 0 if k else base
                for g, w in cut(offset + start, width, split if k else split0):
                    side, column = divmod(g, split if k else split0)
                    if k == 0:
                        mine = (near0 if j else own).at[:, pl.ds(g, w)]
                        other = (a0, b0)[side].at[:, pl.ds(column, w)] if j else far0.at[:, pl.ds(g, w)]
                    else:
                        mine, other = (
                            v[side].at[k - 1, :, pl.ds(g if v[0].shape[2] > split else column, w)]
                            for v in ((near, both) if j else (rest, far))
                        )
                    dst = place(j, rows, g - offset - start, w)
                    first = pltpu.make_async_copy(mine, dst, sems.at[at])
                    second = pltpu.make_async_copy(other, dst, sems.at[at])
                    at += 1

                    @pl.when(home)
                    def _():
                        first.start()

                    @pl.when(jnp.logical_not(home))
                    def _():
                        second.start()

                    lists[n].append(first)
    return lists


def copies_of(rest):
    return 2 * 3 * (1 + rest.shape[0])


def wait_all(waits):
    for made in waits:
        made.wait()


def load_a(meta, pieces, w_a, sems):
    width = w_a.shape[2]
    return load_weights(
        meta, pieces, 0, [(0, width, lambda j, rows, c, w: w_a.at[j, rows, pl.ds(c, w)])], sems
    )[0]


def load_b(meta, pieces, w_i, w_f, sems):
    one = w_i.shape[1] // 2
    base = pieces[0].shape[1] - 2 * one
    return load_weights(
        meta,
        pieces,
        base,
        [
            (0, one, lambda j, rows, c, w: w_i.at[rows, pl.ds(j * one + c, w)]),
            (one, one, lambda j, rows, c, w: w_f.at[rows, pl.ds(j * one + c, w)]),
        ],
        sems,
    )


def attn_forward(level, meta, x_or_mid, parts, norms, pieces, bias, seg_col, seg_row, cols):
    four = 4 * cols
    length, width = x_or_mid.shape
    three = 3 * cols
    heads = 2 * cols // HD

    def body(meta, *refs):
        refs = list(refs)
        src = refs.pop(0)
        if level:
            own, other, gain, shift = (refs.pop(0) for _ in range(4))
        pieces = [refs.pop(0) for _ in range(13)]
        bias, sc, sr = (refs.pop(0) for _ in range(3))
        part_out, qkv_out, probs_out, ctx_out = (refs.pop(0) for _ in range(4))
        if level:
            x_out, xhat_out, scale_out = (refs.pop(0) for _ in range(3))
        w_a, sems = refs
        waits = load_a(meta, pieces, w_a, sems)
        if level:
            for rows in chunks(length):
                z = src[rows, :] + (own[rows, :].astype(F32) + other[rows, :].astype(F32)) + shift[2:3, :]
                xhat, scale = norm_rows(z)
                x_out[rows, :] = (xhat * gain[1:2, :] + shift[3:4, :]).astype(BF16)
                xhat_out[rows, :] = xhat.astype(BF16)
                scale_out[rows, :] = scale
            x_ref = x_out
        else:
            x_ref = src
        wait_all(waits)
        for j in range(2):
            c = slice(j * three, (j + 1) * three)
            for rows in chunks(length, 256):
                qkv_out[rows, c] = (nn(x_ref[rows, :], w_a[j, :, :three]) + bias[:, c]).astype(BF16)
        v_t = jnp.concatenate(
            [qkv_out[:, j * three + 2 * cols : (j + 1) * three].astype(F32) for j in range(2)], 1
        ).T.astype(BF16)
        for queries in chunks(length, 256):
            same = sc[...] == sr[:, queries]
            outs = []
            for h in range(heads):
                j, i = divmod(h, cols // HD)
                at = j * three + i * HD
                q = qkv_out[queries, at : at + HD]
                k = qkv_out[:, at + cols : at + cols + HD]
                st = jnp.where(same, nt(k, q) * 0.125, -1e30)
                p = jnp.exp(st - jnp.max(st, 0, keepdims=True))
                p = (p * (1.0 / jnp.sum(p, 0, keepdims=True))).astype(BF16)
                probs_out[h, :, queries] = p
                outs.append(nn(v_t[h * HD : (h + 1) * HD], p))
            ctx = jnp.concatenate(outs, 0).T.astype(BF16)
            ctx_out[queries, :] = ctx
            part_out[queries, :] = (
                nt(ctx[:, :cols], w_a[0, :, three:]) + nt(ctx[:, cols:], w_a[1, :, three:])
            ).astype(BF16)

    outs = [
        sds((length, width), BF16), sds((length, 2 * three), BF16),
        sds((heads, length, length), BF16), sds((length, 2 * cols), BF16),
    ]
    args = [meta, x_or_mid]
    if level:
        args += [*parts, *norms]
        outs += [sds((length, width), BF16), sds((length, width), BF16), sds((length, 1), F32)]
    specs = [SM] + [VM] * (len(args) - 1) + [ANY] * 13 + [VM] * 3
    args += [*pieces, bias, seg_col, seg_row]
    return pl.pallas_call(
        body,
        out_shape=outs,
        in_specs=specs,
        out_specs=[VM] * len(outs),
        scratch_shapes=[pltpu.VMEM((2, width, four), BF16), pltpu.SemaphoreType.DMA((copies_of(pieces[5]),))],
        compiler_params=params(),
        cost_estimate=takes(13),
        name="attn_forward",
    )(*args)


def ffn_forward(meta, x, parts, gains, shifts, pieces, bias_in, half):
    units = 2 * half
    length, width = x.shape

    def body(meta, x, own, other, gain, shift, p0, p1, p2, p3, p4, p5, p6, p7, p8, p9, p10, p11, p12, bias,
             part_out, mid_out, xhat_out, scale_out, act_out, slope_out, w_i, w_f, low, sems):
        first, second = load_b(meta, (p0, p1, p2, p3, p4, p5, p6, p7, p8, p9, p10, p11, p12), w_i, w_f, sems)
        for rows in chunks(length):
            z = x[rows, :].astype(F32) + (own[rows, :].astype(F32) + other[rows, :].astype(F32)) + shift[0:1, :]
            xhat, scale = norm_rows(z)
            mid = xhat * gain[0:1, :] + shift[1:2, :]
            mid_out[rows, :] = mid
            low[rows, :] = mid.astype(BF16)
            xhat_out[rows, :] = xhat.astype(BF16)
            scale_out[rows, :] = scale
        wait_all(first)
        for rows in chunks(length, 256):
            for c in chunks(units, 512):
                pre = nn(low[rows, :], w_i[:, c]) + bias[:, c]
                act, slope = gelu_parts(pre)
                act_out[rows, c] = act.astype(BF16)
                slope_out[rows, c] = slope.astype(BF16)
        wait_all(second)
        for rows in chunks(length, 256):
            part_out[rows, :] = nt(act_out[rows, :], w_f[...]).astype(BF16)

    return pl.pallas_call(
        body,
        out_shape=[
            sds((length, width), BF16), sds((length, width), F32), sds((length, width), BF16),
            sds((length, 1), F32), sds((length, units), BF16), sds((length, units), BF16),
        ],
        in_specs=[SM] + [VM] * 5 + [ANY] * 13 + [VM],
        out_specs=[VM] * 6,
        scratch_shapes=[
            pltpu.VMEM((width, units), BF16), pltpu.VMEM((width, units), BF16),
            pltpu.VMEM((length, width), BF16), pltpu.SemaphoreType.DMA((copies_of(pieces[5]),)),
        ],
        compiler_params=params(),
        cost_estimate=takes(9),
        name="ffn_forward",
    )(meta, x, *parts, gains, shifts, *pieces, bias_in)


def last_norm(mid, parts, gains, shifts, tok_row, cls_pos):
    length, width = mid.shape
    n_cls = cls_pos.shape[0]

    def body(cls, mid_from, own, other, gain, shift, tok, y_out, xhat_out, scale_out, cls_out, mid, sem):
        get_mid = pltpu.make_async_copy(mid_from, mid, sem.at[0])
        get_mid.start()
        get_mid.wait()
        for rows in chunks(length):
            z = mid[rows, :] + (own[rows, :].astype(F32) + other[rows, :].astype(F32)) + shift[2:3, :]
            xhat, scale = norm_rows(z)
            y_out[rows, :] = (xhat * gain[1:2, :] + shift[3:4, :]).astype(BF16)
            xhat_out[rows, :] = xhat.astype(BF16)
            scale_out[rows, :] = scale
        which = lax.broadcasted_iota(jnp.int32, (16, length), 0)
        hot = jnp.zeros((16, length), F32)
        for p in range(n_cls):
            hot = jnp.where(jnp.logical_and(which == p, tok[...] == cls[p]), 1.0, hot)
        cls_out[...] = nn(hot.astype(BF16), y_out[...])[:n_cls].astype(BF16)

    return pl.pallas_call(
        body,
        out_shape=[
            sds((length, width), BF16), sds((length, width), BF16), sds((length, 1), F32),
            sds((n_cls, width), BF16),
        ],
        in_specs=[SM, ANY] + [VM] * 5,
        out_specs=[VM] * 4,
        scratch_shapes=[pltpu.VMEM((length, width), F32), pltpu.SemaphoreType.DMA((1,))],
        compiler_params=params(),
        cost_estimate=takes(2),
        name="last_norm",
    )(cls_pos, mid, *parts, gains, shifts, tok_row)


def ffn_backward(level, meta, sources, xhat, scale, gains, slope, pieces, half):
    units = 2 * half
    length, width = xhat.shape
    n_cls = sources[3].shape[0] if level else 0

    def body(meta, *refs):
        refs = list(refs)
        if level:
            cls, grad, d_cls, tok = (refs.pop(0) for _ in range(4))
        else:
            d_above, own, other = (refs.pop(0) for _ in range(3))
        xhat_from, scale, gain, slope_from = (refs.pop(0) for _ in range(4))
        pieces = [refs.pop(0) for _ in range(13)]
        part_out, second_out, low_out, pre_out, vec_out, inb_out, w_i, w_f, sems, xhat, slope, kept_sems = refs
        get_hat = pltpu.make_async_copy(xhat_from, xhat, kept_sems.at[0])
        get_slope = pltpu.make_async_copy(slope_from, slope, kept_sems.at[1])
        get_hat.start()
        get_slope.start()
        first, second = load_b(meta, pieces, w_i, w_f, sems)
        sums = [jnp.zeros((1, width), F32) for _ in range(3)]
        get_hat.wait()
        for rows in chunks(length):
            if level:
                d_out = grad[rows, :].astype(F32)
                for p in range(n_cls):
                    d_out = d_out + jnp.where(tok[rows, :] == cls[p], 1.0, 0.0) * d_cls[p : p + 1, :]
            else:
                d_out = d_above[rows, :] + (own[rows, :].astype(F32) + other[rows, :].astype(F32))
                d_out = d_out.astype(BF16).astype(F32)
            hat = xhat[rows, :].astype(F32)
            d_second = norm_back_rows(d_out, gain[1:2, :], hat, scale[rows, :])
            second_out[rows, :] = d_second
            low_out[rows, :] = d_second.astype(BF16)
            for n, item in enumerate((d_out * hat, d_out, d_second)):
                sums[n] = sums[n] + jnp.sum(item, 0, keepdims=True)
        for n in range(3):
            vec_out[n : n + 1, :] = sums[n]
        wait_all(second)
        get_slope.wait()
        for n, rows in enumerate(chunks(length, 256)):
            for c in chunks(units, units // 4):
                d_act = nn(low_out[rows, :], w_f[:, c])
                d_pre = (slope[rows, c].astype(F32) * d_act).astype(BF16)
                pre_out[rows, c] = d_pre
                j, at = divmod(c.start, units // 2)
                at = slice(at, at + c.stop - c.start)
                total = jnp.sum(d_pre.astype(F32), 0, keepdims=True)
                inb_out[j : j + 1, at] = total if n == 0 else inb_out[j : j + 1, at] + total
        wait_all(first)
        for rows in chunks(length, 256):
            part_out[rows, :] = nt(pre_out[rows, :], w_i[...]).astype(BF16)

    if level:
        token_grad, d_cls, tok_col, cls_pos = sources
        args, specs = [meta, cls_pos, token_grad, d_cls, tok_col], [SM, SM, VM, VM, VM]
    else:
        args, specs = [meta, *sources], [SM, VM, VM, VM]
    args += [xhat, scale, gains, slope, *pieces]
    specs += [ANY, VM, VM, ANY] + [ANY] * 13
    return pl.pallas_call(
        body,
        out_shape=[
            sds((length, width), BF16), sds((length, width), F32), sds((length, width), BF16),
            sds((length, units), BF16), sds((3, width), F32), sds((2, units // 2), F32),
        ],
        in_specs=specs,
        out_specs=[VM] * 6,
        scratch_shapes=[
            pltpu.VMEM((width, units), BF16), pltpu.VMEM((width, units), BF16),
            pltpu.SemaphoreType.DMA((copies_of(pieces[5]),)),
            pltpu.VMEM((length, width), BF16), pltpu.VMEM((length, units), BF16),
            pltpu.SemaphoreType.DMA((2,)),
        ],
        compiler_params=params(),
        cost_estimate=takes(9),
        name="ffn_backward",
    )(*args)


def grads_of(nz, rz, width):
    half = nz // 2
    return [sds((nz, rz, width), BF16), sds((half, rz, width), BF16), sds((half, rz, width), BF16)]


def put_grad(outs, j, k, nz, column, value, first=0):
    half, (height, width) = nz // 2, value.shape
    if k < half:
        out, at = outs[0], k + (half if j == 0 else 0)
    else:
        out, at = outs[2 if j == 0 else 1], k - half
    out[at, first : first + height, column : column + width] = value.astype(BF16)


def ffn_grads(meta, mid, d_pre, d_ffn, act, nz):
    length, width = mid.shape
    units = d_pre.shape[1]
    one = units // 2
    rz = width // nz

    def body(meta, mid, d_pre, d_ffn, act, *refs):
        outs, (mid_t, ffn_t) = refs[:3], refs[3:]
        mid_t[...] = mid[...].T.astype(BF16)
        ffn_t[...] = d_ffn[...].astype(F32).T.astype(BF16)
        for j in range(2):
            c = slice(j * one, (j + 1) * one)
            for k in range(nz):
                rows = zrows(meta, k, rz)
                put_grad(outs, j, k, nz, 0, nn(mid_t[rows, :], d_pre[:, c]))
                put_grad(outs, j, k, nz, one, nn(ffn_t[rows, :], act[:, c]))

    return pl.pallas_call(
        body,
        out_shape=grads_of(nz, rz, units),
        in_specs=[SM] + [VM] * 4,
        out_specs=[VM] * 3,
        scratch_shapes=[pltpu.VMEM((width, length), BF16)] * 2,
        compiler_params=params(),
        cost_estimate=takes(7),
        name="ffn_grads",
    )(meta, mid, d_pre, d_ffn, act)


def attn_backward(meta, d_second, parts, xhat, scale, gains, qkv, probs, pieces, cols):
    four = 4 * cols
    length, width = d_second.shape
    three = 3 * cols
    heads = 2 * cols // HD

    def body(meta, d_second, own, other, xhat, scale, gain, qkv, probs, p0, p1, p2, p3, p4, p5, p6, p7, p8, p9, p10, p11, p12,
             part_out, first_out, low_out, dqkv_out, vec_out, sum_out,
             w_a, d_ctx, acc_v, acc_k, sems):
        waits = load_a(meta, (p0, p1, p2, p3, p4, p5, p6, p7, p8, p9, p10, p11, p12), w_a, sems)
        sums = [jnp.zeros((1, width), F32) for _ in range(3)]
        for rows in chunks(length):
            d_mid = d_second[rows, :] + (own[rows, :].astype(F32) + other[rows, :].astype(F32))
            hat = xhat[rows, :].astype(F32)
            d_first = norm_back_rows(d_mid, gain[0:1, :], hat, scale[rows, :])
            first_out[rows, :] = d_first
            low_out[rows, :] = d_first.astype(BF16)
            for n, item in enumerate((d_mid * hat, d_mid, d_first)):
                sums[n] = sums[n] + jnp.sum(item, 0, keepdims=True)
        for n in range(3):
            vec_out[n : n + 1, :] = sums[n]
        wait_all(waits)
        for j in range(2):
            for rows in chunks(length, 256):
                d_ctx[rows, j * cols : (j + 1) * cols] = nn(low_out[rows, :], w_a[j, :, three:]).astype(BF16)
        k_t = jnp.concatenate(
            [qkv[:, j * three + cols : j * three + 2 * cols].astype(F32) for j in range(2)], 1
        ).T.astype(BF16)
        for h in range(heads):
            j, i = divmod(h, cols // HD)
            at = j * three + i * HD
            q_cols, k_cols, v_cols = (slice(at + n * cols, at + n * cols + HD) for n in range(3))
            for n, queries in enumerate(chunks(length, 256)):
                d_o = d_ctx[queries, h * HD : (h + 1) * HD]
                d_p = nt(qkv[:, v_cols], d_o)
                p = probs[h, :, queries]
                wide = p.astype(F32)
                d_s = (wide * (d_p - jnp.sum(wide * d_p, 0, keepdims=True))).astype(BF16)
                d_v = nn(p, d_o)
                d_k = nn(d_s, qkv[queries, q_cols])
                acc_v[...] = d_v if n == 0 else acc_v[...] + d_v
                acc_k[...] = d_k if n == 0 else acc_k[...] + d_k
                d_q = nn(k_t[h * HD : (h + 1) * HD], d_s)
                dqkv_out[queries, q_cols] = (d_q.T * 0.125).astype(BF16)
            dqkv_out[:, v_cols] = acc_v[...].astype(BF16)
            dqkv_out[:, k_cols] = (acc_k[...] * 0.125).astype(BF16)
        for j in range(2):
            sum_out[j : j + 1, :] = jnp.sum(
                dqkv_out[:, j * three : (j + 1) * three].astype(F32), 0, keepdims=True
            )
        for rows in chunks(length, 256):
            part_out[rows, :] = (
                nt(dqkv_out[rows, :three], w_a[0, :, :three]) + nt(dqkv_out[rows, three:], w_a[1, :, :three])
            ).astype(BF16)

    return pl.pallas_call(
        body,
        out_shape=[
            sds((length, width), BF16), sds((length, width), F32), sds((length, width), BF16),
            sds((length, 2 * three), BF16), sds((3, width), F32), sds((2, three), F32),
        ],
        in_specs=[SM] + [VM] * 8 + [ANY] * 13,
        out_specs=[VM] * 6,
        scratch_shapes=[
            pltpu.VMEM((2, width, four), BF16), pltpu.VMEM((length, 2 * cols), BF16),
            pltpu.VMEM((length, HD), F32), pltpu.VMEM((length, HD), F32),
            pltpu.SemaphoreType.DMA((copies_of(pieces[5]),)),
        ],
        compiler_params=params(),
        cost_estimate=takes(15),
        name="attn_backward",
    )(meta, d_second, *parts, xhat, scale, gains, qkv, probs, *pieces)


def attn_grads(meta, places, x, d_attn, d_qkv, ctx, vectors, nz, extra):
    length, width = x.shape
    three = d_qkv.shape[1] // 2
    cols = ctx.shape[1] // 2
    rz = width // nz

    def body(meta, places, x, d_attn, d_qkv, ctx, vec1, vec2, sum_qkv, sum_inb, *refs):
        outs, (x_t, a_t, norm_rows_, qv_rows, inb_rows) = refs[:3], refs[3:]
        x_t[...] = x[...].astype(F32).T.astype(BF16)
        a_t[...] = d_attn[...].astype(F32).T.astype(BF16)
        for j in range(2):
            for k in range(nz):
                rows = zrows(meta, k, rz)
                grad = nn(x_t[rows, :], d_qkv[:, j * three : (j + 1) * three])
                put_grad(outs, j, k, nz, 0, grad)
                put_grad(outs, j, k, nz, three, nn(a_t[rows, :], ctx[:, j * cols : (j + 1) * cols]))
        if not extra:
            return
        piece, part = width // (4 * nz), cols // nz
        units = sum_inb.shape[1] // nz
        norm_rows_[...] = jnp.zeros_like(norm_rows_)
        norm_rows_[0:3, :] = vec1[...]
        norm_rows_[3:6, :] = vec2[...]
        for j in range(2):
            qv_rows[...] = jnp.zeros_like(qv_rows)
            qv_rows[0:1, :cols] = sum_qkv[j : j + 1, :cols]
            qv_rows[1:2, :cols] = sum_qkv[j : j + 1, 2 * cols : three]
            inb_rows[...] = jnp.zeros_like(inb_rows)
            inb_rows[0:1, :] = sum_inb[j : j + 1, :]
            for k in range(nz):
                d = places[2 + k]
                from_norm = pltpu.roll(norm_rows_[...], width - (d * 4 + places[j]) * piece, 1)
                from_qv = pltpu.roll(qv_rows[...], width - d * part, 1)
                from_inb = pltpu.roll(inb_rows[...], width - d * units, 1)
                lane = lax.broadcasted_iota(jnp.int32, (8, 2 * cols), 1)
                upper = jnp.where(lane < piece, from_norm[:, : 2 * cols], 0.0)
                lower = jnp.where(lane < part, from_qv[:, : 2 * cols], 0.0)
                shifted = pltpu.roll(from_inb, 128, 1)[:, : 2 * cols]
                inside = jnp.logical_and(lane >= 128, lane < 128 + units)
                lower = jnp.where(inside, shifted, lower)
                put_grad(outs, j, k, nz, 0, jnp.concatenate([upper, lower], 0), rz)
                put_grad(outs, j, k, nz, 2 * cols, jnp.zeros((extra, 2 * cols), F32), rz)

    return pl.pallas_call(
        body,
        out_shape=grads_of(nz, rz + extra, three + cols),
        in_specs=[SM, SM] + [VM] * 8,
        out_specs=[VM] * 3,
        scratch_shapes=[pltpu.VMEM((width, length), BF16)] * 2 + [pltpu.VMEM((8, width), F32)] * 3,
        compiler_params=params(),
        cost_estimate=takes(4),
        name="attn_grads",
    )(meta, places, x, d_attn, d_qkv, ctx, *vectors)


def loss_kernel(own, perm, slots, queries, positive_col, n_own):
    n_q, width = queries.shape
    n_p = slots.shape[0]

    def body(own, perm_from, slots, queries_from, pos, loss_out, d_out, perm, queries, sems):
        get_perm = pltpu.make_async_copy(perm_from, perm, sems.at[0])
        get_queries = pltpu.make_async_copy(queries_from, queries, sems.at[1])
        get_perm.start()
        get_queries.start()
        get_perm.wait()
        get_queries.wait()
        passages = nn(perm[...], slots[...]).astype(BF16)
        logits = nt(queries[...], passages)
        top = jnp.max(logits, -1, keepdims=True)
        log_total = top + jnp.log(jnp.sum(jnp.exp(logits - top), -1, keepdims=True))
        index = lax.broadcasted_iota(jnp.int32, (n_q, n_p), 1)
        hits = pos[...] == index
        chosen = jnp.sum(jnp.where(hits, logits, 0.0), -1, keepdims=True)
        loss_out[...] = jnp.sum(log_total - chosen, 0, keepdims=True) / n_q
        d_logits = (16.0 * (jnp.exp(logits - log_total) - jnp.where(hits, 1.0, 0.0))).astype(BF16)
        pick = jnp.where(
            lax.broadcasted_iota(jnp.int32, (n_p, 128), 0)
            == lax.broadcasted_iota(jnp.int32, (n_p, 128), 1) + own[0],
            1.0, 0.0,
        ).astype(BF16)
        cols = nn(d_logits, pick)
        d_out[...] = nn(cols.T.astype(BF16), queries[...])[:n_own]

    return pl.pallas_call(
        body,
        out_shape=[sds((1, 1), F32), sds((n_own, width), F32)],
        in_specs=[SM, ANY, VM, ANY, VM],
        out_specs=[VM] * 2,
        scratch_shapes=[
            pltpu.VMEM(perm.shape, BF16), pltpu.VMEM(queries.shape, BF16), pltpu.SemaphoreType.DMA((2,)),
        ],
        compiler_params=params(),
        cost_estimate=takes(1),
        name="contrast",
    )(own, perm, slots, queries, positive_col)


def on_device(
    inputs, cls_pos, w_qkv, qv_bias, w_out, w_in, in_bias, w_ffn_out,
    layer_gains, shifts, queries, positive, token_grad,
):
    core = lax.axis_index("section")
    dp = lax.axis_index("dp")
    me = lax.axis_index("tensor")
    n_dp = lax.axis_size("dp")
    n_t = lax.axis_size("tensor")
    first_core = core == 0
    rows_dev, share, width = inputs.shape
    cols = w_qkv.shape[3]
    units = w_in.shape[2]
    length = n_t * share
    n_chips = n_dp * n_t
    piece = width // n_chips
    order = dp_order()
    direct = direct_dp()
    nz, extra = (4, 16) if direct else (2, 0)
    t_ids = jnp.arange(n_t, dtype=jnp.int32)

    vec = jnp.concatenate(
        [layer_gains.reshape(-1), shifts.reshape(-1), qv_bias.reshape(-1), in_bias.reshape(-1)]
    )
    n_gain, n_shift, n_qv, n_inb = layer_gains.size, shifts.size, qv_bias.size, in_bias.size
    n_vec = vec.shape[0]
    flat = jnp.concatenate(
        [vec, queries.reshape(-1), (positive // 16).astype(BF16), (positive % 16).astype(BF16)]
    )
    flat = jnp.pad(flat, (0, -flat.shape[0] % 2048)).reshape(-1, 128)

    def spread_rows(block):
        blocks = [lax.dynamic_index_in_dim(block, me ^ k, 0, keepdims=False) for k in range(n_t)]
        return jnp.concatenate(exchange_rows(blocks), 0)

    pack = jnp.concatenate(
        [w_qkv[0, :, 0], w_qkv[0, :, 1], w_qkv[0, :, 2], w_out[0].T, w_in[0], w_ffn_out[0].T], 1
    )
    message = spread_dp(flat)
    if direct:
        own = pack
        z_a = rest_dp(after(pack[:, :width], message))
    else:
        pack = lax.all_gather(pack, "dp", axis=0, tiled=True)
        own, other_rows = pack[: width // 2], pack[width // 2 :][None]
    message = spread_tensor(message)
    near0, far0 = gather_own(after(own, message))
    both0 = gather_own_both(near0, far0)
    owns = [own, near0, far0, *both0]

    def halves_of(blocks, first, size, *earlier):
        half = size // 2
        if not direct:
            blocks = other_rows[:, :, first : first + size]
            return blocks[:, :, :half], blocks[:, :, half:]
        blocks = after(blocks, *earlier)
        return jnp.stack([b[:, :half] for b in blocks]), jnp.stack([b[:, half:] for b in blocks])

    rest_a = jnp.stack(after(z_a, near0, far0)) if direct else other_rows[:, :, :width]
    near_a, far_a = gather_own(rest_a)
    if direct:
        z_b = rest_dp(after(pack[:, width:], rest_a))
    rows_in = spread_rows(after(jnp.where(first_core, inputs, token_grad), near_a))
    near_a, far_a = after((near_a, far_a), both0, z_b[:2] if direct else near_a)
    both_a = gather_both(near_a[:, :, : width // 2], far_a[:, :, width // 2 :])
    rows_got = swap_cores(rows_in)
    x_low = jnp.where(first_core, rows_in, rows_got)
    tokens = jnp.where(first_core, rows_got, rows_in)
    rest_b = halves_of(z_b if direct else None, width, 2 * units, both_a)
    near_b = gather_near(rest_b)
    pieces_a = [*owns, rest_a, rest_a, near_a, near_a, far_a, far_a, *both_a]

    zrow = order * (width // n_dp) if direct else jnp.arange(2, dtype=jnp.int32) * (width // 2)
    metas = [
        jnp.concatenate([(core == level)[None].astype(jnp.int32), zrow.astype(jnp.int32)])
        for level in range(2)
    ]
    slots = [me ^ (2 * (core != level) + jnp.arange(2, dtype=jnp.int32)) for level in range(2)]
    places = [jnp.concatenate([s, order[:nz]]).astype(jnp.int32) for s in slots]
    hots = [(s[:, None] == t_ids[None, :]).astype(F32) for s in slots]

    positions = jnp.concatenate(
        [(me ^ k) * share + jnp.arange(share, dtype=jnp.int32) for k in range(n_t)]
    )
    cls_row = lax.dynamic_index_in_dim(cls_pos, me, 0, keepdims=False)
    segments = jnp.sum((positions[:, None] >= cls_row[None, :]).astype(jnp.int32), -1)
    seg_col, seg_row = segments[:, None], segments[None, :]
    tok_col, tok_row = positions[:, None], positions[None, :]

    slot_ids = (order[None, :] * n_t + (me ^ t_ids)[:, None]).reshape(-1)
    to_natural = (jnp.arange(n_chips, dtype=jnp.int32)[:, None] == slot_ids[None, :]).astype(BF16)
    table = nn(to_natural, message.reshape(n_chips, -1))
    own_table = table[:, :n_vec].astype(BF16)
    other_table = swap_cores(own_table)
    tables = jnp.where(
        first_core, jnp.stack([own_table, other_table]), jnp.stack([other_table, own_table])
    ).astype(F32)
    at = 0
    gains = tables[:, :, at : at + n_gain].reshape(2, n_chips, 2, piece).transpose(0, 2, 1, 3).reshape(2, 2, width)
    at += n_gain
    shift = tables[:, :, at : at + n_shift].reshape(2, n_chips, 4, piece).transpose(0, 2, 1, 3).reshape(2, 4, width)
    at += n_shift
    qv = tables[:, :, at : at + n_qv].reshape(2, n_dp, n_t, 2, cols // n_dp)
    qv = qv.transpose(0, 3, 2, 1, 4).reshape(2, 2, n_t, cols)
    at += n_qv
    inb = tables[:, :, at : at + n_inb].reshape(2, n_dp, n_t, n_inb).transpose(0, 2, 1, 3).reshape(2, n_t, units)
    vectors = []
    for level in range(2):
        bias = jnp.sum(hots[level][None, :, :, None] * qv[level][:, None], 2)
        bias = jnp.stack([bias[0], jnp.zeros_like(bias[0]), bias[1]], 1).reshape(1, -1)
        bias_in = jnp.sum(hots[level][:, :, None] * inb[level][None], 1).reshape(1, -1)
        vectors.append((gains[level], shift[level], bias, bias_in))
    at = n_vec
    q_dev = queries.shape[0]
    all_q = table[:, at : at + q_dev * width].reshape(-1, width).astype(BF16)
    at += q_dev * width
    all_pos = table[:, at : at + q_dev] * 16.0 + table[:, at + q_dev : at + 2 * q_dev]
    all_pos = all_pos.astype(jnp.int32).reshape(-1, 1)
    n_cls = cls_row.shape[0]
    perm = jnp.repeat(jnp.repeat(to_natural, n_cls, 0), n_cls, 1)
    perm = perm * jnp.tile(jnp.eye(n_cls, dtype=BF16), (n_chips, n_chips))

    vectors, all_q, all_pos, perm, x_low = lax.optimization_barrier(
        (vectors, all_q, all_pos, perm, x_low)
    )
    saved = []
    source, parts, norms = x_low, None, None
    for level in range(2):
        gain, shift, bias, bias_in = vectors[level]
        outs = attn_forward(
            level, metas[level], source, parts, norms, pieces_a, bias, seg_col, seg_row, cols
        )
        part, qkv, probs, ctx = outs[:4]
        if level == 0:
            pieces_b = [*owns, *rest_b, *near_b, *gather_both(near_b[0], after(near_b[3], part))]
        if level:
            x, xhat2, scale2 = outs[4:]
            saved[0]["second"] = (xhat2, scale2)
        else:
            x = x_low
        part, mid, xhat1, scale1, act, slope = ffn_forward(
            metas[level], x, (part, swap_cores(part)), gain, shift, pieces_b, bias_in, units
        )
        saved.append(
            dict(x=x, qkv=qkv, probs=probs, ctx=ctx, mid=mid, xhat1=xhat1, scale1=scale1, act=act, slope=slope)
        )
        source, parts, norms = mid, (part, swap_cores(part)), (gain, shift)
    y, xhat2, scale2, cls_own = last_norm(source, parts, *norms, tok_row, cls_row)
    saved[1]["second"] = (xhat2, scale2)

    cls_slots = spread_tensor(spread_dp(cls_own)).reshape(n_chips * n_cls, width)
    first_own = ((dp * n_t + me) * n_cls).astype(jnp.int32)[None]
    mean_loss, d_cls = loss_kernel(first_own, perm, cls_slots, all_q, all_pos, n_cls)

    vector_rows = [None, None]
    sources = (tokens, d_cls, tok_col, cls_row)
    sums_a, sums_b = [None, None], [None, None]
    for level in (1, 0):
        gain = vectors[level][0]
        kept = saved[level]
        meta = metas[level]
        xhat2, scale2 = kept["second"]
        if level == 0:
            sources = (after(sources[0], sums_b[1].first(grads_a[1])), *sources[1:])
        part, d_second, d_ffn, d_pre, vec2, sum_inb = ffn_backward(
            level, meta, sources, xhat2, scale2, gain, kept["slope"], pieces_b, units
        )
        other = swap_cores(part)
        if level == 0:
            d_ffn = after(d_ffn, sums_a[1].first(part))
        grads_b = ffn_grads(meta, kept["mid"], d_pre, d_ffn, kept["act"], nz)
        sums_b[level] = Reduction(grads_b, level)
        d_second = after(d_second, grads_b[1])
        if level == 0:
            d_second = after(d_second, sums_b[1].second(grads_b[1]))
        part, d_first, d_attn, d_qkv, vec1, sum_qkv = attn_backward(
            meta, d_second, (part, other), kept["xhat1"], kept["scale1"], gain,
            kept["qkv"], kept["probs"], pieces_a, cols,
        )
        other = swap_cores(part)
        if level == 0:
            d_attn = after(d_attn, sums_b[0].first(sums_a[1].second(part)))
        grads_a = attn_grads(
            meta, places[level], kept["x"], d_attn, d_qkv, kept["ctx"], (vec1, vec2, sum_qkv, sum_inb), nz, extra
        )
        sums_a[level] = Reduction(grads_a, level)
        vector_rows[level] = (vec1, vec2, sum_qkv, sum_inb)
        sources = (d_first, part, other)
    sums_b[1].third(grads_a[1])
    sums_b[0].second_direct(sums_b[1].pieces)
    sums_a[1].third(sums_b[0].sums)
    sums_a[0].first(sums_a[1].pieces, sums_b[0].hops[:1] if direct else sums_b[0].sums)
    sums_a[0].second_direct(sums_a[0].added)
    last_a1, last_b1 = last_dp([sums_a[1], sums_b[1]], sums_a[0].sums)
    total_b0 = sums_b[0].third_direct()
    d_hidden = d_first + (part.astype(F32) + other.astype(F32))
    outgoing = jnp.where(first_core, d_hidden, y.astype(F32))
    low = after(outgoing.astype(BF16), sums_a[0].added).reshape(n_t, share, width)
    incoming = [outgoing[:share]] + [b.astype(F32) for b in exchange_rows([low[k] for k in range(n_t)])[1:]]
    boundary = jnp.zeros((n_t, share, width), F32)
    for k in range(n_t):
        boundary = lax.dynamic_update_index_in_dim(boundary, incoming[k], me ^ k, 0)
    tot_b, tot_a = (
        jnp.where(first_core, low, sum(p.astype(F32) for p in high))
        for low, high in ((total_b0, last_b1), (sums_a[0].third_direct(), last_a1))
    )
    if direct:
        end = width // n_dp
        own = tot_a[end : end + 6, :piece]
        qv = tot_a[end + 8 : end + 10, : qv_bias.shape[3]]
        grad_inb = tot_a[end + 8 : end + 9, 128 : 128 + n_inb]
        tot_a = tot_a[:end]
    else:
        tables = []
        for level in range(2):
            vec1, vec2, sum_qkv, sum_inb = vector_rows[level]
            by_t = lax.dot_general(
                hots[level], jnp.concatenate([sum_qkv, sum_inb], 1), (((0,), (0,)), ((), ())),
                precision=lax.Precision.HIGHEST,
            )
            whole = 0.5 * jnp.concatenate([vec1, vec2])
            whole = jnp.pad(whole, ((0, 0), (0, by_t.shape[1] - width)))
            tables.append(jnp.concatenate([whole, by_t]))
        tables = lax.psum(jnp.stack(tables), ("section", "dp", "tensor"))
        flat = jnp.where(first_core, tables[0], tables[1])
        own = lax.dynamic_slice_in_dim(flat[:6, :width], (dp * n_t + me) * piece, piece, 1)
        by_t = lax.dynamic_slice_in_dim(flat, 6 + me, 1, 0)
        qv = jnp.concatenate([by_t[:, :cols], by_t[:, 2 * cols : 3 * cols]])
        qv = lax.dynamic_slice_in_dim(qv, dp * qv_bias.shape[3], qv_bias.shape[3], 1)
        grad_inb = lax.dynamic_slice_in_dim(by_t[:, 3 * cols :], dp * n_inb, n_inb, 1)
    grad_gains = jnp.concatenate([own[0:1], own[3:4]]).reshape(layer_gains.shape)
    grad_shifts = jnp.concatenate([own[2:3], own[1:2], own[5:6], own[4:5]]).reshape(shifts.shape)
    grad_qv, grad_inb = qv.reshape(qv_bias.shape), grad_inb.reshape(in_bias.shape)

    grad_qkv = jnp.stack([tot_a[:, n * cols : (n + 1) * cols] for n in range(3)], 1)[None]
    grad_out = tot_a[:, 3 * cols :].T[None]
    grad_in = tot_b[:, :units][None]
    grad_ffn = tot_b[:, units:].T[None]
    return (
        grad_qkv, grad_qv, grad_out, grad_in, grad_inb, grad_ffn,
        grad_gains, grad_shifts, boundary[None], mean_loss.reshape(()),
    )


def solution(mesh):
    return jax.shard_map(
        on_device,
        mesh=mesh,
        in_specs=(
            P("dp", "tensor", None),
            P("dp", None),
            P("section", "dp", None, "tensor"),
            P("section", None, "tensor", "dp"),
            P("section", "tensor", "dp"),
            P("section", "dp", "tensor"),
            P("section", "tensor", "dp"),
            P("section", "tensor", "dp"),
            P("section", None, ("dp", "tensor")),
            P("section", None, ("dp", "tensor")),
            P(("dp", "tensor"), None),
            P(("dp", "tensor")),
            P("dp", "tensor", None),
        ),
        out_specs=(
            P("section", "dp", None, "tensor"),
            P("section", None, "tensor", "dp"),
            P("section", "tensor", "dp"),
            P("section", "dp", "tensor"),
            P("section", "tensor", "dp"),
            P("section", "tensor", "dp"),
            P("section", None, ("dp", "tensor")),
            P("section", None, ("dp", "tensor")),
            P("section", "dp", "tensor", None),
            P(),
        ),
        check_vma=False,
    )
```
